32 devices in a mesh: plane: 8 (over y, x, core), depth: 4 (over z).
Axes of the slice: x: 2, y: 2, z: 4, core: 2. Of those that a mesh axis runs over, the one named last changes fastest.
Arguments:
- intensity: int32 [8, 768, 512], P(None, 'plane', 'depth'), may hold values from 0 to 255, as said below
- temp_start: float32 [192, 128], P(('plane', 'depth')), may hold values from 3.8 to 4.6
- cure_start: float32 [192, 128], P(('plane', 'depth')), may hold values from 0.02 to 0.3
- tool_levels: float32 [8], replicated, may hold values from 3.7 to 4.7
- plan: int32 [3, 2], replicated, may hold values from 0 to 7
Outputs:
- temp_final: float32 [192, 128], P(('plane', 'depth'))
- cure_final: float32 [192, 128], P(('plane', 'depth'))
- conduct: float32 [3, 192, 128], P(None, ('plane', 'depth'))
The draws below stay inside these ranges and needn't reach their ends.
Inputs may be any that keep to these rules, and one draw needn't show every extreme that they name: `intensity`: grey levels of a woven laminate.
All inputs are finite; a program needn't handle non-finite values.
Results may differ from the reference program's by a relative error of at most 0.0003.
Values may be sent and summed in bfloat16 or wider, within the bound.
No kernel may reach another device: no remote copies, remote signals or barrier semaphores. Data moves between devices by JAX's collectives and lax.ppermute only.
A program may use at most 64 MiB of HBM per device.

```python
from functools import partial
import jax
import jax.numpy as jnp
import numpy as np
from jax import lax

ROWS = 8
XD = 96
R1 = 6
R2 = 10
COARSE = 4
STEPS = 3
LEVELS = 8
X = 768
Z = 512
XC = 192
NZC = 128


def draw_intensity(key, part):
    key = jax.random.fold_in(key, 11)
    keys = jax.random.split(key, 3)
    blocks_y = (ROWS + 7) // 8
    orient = jax.random.randint(keys[0], (blocks_y, X // 16, Z // 16), 0, 3)
    phases = jax.random.randint(keys[1], (blocks_y, X // 16, Z // 16), 0, 6)
    orient = jnp.repeat(jnp.repeat(jnp.repeat(orient, 8, axis=0)[:ROWS], 16, axis=1), 16, axis=2)
    phases = jnp.repeat(jnp.repeat(jnp.repeat(phases, 8, axis=0)[:ROWS], 16, axis=1), 16, axis=2)
    coord_y = jnp.arange(ROWS, dtype=jnp.int32)[:, None, None]
    coord_x = jnp.arange(X, dtype=jnp.int32)[None, :, None]
    coord_z = jnp.arange(Z, dtype=jnp.int32)[None, None, :]
    coordinate = jnp.where(orient == 0, coord_x, jnp.where(orient == 1, coord_z, coord_y)) + phases
    stripe = coordinate // 3 % 2
    noise = jax.random.randint(keys[2], (ROWS, X, Z), -80, 81)
    return jnp.clip(60 + 130 * stripe + noise, 0, 255).astype(jnp.int32)


def plant(array, own_key, smallest, top_value):
    extent = array.shape
    index_at = [jax.random.randint(jax.random.fold_in(own_key, axis), (), 0, extent[axis]) for axis in range(len(extent))]
    array = array.at[tuple(index_at)].set(smallest)
    longest = extent.index(max(extent))
    index_at[longest] = (index_at[longest] + 1) % extent[longest]
    return array.at[tuple(index_at)].set(top_value)


def block_levels(key, shape, cuts, low, largest):
    factor_of, own = 1.0, jax.random.fold_in(key, 6)
    for axis_at, blocks in cuts:
        draws = jnp.exp(jax.random.uniform(jax.random.fold_in(own, axis_at), (blocks,), jnp.float32, low / len(cuts), largest / len(cuts)))
        factor_of = factor_of * jnp.repeat(draws, shape[axis_at] // blocks).reshape([-1 if axis == axis_at else 1 for axis in range(len(shape))])
    return factor_of


def setup_inputs(seed: int = 0) -> dict:
    seeds = jax.random.split(jax.random.key(seed), 6)
    intensity = draw_intensity(jax.random.fold_in(seeds[5], 71), 0)
    temp_start = jnp.clip(3.8 + 0.79999995 * jax.random.uniform(seeds[1], (XC, NZC), jnp.float32) ** block_levels(seeds[1], (XC, NZC), ((0, 32),), -0.2, 0.2), 3.8, 4.6)
    cure_start = jnp.clip(0.02 + 0.28 * jax.random.uniform(seeds[2], (XC, NZC), jnp.float32) ** block_levels(seeds[2], (XC, NZC), ((0, 32),), -0.2, 0.2), 0.02, 0.3)
    tool_levels = jnp.clip(jax.random.uniform(seeds[3], (LEVELS,), jnp.float32, 3.7, 4.7), 3.7, 4.7)
    plan = plant(jax.random.randint(seeds[4], (STEPS, 2), 0, LEVELS), jax.random.fold_in(seeds[4], 1), 0, LEVELS - 1).astype(jnp.int32)
    return dict(intensity=intensity, temp_start=temp_start, cure_start=cure_start, tool_levels=tool_levels, plan=plan)


sigma_grad = 2.0
sigma_tensor = 3.3
conduct_matrix = 0.3
conduct_fiber = 1.5
time_step = 0.25
heat_release = 0.4
rate_first = 0.15
rate_second = 0.6
energy_first = 30.0
energy_second = 25.0
reference_temp = 4.2
tensor_eps = 1e-06

def smooth_taps(radius, sigma):
    offsets = np.arange(-radius, radius + 1) * 1.0
    weights = np.exp(-0.5 * offsets * offsets / (sigma * sigma))
    return weights / weights.sum()

def slope_taps(radius, sigma):
    offsets = np.arange(-radius, radius + 1) * 1.0
    weights = np.exp(-0.5 * offsets * offsets / (sigma * sigma))
    return offsets * weights / np.sum(offsets * offsets * weights)

def row_weights(count, radius, sigma):
    taps = smooth_taps(radius, sigma)
    result = np.zeros(count)
    for source in range(count):
        for target in range(count):
            offset = target - source
            if abs(offset) <= radius:
                result[source] += taps[offset + radius]
    return result

def valid_conv(values, taps, axis):
    span = len(taps)
    count = values.shape[axis] - span + 1
    total = float(taps[0]) * lax.slice_in_dim(values, 0, count, axis=axis)
    for offset in range(1, span):
        total = total + float(taps[offset]) * lax.slice_in_dim(values, offset, offset + count, axis=axis)
    return total

def same_conv(values, taps, axis):
    radius = (len(taps) - 1) // 2
    widths = [(0, 0)] * values.ndim
    widths[axis] = (radius, radius)
    return valid_conv(jnp.pad(values, widths), taps, axis)

def gradients(field):
    smooth_grad = smooth_taps(R1, sigma_grad)
    slope_grad = slope_taps(R1, sigma_grad)
    flat_z = valid_conv(field, smooth_grad, 2)
    slope_z = valid_conv(field, slope_grad, 2)
    along_x = valid_conv(same_conv(flat_z, smooth_grad, 0), slope_grad, 1)
    along_y = valid_conv(same_conv(flat_z, slope_grad, 0), smooth_grad, 1)
    along_z = valid_conv(same_conv(slope_z, smooth_grad, 0), smooth_grad, 1)
    return (along_y, along_x, along_z)

def reduced_products(field, inside):
    along_y, along_x, along_z = gradients(field)
    weights = jnp.asarray(row_weights(ROWS, R2, sigma_tensor), jnp.float32)[:, None, None]
    pairs = ((along_y, along_y), (along_x, along_x), (along_z, along_z), (along_y, along_x), (along_y, along_z), (along_x, along_z))
    result = jnp.stack([lax.optimization_barrier(jnp.sum(weights * first * second, axis=0)) for first, second in pairs])
    if inside is None:
        return result
    return result * inside

def region_mask(first_x, first_z, count_x, count_z, total_x, total_z):
    position_x = first_x + jnp.arange(count_x, dtype=jnp.int32)[:, None]
    position_z = first_z + jnp.arange(count_z, dtype=jnp.int32)[None, :]
    inside = (position_x >= 0) & (position_x < total_x) & (position_z >= 0) & (position_z < total_z)
    return jnp.where(inside, 1.0, 0.0).astype(jnp.float32)

def smooth_tensor(products):
    taps = smooth_taps(R2, sigma_tensor)
    return valid_conv(valid_conv(products, taps, 1), taps, 2)

def coarse_sums(tensor):
    fields, count_x, count_z = tensor.shape
    return tensor.reshape(fields, count_x // COARSE, COARSE, count_z // COARSE, COARSE).sum(axis=(2, 4))

def conductivity(sums):
    trace = sums[0] + sums[1] + sums[2]
    scale = (conduct_fiber - conduct_matrix) / (2.0 * trace + tensor_eps)
    return jnp.stack([conduct_matrix + scale * (trace - sums[1]), -scale * sums[5], conduct_matrix + scale * (trace - sums[2])])

def tool_value(levels, index):
    return jnp.sum(jnp.where(jnp.arange(LEVELS, dtype=jnp.int32) == index, levels, jnp.zeros_like(levels)))

def cure_rate(temp, cure):
    first = rate_first * jnp.exp(energy_first * (1.0 / reference_temp - 1.0 / temp))
    second = rate_second * jnp.exp(energy_second * (1.0 / reference_temp - 1.0 / temp))
    return (first + second * jnp.sqrt(cure)) * (1.0 - cure) ** 1.5

def advance(padded, conduct, cure, top, bottom):
    height = padded.shape[0]
    upper = jnp.broadcast_to(top, (height, 1)).astype(padded.dtype)
    lower = jnp.broadcast_to(bottom, (height, 1)).astype(padded.dtype)
    full = jnp.concatenate([upper, padded, lower], axis=1)
    centre = full[1:-1, 1:-1]
    second_x = full[2:, 1:-1] - 2.0 * centre + full[:-2, 1:-1]
    second_z = full[1:-1, 2:] - 2.0 * centre + full[1:-1, :-2]
    cross = 0.25 * (full[2:, 2:] - full[2:, :-2] - full[:-2, 2:] + full[:-2, :-2])
    spread = conduct[0] * second_x + 2.0 * conduct[1] * cross + conduct[2] * second_z
    rate = cure_rate(centre, cure)
    return (centre + time_step * (spread + heat_release * rate), cure + time_step * rate)

def block_conductivity(intensity, block):
    rim = R1 + R2
    blocks = X // XD
    start = block * XD
    left = lax.dynamic_slice(intensity, (jnp.int32(0), jnp.maximum(start - rim, 0).astype(jnp.int32), jnp.int32(0)), (ROWS, rim, Z))
    middle = lax.dynamic_slice(intensity, (jnp.int32(0), start.astype(jnp.int32), jnp.int32(0)), (ROWS, XD, Z))
    right = lax.dynamic_slice(intensity, (jnp.int32(0), jnp.minimum(start + XD, X - rim).astype(jnp.int32), jnp.int32(0)), (ROWS, rim, Z))
    left = jnp.where(block > 0, left, jnp.zeros_like(left))
    right = jnp.where(block < blocks - 1, right, jnp.zeros_like(right))
    field = jnp.concatenate([left, middle, right], axis=1).astype(jnp.float32) / 255.0
    field = jnp.pad(field, ((0, 0), (0, 0), (rim, rim)))
    inside = region_mask(start - R2, jnp.int32(-R2), XD + 2 * R2, Z + 2 * R2, X, Z)
    products = reduced_products(field, inside)
    return conductivity(coarse_sums(smooth_tensor(products)))

def reference(intensity, temp_start, cure_start, tool_levels, plan):
    blocks = X // XD
    pieces = lax.map(partial(block_conductivity, intensity), jnp.arange(blocks, dtype=jnp.int32))
    conduct = jnp.transpose(pieces, (1, 0, 2, 3)).reshape(3, X // COARSE, Z // COARSE)
    temp, cure = (temp_start, cure_start)
    for index in range(STEPS):
        top = tool_value(tool_levels, plan[index, 0])
        bottom = tool_value(tool_levels, plan[index, 1])
        padded = jnp.pad(temp, ((1, 1), (0, 0)), mode='edge')
        temp, cure = advance(padded, conduct, cure, top, bottom)
    return (temp, cure, conduct)
```

```python
import functools

import jax
import jax.numpy as jnp
import ml_dtypes
import numpy as np
from jax import lax
from jax.experimental import pallas as pl
from jax.experimental.pallas import tpu as pltpu
from jax.sharding import PartitionSpec as P

ROWS = 8
R1 = 6
R2 = 10
COARSE = 4
STEPS = 3

sigma_grad = 2.0
sigma_tensor = 3.3
conduct_matrix = 0.3
conduct_fiber = 1.5
time_step = 0.25
heat_release = 0.4
rate_first = 0.15
rate_second = 0.6
energy_first = 30.0
energy_second = 25.0
reference_temp = 4.2
tensor_eps = 1e-06

EDGE = 32
RIM = R1 + R2
LANES = 128
HALO = 2
GHOST = 3
BEFORE = EDGE // 2 // COARSE


def smooth_taps(radius, sigma):
    offsets = np.arange(-radius, radius + 1) * 1.0
    weights = np.exp(-0.5 * offsets * offsets / (sigma * sigma))
    return weights / weights.sum()


def slope_taps(radius, sigma):
    offsets = np.arange(-radius, radius + 1) * 1.0
    weights = np.exp(-0.5 * offsets * offsets / (sigma * sigma))
    return offsets * weights / np.sum(offsets * offsets * weights)


def row_weights(count, radius, sigma):
    taps = smooth_taps(radius, sigma)
    result = np.zeros(count)
    for source in range(count):
        for target in range(count):
            offset = target - source
            if abs(offset) <= radius:
                result[source] += taps[offset + radius]
    return result


def halves(matrix):
    high = matrix.astype(np.float32).astype(ml_dtypes.bfloat16)
    low = (matrix - high.astype(np.float64)).astype(np.float32).astype(ml_dtypes.bfloat16)
    return high, low


def sizes(width, depth):
    columns = width // COARSE + 2 * HALO
    cells = depth // COARSE + BEFORE
    span_x = columns * COARSE + 2 * R2
    span_z = cells * COARSE + 2 * R2
    pad_x = -(-span_x // 16) * 16
    return columns, cells, span_x, span_z, pad_x


def x_bands(width, depth):
    columns, cells, span_x, span_z, pad_x = sizes(width, depth)
    bands = np.zeros((2, pad_x, width + 2 * EDGE))
    first = EDGE - HALO * COARSE - R2 - R1
    for kind, taps in enumerate((smooth_taps(R1, sigma_grad), slope_taps(R1, sigma_grad))):
        for out in range(span_x):
            bands[kind, out, out + first : out + first + 2 * R1 + 1] = taps
    return bands.reshape(2 * pad_x, -1)


def z_bands(width, depth):
    columns, cells, span_x, span_z, pad_x = sizes(width, depth)
    bands = np.zeros((2, depth + LANES, 2 * LANES))
    for kind, taps in enumerate((smooth_taps(R1, sigma_grad), slope_taps(R1, sigma_grad))):
        for out in range(span_z):
            for k in range(2 * R1 + 1):
                place = out + k - R1 - R2 - BEFORE * COARSE
                if 0 <= place < depth:
                    bands[kind, place, out] = taps[k]
                elif -EDGE <= place < 0:
                    bands[kind, depth + EDGE + place, out] = taps[k]
    return bands


def coarse_bands(count, padded_in, padded_out):
    taps = smooth_taps(R2, sigma_tensor)
    bands = np.zeros((padded_in, padded_out))
    for cell in range(count):
        for voxel in range(COARSE):
            start = cell * COARSE + voxel
            bands[start : start + 2 * R2 + 1, cell] += taps
    return bands


def three_parts(values):
    high = values.astype(jnp.bfloat16).astype(jnp.float32)
    rest = values - high
    middle = rest.astype(jnp.bfloat16).astype(jnp.float32)
    return high, middle, (rest - middle).astype(jnp.bfloat16).astype(jnp.float32)


def column_slot(temp_ref, cure_ref, first):
    pad = jnp.zeros((8 - 2 * GHOST, temp_ref.shape[1]), jnp.float32)
    rows = pl.ds(first, GHOST)
    both = jnp.concatenate([temp_ref[rows, :], cure_ref[rows, :], pad], axis=0)
    high, middle, low = three_parts(both)
    return jnp.concatenate([high, middle, low, jnp.zeros_like(high)], axis=0).astype(jnp.bfloat16)


def pack_kernel(intensity, temp, cure, up, to_left, to_right, up_left, up_right):
    rows, width, depth = intensity.shape
    lane = lax.broadcasted_iota(jnp.int32, (width, depth), 1)
    for pair in range(2):
        packed = jnp.zeros((width, depth), jnp.float32)
        for block in range(rows // 2):
            values = intensity[2 * block + pair].astype(jnp.float32)
            shift = (EDGE * block + EDGE) % depth
            moved = values if shift == 0 else pltpu.roll(values, shift, 1)
            inside = (lane >= EDGE * block) & (lane < EDGE * block + EDGE)
            packed = jnp.where(inside, moved, packed)
        packed = packed.astype(jnp.bfloat16)
        up[pair] = packed
        up_left[pair] = packed[:EDGE]
        up_right[pair] = packed[width - EDGE :]
    for row in range(rows):
        to_left[row] = intensity[row, :EDGE, :].astype(jnp.float32).astype(jnp.bfloat16)
        to_right[row] = intensity[row, width - EDGE :, :].astype(jnp.float32).astype(jnp.bfloat16)
    count = temp.shape[0]
    left, right = column_slot(temp, cure, 0), column_slot(temp, cure, count - GHOST)
    for slot in range(temp.shape[1] // LANES):
        to_left[rows + slot] = left[:, slot * LANES : (slot + 1) * LANES]
        to_right[rows + slot] = right[:, slot * LANES : (slot + 1) * LANES]


def joined_columns(ref, rows):
    slots = [ref[slot].astype(jnp.float32) for slot in range(rows, ref.shape[0])]
    parts = jnp.concatenate(slots, axis=1)
    return (parts[0:8] + parts[8:16]) + parts[16:24]


def tensor_kernel(
    intensity, temp, cure, below, from_left, from_right, below_left, below_right,
    xh, xl, zh, zl, sx, sz, out, window, across, filtered, grads, products,
):
    rows, width, depth = intensity.shape
    columns, cells, span_x, span_z, pad_x = sizes(width, depth)
    planes, depths = lax.axis_size("plane"), lax.axis_size("depth")
    plane, layer = lax.axis_index("plane"), lax.axis_index("depth")

    for row in range(rows):
        half = (row % 2) * depth
        window[row // 2, 0:EDGE, half : half + depth] = from_left[row]
        window[row // 2, EDGE : EDGE + width, half : half + depth] = (
            intensity[row].astype(jnp.float32).astype(jnp.bfloat16)
        )
        window[row // 2, EDGE + width :, half : half + depth] = from_right[row]
    for pair in range(2):
        half = pair * depth
        window[rows // 2, 0:EDGE, half : half + depth] = below_left[pair]
        window[rows // 2, EDGE : EDGE + width, half : half + depth] = below[pair]
        window[rows // 2, EDGE + width :, half : half + depth] = below_right[pair]

    for pair in range(rows // 2 + 1):
        values = window[pair]
        result = jnp.dot(xh[...], values, preferred_element_type=jnp.float32) + jnp.dot(
            xl[...], values, preferred_element_type=jnp.float32
        )
        across[2 * pair] = result[:, :depth]
        across[2 * pair + 1] = result[:, depth:]

    smooth, slope = smooth_taps(R1, sigma_grad), slope_taps(R1, sigma_grad)

    def along_rows(taps, values, row):
        total = None
        for source in range(rows):
            offset = source - row
            tap = float(taps[offset + R1]) if abs(offset) <= R1 else 0.0
            if tap != 0.0:
                term = tap * values[source]
                total = term if total is None else total + term
        return total

    def filter_rows(group, carry):
        start = pl.multiple_of(group * 16, 16)
        for tile in range(2):
            kinds = []
            for kind in range(2):
                place = pl.ds(kind * pad_x + start, 16)
                if tile == 0:
                    kinds.append([across[row, place, :] for row in range(rows)])
                else:
                    packed = [across[rows + pair, place, :] for pair in range(2)]
                    kinds.append(
                        [
                            packed[row % 2]
                            if row < 2
                            else pltpu.roll(packed[row % 2], depth - EDGE * (row // 2), 1)
                            for row in range(rows)
                        ]
                    )
            flat, steep = kinds
            lanes = pl.ds(tile * depth, depth)
            for row in range(rows):
                target = (row, pl.ds(start, 16), lanes)
                filtered[(0,) + target] = along_rows(slope, flat, row).astype(jnp.bfloat16)
                filtered[(1,) + target] = along_rows(smooth, steep, row).astype(jnp.bfloat16)
                filtered[(2,) + target] = along_rows(smooth, flat, row).astype(jnp.bfloat16)
        return carry

    lax.fori_loop(0, pad_x // 16, filter_rows, 0)

    for kind in range(3):
        band = 1 if kind == 2 else 0
        for row in range(rows):
            values = filtered[kind, row]
            grads[kind, row] = jnp.dot(
                values, zh[band], preferred_element_type=jnp.float32
            ) + jnp.dot(values, zl[band], preferred_element_type=jnp.float32)

    weights = row_weights(rows, R2, sigma_tensor) / (255.0 * 255.0)
    pairs = ((0, 0), (1, 1), (2, 2), (0, 1), (0, 2), (1, 2))

    def multiply(group, carry):
        start = pl.multiple_of(group * 16, 16)
        for tile in range(2):
            place = (pl.ds(start, 16), pl.ds(tile * LANES, LANES))
            x_at = plane * width - HALO * COARSE - R2 + start
            x_at = x_at + lax.broadcasted_iota(jnp.int32, (16, LANES), 0)
            z_at = layer * depth - BEFORE * COARSE - R2 + tile * LANES
            z_at = z_at + lax.broadcasted_iota(jnp.int32, (16, LANES), 1)
            inside = (x_at >= 0) & (x_at < planes * width) & (z_at >= 0) & (z_at < depths * depth)
            inside = jnp.where(inside, 1.0, 0.0)
            totals = [None] * 6
            for row in range(rows):
                three = [grads[(kind, row) + place] for kind in range(3)]
                weighted = [float(weights[row]) * value for value in three]
                for index, (first, second) in enumerate(pairs):
                    term = weighted[first] * three[second]
                    totals[index] = term if row == 0 else totals[index] + term
            for index in range(6):
                products[(index,) + place] = (totals[index] * inside).astype(jnp.bfloat16)
        return carry

    lax.fori_loop(0, pad_x // 16, multiply, 0)

    sums = []
    for index in range(6):
        if index in (3, 4):
            continue
        part = jnp.dot(products[index], sz[...], preferred_element_type=jnp.float32)
        sums.append(jnp.dot(sx[...], part.astype(jnp.bfloat16), preferred_element_type=jnp.float32))
    trace = sums[0] + sums[1] + sums[2]
    scale = (conduct_fiber - conduct_matrix) / (2.0 * trace + tensor_eps)
    xx = conduct_matrix + scale * (trace - sums[1])
    xz = -scale * sums[3]
    zz = conduct_matrix + scale * (trace - sums[2])
    lane = lax.broadcasted_iota(jnp.int32, xx.shape, 1)
    joined = jnp.where(
        lane < cells,
        xx,
        jnp.where(lane < 2 * cells, pltpu.roll(xz, cells, 1), pltpu.roll(zz, 2 * cells, 1)),
    )

    count = temp.shape[0]
    lanes = temp.shape[1]
    pad = jnp.zeros((8 - 2 * GHOST, lanes), jnp.float32)
    own_first = jnp.concatenate([temp[0:GHOST, :], cure[0:GHOST, :], pad], axis=0)
    own_last = jnp.concatenate([temp[count - GHOST :, :], cure[count - GHOST :, :], pad], axis=0)
    left, right = joined_columns(from_left, rows), joined_columns(from_right, rows)
    height = count + 2 * HALO
    for target in range(out.shape[0]):
        piece = jnp.where(layer == target - 1, own_last, 0.0)
        piece = jnp.where(layer == target + 1, own_first, piece)
        if target == 0:
            piece = jnp.where(layer == depths - 1, left, piece)
        if target == out.shape[0] - 1:
            piece = jnp.where(layer == 0, right, piece)
        out[target, 0:height, 0:LANES] = joined[count * target : count * target + height]
        if lanes > LANES:
            out[target, 0:height, LANES:] = jnp.zeros((height, lanes - LANES), jnp.float32)
        out[target, height : height + 2 * GHOST, :] = piece[0 : 2 * GHOST]
        spare = out.shape[1] - height - 2 * GHOST
        if spare:
            out[target, height + 2 * GHOST :, :] = jnp.zeros((spare, lanes), jnp.float32)


def cure_kernel(cells, chunks, temp_in, cure_in, levels, plan, temp_out, cure_out, conduct_out):
    count, lanes = temp_in.shape
    parts = chunks.shape[0]
    planes, depths = lax.axis_size("plane"), lax.axis_size("depth")
    plane, layer = lax.axis_index("plane"), lax.axis_index("depth")
    height = count + 2 * HALO
    own = cells - BEFORE
    lane = lax.broadcasted_iota(jnp.int32, (16, lanes), 1)
    row = lax.broadcasted_iota(jnp.int32, (16, lanes), 0)

    conduct = [jnp.zeros((16, lanes), jnp.float32) for _ in range(3)]
    for part in range(parts):
        chunk = chunks[part, 0:16, :]
        here = lane >= own * part - BEFORE
        for kind in range(3):
            shift = (own * part - BEFORE - kind * cells) % lanes
            moved = chunk if shift == 0 else pltpu.roll(chunk, shift, 1)
            conduct[kind] = jnp.where(here, moved, conduct[kind])
    for kind in range(3):
        conduct_out[kind] = conduct[kind][HALO : HALO + count]

    before = chunks[lax.rem(layer + parts - 1, parts)][height : height + 2 * GHOST]
    after = chunks[lax.rem(layer + 1, parts)][height : height + 2 * GHOST]
    spare = jnp.full((16 - count - 2 * GHOST, lanes), 0.5, jnp.float32)
    temp = jnp.concatenate([before[:GHOST], temp_in[...], after[:GHOST], 8.0 * spare], axis=0)
    cure = jnp.concatenate([before[GHOST:], cure_in[...], after[GHOST:], spare], axis=0)
    gap = GHOST - HALO
    xx, xz, zz = [pltpu.roll(part, gap, 0) for part in conduct]

    first = (plane == 0) & (layer == 0)
    last = (plane == planes - 1) & (layer == depths - 1)
    for step in range(STEPS):
        top, bottom = levels[plan[step, 0]], levels[plan[step, 1]]
        temp = jnp.where((row < GHOST) & first, temp[GHOST : GHOST + 1], temp)
        temp = jnp.where(
            (row >= GHOST + count) & last, temp[GHOST + count - 1 : GHOST + count], temp
        )
        cooler = jnp.where(lane == 0, top, pltpu.roll(temp, 1, 1))
        later = jnp.where(lane == lanes - 1, bottom, pltpu.roll(temp, lanes - 1, 1))
        slant = later - cooler
        second_x = pltpu.roll(temp, 15, 0) - 2.0 * temp + pltpu.roll(temp, 1, 0)
        second_z = later - 2.0 * temp + cooler
        cross = 0.25 * (pltpu.roll(slant, 15, 0) - pltpu.roll(slant, 1, 0))
        spread = xx * second_x + 2.0 * xz * cross + zz * second_z
        inverse = 1.0 / reference_temp - 1.0 / temp
        left = 1.0 - cure
        rate = rate_first * jnp.exp(energy_first * inverse) + rate_second * jnp.exp(
            energy_second * inverse
        ) * jnp.sqrt(cure)
        rate = rate * (left * jnp.sqrt(left))
        temp = temp + time_step * (spread + heat_release * rate)
        cure = cure + time_step * rate
    temp_out[...] = temp[GHOST : GHOST + count]
    cure_out[...] = cure[GHOST : GHOST + count]


def on_device(intensity, temp_start, cure_start, tool_levels, plan):
    rows, width, depth = intensity.shape
    count, lanes = temp_start.shape
    planes, depths = lax.axis_size("plane"), lax.axis_size("depth")
    columns, cells, span_x, span_z, pad_x = sizes(width, depth)
    bf16 = jnp.bfloat16
    slots = rows + lanes // LANES
    params = pltpu.CompilerParams(vmem_limit_bytes=48 * 1024 * 1024)

    up, to_left, to_right, up_left, up_right = pl.pallas_call(
        pack_kernel,
        name="pack",
        out_shape=(
            jax.ShapeDtypeStruct((2, width, depth), bf16),
            jax.ShapeDtypeStruct((slots, EDGE, depth), bf16),
            jax.ShapeDtypeStruct((slots, EDGE, depth), bf16),
            jax.ShapeDtypeStruct((2, EDGE, depth), bf16),
            jax.ShapeDtypeStruct((2, EDGE, depth), bf16),
        ),
        compiler_params=params,
    )(intensity, temp_start, cure_start)

    def shifted(values, by_plane, by_depth):
        pairs = []
        for p in range(planes):
            for d in range(depths):
                q, e = p + by_plane, d + by_depth
                if 0 <= q < planes and 0 <= e < depths:
                    pairs.append((p * depths + d, q * depths + e))
        return lax.ppermute(values, ("plane", "depth"), pairs)

    from_left = shifted(to_right, 1, 0)
    from_right = shifted(to_left, -1, 0)
    below = shifted(up, 0, 1)
    below_left = shifted(up_right, 1, 1)
    below_right = shifted(up_left, -1, 1)

    xh, xl = halves(x_bands(width, depth))
    zh, zl = halves(z_bands(width, depth))
    sx, _ = halves(coarse_bands(columns, pad_x, -(-columns // 16) * 16).T)
    sz, _ = halves(coarse_bands(cells, 2 * LANES, LANES))
    height = -(-(count + 2 * HALO + 2 * GHOST) // 8) * 8
    chunks = pl.pallas_call(
        tensor_kernel,
        name="tensor",
        out_shape=jax.ShapeDtypeStruct((depths, height, lanes), jnp.float32),
        scratch_shapes=[
            pltpu.VMEM((rows // 2 + 1, width + 2 * EDGE, 2 * depth), bf16),
            pltpu.VMEM((rows + 2, 2 * pad_x, depth), jnp.float32),
            pltpu.VMEM((3, rows, pad_x, 2 * LANES), bf16),
            pltpu.VMEM((3, rows, pad_x, 2 * LANES), jnp.float32),
            pltpu.VMEM((6, pad_x, 2 * LANES), bf16),
        ],
        compiler_params=params,
    )(
        intensity, temp_start, cure_start, below, from_left, from_right, below_left, below_right,
        *[jnp.asarray(part) for part in (xh, xl, zh, zl, sx, sz)],
    )

    chunks = lax.all_to_all(chunks, "depth", split_axis=0, concat_axis=0, tiled=True)

    vmem = pl.BlockSpec(memory_space=pltpu.VMEM)
    smem = pl.BlockSpec(memory_space=pltpu.SMEM)
    return pl.pallas_call(
        functools.partial(cure_kernel, cells),
        name="cure",
        out_shape=(
            jax.ShapeDtypeStruct((count, lanes), jnp.float32),
            jax.ShapeDtypeStruct((count, lanes), jnp.float32),
            jax.ShapeDtypeStruct((3, count, lanes), jnp.float32),
        ),
        in_specs=[vmem, vmem, vmem, smem, smem],
        out_specs=(vmem, vmem, vmem),
        compiler_params=params,
    )(chunks, temp_start, cure_start, tool_levels, plan)


def solution(mesh):
    return jax.shard_map(
        on_device,
        mesh=mesh,
        in_specs=(
            P(None, "plane", "depth"),
            P(("plane", "depth"), None),
            P(("plane", "depth"), None),
            P(),
            P(),
        ),
        out_specs=(
            P(("plane", "depth"), None),
            P(("plane", "depth"), None),
            P(None, ("plane", "depth"), None),
        ),
        check_vma=False,
    )
```

```python
import functools

import jax
import jax.numpy as jnp
import ml_dtypes
import numpy as np
from jax import lax
from jax.experimental import pallas as pl
from jax.experimental.pallas import tpu as pltpu
from jax.sharding import PartitionSpec as P

ROWS = 8
R1 = 6
R2 = 10
COARSE = 4
STEPS = 3

sigma_grad = 2.0
sigma_tensor = 3.3
conduct_matrix = 0.3
conduct_fiber = 1.5
time_step = 0.25
heat_release = 0.4
rate_first = 0.15
rate_second = 0.6
energy_first = 30.0
energy_second = 25.0
reference_temp = 4.2
tensor_eps = 1e-06

EDGE = 32
RIM = R1 + R2
LANES = 128
HALO = 2
GHOST = 3
BEFORE = EDGE // 2 // COARSE
FIRST = 16
ROW_KINDS = (1, 0, 0)
X_KINDS = (0, 1, 0)
DEPTH_KINDS = (0, 0, 1)


def smooth_taps(radius, sigma):
    offsets = np.arange(-radius, radius + 1) * 1.0
    weights = np.exp(-0.5 * offsets * offsets / (sigma * sigma))
    return weights / weights.sum()


def slope_taps(radius, sigma):
    offsets = np.arange(-radius, radius + 1) * 1.0
    weights = np.exp(-0.5 * offsets * offsets / (sigma * sigma))
    return offsets * weights / np.sum(offsets * offsets * weights)


def row_weights(count, radius, sigma):
    taps = smooth_taps(radius, sigma)
    result = np.zeros(count)
    for source in range(count):
        for target in range(count):
            offset = target - source
            if abs(offset) <= radius:
                result[source] += taps[offset + radius]
    return result


def rounded(taps):
    best = None
    for factor in np.linspace(1.0, 2.0, 20001)[:-1]:
        near = (taps * factor).astype(np.float32).astype(ml_dtypes.bfloat16).astype(np.float64)
        error = np.abs(near / factor - taps).sum()
        if best is None or error < best[0]:
            best = (error, near, factor)
    return best[1], best[2]


def as_bfloat16(matrix):
    return matrix.astype(np.float32).astype(ml_dtypes.bfloat16)


def sizes(width, depth):
    columns = width // COARSE + 2 * HALO
    cells = depth // COARSE + BEFORE
    span_x = columns * COARSE + 2 * R2
    pad_x = -(-span_x // 16) * 16
    return columns, cells, span_x, pad_x


GRAD_TAPS = tuple(
    rounded(taps(R1, sigma_grad)) for taps in (smooth_taps, slope_taps)
)
GRAD_FACTOR = GRAD_TAPS[0][1] ** 2 * GRAD_TAPS[1][1]


def grad_taps(kind):
    return GRAD_TAPS[kind][0]


def tap(taps, offset):
    radius = (len(taps) - 1) // 2
    return float(taps[offset + radius]) if abs(offset) <= radius else 0.0


def x_bands(width, depth):
    columns, cells, span_x, pad_x = sizes(width, depth)
    bands = np.zeros((2, pad_x, width + 2 * EDGE))
    first = EDGE - HALO * COARSE - R2 - R1
    for kind in range(2):
        for out in range(span_x):
            bands[kind, out, out + first : out + first + 2 * R1 + 1] = grad_taps(kind)
    return bands.reshape(2 * pad_x, -1)


def packed_lane(row, place):
    return (row % 2) * LANES + (row // 2) * EDGE + EDGE + place


def row_bands(rows, size):
    lane = packed_lane if size == EDGE else lambda row, place: row * size + place + EDGE
    bands = np.zeros((2, rows * size, rows * size))
    for kind in range(2):
        for source in range(rows):
            for target in range(rows):
                for place in range(-EDGE, size - EDGE):
                    at = (lane(source, place), lane(target, place))
                    bands[kind][at] = tap(grad_taps(kind), source - target)
    return bands


def low_bands(rows):
    bands = np.zeros((2, 3 * LANES, 2 * LANES))
    for kind in range(2):
        for row in range(rows):
            for place in range(-BEFORE * COARSE - R2, 0):
                for near in range(place - R1, place + R1 + 1):
                    own = 2 * LANES + row * FIRST + near
                    lane = packed_lane(row, near) if near < 0 else own
                    value = tap(grad_taps(kind), near - place)
                    bands[kind, lane, packed_lane(row, place)] = value
    return bands


def depth_bands(rows, depth):
    bands = np.zeros((2, rows // 2, 2 * LANES, LANES))
    for kind in range(2):
        for place in range(depth):
            for near in range(place - R1, min(place + R1 + 1, depth)):
                value = tap(grad_taps(kind), near - place)
                for block in range(rows // 2):
                    lane = near if near >= 0 else LANES + packed_lane(2 * block, near)
                    bands[kind, block, lane, place] = value
    return bands


def product_weights(rows):
    return row_weights(rows, R2, sigma_tensor) / (255.0 * GRAD_FACTOR) ** 2


def coarse_depth_bands(rows, depth):
    taps = smooth_taps(R2, sigma_tensor)
    weights = product_weights(rows)
    columns, cells, span_x, pad_x = sizes(0, depth)
    bands = np.zeros((3 * LANES, LANES))
    for cell in range(cells):
        for voxel in range(COARSE):
            place = (cell - BEFORE) * COARSE + voxel
            for near in range(place - R2, min(place + R2 + 1, depth)):
                value = tap(taps, near - place)
                if near >= 0:
                    bands[near, cell] += value
                else:
                    for row in range(rows):
                        bands[LANES + packed_lane(row, near), cell] += weights[row] * value
    return bands


def coarse_x_bands(count, padded_in, padded_out):
    taps = smooth_taps(R2, sigma_tensor)
    bands = np.zeros((padded_out, padded_in))
    for cell in range(count):
        for voxel in range(COARSE):
            start = cell * COARSE + voxel
            bands[cell, start : start + 2 * R2 + 1] += taps
    return bands


def three_parts(values):
    high = values.astype(jnp.bfloat16).astype(jnp.float32)
    rest = values - high
    middle = rest.astype(jnp.bfloat16).astype(jnp.float32)
    return high, middle, (rest - middle).astype(jnp.bfloat16).astype(jnp.float32)


def column_slot(temp_ref, cure_ref, first):
    pad = jnp.zeros((8 - 2 * GHOST, temp_ref.shape[1]), jnp.float32)
    rows = pl.ds(first, GHOST)
    both = jnp.concatenate([temp_ref[rows, :], cure_ref[rows, :], pad], axis=0)
    high, middle, low = three_parts(both)
    return jnp.concatenate([high, middle, low, jnp.zeros_like(high)], axis=0).astype(jnp.bfloat16)


def pack_kernel(intensity, temp_hbm, cure_hbm, to_left, to_right, own, grey, temp, cure, sems):
    rows, width, depth = intensity.shape
    copies = [
        pltpu.make_async_copy(intensity, grey, sems.at[0]),
        pltpu.make_async_copy(temp_hbm, temp, sems.at[1]),
        pltpu.make_async_copy(cure_hbm, cure, sems.at[2]),
    ]
    for copy in copies:
        copy.start()
    for copy in copies:
        copy.wait()
    for row in range(rows):
        values = grey[row].astype(jnp.float32).astype(jnp.bfloat16)
        own[row] = values
        to_left[row] = values[:EDGE]
        to_right[row] = values[width - EDGE :]
    count = temp.shape[0]
    left, right = column_slot(temp, cure, 0), column_slot(temp, cure, count - GHOST)
    for slot in range(temp.shape[1] // LANES):
        to_left[rows + slot] = left[:, slot * LANES : (slot + 1) * LANES]
        to_right[rows + slot] = right[:, slot * LANES : (slot + 1) * LANES]


def packed_rows(values, size, first):
    depth = values[0].shape[1]
    lane = lax.broadcasted_iota(jnp.int32, values[0].shape, 1)
    packed = None
    for block, value in enumerate(values):
        shift = (size * block - first) % depth
        moved = value if shift == 0 else pltpu.roll(value, shift, 1)
        packed = moved if block == 0 else jnp.where(lane >= size * block, moved, packed)
    return packed


def window_kernel(own, from_left, from_right, window, up):
    rows, width, depth = own.shape
    values = []
    for row in range(rows):
        half = (row % 2) * depth
        whole = jnp.concatenate([from_left[row], own[row], from_right[row]], axis=0)
        window[row // 2, :, half : half + depth] = whole
        values.append(whole.astype(jnp.float32))
    for pair in range(2):
        up[pair] = packed_rows(values[pair::2], EDGE, depth - EDGE).astype(jnp.bfloat16)


def joined_columns(ref, rows):
    slots = [ref[slot].astype(jnp.float32) for slot in range(rows, ref.shape[0])]
    parts = jnp.concatenate(slots, axis=1)
    return (parts[0:8] + parts[8:16]) + parts[16:24]


def product(first, second):
    return jnp.dot(first, second, preferred_element_type=jnp.float32)


def along_rows(kind, values, row):
    total = None
    for source, value in enumerate(values):
        weight = tap(grad_taps(kind), source - row)
        if weight != 0.0:
            total = weight * value if total is None else total + weight * value
    return total


def own_kernel(window, x_parts, filtered, first_flat, first_steep, across):
    pairs, height, double = window.shape
    rows, depth = 2 * pairs, double // 2
    pad_x = x_parts.shape[0] // 2
    for pair in range(pairs):
        result = product(x_parts[...], window[pair])
        across[2 * pair] = result[:, :depth]
        across[2 * pair + 1] = result[:, depth:]

    values = [
        window[row // 2, :, (row % 2) * depth : (row % 2 + 1) * depth].astype(jnp.float32)
        for row in range(rows)
    ]
    result = product(x_parts[...], packed_rows(values, FIRST, 0).astype(jnp.bfloat16))
    first_flat[...] = result[:pad_x].astype(jnp.bfloat16)
    first_steep[...] = result[pad_x:].astype(jnp.bfloat16)

    def filter_rows(group, carry):
        start = pl.multiple_of(group * 16, 16)
        kinds = [
            [across[row, pl.ds(kind * pad_x + start, 16), :] for row in range(rows)]
            for kind in range(2)
        ]
        for part in range(3):
            for row in range(rows):
                result = along_rows(ROW_KINDS[part], kinds[X_KINDS[part]], row)
                filtered[part, row, pl.ds(start, 16), :] = result.astype(jnp.bfloat16)
        return carry

    lax.fori_loop(0, pad_x // 16, filter_rows, 0)


def tensor_kernel(
    width, temp, cure, below, from_left, from_right, filtered, first_flat, first_steep,
    x_parts, wide, narrow, sx, out, grads, low, products,
):
    parts, rows, pad_x, depth = filtered.shape
    columns, cells, span_x, pad_x = sizes(width, depth)
    planes, depths = lax.axis_size("plane"), lax.axis_size("depth")
    plane, layer = lax.axis_index("plane"), lax.axis_index("depth")

    edge = jnp.concatenate([below[0], below[1]], axis=1)
    result = product(x_parts[...], edge).astype(jnp.bfloat16)
    kinds = (result[:pad_x], result[pad_x:])
    firsts = (first_flat[...], first_steep[...])
    at_first = rows * 2 * LANES + 3 * LANES
    for part in range(3):
        kind, row_kind, depth_kind = X_KINDS[part], ROW_KINDS[part], DEPTH_KINDS[part]
        at = 5 * LANES * row_kind
        edge_rows = product(kinds[kind], wide[at : at + 2 * LANES, :]).astype(jnp.bfloat16)
        at = at_first + row_kind * LANES
        first_rows = product(firsts[kind], narrow[at : at + LANES, :]).astype(jnp.bfloat16)
        at = 5 * LANES * depth_kind + 2 * LANES
        both = jnp.concatenate([edge_rows, first_rows], axis=1)
        low[part] = product(both, wide[at : at + 3 * LANES, :])
        for row in range(rows):
            half = (row % 2) * LANES
            both = jnp.concatenate(
                [filtered[part, row], edge_rows[:, half : half + LANES]], axis=1
            )
            at = (depth_kind * (rows // 2) + row // 2) * 2 * LANES
            grads[part, row] = product(both, narrow[at : at + 2 * LANES, :])

    weights = product_weights(rows)
    pairs = ((0, 0), (1, 1), (2, 2), (0, 1), (0, 2), (1, 2))
    has_below = jnp.where(layer > 0, 1.0, 0.0)

    def multiply(group, carry):
        start = pl.multiple_of(group * 16, 16)
        x_at = plane * width - HALO * COARSE - R2 + start
        x_at = x_at + lax.broadcasted_iota(jnp.int32, (16, LANES), 0)
        inside = jnp.where((x_at >= 0) & (x_at < planes * width), 1.0, 0.0)
        place = pl.ds(start, 16)
        totals = [None] * 6
        for row in range(rows):
            three = [grads[part, row, place, :] for part in range(3)]
            weighted = [float(weights[row]) * value for value in three]
            for index, (first, second) in enumerate(pairs):
                term = weighted[first] * three[second]
                totals[index] = term if row == 0 else totals[index] + term
        for index in range(6):
            products[index, place, 0:LANES] = (totals[index] * inside).astype(jnp.bfloat16)
        inside = inside * has_below
        for tile in range(2):
            lanes = slice(tile * LANES, (tile + 1) * LANES)
            three = [low[part, place, lanes] for part in range(3)]
            masked = [value * inside for value in three]
            for index, (first, second) in enumerate(pairs):
                term = masked[first] * three[second]
                products[index, place, LANES + tile * LANES : 2 * LANES + tile * LANES] = (
                    term.astype(jnp.bfloat16)
                )
        return carry

    lax.fori_loop(0, pad_x // 16, multiply, 0)

    coarse = narrow[rows * 2 * LANES : rows * 2 * LANES + 3 * LANES, :]
    sums = []
    for index in range(6):
        part = product(products[index], coarse).astype(jnp.bfloat16)
        sums.append(product(sx[...], part))
    trace = sums[0] + sums[1] + sums[2]
    scale = (conduct_fiber - conduct_matrix) / (2.0 * trace + tensor_eps)
    xx = conduct_matrix + scale * (trace - sums[1])
    xz = -scale * sums[5]
    zz = conduct_matrix + scale * (trace - sums[2])
    lane = lax.broadcasted_iota(jnp.int32, xx.shape, 1)
    joined = jnp.where(
        lane < cells,
        xx,
        jnp.where(lane < 2 * cells, pltpu.roll(xz, cells, 1), pltpu.roll(zz, 2 * cells, 1)),
    )

    count = temp.shape[0]
    lanes = temp.shape[1]
    pad = jnp.zeros((8 - 2 * GHOST, lanes), jnp.float32)
    own_first = jnp.concatenate([temp[0:GHOST, :], cure[0:GHOST, :], pad], axis=0)
    own_last = jnp.concatenate([temp[count - GHOST :, :], cure[count - GHOST :, :], pad], axis=0)
    left, right = joined_columns(from_left, rows), joined_columns(from_right, rows)
    height = count + 2 * HALO
    for target in range(out.shape[0]):
        piece = jnp.where(layer == target - 1, own_last, 0.0)
        piece = jnp.where(layer == target + 1, own_first, piece)
        if target == 0:
            piece = jnp.where(layer == depths - 1, left, piece)
        if target == out.shape[0] - 1:
            piece = jnp.where(layer == 0, right, piece)
        out[target, 0:height, 0:LANES] = joined[count * target : count * target + height]
        if lanes > LANES:
            out[target, 0:height, LANES:] = jnp.zeros((height, lanes - LANES), jnp.float32)
        out[target, height : height + 2 * GHOST, :] = piece[0 : 2 * GHOST]
        spare = out.shape[1] - height - 2 * GHOST
        if spare:
            out[target, height + 2 * GHOST :, :] = jnp.zeros((spare, lanes), jnp.float32)


def cure_kernel(cells, chunks, temp_in, cure_in, levels, plan, temp_out, cure_out, conduct_out):
    count, lanes = temp_in.shape
    parts = chunks.shape[0]
    planes, depths = lax.axis_size("plane"), lax.axis_size("depth")
    plane, layer = lax.axis_index("plane"), lax.axis_index("depth")
    height = count + 2 * HALO
    own = cells - BEFORE
    lane = lax.broadcasted_iota(jnp.int32, (16, lanes), 1)
    row = lax.broadcasted_iota(jnp.int32, (16, lanes), 0)

    conduct = [jnp.zeros((16, lanes), jnp.float32) for _ in range(3)]
    for part in range(parts):
        chunk = chunks[part, 0:16, :]
        here = lane >= own * part - BEFORE
        for kind in range(3):
            shift = (own * part - BEFORE - kind * cells) % lanes
            moved = chunk if shift == 0 else pltpu.roll(chunk, shift, 1)
            conduct[kind] = jnp.where(here, moved, conduct[kind])
    for kind in range(3):
        conduct_out[kind] = conduct[kind][HALO : HALO + count]

    before = chunks[lax.rem(layer + parts - 1, parts)][height : height + 2 * GHOST]
    after = chunks[lax.rem(layer + 1, parts)][height : height + 2 * GHOST]
    spare = jnp.full((16 - count - 2 * GHOST, lanes), 0.5, jnp.float32)
    temp = jnp.concatenate([before[:GHOST], temp_in[...], after[:GHOST], 8.0 * spare], axis=0)
    cure = jnp.concatenate([before[GHOST:], cure_in[...], after[GHOST:], spare], axis=0)
    gap = GHOST - HALO
    xx, xz, zz = [pltpu.roll(part, gap, 0) for part in conduct]

    first = (plane == 0) & (layer == 0)
    last = (plane == planes - 1) & (layer == depths - 1)
    for step in range(STEPS):
        top, bottom = levels[plan[step, 0]], levels[plan[step, 1]]
        temp = jnp.where((row < GHOST) & first, temp[GHOST : GHOST + 1], temp)
        temp = jnp.where(
            (row >= GHOST + count) & last, temp[GHOST + count - 1 : GHOST + count], temp
        )
        cooler = jnp.where(lane == 0, top, pltpu.roll(temp, 1, 1))
        later = jnp.where(lane == lanes - 1, bottom, pltpu.roll(temp, lanes - 1, 1))
        slant = later - cooler
        second_x = pltpu.roll(temp, 15, 0) - 2.0 * temp + pltpu.roll(temp, 1, 0)
        second_z = later - 2.0 * temp + cooler
        cross = 0.25 * (pltpu.roll(slant, 15, 0) - pltpu.roll(slant, 1, 0))
        spread = xx * second_x + 2.0 * xz * cross + zz * second_z
        inverse = 1.0 / reference_temp - 1.0 / temp
        left = 1.0 - cure
        rate = rate_first * jnp.exp(energy_first * inverse) + rate_second * jnp.exp(
            energy_second * inverse
        ) * jnp.sqrt(cure)
        rate = rate * (left * jnp.sqrt(left))
        temp = temp + time_step * (spread + heat_release * rate)
        cure = cure + time_step * rate
    temp_out[...] = temp[GHOST : GHOST + count]
    cure_out[...] = cure[GHOST : GHOST + count]


def on_device(intensity, temp_start, cure_start, tool_levels, plan):
    rows, width, depth = intensity.shape
    count, lanes = temp_start.shape
    planes, depths = lax.axis_size("plane"), lax.axis_size("depth")
    columns, cells, span_x, pad_x = sizes(width, depth)
    bf16 = jnp.bfloat16
    slots = rows + lanes // LANES
    params = pltpu.CompilerParams(vmem_limit_bytes=24 * 1024 * 1024)
    vmem = pl.BlockSpec(memory_space=pltpu.VMEM)
    smem = pl.BlockSpec(memory_space=pltpu.SMEM)
    stay = pl.BlockSpec(memory_space=pltpu.HBM)

    to_left, to_right, own = pl.pallas_call(
        pack_kernel,
        name="pack",
        out_shape=(
            jax.ShapeDtypeStruct((slots, EDGE, depth), bf16),
            jax.ShapeDtypeStruct((slots, EDGE, depth), bf16),
            jax.ShapeDtypeStruct((rows, width, depth), bf16),
        ),
        in_specs=[stay, stay, stay],
        scratch_shapes=[
            pltpu.VMEM((rows, width, depth), jnp.int32),
            pltpu.VMEM((count, lanes), jnp.float32),
            pltpu.VMEM((count, lanes), jnp.float32),
            pltpu.SemaphoreType.DMA((3,)),
        ],
        compiler_params=params,
    )(*[pltpu.with_memory_space_constraint(x, pltpu.HBM) for x in (intensity, temp_start, cure_start)])

    def shifted(values, by_plane, by_depth):
        pairs = []
        for p in range(planes):
            for d in range(depths):
                q, e = p + by_plane, d + by_depth
                if 0 <= q < planes and 0 <= e < depths:
                    pairs.append((p * depths + d, q * depths + e))
        return lax.ppermute(values, ("plane", "depth"), pairs)

    from_left = shifted(to_right, 1, 0)
    from_right = shifted(to_left, -1, 0)

    span = width + 2 * EDGE
    window, up = pl.pallas_call(
        window_kernel,
        name="window",
        out_shape=(
            jax.ShapeDtypeStruct((rows // 2, span, 2 * depth), bf16),
            jax.ShapeDtypeStruct((2, span, depth), bf16),
        ),
        compiler_params=params,
    )(own, from_left, from_right)
    below = shifted(up, 0, 1)

    x_parts = jnp.asarray(as_bfloat16(x_bands(width, depth)))
    filtered, first_flat, first_steep = pl.pallas_call(
        own_kernel,
        name="own",
        out_shape=(
            jax.ShapeDtypeStruct((3, rows, pad_x, depth), bf16),
            jax.ShapeDtypeStruct((pad_x, depth), bf16),
            jax.ShapeDtypeStruct((pad_x, depth), bf16),
        ),
        scratch_shapes=[pltpu.VMEM((rows, 2 * pad_x, depth), jnp.float32)],
        cost_estimate=pl.CostEstimate(
            flops=2 * rows * 2 * pad_x * span * depth, bytes_accessed=4_000_000, transcendentals=0
        ),
        compiler_params=params,
    )(window, x_parts)

    wide, narrow = [], [*depth_bands(rows, depth).reshape(rows, 2 * LANES, LANES)]
    for edge_rows, low in zip(row_bands(rows, EDGE), low_bands(rows)):
        wide += [edge_rows, low]
    narrow += [coarse_depth_bands(rows, depth), *row_bands(rows, FIRST)]
    wide, narrow = [jnp.asarray(as_bfloat16(np.concatenate(bands))) for bands in (wide, narrow)]
    sx = jnp.asarray(as_bfloat16(coarse_x_bands(columns, pad_x, -(-columns // 16) * 16)))
    height = -(-(count + 2 * HALO + 2 * GHOST) // 8) * 8
    chunks = pl.pallas_call(
        functools.partial(tensor_kernel, width),
        name="tensor",
        out_shape=jax.ShapeDtypeStruct((depths, height, lanes), jnp.float32),
        scratch_shapes=[
            pltpu.VMEM((3, rows, pad_x, depth), jnp.float32),
            pltpu.VMEM((3, pad_x, 2 * LANES), jnp.float32),
            pltpu.VMEM((6, pad_x, 3 * LANES), bf16),
        ],
        compiler_params=params,
    )(
        temp_start, cure_start, below, from_left, from_right, filtered, first_flat, first_steep,
        x_parts, wide, narrow, sx,
    )

    chunks = lax.all_to_all(chunks, "depth", split_axis=0, concat_axis=0, tiled=True)

    return pl.pallas_call(
        functools.partial(cure_kernel, cells),
        name="cure",
        out_shape=(
            jax.ShapeDtypeStruct((count, lanes), jnp.float32),
            jax.ShapeDtypeStruct((count, lanes), jnp.float32),
            jax.ShapeDtypeStruct((3, count, lanes), jnp.float32),
        ),
        in_specs=[vmem, vmem, vmem, smem, smem],
        out_specs=(vmem, vmem, vmem),
        compiler_params=params,
    )(chunks, temp_start, cure_start, tool_levels, plan)


def solution(mesh):
    return jax.shard_map(
        on_device,
        mesh=mesh,
        in_specs=(
            P(None, "plane", "depth"),
            P(("plane", "depth"), None),
            P(("plane", "depth"), None),
            P(),
            P(),
        ),
        out_specs=(
            P(("plane", "depth"), None),
            P(("plane", "depth"), None),
            P(None, ("plane", "depth"), None),
        ),
        check_vma=False,
    )
```

```python
import functools

import jax
import jax.numpy as jnp
import ml_dtypes
import numpy as np
from jax import lax
from jax.experimental import pallas as pl
from jax.experimental.pallas import tpu as pltpu
from jax.sharding import PartitionSpec as P

ROWS = 8
R1 = 6
R2 = 10
COARSE = 4
STEPS = 3

sigma_grad = 2.0
sigma_tensor = 3.3
conduct_matrix = 0.3
conduct_fiber = 1.5
time_step = 0.25
heat_release = 0.4
rate_first = 0.15
rate_second = 0.6
energy_first = 30.0
energy_second = 25.0
reference_temp = 4.2
tensor_eps = 1e-06

EDGE = 32
RIM = R1 + R2
LANES = 128
HALO = 2
GHOST = 3
BEFORE = EDGE // 2 // COARSE
FIRST = 16
ROW_KINDS = (1, 0, 0)
X_KINDS = (0, 1, 0)
DEPTH_KINDS = (0, 0, 1)


def smooth_taps(radius, sigma):
    offsets = np.arange(-radius, radius + 1) * 1.0
    weights = np.exp(-0.5 * offsets * offsets / (sigma * sigma))
    return weights / weights.sum()


def slope_taps(radius, sigma):
    offsets = np.arange(-radius, radius + 1) * 1.0
    weights = np.exp(-0.5 * offsets * offsets / (sigma * sigma))
    return offsets * weights / np.sum(offsets * offsets * weights)


def row_weights(count, radius, sigma):
    taps = smooth_taps(radius, sigma)
    result = np.zeros(count)
    for source in range(count):
        for target in range(count):
            offset = target - source
            if abs(offset) <= radius:
                result[source] += taps[offset + radius]
    return result


def rounded(taps):
    best = None
    for factor in np.linspace(1.0, 2.0, 20001)[:-1]:
        near = (taps * factor).astype(np.float32).astype(ml_dtypes.bfloat16).astype(np.float64)
        error = np.abs(near / factor - taps).sum()
        if best is None or error < best[0]:
            best = (error, near, factor)
    return best[1], best[2]


def as_bfloat16(matrix):
    return matrix.astype(np.float32).astype(ml_dtypes.bfloat16)


def sizes(width, depth):
    columns = width // COARSE + 2 * HALO
    cells = depth // COARSE + BEFORE
    span_x = columns * COARSE + 2 * R2
    pad_x = -(-span_x // 16) * 16
    return columns, cells, span_x, pad_x


GRAD_TAPS = tuple(
    rounded(taps(R1, sigma_grad)) for taps in (smooth_taps, slope_taps)
)
GRAD_FACTOR = GRAD_TAPS[0][1] ** 2 * GRAD_TAPS[1][1]


def grad_taps(kind):
    return GRAD_TAPS[kind][0]


def tap(taps, offset):
    radius = (len(taps) - 1) // 2
    return float(taps[offset + radius]) if abs(offset) <= radius else 0.0


def x_bands(width, depth):
    columns, cells, span_x, pad_x = sizes(width, depth)
    bands = np.zeros((2, pad_x, width + 2 * EDGE))
    first = EDGE - HALO * COARSE - R2 - R1
    for kind in range(2):
        for out in range(span_x):
            bands[kind, out, out + first : out + first + 2 * R1 + 1] = grad_taps(kind)
    return bands.reshape(2 * pad_x, -1)


def packed_lane(row, place):
    return (row % 2) * LANES + (row // 2) * EDGE + EDGE + place


def row_bands(rows, size):
    lane = packed_lane if size == EDGE else lambda row, place: row * size + place + EDGE
    bands = np.zeros((2, rows * size, rows * size))
    for kind in range(2):
        for source in range(rows):
            for target in range(rows):
                for place in range(-EDGE, size - EDGE):
                    at = (lane(source, place), lane(target, place))
                    bands[kind][at] = tap(grad_taps(kind), source - target)
    return bands


def low_bands(rows):
    bands = np.zeros((2, 3 * LANES, 2 * LANES))
    for kind in range(2):
        for row in range(rows):
            for place in range(-BEFORE * COARSE - R2, 0):
                for near in range(place - R1, place + R1 + 1):
                    own = 2 * LANES + row * FIRST + near
                    lane = packed_lane(row, near) if near < 0 else own
                    value = tap(grad_taps(kind), near - place)
                    bands[kind, lane, packed_lane(row, place)] = value
    return bands


def depth_bands(rows, depth):
    bands = np.zeros((2, rows // 2, 2 * LANES, LANES))
    for kind in range(2):
        for place in range(depth):
            for near in range(place - R1, min(place + R1 + 1, depth)):
                value = tap(grad_taps(kind), near - place)
                for block in range(rows // 2):
                    lane = near if near >= 0 else LANES + packed_lane(2 * block, near)
                    bands[kind, block, lane, place] = value
    return bands


def product_weights(rows):
    return row_weights(rows, R2, sigma_tensor) / (255.0 * GRAD_FACTOR) ** 2


def coarse_depth_bands(rows, depth):
    taps = smooth_taps(R2, sigma_tensor)
    weights = product_weights(rows)
    columns, cells, span_x, pad_x = sizes(0, depth)
    bands = np.zeros((3 * LANES, LANES))
    for cell in range(cells):
        for voxel in range(COARSE):
            place = (cell - BEFORE) * COARSE + voxel
            for near in range(place - R2, min(place + R2 + 1, depth)):
                value = tap(taps, near - place)
                if near >= 0:
                    bands[near, cell] += value
                else:
                    for row in range(rows):
                        bands[LANES + packed_lane(row, near), cell] += weights[row] * value
    return bands


def coarse_x_bands(count, padded_in, padded_out):
    taps = smooth_taps(R2, sigma_tensor)
    bands = np.zeros((padded_out, padded_in))
    for cell in range(count):
        for voxel in range(COARSE):
            start = cell * COARSE + voxel
            bands[cell, start : start + 2 * R2 + 1] += taps
    return bands


def three_parts(values):
    high = values.astype(jnp.bfloat16).astype(jnp.float32)
    rest = values - high
    middle = rest.astype(jnp.bfloat16).astype(jnp.float32)
    return high, middle, (rest - middle).astype(jnp.bfloat16).astype(jnp.float32)


def column_slot(temp_ref, cure_ref, first):
    pad = jnp.zeros((8 - 2 * GHOST, temp_ref.shape[1]), jnp.float32)
    rows = pl.ds(first, GHOST)
    both = jnp.concatenate([temp_ref[rows, :], cure_ref[rows, :], pad], axis=0)
    high, middle, low = three_parts(both)
    return jnp.concatenate([high, middle, low, jnp.zeros_like(high)], axis=0).astype(jnp.bfloat16)


def is_odd():
    return lax.rem(lax.axis_index("plane"), 2) == 1


def pack_kernel(
    intensity, temp_hbm, cure_hbm, x_hbm, far, near, own, x_parts, grey, temp, cure, sems
):
    rows, width, depth = intensity.shape
    copies = [
        pltpu.make_async_copy(intensity, grey, sems.at[0]),
        pltpu.make_async_copy(temp_hbm, temp, sems.at[1]),
        pltpu.make_async_copy(cure_hbm, cure, sems.at[2]),
        pltpu.make_async_copy(x_hbm, x_parts, sems.at[3]),
    ]
    for copy in copies:
        copy.start()
    for copy in copies:
        copy.wait()
    odd = is_odd()
    count = temp.shape[0]
    sides = (column_slot(temp, cure, 0), column_slot(temp, cure, count - GHOST))

    def send(left, right):
        for row in range(rows):
            left[row] = grey[row, :EDGE, :].astype(jnp.float32).astype(jnp.bfloat16)
            right[row] = grey[row, width - EDGE :, :].astype(jnp.float32).astype(jnp.bfloat16)
        for slot in range(temp.shape[1] // LANES):
            left[rows + slot] = sides[0][:, slot * LANES : (slot + 1) * LANES]
            right[rows + slot] = sides[1][:, slot * LANES : (slot + 1) * LANES]

    @pl.when(odd)
    def _():
        send(near, far)

    @pl.when(jnp.logical_not(odd))
    def _():
        send(far, near)

    for row in range(rows):
        own[row] = grey[row].astype(jnp.float32).astype(jnp.bfloat16)


def packed_rows(values, size, first):
    depth = values[0].shape[1]
    lane = lax.broadcasted_iota(jnp.int32, values[0].shape, 1)
    packed = None
    for block, value in enumerate(values):
        shift = (size * block - first) % depth
        moved = value if shift == 0 else pltpu.roll(value, shift, 1)
        packed = moved if block == 0 else jnp.where(lane >= size * block, moved, packed)
    return packed


def window_kernel(own, far, near, window, up):
    rows, width, depth = own.shape
    odd = is_odd()

    def fill(from_left, from_right):
        values = []
        for row in range(rows):
            half = (row % 2) * depth
            whole = jnp.concatenate([from_left[row], own[row], from_right[row]], axis=0)
            window[row // 2, :, half : half + depth] = whole
            values.append(whole.astype(jnp.float32))
        for pair in range(2):
            up[pair] = packed_rows(values[pair::2], EDGE, depth - EDGE).astype(jnp.bfloat16)

    @pl.when(odd)
    def _():
        fill(near, far)

    @pl.when(jnp.logical_not(odd))
    def _():
        fill(far, near)


def joined_columns(ref, rows):
    slots = [ref[slot].astype(jnp.float32) for slot in range(rows, ref.shape[0])]
    parts = jnp.concatenate(slots, axis=1)
    return (parts[0:8] + parts[8:16]) + parts[16:24]


def product(first, second):
    return jnp.dot(first, second, preferred_element_type=jnp.float32)


def along_rows(kind, values, row):
    total = None
    for source, value in enumerate(values):
        weight = tap(grad_taps(kind), source - row)
        if weight != 0.0:
            total = weight * value if total is None else total + weight * value
    return total


def own_kernel(
    window, x_parts, wide_hbm, narrow_hbm, filtered, first_flat, first_steep, wide, narrow,
    across, sems,
):
    copies = [
        pltpu.make_async_copy(wide_hbm, wide, sems.at[0]),
        pltpu.make_async_copy(narrow_hbm, narrow, sems.at[1]),
    ]
    for copy in copies:
        copy.start()
    pairs, height, double = window.shape
    rows, depth = 2 * pairs, double // 2
    pad_x = x_parts.shape[0] // 2
    for pair in range(pairs):
        result = product(x_parts[...], window[pair])
        across[2 * pair] = result[:, :depth]
        across[2 * pair + 1] = result[:, depth:]

    values = [
        window[row // 2, :, (row % 2) * depth : (row % 2 + 1) * depth].astype(jnp.float32)
        for row in range(rows)
    ]
    result = product(x_parts[...], packed_rows(values, FIRST, 0).astype(jnp.bfloat16))
    first_flat[...] = result[:pad_x].astype(jnp.bfloat16)
    first_steep[...] = result[pad_x:].astype(jnp.bfloat16)

    def filter_rows(group, carry):
        start = pl.multiple_of(group * 16, 16)
        kinds = [
            [across[row, pl.ds(kind * pad_x + start, 16), :] for row in range(rows)]
            for kind in range(2)
        ]
        for part in range(3):
            for row in range(rows):
                result = along_rows(ROW_KINDS[part], kinds[X_KINDS[part]], row)
                filtered[part, row, pl.ds(start, 16), :] = result.astype(jnp.bfloat16)
        return carry

    lax.fori_loop(0, pad_x // 16, filter_rows, 0)
    for copy in copies:
        copy.wait()


def tensor_kernel(
    width, temp, cure, below, far, near, filtered, first_flat, first_steep,
    x_parts, wide, narrow, sx, out, grads, low, products,
):
    parts, rows, pad_x, depth = filtered.shape
    columns, cells, span_x, pad_x = sizes(width, depth)
    planes, depths = lax.axis_size("plane"), lax.axis_size("depth")
    plane, layer = lax.axis_index("plane"), lax.axis_index("depth")

    edge = jnp.concatenate([below[0], below[1]], axis=1)
    result = product(x_parts[...], edge).astype(jnp.bfloat16)
    kinds = (result[:pad_x], result[pad_x:])
    firsts = (first_flat[...], first_steep[...])
    at_first = rows * 2 * LANES + 3 * LANES
    for part in range(3):
        kind, row_kind, depth_kind = X_KINDS[part], ROW_KINDS[part], DEPTH_KINDS[part]
        at = 5 * LANES * row_kind
        edge_rows = product(kinds[kind], wide[at : at + 2 * LANES, :]).astype(jnp.bfloat16)
        at = at_first + row_kind * LANES
        first_rows = product(firsts[kind], narrow[at : at + LANES, :]).astype(jnp.bfloat16)
        at = 5 * LANES * depth_kind + 2 * LANES
        both = jnp.concatenate([edge_rows, first_rows], axis=1)
        low[part] = product(both, wide[at : at + 3 * LANES, :])
        for row in range(rows):
            half = (row % 2) * LANES
            both = jnp.concatenate(
                [filtered[part, row], edge_rows[:, half : half + LANES]], axis=1
            )
            at = (depth_kind * (rows // 2) + row // 2) * 2 * LANES
            grads[part, row] = product(both, narrow[at : at + 2 * LANES, :])

    weights = product_weights(rows)
    pairs = ((0, 0), (1, 1), (2, 2), (0, 1), (0, 2), (1, 2))
    has_below = jnp.where(layer > 0, 1.0, 0.0)

    def multiply(group, carry):
        start = pl.multiple_of(group * 16, 16)
        x_at = plane * width - HALO * COARSE - R2 + start
        x_at = x_at + lax.broadcasted_iota(jnp.int32, (16, LANES), 0)
        inside = jnp.where((x_at >= 0) & (x_at < planes * width), 1.0, 0.0)
        place = pl.ds(start, 16)
        totals = [None] * 6
        for row in range(rows):
            three = [grads[part, row, place, :] for part in range(3)]
            weighted = [float(weights[row]) * value for value in three]
            for index, (first, second) in enumerate(pairs):
                term = weighted[first] * three[second]
                totals[index] = term if row == 0 else totals[index] + term
        for index in range(6):
            products[index, place, 0:LANES] = (totals[index] * inside).astype(jnp.bfloat16)
        inside = inside * has_below
        for tile in range(2):
            lanes = slice(tile * LANES, (tile + 1) * LANES)
            three = [low[part, place, lanes] for part in range(3)]
            masked = [value * inside for value in three]
            for index, (first, second) in enumerate(pairs):
                term = masked[first] * three[second]
                products[index, place, LANES + tile * LANES : 2 * LANES + tile * LANES] = (
                    term.astype(jnp.bfloat16)
                )
        return carry

    lax.fori_loop(0, pad_x // 16, multiply, 0)

    coarse = narrow[rows * 2 * LANES : rows * 2 * LANES + 3 * LANES, :]
    sums = []
    for index in range(6):
        part = product(products[index], coarse).astype(jnp.bfloat16)
        sums.append(product(sx[...], part))
    trace = sums[0] + sums[1] + sums[2]
    scale = (conduct_fiber - conduct_matrix) / (2.0 * trace + tensor_eps)
    xx = conduct_matrix + scale * (trace - sums[1])
    xz = -scale * sums[5]
    zz = conduct_matrix + scale * (trace - sums[2])
    lane = lax.broadcasted_iota(jnp.int32, xx.shape, 1)
    joined = jnp.where(
        lane < cells,
        xx,
        jnp.where(lane < 2 * cells, pltpu.roll(xz, cells, 1), pltpu.roll(zz, 2 * cells, 1)),
    )

    count = temp.shape[0]
    lanes = temp.shape[1]
    pad = jnp.zeros((8 - 2 * GHOST, lanes), jnp.float32)
    own_first = jnp.concatenate([temp[0:GHOST, :], cure[0:GHOST, :], pad], axis=0)
    own_last = jnp.concatenate([temp[count - GHOST :, :], cure[count - GHOST :, :], pad], axis=0)
    odd = is_odd()
    outer, inner = joined_columns(far, rows), joined_columns(near, rows)
    left, right = jnp.where(odd, inner, outer), jnp.where(odd, outer, inner)
    height = count + 2 * HALO
    for target in range(out.shape[0]):
        piece = jnp.where(layer == target - 1, own_last, 0.0)
        piece = jnp.where(layer == target + 1, own_first, piece)
        if target == 0:
            piece = jnp.where(layer == depths - 1, left, piece)
        if target == out.shape[0] - 1:
            piece = jnp.where(layer == 0, right, piece)
        out[target, 0:height, 0:LANES] = joined[count * target : count * target + height]
        if lanes > LANES:
            out[target, 0:height, LANES:] = jnp.zeros((height, lanes - LANES), jnp.float32)
        out[target, height : height + 2 * GHOST, :] = piece[0 : 2 * GHOST]
        spare = out.shape[1] - height - 2 * GHOST
        if spare:
            out[target, height + 2 * GHOST :, :] = jnp.zeros((spare, lanes), jnp.float32)


def cure_kernel(cells, chunks, temp_in, cure_in, levels, plan, temp_out, cure_out, conduct_out):
    count, lanes = temp_in.shape
    parts = chunks.shape[0]
    planes, depths = lax.axis_size("plane"), lax.axis_size("depth")
    plane, layer = lax.axis_index("plane"), lax.axis_index("depth")
    height = count + 2 * HALO
    own = cells - BEFORE
    lane = lax.broadcasted_iota(jnp.int32, (16, lanes), 1)
    row = lax.broadcasted_iota(jnp.int32, (16, lanes), 0)

    conduct = [jnp.zeros((16, lanes), jnp.float32) for _ in range(3)]
    for part in range(parts):
        chunk = chunks[part, 0:16, :]
        here = lane >= own * part - BEFORE
        for kind in range(3):
            shift = (own * part - BEFORE - kind * cells) % lanes
            moved = chunk if shift == 0 else pltpu.roll(chunk, shift, 1)
            conduct[kind] = jnp.where(here, moved, conduct[kind])
    for kind in range(3):
        conduct_out[kind] = conduct[kind][HALO : HALO + count]

    before = chunks[lax.rem(layer + parts - 1, parts)][height : height + 2 * GHOST]
    after = chunks[lax.rem(layer + 1, parts)][height : height + 2 * GHOST]
    spare = jnp.full((16 - count - 2 * GHOST, lanes), 0.5, jnp.float32)
    temp = jnp.concatenate([before[:GHOST], temp_in[...], after[:GHOST], 8.0 * spare], axis=0)
    cure = jnp.concatenate([before[GHOST:], cure_in[...], after[GHOST:], spare], axis=0)
    gap = GHOST - HALO
    xx, xz, zz = [pltpu.roll(part, gap, 0) for part in conduct]

    first = (plane == 0) & (layer == 0)
    last = (plane == planes - 1) & (layer == depths - 1)
    for step in range(STEPS):
        top, bottom = levels[plan[step, 0]], levels[plan[step, 1]]
        temp = jnp.where((row < GHOST) & first, temp[GHOST : GHOST + 1], temp)
        temp = jnp.where(
            (row >= GHOST + count) & last, temp[GHOST + count - 1 : GHOST + count], temp
        )
        cooler = jnp.where(lane == 0, top, pltpu.roll(temp, 1, 1))
        later = jnp.where(lane == lanes - 1, bottom, pltpu.roll(temp, lanes - 1, 1))
        slant = later - cooler
        second_x = pltpu.roll(temp, 15, 0) - 2.0 * temp + pltpu.roll(temp, 1, 0)
        second_z = later - 2.0 * temp + cooler
        cross = 0.25 * (pltpu.roll(slant, 15, 0) - pltpu.roll(slant, 1, 0))
        spread = xx * second_x + 2.0 * xz * cross + zz * second_z
        inverse = 1.0 / reference_temp - 1.0 / temp
        left = 1.0 - cure
        rate = rate_first * jnp.exp(energy_first * inverse) + rate_second * jnp.exp(
            energy_second * inverse
        ) * jnp.sqrt(cure)
        rate = rate * (left * jnp.sqrt(left))
        temp = temp + time_step * (spread + heat_release * rate)
        cure = cure + time_step * rate
    temp_out[...] = temp[GHOST : GHOST + count]
    cure_out[...] = cure[GHOST : GHOST + count]


def on_device(intensity, temp_start, cure_start, tool_levels, plan):
    rows, width, depth = intensity.shape
    count, lanes = temp_start.shape
    planes, depths = lax.axis_size("plane"), lax.axis_size("depth")
    columns, cells, span_x, pad_x = sizes(width, depth)
    bf16 = jnp.bfloat16
    slots = rows + lanes // LANES
    params = pltpu.CompilerParams(vmem_limit_bytes=24 * 1024 * 1024)
    vmem = pl.BlockSpec(memory_space=pltpu.VMEM)
    smem = pl.BlockSpec(memory_space=pltpu.SMEM)
    stay = pl.BlockSpec(memory_space=pltpu.HBM)

    fixed = lambda values: pltpu.with_memory_space_constraint(values, pltpu.HBM)
    x_hbm = jnp.asarray(as_bfloat16(x_bands(width, depth)))
    far, near, own, x_parts = pl.pallas_call(
        pack_kernel,
        name="pack",
        out_shape=(
            pltpu.VMEM((slots, EDGE, depth), bf16),
            pltpu.VMEM((slots, EDGE, depth), bf16),
            pltpu.VMEM((rows, width, depth), bf16),
            pltpu.VMEM(x_hbm.shape, bf16),
        ),
        in_specs=[stay] * 4,
        scratch_shapes=[
            pltpu.VMEM((rows, width, depth), jnp.int32),
            pltpu.VMEM((count, lanes), jnp.float32),
            pltpu.VMEM((count, lanes), jnp.float32),
            pltpu.SemaphoreType.DMA((4,)),
        ],
        compiler_params=params,
    )(*[fixed(values) for values in (intensity, temp_start, cure_start, x_hbm)])

    def moved(values, pairs):
        index = [(p * depths + d, q * depths + e) for (p, d), (q, e) in pairs]
        return lax.ppermute(values, ("plane", "depth"), index)

    def swapped(values, first):
        pairs = [(p, p + 1) for p in range(first, planes - 1, 2)]
        pairs += [(q, p) for p, q in pairs]
        return moved(values, [((p, d), (q, d)) for p, q in pairs for d in range(depths)])

    far = swapped(far, 1)
    near = swapped(near, 0)

    span = width + 2 * EDGE
    window, up = pl.pallas_call(
        window_kernel,
        name="window",
        out_shape=(
            jax.ShapeDtypeStruct((rows // 2, span, 2 * depth), bf16),
            jax.ShapeDtypeStruct((2, span, depth), bf16),
        ),
        compiler_params=params,
    )(own, far, near)
    below = moved(up, [((p, d), (p, d + 1)) for p in range(planes) for d in range(depths - 1)])

    wide, narrow = [], [*depth_bands(rows, depth).reshape(rows, 2 * LANES, LANES)]
    for edge_rows, low in zip(row_bands(rows, EDGE), low_bands(rows)):
        wide += [edge_rows, low]
    narrow += [coarse_depth_bands(rows, depth), *row_bands(rows, FIRST)]
    wide, narrow = [jnp.asarray(as_bfloat16(np.concatenate(bands))) for bands in (wide, narrow)]
    wide_hbm, narrow_hbm = wide, narrow
    sx = jnp.asarray(as_bfloat16(coarse_x_bands(columns, pad_x, -(-columns // 16) * 16)))
    filtered, first_flat, first_steep, wide, narrow = pl.pallas_call(
        own_kernel,
        name="own",
        out_shape=(
            jax.ShapeDtypeStruct((3, rows, pad_x, depth), bf16),
            jax.ShapeDtypeStruct((pad_x, depth), bf16),
            jax.ShapeDtypeStruct((pad_x, depth), bf16),
            pltpu.VMEM(wide_hbm.shape, bf16),
            pltpu.VMEM(narrow_hbm.shape, bf16),
        ),
        in_specs=[vmem, vmem, stay, stay],
        scratch_shapes=[
            pltpu.VMEM((rows, 2 * pad_x, depth), jnp.float32),
            pltpu.SemaphoreType.DMA((2,)),
        ],
        cost_estimate=pl.CostEstimate(
            flops=2 * rows * 2 * pad_x * span * depth, bytes_accessed=4_000_000, transcendentals=0
        ),
        compiler_params=params,
    )(window, x_parts, fixed(wide_hbm), fixed(narrow_hbm))

    height = -(-(count + 2 * HALO + 2 * GHOST) // 8) * 8
    chunks = pl.pallas_call(
        functools.partial(tensor_kernel, width),
        name="tensor",
        out_shape=pltpu.VMEM((depths, height, lanes), jnp.float32),
        scratch_shapes=[
            pltpu.VMEM((3, rows, pad_x, depth), jnp.float32),
            pltpu.VMEM((3, pad_x, 2 * LANES), jnp.float32),
            pltpu.VMEM((6, pad_x, 3 * LANES), bf16),
        ],
        compiler_params=params,
    )(
        temp_start, cure_start, below, far, near, filtered, first_flat, first_steep,
        x_parts, wide, narrow, sx,
    )

    chunks = lax.all_to_all(chunks, "depth", split_axis=0, concat_axis=0, tiled=True)

    return pl.pallas_call(
        functools.partial(cure_kernel, cells),
        name="cure",
        out_shape=(
            jax.ShapeDtypeStruct((count, lanes), jnp.float32),
            jax.ShapeDtypeStruct((count, lanes), jnp.float32),
            jax.ShapeDtypeStruct((3, count, lanes), jnp.float32),
        ),
        in_specs=[vmem, vmem, vmem, smem, smem],
        out_specs=(vmem, vmem, vmem),
        compiler_params=params,
    )(chunks, temp_start, cure_start, tool_levels, plan)


def solution(mesh):
    return jax.shard_map(
        on_device,
        mesh=mesh,
        in_specs=(
            P(None, "plane", "depth"),
            P(("plane", "depth"), None),
            P(("plane", "depth"), None),
            P(),
            P(),
        ),
        out_specs=(
            P(("plane", "depth"), None),
            P(("plane", "depth"), None),
            P(None, ("plane", "depth"), None),
        ),
        check_vma=False,
    )
```

```python
import functools

import jax
import jax.numpy as jnp
import ml_dtypes
import numpy as np
from jax import lax
from jax.experimental import pallas as pl
from jax.experimental.pallas import tpu as pltpu
from jax.sharding import PartitionSpec as P

ROWS = 8
R1 = 6
R2 = 10
COARSE = 4
STEPS = 3

sigma_grad = 2.0
sigma_tensor = 3.3
conduct_matrix = 0.3
conduct_fiber = 1.5
time_step = 0.25
heat_release = 0.4
rate_first = 0.15
rate_second = 0.6
energy_first = 30.0
energy_second = 25.0
reference_temp = 4.2
tensor_eps = 1e-06

EDGE = 32
LANES = 128
HALO = 2
GHOST = 3
FIRST = 16
START = 8
BEFORE = -(-(R1 + R2) // COARSE)
AFTER = 1
HALF = LANES // 2
ROW_KINDS = (1, 0, 0)
X_KINDS = (0, 1, 0)
DEPTH_KINDS = (0, 0, 1)


def smooth_taps(radius, sigma):
    offsets = np.arange(-radius, radius + 1) * 1.0
    weights = np.exp(-0.5 * offsets * offsets / (sigma * sigma))
    return weights / weights.sum()


def slope_taps(radius, sigma):
    offsets = np.arange(-radius, radius + 1) * 1.0
    weights = np.exp(-0.5 * offsets * offsets / (sigma * sigma))
    return offsets * weights / np.sum(offsets * offsets * weights)


def row_weights(count, radius, sigma):
    taps = smooth_taps(radius, sigma)
    result = np.zeros(count)
    for source in range(count):
        for target in range(count):
            offset = target - source
            if abs(offset) <= radius:
                result[source] += taps[offset + radius]
    return result


def rounded(taps):
    best = None
    for factor in np.linspace(1.0, 2.0, 20001)[:-1]:
        near = (taps * factor).astype(np.float32).astype(ml_dtypes.bfloat16).astype(np.float64)
        error = np.abs(near / factor - taps).sum()
        if best is None or error < best[0]:
            best = (error, near, factor)
    return best[1], best[2]


def as_bfloat16(matrix):
    return matrix.astype(np.float32).astype(ml_dtypes.bfloat16)


def halves(matrix):
    high = as_bfloat16(matrix)
    return high, as_bfloat16(matrix - high.astype(np.float64))


def sizes(width, depth):
    columns = width // COARSE + 2 * HALO
    cells = depth // COARSE + BEFORE + AFTER
    span_x = columns * COARSE + 2 * R2
    pad_x = -(-span_x // 16) * 16
    return columns, cells, span_x, pad_x


GRAD_TAPS = tuple(
    rounded(taps(R1, sigma_grad)) for taps in (smooth_taps, slope_taps)
)
GRAD_FACTOR = GRAD_TAPS[0][1] ** 2 * GRAD_TAPS[1][1]


def grad_taps(kind):
    return GRAD_TAPS[kind][0]


def tap(taps, offset):
    radius = (len(taps) - 1) // 2
    return float(taps[offset + radius]) if abs(offset) <= radius else 0.0


def x_bands(width, depth):
    columns, cells, span_x, pad_x = sizes(width, depth)
    bands = np.zeros((2, pad_x, width + 2 * EDGE))
    first = EDGE - HALO * COARSE - R2 - R1
    for kind in range(2):
        for out in range(span_x):
            bands[kind, out, out + first : out + first + 2 * R1 + 1] = grad_taps(kind)
    return bands.reshape(2 * pad_x, -1)


def edge_bands(rows):
    bands = np.zeros((2, 3, rows * FIRST, rows * FIRST))
    for part in range(3):
        row_taps, depth_taps = grad_taps(ROW_KINDS[part]), grad_taps(DEPTH_KINDS[part])
        for source in range(rows):
            for target in range(rows):
                row_tap = tap(row_taps, source - target)
                for near in range(-FIRST, FIRST):
                    side, lane = int(near >= 0), source * FIRST + near % FIRST
                    for place in range(-R1, START):
                        value = row_tap * tap(depth_taps, near - place)
                        bands[side, part, lane, target * FIRST + START + place] = value
    return bands


def depth_bands(depth):
    bands = np.zeros((2, depth, depth))
    for kind in range(2):
        for place in range(depth):
            for near in range(max(place - R1, 0), min(place + R1 + 1, depth)):
                bands[kind, near, place] = tap(grad_taps(kind), near - place)
    return bands


def product_weights(rows):
    return row_weights(rows, R2, sigma_tensor) / (255.0 * GRAD_FACTOR) ** 2


def coarse_depth_bands(rows, depth):
    taps = smooth_taps(R2, sigma_tensor)
    weights = product_weights(rows)
    columns, cells, span_x, pad_x = sizes(0, depth)
    bands = np.zeros((2, depth, LANES))
    for cell in range(cells):
        for voxel in range(COARSE):
            place = (cell - BEFORE) * COARSE + voxel
            for near in range(max(place - R2, -R1), min(place + R2 + 1, depth)):
                value = tap(taps, near - place)
                if near >= START:
                    bands[0, near, cell] += value
                else:
                    for row in range(rows):
                        bands[1, row * FIRST + START + near, cell] += weights[row] * value
    return bands


def coarse_x_bands(count, padded_in, padded_out):
    taps = smooth_taps(R2, sigma_tensor)
    bands = np.zeros((padded_out, padded_in))
    for cell in range(count):
        for voxel in range(COARSE):
            start = cell * COARSE + voxel
            bands[cell, start : start + 2 * R2 + 1] += taps
    return bands


def three_parts(values):
    high = values.astype(jnp.bfloat16).astype(jnp.float32)
    rest = values - high
    middle = rest.astype(jnp.bfloat16).astype(jnp.float32)
    return high, middle, (rest - middle).astype(jnp.bfloat16).astype(jnp.float32)


def column_slot(temp_ref, cure_ref, first):
    pad = jnp.zeros((8 - 2 * GHOST, temp_ref.shape[1]), jnp.float32)
    rows = pl.ds(first, GHOST)
    both = jnp.concatenate([temp_ref[rows, :], cure_ref[rows, :], pad], axis=0)
    high, middle, low = three_parts(both)
    return jnp.concatenate([high, middle, low, jnp.zeros_like(high)], axis=0).astype(jnp.bfloat16)


def is_odd():
    return lax.rem(lax.axis_index("plane"), 2) == 1


def pack_kernel(
    intensity, temp_hbm, cure_hbm, x_hbm, far, near, own, x_parts, temp, cure, grey, sems
):
    rows, width, depth = intensity.shape
    copies = [
        pltpu.make_async_copy(intensity, grey, sems.at[0]),
        pltpu.make_async_copy(temp_hbm, temp, sems.at[1]),
        pltpu.make_async_copy(cure_hbm, cure, sems.at[2]),
        pltpu.make_async_copy(x_hbm, x_parts, sems.at[3]),
    ]
    for copy in copies:
        copy.start()
    for copy in copies:
        copy.wait()
    odd = is_odd()
    count = temp.shape[0]
    sides = (column_slot(temp, cure, 0), column_slot(temp, cure, count - GHOST))

    def send(left, right):
        for row in range(rows):
            left[row] = grey[row, :EDGE, :].astype(jnp.float32).astype(jnp.bfloat16)
            right[row] = grey[row, width - EDGE :, :].astype(jnp.float32).astype(jnp.bfloat16)
        for slot in range(temp.shape[1] // LANES):
            left[rows + slot] = sides[0][:, slot * LANES : (slot + 1) * LANES]
            right[rows + slot] = sides[1][:, slot * LANES : (slot + 1) * LANES]

    @pl.when(odd)
    def _():
        send(near, far)

    @pl.when(jnp.logical_not(odd))
    def _():
        send(far, near)

    for row in range(rows):
        own[row] = grey[row].astype(jnp.float32).astype(jnp.bfloat16)


def packed_rows(values, size, first):
    depth = values[0].shape[1]
    lane = lax.broadcasted_iota(jnp.int32, values[0].shape, 1)
    packed = None
    for block, value in enumerate(values):
        shift = (size * block - first) % depth
        moved = value if shift == 0 else pltpu.roll(value, shift, 1)
        packed = moved if block == 0 else jnp.where(lane >= size * block, moved, packed)
    return packed


def window_kernel(own, far, near, window, up):
    rows, width, depth = own.shape
    odd = is_odd()

    def fill(from_left, from_right):
        values = []
        for row in range(rows):
            half = (row % 2) * depth
            whole = jnp.concatenate([from_left[row], own[row], from_right[row]], axis=0)
            window[row // 2, :, half : half + depth] = whole
            values.append(whole.astype(jnp.float32))
        up[...] = packed_rows(values, FIRST, depth - FIRST).astype(jnp.bfloat16)

    @pl.when(odd)
    def _():
        fill(near, far)

    @pl.when(jnp.logical_not(odd))
    def _():
        fill(far, near)


def joined_columns(ref, rows):
    slots = [ref[slot].astype(jnp.float32) for slot in range(rows, ref.shape[0])]
    parts = jnp.concatenate(slots, axis=1)
    return (parts[0:8] + parts[8:16]) + parts[16:24]


def product(first, second):
    return jnp.dot(first, second, preferred_element_type=jnp.float32)


def along_rows(kind, values, row):
    total = None
    for source, value in enumerate(values):
        weight = tap(grad_taps(kind), source - row)
        if weight != 0.0:
            total = weight * value if total is None else total + weight * value
    return total


def weighted_products(three, weight):
    pairs = ((0, 0), (1, 1), (2, 2), (0, 1), (0, 2), (1, 2))
    first = [weight * value for value in three]
    return [first[a] * three[b] for a, b in pairs]


def inside_x(start, count, width):
    place = lax.axis_index("plane") * width - HALO * COARSE - R2 + start
    place = place + lax.broadcasted_iota(jnp.int32, (count, LANES), 0)
    inside = (place >= 0) & (place < lax.axis_size("plane") * width)
    return jnp.where(inside, 1.0, 0.0)


def block_sums(products, coarse, sx, index):
    part = product(products[index], coarse).astype(jnp.bfloat16)
    return product(sx, part)


def own_kernel(
    window, x_parts, bands_hbm, sums, edge, bands, across, filtered, grads, products, sem
):
    pairs, height, double = window.shape
    rows, depth = 2 * pairs, double // 2
    width = height - 2 * EDGE
    columns, cells, span_x, pad_x = sizes(width, depth)
    copy = pltpu.make_async_copy(bands_hbm, bands, sem.at[0])
    copy.start()
    x_bands_of = x_parts[: 2 * pad_x, :]
    for pair in range(pairs):
        result = product(x_bands_of, window[pair])
        across[2 * pair] = result[:, :depth]
        across[2 * pair + 1] = result[:, depth:]

    def filter_rows(group, carry):
        start = pl.multiple_of(group * 16, 16)
        kinds = [
            [across[row, pl.ds(kind * pad_x + start, 16), :] for row in range(rows)]
            for kind in range(2)
        ]
        for part in range(3):
            for row in range(rows):
                result = along_rows(ROW_KINDS[part], kinds[X_KINDS[part]], row)
                filtered[part, row, pl.ds(start, 16), :] = result.astype(jnp.bfloat16)
        return carry

    lax.fori_loop(0, pad_x // 16, filter_rows, 0)

    values = [
        window[row // 2, :, (row % 2) * depth : (row % 2 + 1) * depth].astype(jnp.float32)
        for row in range(rows)
    ]
    first = product(x_bands_of, packed_rows(values, FIRST, 0).astype(jnp.bfloat16))
    first = first.astype(jnp.bfloat16)
    copy.wait()
    for part in range(3):
        at = DEPTH_KINDS[part] * depth
        for row in range(rows):
            grads[part, row] = product(filtered[part, row], bands[at : at + depth, :])
        at = (4 + 2 * part) * depth
        kind = X_KINDS[part]
        values = first[kind * pad_x : (kind + 1) * pad_x]
        edge[part] = product(values, bands[at : at + depth, :]) + product(
            values, bands[at + depth : at + 2 * depth, :]
        )

    weights = product_weights(rows)
    is_last = lax.axis_index("depth") == lax.axis_size("depth") - 1
    place = lax.broadcasted_iota(jnp.int32, (16, depth), 1)
    complete = jnp.where((place < depth - R1) | is_last, 1.0, 0.0)

    def multiply(group, carry):
        start = pl.multiple_of(group * 16, 16)
        inside = inside_x(start, 16, width) * complete
        totals = None
        for row in range(rows):
            three = [grads[part, row, pl.ds(start, 16), :] for part in range(3)]
            terms = weighted_products(three, float(weights[row]))
            totals = terms if row == 0 else [a + b for a, b in zip(totals, terms)]
        for index in range(6):
            products[index, pl.ds(start, 16), :] = (totals[index] * inside).astype(jnp.bfloat16)
        return carry

    lax.fori_loop(0, pad_x // 16, multiply, 0)
    sx = x_parts[2 * pad_x :, :pad_x]
    for index in range(6):
        sums[index] = block_sums(products, bands[2 * depth : 3 * depth, :], sx, index)


def edge_kernel(
    width, temp, cure, below, far, near, sums, edge, x_parts, bands, out, products
):
    rows = below.shape[1] // FIRST
    depth = LANES
    columns, cells, span_x, pad_x = sizes(width, depth)
    depths, layer = lax.axis_size("depth"), lax.axis_index("depth")
    result = product(x_parts[: 2 * pad_x, :], below[...]).astype(jnp.bfloat16)
    three = []
    for part in range(3):
        at = (10 + 2 * part) * depth
        kind = X_KINDS[part]
        values = result[kind * pad_x : (kind + 1) * pad_x]
        three.append(
            edge[part]
            + product(values, bands[at : at + depth, :])
            + product(values, bands[at + depth : at + 2 * depth, :])
        )
    place = lax.rem(lax.broadcasted_iota(jnp.int32, (pad_x, LANES), 1), FIRST) - START
    inside = inside_x(0, pad_x, width) * jnp.where((place >= 0) | (layer > 0), 1.0, 0.0)
    for index, term in enumerate(weighted_products(three, inside)):
        products[index] = term.astype(jnp.bfloat16)
    sx = x_parts[2 * pad_x :, :pad_x]
    total = [
        sums[index] + block_sums(products, bands[3 * depth : 4 * depth, :], sx, index)
        for index in range(6)
    ]
    trace = total[0] + total[1] + total[2]
    lane = lax.broadcasted_iota(jnp.int32, trace.shape, 1)
    joined = [
        jnp.where(lane < HALF, a, pltpu.roll(b, HALF, 1))
        for a, b in ((trace, total[1]), (total[2], total[5]))
    ]

    count = temp.shape[0]
    lanes = temp.shape[1]
    pad = jnp.zeros((8 - 2 * GHOST, lanes), jnp.float32)
    own_first = jnp.concatenate([temp[0:GHOST, :], cure[0:GHOST, :], pad], axis=0)
    own_last = jnp.concatenate([temp[count - GHOST :, :], cure[count - GHOST :, :], pad], axis=0)
    odd = is_odd()
    outer, inner = joined_columns(far, rows), joined_columns(near, rows)
    left, right = jnp.where(odd, inner, outer), jnp.where(odd, outer, inner)
    height = count + 2 * HALO
    for target in range(out.shape[0]):
        piece = jnp.where(layer == target - 1, own_last, 0.0)
        piece = jnp.where(layer == target + 1, own_first, piece)
        if target == 0:
            piece = jnp.where(layer == depths - 1, left, piece)
        if target == out.shape[0] - 1:
            piece = jnp.where(layer == 0, right, piece)
        parts = [values[count * target : count * target + height] for values in joined]
        spare = out.shape[1] - 2 * height - 2 * GHOST
        out[target, 0 : 2 * height, 0:LANES] = jnp.concatenate(parts, axis=0)
        if lanes > LANES:
            out[target, 0 : 2 * height, LANES:] = jnp.zeros((2 * height, lanes - LANES), jnp.float32)
        out[target, 2 * height : 2 * height + 2 * GHOST, :] = piece[0 : 2 * GHOST]
        if spare:
            out[target, 2 * height + 2 * GHOST :, :] = jnp.zeros((spare, lanes), jnp.float32)


def cure_kernel(cells, chunks, temp_in, cure_in, levels, plan, temp_out, cure_out, conduct_out):
    count, lanes = temp_in.shape
    parts = chunks.shape[0]
    planes, depths = lax.axis_size("plane"), lax.axis_size("depth")
    plane, layer = lax.axis_index("plane"), lax.axis_index("depth")
    height = count + 2 * HALO
    own = cells - BEFORE - AFTER
    lane = lax.broadcasted_iota(jnp.int32, (16, lanes), 1)
    row = lax.broadcasted_iota(jnp.int32, (16, lanes), 0)

    sums = [jnp.zeros((16, lanes), jnp.float32) for _ in range(4)]
    for part in range(parts):
        first_cell = own * part - BEFORE
        here = (lane >= first_cell) & (lane < first_cell + cells)
        for index in range(4):
            at = (index // 2) * height
            chunk = chunks[part, at : at + 16, :]
            shift = (first_cell - (index % 2) * HALF) % lanes
            moved = chunk if shift == 0 else pltpu.roll(chunk, shift, 1)
            sums[index] = sums[index] + jnp.where(here, moved, 0.0)
    trace = sums[0]
    scale = (conduct_fiber - conduct_matrix) / (2.0 * trace + tensor_eps)
    conduct = [
        conduct_matrix + scale * (trace - sums[1]),
        -scale * sums[3],
        conduct_matrix + scale * (trace - sums[2]),
    ]
    for kind in range(3):
        conduct_out[kind] = conduct[kind][HALO : HALO + count]

    before = chunks[lax.rem(layer + parts - 1, parts)][2 * height : 2 * height + 2 * GHOST]
    after = chunks[lax.rem(layer + 1, parts)][2 * height : 2 * height + 2 * GHOST]
    spare = jnp.full((16 - count - 2 * GHOST, lanes), 0.5, jnp.float32)
    temp = jnp.concatenate([before[:GHOST], temp_in[...], after[:GHOST], 8.0 * spare], axis=0)
    cure = jnp.concatenate([before[GHOST:], cure_in[...], after[GHOST:], spare], axis=0)
    gap = GHOST - HALO
    xx, xz, zz = [pltpu.roll(part, gap, 0) for part in conduct]

    first = (plane == 0) & (layer == 0)
    last = (plane == planes - 1) & (layer == depths - 1)
    for step in range(STEPS):
        top, bottom = levels[plan[step, 0]], levels[plan[step, 1]]
        temp = jnp.where((row < GHOST) & first, temp[GHOST : GHOST + 1], temp)
        temp = jnp.where(
            (row >= GHOST + count) & last, temp[GHOST + count - 1 : GHOST + count], temp
        )
        cooler = jnp.where(lane == 0, top, pltpu.roll(temp, 1, 1))
        later = jnp.where(lane == lanes - 1, bottom, pltpu.roll(temp, lanes - 1, 1))
        slant = later - cooler
        second_x = pltpu.roll(temp, 15, 0) - 2.0 * temp + pltpu.roll(temp, 1, 0)
        second_z = later - 2.0 * temp + cooler
        cross = 0.25 * (pltpu.roll(slant, 15, 0) - pltpu.roll(slant, 1, 0))
        spread = xx * second_x + 2.0 * xz * cross + zz * second_z
        inverse = 1.0 / reference_temp - 1.0 / temp
        left = 1.0 - cure
        rate = rate_first * jnp.exp(energy_first * inverse) + rate_second * jnp.exp(
            energy_second * inverse
        ) * jnp.sqrt(cure)
        rate = rate * (left * jnp.sqrt(left))
        temp = temp + time_step * (spread + heat_release * rate)
        cure = cure + time_step * rate
    temp_out[...] = temp[GHOST : GHOST + count]
    cure_out[...] = cure[GHOST : GHOST + count]


def on_device(intensity, temp_start, cure_start, tool_levels, plan):
    rows, width, depth = intensity.shape
    count, lanes = temp_start.shape
    planes, depths = lax.axis_size("plane"), lax.axis_size("depth")
    columns, cells, span_x, pad_x = sizes(width, depth)
    bf16 = jnp.bfloat16
    slots = rows + lanes // LANES
    params = pltpu.CompilerParams(vmem_limit_bytes=24 * 1024 * 1024)
    vmem = pl.BlockSpec(memory_space=pltpu.VMEM)
    smem = pl.BlockSpec(memory_space=pltpu.SMEM)
    stay = pl.BlockSpec(memory_space=pltpu.HBM)

    fixed = lambda values: pltpu.with_memory_space_constraint(values, pltpu.HBM)
    coarse_x = coarse_x_bands(columns, width + 2 * EDGE, -(-columns // 16) * 16)
    x_hbm = jnp.asarray(as_bfloat16(np.concatenate([x_bands(width, depth), coarse_x])))
    far, near, own, x_parts, temp, cure = pl.pallas_call(
        pack_kernel,
        name="pack",
        out_shape=(
            pltpu.VMEM((slots, EDGE, depth), bf16),
            pltpu.VMEM((slots, EDGE, depth), bf16),
            pltpu.VMEM((rows, width, depth), bf16),
            pltpu.VMEM(x_hbm.shape, bf16),
            pltpu.VMEM((count, lanes), jnp.float32),
            pltpu.VMEM((count, lanes), jnp.float32),
        ),
        in_specs=[stay] * 4,
        scratch_shapes=[
            pltpu.VMEM((rows, width, depth), jnp.int32),
            pltpu.SemaphoreType.DMA((4,)),
        ],
        compiler_params=params,
    )(*[fixed(values) for values in (intensity, temp_start, cure_start, x_hbm)])

    def moved(values, pairs):
        index = [(p * depths + d, q * depths + e) for (p, d), (q, e) in pairs]
        return lax.ppermute(values, ("plane", "depth"), index)

    def swapped(values, first):
        pairs = [(p, p + 1) for p in range(first, planes - 1, 2)]
        pairs += [(q, p) for p, q in pairs]
        return moved(values, [((p, d), (q, d)) for p, q in pairs for d in range(depths)])

    far = swapped(far, 1)
    near = swapped(near, 0)

    span = width + 2 * EDGE
    window, up = pl.pallas_call(
        window_kernel,
        name="window",
        out_shape=(
            pltpu.VMEM((rows // 2, span, 2 * depth), bf16),
            pltpu.VMEM((span, depth), bf16),
        ),
        compiler_params=params,
    )(own, far, near)
    below = moved(up, [((p, d), (p, d + 1)) for p in range(planes) for d in range(depths - 1)])

    pieces = [*depth_bands(depth), *coarse_depth_bands(rows, depth)]
    for side in edge_bands(rows)[::-1]:
        for part in side:
            pieces += halves(part)
    bands_hbm = jnp.asarray(np.concatenate([as_bfloat16(piece) for piece in pieces]))
    sums, edge, bands = pl.pallas_call(
        own_kernel,
        name="own",
        out_shape=(
            pltpu.VMEM((6, x_hbm.shape[0] - 2 * pad_x, LANES), jnp.float32),
            pltpu.VMEM((3, pad_x, LANES), jnp.float32),
            pltpu.VMEM(bands_hbm.shape, bf16),
        ),
        in_specs=[vmem, vmem, stay],
        scratch_shapes=[
            pltpu.VMEM((rows, 2 * pad_x, depth), jnp.float32),
            pltpu.VMEM((3, rows, pad_x, depth), bf16),
            pltpu.VMEM((3, rows, pad_x, depth), jnp.float32),
            pltpu.VMEM((6, pad_x, depth), bf16),
            pltpu.SemaphoreType.DMA((1,)),
        ],
        cost_estimate=pl.CostEstimate(
            flops=4 * rows * pad_x * span * depth, bytes_accessed=4_000_000, transcendentals=0
        ),
        compiler_params=params,
    )(window, x_parts, fixed(bands_hbm))

    height = -(-(2 * (count + 2 * HALO) + 2 * GHOST) // 8) * 8
    chunks = pl.pallas_call(
        functools.partial(edge_kernel, width),
        name="edge",
        out_shape=pltpu.VMEM((depths, height, lanes), jnp.float32),
        scratch_shapes=[pltpu.VMEM((6, pad_x, depth), bf16)],
        compiler_params=params,
    )(temp, cure, below, far, near, sums, edge, x_parts, bands)

    chunks = lax.all_to_all(chunks, "depth", split_axis=0, concat_axis=0, tiled=True)

    return pl.pallas_call(
        functools.partial(cure_kernel, cells),
        name="cure",
        out_shape=(
            jax.ShapeDtypeStruct((count, lanes), jnp.float32),
            jax.ShapeDtypeStruct((count, lanes), jnp.float32),
            jax.ShapeDtypeStruct((3, count, lanes), jnp.float32),
        ),
        in_specs=[vmem, vmem, vmem, smem, smem],
        out_specs=(vmem, vmem, vmem),
        compiler_params=params,
    )(chunks, temp, cure, tool_levels, plan)


def solution(mesh):
    return jax.shard_map(
        on_device,
        mesh=mesh,
        in_specs=(
            P(None, "plane", "depth"),
            P(("plane", "depth"), None),
            P(("plane", "depth"), None),
            P(),
            P(),
        ),
        out_specs=(
            P(("plane", "depth"), None),
            P(("plane", "depth"), None),
            P(None, ("plane", "depth"), None),
        ),
        check_vma=False,
    )
```

```python
import functools

import jax
import jax.numpy as jnp
import ml_dtypes
import numpy as np
from jax import lax
from jax.experimental import pallas as pl
from jax.experimental.pallas import tpu as pltpu
from jax.sharding import PartitionSpec as P

ROWS = 8
R1 = 6
R2 = 10
COARSE = 4
STEPS = 3

sigma_grad = 2.0
sigma_tensor = 3.3
conduct_matrix = 0.3
conduct_fiber = 1.5
time_step = 0.25
heat_release = 0.4
rate_first = 0.15
rate_second = 0.6
energy_first = 30.0
energy_second = 25.0
reference_temp = 4.2
tensor_eps = 1e-06

EDGE = 32
LANES = 128
HALO = 2
GHOST = 3
FIRST = 16
START = 8
BEFORE = -(-(R1 + R2) // COARSE)
AFTER = 1
HALF = LANES // 2
ROW_KINDS = (1, 0, 0)
X_KINDS = (0, 1, 0)
DEPTH_KINDS = (0, 0, 1)


def smooth_taps(radius, sigma):
    offsets = np.arange(-radius, radius + 1) * 1.0
    weights = np.exp(-0.5 * offsets * offsets / (sigma * sigma))
    return weights / weights.sum()


def slope_taps(radius, sigma):
    offsets = np.arange(-radius, radius + 1) * 1.0
    weights = np.exp(-0.5 * offsets * offsets / (sigma * sigma))
    return offsets * weights / np.sum(offsets * offsets * weights)


def row_weights(count, radius, sigma):
    taps = smooth_taps(radius, sigma)
    result = np.zeros(count)
    for source in range(count):
        for target in range(count):
            offset = target - source
            if abs(offset) <= radius:
                result[source] += taps[offset + radius]
    return result


def rounded(taps):
    best = None
    for factor in np.linspace(1.0, 2.0, 20001)[:-1]:
        near = (taps * factor).astype(np.float32).astype(ml_dtypes.bfloat16).astype(np.float64)
        error = np.abs(near / factor - taps).sum()
        if best is None or error < best[0]:
            best = (error, near, factor)
    return best[1], best[2]


def as_bfloat16(matrix):
    return matrix.astype(np.float32).astype(ml_dtypes.bfloat16)


def halves(matrix):
    high = as_bfloat16(matrix)
    return high, as_bfloat16(matrix - high.astype(np.float64))


def sizes(width, depth):
    columns = width // COARSE + 2 * HALO
    cells = depth // COARSE + BEFORE + AFTER
    span_x = columns * COARSE + 2 * R2
    pad_x = -(-span_x // 16) * 16
    return columns, cells, span_x, pad_x


GRAD_TAPS = tuple(
    rounded(taps(R1, sigma_grad)) for taps in (smooth_taps, slope_taps)
)
GRAD_FACTOR = GRAD_TAPS[0][1] ** 2 * GRAD_TAPS[1][1]


def grad_taps(kind):
    return GRAD_TAPS[kind][0]


def tap(taps, offset):
    radius = (len(taps) - 1) // 2
    return float(taps[offset + radius]) if abs(offset) <= radius else 0.0


def x_bands(width, depth):
    columns, cells, span_x, pad_x = sizes(width, depth)
    bands = np.zeros((2, pad_x, width + 2 * EDGE))
    first = EDGE - HALO * COARSE - R2 - R1
    for kind in range(2):
        for out in range(span_x):
            bands[kind, out, out + first : out + first + 2 * R1 + 1] = grad_taps(kind)
    return bands.reshape(2 * pad_x, -1)


def edge_bands(rows):
    bands = np.zeros((2, 3, rows * FIRST, rows * FIRST))
    for part in range(3):
        row_taps, depth_taps = grad_taps(ROW_KINDS[part]), grad_taps(DEPTH_KINDS[part])
        for source in range(rows):
            for target in range(rows):
                row_tap = tap(row_taps, source - target)
                for near in range(-FIRST, FIRST):
                    side, lane = int(near >= 0), source * FIRST + near % FIRST
                    for place in range(-R1, START):
                        value = row_tap * tap(depth_taps, near - place)
                        bands[side, part, lane, target * FIRST + START + place] = value
    return bands


def depth_bands(depth):
    bands = np.zeros((2, depth, depth))
    for kind in range(2):
        for place in range(depth):
            for near in range(max(place - R1, 0), min(place + R1 + 1, depth)):
                bands[kind, near, place] = tap(grad_taps(kind), near - place)
    return bands


def product_weights(rows):
    return row_weights(rows, R2, sigma_tensor) / (255.0 * GRAD_FACTOR) ** 2


def coarse_depth_bands(rows, depth):
    taps = smooth_taps(R2, sigma_tensor)
    weights = product_weights(rows)
    columns, cells, span_x, pad_x = sizes(0, depth)
    bands = np.zeros((2, depth, LANES))
    for cell in range(cells):
        for voxel in range(COARSE):
            place = (cell - BEFORE) * COARSE + voxel
            for near in range(max(place - R2, -R1), min(place + R2 + 1, depth)):
                value = tap(taps, near - place)
                if near >= START:
                    bands[0, near, cell] += value
                else:
                    for row in range(rows):
                        bands[1, row * FIRST + START + near, cell] += weights[row] * value
    return bands


def coarse_x_bands(count, padded_in, padded_out):
    taps = smooth_taps(R2, sigma_tensor)
    bands = np.zeros((padded_out, padded_in))
    for cell in range(count):
        for voxel in range(COARSE):
            start = cell * COARSE + voxel
            bands[cell, start : start + 2 * R2 + 1] += taps
    return bands


def three_parts(values):
    high = values.astype(jnp.bfloat16).astype(jnp.float32)
    rest = values - high
    middle = rest.astype(jnp.bfloat16).astype(jnp.float32)
    return high, middle, (rest - middle).astype(jnp.bfloat16).astype(jnp.float32)


def column_slot(temp_ref, cure_ref, first):
    pad = jnp.zeros((8 - 2 * GHOST, temp_ref.shape[1]), jnp.float32)
    rows = pl.ds(first, GHOST)
    both = jnp.concatenate([temp_ref[rows, :], cure_ref[rows, :], pad], axis=0)
    high, middle, low = three_parts(both)
    return jnp.concatenate([high, middle, low, jnp.zeros_like(high)], axis=0).astype(jnp.bfloat16)


def is_odd():
    return lax.rem(lax.axis_index("plane"), 2) == 1


def pack_kernel(
    intensity, temp_hbm, cure_hbm, x_hbm, far, near, own, x_parts, temp, cure, grey, sems
):
    rows, width, depth = intensity.shape
    copies = [
        pltpu.make_async_copy(intensity, grey, sems.at[0]),
        pltpu.make_async_copy(temp_hbm, temp, sems.at[1]),
        pltpu.make_async_copy(cure_hbm, cure, sems.at[2]),
        pltpu.make_async_copy(x_hbm, x_parts, sems.at[3]),
    ]
    for copy in copies:
        copy.start()
    for copy in copies:
        copy.wait()
    odd = is_odd()
    count = temp.shape[0]
    sides = (column_slot(temp, cure, 0), column_slot(temp, cure, count - GHOST))

    def send(left, right):
        for row in range(rows):
            left[row] = grey[row, :EDGE, :].astype(jnp.float32).astype(jnp.bfloat16)
            right[row] = grey[row, width - EDGE :, :].astype(jnp.float32).astype(jnp.bfloat16)
        for slot in range(temp.shape[1] // LANES):
            left[rows + slot] = sides[0][:, slot * LANES : (slot + 1) * LANES]
            right[rows + slot] = sides[1][:, slot * LANES : (slot + 1) * LANES]

    @pl.when(odd)
    def _():
        send(near, far)

    @pl.when(jnp.logical_not(odd))
    def _():
        send(far, near)

    for row in range(rows):
        own[row] = grey[row].astype(jnp.float32).astype(jnp.bfloat16)


def packed_rows(values, size, first):
    depth = values[0].shape[1]
    lane = lax.broadcasted_iota(jnp.int32, values[0].shape, 1)
    packed = None
    for block, value in enumerate(values):
        shift = (size * block - first) % depth
        moved = value if shift == 0 else pltpu.roll(value, shift, 1)
        packed = moved if block == 0 else jnp.where(lane >= size * block, moved, packed)
    return packed


def window_kernel(own, far, near, window, up):
    rows, width, depth = own.shape
    odd = is_odd()

    def fill(from_left, from_right):
        values = []
        for row in range(rows):
            half = (row % 2) * depth
            whole = jnp.concatenate([from_left[row], own[row], from_right[row]], axis=0)
            window[row // 2, :, half : half + depth] = whole
            values.append(whole.astype(jnp.float32))
        up[...] = packed_rows(values, FIRST, depth - FIRST).astype(jnp.bfloat16)

    @pl.when(odd)
    def _():
        fill(near, far)

    @pl.when(jnp.logical_not(odd))
    def _():
        fill(far, near)


def joined_columns(ref, rows):
    slots = [ref[slot].astype(jnp.float32) for slot in range(rows, ref.shape[0])]
    parts = jnp.concatenate(slots, axis=1)
    return (parts[0:8] + parts[8:16]) + parts[16:24]


def product(first, second):
    return jnp.dot(first, second, preferred_element_type=jnp.float32)


def along_rows(kind, values, row):
    total = None
    for source, value in enumerate(values):
        weight = tap(grad_taps(kind), source - row)
        if weight != 0.0:
            total = weight * value if total is None else total + weight * value
    return total


def weighted_products(three, weight):
    pairs = ((0, 0), (1, 1), (2, 2), (0, 1), (0, 2), (1, 2))
    first = [weight * value for value in three]
    return [first[a] * three[b] for a, b in pairs]


def inside_x(start, count, width):
    place = lax.axis_index("plane") * width - HALO * COARSE - R2 + start
    place = place + lax.broadcasted_iota(jnp.int32, (count, LANES), 0)
    inside = (place >= 0) & (place < lax.axis_size("plane") * width)
    return jnp.where(inside, 1.0, 0.0)


def block_sums(products, coarse, sx, index):
    part = product(products[index], coarse).astype(jnp.bfloat16)
    return product(sx, part)


def own_kernel(
    window, x_parts, bands_hbm, sums, edge, bands, across, filtered, grads, products, sem
):
    pairs, height, double = window.shape
    rows, depth = 2 * pairs, double // 2
    width = height - 2 * EDGE
    columns, cells, span_x, pad_x = sizes(width, depth)
    copy = pltpu.make_async_copy(bands_hbm, bands, sem.at[0])
    copy.start()
    x_bands_of = x_parts[: 2 * pad_x, :]
    for pair in range(pairs):
        result = product(x_bands_of, window[pair])
        across[2 * pair] = result[:, :depth]
        across[2 * pair + 1] = result[:, depth:]

    def filter_rows(group, carry):
        start = pl.multiple_of(group * 16, 16)
        kinds = [
            [across[row, pl.ds(kind * pad_x + start, 16), :] for row in range(rows)]
            for kind in range(2)
        ]
        for part in range(3):
            for row in range(rows):
                result = along_rows(ROW_KINDS[part], kinds[X_KINDS[part]], row)
                filtered[part, row, pl.ds(start, 16), :] = result.astype(jnp.bfloat16)
        return carry

    lax.fori_loop(0, pad_x // 16, filter_rows, 0)

    values = [
        window[row // 2, :, (row % 2) * depth : (row % 2 + 1) * depth].astype(jnp.float32)
        for row in range(rows)
    ]
    first = product(x_bands_of, packed_rows(values, FIRST, 0).astype(jnp.bfloat16))
    first = first.astype(jnp.bfloat16)
    copy.wait()
    for part in range(3):
        at = DEPTH_KINDS[part] * depth
        for row in range(rows):
            grads[part, row] = product(filtered[part, row], bands[at : at + depth, :])
        at = (4 + 2 * part) * depth
        kind = X_KINDS[part]
        values = first[kind * pad_x : (kind + 1) * pad_x]
        edge[part] = product(values, bands[at : at + depth, :]) + product(
            values, bands[at + depth : at + 2 * depth, :]
        )

    weights = product_weights(rows)
    is_last = lax.axis_index("depth") == lax.axis_size("depth") - 1
    place = lax.broadcasted_iota(jnp.int32, (16, depth), 1)
    complete = jnp.where((place < depth - R1) | is_last, 1.0, 0.0)

    def multiply(group, carry):
        start = pl.multiple_of(group * 16, 16)
        inside = inside_x(start, 16, width) * complete
        totals = None
        for row in range(rows):
            three = [grads[part, row, pl.ds(start, 16), :] for part in range(3)]
            terms = weighted_products(three, float(weights[row]))
            totals = terms if row == 0 else [a + b for a, b in zip(totals, terms)]
        for index in range(6):
            products[index, pl.ds(start, 16), :] = (totals[index] * inside).astype(jnp.bfloat16)
        return carry

    lax.fori_loop(0, pad_x // 16, multiply, 0)
    sx = x_parts[2 * pad_x :, :pad_x]
    for index in range(6):
        sums[index] = block_sums(products, bands[2 * depth : 3 * depth, :], sx, index)


def edge_kernel(
    width, temp, cure, below, far, near, sums, edge, x_parts, bands, out, products
):
    rows = below.shape[1] // FIRST
    depth = LANES
    columns, cells, span_x, pad_x = sizes(width, depth)
    depths, layer = lax.axis_size("depth"), lax.axis_index("depth")
    result = product(x_parts[: 2 * pad_x, :], below[...]).astype(jnp.bfloat16)
    three = []
    for part in range(3):
        at = (10 + 2 * part) * depth
        kind = X_KINDS[part]
        values = result[kind * pad_x : (kind + 1) * pad_x]
        three.append(
            edge[part]
            + product(values, bands[at : at + depth, :])
            + product(values, bands[at + depth : at + 2 * depth, :])
        )
    place = lax.rem(lax.broadcasted_iota(jnp.int32, (pad_x, LANES), 1), FIRST) - START
    inside = inside_x(0, pad_x, width) * jnp.where((place >= 0) | (layer > 0), 1.0, 0.0)
    for index, term in enumerate(weighted_products(three, inside)):
        products[index] = term.astype(jnp.bfloat16)
    sx = x_parts[2 * pad_x :, :pad_x]
    total = [
        sums[index] + block_sums(products, bands[3 * depth : 4 * depth, :], sx, index)
        for index in range(6)
    ]
    trace = total[0] + total[1] + total[2]
    lane = lax.broadcasted_iota(jnp.int32, trace.shape, 1)
    joined = [
        jnp.where(lane < HALF, a, pltpu.roll(b, HALF, 1))
        for a, b in ((trace, total[1]), (total[2], total[5]))
    ]

    count = temp.shape[0]
    lanes = temp.shape[1]
    pad = jnp.zeros((8 - 2 * GHOST, lanes), jnp.float32)
    own_first = jnp.concatenate([temp[0:GHOST, :], cure[0:GHOST, :], pad], axis=0)
    own_last = jnp.concatenate([temp[count - GHOST :, :], cure[count - GHOST :, :], pad], axis=0)
    odd = is_odd()
    outer, inner = joined_columns(far, rows), joined_columns(near, rows)
    left, right = jnp.where(odd, inner, outer), jnp.where(odd, outer, inner)
    relay = jnp.where(layer == 0, right, left)
    half = joined[0].shape[0]
    for index, values in enumerate(joined):
        at = slice(index * half, (index + 1) * half)
        out[at, 0:LANES] = values
        if lanes > LANES:
            out[at, LANES:] = jnp.zeros((half, lanes - LANES), jnp.float32)
    for index, values in enumerate((own_last, own_first, relay)):
        out[2 * half + 8 * index : 2 * half + 8 * index + 8, :] = values


def cure_kernel(cells, chunks, temp_in, cure_in, levels, plan, temp_out, cure_out, conduct_out):
    count, lanes = temp_in.shape
    parts = chunks.shape[0]
    planes, depths = lax.axis_size("plane"), lax.axis_size("depth")
    plane, layer = lax.axis_index("plane"), lax.axis_index("depth")
    height = count + 2 * HALO
    own = cells - BEFORE - AFTER
    half = (chunks.shape[1] - 24) // 2
    lane = lax.broadcasted_iota(jnp.int32, (16, lanes), 1)
    row = lax.broadcasted_iota(jnp.int32, (16, lanes), 0)

    sums = [jnp.zeros((16, lanes), jnp.float32) for _ in range(4)]
    for part in range(parts):
        first_cell = own * part - BEFORE
        here = (lane >= first_cell) & (lane < first_cell + cells)
        for index in range(4):
            chunk = chunks[part, (index // 2) * half : (index // 2 + 1) * half, :]
            chunk = pltpu.roll(chunk, lax.rem(half - layer * count, half), 0)[0:16]
            shift = (first_cell - (index % 2) * HALF) % lanes
            moved = chunk if shift == 0 else pltpu.roll(chunk, shift, 1)
            sums[index] = sums[index] + jnp.where(here, moved, 0.0)
    trace = sums[0]
    scale = (conduct_fiber - conduct_matrix) / (2.0 * trace + tensor_eps)
    conduct = [
        conduct_matrix + scale * (trace - sums[1]),
        -scale * sums[3],
        conduct_matrix + scale * (trace - sums[2]),
    ]
    for kind in range(3):
        conduct_out[kind] = conduct[kind][HALO : HALO + count]

    rank = (layer + parts - 1, layer + 1)
    start = (jnp.where(layer == 0, 16, 0), jnp.where(layer == parts - 1, 16, 8))
    before, after = [
        chunks[lax.rem(rank[side], parts), pl.ds(pl.multiple_of(2 * half + start[side], 8), 8), :]
        for side in range(2)
    ]
    spare = jnp.full((16 - count - 2 * GHOST, lanes), 0.5, jnp.float32)
    temp = jnp.concatenate([before[:GHOST], temp_in[...], after[:GHOST], 8.0 * spare], axis=0)
    cure = jnp.concatenate([before[GHOST : 2 * GHOST], cure_in[...], after[GHOST : 2 * GHOST], spare], axis=0)
    gap = GHOST - HALO
    xx, xz, zz = [pltpu.roll(part, gap, 0) for part in conduct]

    first = (plane == 0) & (layer == 0)
    last = (plane == planes - 1) & (layer == depths - 1)
    for step in range(STEPS):
        top, bottom = levels[plan[step, 0]], levels[plan[step, 1]]
        temp = jnp.where((row < GHOST) & first, temp[GHOST : GHOST + 1], temp)
        temp = jnp.where(
            (row >= GHOST + count) & last, temp[GHOST + count - 1 : GHOST + count], temp
        )
        cooler = jnp.where(lane == 0, top, pltpu.roll(temp, 1, 1))
        later = jnp.where(lane == lanes - 1, bottom, pltpu.roll(temp, lanes - 1, 1))
        slant = later - cooler
        second_x = pltpu.roll(temp, 15, 0) - 2.0 * temp + pltpu.roll(temp, 1, 0)
        second_z = later - 2.0 * temp + cooler
        cross = 0.25 * (pltpu.roll(slant, 15, 0) - pltpu.roll(slant, 1, 0))
        spread = xx * second_x + 2.0 * xz * cross + zz * second_z
        inverse = 1.0 / reference_temp - 1.0 / temp
        left = 1.0 - cure
        rate = rate_first * jnp.exp(energy_first * inverse) + rate_second * jnp.exp(
            energy_second * inverse
        ) * jnp.sqrt(cure)
        rate = rate * (left * jnp.sqrt(left))
        temp = temp + time_step * (spread + heat_release * rate)
        cure = cure + time_step * rate
    temp_out[...] = temp[GHOST : GHOST + count]
    cure_out[...] = cure[GHOST : GHOST + count]


def on_device(intensity, temp_start, cure_start, tool_levels, plan):
    rows, width, depth = intensity.shape
    count, lanes = temp_start.shape
    planes, depths = lax.axis_size("plane"), lax.axis_size("depth")
    columns, cells, span_x, pad_x = sizes(width, depth)
    bf16 = jnp.bfloat16
    slots = rows + lanes // LANES
    params = pltpu.CompilerParams(vmem_limit_bytes=24 * 1024 * 1024)
    vmem = pl.BlockSpec(memory_space=pltpu.VMEM)
    smem = pl.BlockSpec(memory_space=pltpu.SMEM)
    stay = pl.BlockSpec(memory_space=pltpu.HBM)

    fixed = lambda values: pltpu.with_memory_space_constraint(values, pltpu.HBM)
    coarse_x = coarse_x_bands(columns, width + 2 * EDGE, -(-columns // 16) * 16)
    x_hbm = jnp.asarray(as_bfloat16(np.concatenate([x_bands(width, depth), coarse_x])))
    far, near, own, x_parts, temp, cure = pl.pallas_call(
        pack_kernel,
        name="pack",
        out_shape=(
            pltpu.VMEM((slots, EDGE, depth), bf16),
            pltpu.VMEM((slots, EDGE, depth), bf16),
            pltpu.VMEM((rows, width, depth), bf16),
            pltpu.VMEM(x_hbm.shape, bf16),
            pltpu.VMEM((count, lanes), jnp.float32),
            pltpu.VMEM((count, lanes), jnp.float32),
        ),
        in_specs=[stay] * 4,
        scratch_shapes=[
            pltpu.VMEM((rows, width, depth), jnp.int32),
            pltpu.SemaphoreType.DMA((4,)),
        ],
        compiler_params=params,
    )(*[fixed(values) for values in (intensity, temp_start, cure_start, x_hbm)])

    def moved(values, pairs):
        index = [(p * depths + d, q * depths + e) for (p, d), (q, e) in pairs]
        return lax.ppermute(values, ("plane", "depth"), index)

    def swapped(values, first):
        pairs = [(p, p + 1) for p in range(first, planes - 1, 2)]
        pairs += [(q, p) for p, q in pairs]
        return moved(values, [((p, d), (q, d)) for p, q in pairs for d in range(depths)])

    far = swapped(far, 1)
    near = swapped(near, 0)

    span = width + 2 * EDGE
    window, up = pl.pallas_call(
        window_kernel,
        name="window",
        out_shape=(
            pltpu.VMEM((rows // 2, span, 2 * depth), bf16),
            pltpu.VMEM((span, depth), bf16),
        ),
        compiler_params=params,
    )(own, far, near)
    below = moved(up, [((p, d), (p, d + 1)) for p in range(planes) for d in range(depths - 1)])

    pieces = [*depth_bands(depth), *coarse_depth_bands(rows, depth)]
    for side in edge_bands(rows)[::-1]:
        for part in side:
            pieces += halves(part)
    bands_hbm = jnp.asarray(np.concatenate([as_bfloat16(piece) for piece in pieces]))
    sums, edge, bands = pl.pallas_call(
        own_kernel,
        name="own",
        out_shape=(
            pltpu.VMEM((6, x_hbm.shape[0] - 2 * pad_x, LANES), jnp.float32),
            pltpu.VMEM((3, pad_x, LANES), jnp.float32),
            pltpu.VMEM(bands_hbm.shape, bf16),
        ),
        in_specs=[vmem, vmem, stay],
        scratch_shapes=[
            pltpu.VMEM((rows, 2 * pad_x, depth), jnp.float32),
            pltpu.VMEM((3, rows, pad_x, depth), bf16),
            pltpu.VMEM((3, rows, pad_x, depth), jnp.float32),
            pltpu.VMEM((6, pad_x, depth), bf16),
            pltpu.SemaphoreType.DMA((1,)),
        ],
        cost_estimate=pl.CostEstimate(
            flops=4 * rows * pad_x * span * depth, bytes_accessed=4_000_000, transcendentals=0
        ),
        compiler_params=params,
    )(window, x_parts, fixed(bands_hbm))

    height = 2 * (x_hbm.shape[0] - 2 * pad_x) + 24
    chunks = pl.pallas_call(
        functools.partial(edge_kernel, width),
        name="edge",
        out_shape=jax.ShapeDtypeStruct((height, lanes), jnp.float32),
        scratch_shapes=[pltpu.VMEM((6, pad_x, depth), bf16)],
        compiler_params=params,
    )(temp, cure, below, far, near, sums, edge, x_parts, bands)

    chunks = lax.all_gather(chunks, "depth")

    return pl.pallas_call(
        functools.partial(cure_kernel, cells),
        name="cure",
        out_shape=(
            jax.ShapeDtypeStruct((count, lanes), jnp.float32),
            jax.ShapeDtypeStruct((count, lanes), jnp.float32),
            jax.ShapeDtypeStruct((3, count, lanes), jnp.float32),
        ),
        in_specs=[vmem, vmem, vmem, smem, smem],
        out_specs=(vmem, vmem, vmem),
        compiler_params=params,
    )(chunks, temp, cure, tool_levels, plan)


def solution(mesh):
    return jax.shard_map(
        on_device,
        mesh=mesh,
        in_specs=(
            P(None, "plane", "depth"),
            P(("plane", "depth"), None),
            P(("plane", "depth"), None),
            P(),
            P(),
        ),
        out_specs=(
            P(("plane", "depth"), None),
            P(("plane", "depth"), None),
            P(None, ("plane", "depth"), None),
        ),
        check_vma=False,
    )
```

```python
import functools

import jax
import jax.numpy as jnp
import ml_dtypes
import numpy as np
from jax import lax
from jax.experimental import pallas as pl
from jax.experimental.pallas import tpu as pltpu
from jax.sharding import PartitionSpec as P

ROWS = 8
R1 = 6
R2 = 10
COARSE = 4
STEPS = 3

sigma_grad = 2.0
sigma_tensor = 3.3
conduct_matrix = 0.3
conduct_fiber = 1.5
time_step = 0.25
heat_release = 0.4
rate_first = 0.15
rate_second = 0.6
energy_first = 30.0
energy_second = 25.0
reference_temp = 4.2
tensor_eps = 1e-06

EDGE = 32
LANES = 128
HALO = 2
GHOST = 3
PACK = 16
BACK = 8
BEFORE = 1
AFTER = -(-(R1 + R2) // COARSE)
HALF = LANES // 2
ROW_KINDS = (1, 0, 0)
X_KINDS = (0, 1, 0)
DEPTH_KINDS = (0, 0, 1)


def smooth_taps(radius, sigma):
    offsets = np.arange(-radius, radius + 1) * 1.0
    weights = np.exp(-0.5 * offsets * offsets / (sigma * sigma))
    return weights / weights.sum()


def slope_taps(radius, sigma):
    offsets = np.arange(-radius, radius + 1) * 1.0
    weights = np.exp(-0.5 * offsets * offsets / (sigma * sigma))
    return offsets * weights / np.sum(offsets * offsets * weights)


def row_weights(count, radius, sigma):
    taps = smooth_taps(radius, sigma)
    result = np.zeros(count)
    for source in range(count):
        for target in range(count):
            offset = target - source
            if abs(offset) <= radius:
                result[source] += taps[offset + radius]
    return result


def rounded(taps):
    best = None
    for factor in np.linspace(1.0, 2.0, 20001)[:-1]:
        near = (taps * factor).astype(np.float32).astype(ml_dtypes.bfloat16).astype(np.float64)
        error = np.abs(near / factor - taps).sum()
        if best is None or error < best[0]:
            best = (error, near, factor)
    return best[1], best[2]


def as_bfloat16(matrix):
    return matrix.astype(np.float32).astype(ml_dtypes.bfloat16)


def halves(matrix):
    high = as_bfloat16(matrix)
    return high, as_bfloat16(matrix - high.astype(np.float64))


def sizes(width, depth):
    columns = width // COARSE + 2 * HALO
    cells = depth // COARSE + BEFORE + AFTER
    side = HALO * COARSE + R2 + R1
    inner = -(-(width - 2 * R1) // 16) * 16
    return columns, cells, side, inner


def product_rows(width):
    columns, cells, side, inner = sizes(width, 0)
    places = [R1 + i if R1 + i < width - R1 else None for i in range(inner)]
    places += [R1 - side + i for i in range(side)] + [width - R1 + i for i in range(side)]
    return places


GRAD_TAPS = tuple(
    rounded(taps(R1, sigma_grad)) for taps in (smooth_taps, slope_taps)
)
GRAD_FACTOR = GRAD_TAPS[0][1] ** 2 * GRAD_TAPS[1][1]


def grad_taps(kind):
    return GRAD_TAPS[kind][0]


def tap(taps, offset):
    radius = (len(taps) - 1) // 2
    return float(taps[offset + radius]) if abs(offset) <= radius else 0.0


def x_bands(width):
    places = product_rows(width)
    bands = np.zeros((2, len(places), width + 2 * EDGE))
    for kind in range(2):
        for row, place in enumerate(places):
            if place is not None:
                first = place + EDGE - R1
                bands[kind, row, first : first + 2 * R1 + 1] = grad_taps(kind)
    return bands


def edge_bands(rows, depth):
    bands = np.zeros((2, 3, rows * PACK, rows * PACK))
    for part in range(3):
        row_taps, depth_taps = grad_taps(ROW_KINDS[part]), grad_taps(DEPTH_KINDS[part])
        for source in range(rows):
            for target in range(rows):
                row_tap = tap(row_taps, source - target)
                for near in range(-PACK, PACK):
                    side, lane = int(near >= 0), source * PACK + near % PACK
                    for place in range(-BACK, R1):
                        value = row_tap * tap(depth_taps, near - place)
                        bands[side, part, lane, target * PACK + BACK + place] = value
    return bands


def depth_bands(depth):
    bands = np.zeros((2, 2 * depth, 2 * depth))
    for kind in range(2):
        for place in range(depth):
            for near in range(max(place - R1, 0), min(place + R1 + 1, depth)):
                value = tap(grad_taps(kind), near - place)
                bands[kind, near, place] = bands[kind, depth + near, depth + place] = value
    return bands


def product_weights(rows):
    return row_weights(rows, R2, sigma_tensor) / (255.0 * GRAD_FACTOR) ** 2


def coarse_depth_bands(rows, depth):
    taps = smooth_taps(R2, sigma_tensor)
    weights = product_weights(rows)
    columns, cells, side, inner = sizes(0, depth)
    bands = np.zeros((2, depth, LANES))
    for cell in range(cells):
        for voxel in range(COARSE):
            place = (cell - BEFORE) * COARSE + voxel
            for near in range(max(place - R2, 0), min(place + R2 + 1, depth + R1)):
                value = tap(taps, near - place)
                if near < depth - BACK:
                    bands[0, near, cell] += value
                else:
                    for row in range(rows):
                        lane = row * PACK + near - depth + BACK
                        bands[1, lane, cell] += weights[row] * value
    return bands


def coarse_x_bands(width):
    taps = smooth_taps(R2, sigma_tensor)
    places = product_rows(width)
    columns, cells, side, inner = sizes(width, 0)
    bands = np.zeros((-(-columns // 16) * 16, len(places)))
    for column in range(columns):
        for voxel in range(COARSE):
            middle = (column - HALO) * COARSE + voxel
            for row, place in enumerate(places):
                if place is not None:
                    bands[column, row] += tap(taps, place - middle)
    return bands


def x_constants(width):
    columns, cells, side, inner = sizes(width, 0)
    bands, coarse = x_bands(width), coarse_x_bands(width)
    pieces = [
        bands[:, :inner].reshape(2 * inner, -1),
        bands[:, inner:].reshape(4 * side, -1),
        bands[:, :inner, EDGE : EDGE + width].reshape(2 * inner, -1),
        coarse,
        coarse[:, inner:],
    ]
    widest = max(piece.shape[1] for piece in pieces)
    padded = [np.pad(piece, ((0, 0), (0, widest - piece.shape[1]))) for piece in pieces]
    return as_bfloat16(np.concatenate(padded)), [len(piece) for piece in pieces]


def depth_constants(rows, depth):
    above = [[np.concatenate(halves(part)) for part in side] for side in edge_bands(rows, depth)]
    wide = [*depth_bands(depth)]
    wide += [np.concatenate([side[0], side[2]], axis=1) for side in above]
    narrow = [*coarse_depth_bands(rows, depth)] + [side[1] for side in above]
    return [np.concatenate([as_bfloat16(piece) for piece in pieces]) for pieces in (wide, narrow)]


def three_parts(values):
    high = values.astype(jnp.bfloat16).astype(jnp.float32)
    rest = values - high
    middle = rest.astype(jnp.bfloat16).astype(jnp.float32)
    return high, middle, (rest - middle).astype(jnp.bfloat16).astype(jnp.float32)


def column_slot(temp_ref, cure_ref, first):
    pad = jnp.zeros((8 - 2 * GHOST, temp_ref.shape[1]), jnp.float32)
    rows = pl.ds(first, GHOST)
    both = jnp.concatenate([temp_ref[rows, :], cure_ref[rows, :], pad], axis=0)
    high, middle, low = three_parts(both)
    return jnp.concatenate([high, middle, low, jnp.zeros_like(high)], axis=0).astype(jnp.bfloat16)


def is_odd():
    return lax.rem(lax.axis_index("plane"), 2) == 1


def pack_kernel(
    intensity, temp_hbm, cure_hbm, x_hbm, far, near, own, x_parts, temp, cure, grey, sems
):
    rows, width, depth = intensity.shape
    copies = [
        pltpu.make_async_copy(intensity, grey, sems.at[0]),
        pltpu.make_async_copy(temp_hbm, temp, sems.at[1]),
        pltpu.make_async_copy(cure_hbm, cure, sems.at[2]),
        pltpu.make_async_copy(x_hbm, x_parts, sems.at[3]),
    ]
    for copy in copies:
        copy.start()
    for copy in copies:
        copy.wait()
    odd = is_odd()
    count = temp.shape[0]
    sides = (column_slot(temp, cure, 0), column_slot(temp, cure, count - GHOST))

    def send(left, right):
        for row in range(rows):
            left[row] = grey[row, :EDGE, :].astype(jnp.float32).astype(jnp.bfloat16)
            right[row] = grey[row, width - EDGE :, :].astype(jnp.float32).astype(jnp.bfloat16)
        for slot in range(temp.shape[1] // LANES):
            left[rows + slot] = sides[0][:, slot * LANES : (slot + 1) * LANES]
            right[rows + slot] = sides[1][:, slot * LANES : (slot + 1) * LANES]

    @pl.when(odd)
    def _():
        send(near, far)

    @pl.when(jnp.logical_not(odd))
    def _():
        send(far, near)

    for row in range(rows):
        half = (row % 2) * depth
        own[row // 2, :, half : half + depth] = grey[row].astype(jnp.float32).astype(jnp.bfloat16)


def packed_rows(values, size, first):
    depth = values[0].shape[1]
    lane = lax.broadcasted_iota(jnp.int32, values[0].shape, 1)
    packed = None
    for block, value in enumerate(values):
        shift = (size * block - first) % depth
        moved = value if shift == 0 else pltpu.roll(value, shift, 1)
        packed = moved if block == 0 else jnp.where(lane >= size * block, moved, packed)
    return packed


def window_kernel(own, far, near, inner_sums, window, down):
    pairs, width, double = own.shape
    rows, depth = 2 * pairs, double // 2
    odd = is_odd()

    def fill(from_left, from_right):
        values = []
        for row in range(rows):
            half = (row % 2) * depth
            middle = own[row // 2, :, half : half + depth]
            whole = jnp.concatenate([from_left[row], middle, from_right[row]], axis=0)
            window[row // 2, :, half : half + depth] = whole
            values.append(whole.astype(jnp.float32))
        down[...] = packed_rows(values, PACK, 0).astype(jnp.bfloat16)

    @pl.when(odd)
    def _():
        fill(near, far)

    @pl.when(jnp.logical_not(odd))
    def _():
        fill(far, near)


def joined_columns(ref, rows):
    slots = [ref[slot].astype(jnp.float32) for slot in range(rows, ref.shape[0])]
    parts = jnp.concatenate(slots, axis=1)
    return (parts[0:8] + parts[8:16]) + parts[16:24]


def product(first, second):
    return jnp.dot(first, second, preferred_element_type=jnp.float32)


def along_rows(kind, values, row):
    total = None
    for source, value in enumerate(values):
        weight = tap(grad_taps(kind), source - row)
        if weight != 0.0:
            total = weight * value if total is None else total + weight * value
    return total


def weighted_products(three, weight):
    pairs = ((0, 0), (1, 1), (2, 2), (0, 1), (0, 2), (1, 2))
    first = [weight * value for value in three]
    return [first[a] * three[b] for a, b in pairs]


def side_mask(side, width):
    row = lax.broadcasted_iota(jnp.int32, (2 * side, LANES), 0)
    place = jnp.where(row < side, row + R1 - side, row + width - R1 - side)
    place = place + lax.axis_index("plane") * width
    inside = (place >= 0) & (place < lax.axis_size("plane") * width)
    return jnp.where(inside, 1.0, 0.0)


def all_sums(products, coarse, sx):
    kinds, count, lanes = products.shape
    along = product(products[...].reshape(kinds * count, lanes), coarse).astype(jnp.bfloat16)
    parts = [along[index * count : (index + 1) * count] for index in range(kinds)]
    return product(sx, jnp.concatenate(parts, axis=1))


def tensor_sums(window, bands, sx, mask, ready, wide, narrow, across, filtered, grads, products):
    pairs, height, double = window.shape
    rows, depth = 2 * pairs, double // 2
    count = bands.shape[0] // 2
    for pair in range(pairs):
        across[pair] = product(bands, window[pair])

    def filter_rows(group, carry):
        start = pl.multiple_of(group * 16, 16)
        kinds = [
            [
                across[row // 2, pl.ds(kind * count + start, 16), pl.ds((row % 2) * depth, depth)]
                for row in range(rows)
            ]
            for kind in range(2)
        ]
        for part in range(3):
            for row in range(rows):
                result = along_rows(ROW_KINDS[part], kinds[X_KINDS[part]], row)
                lanes = pl.ds((row % 2) * depth, depth)
                filtered[part, row // 2, pl.ds(start, 16), lanes] = result.astype(jnp.bfloat16)
        return carry

    lax.fori_loop(0, count // 16, filter_rows, 0)
    ready()
    for part in range(3):
        at = DEPTH_KINDS[part] * double
        for pair in range(pairs):
            grads[part, pair] = product(filtered[part, pair], wide[at : at + double, :])

    weights = product_weights(rows)
    first = lax.axis_index("depth") == 0
    place = lax.broadcasted_iota(jnp.int32, (16, depth), 1)
    complete = jnp.where((place >= R1) | first, 1.0, 0.0)

    def multiply(group, carry):
        start = pl.multiple_of(group * 16, 16)
        inside = complete if mask is None else complete * mask[pl.ds(start, 16), :]
        totals = None
        for row in range(rows):
            lanes = pl.ds((row % 2) * depth, depth)
            three = [grads[part, row // 2, pl.ds(start, 16), lanes] for part in range(3)]
            terms = weighted_products(three, float(weights[row]))
            totals = terms if row == 0 else [a + b for a, b in zip(totals, terms)]
        for index in range(6):
            products[index, pl.ds(start, 16), :] = (totals[index] * inside).astype(jnp.bfloat16)
        return carry

    lax.fori_loop(0, count // 16, multiply, 0)
    return all_sums(products, narrow[0:depth, :], sx)


def inner_kernel(
    starts, own, x_parts, wide_hbm, narrow_hbm, sums, wide, narrow, across, filtered, grads,
    products, sems,
):
    copies = [
        pltpu.make_async_copy(wide_hbm, wide, sems.at[0]),
        pltpu.make_async_copy(narrow_hbm, narrow, sems.at[1]),
    ]
    for copy in copies:
        copy.start()

    def ready():
        for copy in copies:
            copy.wait()

    width, count = own.shape[1], across.shape[1] // 2
    bands = x_parts[starts[2] : starts[3], :width]
    sx = x_parts[starts[3] : starts[4], :count]
    sums[...] = tensor_sums(
        own, bands, sx, None, ready, wide, narrow, across, filtered, grads, products
    )


def side_kernel(
    starts, window, x_parts, wide, narrow, inner_sums, sums, edge, across, filtered, grads,
    products, mask,
):
    pairs, height, double = window.shape
    rows, depth = 2 * pairs, double // 2
    count = across.shape[1] // 2
    mask[...] = side_mask(count // 2, height - 2 * EDGE)
    bands = x_parts[starts[1] : starts[2], :]
    sx = x_parts[starts[4] : starts[5], :count]
    sums[...] = inner_sums[...] + tensor_sums(
        window, bands, sx, mask, lambda: None, wide, narrow, across, filtered, grads, products
    )
    values = [
        window[row // 2, :, (row % 2) * depth : (row % 2 + 1) * depth].astype(jnp.float32)
        for row in range(rows)
    ]
    last = packed_rows(values, PACK, depth - PACK).astype(jnp.bfloat16)
    results = edge_gradients(starts, last, x_parts, wide, narrow, 0)
    for part in range(3):
        edge[part] = results[part]


def edge_gradients(starts, packed, x_parts, wide, narrow, side):
    result = product(x_parts[: starts[2], :], packed).astype(jnp.bfloat16)
    inner, outer = starts[1] // 2, (starts[2] - starts[1]) // 2
    kinds = []
    for kind in range(2):
        at, after = kind * inner, starts[1] + kind * outer
        both = jnp.concatenate([result[at : at + inner], result[after : after + outer]], axis=0)
        kinds.append(jnp.concatenate([both, both], axis=1))
    lanes = packed.shape[1]
    at = (4 + 2 * side) * lanes
    flat = product(kinds[0], wide[at : at + 2 * lanes, :])
    at = (2 + 2 * side) * lanes
    steep = product(kinds[1], narrow[at : at + 2 * lanes, :])
    return flat[:, :lanes], steep, flat[:, lanes:]


def edge_kernel(
    starts, width, temp, cure, above, far, near, sums, edge, x_parts, wide, narrow, out, products
):
    kinds, pad_x, depth = edge.shape
    rows = depth // PACK
    depths, layer = lax.axis_size("depth"), lax.axis_index("depth")
    side = (starts[2] - starts[1]) // 4
    results = edge_gradients(starts, above[...], x_parts, wide, narrow, 1)
    three = [edge[part] + results[part] for part in range(3)]
    place = lax.rem(lax.broadcasted_iota(jnp.int32, (pad_x, LANES), 1), PACK) - BACK
    inside = jnp.where((place < 0) | (layer < depths - 1), 1.0, 0.0)
    inner = jnp.ones((pad_x - 2 * side, LANES), jnp.float32)
    inside = inside * jnp.concatenate([inner, side_mask(side, width)], axis=0)
    for index, term in enumerate(weighted_products(three, inside)):
        products[index] = term.astype(jnp.bfloat16)
    sx = x_parts[starts[3] : starts[4], :pad_x]
    total = sums[...] + all_sums(products, narrow[depth : 2 * depth, :], sx)
    total = [total[:, index * LANES : (index + 1) * LANES] for index in range(6)]
    trace = total[0] + total[1] + total[2]
    lane = lax.broadcasted_iota(jnp.int32, trace.shape, 1)
    joined = [
        jnp.where(lane < HALF, a, pltpu.roll(b, HALF, 1))
        for a, b in ((trace, total[1]), (total[2], total[5]))
    ]

    count = temp.shape[0]
    lanes = temp.shape[1]
    pad = jnp.zeros((8 - 2 * GHOST, lanes), jnp.float32)
    own_first = jnp.concatenate([temp[0:GHOST, :], cure[0:GHOST, :], pad], axis=0)
    own_last = jnp.concatenate([temp[count - GHOST :, :], cure[count - GHOST :, :], pad], axis=0)
    odd = is_odd()
    outer, inner = joined_columns(far, rows), joined_columns(near, rows)
    left, right = jnp.where(odd, inner, outer), jnp.where(odd, outer, inner)
    height = count + 2 * HALO
    for target in range(out.shape[0]):
        piece = jnp.where(layer == target - 1, own_last, 0.0)
        piece = jnp.where(layer == target + 1, own_first, piece)
        if target == 0:
            piece = jnp.where(layer == depths - 1, left, piece)
        if target == out.shape[0] - 1:
            piece = jnp.where(layer == 0, right, piece)
        for index, values in enumerate(joined):
            at = index * height
            out[target, at : at + height, 0:LANES] = values[
                count * target : count * target + height
            ]
        if lanes > LANES:
            out[target, 0 : 2 * height, LANES:] = jnp.zeros((2 * height, lanes - LANES), jnp.float32)
        out[target, 2 * height : 2 * height + 2 * GHOST, :] = piece[0 : 2 * GHOST]
        spare = out.shape[1] - 2 * height - 2 * GHOST
        if spare:
            out[target, 2 * height + 2 * GHOST :, :] = jnp.zeros((spare, lanes), jnp.float32)


def cure_kernel(
    cells, chunks, temp_in, cure_in, levels, plan, temp_hbm, cure_hbm, conduct_hbm, temp_out,
    cure_out, conduct_out, sems,
):
    count, lanes = temp_in.shape
    parts = chunks.shape[0]
    planes, depths = lax.axis_size("plane"), lax.axis_size("depth")
    plane, layer = lax.axis_index("plane"), lax.axis_index("depth")
    height = count + 2 * HALO
    own = cells - BEFORE - AFTER
    lane = lax.broadcasted_iota(jnp.int32, (16, lanes), 1)
    row = lax.broadcasted_iota(jnp.int32, (16, lanes), 0)

    sums = [jnp.zeros((16, lanes), jnp.float32) for _ in range(4)]
    for part in range(parts):
        first_cell = own * part - BEFORE
        here = (lane >= first_cell) & (lane < first_cell + cells)
        for index in range(4):
            at = (index // 2) * height
            chunk = chunks[part, at : at + 16, :]
            shift = (first_cell - (index % 2) * HALF) % lanes
            moved = chunk if shift == 0 else pltpu.roll(chunk, shift, 1)
            sums[index] = sums[index] + jnp.where(here, moved, 0.0)
    trace = sums[0]
    scale = (conduct_fiber - conduct_matrix) / (2.0 * trace + tensor_eps)
    conduct = [
        conduct_matrix + scale * (trace - sums[1]),
        -scale * sums[3],
        conduct_matrix + scale * (trace - sums[2]),
    ]
    for kind in range(3):
        conduct_out[kind] = conduct[kind][HALO : HALO + count]
    copies = [
        pltpu.make_async_copy(conduct_out, conduct_hbm, sems.at[0]),
        pltpu.make_async_copy(temp_out, temp_hbm, sems.at[1]),
        pltpu.make_async_copy(cure_out, cure_hbm, sems.at[2]),
    ]
    copies[0].start()

    before = chunks[lax.rem(layer + parts - 1, parts)][2 * height : 2 * height + 2 * GHOST]
    after = chunks[lax.rem(layer + 1, parts)][2 * height : 2 * height + 2 * GHOST]
    spare = jnp.full((16 - count - 2 * GHOST, lanes), 0.5, jnp.float32)
    temp = jnp.concatenate([before[:GHOST], temp_in[...], after[:GHOST], 8.0 * spare], axis=0)
    cure = jnp.concatenate([before[GHOST:], cure_in[...], after[GHOST:], spare], axis=0)
    gap = GHOST - HALO
    xx, xz, zz = [pltpu.roll(part, gap, 0) for part in conduct]

    first = (plane == 0) & (layer == 0)
    last = (plane == planes - 1) & (layer == depths - 1)
    for step in range(STEPS):
        top, bottom = levels[plan[step, 0]], levels[plan[step, 1]]
        temp = jnp.where((row < GHOST) & first, temp[GHOST : GHOST + 1], temp)
        temp = jnp.where(
            (row >= GHOST + count) & last, temp[GHOST + count - 1 : GHOST + count], temp
        )
        cooler = jnp.where(lane == 0, top, pltpu.roll(temp, 1, 1))
        later = jnp.where(lane == lanes - 1, bottom, pltpu.roll(temp, lanes - 1, 1))
        slant = later - cooler
        second_x = pltpu.roll(temp, 15, 0) - 2.0 * temp + pltpu.roll(temp, 1, 0)
        second_z = later - 2.0 * temp + cooler
        cross = 0.25 * (pltpu.roll(slant, 15, 0) - pltpu.roll(slant, 1, 0))
        spread = xx * second_x + 2.0 * xz * cross + zz * second_z
        inverse = 1.0 / reference_temp - 1.0 / temp
        left = 1.0 - cure
        rate = rate_first * jnp.exp(energy_first * inverse) + rate_second * jnp.exp(
            energy_second * inverse
        ) * jnp.sqrt(cure)
        rate = rate * (left * jnp.sqrt(left))
        temp = temp + time_step * (spread + heat_release * rate)
        cure = cure + time_step * rate
    temp_out[...] = temp[GHOST : GHOST + count]
    cure_out[...] = cure[GHOST : GHOST + count]
    for copy in copies[1:]:
        copy.start()
    for copy in copies:
        copy.wait()


def on_device(intensity, temp_start, cure_start, tool_levels, plan):
    rows, width, depth = intensity.shape
    count, lanes = temp_start.shape
    planes, depths = lax.axis_size("plane"), lax.axis_size("depth")
    columns, cells, side, inner = sizes(width, depth)
    bf16 = jnp.bfloat16
    slots = rows + lanes // LANES
    params = pltpu.CompilerParams(vmem_limit_bytes=24 * 1024 * 1024)
    vmem = pl.BlockSpec(memory_space=pltpu.VMEM)
    smem = pl.BlockSpec(memory_space=pltpu.SMEM)
    stay = pl.BlockSpec(memory_space=pltpu.HBM)

    fixed = lambda values: pltpu.with_memory_space_constraint(values, pltpu.HBM)
    x_constant, lengths = x_constants(width)
    x_hbm = jnp.asarray(x_constant)
    starts = tuple(int(start) for start in np.cumsum([0] + lengths))
    far, near, own, x_parts, temp, cure = pl.pallas_call(
        pack_kernel,
        name="pack",
        out_shape=(
            pltpu.VMEM((slots, EDGE, depth), bf16),
            pltpu.VMEM((slots, EDGE, depth), bf16),
            pltpu.VMEM((rows // 2, width, 2 * depth), bf16),
            pltpu.VMEM(x_hbm.shape, bf16),
            pltpu.VMEM((count, lanes), jnp.float32),
            pltpu.VMEM((count, lanes), jnp.float32),
        ),
        in_specs=[stay] * 4,
        scratch_shapes=[
            pltpu.VMEM((rows, width, depth), jnp.int32),
            pltpu.SemaphoreType.DMA((4,)),
        ],
        compiler_params=params,
    )(*[fixed(values) for values in (intensity, temp_start, cure_start, x_hbm)])

    def moved(values, pairs):
        index = [(p * depths + d, q * depths + e) for (p, d), (q, e) in pairs]
        return lax.ppermute(values, ("plane", "depth"), index)

    def swapped(values, first):
        pairs = [(p, p + 1) for p in range(first, planes - 1, 2)]
        pairs += [(q, p) for p, q in pairs]
        return moved(values, [((p, d), (q, d)) for p, q in pairs for d in range(depths)])

    far = swapped(far, 1)
    near = swapped(near, 0)

    wide_hbm, narrow_hbm = [jnp.asarray(values) for values in depth_constants(rows, depth)]
    high = starts[4] - starts[3]

    def scratch(count):
        return [
            pltpu.VMEM((rows // 2, 2 * count, 2 * depth), jnp.float32),
            pltpu.VMEM((3, rows // 2, count, 2 * depth), bf16),
            pltpu.VMEM((3, rows // 2, count, 2 * depth), jnp.float32),
            pltpu.VMEM((6, count, depth), bf16),
        ]

    def cost(count):
        return pl.CostEstimate(
            flops=2 * rows * (2 * count) * 160 * depth * 4,
            bytes_accessed=4_000_000,
            transcendentals=0,
        )

    inner_sums, wide, narrow = pl.pallas_call(
        functools.partial(inner_kernel, starts),
        name="inner",
        out_shape=(
            pltpu.VMEM((high, 6 * LANES), jnp.float32),
            pltpu.VMEM(wide_hbm.shape, bf16),
            pltpu.VMEM(narrow_hbm.shape, bf16),
        ),
        in_specs=[vmem, vmem, stay, stay],
        scratch_shapes=scratch(inner) + [pltpu.SemaphoreType.DMA((2,))],
        cost_estimate=cost(inner),
        compiler_params=params,
    )(own, x_parts, fixed(wide_hbm), fixed(narrow_hbm))

    span = width + 2 * EDGE
    window, down = pl.pallas_call(
        window_kernel,
        name="window",
        out_shape=(
            pltpu.VMEM((rows // 2, span, 2 * depth), bf16),
            pltpu.VMEM((span, depth), bf16),
        ),
        compiler_params=params,
    )(own, far, near, inner_sums)
    above = moved(down, [((p, d + 1), (p, d)) for p in range(planes) for d in range(depths - 1)])

    sums, edge = pl.pallas_call(
        functools.partial(side_kernel, starts),
        name="side",
        out_shape=(
            pltpu.VMEM((high, 6 * LANES), jnp.float32),
            pltpu.VMEM((3, inner + 2 * side, LANES), jnp.float32),
        ),
        scratch_shapes=scratch(2 * side) + [pltpu.VMEM((2 * side, LANES), jnp.float32)],
        cost_estimate=cost(2 * side),
        compiler_params=params,
    )(window, x_parts, wide, narrow, inner_sums)

    height = -(-(2 * (count + 2 * HALO) + 2 * GHOST) // 8) * 8
    chunks = pl.pallas_call(
        functools.partial(edge_kernel, starts, width),
        name="edge",
        out_shape=pltpu.VMEM((depths, height, lanes), jnp.float32),
        scratch_shapes=[pltpu.VMEM((6, inner + 2 * side, depth), bf16)],
        compiler_params=params,
    )(temp, cure, above, far, near, sums, edge, x_parts, wide, narrow)

    chunks = lax.all_to_all(chunks, "depth", split_axis=0, concat_axis=0, tiled=True)

    return pl.pallas_call(
        functools.partial(cure_kernel, cells),
        name="cure",
        out_shape=(
            pltpu.HBM((count, lanes), jnp.float32),
            pltpu.HBM((count, lanes), jnp.float32),
            pltpu.HBM((3, count, lanes), jnp.float32),
        ),
        in_specs=[vmem, vmem, vmem, smem, smem],
        out_specs=(stay, stay, stay),
        scratch_shapes=[
            pltpu.VMEM((count, lanes), jnp.float32),
            pltpu.VMEM((count, lanes), jnp.float32),
            pltpu.VMEM((3, count, lanes), jnp.float32),
            pltpu.SemaphoreType.DMA((3,)),
        ],
        compiler_params=params,
    )(chunks, temp, cure, tool_levels, plan)


def solution(mesh):
    return jax.shard_map(
        on_device,
        mesh=mesh,
        in_specs=(
            P(None, "plane", "depth"),
            P(("plane", "depth"), None),
            P(("plane", "depth"), None),
            P(),
            P(),
        ),
        out_specs=(
            P(("plane", "depth"), None),
            P(("plane", "depth"), None),
            P(None, ("plane", "depth"), None),
        ),
        check_vma=False,
    )
```

```python
import functools

import jax
import jax.numpy as jnp
import ml_dtypes
import numpy as np
from jax import lax
from jax.experimental import pallas as pl
from jax.experimental.pallas import tpu as pltpu
from jax.sharding import PartitionSpec as P

ROWS = 8
R1 = 6
R2 = 10
COARSE = 4
STEPS = 3

sigma_grad = 2.0
sigma_tensor = 3.3
conduct_matrix = 0.3
conduct_fiber = 1.5
time_step = 0.25
heat_release = 0.4
rate_first = 0.15
rate_second = 0.6
energy_first = 30.0
energy_second = 25.0
reference_temp = 4.2
tensor_eps = 1e-06

LANES = 128
HALO = 2
EDGE = HALO * COARSE + R1 + R2
EARLY = 48
GHOST = 3
PACK = 16
BACK = 8
BEFORE = 1
AFTER = -(-(R1 + R2) // COARSE)
HALF = LANES // 2
ROW_KINDS = (1, 0, 0)
X_KINDS = (0, 1, 0)
DEPTH_KINDS = (0, 0, 1)


def smooth_taps(radius, sigma):
    offsets = np.arange(-radius, radius + 1) * 1.0
    weights = np.exp(-0.5 * offsets * offsets / (sigma * sigma))
    return weights / weights.sum()


def slope_taps(radius, sigma):
    offsets = np.arange(-radius, radius + 1) * 1.0
    weights = np.exp(-0.5 * offsets * offsets / (sigma * sigma))
    return offsets * weights / np.sum(offsets * offsets * weights)


def row_weights(count, radius, sigma):
    taps = smooth_taps(radius, sigma)
    result = np.zeros(count)
    for source in range(count):
        for target in range(count):
            offset = target - source
            if abs(offset) <= radius:
                result[source] += taps[offset + radius]
    return result


def rounded(taps):
    best = None
    for factor in np.linspace(1.0, 2.0, 20001)[:-1]:
        near = (taps * factor).astype(np.float32).astype(ml_dtypes.bfloat16).astype(np.float64)
        error = np.abs(near / factor - taps).sum()
        if best is None or error < best[0]:
            best = (error, near, factor)
    return best[1], best[2]


def as_bfloat16(matrix):
    return matrix.astype(np.float32).astype(ml_dtypes.bfloat16)


def halves(matrix):
    high = as_bfloat16(matrix)
    return high, as_bfloat16(matrix - high.astype(np.float64))


def sizes(width, depth):
    columns = width // COARSE + 2 * HALO
    cells = depth // COARSE + BEFORE + AFTER
    return columns, cells


def product_rows(width):
    places = [*range(R1, width - R1), *range(R1 - EDGE, R1), *range(width - R1, width + EDGE - R1)]
    return places + [None] * (-len(places) % 16)


GRAD_TAPS = tuple(
    rounded(taps(R1, sigma_grad)) for taps in (smooth_taps, slope_taps)
)
GRAD_FACTOR = GRAD_TAPS[0][1] ** 2 * GRAD_TAPS[1][1]


def grad_taps(kind):
    return GRAD_TAPS[kind][0]


def tap(taps, offset):
    radius = (len(taps) - 1) // 2
    return float(taps[offset + radius]) if abs(offset) <= radius else 0.0


def x_bands(width):
    places = product_rows(width)
    bands = np.zeros((2, len(places), width + 2 * EDGE))
    for kind in range(2):
        for row, place in enumerate(places):
            if place is not None:
                first = place + EDGE - R1
                bands[kind, row, first : first + 2 * R1 + 1] = grad_taps(kind)
    return bands


def edge_bands(rows, depth):
    bands = np.zeros((2, 3, rows * PACK, rows * PACK))
    for part in range(3):
        row_taps, depth_taps = grad_taps(ROW_KINDS[part]), grad_taps(DEPTH_KINDS[part])
        for source in range(rows):
            for target in range(rows):
                row_tap = tap(row_taps, source - target)
                for near in range(-PACK, PACK):
                    side, lane = int(near >= 0), source * PACK + near % PACK
                    for place in range(-BACK, R1):
                        value = row_tap * tap(depth_taps, near - place)
                        bands[side, part, lane, target * PACK + BACK + place] = value
    return bands


def depth_bands(depth):
    bands = np.zeros((2, 2 * depth, 2 * depth))
    for kind in range(2):
        for place in range(depth):
            for near in range(max(place - R1, 0), min(place + R1 + 1, depth)):
                value = tap(grad_taps(kind), near - place)
                bands[kind, near, place] = bands[kind, depth + near, depth + place] = value
    return bands


def product_weights(rows):
    return row_weights(rows, R2, sigma_tensor) / (255.0 * GRAD_FACTOR) ** 2


def coarse_depth_bands(rows, depth):
    taps = smooth_taps(R2, sigma_tensor)
    weights = product_weights(rows)
    columns, cells = sizes(0, depth)
    bands = np.zeros((2, depth, LANES))
    for cell in range(cells):
        for voxel in range(COARSE):
            place = (cell - BEFORE) * COARSE + voxel
            for near in range(max(place - R2, 0), min(place + R2 + 1, depth + R1)):
                value = tap(taps, near - place)
                if near < depth - BACK:
                    bands[0, near, cell] += value
                else:
                    for row in range(rows):
                        lane = row * PACK + near - depth + BACK
                        bands[1, lane, cell] += weights[row] * value
    return bands


def coarse_x_bands(width):
    taps = smooth_taps(R2, sigma_tensor)
    places = product_rows(width)
    columns, cells = sizes(width, 0)
    bands = np.zeros((-(-columns // 16) * 16, len(places)))
    for column in range(columns):
        for voxel in range(COARSE):
            middle = (column - HALO) * COARSE + voxel
            for row, place in enumerate(places):
                if place is not None:
                    bands[column, row] += tap(taps, place - middle)
    return bands


def x_constants(width):
    bands, coarse = x_bands(width), coarse_x_bands(width)
    pieces = [
        bands[:, :EARLY].reshape(2 * EARLY, -1),
        bands[:, EARLY:].reshape(2 * (bands.shape[1] - EARLY), -1),
        bands[:, :EARLY, EDGE : EDGE + width].reshape(2 * EARLY, -1),
        coarse,
        coarse[:, EARLY:],
    ]
    widest = max(piece.shape[1] for piece in pieces)
    padded = [np.pad(piece, ((0, 0), (0, widest - piece.shape[1]))) for piece in pieces]
    return as_bfloat16(np.concatenate(padded)), [len(piece) for piece in pieces]


def depth_constants(rows, depth):
    above = [[np.concatenate(halves(part)) for part in side] for side in edge_bands(rows, depth)]
    wide = [*depth_bands(depth)]
    wide += [np.concatenate([side[0], side[2]], axis=1) for side in above]
    narrow = [*coarse_depth_bands(rows, depth)] + [side[1] for side in above]
    return [np.concatenate([as_bfloat16(piece) for piece in pieces]) for pieces in (wide, narrow)]


def three_parts(values):
    high = values.astype(jnp.bfloat16).astype(jnp.float32)
    rest = values - high
    middle = rest.astype(jnp.bfloat16).astype(jnp.float32)
    return high, middle, (rest - middle).astype(jnp.bfloat16).astype(jnp.float32)


def column_slot(temp_ref, cure_ref, first):
    pad = jnp.zeros((8 - 2 * GHOST, temp_ref.shape[1]), jnp.float32)
    rows = pl.ds(first, GHOST)
    both = jnp.concatenate([temp_ref[rows, :], cure_ref[rows, :], pad], axis=0)
    high, middle, low = three_parts(both)
    return jnp.concatenate([high, middle, low, jnp.zeros_like(high)], axis=0).astype(jnp.bfloat16)


def is_odd():
    return lax.rem(lax.axis_index("plane"), 2) == 1


def pack_kernel(
    intensity, temp_hbm, cure_hbm, x_hbm, far, near, own, x_parts, temp, cure, grey, sems
):
    rows, width, depth = intensity.shape
    copies = [
        pltpu.make_async_copy(intensity, grey, sems.at[0]),
        pltpu.make_async_copy(temp_hbm, temp, sems.at[1]),
        pltpu.make_async_copy(cure_hbm, cure, sems.at[2]),
        pltpu.make_async_copy(x_hbm, x_parts, sems.at[3]),
    ]
    for copy in copies:
        copy.start()
    for copy in copies:
        copy.wait()
    odd = is_odd()
    count = temp.shape[0]
    sides = (column_slot(temp, cure, 0), column_slot(temp, cure, count - GHOST))

    def send(left, right):
        for place, target in ((0, left), (width - EDGE, right)):
            for pair in range(rows // 2):
                two = [grey[2 * pair + i, place : place + EDGE, :] for i in range(2)]
                two = jnp.concatenate(two, axis=0).astype(jnp.float32)
                target[2 * EDGE * pair : 2 * EDGE * (pair + 1), :] = two.astype(jnp.bfloat16)
        for slot in range(temp.shape[1] // LANES):
            at = rows * EDGE + 32 * slot
            left[at : at + 32, :] = sides[0][:, slot * LANES : (slot + 1) * LANES]
            right[at : at + 32, :] = sides[1][:, slot * LANES : (slot + 1) * LANES]

    @pl.when(odd)
    def _():
        send(near, far)

    @pl.when(jnp.logical_not(odd))
    def _():
        send(far, near)

    for row in range(rows):
        half = (row % 2) * depth
        own[row // 2, :, half : half + depth] = grey[row].astype(jnp.float32).astype(jnp.bfloat16)


def packed_rows(values, size, first):
    depth = values[0].shape[1]
    lane = lax.broadcasted_iota(jnp.int32, values[0].shape, 1)
    packed = None
    for block, value in enumerate(values):
        shift = (size * block - first) % depth
        moved = value if shift == 0 else pltpu.roll(value, shift, 1)
        packed = moved if block == 0 else jnp.where(lane >= size * block, moved, packed)
    return packed


def window_kernel(own, far, near, early_sums, window, down):
    pairs, width, double = own.shape
    rows, depth = 2 * pairs, double // 2
    odd = is_odd()

    def edges_of(ref):
        two = [
            ref[2 * EDGE * pair : 2 * EDGE * (pair + 1), :].astype(jnp.float32)
            for pair in range(pairs)
        ]
        return [two[row // 2][row % 2 * EDGE : (row % 2 + 1) * EDGE] for row in range(rows)]

    def fill(from_left, from_right):
        lefts, rights, values = edges_of(from_left), edges_of(from_right), []
        for row in range(rows):
            half = (row % 2) * depth
            middle = own[row // 2, :, half : half + depth].astype(jnp.float32)
            whole = jnp.concatenate([lefts[row], middle, rights[row]], axis=0)
            window[row // 2, :, half : half + depth] = whole.astype(jnp.bfloat16)
            values.append(whole)
        down[...] = packed_rows(values, PACK, 0).astype(jnp.bfloat16)

    @pl.when(odd)
    def _():
        fill(near, far)

    @pl.when(jnp.logical_not(odd))
    def _():
        fill(far, near)


def joined_columns(ref, rows):
    slots = range(rows * EDGE, ref.shape[0], 32)
    parts = [ref[at : at + 32, :].astype(jnp.float32) for at in slots]
    parts = jnp.concatenate(parts, axis=1)
    return (parts[0:8] + parts[8:16]) + parts[16:24]


def product(first, second):
    return jnp.dot(first, second, preferred_element_type=jnp.float32)


def along_rows(kind, values, row):
    total = None
    for source, value in enumerate(values):
        weight = tap(grad_taps(kind), source - row)
        if weight != 0.0:
            total = weight * value if total is None else total + weight * value
    return total


def weighted_products(three, weight):
    pairs = ((0, 0), (1, 1), (2, 2), (0, 1), (0, 2), (1, 2))
    first = [weight * value for value in three]
    return [first[a] * three[b] for a, b in pairs]


def late_mask(count, width):
    row = lax.broadcasted_iota(jnp.int32, (count, LANES), 0)
    left = width - 2 * R1 - EARLY
    place = jnp.where(row < left + EDGE, row - left + R1 - EDGE, row - left - EDGE + width - R1)
    place = place + lax.axis_index("plane") * width
    inside = (place >= 0) & (place < lax.axis_size("plane") * width)
    return jnp.where(inside | (row < left), 1.0, 0.0)


def all_sums(products, coarse, sx):
    kinds, count, lanes = products.shape
    along = product(products[...].reshape(kinds * count, lanes), coarse).astype(jnp.bfloat16)
    parts = [along[index * count : (index + 1) * count] for index in range(kinds)]
    return product(sx, jnp.concatenate(parts, axis=1))


def tensor_sums(window, bands, sx, mask, ready, wide, narrow, across, filtered, grads, products):
    pairs, height, double = window.shape
    rows, depth = 2 * pairs, double // 2
    count = bands.shape[0] // 2
    for pair in range(pairs):
        across[pair] = product(bands, window[pair])

    def filter_rows(group, carry):
        start = pl.multiple_of(group * 16, 16)
        kinds = [
            [
                across[row // 2, pl.ds(kind * count + start, 16), pl.ds((row % 2) * depth, depth)]
                for row in range(rows)
            ]
            for kind in range(2)
        ]
        for part in range(3):
            for row in range(rows):
                result = along_rows(ROW_KINDS[part], kinds[X_KINDS[part]], row)
                lanes = pl.ds((row % 2) * depth, depth)
                filtered[part, row // 2, pl.ds(start, 16), lanes] = result.astype(jnp.bfloat16)
        return carry

    lax.fori_loop(0, count // 16, filter_rows, 0)
    ready()
    for part in range(3):
        at = DEPTH_KINDS[part] * double
        for pair in range(pairs):
            grads[part, pair] = product(filtered[part, pair], wide[at : at + double, :])

    weights = product_weights(rows)
    first = lax.axis_index("depth") == 0
    place = lax.broadcasted_iota(jnp.int32, (16, depth), 1)
    complete = jnp.where((place >= R1) | first, 1.0, 0.0)

    def multiply(group, carry):
        start = pl.multiple_of(group * 16, 16)
        inside = complete if mask is None else complete * mask[pl.ds(start, 16), :]
        totals = None
        for row in range(rows):
            lanes = pl.ds((row % 2) * depth, depth)
            three = [grads[part, row // 2, pl.ds(start, 16), lanes] for part in range(3)]
            terms = weighted_products(three, float(weights[row]))
            totals = terms if row == 0 else [a + b for a, b in zip(totals, terms)]
        for index in range(6):
            products[index, pl.ds(start, 16), :] = (totals[index] * inside).astype(jnp.bfloat16)
        return carry

    lax.fori_loop(0, count // 16, multiply, 0)
    return all_sums(products, narrow[0:depth, :], sx)


def early_kernel(
    starts, own, x_parts, wide_hbm, narrow_hbm, sums, wide, narrow, across, filtered, grads,
    products, sems,
):
    copies = [
        pltpu.make_async_copy(wide_hbm, wide, sems.at[0]),
        pltpu.make_async_copy(narrow_hbm, narrow, sems.at[1]),
    ]
    for copy in copies:
        copy.start()

    def ready():
        for copy in copies:
            copy.wait()

    width, count = own.shape[1], across.shape[1] // 2
    bands = x_parts[starts[2] : starts[3], :width]
    sx = x_parts[starts[3] : starts[4], :count]
    sums[...] = tensor_sums(
        own, bands, sx, None, ready, wide, narrow, across, filtered, grads, products
    )


def late_kernel(
    starts, window, x_parts, wide, narrow, early_sums, sums, edge, across, filtered, grads,
    products, mask,
):
    pairs, height, double = window.shape
    rows, depth = 2 * pairs, double // 2
    count = across.shape[1] // 2
    mask[...] = late_mask(count, height - 2 * EDGE)
    bands = x_parts[starts[1] : starts[2], :height]
    sx = x_parts[starts[4] : starts[5], :count]
    sums[...] = early_sums[...] + tensor_sums(
        window, bands, sx, mask, lambda: None, wide, narrow, across, filtered, grads, products
    )
    values = [
        window[row // 2, :, (row % 2) * depth : (row % 2 + 1) * depth].astype(jnp.float32)
        for row in range(rows)
    ]
    last = packed_rows(values, PACK, depth - PACK).astype(jnp.bfloat16)
    results = edge_gradients(starts, last, x_parts, wide, narrow, 0)
    for part in range(3):
        edge[part] = results[part]


def edge_gradients(starts, packed, x_parts, wide, narrow, side):
    result = product(x_parts[: starts[2], : packed.shape[0]], packed).astype(jnp.bfloat16)
    inner, outer = starts[1] // 2, (starts[2] - starts[1]) // 2
    kinds = []
    for kind in range(2):
        at, after = kind * inner, starts[1] + kind * outer
        both = jnp.concatenate([result[at : at + inner], result[after : after + outer]], axis=0)
        kinds.append(jnp.concatenate([both, both], axis=1))
    lanes = packed.shape[1]
    at = (4 + 2 * side) * lanes
    flat = product(kinds[0], wide[at : at + 2 * lanes, :])
    at = (2 + 2 * side) * lanes
    steep = product(kinds[1], narrow[at : at + 2 * lanes, :])
    return flat[:, :lanes], steep, flat[:, lanes:]


def edge_kernel(
    starts, width, temp, cure, above, far, near, sums, edge, x_parts, wide, narrow, out, products
):
    kinds, pad_x, depth = edge.shape
    rows = depth // PACK
    depths, layer = lax.axis_size("depth"), lax.axis_index("depth")
    results = edge_gradients(starts, above[...], x_parts, wide, narrow, 1)
    three = [edge[part] + results[part] for part in range(3)]
    place = lax.rem(lax.broadcasted_iota(jnp.int32, (pad_x, LANES), 1), PACK) - BACK
    inside = jnp.where((place < 0) | (layer < depths - 1), 1.0, 0.0)
    mask = [jnp.ones((EARLY, LANES), jnp.float32), late_mask(pad_x - EARLY, width)]
    inside = inside * jnp.concatenate(mask, axis=0)
    for index, term in enumerate(weighted_products(three, inside)):
        products[index] = term.astype(jnp.bfloat16)
    sx = x_parts[starts[3] : starts[4], :pad_x]
    total = sums[...] + all_sums(products, narrow[depth : 2 * depth, :], sx)
    total = [total[:, index * LANES : (index + 1) * LANES] for index in range(6)]
    trace = total[0] + total[1] + total[2]
    lane = lax.broadcasted_iota(jnp.int32, trace.shape, 1)
    joined = [
        jnp.where(lane < HALF, a, pltpu.roll(b, HALF, 1))
        for a, b in ((trace, total[1]), (total[2], total[5]))
    ]

    count = temp.shape[0]
    lanes = temp.shape[1]
    pad = jnp.zeros((8 - 2 * GHOST, lanes), jnp.float32)
    own_first = jnp.concatenate([temp[0:GHOST, :], cure[0:GHOST, :], pad], axis=0)
    own_last = jnp.concatenate([temp[count - GHOST :, :], cure[count - GHOST :, :], pad], axis=0)
    odd = is_odd()
    outer, inner = joined_columns(far, rows), joined_columns(near, rows)
    left, right = jnp.where(odd, inner, outer), jnp.where(odd, outer, inner)
    height = count + 2 * HALO
    for target in range(out.shape[0]):
        piece = jnp.where(layer == target - 1, own_last, 0.0)
        piece = jnp.where(layer == target + 1, own_first, piece)
        if target == 0:
            piece = jnp.where(layer == depths - 1, left, piece)
        if target == out.shape[0] - 1:
            piece = jnp.where(layer == 0, right, piece)
        for index, values in enumerate(joined):
            at = index * height
            out[target, at : at + height, 0:LANES] = values[
                count * target : count * target + height
            ]
        if lanes > LANES:
            out[target, 0 : 2 * height, LANES:] = jnp.zeros((2 * height, lanes - LANES), jnp.float32)
        out[target, 2 * height : 2 * height + 2 * GHOST, :] = piece[0 : 2 * GHOST]
        spare = out.shape[1] - 2 * height - 2 * GHOST
        if spare:
            out[target, 2 * height + 2 * GHOST :, :] = jnp.zeros((spare, lanes), jnp.float32)


def cure_kernel(
    cells, chunks, temp_in, cure_in, tools, temp_hbm, cure_hbm, conduct_hbm, temp_out,
    cure_out, conduct_out, sems,
):
    count, lanes = temp_in.shape
    parts = chunks.shape[0]
    planes, depths = lax.axis_size("plane"), lax.axis_size("depth")
    plane, layer = lax.axis_index("plane"), lax.axis_index("depth")
    height = count + 2 * HALO
    own = cells - BEFORE - AFTER
    lane = lax.broadcasted_iota(jnp.int32, (16, lanes), 1)
    row = lax.broadcasted_iota(jnp.int32, (16, lanes), 0)

    sums = [jnp.zeros((16, lanes), jnp.float32) for _ in range(4)]
    for part in range(parts):
        first_cell = own * part - BEFORE
        here = (lane >= first_cell) & (lane < first_cell + cells)
        for index in range(4):
            at = (index // 2) * height
            chunk = chunks[part, at : at + 16, :]
            shift = (first_cell - (index % 2) * HALF) % lanes
            moved = chunk if shift == 0 else pltpu.roll(chunk, shift, 1)
            sums[index] = sums[index] + jnp.where(here, moved, 0.0)
    trace = sums[0]
    scale = (conduct_fiber - conduct_matrix) / (2.0 * trace + tensor_eps)
    conduct = [
        conduct_matrix + scale * (trace - sums[1]),
        -scale * sums[3],
        conduct_matrix + scale * (trace - sums[2]),
    ]
    for kind in range(3):
        conduct_out[kind] = conduct[kind][HALO : HALO + count]
    copies = [
        pltpu.make_async_copy(conduct_out, conduct_hbm, sems.at[0]),
        pltpu.make_async_copy(temp_out, temp_hbm, sems.at[1]),
        pltpu.make_async_copy(cure_out, cure_hbm, sems.at[2]),
    ]
    copies[0].start()

    before = chunks[lax.rem(layer + parts - 1, parts)][2 * height : 2 * height + 2 * GHOST]
    after = chunks[lax.rem(layer + 1, parts)][2 * height : 2 * height + 2 * GHOST]
    spare = jnp.full((16 - count - 2 * GHOST, lanes), 0.5, jnp.float32)
    temp = jnp.concatenate([before[:GHOST], temp_in[...], after[:GHOST], 8.0 * spare], axis=0)
    cure = jnp.concatenate([before[GHOST:], cure_in[...], after[GHOST:], spare], axis=0)
    gap = GHOST - HALO
    xx, xz, zz = [pltpu.roll(part, gap, 0) for part in conduct]

    first = (plane == 0) & (layer == 0)
    last = (plane == planes - 1) & (layer == depths - 1)
    for step in range(STEPS):
        top, bottom = tools[2 * step : 2 * step + 1, :], tools[2 * step + 1 : 2 * step + 2, :]
        temp = jnp.where((row < GHOST) & first, temp[GHOST : GHOST + 1], temp)
        temp = jnp.where(
            (row >= GHOST + count) & last, temp[GHOST + count - 1 : GHOST + count], temp
        )
        cooler = jnp.where(lane == 0, top, pltpu.roll(temp, 1, 1))
        later = jnp.where(lane == lanes - 1, bottom, pltpu.roll(temp, lanes - 1, 1))
        slant = later - cooler
        second_x = pltpu.roll(temp, 15, 0) - 2.0 * temp + pltpu.roll(temp, 1, 0)
        second_z = later - 2.0 * temp + cooler
        cross = 0.25 * (pltpu.roll(slant, 15, 0) - pltpu.roll(slant, 1, 0))
        spread = xx * second_x + 2.0 * xz * cross + zz * second_z
        inverse = 1.0 / reference_temp - 1.0 / temp
        left = 1.0 - cure
        rate = rate_first * jnp.exp(energy_first * inverse) + rate_second * jnp.exp(
            energy_second * inverse
        ) * jnp.sqrt(cure)
        rate = rate * (left * jnp.sqrt(left))
        temp = temp + time_step * (spread + heat_release * rate)
        cure = cure + time_step * rate
    temp_out[...] = temp[GHOST : GHOST + count]
    cure_out[...] = cure[GHOST : GHOST + count]
    for copy in copies[1:]:
        copy.start()
    for copy in copies:
        copy.wait()


def on_device(intensity, temp_start, cure_start, tool_levels, plan):
    rows, width, depth = intensity.shape
    count, lanes = temp_start.shape
    planes, depths = lax.axis_size("plane"), lax.axis_size("depth")
    columns, cells = sizes(width, depth)
    bf16 = jnp.bfloat16
    slots = rows * EDGE + 32 * (lanes // LANES)
    params = pltpu.CompilerParams(vmem_limit_bytes=24 * 1024 * 1024)
    vmem = pl.BlockSpec(memory_space=pltpu.VMEM)
    stay = pl.BlockSpec(memory_space=pltpu.HBM)

    fixed = lambda values: pltpu.with_memory_space_constraint(values, pltpu.HBM)
    x_constant, lengths = x_constants(width)
    x_hbm = jnp.asarray(x_constant)
    starts = tuple(int(start) for start in np.cumsum([0] + lengths))
    far, near, own, x_parts, temp, cure = pl.pallas_call(
        pack_kernel,
        name="pack",
        out_shape=(
            pltpu.VMEM((slots, depth), bf16),
            pltpu.VMEM((slots, depth), bf16),
            pltpu.VMEM((rows // 2, width, 2 * depth), bf16),
            pltpu.VMEM(x_hbm.shape, bf16),
            pltpu.VMEM((count, lanes), jnp.float32),
            pltpu.VMEM((count, lanes), jnp.float32),
        ),
        in_specs=[stay] * 4,
        scratch_shapes=[
            pltpu.VMEM((rows, width, depth), jnp.int32),
            pltpu.SemaphoreType.DMA((4,)),
        ],
        compiler_params=params,
    )(*[fixed(values) for values in (intensity, temp_start, cure_start, x_hbm)])

    def moved(values, pairs):
        index = [(p * depths + d, q * depths + e) for (p, d), (q, e) in pairs]
        return lax.ppermute(values, ("plane", "depth"), index)

    def swapped(values, first):
        pairs = [(p, p + 1) for p in range(first, planes - 1, 2)]
        pairs += [(q, p) for p, q in pairs]
        return moved(values, [((p, d), (q, d)) for p, q in pairs for d in range(depths)])

    far = swapped(far, 1)
    near = swapped(near, 0)

    wide_hbm, narrow_hbm = [jnp.asarray(values) for values in depth_constants(rows, depth)]
    high = starts[4] - starts[3]
    late = (starts[2] - starts[1]) // 2

    def scratch(count):
        return [
            pltpu.VMEM((rows // 2, 2 * count, 2 * depth), jnp.float32),
            pltpu.VMEM((3, rows // 2, count, 2 * depth), bf16),
            pltpu.VMEM((3, rows // 2, count, 2 * depth), jnp.float32),
            pltpu.VMEM((6, count, depth), bf16),
        ]

    def cost(count):
        return pl.CostEstimate(
            flops=2 * rows * (2 * count) * 160 * depth * 4,
            bytes_accessed=4_000_000,
            transcendentals=0,
        )

    early_sums, wide, narrow = pl.pallas_call(
        functools.partial(early_kernel, starts),
        name="early",
        out_shape=(
            pltpu.VMEM((high, 6 * LANES), jnp.float32),
            pltpu.VMEM(wide_hbm.shape, bf16),
            pltpu.VMEM(narrow_hbm.shape, bf16),
        ),
        in_specs=[vmem, vmem, stay, stay],
        scratch_shapes=scratch(EARLY) + [pltpu.SemaphoreType.DMA((2,))],
        cost_estimate=cost(EARLY),
        compiler_params=params,
    )(own, x_parts, fixed(wide_hbm), fixed(narrow_hbm))

    span = width + 2 * EDGE
    window, down = pl.pallas_call(
        window_kernel,
        name="window",
        out_shape=(
            pltpu.VMEM((rows // 2, span, 2 * depth), bf16),
            pltpu.VMEM((span, depth), bf16),
        ),
        compiler_params=params,
    )(own, far, near, early_sums)
    above = moved(down, [((p, d + 1), (p, d)) for p in range(planes) for d in range(depths - 1)])

    sums, edge = pl.pallas_call(
        functools.partial(late_kernel, starts),
        name="late",
        out_shape=(
            pltpu.VMEM((high, 6 * LANES), jnp.float32),
            pltpu.VMEM((3, EARLY + late, LANES), jnp.float32),
        ),
        scratch_shapes=scratch(late) + [pltpu.VMEM((late, LANES), jnp.float32)],
        cost_estimate=cost(late),
        compiler_params=params,
    )(window, x_parts, wide, narrow, early_sums)

    height = -(-(2 * (count + 2 * HALO) + 2 * GHOST) // 8) * 8
    chunks = pl.pallas_call(
        functools.partial(edge_kernel, starts, width),
        name="edge",
        out_shape=pltpu.VMEM((depths, height, lanes), jnp.float32),
        scratch_shapes=[pltpu.VMEM((6, EARLY + late, depth), bf16)],
        compiler_params=params,
    )(temp, cure, above, far, near, sums, edge, x_parts, wide, narrow)

    faces = plan.reshape(2 * STEPS, 1) == jnp.arange(tool_levels.shape[0], dtype=jnp.int32)
    tools = jnp.sum(jnp.where(faces, tool_levels, jnp.zeros_like(tool_levels)), axis=1)
    tools = jnp.broadcast_to(tools[:, None], (2 * STEPS, lanes))

    chunks = lax.all_to_all(chunks, "depth", split_axis=0, concat_axis=0, tiled=True)

    return pl.pallas_call(
        functools.partial(cure_kernel, cells),
        name="cure",
        out_shape=(
            pltpu.HBM((count, lanes), jnp.float32),
            pltpu.HBM((count, lanes), jnp.float32),
            pltpu.HBM((3, count, lanes), jnp.float32),
        ),
        in_specs=[vmem, vmem, vmem, vmem],
        out_specs=(stay, stay, stay),
        scratch_shapes=[
            pltpu.VMEM((count, lanes), jnp.float32),
            pltpu.VMEM((count, lanes), jnp.float32),
            pltpu.VMEM((3, count, lanes), jnp.float32),
            pltpu.SemaphoreType.DMA((3,)),
        ],
        compiler_params=params,
    )(chunks, temp, cure, tools)


def solution(mesh):
    return jax.shard_map(
        on_device,
        mesh=mesh,
        in_specs=(
            P(None, "plane", "depth"),
            P(("plane", "depth"), None),
            P(("plane", "depth"), None),
            P(),
            P(),
        ),
        out_specs=(
            P(("plane", "depth"), None),
            P(("plane", "depth"), None),
            P(None, ("plane", "depth"), None),
        ),
        check_vma=False,
    )
```

```python
import functools

import jax
import jax.numpy as jnp
import ml_dtypes
import numpy as np
from jax import lax
from jax.experimental import pallas as pl
from jax.experimental.pallas import tpu as pltpu
from jax.sharding import PartitionSpec as P

ROWS = 8
R1 = 6
R2 = 10
COARSE = 4
STEPS = 3

sigma_grad = 2.0
sigma_tensor = 3.3
conduct_matrix = 0.3
conduct_fiber = 1.5
time_step = 0.25
heat_release = 0.4
rate_first = 0.15
rate_second = 0.6
energy_first = 30.0
energy_second = 25.0
reference_temp = 4.2
tensor_eps = 1e-06

LANES = 128
HALO = 2
EDGE = HALO * COARSE + R1 + R2
EARLY = 48
GHOST = 3
PACK = 16
BACK = 8
BEFORE = 1
AFTER = -(-(R1 + R2) // COARSE)
HALF = LANES // 2
ROW_KINDS = (1, 0, 0)
X_KINDS = (0, 1, 0)
DEPTH_KINDS = (0, 0, 1)


def smooth_taps(radius, sigma):
    offsets = np.arange(-radius, radius + 1) * 1.0
    weights = np.exp(-0.5 * offsets * offsets / (sigma * sigma))
    return weights / weights.sum()


def slope_taps(radius, sigma):
    offsets = np.arange(-radius, radius + 1) * 1.0
    weights = np.exp(-0.5 * offsets * offsets / (sigma * sigma))
    return offsets * weights / np.sum(offsets * offsets * weights)


def row_weights(count, radius, sigma):
    taps = smooth_taps(radius, sigma)
    result = np.zeros(count)
    for source in range(count):
        for target in range(count):
            offset = target - source
            if abs(offset) <= radius:
                result[source] += taps[offset + radius]
    return result


def rounded(taps):
    best = None
    for factor in np.linspace(1.0, 2.0, 20001)[:-1]:
        near = (taps * factor).astype(np.float32).astype(ml_dtypes.bfloat16).astype(np.float64)
        error = np.abs(near / factor - taps).sum()
        if best is None or error < best[0]:
            best = (error, near, factor)
    return best[1], best[2]


def as_bfloat16(matrix):
    return matrix.astype(np.float32).astype(ml_dtypes.bfloat16)


def halves(matrix):
    high = as_bfloat16(matrix)
    return high, as_bfloat16(matrix - high.astype(np.float64))


def sizes(width, depth):
    columns = width // COARSE + 2 * HALO
    cells = depth // COARSE + BEFORE + AFTER
    return columns, cells


def product_rows(width):
    places = [*range(R1, width - R1), *range(R1 - EDGE, R1), *range(width - R1, width + EDGE - R1)]
    return places + [None] * (-len(places) % 16)


GRAD_TAPS = tuple(
    rounded(taps(R1, sigma_grad)) for taps in (smooth_taps, slope_taps)
)
GRAD_FACTOR = GRAD_TAPS[0][1] ** 2 * GRAD_TAPS[1][1]


def grad_taps(kind):
    return GRAD_TAPS[kind][0]


def tap(taps, offset):
    radius = (len(taps) - 1) // 2
    return float(taps[offset + radius]) if abs(offset) <= radius else 0.0


def x_bands(width):
    places = product_rows(width)
    bands = np.zeros((2, len(places), width + 2 * EDGE))
    for kind in range(2):
        for row, place in enumerate(places):
            if place is not None:
                first = place + EDGE - R1
                bands[kind, row, first : first + 2 * R1 + 1] = grad_taps(kind)
    return bands


def edge_bands(rows, depth):
    bands = np.zeros((2, 3, rows * PACK, rows * PACK))
    for part in range(3):
        row_taps, depth_taps = grad_taps(ROW_KINDS[part]), grad_taps(DEPTH_KINDS[part])
        for source in range(rows):
            for target in range(rows):
                row_tap = tap(row_taps, source - target)
                for near in range(-PACK, PACK):
                    side, lane = int(near >= 0), source * PACK + near % PACK
                    for place in range(-BACK, R1):
                        value = row_tap * tap(depth_taps, near - place)
                        bands[side, part, lane, target * PACK + BACK + place] = value
    return bands


def depth_bands(depth):
    bands = np.zeros((2, depth, depth))
    for kind in range(2):
        for place in range(depth):
            for near in range(max(place - R1, 0), min(place + R1 + 1, depth)):
                bands[kind, near, place] = tap(grad_taps(kind), near - place)
    return bands


def product_weights(rows):
    return row_weights(rows, R2, sigma_tensor) / (255.0 * GRAD_FACTOR) ** 2


def coarse_depth_bands(rows, depth):
    taps = smooth_taps(R2, sigma_tensor)
    weights = product_weights(rows)
    columns, cells = sizes(0, depth)
    bands = np.zeros((2, depth, LANES))
    for cell in range(cells):
        for voxel in range(COARSE):
            place = (cell - BEFORE) * COARSE + voxel
            for near in range(max(place - R2, 0), min(place + R2 + 1, depth + R1)):
                value = tap(taps, near - place)
                if near < depth - BACK:
                    bands[0, near, cell] += value
                else:
                    for row in range(rows):
                        lane = row * PACK + near - depth + BACK
                        bands[1, lane, cell] += weights[row] * value
    return bands


def coarse_x_bands(width):
    taps = smooth_taps(R2, sigma_tensor)
    places = product_rows(width)
    columns, cells = sizes(width, 0)
    bands = np.zeros((-(-columns // 16) * 16, len(places)))
    for column in range(columns):
        for voxel in range(COARSE):
            middle = (column - HALO) * COARSE + voxel
            for row, place in enumerate(places):
                if place is not None:
                    bands[column, row] += tap(taps, place - middle)
    return bands


def x_constants(width):
    bands, coarse = x_bands(width), coarse_x_bands(width)
    pieces = [
        bands[:, :EARLY].reshape(2 * EARLY, -1),
        bands[:, EARLY:].reshape(2 * (bands.shape[1] - EARLY), -1),
        bands[:, :EARLY, EDGE : EDGE + width].reshape(2 * EARLY, -1),
        coarse,
        coarse[:, EARLY:],
    ]
    widest = max(piece.shape[1] for piece in pieces)
    padded = [np.pad(piece, ((0, 0), (0, widest - piece.shape[1]))) for piece in pieces]
    return as_bfloat16(np.concatenate(padded)), [len(piece) for piece in pieces]


def depth_constants(rows, depth):
    own = [*depth_bands(depth), *coarse_depth_bands(rows, depth)]
    above = [[np.concatenate(halves(part)) for part in side] for side in edge_bands(rows, depth)]
    wide = [np.concatenate([side[0], side[2]], axis=1) for side in above]
    narrow = [side[1] for side in above]
    return [as_bfloat16(np.concatenate(pieces)) for pieces in (own, wide, narrow)]


def three_parts(values):
    high = values.astype(jnp.bfloat16).astype(jnp.float32)
    rest = values - high
    middle = rest.astype(jnp.bfloat16).astype(jnp.float32)
    return high, middle, (rest - middle).astype(jnp.bfloat16).astype(jnp.float32)


def column_slot(temp_ref, cure_ref, first):
    pad = jnp.zeros((8 - 2 * GHOST, temp_ref.shape[1]), jnp.float32)
    rows = pl.ds(first, GHOST)
    both = jnp.concatenate([temp_ref[rows, :], cure_ref[rows, :], pad], axis=0)
    high, middle, low = three_parts(both)
    return jnp.concatenate([high, middle, low, jnp.zeros_like(high)], axis=0).astype(jnp.bfloat16)


def is_odd():
    return lax.rem(lax.axis_index("plane"), 2) == 1


def pack_kernel(
    intensity, temp_hbm, cure_hbm, x_hbm, z_hbm, far, near, own, x_parts, z_parts, temp, cure,
    grey, sems,
):
    rows, width, depth = intensity.shape
    copies = [
        pltpu.make_async_copy(intensity, grey, sems.at[0]),
        pltpu.make_async_copy(temp_hbm, temp, sems.at[1]),
        pltpu.make_async_copy(cure_hbm, cure, sems.at[2]),
        pltpu.make_async_copy(x_hbm, x_parts, sems.at[3]),
        pltpu.make_async_copy(z_hbm, z_parts, sems.at[4]),
    ]
    for copy in copies:
        copy.start()
    for copy in copies:
        copy.wait()
    odd = is_odd()
    count = temp.shape[0]
    sides = (column_slot(temp, cure, 0), column_slot(temp, cure, count - GHOST))

    def send(left, right):
        for place, target in ((0, left), (width - EDGE, right)):
            for pair in range(rows // 2):
                two = [grey[2 * pair + i, place : place + EDGE, :] for i in range(2)]
                two = jnp.concatenate(two, axis=0).astype(jnp.float32)
                target[2 * EDGE * pair : 2 * EDGE * (pair + 1), :] = two.astype(jnp.bfloat16)
        for slot in range(temp.shape[1] // LANES):
            at = rows * EDGE + 32 * slot
            left[at : at + 32, :] = sides[0][:, slot * LANES : (slot + 1) * LANES]
            right[at : at + 32, :] = sides[1][:, slot * LANES : (slot + 1) * LANES]

    @pl.when(odd)
    def _():
        send(near, far)

    @pl.when(jnp.logical_not(odd))
    def _():
        send(far, near)

    for row in range(rows):
        half = (row % 2) * depth
        own[row // 2, :, half : half + depth] = grey[row].astype(jnp.float32).astype(jnp.bfloat16)


def packed_rows(values, size, first):
    depth = values[0].shape[1]
    lane = lax.broadcasted_iota(jnp.int32, values[0].shape, 1)
    packed = None
    for block, value in enumerate(values):
        shift = (size * block - first) % depth
        moved = value if shift == 0 else pltpu.roll(value, shift, 1)
        packed = moved if block == 0 else jnp.where(lane >= size * block, moved, packed)
    return packed


def window_kernel(own, far, near, early_sums, window, down):
    pairs, width, double = own.shape
    rows, depth = 2 * pairs, double // 2
    odd = is_odd()

    def edges_of(ref):
        two = [
            ref[2 * EDGE * pair : 2 * EDGE * (pair + 1), :].astype(jnp.float32)
            for pair in range(pairs)
        ]
        return [two[row // 2][row % 2 * EDGE : (row % 2 + 1) * EDGE] for row in range(rows)]

    def fill(from_left, from_right):
        lefts, rights, values = edges_of(from_left), edges_of(from_right), []
        for row in range(rows):
            half = (row % 2) * depth
            middle = own[row // 2, :, half : half + depth].astype(jnp.float32)
            whole = jnp.concatenate([lefts[row], middle, rights[row]], axis=0)
            window[row // 2, :, half : half + depth] = whole.astype(jnp.bfloat16)
            values.append(whole)
        down[...] = packed_rows(values, PACK, 0).astype(jnp.bfloat16)

    @pl.when(odd)
    def _():
        fill(near, far)

    @pl.when(jnp.logical_not(odd))
    def _():
        fill(far, near)


def joined_columns(ref, rows):
    slots = range(rows * EDGE, ref.shape[0], 32)
    parts = [ref[at : at + 32, :].astype(jnp.float32) for at in slots]
    parts = jnp.concatenate(parts, axis=1)
    return (parts[0:8] + parts[8:16]) + parts[16:24]


def product(first, second):
    return jnp.dot(first, second, preferred_element_type=jnp.float32)


def along_rows(kind, values, row):
    total = None
    for source, value in enumerate(values):
        weight = tap(grad_taps(kind), source - row)
        if weight != 0.0:
            total = weight * value if total is None else total + weight * value
    return total


def weighted_products(three, weight):
    pairs = ((0, 0), (1, 1), (2, 2), (0, 1), (0, 2), (1, 2))
    first = [weight * value for value in three]
    return [first[a] * three[b] for a, b in pairs]


def late_mask(count, width):
    row = lax.broadcasted_iota(jnp.int32, (count, LANES), 0)
    left = width - 2 * R1 - EARLY
    place = jnp.where(row < left + EDGE, row - left + R1 - EDGE, row - left - EDGE + width - R1)
    place = place + lax.axis_index("plane") * width
    inside = (place >= 0) & (place < lax.axis_size("plane") * width)
    return jnp.where(inside | (row < left), 1.0, 0.0)


def all_sums(products, coarse, sx):
    kinds, count, lanes = products.shape
    side_by_side = jnp.concatenate([products[index] for index in range(kinds)], axis=1)
    along = product(sx, side_by_side).astype(jnp.bfloat16)
    parts = [along[:, index * lanes : (index + 1) * lanes] for index in range(kinds)]
    return product(jnp.concatenate(parts, axis=0), coarse)


def tensor_sums(window, bands, sx, mask, diagonal, z_parts, across, filtered, grads, products):
    pairs, height, double = window.shape
    rows, depth = 2 * pairs, double // 2
    count = bands.shape[0] // 2
    for pair in range(pairs):
        across[pair] = product(bands, window[pair])

    def filter_rows(group, carry):
        start = pl.multiple_of(group * 16, 16)
        kinds = [
            [
                across[row // 2, pl.ds(kind * count + start, 16), pl.ds((row % 2) * depth, depth)]
                for row in range(rows)
            ]
            for kind in range(2)
        ]
        for part in range(3):
            for row in range(rows):
                result = along_rows(ROW_KINDS[part], kinds[X_KINDS[part]], row)
                lanes = pl.ds((row % 2) * depth, depth)
                filtered[part, row // 2, pl.ds(start, 16), lanes] = result.astype(jnp.bfloat16)
        return carry

    lax.fori_loop(0, count // 16, filter_rows, 0)
    for part in range(3):
        at = DEPTH_KINDS[part] * double
        for pair in range(pairs):
            grads[part, pair] = product(filtered[part, pair], diagonal[at : at + double, :])

    weights = product_weights(rows)
    first = lax.axis_index("depth") == 0
    place = lax.broadcasted_iota(jnp.int32, (16, depth), 1)
    complete = jnp.where((place >= R1) | first, 1.0, 0.0)

    def multiply(group, carry):
        start = pl.multiple_of(group * 16, 16)
        inside = complete if mask is None else complete * mask[pl.ds(start, 16), :]
        totals = None
        for row in range(rows):
            lanes = pl.ds((row % 2) * depth, depth)
            three = [grads[part, row // 2, pl.ds(start, 16), lanes] for part in range(3)]
            terms = weighted_products(three, float(weights[row]))
            totals = terms if row == 0 else [a + b for a, b in zip(totals, terms)]
        for index in range(6):
            products[index, pl.ds(start, 16), :] = (totals[index] * inside).astype(jnp.bfloat16)
        return carry

    lax.fori_loop(0, count // 16, multiply, 0)
    return all_sums(products, z_parts[double : double + depth, :], sx)


def early_kernel(
    starts, own, x_parts, z_parts, sums, diagonal, across, filtered, grads, products
):
    pairs, width, double = own.shape
    depth = double // 2
    empty = jnp.zeros((depth, depth), jnp.bfloat16)
    for kind in range(2):
        for half in range(2):
            at = pl.ds(kind * double + half * depth, depth)
            band = z_parts[kind * depth : (kind + 1) * depth, :]
            diagonal[at, half * depth : (half + 1) * depth] = band
            diagonal[at, (1 - half) * depth : (2 - half) * depth] = empty
    bands = x_parts[starts[2] : starts[3], :width]
    sx = x_parts[starts[3] : starts[4], :EARLY]
    sums[...] = tensor_sums(
        own, bands, sx, None, diagonal, z_parts, across, filtered, grads, products
    )


def late_kernel(
    starts, window, x_parts, z_parts, diagonal, early_sums, wide_hbm, narrow_hbm, sums, edge,
    wide, narrow, across, filtered, grads, products, mask, sems,
):
    pairs, height, double = window.shape
    rows, depth = 2 * pairs, double // 2
    copies = [
        pltpu.make_async_copy(wide_hbm, wide, sems.at[0]),
        pltpu.make_async_copy(narrow_hbm, narrow, sems.at[1]),
    ]
    for copy in copies:
        copy.start()
    count = across.shape[1] // 2
    mask[...] = late_mask(count, height - 2 * EDGE)
    bands = x_parts[starts[1] : starts[2], :height]
    sx = x_parts[starts[4] : starts[5], :count]
    sums[...] = early_sums[...] + tensor_sums(
        window, bands, sx, mask, diagonal, z_parts, across, filtered, grads, products
    )
    values = [
        window[row // 2, :, (row % 2) * depth : (row % 2 + 1) * depth].astype(jnp.float32)
        for row in range(rows)
    ]
    last = packed_rows(values, PACK, depth - PACK).astype(jnp.bfloat16)
    for copy in copies:
        copy.wait()
    results = edge_gradients(starts, last, x_parts, wide, narrow, 0)
    for part in range(3):
        edge[part] = results[part]


def edge_gradients(starts, packed, x_parts, wide, narrow, side):
    result = product(x_parts[: starts[2], : packed.shape[0]], packed).astype(jnp.bfloat16)
    inner, outer = starts[1] // 2, (starts[2] - starts[1]) // 2
    kinds = []
    for kind in range(2):
        at, after = kind * inner, starts[1] + kind * outer
        both = jnp.concatenate([result[at : at + inner], result[after : after + outer]], axis=0)
        kinds.append(jnp.concatenate([both, both], axis=1))
    lanes = packed.shape[1]
    at = 2 * side * lanes
    flat = product(kinds[0], wide[at : at + 2 * lanes, :])
    steep = product(kinds[1], narrow[at : at + 2 * lanes, :])
    return flat[:, :lanes], steep, flat[:, lanes:]


def edge_kernel(
    starts, width, temp, cure, above, far, near, sums, edge, x_parts, z_parts, wide, narrow, out,
    products,
):
    kinds, pad_x, depth = edge.shape
    rows = depth // PACK
    depths, layer = lax.axis_size("depth"), lax.axis_index("depth")
    results = edge_gradients(starts, above[...], x_parts, wide, narrow, 1)
    three = [edge[part] + results[part] for part in range(3)]
    place = lax.rem(lax.broadcasted_iota(jnp.int32, (pad_x, LANES), 1), PACK) - BACK
    inside = jnp.where((place < 0) | (layer < depths - 1), 1.0, 0.0)
    mask = [jnp.ones((EARLY, LANES), jnp.float32), late_mask(pad_x - EARLY, width)]
    inside = inside * jnp.concatenate(mask, axis=0)
    for index, term in enumerate(weighted_products(three, inside)):
        products[index] = term.astype(jnp.bfloat16)
    sx = x_parts[starts[3] : starts[4], :pad_x]
    total = sums[...] + all_sums(products, z_parts[3 * depth : 4 * depth, :], sx)
    high = sx.shape[0]
    total = [total[index * high : (index + 1) * high] for index in range(6)]
    trace = total[0] + total[1] + total[2]
    lane = lax.broadcasted_iota(jnp.int32, trace.shape, 1)
    joined = [
        jnp.where(lane < HALF, a, pltpu.roll(b, HALF, 1))
        for a, b in ((trace, total[1]), (total[2], total[5]))
    ]

    count = temp.shape[0]
    lanes = temp.shape[1]
    pad = jnp.zeros((8 - 2 * GHOST, lanes), jnp.float32)
    own_first = jnp.concatenate([temp[0:GHOST, :], cure[0:GHOST, :], pad], axis=0)
    own_last = jnp.concatenate([temp[count - GHOST :, :], cure[count - GHOST :, :], pad], axis=0)
    odd = is_odd()
    outer, inner = joined_columns(far, rows), joined_columns(near, rows)
    left, right = jnp.where(odd, inner, outer), jnp.where(odd, outer, inner)
    height = count + 2 * HALO
    for target in range(out.shape[0]):
        piece = jnp.where(layer == target - 1, own_last, 0.0)
        piece = jnp.where(layer == target + 1, own_first, piece)
        if target == 0:
            piece = jnp.where(layer == depths - 1, left, piece)
        if target == out.shape[0] - 1:
            piece = jnp.where(layer == 0, right, piece)
        for index, values in enumerate(joined):
            at = index * height
            out[target, at : at + height, 0:LANES] = values[
                count * target : count * target + height
            ]
        if lanes > LANES:
            out[target, 0 : 2 * height, LANES:] = jnp.zeros((2 * height, lanes - LANES), jnp.float32)
        out[target, 2 * height : 2 * height + 2 * GHOST, :] = piece[0 : 2 * GHOST]
        spare = out.shape[1] - 2 * height - 2 * GHOST
        if spare:
            out[target, 2 * height + 2 * GHOST :, :] = jnp.zeros((spare, lanes), jnp.float32)


def cure_kernel(
    cells, chunks, temp_in, cure_in, tools, temp_hbm, cure_hbm, conduct_hbm, temp_out,
    cure_out, conduct_out, sems,
):
    count, lanes = temp_in.shape
    parts = chunks.shape[0]
    planes, depths = lax.axis_size("plane"), lax.axis_size("depth")
    plane, layer = lax.axis_index("plane"), lax.axis_index("depth")
    height = count + 2 * HALO
    own = cells - BEFORE - AFTER
    lane = lax.broadcasted_iota(jnp.int32, (16, lanes), 1)
    row = lax.broadcasted_iota(jnp.int32, (16, lanes), 0)

    sums = [jnp.zeros((16, lanes), jnp.float32) for _ in range(4)]
    for part in range(parts):
        first_cell = own * part - BEFORE
        here = (lane >= first_cell) & (lane < first_cell + cells)
        for index in range(4):
            at = (index // 2) * height
            chunk = chunks[part, at : at + 16, :]
            shift = (first_cell - (index % 2) * HALF) % lanes
            moved = chunk if shift == 0 else pltpu.roll(chunk, shift, 1)
            sums[index] = sums[index] + jnp.where(here, moved, 0.0)
    trace = sums[0]
    scale = (conduct_fiber - conduct_matrix) / (2.0 * trace + tensor_eps)
    conduct = [
        conduct_matrix + scale * (trace - sums[1]),
        -scale * sums[3],
        conduct_matrix + scale * (trace - sums[2]),
    ]
    for kind in range(3):
        conduct_out[kind] = conduct[kind][HALO : HALO + count]
    copies = [
        pltpu.make_async_copy(conduct_out, conduct_hbm, sems.at[0]),
        pltpu.make_async_copy(temp_out, temp_hbm, sems.at[1]),
        pltpu.make_async_copy(cure_out, cure_hbm, sems.at[2]),
    ]
    copies[0].start()

    before = chunks[lax.rem(layer + parts - 1, parts)][2 * height : 2 * height + 2 * GHOST]
    after = chunks[lax.rem(layer + 1, parts)][2 * height : 2 * height + 2 * GHOST]
    spare = jnp.full((16 - count - 2 * GHOST, lanes), 0.5, jnp.float32)
    temp = jnp.concatenate([before[:GHOST], temp_in[...], after[:GHOST], 8.0 * spare], axis=0)
    cure = jnp.concatenate([before[GHOST:], cure_in[...], after[GHOST:], spare], axis=0)
    gap = GHOST - HALO
    xx, xz, zz = [pltpu.roll(part, gap, 0) for part in conduct]

    first = (plane == 0) & (layer == 0)
    last = (plane == planes - 1) & (layer == depths - 1)
    for step in range(STEPS):
        top, bottom = tools[2 * step : 2 * step + 1, :], tools[2 * step + 1 : 2 * step + 2, :]
        temp = jnp.where((row < GHOST) & first, temp[GHOST : GHOST + 1], temp)
        temp = jnp.where(
            (row >= GHOST + count) & last, temp[GHOST + count - 1 : GHOST + count], temp
        )
        cooler = jnp.where(lane == 0, top, pltpu.roll(temp, 1, 1))
        later = jnp.where(lane == lanes - 1, bottom, pltpu.roll(temp, lanes - 1, 1))
        slant = later - cooler
        second_x = pltpu.roll(temp, 15, 0) - 2.0 * temp + pltpu.roll(temp, 1, 0)
        second_z = later - 2.0 * temp + cooler
        cross = 0.25 * (pltpu.roll(slant, 15, 0) - pltpu.roll(slant, 1, 0))
        spread = xx * second_x + 2.0 * xz * cross + zz * second_z
        inverse = 1.0 / reference_temp - 1.0 / temp
        left = 1.0 - cure
        rate = rate_first * jnp.exp(energy_first * inverse) + rate_second * jnp.exp(
            energy_second * inverse
        ) * jnp.sqrt(cure)
        rate = rate * (left * jnp.sqrt(left))
        temp = temp + time_step * (spread + heat_release * rate)
        cure = cure + time_step * rate
    temp_out[...] = temp[GHOST : GHOST + count]
    cure_out[...] = cure[GHOST : GHOST + count]
    for copy in copies[1:]:
        copy.start()
    for copy in copies:
        copy.wait()


def on_device(intensity, temp_start, cure_start, tool_levels, plan):
    rows, width, depth = intensity.shape
    count, lanes = temp_start.shape
    planes, depths = lax.axis_size("plane"), lax.axis_size("depth")
    columns, cells = sizes(width, depth)
    bf16 = jnp.bfloat16
    slots = rows * EDGE + 32 * (lanes // LANES)
    params = pltpu.CompilerParams(vmem_limit_bytes=24 * 1024 * 1024)
    vmem = pl.BlockSpec(memory_space=pltpu.VMEM)
    stay = pl.BlockSpec(memory_space=pltpu.HBM)

    fixed = lambda values: pltpu.with_memory_space_constraint(values, pltpu.HBM)
    x_constant, lengths = x_constants(width)
    x_hbm = jnp.asarray(x_constant)
    starts = tuple(int(start) for start in np.cumsum([0] + lengths))
    constants = [jnp.asarray(values) for values in depth_constants(rows, depth)]
    z_hbm, wide_hbm, narrow_hbm = constants
    far, near, own, x_parts, z_parts, temp, cure = pl.pallas_call(
        pack_kernel,
        name="pack",
        out_shape=(
            pltpu.VMEM((slots, depth), bf16),
            pltpu.VMEM((slots, depth), bf16),
            pltpu.VMEM((rows // 2, width, 2 * depth), bf16),
            pltpu.VMEM(x_hbm.shape, bf16),
            pltpu.VMEM(z_hbm.shape, bf16),
            pltpu.VMEM((count, lanes), jnp.float32),
            pltpu.VMEM((count, lanes), jnp.float32),
        ),
        in_specs=[stay] * 5,
        scratch_shapes=[
            pltpu.VMEM((rows, width, depth), jnp.int32),
            pltpu.SemaphoreType.DMA((5,)),
        ],
        compiler_params=params,
    )(*[fixed(values) for values in (intensity, temp_start, cure_start, x_hbm, z_hbm)])

    def moved(values, pairs):
        index = [(p * depths + d, q * depths + e) for (p, d), (q, e) in pairs]
        return lax.ppermute(values, ("plane", "depth"), index)

    def swapped(values, first):
        pairs = [(p, p + 1) for p in range(first, planes - 1, 2)]
        pairs += [(q, p) for p, q in pairs]
        return moved(values, [((p, d), (q, d)) for p, q in pairs for d in range(depths)])

    far = swapped(far, 1)
    near = swapped(near, 0)

    high = starts[4] - starts[3]
    late = (starts[2] - starts[1]) // 2

    def scratch(count):
        return [
            pltpu.VMEM((rows // 2, 2 * count, 2 * depth), jnp.float32),
            pltpu.VMEM((3, rows // 2, count, 2 * depth), bf16),
            pltpu.VMEM((3, rows // 2, count, 2 * depth), jnp.float32),
            pltpu.VMEM((6, count, depth), bf16),
        ]

    def cost(count):
        return pl.CostEstimate(
            flops=2 * rows * (2 * count) * 160 * depth * 4,
            bytes_accessed=4_000_000,
            transcendentals=0,
        )

    early_sums, diagonal = pl.pallas_call(
        functools.partial(early_kernel, starts),
        name="early",
        out_shape=(
            pltpu.VMEM((6 * high, LANES), jnp.float32),
            pltpu.VMEM((4 * depth, 2 * depth), bf16),
        ),
        scratch_shapes=scratch(EARLY),
        cost_estimate=cost(EARLY),
        compiler_params=params,
    )(own, x_parts, z_parts)

    span = width + 2 * EDGE
    window, down = pl.pallas_call(
        window_kernel,
        name="window",
        out_shape=(
            pltpu.VMEM((rows // 2, span, 2 * depth), bf16),
            pltpu.VMEM((span, depth), bf16),
        ),
        compiler_params=params,
    )(own, far, near, early_sums)
    above = moved(down, [((p, d + 1), (p, d)) for p in range(planes) for d in range(depths - 1)])

    sums, edge, wide, narrow = pl.pallas_call(
        functools.partial(late_kernel, starts),
        name="late",
        out_shape=(
            pltpu.VMEM((6 * high, LANES), jnp.float32),
            pltpu.VMEM((3, EARLY + late, LANES), jnp.float32),
            pltpu.VMEM(wide_hbm.shape, bf16),
            pltpu.VMEM(narrow_hbm.shape, bf16),
        ),
        in_specs=[vmem] * 5 + [stay] * 2,
        scratch_shapes=scratch(late)
        + [pltpu.VMEM((late, LANES), jnp.float32), pltpu.SemaphoreType.DMA((2,))],
        cost_estimate=cost(late),
        compiler_params=params,
    )(window, x_parts, z_parts, diagonal, early_sums, fixed(wide_hbm), fixed(narrow_hbm))

    height = -(-(2 * (count + 2 * HALO) + 2 * GHOST) // 8) * 8
    chunks = pl.pallas_call(
        functools.partial(edge_kernel, starts, width),
        name="edge",
        out_shape=pltpu.VMEM((depths, height, lanes), jnp.float32),
        scratch_shapes=[pltpu.VMEM((6, EARLY + late, depth), bf16)],
        compiler_params=params,
    )(temp, cure, above, far, near, sums, edge, x_parts, z_parts, wide, narrow)

    faces = plan.reshape(2 * STEPS, 1) == jnp.arange(tool_levels.shape[0], dtype=jnp.int32)
    tools = jnp.sum(jnp.where(faces, tool_levels, jnp.zeros_like(tool_levels)), axis=1)
    tools = jnp.broadcast_to(tools[:, None], (2 * STEPS, lanes))

    chunks = lax.all_to_all(chunks, "depth", split_axis=0, concat_axis=0, tiled=True)

    return pl.pallas_call(
        functools.partial(cure_kernel, cells),
        name="cure",
        out_shape=(
            pltpu.HBM((count, lanes), jnp.float32),
            pltpu.HBM((count, lanes), jnp.float32),
            pltpu.HBM((3, count, lanes), jnp.float32),
        ),
        in_specs=[vmem, vmem, vmem, vmem],
        out_specs=(stay, stay, stay),
        scratch_shapes=[
            pltpu.VMEM((count, lanes), jnp.float32),
            pltpu.VMEM((count, lanes), jnp.float32),
            pltpu.VMEM((3, count, lanes), jnp.float32),
            pltpu.SemaphoreType.DMA((3,)),
        ],
        compiler_params=params,
    )(chunks, temp, cure, tools)


def solution(mesh):
    return jax.shard_map(
        on_device,
        mesh=mesh,
        in_specs=(
            P(None, "plane", "depth"),
            P(("plane", "depth"), None),
            P(("plane", "depth"), None),
            P(),
            P(),
        ),
        out_specs=(
            P(("plane", "depth"), None),
            P(("plane", "depth"), None),
            P(None, ("plane", "depth"), None),
        ),
        check_vma=False,
    )
```

```python
import functools

import jax
import jax.numpy as jnp
import ml_dtypes
import numpy as np
from jax import lax
from jax.experimental import pallas as pl
from jax.experimental.pallas import tpu as pltpu
from jax.sharding import PartitionSpec as P

ROWS = 8
R1 = 6
R2 = 10
COARSE = 4
STEPS = 3

sigma_grad = 2.0
sigma_tensor = 3.3
conduct_matrix = 0.3
conduct_fiber = 1.5
time_step = 0.25
heat_release = 0.4
rate_first = 0.15
rate_second = 0.6
energy_first = 30.0
energy_second = 25.0
reference_temp = 4.2
tensor_eps = 1e-06

LANES = 128
HALO = 2
EDGE = HALO * COARSE + R1 + R2
EARLY = 64
GHOST = 3
RIM = 2 * R1
BEFORE = -(-(R2 - R1) // COARSE)
AFTER = BEFORE
HALF = LANES // 2
ROW_KINDS = (1, 0, 0)
X_KINDS = (0, 1, 0)
DEPTH_KINDS = (0, 0, 1)


def smooth_taps(radius, sigma):
    offsets = np.arange(-radius, radius + 1) * 1.0
    weights = np.exp(-0.5 * offsets * offsets / (sigma * sigma))
    return weights / weights.sum()


def slope_taps(radius, sigma):
    offsets = np.arange(-radius, radius + 1) * 1.0
    weights = np.exp(-0.5 * offsets * offsets / (sigma * sigma))
    return offsets * weights / np.sum(offsets * offsets * weights)


def row_weights(count, radius, sigma):
    taps = smooth_taps(radius, sigma)
    result = np.zeros(count)
    for source in range(count):
        for target in range(count):
            offset = target - source
            if abs(offset) <= radius:
                result[source] += taps[offset + radius]
    return result


def rounded(taps):
    best = None
    for factor in np.linspace(1.0, 2.0, 20001)[:-1]:
        near = (taps * factor).astype(np.float32).astype(ml_dtypes.bfloat16).astype(np.float64)
        error = np.abs(near / factor - taps).sum()
        if best is None or error < best[0]:
            best = (error, near, factor)
    return best[1], best[2]


def as_bfloat16(matrix):
    return matrix.astype(np.float32).astype(ml_dtypes.bfloat16)


def halves(matrix):
    high = as_bfloat16(matrix)
    return high, as_bfloat16(matrix - high.astype(np.float64))


def sizes(width, depth):
    columns = width // COARSE + 2 * HALO
    cells = depth // COARSE + BEFORE + AFTER
    return columns, cells


def product_rows(width):
    places = [*range(R1, width - R1), *range(R1 - EDGE, R1), *range(width - R1, width + EDGE - R1)]
    return places + [None] * (-len(places) % 16)


GRAD_TAPS = tuple(
    rounded(taps(R1, sigma_grad)) for taps in (smooth_taps, slope_taps)
)
GRAD_FACTOR = GRAD_TAPS[0][1] ** 2 * GRAD_TAPS[1][1]


def grad_taps(kind):
    return GRAD_TAPS[kind][0]


def tap(taps, offset):
    radius = (len(taps) - 1) // 2
    return float(taps[offset + radius]) if abs(offset) <= radius else 0.0


def x_bands(width):
    places = product_rows(width)
    bands = np.zeros((2, len(places), width + 2 * EDGE))
    for kind in range(2):
        for row, place in enumerate(places):
            if place is not None:
                first = place + EDGE - R1
                bands[kind, row, first : first + 2 * R1 + 1] = grad_taps(kind)
    return bands


def rim_bands(rows):
    bands = np.zeros((3, 3 * LANES, LANES))
    for part in range(3):
        row_taps, depth_taps = grad_taps(ROW_KINDS[part]), grad_taps(DEPTH_KINDS[part])
        for source in range(rows):
            for target in range(rows):
                row_tap = tap(row_taps, source - target)
                for near in range(-RIM, RIM):
                    lane = source * RIM + near % RIM
                    if near >= 0:
                        lane += rows * RIM + LANES
                    for place in range(-R1, R1):
                        value = row_tap * tap(depth_taps, near - place)
                        bands[part, lane, target * 2 * R1 + R1 + place] = value
    return bands


def rim_cells(rows, depth, blocks):
    taps = smooth_taps(R2, sigma_tensor)
    weights = product_weights(rows)
    bands = np.zeros((blocks - 1, LANES, blocks * depth // COARSE))
    for boundary in range(blocks - 1):
        middle = (boundary + 1) * depth
        for cell in range(bands.shape[2]):
            for voxel in range(cell * COARSE, (cell + 1) * COARSE):
                for place in range(-R1, R1):
                    value = tap(taps, middle + place - voxel)
                    for row in range(rows):
                        bands[boundary, row * 2 * R1 + R1 + place, cell] += weights[row] * value
    return bands.reshape(-1, bands.shape[2])


def own_columns(count):
    products = (count + 2 * HALO) * COARSE + 2 * R2
    voxels = products + 2 * R1
    return -(-products // 16) * 16, -(-voxels // 8) * 8


def fold(voxels):
    return -(-voxels // 16) * 8


def rim_x_bands(count):
    products, voxels = own_columns(count)
    bands = np.zeros((2, products, -(-voxels // 16) * 16))
    valid = (count + 2 * HALO) * COARSE + 2 * R2
    for kind in range(2):
        for row in range(valid):
            bands[kind, row, row : row + 2 * R1 + 1] = grad_taps(kind)
    taps = smooth_taps(R2, sigma_tensor)
    coarse = np.zeros((16, products))
    for column in range(count + 2 * HALO):
        for voxel in range(column * COARSE, (column + 1) * COARSE):
            coarse[column, voxel : voxel + 2 * R2 + 1] += taps
    return bands.reshape(2 * products, -1), coarse


def depth_bands(depth):
    bands = np.zeros((2, depth, depth))
    for kind in range(2):
        for place in range(depth):
            for near in range(max(place - R1, 0), min(place + R1 + 1, depth)):
                bands[kind, near, place] = tap(grad_taps(kind), near - place)
    return bands


def product_weights(rows):
    return row_weights(rows, R2, sigma_tensor) / (255.0 * GRAD_FACTOR) ** 2


def coarse_depth_bands(depth):
    taps = smooth_taps(R2, sigma_tensor)
    columns, cells = sizes(0, depth)
    bands = np.zeros((depth, LANES))
    for cell in range(cells):
        for voxel in range(COARSE):
            place = (cell - BEFORE) * COARSE + voxel
            for near in range(max(place - R2, 0), min(place + R2 + 1, depth)):
                bands[near, cell] += tap(taps, near - place)
    return bands


def coarse_x_bands(width):
    taps = smooth_taps(R2, sigma_tensor)
    places = product_rows(width)
    columns, cells = sizes(width, 0)
    bands = np.zeros((-(-columns // 16) * 16, len(places)))
    for column in range(columns):
        for voxel in range(COARSE):
            middle = (column - HALO) * COARSE + voxel
            for row, place in enumerate(places):
                if place is not None:
                    bands[column, row] += tap(taps, place - middle)
    return bands


def stacked(*pieces):
    widest = max(piece.shape[1] for piece in pieces)
    padded = [np.pad(piece, ((0, 0), (0, widest - piece.shape[1]))) for piece in pieces]
    starts = np.cumsum([0] + [len(piece) for piece in pieces])
    return jnp.asarray(as_bfloat16(np.concatenate(padded))), tuple(int(start) for start in starts)


def two_parts(values):
    high = values.astype(jnp.bfloat16).astype(jnp.float32)
    return jnp.concatenate([high, (values - high).astype(jnp.bfloat16).astype(jnp.float32)], axis=0)


def joined(parts):
    half = parts.shape[0] // 2
    return parts[:half] + parts[half:]


def column_rows(temp, cure, first):
    pad = jnp.zeros((8 - 2 * GHOST, temp.shape[1]), jnp.float32)
    return jnp.concatenate(
        [temp[first : first + GHOST, :], cure[first : first + GHOST, :], pad], axis=0
    )


def is_odd():
    return lax.rem(lax.axis_index("plane"), 2) == 1


def pack_kernel(
    intensity, temp_hbm, cure_hbm, x_hbm, z_hbm, far, near, own, x_parts, z_parts, temp, cure,
    grey, sems,
):
    rows, width, depth = intensity.shape
    copies = [
        pltpu.make_async_copy(intensity, grey, sems.at[0]),
        pltpu.make_async_copy(temp_hbm, temp, sems.at[1]),
        pltpu.make_async_copy(cure_hbm, cure, sems.at[2]),
        pltpu.make_async_copy(x_hbm, x_parts, sems.at[3]),
        pltpu.make_async_copy(z_hbm, z_parts, sems.at[4]),
    ]
    for copy in copies:
        copy.start()
    for copy in copies:
        copy.wait()
    odd = is_odd()
    count = temp.shape[0]
    sides = [
        two_parts(column_rows(temp, cure, first)).astype(jnp.bfloat16)
        for first in (0, count - GHOST)
    ]

    def send(left, right):
        for place, target, columns in ((0, left, sides[0]), (width - EDGE, right, sides[1])):
            for pair in range(rows // 2):
                two = [grey[2 * pair + i, place : place + EDGE, :] for i in range(2)]
                two = jnp.concatenate(two, axis=0).astype(jnp.float32)
                target[2 * EDGE * pair : 2 * EDGE * (pair + 1), :] = two.astype(jnp.bfloat16)
            for slot in range(temp.shape[1] // LANES):
                at = rows * EDGE + 16 * slot
                target[at : at + 16, :] = columns[:, slot * LANES : (slot + 1) * LANES]

    @pl.when(odd)
    def _():
        send(near, far)

    @pl.when(jnp.logical_not(odd))
    def _():
        send(far, near)

    for row in range(rows):
        half = (row % 2) * depth
        own[row // 2, :, half : half + depth] = grey[row].astype(jnp.float32).astype(jnp.bfloat16)


def packed_rows(values, size, first):
    depth = values[0].shape[1]
    lane = lax.broadcasted_iota(jnp.int32, values[0].shape, 1)
    packed = None
    for block, value in enumerate(values):
        shift = (size * block - first) % depth
        moved = value if shift == 0 else pltpu.roll(value, shift, 1)
        packed = moved if block == 0 else jnp.where(lane >= size * block, moved, packed)
    return packed


def edges_of(ref, rows):
    two = [
        ref[2 * EDGE * pair : 2 * EDGE * (pair + 1), :].astype(jnp.float32)
        for pair in range(rows // 2)
    ]
    voxels = [two[row // 2][row % 2 * EDGE : (row % 2 + 1) * EDGE] for row in range(rows)]
    slots = range(rows * EDGE, ref.shape[0], 16)
    columns = [joined(ref[at : at + 16, :].astype(jnp.float32)) for at in slots]
    return voxels, jnp.concatenate(columns, axis=1)


def product(first, second):
    return jnp.dot(first, second, preferred_element_type=jnp.float32)


def along_rows(kind, values, row):
    total = None
    for source, value in enumerate(values):
        weight = tap(grad_taps(kind), source - row)
        if weight != 0.0:
            total = weight * value if total is None else total + weight * value
    return total


def weighted_products(three, weight):
    pairs = ((0, 0), (1, 1), (2, 2), (0, 1), (0, 2), (1, 2))
    first = [weight * value for value in three]
    return [first[a] * three[b] for a, b in pairs]


def late_mask(count, width):
    row = lax.broadcasted_iota(jnp.int32, (count, LANES), 0)
    left = width - 2 * R1 - EARLY
    place = jnp.where(row < left + EDGE, row - left + R1 - EDGE, row - left - EDGE + width - R1)
    place = place + lax.axis_index("plane") * width
    inside = (place >= 0) & (place < lax.axis_size("plane") * width)
    return jnp.where(inside | (row < left), 1.0, 0.0)


def all_sums(products, coarse, sx):
    kinds, count, lanes = products.shape
    side_by_side = jnp.concatenate([products[index] for index in range(kinds)], axis=1)
    along = product(sx, side_by_side).astype(jnp.bfloat16)
    parts = [along[:, index * lanes : (index + 1) * lanes] for index in range(kinds)]
    return product(jnp.concatenate(parts, axis=0), coarse)


def tensor_sums(window, bands, sx, mask, diagonal, z_parts, across, filtered, grads, products):
    pairs, height, double = window.shape
    rows, depth = 2 * pairs, double // 2
    count = bands.shape[0] // 2
    for pair in range(pairs):
        across[pair] = product(bands, window[pair])

    def filter_rows(group, carry):
        start = pl.multiple_of(group * 16, 16)
        kinds = [
            [
                across[row // 2, pl.ds(kind * count + start, 16), pl.ds((row % 2) * depth, depth)]
                for row in range(rows)
            ]
            for kind in range(2)
        ]
        for part in range(3):
            for row in range(rows):
                result = along_rows(ROW_KINDS[part], kinds[X_KINDS[part]], row)
                lanes = pl.ds((row % 2) * depth, depth)
                filtered[part, row // 2, pl.ds(start, 16), lanes] = result.astype(jnp.bfloat16)
        return carry

    lax.fori_loop(0, count // 16, filter_rows, 0)
    for part in range(3):
        at = DEPTH_KINDS[part] * double
        for pair in range(pairs):
            grads[part, pair] = product(filtered[part, pair], diagonal[at : at + double, :])

    weights = product_weights(rows)
    layer = lax.axis_index("depth")
    first, last = layer == 0, layer == lax.axis_size("depth") - 1
    place = lax.broadcasted_iota(jnp.int32, (16, depth), 1)
    complete = ((place >= R1) | first) & ((place < depth - R1) | last)
    complete = jnp.where(complete, 1.0, 0.0)

    def multiply(group, carry):
        start = pl.multiple_of(group * 16, 16)
        inside = complete if mask is None else complete * mask[pl.ds(start, 16), :]
        totals = None
        for row in range(rows):
            lanes = pl.ds((row % 2) * depth, depth)
            three = [grads[part, row // 2, pl.ds(start, 16), lanes] for part in range(3)]
            terms = weighted_products(three, float(weights[row]))
            totals = terms if row == 0 else [a + b for a, b in zip(totals, terms)]
        for index in range(6):
            products[index, pl.ds(start, 16), :] = (totals[index] * inside).astype(jnp.bfloat16)
        return carry

    lax.fori_loop(0, count // 16, multiply, 0)
    return all_sums(products, z_parts[double : double + depth, :], sx)


def early_kernel(*refs):
    starts, own, x_parts, z_parts, *rest = refs
    count = (len(rest) - 7) // 2
    constants, (sums, diagonal), held = rest[:count], rest[count : count + 2], rest[count + 2 : -5]
    across, filtered, grads, products, sems = rest[-5:]
    copies = [
        pltpu.make_async_copy(source, target, sems.at[index])
        for index, (source, target) in enumerate(zip(constants, held))
    ]
    for copy in copies:
        copy.start()
    pairs, width, double = own.shape
    depth = double // 2
    empty = jnp.zeros((depth, depth), jnp.bfloat16)
    for kind in range(2):
        for half in range(2):
            at = pl.ds(kind * double + half * depth, depth)
            band = z_parts[kind * depth : (kind + 1) * depth, :]
            diagonal[at, half * depth : (half + 1) * depth] = band
            diagonal[at, (1 - half) * depth : (2 - half) * depth] = empty
    bands = x_parts[starts[0] : starts[1], :width]
    sx = x_parts[starts[1] : starts[2], :EARLY]
    sums[...] = tensor_sums(
        own, bands, sx, None, diagonal, z_parts, across, filtered, grads, products
    )
    for copy in copies:
        copy.wait()


def late_kernel(
    starts, own, far, near, x_late, z_parts, diagonal, early_sums, temp, cure, out,
    window, across, filtered, grads, products, mask,
):
    pairs, width, double = own.shape
    rows, depth = 2 * pairs, double // 2
    count, lanes = temp.shape
    odd = is_odd()
    depths, layer = lax.axis_size("depth"), lax.axis_index("depth")
    outer, outer_columns = edges_of(far, rows)
    inner, inner_columns = edges_of(near, rows)
    values = []
    for row in range(rows):
        half = (row % 2) * depth
        middle = own[row // 2, :, half : half + depth].astype(jnp.float32)
        left = jnp.where(odd, inner[row], outer[row])
        right = jnp.where(odd, outer[row], inner[row])
        whole = jnp.concatenate([left, middle, right], axis=0)
        window[row // 2, :, half : half + depth] = whole.astype(jnp.bfloat16)
        values.append(whole)
    left = jnp.where(odd, inner_columns, outer_columns)
    right = jnp.where(odd, outer_columns, inner_columns)

    products_x, voxels = own_columns(count)
    folded, stride = fold(voxels), COARSE * count
    below = packed_rows(values, RIM, depth - RIM)
    above = pltpu.roll(packed_rows(values, RIM, 0), rows * RIM, 1)
    lane = lax.broadcasted_iota(jnp.int32, below.shape, 1)
    tiles = [jnp.where(lane < rows * RIM, below, above), above, pltpu.roll(above, HALF, 1)]
    missing = stride * (depths - 1) + voxels - below.shape[0]
    if missing > 0:
        spare = jnp.zeros((-(-missing // 8) * 8, LANES), jnp.float32)
        tiles = [jnp.concatenate([tile, spare], axis=0) for tile in tiles]

    late = across.shape[1] // 2
    mask[...] = late_mask(late, width)
    bands = x_late[starts[0] : starts[1], :]
    sx = x_late[starts[1] : starts[2], :late]
    sums = early_sums[...] + tensor_sums(
        window, bands, sx, mask, diagonal, z_parts, across, filtered, grads, products
    )
    high = sx.shape[0]
    total = [sums[index * high : (index + 1) * high] for index in range(6)]
    trace = total[0] + total[1] + total[2]
    lane = lax.broadcasted_iota(jnp.int32, trace.shape, 1)
    both = [
        jnp.where(lane < HALF, a, pltpu.roll(b, HALF, 1))
        for a, b in ((trace, total[1]), (total[2], total[5]))
    ]

    own_first, own_last = column_rows(temp, cure, 0), column_rows(temp, cure, count - GHOST)
    height = count + 2 * HALO
    half_lane = lax.broadcasted_iota(jnp.int32, (folded, LANES), 1) < HALF
    for target in range(out.shape[0]):
        at = stride * target
        second = jnp.where(
            half_lane,
            tiles[1][at : at + folded],
            tiles[2][at + voxels - folded : at + voxels],
        )
        rims = jnp.concatenate([tiles[0][at : at + voxels], second], axis=0)
        piece = jnp.where(layer == target - 1, own_last, 0.0)
        piece = jnp.where(layer == target + 1, own_first, piece)
        if target == 0:
            piece = jnp.where(layer == depths - 1, left, piece)
        if target == out.shape[0] - 1:
            piece = jnp.where(layer == 0, right, piece)
        pieces = [values[count * target : count * target + height] for values in both]
        for slot in range(lanes // LANES):
            pieces.append(piece[0 : 2 * GHOST, slot * LANES : (slot + 1) * LANES])
        filled = sum(part.shape[0] for part in pieces)
        pieces.append(jnp.zeros((32 - filled, LANES), jnp.float32))
        sent = jnp.concatenate([rims, two_parts(jnp.concatenate(pieces, axis=0))], axis=0)
        out[target] = sent.astype(jnp.bfloat16)


def rim_sums(chunks, count, starts, flat, steep, cells):
    parts = chunks.shape[0]
    rows_x, voxels = own_columns(count)
    folded = fold(voxels)
    tall = -(-voxels // 16) * 16
    spare = [jnp.zeros((tall - voxels, LANES), jnp.float32)] if tall > voxels else []
    tiles = []
    for part in range(parts):
        rims = chunks[part, 0 : voxels + folded, :].astype(jnp.float32)
        second = rims[voxels:]
        second = [second[: voxels - folded], pltpu.roll(second, HALF, 1)]
        for tile in ([rims[:voxels]], second):
            tiles.append(jnp.concatenate(tile + spare, axis=0).astype(jnp.bfloat16))
    result = product(
        steep[starts[1] : starts[2], :tall], jnp.concatenate(tiles, axis=1)
    ).astype(jnp.bfloat16)
    kinds = []
    for kind in range(2):
        values = result[kind * rows_x : (kind + 1) * rows_x]
        tile = lambda index: values[:, index * LANES : (index + 1) * LANES]
        stack = [
            jnp.concatenate([tile(2 * part), tile(2 * part + 2), tile(2 * part + 3)], axis=1)
            for part in range(parts - 1)
        ]
        kinds.append(jnp.concatenate(stack, axis=0))
    both = product(kinds[0], flat[...])
    three = (both[:, :LANES], product(kinds[1], steep[starts[0] : starts[1], :]), both[:, LANES:])

    index = lax.axis_index("plane") * lax.axis_size("depth") + lax.axis_index("depth")
    total = lax.axis_size("plane") * lax.axis_size("depth") * count * COARSE
    place = lax.rem(lax.broadcasted_iota(jnp.int32, three[0].shape, 0), rows_x)
    place = place + (index * count - HALO) * COARSE - R2
    inside = jnp.where((place >= 0) & (place < total), 1.0, 0.0)
    wide = []
    for term in weighted_products(three, inside):
        term = term.astype(jnp.bfloat16)
        wide += [term[part * rows_x : (part + 1) * rows_x] for part in range(parts - 1)]
    sx = steep[starts[2] : starts[3], :rows_x]
    along = product(sx, jnp.concatenate(wide, axis=1)).astype(jnp.bfloat16)
    step = (parts - 1) * LANES
    along = [along[:, kind * step : (kind + 1) * step] for kind in range(6)]
    sums = product(jnp.concatenate(along, axis=0), cells[...])
    return [sums[kind * 16 : (kind + 1) * 16] for kind in range(6)]


def cure_kernel(
    cells, starts, chunks, temp_in, cure_in, tools, flat, steep, rim_bands, temp_hbm, cure_hbm,
    conduct_hbm, temp_out, cure_out, conduct_out, sems,
):
    count, lanes = temp_in.shape
    parts = chunks.shape[0]
    planes, depths = lax.axis_size("plane"), lax.axis_size("depth")
    plane, layer = lax.axis_index("plane"), lax.axis_index("depth")
    height = count + 2 * HALO
    own = cells - BEFORE - AFTER
    lane = lax.broadcasted_iota(jnp.int32, (16, lanes), 1)
    row = lax.broadcasted_iota(jnp.int32, (16, lanes), 0)
    at_sums = chunks.shape[1] - 64

    near = rim_sums(chunks, count, starts, flat, steep, rim_bands)
    sums = [near[0] + near[1] + near[2], near[1], near[2], near[5]]
    for part in range(parts):
        first_cell = own * part - BEFORE
        here = (lane >= first_cell) & (lane < first_cell + cells)
        values = joined(chunks[part, at_sums:, :].astype(jnp.float32))
        for index in range(4):
            at = (index // 2) * height
            chunk = values[at : at + 16]
            if lanes > LANES:
                spare = jnp.zeros((16, lanes - LANES), jnp.float32)
                chunk = jnp.concatenate([chunk, spare], axis=1)
            shift = (first_cell - (index % 2) * HALF) % lanes
            moved = chunk if shift == 0 else pltpu.roll(chunk, shift, 1)
            sums[index] = sums[index] + jnp.where(here, moved, 0.0)
    trace = sums[0]
    scale = (conduct_fiber - conduct_matrix) / (2.0 * trace + tensor_eps)
    conduct = [
        conduct_matrix + scale * (trace - sums[1]),
        -scale * sums[3],
        conduct_matrix + scale * (trace - sums[2]),
    ]
    for kind in range(3):
        conduct_out[kind] = conduct[kind][HALO : HALO + count]
    copies = [
        pltpu.make_async_copy(conduct_out, conduct_hbm, sems.at[0]),
        pltpu.make_async_copy(temp_out, temp_hbm, sems.at[1]),
        pltpu.make_async_copy(cure_out, cure_hbm, sems.at[2]),
    ]
    copies[0].start()

    def columns_of(part):
        values = joined(chunks[part, at_sums:, :].astype(jnp.float32))
        slots = range(2 * height, 2 * height + 2 * GHOST * (lanes // LANES), 2 * GHOST)
        return jnp.concatenate([values[at : at + 2 * GHOST] for at in slots], axis=1)

    before = columns_of(lax.rem(layer + parts - 1, parts))
    after = columns_of(lax.rem(layer + 1, parts))
    spare = jnp.full((16 - count - 2 * GHOST, lanes), 0.5, jnp.float32)
    temp = jnp.concatenate([before[:GHOST], temp_in[...], after[:GHOST], 8.0 * spare], axis=0)
    cure = jnp.concatenate([before[GHOST:], cure_in[...], after[GHOST:], spare], axis=0)
    gap = GHOST - HALO
    xx, xz, zz = [pltpu.roll(part, gap, 0) for part in conduct]

    first = (plane == 0) & (layer == 0)
    last = (plane == planes - 1) & (layer == depths - 1)
    for step in range(STEPS):
        top, bottom = tools[2 * step : 2 * step + 1, :], tools[2 * step + 1 : 2 * step + 2, :]
        temp = jnp.where((row < GHOST) & first, temp[GHOST : GHOST + 1], temp)
        temp = jnp.where(
            (row >= GHOST + count) & last, temp[GHOST + count - 1 : GHOST + count], temp
        )
        cooler = jnp.where(lane == 0, top, pltpu.roll(temp, 1, 1))
        later = jnp.where(lane == lanes - 1, bottom, pltpu.roll(temp, lanes - 1, 1))
        slant = later - cooler
        second_x = pltpu.roll(temp, 15, 0) - 2.0 * temp + pltpu.roll(temp, 1, 0)
        second_z = later - 2.0 * temp + cooler
        cross = 0.25 * (pltpu.roll(slant, 15, 0) - pltpu.roll(slant, 1, 0))
        spread = xx * second_x + 2.0 * xz * cross + zz * second_z
        inverse = 1.0 / reference_temp - 1.0 / temp
        left = 1.0 - cure
        rate = rate_first * jnp.exp(energy_first * inverse) + rate_second * jnp.exp(
            energy_second * inverse
        ) * jnp.sqrt(cure)
        rate = rate * (left * jnp.sqrt(left))
        temp = temp + time_step * (spread + heat_release * rate)
        cure = cure + time_step * rate
    temp_out[...] = temp[GHOST : GHOST + count]
    cure_out[...] = cure[GHOST : GHOST + count]
    for copy in copies[1:]:
        copy.start()
    for copy in copies:
        copy.wait()


def on_device(intensity, temp_start, cure_start, tool_levels, plan):
    rows, width, depth = intensity.shape
    count, lanes = temp_start.shape
    planes, depths = lax.axis_size("plane"), lax.axis_size("depth")
    columns, cells = sizes(width, depth)
    bf16 = jnp.bfloat16
    slots = rows * EDGE + 16 * (lanes // LANES)
    params = pltpu.CompilerParams(vmem_limit_bytes=24 * 1024 * 1024)
    vmem = pl.BlockSpec(memory_space=pltpu.VMEM)
    stay = pl.BlockSpec(memory_space=pltpu.HBM)

    fixed = lambda values: pltpu.with_memory_space_constraint(values, pltpu.HBM)
    bands, coarse = x_bands(width), coarse_x_bands(width)
    late = bands.shape[1] - EARLY
    middle = bands[:, :EARLY, EDGE : EDGE + width]
    x_hbm, early_starts = stacked(middle.reshape(2 * EARLY, -1), coarse[:, :EARLY])
    z_hbm, _ = stacked(*depth_bands(depth), coarse_depth_bands(depth))
    x_late, late_starts = stacked(bands[:, EARLY:].reshape(2 * late, -1), coarse[:, EARLY:])
    rims = rim_bands(rows)
    flat, _ = stacked(np.concatenate([rims[0], rims[2]], axis=1))
    steep, rim_starts = stacked(rims[1], *rim_x_bands(count))
    cell_bands, _ = stacked(rim_cells(rows, depth, depths))
    constants = (x_late, flat, steep, cell_bands)
    far, near, own, x_parts, z_parts, temp, cure = pl.pallas_call(
        pack_kernel,
        name="pack",
        out_shape=(
            pltpu.VMEM((slots, depth), bf16),
            pltpu.VMEM((slots, depth), bf16),
            pltpu.VMEM((rows // 2, width, 2 * depth), bf16),
            pltpu.VMEM(x_hbm.shape, bf16),
            pltpu.VMEM(z_hbm.shape, bf16),
            pltpu.VMEM((count, lanes), jnp.float32),
            pltpu.VMEM((count, lanes), jnp.float32),
        ),
        in_specs=[stay] * 5,
        scratch_shapes=[
            pltpu.VMEM((rows, width, depth), jnp.int32),
            pltpu.SemaphoreType.DMA((5,)),
        ],
        compiler_params=params,
    )(*[fixed(values) for values in (intensity, temp_start, cure_start, x_hbm, z_hbm)])

    def moved(values, pairs):
        index = [(p * depths + d, q * depths + e) for (p, d), (q, e) in pairs]
        return lax.ppermute(values, ("plane", "depth"), index)

    def swapped(values, first):
        pairs = [(p, p + 1) for p in range(first, planes - 1, 2)]
        pairs += [(q, p) for p, q in pairs]
        return moved(values, [((p, d), (q, d)) for p, q in pairs for d in range(depths)])

    far = swapped(far, 1)
    near = swapped(near, 0)

    high = coarse.shape[0]

    def scratch(count):
        return [
            pltpu.VMEM((rows // 2, 2 * count, 2 * depth), jnp.float32),
            pltpu.VMEM((3, rows // 2, count, 2 * depth), bf16),
            pltpu.VMEM((3, rows // 2, count, 2 * depth), jnp.float32),
            pltpu.VMEM((6, count, depth), bf16),
        ]

    def cost(count):
        return pl.CostEstimate(
            flops=2 * rows * (2 * count) * 160 * depth * 4,
            bytes_accessed=4_000_000,
            transcendentals=0,
        )

    early_sums, diagonal, x_late, flat, steep, cell_bands = pl.pallas_call(
        functools.partial(early_kernel, early_starts),
        name="early",
        out_shape=(
            pltpu.VMEM((6 * high, LANES), jnp.float32),
            pltpu.VMEM((4 * depth, 2 * depth), bf16),
            *[pltpu.VMEM(values.shape, bf16) for values in constants],
        ),
        in_specs=[vmem] * 3 + [stay] * len(constants),
        scratch_shapes=scratch(EARLY) + [pltpu.SemaphoreType.DMA((len(constants),))],
        cost_estimate=cost(EARLY),
        compiler_params=params,
    )(own, x_parts, z_parts, *[fixed(values) for values in constants])

    products_x, voxels = own_columns(count)
    chunks = pl.pallas_call(
        functools.partial(late_kernel, late_starts),
        name="late",
        out_shape=pltpu.VMEM((depths, voxels + fold(voxels) + 64, LANES), bf16),
        scratch_shapes=[pltpu.VMEM((rows // 2, width + 2 * EDGE, 2 * depth), bf16)]
        + scratch(late)
        + [pltpu.VMEM((late, LANES), jnp.float32)],
        cost_estimate=cost(late),
        compiler_params=params,
    )(own, far, near, x_late, z_parts, diagonal, early_sums, temp, cure)

    faces = plan.reshape(2 * STEPS, 1) == jnp.arange(tool_levels.shape[0], dtype=jnp.int32)
    tools = jnp.sum(jnp.where(faces, tool_levels, jnp.zeros_like(tool_levels)), axis=1)
    tools = jnp.broadcast_to(tools[:, None], (2 * STEPS, lanes))

    chunks = lax.all_to_all(chunks, "depth", split_axis=0, concat_axis=0, tiled=True)

    return pl.pallas_call(
        functools.partial(cure_kernel, cells, rim_starts),
        name="cure",
        out_shape=(
            pltpu.HBM((count, lanes), jnp.float32),
            pltpu.HBM((count, lanes), jnp.float32),
            pltpu.HBM((3, count, lanes), jnp.float32),
        ),
        in_specs=[vmem] * 7,
        out_specs=(stay, stay, stay),
        scratch_shapes=[
            pltpu.VMEM((count, lanes), jnp.float32),
            pltpu.VMEM((count, lanes), jnp.float32),
            pltpu.VMEM((3, count, lanes), jnp.float32),
            pltpu.SemaphoreType.DMA((3,)),
        ],
        compiler_params=params,
    )(chunks, temp, cure, tools, flat, steep, cell_bands)


def solution(mesh):
    return jax.shard_map(
        on_device,
        mesh=mesh,
        in_specs=(
            P(None, "plane", "depth"),
            P(("plane", "depth"), None),
            P(("plane", "depth"), None),
            P(),
            P(),
        ),
        out_specs=(
            P(("plane", "depth"), None),
            P(("plane", "depth"), None),
            P(None, ("plane", "depth"), None),
        ),
        check_vma=False,
    )
```

```python
import functools

import jax
import jax.numpy as jnp
import ml_dtypes
import numpy as np
from jax import lax
from jax.experimental import pallas as pl
from jax.experimental.pallas import tpu as pltpu
from jax.sharding import PartitionSpec as P

ROWS = 8
R1 = 6
R2 = 10
COARSE = 4
STEPS = 3

sigma_grad = 2.0
sigma_tensor = 3.3
conduct_matrix = 0.3
conduct_fiber = 1.5
time_step = 0.25
heat_release = 0.4
rate_first = 0.15
rate_second = 0.6
energy_first = 30.0
energy_second = 25.0
reference_temp = 4.2
tensor_eps = 1e-06

LANES = 128
HALO = 2
EDGE = HALO * COARSE + R1 + R2
EARLY = 80
GHOST = 3
RIM = 2 * R1
BEFORE = -(-(R2 - R1) // COARSE)
AFTER = BEFORE
HALF = LANES // 2
SLOT = 40
ROW_KINDS = (1, 0, 0)
X_KINDS = (0, 1, 0)
DEPTH_KINDS = (0, 0, 1)


def smooth_taps(radius, sigma):
    offsets = np.arange(-radius, radius + 1) * 1.0
    weights = np.exp(-0.5 * offsets * offsets / (sigma * sigma))
    return weights / weights.sum()


def slope_taps(radius, sigma):
    offsets = np.arange(-radius, radius + 1) * 1.0
    weights = np.exp(-0.5 * offsets * offsets / (sigma * sigma))
    return offsets * weights / np.sum(offsets * offsets * weights)


def row_weights(count, radius, sigma):
    taps = smooth_taps(radius, sigma)
    result = np.zeros(count)
    for source in range(count):
        for target in range(count):
            offset = target - source
            if abs(offset) <= radius:
                result[source] += taps[offset + radius]
    return result


def rounded(taps):
    best = None
    for factor in np.linspace(1.0, 2.0, 20001)[:-1]:
        near = (taps * factor).astype(np.float32).astype(ml_dtypes.bfloat16).astype(np.float64)
        error = np.abs(near / factor - taps).sum()
        if best is None or error < best[0]:
            best = (error, near, factor)
    return best[1], best[2]


def as_bfloat16(matrix):
    return matrix.astype(np.float32).astype(ml_dtypes.bfloat16)


def halves(matrix):
    high = as_bfloat16(matrix)
    return high, as_bfloat16(matrix - high.astype(np.float64))


def sizes(width, depth):
    columns = width // COARSE + 2 * HALO
    cells = depth // COARSE + BEFORE + AFTER
    return columns, cells


def product_rows(width):
    places = [*range(R1, width - R1), *range(R1 - EDGE, R1), *range(width - R1, width + EDGE - R1)]
    return places + [None] * (-len(places) % 16)


GRAD_TAPS = tuple(
    rounded(taps(R1, sigma_grad)) for taps in (smooth_taps, slope_taps)
)
GRAD_FACTOR = GRAD_TAPS[0][1] ** 2 * GRAD_TAPS[1][1]


def grad_taps(kind):
    return GRAD_TAPS[kind][0]


def tap(taps, offset):
    radius = (len(taps) - 1) // 2
    return float(taps[offset + radius]) if abs(offset) <= radius else 0.0


def x_bands(width):
    places = product_rows(width)
    bands = np.zeros((2, len(places), width + 2 * EDGE))
    for kind in range(2):
        for row, place in enumerate(places):
            if place is not None:
                first = place + EDGE - R1
                bands[kind, row, first : first + 2 * R1 + 1] = grad_taps(kind)
    return bands


def rim_bands(rows):
    bands = np.zeros((3, 3 * LANES, LANES))
    for part in range(3):
        row_taps, depth_taps = grad_taps(ROW_KINDS[part]), grad_taps(DEPTH_KINDS[part])
        for source in range(rows):
            for target in range(rows):
                row_tap = tap(row_taps, source - target)
                for near in range(-RIM, RIM):
                    lane = source * RIM + near % RIM
                    if near >= 0:
                        lane += rows * RIM + LANES
                    for place in range(-R1, R1):
                        value = row_tap * tap(depth_taps, near - place)
                        bands[part, lane, target * 2 * R1 + R1 + place] = value
    return bands


def rim_cells(rows, depth, blocks):
    taps = smooth_taps(R2, sigma_tensor)
    weights = product_weights(rows)
    bands = np.zeros((blocks - 1, LANES, blocks * depth // COARSE))
    for boundary in range(blocks - 1):
        middle = (boundary + 1) * depth
        for cell in range(bands.shape[2]):
            for voxel in range(cell * COARSE, (cell + 1) * COARSE):
                for place in range(-R1, R1):
                    value = tap(taps, middle + place - voxel)
                    for row in range(rows):
                        bands[boundary, row * 2 * R1 + R1 + place, cell] += weights[row] * value
    return bands.reshape(-1, bands.shape[2])


def own_columns(count):
    products = (count + 2 * HALO) * COARSE + 2 * R2
    voxels = products + 2 * R1
    return -(-products // 16) * 16, -(-voxels // 8) * 8


def fold(voxels):
    return -(-voxels // 16) * 8


def rim_x_bands(count):
    products, voxels = own_columns(count)
    bands = np.zeros((2, products, -(-voxels // 16) * 16))
    valid = (count + 2 * HALO) * COARSE + 2 * R2
    for kind in range(2):
        for row in range(valid):
            bands[kind, row, row : row + 2 * R1 + 1] = grad_taps(kind)
    taps = smooth_taps(R2, sigma_tensor)
    coarse = np.zeros((16, products))
    for column in range(count + 2 * HALO):
        for voxel in range(column * COARSE, (column + 1) * COARSE):
            coarse[column, voxel : voxel + 2 * R2 + 1] += taps
    return bands.reshape(2 * products, -1), coarse


def depth_bands(depth):
    bands = np.zeros((2, depth, depth))
    for kind in range(2):
        for place in range(depth):
            for near in range(max(place - R1, 0), min(place + R1 + 1, depth)):
                bands[kind, near, place] = tap(grad_taps(kind), near - place)
    return bands


def product_weights(rows):
    return row_weights(rows, R2, sigma_tensor) / (255.0 * GRAD_FACTOR) ** 2


def coarse_depth_bands(depth):
    taps = smooth_taps(R2, sigma_tensor)
    columns, cells = sizes(0, depth)
    bands = np.zeros((depth, LANES))
    for cell in range(cells):
        for voxel in range(COARSE):
            place = (cell - BEFORE) * COARSE + voxel
            for near in range(max(place - R2, 0), min(place + R2 + 1, depth)):
                bands[near, cell] += tap(taps, near - place)
    return bands


def coarse_x_bands(width):
    taps = smooth_taps(R2, sigma_tensor)
    places = product_rows(width)
    columns, cells = sizes(width, 0)
    bands = np.zeros((-(-columns // 16) * 16, len(places)))
    for column in range(columns):
        for voxel in range(COARSE):
            middle = (column - HALO) * COARSE + voxel
            for row, place in enumerate(places):
                if place is not None:
                    bands[column, row] += tap(taps, place - middle)
    return bands


def stacked(*pieces):
    widest = max(piece.shape[1] for piece in pieces)
    padded = [np.pad(piece, ((0, 0), (0, widest - piece.shape[1]))) for piece in pieces]
    starts = np.cumsum([0] + [len(piece) for piece in pieces])
    return jnp.asarray(as_bfloat16(np.concatenate(padded))), tuple(int(start) for start in starts)


def two_parts(values):
    high = values.astype(jnp.bfloat16).astype(jnp.float32)
    return jnp.concatenate([high, (values - high).astype(jnp.bfloat16).astype(jnp.float32)], axis=0)


def joined(parts):
    half = parts.shape[0] // 2
    return parts[:half] + parts[half:]


def column_rows(temp, cure, first):
    pad = jnp.zeros((8 - 2 * GHOST, temp.shape[1]), jnp.float32)
    return jnp.concatenate(
        [temp[first : first + GHOST, :], cure[first : first + GHOST, :], pad], axis=0
    )


def is_odd():
    return lax.rem(lax.axis_index("plane"), 2) == 1


def pack_kernel(
    intensity, temp_hbm, cure_hbm, x_hbm, z_hbm, far, near, own, x_parts, z_parts, temp, cure,
    grey, sems,
):
    rows, width, depth = intensity.shape
    copies = [
        pltpu.make_async_copy(intensity, grey, sems.at[0]),
        pltpu.make_async_copy(temp_hbm, temp, sems.at[1]),
        pltpu.make_async_copy(cure_hbm, cure, sems.at[2]),
        pltpu.make_async_copy(x_hbm, x_parts, sems.at[3]),
        pltpu.make_async_copy(z_hbm, z_parts, sems.at[4]),
    ]
    for copy in copies:
        copy.start()
    for copy in copies:
        copy.wait()
    odd = is_odd()
    count = temp.shape[0]
    sides = [
        two_parts(column_rows(temp, cure, first)).astype(jnp.bfloat16)
        for first in (0, count - GHOST)
    ]

    def send(left, right):
        for place, target, columns in ((0, left, sides[0]), (width - EDGE, right, sides[1])):
            for pair in range(rows // 2):
                two = [grey[2 * pair + i, place : place + EDGE, :] for i in range(2)]
                two = jnp.concatenate(two, axis=0).astype(jnp.float32)
                target[2 * EDGE * pair : 2 * EDGE * (pair + 1), :] = two.astype(jnp.bfloat16)
            for slot in range(temp.shape[1] // LANES):
                at = rows * EDGE + 16 * slot
                target[at : at + 16, :] = columns[:, slot * LANES : (slot + 1) * LANES]

    @pl.when(odd)
    def _():
        send(near, far)

    @pl.when(jnp.logical_not(odd))
    def _():
        send(far, near)

    for row in range(rows):
        half = (row % 2) * depth
        own[row // 2, :, half : half + depth] = grey[row].astype(jnp.float32).astype(jnp.bfloat16)


def packed_rows(values, size, first):
    depth = values[0].shape[1]
    lane = lax.broadcasted_iota(jnp.int32, values[0].shape, 1)
    packed = None
    for block, value in enumerate(values):
        shift = (size * block - first) % depth
        moved = value if shift == 0 else pltpu.roll(value, shift, 1)
        packed = moved if block == 0 else jnp.where(lane >= size * block, moved, packed)
    return packed


def edges_of(ref, rows):
    two = [
        ref[2 * EDGE * pair : 2 * EDGE * (pair + 1), :].astype(jnp.float32)
        for pair in range(rows // 2)
    ]
    voxels = [two[row // 2][row % 2 * EDGE : (row % 2 + 1) * EDGE] for row in range(rows)]
    slots = range(rows * EDGE, ref.shape[0], 16)
    columns = [joined(ref[at : at + 16, :].astype(jnp.float32)) for at in slots]
    return voxels, jnp.concatenate(columns, axis=1)


def product(first, second):
    return jnp.dot(first, second, preferred_element_type=jnp.float32)


def mirrored_filter(kind, values, even):
    rows = len(values)
    use_sum = even == (kind == 0)
    sign = 1.0 if use_sum else -1.0
    half = [values[row] + sign * values[rows - 1 - row] for row in range(rows // 2)]
    results = []
    for row in range(rows // 2):
        total = None
        for source, value in enumerate(half):
            near = tap(grad_taps(kind), source - row)
            far = tap(grad_taps(kind), rows - 1 - source - row)
            weight = 0.5 * (near + sign * far)
            total = weight * value if total is None else total + weight * value
        results.append(total)
    return results


def weighted_products(three, weight):
    pairs = ((0, 0), (1, 1), (2, 2), (0, 1), (0, 2), (1, 2))
    first = [weight * value for value in three]
    return [first[a] * three[b] for a, b in pairs]


def late_mask(count, width):
    row = lax.broadcasted_iota(jnp.int32, (count, LANES), 0)
    left = width - 2 * R1 - EARLY
    place = jnp.where(row < left + EDGE, row - left + R1 - EDGE, row - left - EDGE + width - R1)
    place = place + lax.axis_index("plane") * width
    inside = (place >= 0) & (place < lax.axis_size("plane") * width)
    return jnp.where(inside | (row < left), 1.0, 0.0)


def all_sums(products, coarse, sx):
    kinds, count, lanes = products.shape
    side_by_side = jnp.concatenate([products[index] for index in range(kinds)], axis=1)
    along = product(sx, side_by_side).astype(jnp.bfloat16)
    parts = [along[:, index * lanes : (index + 1) * lanes] for index in range(kinds)]
    return product(jnp.concatenate(parts, axis=0), coarse)


def tensor_sums(window, bands, sx, mask, diagonal, z_parts, across, filtered, grads, products):
    pairs, height, double = window.shape
    rows, depth = 2 * pairs, double // 2
    count = bands.shape[0] // 2
    for pair in range(pairs):
        across[pair] = product(bands, window[pair])

    def filter_rows(group, carry):
        start = pl.multiple_of(group * 16, 16)
        kinds = [
            [
                across[row // 2, pl.ds(kind * count + start, 16), pl.ds((row % 2) * depth, depth)]
                for row in range(rows)
            ]
            for kind in range(2)
        ]
        for part in range(3):
            values = kinds[X_KINDS[part]]
            results = mirrored_filter(ROW_KINDS[part], values, True)
            results += mirrored_filter(ROW_KINDS[part], values, False)
            for row, result in enumerate(results):
                lanes = pl.ds((row % 2) * depth, depth)
                filtered[part, row // 2, pl.ds(start, 16), lanes] = result.astype(jnp.bfloat16)
        return carry

    lax.fori_loop(0, count // 16, filter_rows, 0)
    for part in range(3):
        at = DEPTH_KINDS[part] * double
        for pair in range(pairs):
            grads[part, pair] = product(filtered[part, pair], diagonal[at : at + double, :])

    weights = product_weights(rows)
    layer = lax.axis_index("depth")
    first, last = layer == 0, layer == lax.axis_size("depth") - 1
    place = lax.broadcasted_iota(jnp.int32, (16, depth), 1)
    complete = ((place >= R1) | first) & ((place < depth - R1) | last)
    complete = jnp.where(complete, 1.0, 0.0)

    def multiply(group, carry):
        start = pl.multiple_of(group * 16, 16)
        inside = complete if mask is None else complete * mask[pl.ds(start, 16), :]
        totals = None
        for row in range(rows):
            lanes = pl.ds((row % 2) * depth, depth)
            three = [grads[part, row // 2, pl.ds(start, 16), lanes] for part in range(3)]
            terms = weighted_products(three, 2.0 * float(weights[row % (rows // 2)]))
            totals = terms if row == 0 else [a + b for a, b in zip(totals, terms)]
        for index in range(6):
            products[index, pl.ds(start, 16), :] = (totals[index] * inside).astype(jnp.bfloat16)
        return carry

    lax.fori_loop(0, count // 16, multiply, 0)
    return all_sums(products, z_parts[double : double + depth, :], sx)


def early_kernel(*refs):
    starts, own, x_parts, z_parts, *rest = refs
    count = (len(rest) - 7) // 2
    constants, (sums, diagonal), held = rest[:count], rest[count : count + 2], rest[count + 2 : -5]
    across, filtered, grads, products, sems = rest[-5:]
    copies = [
        pltpu.make_async_copy(source, target, sems.at[index])
        for index, (source, target) in enumerate(zip(constants, held))
    ]
    for copy in copies:
        copy.start()
    pairs, width, double = own.shape
    depth = double // 2
    empty = jnp.zeros((depth, depth), jnp.bfloat16)
    for kind in range(2):
        for half in range(2):
            at = pl.ds(kind * double + half * depth, depth)
            band = z_parts[kind * depth : (kind + 1) * depth, :]
            diagonal[at, half * depth : (half + 1) * depth] = band
            diagonal[at, (1 - half) * depth : (2 - half) * depth] = empty
    bands = x_parts[starts[0] : starts[1], :width]
    sx = x_parts[starts[1] : starts[2], :EARLY]
    sums[...] = tensor_sums(
        own, bands, sx, None, diagonal, z_parts, across, filtered, grads, products
    )
    for copy in copies:
        copy.wait()


def late_kernel(
    starts, own, far, near, x_late, z_parts, diagonal, early_sums, temp, cure, out_hbm,
    window, across, filtered, grads, products, mask, out, sems,
):
    pairs, width, double = own.shape
    rows, depth = 2 * pairs, double // 2
    count, lanes = temp.shape
    odd = is_odd()
    depths, layer = lax.axis_size("depth"), lax.axis_index("depth")
    outer, outer_columns = edges_of(far, rows)
    inner, inner_columns = edges_of(near, rows)
    values = []
    for row in range(rows):
        half = (row % 2) * depth
        middle = own[row // 2, :, half : half + depth].astype(jnp.float32)
        left = jnp.where(odd, inner[row], outer[row])
        right = jnp.where(odd, outer[row], inner[row])
        whole = jnp.concatenate([left, middle, right], axis=0)
        window[row // 2, :, half : half + depth] = whole.astype(jnp.bfloat16)
        values.append(whole)
    left = jnp.where(odd, inner_columns, outer_columns)
    right = jnp.where(odd, outer_columns, inner_columns)

    products_x, voxels = own_columns(count)
    folded, stride = fold(voxels), COARSE * count
    below = packed_rows(values, RIM, depth - RIM)
    above = pltpu.roll(packed_rows(values, RIM, 0), rows * RIM, 1)
    lane = lax.broadcasted_iota(jnp.int32, below.shape, 1)
    tiles = [jnp.where(lane < rows * RIM, below, above), above, pltpu.roll(above, HALF, 1)]
    missing = stride * (depths - 1) + voxels - below.shape[0]
    if missing > 0:
        spare = jnp.zeros((-(-missing // 8) * 8, LANES), jnp.float32)
        tiles = [jnp.concatenate([tile, spare], axis=0) for tile in tiles]

    height = count + 2 * HALO
    half_lane = lax.broadcasted_iota(jnp.int32, (folded, LANES), 1) < HALF
    for target in range(out.shape[0]):
        at = stride * target
        second = jnp.where(
            half_lane,
            tiles[1][at : at + folded],
            tiles[2][at + voxels - folded : at + voxels],
        )
        rims = jnp.concatenate([tiles[0][at : at + voxels], second], axis=0)
        out[target, 0 : voxels + folded, :] = rims.astype(jnp.bfloat16)
    split = (pl.ds(0, voxels + folded), pl.ds(voxels + folded, out.shape[1] - voxels - folded))
    copies = [
        pltpu.make_async_copy(out.at[:, part, :], out_hbm.at[:, part, :], sems.at[index])
        for index, part in enumerate(split)
    ]
    copies[0].start()

    late = across.shape[1] // 2
    mask[...] = late_mask(late, width)
    bands = x_late[starts[0] : starts[1], :]
    sx = x_late[starts[1] : starts[2], :late]
    sums = early_sums[...] + tensor_sums(
        window, bands, sx, mask, diagonal, z_parts, across, filtered, grads, products
    )
    high = sx.shape[0]
    total = [sums[index * high : (index + 1) * high] for index in range(6)]
    trace = total[0] + total[1] + total[2]
    lane = lax.broadcasted_iota(jnp.int32, trace.shape, 1)
    three = jnp.where(lane < SLOT, trace, pltpu.roll(total[1], SLOT, 1))
    three = jnp.where(lane < 2 * SLOT, three, pltpu.roll(total[2], 2 * SLOT, 1))
    xz = [total[5]] + [pltpu.roll(total[5], index * SLOT, 1) for index in range(1, 3)]

    own_first, own_last = column_rows(temp, cure, 0), column_rows(temp, cure, count - GHOST)
    for target in range(out.shape[0]):
        piece = jnp.where(layer == target - 1, own_last, 0.0)
        piece = jnp.where(layer == target + 1, own_first, piece)
        if target == 0:
            piece = jnp.where(layer == depths - 1, left, piece)
        if target == out.shape[0] - 1:
            piece = jnp.where(layer == 0, right, piece)
        at = count * target
        pieces = [three[at : at + height], jnp.zeros((4, LANES), jnp.float32)]
        for index in range(3):
            size = min(4, height - 4 * index)
            if size > 0:
                part = xz[index][at + 4 * index : at + 4 * index + size]
                if size < 4:
                    spare = jnp.zeros((4 - size, LANES), jnp.float32)
                    part = jnp.concatenate([part, spare], axis=0)
                pieces[1] = jnp.where(lane[:4] < index * SLOT, pieces[1], part)
        for slot in range(lanes // LANES):
            pieces.append(piece[0 : 2 * GHOST, slot * LANES : (slot + 1) * LANES])
        filled = sum(part.shape[0] for part in pieces)
        if filled < 24:
            pieces.append(jnp.zeros((24 - filled, LANES), jnp.float32))
        sent = two_parts(jnp.concatenate(pieces, axis=0))
        out[target, voxels + folded :, :] = sent.astype(jnp.bfloat16)
    copies[1].start()
    for copy in copies:
        copy.wait()


def rim_sums(chunks, count, starts, flat, steep, cells):
    parts = chunks.shape[0]
    rows_x, voxels = own_columns(count)
    folded = fold(voxels)
    tall = -(-voxels // 16) * 16
    spare = [jnp.zeros((tall - voxels, LANES), jnp.float32)] if tall > voxels else []
    tiles = []
    for part in range(parts):
        rims = chunks[part, 0 : voxels + folded, :].astype(jnp.float32)
        second = rims[voxels:]
        second = [second[: voxels - folded], pltpu.roll(second, HALF, 1)]
        for tile in ([rims[:voxels]], second):
            tiles.append(jnp.concatenate(tile + spare, axis=0).astype(jnp.bfloat16))
    result = product(
        steep[starts[1] : starts[2], :tall], jnp.concatenate(tiles, axis=1)
    ).astype(jnp.bfloat16)
    kinds = []
    for kind in range(2):
        values = result[kind * rows_x : (kind + 1) * rows_x]
        tile = lambda index: values[:, index * LANES : (index + 1) * LANES]
        stack = [
            jnp.concatenate([tile(2 * part), tile(2 * part + 2), tile(2 * part + 3)], axis=1)
            for part in range(parts - 1)
        ]
        kinds.append(jnp.concatenate(stack, axis=0))
    both = product(kinds[0], flat[...])
    three = (both[:, :LANES], product(kinds[1], steep[starts[0] : starts[1], :]), both[:, LANES:])

    index = lax.axis_index("plane") * lax.axis_size("depth") + lax.axis_index("depth")
    total = lax.axis_size("plane") * lax.axis_size("depth") * count * COARSE
    place = lax.rem(lax.broadcasted_iota(jnp.int32, three[0].shape, 0), rows_x)
    place = place + (index * count - HALO) * COARSE - R2
    inside = jnp.where((place >= 0) & (place < total), 1.0, 0.0)
    wide = []
    for term in weighted_products(three, inside):
        term = term.astype(jnp.bfloat16)
        wide += [term[part * rows_x : (part + 1) * rows_x] for part in range(parts - 1)]
    sx = steep[starts[2] : starts[3], :rows_x]
    along = product(sx, jnp.concatenate(wide, axis=1)).astype(jnp.bfloat16)
    step = (parts - 1) * LANES
    along = [along[:, kind * step : (kind + 1) * step] for kind in range(6)]
    sums = product(jnp.concatenate(along, axis=0), cells[...])
    return [sums[kind * 16 : (kind + 1) * 16] for kind in range(6)]


def cure_kernel(
    cells, starts, chunks, temp_in, cure_in, tools, flat, steep, rim_bands, temp_hbm, cure_hbm,
    conduct_hbm, temp_out, cure_out, conduct_out, sems,
):
    count, lanes = temp_in.shape
    parts = chunks.shape[0]
    planes, depths = lax.axis_size("plane"), lax.axis_size("depth")
    plane, layer = lax.axis_index("plane"), lax.axis_index("depth")
    height = count + 2 * HALO
    own = cells - BEFORE - AFTER
    lane = lax.broadcasted_iota(jnp.int32, (16, lanes), 1)
    row = lax.broadcasted_iota(jnp.int32, (16, lanes), 0)
    at_sums = chunks.shape[1] - 48

    near = rim_sums(chunks, count, starts, flat, steep, rim_bands)
    sums = [near[0] + near[1] + near[2], near[1], near[2], near[5]]
    for part in range(parts):
        first_cell = own * part - BEFORE
        here = (lane >= first_cell) & (lane < first_cell + cells)
        values = joined(chunks[part, at_sums:, :].astype(jnp.float32))
        xz = values[height : height + 4]
        xz = [xz] + [pltpu.roll(xz, LANES - index * SLOT, 1) for index in range(1, 3)]
        spare = jnp.zeros((4, LANES), jnp.float32)
        xz = jnp.concatenate([*xz, spare], axis=0)
        for index in range(4):
            chunk = values[0:16] if index < 3 else xz
            if lanes > LANES:
                spare = jnp.zeros((16, lanes - LANES), jnp.float32)
                chunk = jnp.concatenate([chunk, spare], axis=1)
            shift = (first_cell - (index % 3) * SLOT) % lanes
            moved = chunk if shift == 0 else pltpu.roll(chunk, shift, 1)
            sums[index] = sums[index] + jnp.where(here, moved, 0.0)
    trace = sums[0]
    scale = (conduct_fiber - conduct_matrix) / (2.0 * trace + tensor_eps)
    conduct = [
        conduct_matrix + scale * (trace - sums[1]),
        -scale * sums[3],
        conduct_matrix + scale * (trace - sums[2]),
    ]
    for kind in range(3):
        conduct_out[kind] = conduct[kind][HALO : HALO + count]
    copies = [
        pltpu.make_async_copy(conduct_out, conduct_hbm, sems.at[0]),
        pltpu.make_async_copy(temp_out, temp_hbm, sems.at[1]),
        pltpu.make_async_copy(cure_out, cure_hbm, sems.at[2]),
    ]
    copies[0].start()

    def columns_of(part):
        values = joined(chunks[part, at_sums:, :].astype(jnp.float32))
        slots = range(height + 4, height + 4 + 2 * GHOST * (lanes // LANES), 2 * GHOST)
        return jnp.concatenate([values[at : at + 2 * GHOST] for at in slots], axis=1)

    before = columns_of(lax.rem(layer + parts - 1, parts))
    after = columns_of(lax.rem(layer + 1, parts))
    spare = jnp.full((16 - count - 2 * GHOST, lanes), 0.5, jnp.float32)
    temp = jnp.concatenate([before[:GHOST], temp_in[...], after[:GHOST], 8.0 * spare], axis=0)
    cure = jnp.concatenate([before[GHOST:], cure_in[...], after[GHOST:], spare], axis=0)
    gap = GHOST - HALO
    xx, xz, zz = [pltpu.roll(part, gap, 0) for part in conduct]

    first = (plane == 0) & (layer == 0)
    last = (plane == planes - 1) & (layer == depths - 1)
    for step in range(STEPS):
        top, bottom = tools[2 * step : 2 * step + 1, :], tools[2 * step + 1 : 2 * step + 2, :]
        temp = jnp.where((row < GHOST) & first, temp[GHOST : GHOST + 1], temp)
        temp = jnp.where(
            (row >= GHOST + count) & last, temp[GHOST + count - 1 : GHOST + count], temp
        )
        cooler = jnp.where(lane == 0, top, pltpu.roll(temp, 1, 1))
        later = jnp.where(lane == lanes - 1, bottom, pltpu.roll(temp, lanes - 1, 1))
        slant = later - cooler
        second_x = pltpu.roll(temp, 15, 0) - 2.0 * temp + pltpu.roll(temp, 1, 0)
        second_z = later - 2.0 * temp + cooler
        cross = 0.25 * (pltpu.roll(slant, 15, 0) - pltpu.roll(slant, 1, 0))
        spread = xx * second_x + 2.0 * xz * cross + zz * second_z
        inverse = 1.0 / reference_temp - 1.0 / temp
        left = 1.0 - cure
        rate = rate_first * jnp.exp(energy_first * inverse) + rate_second * jnp.exp(
            energy_second * inverse
        ) * jnp.sqrt(cure)
        rate = rate * (left * jnp.sqrt(left))
        temp = temp + time_step * (spread + heat_release * rate)
        cure = cure + time_step * rate
    temp_out[...] = temp[GHOST : GHOST + count]
    cure_out[...] = cure[GHOST : GHOST + count]
    for copy in copies[1:]:
        copy.start()
    for copy in copies:
        copy.wait()


def on_device(intensity, temp_start, cure_start, tool_levels, plan):
    rows, width, depth = intensity.shape
    count, lanes = temp_start.shape
    planes, depths = lax.axis_size("plane"), lax.axis_size("depth")
    columns, cells = sizes(width, depth)
    bf16 = jnp.bfloat16
    slots = rows * EDGE + 16 * (lanes // LANES)
    params = pltpu.CompilerParams(vmem_limit_bytes=24 * 1024 * 1024)
    vmem = pl.BlockSpec(memory_space=pltpu.VMEM)
    stay = pl.BlockSpec(memory_space=pltpu.HBM)

    fixed = lambda values: pltpu.with_memory_space_constraint(values, pltpu.HBM)
    bands, coarse = x_bands(width), coarse_x_bands(width)
    late = bands.shape[1] - EARLY
    middle = bands[:, :EARLY, EDGE : EDGE + width]
    x_hbm, early_starts = stacked(middle.reshape(2 * EARLY, -1), coarse[:, :EARLY])
    z_hbm, _ = stacked(*depth_bands(depth), coarse_depth_bands(depth))
    x_late, late_starts = stacked(bands[:, EARLY:].reshape(2 * late, -1), coarse[:, EARLY:])
    rims = rim_bands(rows)
    flat, _ = stacked(np.concatenate([rims[0], rims[2]], axis=1))
    steep, rim_starts = stacked(rims[1], *rim_x_bands(count))
    cell_bands, _ = stacked(rim_cells(rows, depth, depths))
    constants = (x_late, flat, steep, cell_bands)
    far, near, own, x_parts, z_parts, temp, cure = pl.pallas_call(
        pack_kernel,
        name="pack",
        out_shape=(
            pltpu.VMEM((slots, depth), bf16),
            pltpu.VMEM((slots, depth), bf16),
            pltpu.VMEM((rows // 2, width, 2 * depth), bf16),
            pltpu.VMEM(x_hbm.shape, bf16),
            pltpu.VMEM(z_hbm.shape, bf16),
            pltpu.VMEM((count, lanes), jnp.float32),
            pltpu.VMEM((count, lanes), jnp.float32),
        ),
        in_specs=[stay] * 5,
        scratch_shapes=[
            pltpu.VMEM((rows, width, depth), jnp.int32),
            pltpu.SemaphoreType.DMA((5,)),
        ],
        compiler_params=params,
    )(*[fixed(values) for values in (intensity, temp_start, cure_start, x_hbm, z_hbm)])

    def moved(values, pairs):
        index = [(p * depths + d, q * depths + e) for (p, d), (q, e) in pairs]
        return lax.ppermute(values, ("plane", "depth"), index)

    def swapped(values, first):
        pairs = [(p, p + 1) for p in range(first, planes - 1, 2)]
        pairs += [(q, p) for p, q in pairs]
        return moved(values, [((p, d), (q, d)) for p, q in pairs for d in range(depths)])

    far = swapped(far, 1)
    near = swapped(near, 0)

    high = coarse.shape[0]

    def scratch(count):
        return [
            pltpu.VMEM((rows // 2, 2 * count, 2 * depth), jnp.float32),
            pltpu.VMEM((3, rows // 2, count, 2 * depth), bf16),
            pltpu.VMEM((3, rows // 2, count, 2 * depth), jnp.float32),
            pltpu.VMEM((6, count, depth), bf16),
        ]

    def cost(count):
        return pl.CostEstimate(
            flops=2 * rows * (2 * count) * 160 * depth * 4,
            bytes_accessed=4_000_000,
            transcendentals=0,
        )

    early_sums, diagonal, x_late, flat, steep, cell_bands = pl.pallas_call(
        functools.partial(early_kernel, early_starts),
        name="early",
        out_shape=(
            pltpu.VMEM((6 * high, LANES), jnp.float32),
            pltpu.VMEM((4 * depth, 2 * depth), bf16),
            *[pltpu.VMEM(values.shape, bf16) for values in constants],
        ),
        in_specs=[vmem] * 3 + [stay] * len(constants),
        scratch_shapes=scratch(EARLY) + [pltpu.SemaphoreType.DMA((len(constants),))],
        cost_estimate=cost(EARLY),
        compiler_params=params,
    )(own, x_parts, z_parts, *[fixed(values) for values in constants])

    products_x, voxels = own_columns(count)
    chunk_shape = (depths, voxels + fold(voxels) + 48, LANES)
    chunks = pl.pallas_call(
        functools.partial(late_kernel, late_starts),
        name="late",
        out_shape=pltpu.HBM(chunk_shape, bf16),
        in_specs=[vmem] * 9,
        out_specs=stay,
        scratch_shapes=[pltpu.VMEM((rows // 2, width + 2 * EDGE, 2 * depth), bf16)]
        + scratch(late)
        + [
            pltpu.VMEM((late, LANES), jnp.float32),
            pltpu.VMEM(chunk_shape, bf16),
            pltpu.SemaphoreType.DMA((2,)),
        ],
        cost_estimate=cost(late),
        compiler_params=params,
    )(own, far, near, x_late, z_parts, diagonal, early_sums, temp, cure)

    faces = plan.reshape(2 * STEPS, 1) == jnp.arange(tool_levels.shape[0], dtype=jnp.int32)
    tools = jnp.sum(
        jnp.where(faces, tool_levels, jnp.zeros_like(tool_levels)), axis=1, keepdims=True
    )

    chunks = lax.all_to_all(chunks, "depth", split_axis=0, concat_axis=0, tiled=True)

    return pl.pallas_call(
        functools.partial(cure_kernel, cells, rim_starts),
        name="cure",
        out_shape=(
            pltpu.HBM((count, lanes), jnp.float32),
            pltpu.HBM((count, lanes), jnp.float32),
            pltpu.HBM((3, count, lanes), jnp.float32),
        ),
        in_specs=[vmem] * 7,
        out_specs=(stay, stay, stay),
        scratch_shapes=[
            pltpu.VMEM((count, lanes), jnp.float32),
            pltpu.VMEM((count, lanes), jnp.float32),
            pltpu.VMEM((3, count, lanes), jnp.float32),
            pltpu.SemaphoreType.DMA((3,)),
        ],
        compiler_params=params,
    )(chunks, temp, cure, tools, flat, steep, cell_bands)


def solution(mesh):
    return jax.shard_map(
        on_device,
        mesh=mesh,
        in_specs=(
            P(None, "plane", "depth"),
            P(("plane", "depth"), None),
            P(("plane", "depth"), None),
            P(),
            P(),
        ),
        out_specs=(
            P(("plane", "depth"), None),
            P(("plane", "depth"), None),
            P(None, ("plane", "depth"), None),
        ),
        check_vma=False,
    )
```

```python
import functools

import jax
import jax.numpy as jnp
import ml_dtypes
import numpy as np
from jax import lax
from jax.experimental import pallas as pl
from jax.experimental.pallas import tpu as pltpu
from jax.sharding import PartitionSpec as P

ROWS = 8
R1 = 6
R2 = 10
COARSE = 4
STEPS = 3

sigma_grad = 2.0
sigma_tensor = 3.3
conduct_matrix = 0.3
conduct_fiber = 1.5
time_step = 0.25
heat_release = 0.4
rate_first = 0.15
rate_second = 0.6
energy_first = 30.0
energy_second = 25.0
reference_temp = 4.2
tensor_eps = 1e-06

LANES = 128
HALO = 2
EDGE = HALO * COARSE + R1 + R2
EARLY = 80
GHOST = 3
RIM = 2 * R1
BEFORE = -(-(R2 - R1) // COARSE)
AFTER = BEFORE
HALF = LANES // 2
SLOT = 40
ROW_KINDS = (1, 0, 0)
X_KINDS = (0, 1, 0)
DEPTH_KINDS = (0, 0, 1)


def smooth_taps(radius, sigma):
    offsets = np.arange(-radius, radius + 1) * 1.0
    weights = np.exp(-0.5 * offsets * offsets / (sigma * sigma))
    return weights / weights.sum()


def slope_taps(radius, sigma):
    offsets = np.arange(-radius, radius + 1) * 1.0
    weights = np.exp(-0.5 * offsets * offsets / (sigma * sigma))
    return offsets * weights / np.sum(offsets * offsets * weights)


def row_weights(count, radius, sigma):
    taps = smooth_taps(radius, sigma)
    result = np.zeros(count)
    for source in range(count):
        for target in range(count):
            offset = target - source
            if abs(offset) <= radius:
                result[source] += taps[offset + radius]
    return result


def rounded(taps):
    best = None
    for factor in np.linspace(1.0, 2.0, 20001)[:-1]:
        near = (taps * factor).astype(np.float32).astype(ml_dtypes.bfloat16).astype(np.float64)
        error = np.abs(near / factor - taps).sum()
        if best is None or error < best[0]:
            best = (error, near, factor)
    return best[1], best[2]


def as_bfloat16(matrix):
    return matrix.astype(np.float32).astype(ml_dtypes.bfloat16)


def halves(matrix):
    high = as_bfloat16(matrix)
    return high, as_bfloat16(matrix - high.astype(np.float64))


def sizes(width, depth):
    columns = width // COARSE + 2 * HALO
    cells = depth // COARSE + BEFORE + AFTER
    return columns, cells


def product_rows(width):
    places = [*range(R1, width - R1), *range(R1 - EDGE, R1), *range(width - R1, width + EDGE - R1)]
    return places + [None] * (-len(places) % 16)


GRAD_TAPS = tuple(
    rounded(taps(R1, sigma_grad)) for taps in (smooth_taps, slope_taps)
)
GRAD_FACTOR = GRAD_TAPS[0][1] ** 2 * GRAD_TAPS[1][1]


def grad_taps(kind):
    return GRAD_TAPS[kind][0]


def tap(taps, offset):
    radius = (len(taps) - 1) // 2
    return float(taps[offset + radius]) if abs(offset) <= radius else 0.0


def x_bands(width):
    places = product_rows(width)
    bands = np.zeros((2, len(places), width + 2 * EDGE))
    for kind in range(2):
        for row, place in enumerate(places):
            if place is not None:
                first = place + EDGE - R1
                bands[kind, row, first : first + 2 * R1 + 1] = grad_taps(kind)
    return bands


def rim_bands(rows):
    bands = np.zeros((3, 3 * LANES, LANES))
    for part in range(3):
        row_taps, depth_taps = grad_taps(ROW_KINDS[part]), grad_taps(DEPTH_KINDS[part])
        for source in range(rows):
            for target in range(rows):
                row_tap = tap(row_taps, source - target)
                for near in range(-RIM, RIM):
                    lane = source * RIM + near % RIM
                    if near >= 0:
                        lane += rows * RIM + LANES
                    for place in range(-R1, R1):
                        value = row_tap * tap(depth_taps, near - place)
                        bands[part, lane, target * 2 * R1 + R1 + place] = value
    return bands


def rim_cells(rows, depth, blocks):
    taps = smooth_taps(R2, sigma_tensor)
    weights = product_weights(rows)
    bands = np.zeros((blocks - 1, LANES, blocks * depth // COARSE))
    for boundary in range(blocks - 1):
        middle = (boundary + 1) * depth
        for cell in range(bands.shape[2]):
            for voxel in range(cell * COARSE, (cell + 1) * COARSE):
                for place in range(-R1, R1):
                    value = tap(taps, middle + place - voxel)
                    for row in range(rows):
                        bands[boundary, row * 2 * R1 + R1 + place, cell] += weights[row] * value
    return bands.reshape(-1, bands.shape[2])


def meeting_order(blocks):
    middle = blocks // 2
    return [middle, *range(middle + 1, blocks), *range(middle - 1, -1, -1)]


def own_columns(count):
    products = (count + 2 * HALO) * COARSE + 2 * R2
    voxels = products + 2 * R1
    return -(-products // 16) * 16, -(-voxels // 8) * 8


def fold(voxels):
    return -(-voxels // 16) * 8


def rim_x_bands(count):
    products, voxels = own_columns(count)
    bands = np.zeros((2, products, -(-voxels // 16) * 16))
    valid = (count + 2 * HALO) * COARSE + 2 * R2
    for kind in range(2):
        for row in range(valid):
            bands[kind, row, row : row + 2 * R1 + 1] = grad_taps(kind)
    taps = smooth_taps(R2, sigma_tensor)
    coarse = np.zeros((16, products))
    for column in range(count + 2 * HALO):
        for voxel in range(column * COARSE, (column + 1) * COARSE):
            coarse[column, voxel : voxel + 2 * R2 + 1] += taps
    return bands.reshape(2 * products, -1), coarse


def depth_bands(depth):
    bands = np.zeros((2, depth, depth))
    for kind in range(2):
        for place in range(depth):
            for near in range(max(place - R1, 0), min(place + R1 + 1, depth)):
                bands[kind, near, place] = tap(grad_taps(kind), near - place)
    return bands


def product_weights(rows):
    return row_weights(rows, R2, sigma_tensor) / (255.0 * GRAD_FACTOR) ** 2


def coarse_depth_bands(depth):
    taps = smooth_taps(R2, sigma_tensor)
    columns, cells = sizes(0, depth)
    bands = np.zeros((depth, LANES))
    for cell in range(cells):
        for voxel in range(COARSE):
            place = (cell - BEFORE) * COARSE + voxel
            for near in range(max(place - R2, 0), min(place + R2 + 1, depth)):
                bands[near, cell] += tap(taps, near - place)
    return bands


def coarse_x_bands(width):
    taps = smooth_taps(R2, sigma_tensor)
    places = product_rows(width)
    columns, cells = sizes(width, 0)
    bands = np.zeros((-(-columns // 16) * 16, len(places)))
    for column in range(columns):
        for voxel in range(COARSE):
            middle = (column - HALO) * COARSE + voxel
            for row, place in enumerate(places):
                if place is not None:
                    bands[column, row] += tap(taps, place - middle)
    return bands


def stacked(*pieces):
    widest = max(piece.shape[1] for piece in pieces)
    padded = [np.pad(piece, ((0, 0), (0, widest - piece.shape[1]))) for piece in pieces]
    starts = np.cumsum([0] + [len(piece) for piece in pieces])
    return jnp.asarray(as_bfloat16(np.concatenate(padded))), tuple(int(start) for start in starts)


def two_parts(values):
    high = values.astype(jnp.bfloat16).astype(jnp.float32)
    return jnp.concatenate([high, (values - high).astype(jnp.bfloat16).astype(jnp.float32)], axis=0)


def joined(parts):
    half = parts.shape[0] // 2
    return parts[:half] + parts[half:]


def column_rows(temp, cure, first):
    pad = jnp.zeros((8 - 2 * GHOST, temp.shape[1]), jnp.float32)
    return jnp.concatenate(
        [temp[first : first + GHOST, :], cure[first : first + GHOST, :], pad], axis=0
    )


def is_odd():
    return lax.rem(lax.axis_index("plane"), 2) == 1


def pack_kernel(
    intensity, temp_hbm, cure_hbm, x_hbm, z_hbm, far, near, own, x_parts, z_parts, temp, cure,
    grey, sems,
):
    rows, width, depth = intensity.shape
    copies = [
        pltpu.make_async_copy(intensity, grey, sems.at[0]),
        pltpu.make_async_copy(temp_hbm, temp, sems.at[1]),
        pltpu.make_async_copy(cure_hbm, cure, sems.at[2]),
        pltpu.make_async_copy(x_hbm, x_parts, sems.at[3]),
        pltpu.make_async_copy(z_hbm, z_parts, sems.at[4]),
    ]
    for copy in copies:
        copy.start()
    for copy in copies:
        copy.wait()
    odd = is_odd()
    count = temp.shape[0]
    sides = [
        two_parts(column_rows(temp, cure, first)).astype(jnp.bfloat16)
        for first in (0, count - GHOST)
    ]

    def send(left, right):
        for place, target, columns in ((0, left, sides[0]), (width - EDGE, right, sides[1])):
            for pair in range(rows // 2):
                two = [grey[2 * pair + i, place : place + EDGE, :] for i in range(2)]
                two = jnp.concatenate(two, axis=0).astype(jnp.float32)
                target[2 * EDGE * pair : 2 * EDGE * (pair + 1), :] = two.astype(jnp.bfloat16)
            for slot in range(temp.shape[1] // LANES):
                at = rows * EDGE + 16 * slot
                target[at : at + 16, :] = columns[:, slot * LANES : (slot + 1) * LANES]

    @pl.when(odd)
    def _():
        send(near, far)

    @pl.when(jnp.logical_not(odd))
    def _():
        send(far, near)

    for row in range(rows):
        half = (row % 2) * depth
        own[row // 2, :, half : half + depth] = grey[row].astype(jnp.float32).astype(jnp.bfloat16)


def packed_rows(values, size, first):
    depth = values[0].shape[1]
    lane = lax.broadcasted_iota(jnp.int32, values[0].shape, 1)
    packed = None
    for block, value in enumerate(values):
        shift = (size * block - first) % depth
        moved = value if shift == 0 else pltpu.roll(value, shift, 1)
        packed = moved if block == 0 else jnp.where(lane >= size * block, moved, packed)
    return packed


def edges_of(ref, rows):
    two = [
        ref[2 * EDGE * pair : 2 * EDGE * (pair + 1), :].astype(jnp.float32)
        for pair in range(rows // 2)
    ]
    voxels = [two[row // 2][row % 2 * EDGE : (row % 2 + 1) * EDGE] for row in range(rows)]
    slots = range(rows * EDGE, ref.shape[0], 16)
    columns = [joined(ref[at : at + 16, :].astype(jnp.float32)) for at in slots]
    return voxels, jnp.concatenate(columns, axis=1)


def product(first, second):
    return jnp.dot(first, second, preferred_element_type=jnp.float32)


def mirrored_filter(kind, values, even):
    rows = len(values)
    use_sum = even == (kind == 0)
    sign = 1.0 if use_sum else -1.0
    half = [values[row] + sign * values[rows - 1 - row] for row in range(rows // 2)]
    results = []
    for row in range(rows // 2):
        total = None
        for source, value in enumerate(half):
            near = tap(grad_taps(kind), source - row)
            far = tap(grad_taps(kind), rows - 1 - source - row)
            weight = 0.5 * (near + sign * far)
            total = weight * value if total is None else total + weight * value
        results.append(total)
    return results


def weighted_products(three, weight):
    pairs = ((0, 0), (1, 1), (2, 2), (0, 1), (0, 2), (1, 2))
    first = [weight * value for value in three]
    return [first[a] * three[b] for a, b in pairs]


def late_mask(count, width):
    row = lax.broadcasted_iota(jnp.int32, (count, LANES), 0)
    left = width - 2 * R1 - EARLY
    place = jnp.where(row < left + EDGE, row - left + R1 - EDGE, row - left - EDGE + width - R1)
    place = place + lax.axis_index("plane") * width
    inside = (place >= 0) & (place < lax.axis_size("plane") * width)
    return jnp.where(inside | (row < left), 1.0, 0.0)


def all_sums(products, coarse, sx):
    kinds, count, lanes = products.shape
    side_by_side = jnp.concatenate([products[index] for index in range(kinds)], axis=1)
    along = product(sx, side_by_side).astype(jnp.bfloat16)
    parts = [along[:, index * lanes : (index + 1) * lanes] for index in range(kinds)]
    return product(jnp.concatenate(parts, axis=0), coarse)


def tensor_sums(window, bands, sx, mask, diagonal, z_parts, across, filtered, grads, products):
    pairs, height, double = window.shape
    rows, depth = 2 * pairs, double // 2
    count = bands.shape[0] // 2
    for pair in range(pairs):
        across[pair] = product(bands, window[pair])

    def filter_rows(group, carry):
        start = pl.multiple_of(group * 16, 16)
        kinds = [
            [
                across[row // 2, pl.ds(kind * count + start, 16), pl.ds((row % 2) * depth, depth)]
                for row in range(rows)
            ]
            for kind in range(2)
        ]
        for part in range(3):
            values = kinds[X_KINDS[part]]
            results = mirrored_filter(ROW_KINDS[part], values, True)
            results += mirrored_filter(ROW_KINDS[part], values, False)
            for row, result in enumerate(results):
                lanes = pl.ds((row % 2) * depth, depth)
                filtered[part, row // 2, pl.ds(start, 16), lanes] = result.astype(jnp.bfloat16)
        return carry

    lax.fori_loop(0, count // 16, filter_rows, 0)
    for part in range(3):
        at = DEPTH_KINDS[part] * double
        for pair in range(pairs):
            grads[part, pair] = product(filtered[part, pair], diagonal[at : at + double, :])

    weights = product_weights(rows)
    layer = lax.axis_index("depth")
    first, last = layer == 0, layer == lax.axis_size("depth") - 1
    place = lax.broadcasted_iota(jnp.int32, (16, depth), 1)
    complete = ((place >= R1) | first) & ((place < depth - R1) | last)
    complete = jnp.where(complete, 1.0, 0.0)

    def multiply(group, carry):
        start = pl.multiple_of(group * 16, 16)
        inside = complete if mask is None else complete * mask[pl.ds(start, 16), :]
        totals = None
        for row in range(rows):
            lanes = pl.ds((row % 2) * depth, depth)
            three = [grads[part, row // 2, pl.ds(start, 16), lanes] for part in range(3)]
            terms = weighted_products(three, 2.0 * float(weights[row % (rows // 2)]))
            totals = terms if row == 0 else [a + b for a, b in zip(totals, terms)]
        for index in range(6):
            products[index, pl.ds(start, 16), :] = (totals[index] * inside).astype(jnp.bfloat16)
        return carry

    lax.fori_loop(0, count // 16, multiply, 0)
    return all_sums(products, z_parts[double : double + depth, :], sx)


def early_kernel(*refs):
    starts, own, x_parts, z_parts, *rest = refs
    count = (len(rest) - 7) // 2
    constants, (sums, diagonal), held = rest[:count], rest[count : count + 2], rest[count + 2 : -5]
    across, filtered, grads, products, sems = rest[-5:]
    copies = [
        pltpu.make_async_copy(source, target, sems.at[index])
        for index, (source, target) in enumerate(zip(constants, held))
    ]
    for copy in copies:
        copy.start()
    pairs, width, double = own.shape
    depth = double // 2
    empty = jnp.zeros((depth, depth), jnp.bfloat16)
    for kind in range(2):
        for half in range(2):
            at = pl.ds(kind * double + half * depth, depth)
            band = z_parts[kind * depth : (kind + 1) * depth, :]
            diagonal[at, half * depth : (half + 1) * depth] = band
            diagonal[at, (1 - half) * depth : (2 - half) * depth] = empty
    bands = x_parts[starts[0] : starts[1], :width]
    sx = x_parts[starts[1] : starts[2], :EARLY]
    sums[...] = tensor_sums(
        own, bands, sx, None, diagonal, z_parts, across, filtered, grads, products
    )
    for copy in copies:
        copy.wait()


def late_kernel(
    starts, own, far, near, x_late, z_parts, diagonal, early_sums, temp, cure, out_hbm,
    window, across, filtered, grads, products, mask, out, sems,
):
    pairs, width, double = own.shape
    rows, depth = 2 * pairs, double // 2
    count, lanes = temp.shape
    odd = is_odd()
    depths, layer = lax.axis_size("depth"), lax.axis_index("depth")
    outer, outer_columns = edges_of(far, rows)
    inner, inner_columns = edges_of(near, rows)
    values = []
    for row in range(rows):
        half = (row % 2) * depth
        middle = own[row // 2, :, half : half + depth].astype(jnp.float32)
        left = jnp.where(odd, inner[row], outer[row])
        right = jnp.where(odd, outer[row], inner[row])
        whole = jnp.concatenate([left, middle, right], axis=0)
        window[row // 2, :, half : half + depth] = whole.astype(jnp.bfloat16)
        values.append(whole)
    left = jnp.where(odd, inner_columns, outer_columns)
    right = jnp.where(odd, outer_columns, inner_columns)

    products_x, voxels = own_columns(count)
    folded, stride = fold(voxels), COARSE * count
    below = packed_rows(values, RIM, depth - RIM)
    above = pltpu.roll(packed_rows(values, RIM, 0), rows * RIM, 1)
    lane = lax.broadcasted_iota(jnp.int32, below.shape, 1)
    tiles = [jnp.where(lane < rows * RIM, below, above), above, pltpu.roll(above, HALF, 1)]
    missing = stride * (depths - 1) + voxels - below.shape[0]
    if missing > 0:
        spare = jnp.zeros((-(-missing // 8) * 8, LANES), jnp.float32)
        tiles = [jnp.concatenate([tile, spare], axis=0) for tile in tiles]

    height = count + 2 * HALO
    half_lane = lax.broadcasted_iota(jnp.int32, (folded, LANES), 1) < HALF
    order = meeting_order(out.shape[0])
    for position, target in enumerate(order):
        at = stride * target
        second = jnp.where(
            half_lane,
            tiles[1][at : at + folded],
            tiles[2][at + voxels - folded : at + voxels],
        )
        rims = jnp.concatenate([tiles[0][at : at + voxels], second], axis=0)
        out[position, 0 : voxels + folded, :] = rims.astype(jnp.bfloat16)
    split = (pl.ds(0, voxels + folded), pl.ds(voxels + folded, out.shape[1] - voxels - folded))
    copies = [
        pltpu.make_async_copy(out.at[:, part, :], out_hbm.at[:, part, :], sems.at[index])
        for index, part in enumerate(split)
    ]
    copies[0].start()

    late = across.shape[1] // 2
    mask[...] = late_mask(late, width)
    bands = x_late[starts[0] : starts[1], :]
    sx = x_late[starts[1] : starts[2], :late]
    sums = early_sums[...] + tensor_sums(
        window, bands, sx, mask, diagonal, z_parts, across, filtered, grads, products
    )
    high = sx.shape[0]
    total = [sums[index * high : (index + 1) * high] for index in range(6)]
    trace = total[0] + total[1] + total[2]
    lane = lax.broadcasted_iota(jnp.int32, trace.shape, 1)
    three = jnp.where(lane < SLOT, trace, pltpu.roll(total[1], SLOT, 1))
    three = jnp.where(lane < 2 * SLOT, three, pltpu.roll(total[2], 2 * SLOT, 1))
    xz = [total[5]] + [pltpu.roll(total[5], index * SLOT, 1) for index in range(1, 3)]

    own_first, own_last = column_rows(temp, cure, 0), column_rows(temp, cure, count - GHOST)
    for position, target in enumerate(order):
        piece = jnp.where(layer == target - 1, own_last, 0.0)
        piece = jnp.where(layer == target + 1, own_first, piece)
        if target == 0:
            piece = jnp.where(layer == depths - 1, left, piece)
        if target == out.shape[0] - 1:
            piece = jnp.where(layer == 0, right, piece)
        at = count * target
        pieces = [three[at : at + height], jnp.zeros((4, LANES), jnp.float32)]
        for index in range(3):
            size = min(4, height - 4 * index)
            if size > 0:
                part = xz[index][at + 4 * index : at + 4 * index + size]
                if size < 4:
                    spare = jnp.zeros((4 - size, LANES), jnp.float32)
                    part = jnp.concatenate([part, spare], axis=0)
                pieces[1] = jnp.where(lane[:4] < index * SLOT, pieces[1], part)
        for slot in range(lanes // LANES):
            pieces.append(piece[0 : 2 * GHOST, slot * LANES : (slot + 1) * LANES])
        filled = sum(part.shape[0] for part in pieces)
        if filled < 24:
            pieces.append(jnp.zeros((24 - filled, LANES), jnp.float32))
        sent = two_parts(jnp.concatenate(pieces, axis=0))
        out[position, voxels + folded :, :] = sent.astype(jnp.bfloat16)
    copies[1].start()
    for copy in copies:
        copy.wait()


def rim_sums(chunks, count, starts, flat, steep, cells):
    parts = chunks.shape[0]
    rows_x, voxels = own_columns(count)
    folded = fold(voxels)
    tall = -(-voxels // 16) * 16
    spare = [jnp.zeros((tall - voxels, LANES), jnp.float32)] if tall > voxels else []
    tiles = []
    order = meeting_order(parts)
    for part in range(parts):
        rims = chunks[order.index(part), 0 : voxels + folded, :].astype(jnp.float32)
        second = rims[voxels:]
        second = [second[: voxels - folded], pltpu.roll(second, HALF, 1)]
        for tile in ([rims[:voxels]], second):
            tiles.append(jnp.concatenate(tile + spare, axis=0).astype(jnp.bfloat16))
    result = product(
        steep[starts[1] : starts[2], :tall], jnp.concatenate(tiles, axis=1)
    ).astype(jnp.bfloat16)
    kinds = []
    for kind in range(2):
        values = result[kind * rows_x : (kind + 1) * rows_x]
        tile = lambda index: values[:, index * LANES : (index + 1) * LANES]
        stack = [
            jnp.concatenate([tile(2 * part), tile(2 * part + 2), tile(2 * part + 3)], axis=1)
            for part in range(parts - 1)
        ]
        kinds.append(jnp.concatenate(stack, axis=0))
    both = product(kinds[0], flat[...])
    three = (both[:, :LANES], product(kinds[1], steep[starts[0] : starts[1], :]), both[:, LANES:])

    index = lax.axis_index("plane") * lax.axis_size("depth") + lax.axis_index("depth")
    total = lax.axis_size("plane") * lax.axis_size("depth") * count * COARSE
    place = lax.rem(lax.broadcasted_iota(jnp.int32, three[0].shape, 0), rows_x)
    place = place + (index * count - HALO) * COARSE - R2
    inside = jnp.where((place >= 0) & (place < total), 1.0, 0.0)
    wide = []
    for term in weighted_products(three, inside):
        term = term.astype(jnp.bfloat16)
        wide += [term[part * rows_x : (part + 1) * rows_x] for part in range(parts - 1)]
    sx = steep[starts[2] : starts[3], :rows_x]
    along = product(sx, jnp.concatenate(wide, axis=1)).astype(jnp.bfloat16)
    step = (parts - 1) * LANES
    along = [along[:, kind * step : (kind + 1) * step] for kind in range(6)]
    sums = product(jnp.concatenate(along, axis=0), cells[...])
    return [sums[kind * 16 : (kind + 1) * 16] for kind in range(6)]


def cure_kernel(
    cells, starts, chunks, temp_in, cure_in, tools, flat, steep, rim_bands, temp_hbm, cure_hbm,
    conduct_hbm, temp_out, cure_out, conduct_out, sems,
):
    count, lanes = temp_in.shape
    parts = chunks.shape[0]
    planes, depths = lax.axis_size("plane"), lax.axis_size("depth")
    plane, layer = lax.axis_index("plane"), lax.axis_index("depth")
    height = count + 2 * HALO
    own = cells - BEFORE - AFTER
    lane = lax.broadcasted_iota(jnp.int32, (16, lanes), 1)
    row = lax.broadcasted_iota(jnp.int32, (16, lanes), 0)
    at_sums = chunks.shape[1] - 48
    order = meeting_order(parts)

    near = rim_sums(chunks, count, starts, flat, steep, rim_bands)
    sums = [near[0] + near[1] + near[2], near[1], near[2], near[5]]
    blocks = []
    for part in range(parts):
        first_cell = own * part - BEFORE
        here = (lane >= first_cell) & (lane < first_cell + cells)
        values = joined(chunks[order.index(part), at_sums:, :].astype(jnp.float32))
        blocks.append(values)
        xz = values[height : height + 4]
        xz = [xz] + [pltpu.roll(xz, LANES - index * SLOT, 1) for index in range(1, 3)]
        spare = jnp.zeros((4, LANES), jnp.float32)
        xz = jnp.concatenate([*xz, spare], axis=0)
        for index in range(4):
            chunk = values[0:16] if index < 3 else xz
            if lanes > LANES:
                spare = jnp.zeros((16, lanes - LANES), jnp.float32)
                chunk = jnp.concatenate([chunk, spare], axis=1)
            shift = (first_cell - (index % 3) * SLOT) % lanes
            moved = chunk if shift == 0 else pltpu.roll(chunk, shift, 1)
            sums[index] = sums[index] + jnp.where(here, moved, 0.0)
    trace = sums[0]
    scale = (conduct_fiber - conduct_matrix) / (2.0 * trace + tensor_eps)
    conduct = [
        conduct_matrix + scale * (trace - sums[1]),
        -scale * sums[3],
        conduct_matrix + scale * (trace - sums[2]),
    ]
    for kind in range(3):
        conduct_out[kind] = conduct[kind][HALO : HALO + count]
    copies = [
        pltpu.make_async_copy(conduct_out, conduct_hbm, sems.at[0]),
        pltpu.make_async_copy(temp_out, temp_hbm, sems.at[1]),
        pltpu.make_async_copy(cure_out, cure_hbm, sems.at[2]),
    ]
    copies[0].start()

    slots = range(height + 4, height + 4 + 2 * GHOST * (lanes // LANES), 2 * GHOST)
    columns = [
        jnp.concatenate([values[at : at + 2 * GHOST] for at in slots], axis=1) for values in blocks
    ]
    before, after = columns[parts - 1], columns[0]
    for part in range(parts - 1):
        before = jnp.where(layer == part + 1, columns[part], before)
        after = jnp.where(layer == part, columns[part + 1], after)
    spare = jnp.full((16 - count - 2 * GHOST, lanes), 0.5, jnp.float32)
    temp = jnp.concatenate([before[:GHOST], temp_in[...], after[:GHOST], 8.0 * spare], axis=0)
    cure = jnp.concatenate([before[GHOST:], cure_in[...], after[GHOST:], spare], axis=0)
    gap = GHOST - HALO
    xx, xz, zz = [pltpu.roll(part, gap, 0) for part in conduct]

    first = (plane == 0) & (layer == 0)
    last = (plane == planes - 1) & (layer == depths - 1)
    for step in range(STEPS):
        top, bottom = tools[2 * step : 2 * step + 1, :], tools[2 * step + 1 : 2 * step + 2, :]
        temp = jnp.where((row < GHOST) & first, temp[GHOST : GHOST + 1], temp)
        temp = jnp.where(
            (row >= GHOST + count) & last, temp[GHOST + count - 1 : GHOST + count], temp
        )
        cooler = jnp.where(lane == 0, top, pltpu.roll(temp, 1, 1))
        later = jnp.where(lane == lanes - 1, bottom, pltpu.roll(temp, lanes - 1, 1))
        slant = later - cooler
        second_x = pltpu.roll(temp, 15, 0) - 2.0 * temp + pltpu.roll(temp, 1, 0)
        second_z = later - 2.0 * temp + cooler
        cross = 0.25 * (pltpu.roll(slant, 15, 0) - pltpu.roll(slant, 1, 0))
        spread = xx * second_x + 2.0 * xz * cross + zz * second_z
        inverse = 1.0 / reference_temp - 1.0 / temp
        left = 1.0 - cure
        rate = rate_first * jnp.exp(energy_first * inverse) + rate_second * jnp.exp(
            energy_second * inverse
        ) * jnp.sqrt(cure)
        rate = rate * (left * jnp.sqrt(left))
        temp = temp + time_step * (spread + heat_release * rate)
        cure = cure + time_step * rate
    temp_out[...] = temp[GHOST : GHOST + count]
    cure_out[...] = cure[GHOST : GHOST + count]
    for copy in copies[1:]:
        copy.start()
    for copy in copies:
        copy.wait()


def on_device(intensity, temp_start, cure_start, tool_levels, plan):
    rows, width, depth = intensity.shape
    count, lanes = temp_start.shape
    planes, depths = lax.axis_size("plane"), lax.axis_size("depth")
    columns, cells = sizes(width, depth)
    bf16 = jnp.bfloat16
    slots = rows * EDGE + 16 * (lanes // LANES)
    params = pltpu.CompilerParams(vmem_limit_bytes=24 * 1024 * 1024)
    vmem = pl.BlockSpec(memory_space=pltpu.VMEM)
    stay = pl.BlockSpec(memory_space=pltpu.HBM)

    fixed = lambda values: pltpu.with_memory_space_constraint(values, pltpu.HBM)
    bands, coarse = x_bands(width), coarse_x_bands(width)
    late = bands.shape[1] - EARLY
    middle = bands[:, :EARLY, EDGE : EDGE + width]
    x_hbm, early_starts = stacked(middle.reshape(2 * EARLY, -1), coarse[:, :EARLY])
    z_hbm, _ = stacked(*depth_bands(depth), coarse_depth_bands(depth))
    x_late, late_starts = stacked(bands[:, EARLY:].reshape(2 * late, -1), coarse[:, EARLY:])
    rims = rim_bands(rows)
    flat, _ = stacked(np.concatenate([rims[0], rims[2]], axis=1))
    steep, rim_starts = stacked(rims[1], *rim_x_bands(count))
    cell_bands, _ = stacked(rim_cells(rows, depth, depths))
    constants = (x_late, flat, steep, cell_bands)
    far, near, own, x_parts, z_parts, temp, cure = pl.pallas_call(
        pack_kernel,
        name="pack",
        out_shape=(
            pltpu.VMEM((slots, depth), bf16),
            pltpu.VMEM((slots, depth), bf16),
            pltpu.VMEM((rows // 2, width, 2 * depth), bf16),
            pltpu.VMEM(x_hbm.shape, bf16),
            pltpu.VMEM(z_hbm.shape, bf16),
            pltpu.VMEM((count, lanes), jnp.float32),
            pltpu.VMEM((count, lanes), jnp.float32),
        ),
        in_specs=[stay] * 5,
        scratch_shapes=[
            pltpu.VMEM((rows, width, depth), jnp.int32),
            pltpu.SemaphoreType.DMA((5,)),
        ],
        compiler_params=params,
    )(*[fixed(values) for values in (intensity, temp_start, cure_start, x_hbm, z_hbm)])

    def moved(values, pairs):
        index = [(p * depths + d, q * depths + e) for (p, d), (q, e) in pairs]
        return lax.ppermute(values, ("plane", "depth"), index)

    def swapped(values, first):
        pairs = [(p, p + 1) for p in range(first, planes - 1, 2)]
        pairs += [(q, p) for p, q in pairs]
        return moved(values, [((p, d), (q, d)) for p, q in pairs for d in range(depths)])

    far = swapped(far, 1)
    near = swapped(near, 0)

    high = coarse.shape[0]

    def scratch(count):
        return [
            pltpu.VMEM((rows // 2, 2 * count, 2 * depth), jnp.float32),
            pltpu.VMEM((3, rows // 2, count, 2 * depth), bf16),
            pltpu.VMEM((3, rows // 2, count, 2 * depth), jnp.float32),
            pltpu.VMEM((6, count, depth), bf16),
        ]

    def cost(count):
        return pl.CostEstimate(
            flops=2 * rows * (2 * count) * 160 * depth * 4,
            bytes_accessed=4_000_000,
            transcendentals=0,
        )

    early_sums, diagonal, x_late, flat, steep, cell_bands = pl.pallas_call(
        functools.partial(early_kernel, early_starts),
        name="early",
        out_shape=(
            pltpu.VMEM((6 * high, LANES), jnp.float32),
            pltpu.VMEM((4 * depth, 2 * depth), bf16),
            *[pltpu.VMEM(values.shape, bf16) for values in constants],
        ),
        in_specs=[vmem] * 3 + [stay] * len(constants),
        scratch_shapes=scratch(EARLY) + [pltpu.SemaphoreType.DMA((len(constants),))],
        cost_estimate=cost(EARLY),
        compiler_params=params,
    )(own, x_parts, z_parts, *[fixed(values) for values in constants])

    products_x, voxels = own_columns(count)
    chunk_shape = (depths, voxels + fold(voxels) + 48, LANES)
    chunks = pl.pallas_call(
        functools.partial(late_kernel, late_starts),
        name="late",
        out_shape=pltpu.HBM(chunk_shape, bf16),
        in_specs=[vmem] * 9,
        out_specs=stay,
        scratch_shapes=[pltpu.VMEM((rows // 2, width + 2 * EDGE, 2 * depth), bf16)]
        + scratch(late)
        + [
            pltpu.VMEM((late, LANES), jnp.float32),
            pltpu.VMEM(chunk_shape, bf16),
            pltpu.SemaphoreType.DMA((2,)),
        ],
        cost_estimate=cost(late),
        compiler_params=params,
    )(own, far, near, x_late, z_parts, diagonal, early_sums, temp, cure)

    faces = plan.reshape(2 * STEPS, 1) == jnp.arange(tool_levels.shape[0], dtype=jnp.int32)
    tools = jnp.sum(
        jnp.where(faces, tool_levels, jnp.zeros_like(tool_levels)), axis=1, keepdims=True
    )

    chunks = lax.all_to_all(
        chunks,
        "depth",
        split_axis=0,
        concat_axis=0,
        tiled=True,
        axis_index_groups=[meeting_order(depths)],
    )

    return pl.pallas_call(
        functools.partial(cure_kernel, cells, rim_starts),
        name="cure",
        out_shape=(
            pltpu.HBM((count, lanes), jnp.float32),
            pltpu.HBM((count, lanes), jnp.float32),
            pltpu.HBM((3, count, lanes), jnp.float32),
        ),
        in_specs=[vmem] * 7,
        out_specs=(stay, stay, stay),
        scratch_shapes=[
            pltpu.VMEM((count, lanes), jnp.float32),
            pltpu.VMEM((count, lanes), jnp.float32),
            pltpu.VMEM((3, count, lanes), jnp.float32),
            pltpu.SemaphoreType.DMA((3,)),
        ],
        compiler_params=params,
    )(chunks, temp, cure, tools, flat, steep, cell_bands)


def solution(mesh):
    return jax.shard_map(
        on_device,
        mesh=mesh,
        in_specs=(
            P(None, "plane", "depth"),
            P(("plane", "depth"), None),
            P(("plane", "depth"), None),
            P(),
            P(),
        ),
        out_specs=(
            P(("plane", "depth"), None),
            P(("plane", "depth"), None),
            P(None, ("plane", "depth"), None),
        ),
        check_vma=False,
    )
```

```python
import functools

import jax
import jax.numpy as jnp
import ml_dtypes
import numpy as np
from jax import lax
from jax.experimental import pallas as pl
from jax.experimental.pallas import tpu as pltpu
from jax.sharding import PartitionSpec as P

ROWS = 8
R1 = 6
R2 = 10
COARSE = 4
STEPS = 3

sigma_grad = 2.0
sigma_tensor = 3.3
conduct_matrix = 0.3
conduct_fiber = 1.5
time_step = 0.25
heat_release = 0.4
rate_first = 0.15
rate_second = 0.6
energy_first = 30.0
energy_second = 25.0
reference_temp = 4.2
tensor_eps = 1e-06

LANES = 128
HALO = 2
EDGE = HALO * COARSE + R1 + R2
EARLY = 80
GHOST = 3
RIM = 2 * R1
BEFORE = -(-(R2 - R1) // COARSE)
AFTER = BEFORE
HALF = LANES // 2
SLOT = 40
ROW_KINDS = (1, 0, 0)
X_KINDS = (0, 1, 0)
DEPTH_KINDS = (0, 0, 1)


def smooth_taps(radius, sigma):
    offsets = np.arange(-radius, radius + 1) * 1.0
    weights = np.exp(-0.5 * offsets * offsets / (sigma * sigma))
    return weights / weights.sum()


def slope_taps(radius, sigma):
    offsets = np.arange(-radius, radius + 1) * 1.0
    weights = np.exp(-0.5 * offsets * offsets / (sigma * sigma))
    return offsets * weights / np.sum(offsets * offsets * weights)


def row_weights(count, radius, sigma):
    taps = smooth_taps(radius, sigma)
    result = np.zeros(count)
    for source in range(count):
        for target in range(count):
            offset = target - source
            if abs(offset) <= radius:
                result[source] += taps[offset + radius]
    return result


def rounded(taps):
    best = None
    for factor in np.linspace(1.0, 2.0, 20001)[:-1]:
        near = (taps * factor).astype(np.float32).astype(ml_dtypes.bfloat16).astype(np.float64)
        error = np.abs(near / factor - taps).sum()
        if best is None or error < best[0]:
            best = (error, near, factor)
    return best[1], best[2]


def as_bfloat16(matrix):
    return matrix.astype(np.float32).astype(ml_dtypes.bfloat16)


def halves(matrix):
    high = as_bfloat16(matrix)
    return high, as_bfloat16(matrix - high.astype(np.float64))


def sizes(width, depth):
    columns = width // COARSE + 2 * HALO
    cells = depth // COARSE + BEFORE + AFTER
    return columns, cells


def product_rows(width):
    places = [*range(R1, width - R1), *range(R1 - EDGE, R1), *range(width - R1, width + EDGE - R1)]
    return places + [None] * (-len(places) % 16)


GRAD_TAPS = tuple(
    rounded(taps(R1, sigma_grad)) for taps in (smooth_taps, slope_taps)
)
GRAD_FACTOR = GRAD_TAPS[0][1] ** 2 * GRAD_TAPS[1][1]


def grad_taps(kind):
    return GRAD_TAPS[kind][0]


def tap(taps, offset):
    radius = (len(taps) - 1) // 2
    return float(taps[offset + radius]) if abs(offset) <= radius else 0.0


def x_bands(width):
    places = product_rows(width)
    bands = np.zeros((2, len(places), width + 2 * EDGE))
    for kind in range(2):
        for row, place in enumerate(places):
            if place is not None:
                first = place + EDGE - R1
                bands[kind, row, first : first + 2 * R1 + 1] = grad_taps(kind)
    return bands


def rim_bands(rows):
    bands = np.zeros((3, 3 * LANES, LANES))
    for part in range(3):
        row_taps, depth_taps = grad_taps(ROW_KINDS[part]), grad_taps(DEPTH_KINDS[part])
        for source in range(rows):
            for target in range(rows):
                row_tap = tap(row_taps, source - target)
                for near in range(-RIM, RIM):
                    lane = source * RIM + near % RIM
                    if near >= 0:
                        lane += rows * RIM + LANES
                    for place in range(-R1, R1):
                        value = row_tap * tap(depth_taps, near - place)
                        bands[part, lane, target * 2 * R1 + R1 + place] = value
    return bands


def rim_cells(rows, depth, blocks):
    taps = smooth_taps(R2, sigma_tensor)
    weights = product_weights(rows)
    bands = np.zeros((blocks - 1, LANES, blocks * depth // COARSE))
    for boundary in range(blocks - 1):
        middle = (boundary + 1) * depth
        for cell in range(bands.shape[2]):
            for voxel in range(cell * COARSE, (cell + 1) * COARSE):
                for place in range(-R1, R1):
                    value = tap(taps, middle + place - voxel)
                    for row in range(rows):
                        bands[boundary, row * 2 * R1 + R1 + place, cell] += weights[row] * value
    return bands.reshape(-1, bands.shape[2])


def meeting_order(blocks):
    return [*range(blocks - 1, -1, -1)]


def own_columns(count):
    products = (count + 2 * HALO) * COARSE + 2 * R2
    voxels = products + 2 * R1
    return -(-products // 16) * 16, -(-voxels // 8) * 8


def fold(voxels):
    return -(-voxels // 16) * 8


def rim_x_bands(count):
    products, voxels = own_columns(count)
    bands = np.zeros((2, products, -(-voxels // 16) * 16))
    valid = (count + 2 * HALO) * COARSE + 2 * R2
    for kind in range(2):
        for row in range(valid):
            bands[kind, row, row : row + 2 * R1 + 1] = grad_taps(kind)
    taps = smooth_taps(R2, sigma_tensor)
    coarse = np.zeros((16, products))
    for column in range(count + 2 * HALO):
        for voxel in range(column * COARSE, (column + 1) * COARSE):
            coarse[column, voxel : voxel + 2 * R2 + 1] += taps
    return bands.reshape(2 * products, -1), coarse


def depth_bands(depth):
    bands = np.zeros((2, depth, depth))
    for kind in range(2):
        for place in range(depth):
            for near in range(max(place - R1, 0), min(place + R1 + 1, depth)):
                bands[kind, near, place] = tap(grad_taps(kind), near - place)
    return bands


def product_weights(rows):
    return row_weights(rows, R2, sigma_tensor) / (255.0 * GRAD_FACTOR) ** 2


def coarse_depth_bands(depth):
    taps = smooth_taps(R2, sigma_tensor)
    columns, cells = sizes(0, depth)
    bands = np.zeros((depth, LANES))
    for cell in range(cells):
        for voxel in range(COARSE):
            place = (cell - BEFORE) * COARSE + voxel
            for near in range(max(place - R2, 0), min(place + R2 + 1, depth)):
                bands[near, cell] += tap(taps, near - place)
    return bands


def coarse_x_bands(width):
    taps = smooth_taps(R2, sigma_tensor)
    places = product_rows(width)
    columns, cells = sizes(width, 0)
    bands = np.zeros((-(-columns // 16) * 16, len(places)))
    for column in range(columns):
        for voxel in range(COARSE):
            middle = (column - HALO) * COARSE + voxel
            for row, place in enumerate(places):
                if place is not None:
                    bands[column, row] += tap(taps, place - middle)
    return bands


def stacked(*pieces):
    widest = max(piece.shape[1] for piece in pieces)
    padded = [np.pad(piece, ((0, 0), (0, widest - piece.shape[1]))) for piece in pieces]
    starts = np.cumsum([0] + [len(piece) for piece in pieces])
    return jnp.asarray(as_bfloat16(np.concatenate(padded))), tuple(int(start) for start in starts)


def two_parts(values):
    high = values.astype(jnp.bfloat16).astype(jnp.float32)
    return jnp.concatenate([high, (values - high).astype(jnp.bfloat16).astype(jnp.float32)], axis=0)


def joined(parts):
    half = parts.shape[0] // 2
    return parts[:half] + parts[half:]


def column_rows(temp, cure, first):
    pad = jnp.zeros((8 - 2 * GHOST, temp.shape[1]), jnp.float32)
    return jnp.concatenate(
        [temp[first : first + GHOST, :], cure[first : first + GHOST, :], pad], axis=0
    )


def is_odd():
    return lax.rem(lax.axis_index("plane"), 2) == 1


def pack_kernel(
    intensity, temp_hbm, cure_hbm, x_hbm, z_hbm, far, near, own, x_parts, z_parts, temp, cure,
    grey, sems,
):
    rows, width, depth = intensity.shape
    copies = [
        pltpu.make_async_copy(intensity, grey, sems.at[0]),
        pltpu.make_async_copy(temp_hbm, temp, sems.at[1]),
        pltpu.make_async_copy(cure_hbm, cure, sems.at[2]),
        pltpu.make_async_copy(x_hbm, x_parts, sems.at[3]),
        pltpu.make_async_copy(z_hbm, z_parts, sems.at[4]),
    ]
    for copy in copies:
        copy.start()
    for copy in copies:
        copy.wait()
    odd = is_odd()
    count = temp.shape[0]
    sides = [
        two_parts(column_rows(temp, cure, first)).astype(jnp.bfloat16)
        for first in (0, count - GHOST)
    ]

    def send(left, right):
        for place, target, columns in ((0, left, sides[0]), (width - EDGE, right, sides[1])):
            for pair in range(rows // 2):
                two = [grey[2 * pair + i, place : place + EDGE, :] for i in range(2)]
                two = jnp.concatenate(two, axis=0).astype(jnp.float32)
                target[2 * EDGE * pair : 2 * EDGE * (pair + 1), :] = two.astype(jnp.bfloat16)
            for slot in range(temp.shape[1] // LANES):
                at = rows * EDGE + 16 * slot
                target[at : at + 16, :] = columns[:, slot * LANES : (slot + 1) * LANES]

    @pl.when(odd)
    def _():
        send(near, far)

    @pl.when(jnp.logical_not(odd))
    def _():
        send(far, near)

    for row in range(rows):
        half = (row % 2) * depth
        own[row // 2, :, half : half + depth] = grey[row].astype(jnp.float32).astype(jnp.bfloat16)


def packed_rows(values, size, first):
    depth = values[0].shape[1]
    lane = lax.broadcasted_iota(jnp.int32, values[0].shape, 1)
    packed = None
    for block, value in enumerate(values):
        shift = (size * block - first) % depth
        moved = value if shift == 0 else pltpu.roll(value, shift, 1)
        packed = moved if block == 0 else jnp.where(lane >= size * block, moved, packed)
    return packed


def edges_of(ref, rows):
    two = [
        ref[2 * EDGE * pair : 2 * EDGE * (pair + 1), :].astype(jnp.float32)
        for pair in range(rows // 2)
    ]
    voxels = [two[row // 2][row % 2 * EDGE : (row % 2 + 1) * EDGE] for row in range(rows)]
    slots = range(rows * EDGE, ref.shape[0], 16)
    columns = [joined(ref[at : at + 16, :].astype(jnp.float32)) for at in slots]
    return voxels, jnp.concatenate(columns, axis=1)


def product(first, second):
    return jnp.dot(first, second, preferred_element_type=jnp.float32)


def mirrored_filter(kind, values, even):
    rows = len(values)
    use_sum = even == (kind == 0)
    sign = 1.0 if use_sum else -1.0
    half = [values[row] + sign * values[rows - 1 - row] for row in range(rows // 2)]
    results = []
    for row in range(rows // 2):
        total = None
        for source, value in enumerate(half):
            near = tap(grad_taps(kind), source - row)
            far = tap(grad_taps(kind), rows - 1 - source - row)
            weight = 0.5 * (near + sign * far)
            total = weight * value if total is None else total + weight * value
        results.append(total)
    return results


def weighted_products(three, weight):
    pairs = ((0, 0), (1, 1), (2, 2), (0, 1), (0, 2), (1, 2))
    first = [weight * value for value in three]
    return [first[a] * three[b] for a, b in pairs]


def late_mask(count, width):
    row = lax.broadcasted_iota(jnp.int32, (count, LANES), 0)
    left = width - 2 * R1 - EARLY
    place = jnp.where(row < left + EDGE, row - left + R1 - EDGE, row - left - EDGE + width - R1)
    place = place + lax.axis_index("plane") * width
    inside = (place >= 0) & (place < lax.axis_size("plane") * width)
    return jnp.where(inside | (row < left), 1.0, 0.0)


def all_sums(products, coarse, sx):
    kinds, count, lanes = products.shape
    side_by_side = jnp.concatenate([products[index] for index in range(kinds)], axis=1)
    along = product(sx, side_by_side).astype(jnp.bfloat16)
    parts = [along[:, index * lanes : (index + 1) * lanes] for index in range(kinds)]
    return product(jnp.concatenate(parts, axis=0), coarse)


def tensor_sums(window, bands, sx, mask, diagonal, z_parts, across, filtered, grads, products):
    pairs, height, double = window.shape
    rows, depth = 2 * pairs, double // 2
    count = bands.shape[0] // 2
    for pair in range(pairs):
        across[pair] = product(bands, window[pair])

    def filter_rows(group, carry):
        start = pl.multiple_of(group * 16, 16)
        kinds = [
            [
                across[row // 2, pl.ds(kind * count + start, 16), pl.ds((row % 2) * depth, depth)]
                for row in range(rows)
            ]
            for kind in range(2)
        ]
        for part in range(3):
            values = kinds[X_KINDS[part]]
            results = mirrored_filter(ROW_KINDS[part], values, True)
            results += mirrored_filter(ROW_KINDS[part], values, False)
            for row, result in enumerate(results):
                lanes = pl.ds((row % 2) * depth, depth)
                filtered[part, row // 2, pl.ds(start, 16), lanes] = result.astype(jnp.bfloat16)
        return carry

    lax.fori_loop(0, count // 16, filter_rows, 0)
    for part in range(3):
        at = DEPTH_KINDS[part] * double
        for pair in range(pairs):
            grads[part, pair] = product(filtered[part, pair], diagonal[at : at + double, :])

    weights = product_weights(rows)
    layer = lax.axis_index("depth")
    first, last = layer == 0, layer == lax.axis_size("depth") - 1
    place = lax.broadcasted_iota(jnp.int32, (16, depth), 1)
    complete = ((place >= R1) | first) & ((place < depth - R1) | last)
    complete = jnp.where(complete, 1.0, 0.0)

    def multiply(group, carry):
        start = pl.multiple_of(group * 16, 16)
        inside = complete if mask is None else complete * mask[pl.ds(start, 16), :]
        totals = None
        for row in range(rows):
            lanes = pl.ds((row % 2) * depth, depth)
            three = [grads[part, row // 2, pl.ds(start, 16), lanes] for part in range(3)]
            terms = weighted_products(three, 2.0 * float(weights[row % (rows // 2)]))
            totals = terms if row == 0 else [a + b for a, b in zip(totals, terms)]
        for index in range(6):
            products[index, pl.ds(start, 16), :] = (totals[index] * inside).astype(jnp.bfloat16)
        return carry

    lax.fori_loop(0, count // 16, multiply, 0)
    return all_sums(products, z_parts[double : double + depth, :], sx)


def early_kernel(*refs):
    starts, own, x_parts, z_parts, *rest = refs
    count = (len(rest) - 7) // 2
    constants, (sums, diagonal), held = rest[:count], rest[count : count + 2], rest[count + 2 : -5]
    across, filtered, grads, products, sems = rest[-5:]
    copies = [
        pltpu.make_async_copy(source, target, sems.at[index])
        for index, (source, target) in enumerate(zip(constants, held))
    ]
    for copy in copies:
        copy.start()
    pairs, width, double = own.shape
    depth = double // 2
    empty = jnp.zeros((depth, depth), jnp.bfloat16)
    for kind in range(2):
        for half in range(2):
            at = pl.ds(kind * double + half * depth, depth)
            band = z_parts[kind * depth : (kind + 1) * depth, :]
            diagonal[at, half * depth : (half + 1) * depth] = band
            diagonal[at, (1 - half) * depth : (2 - half) * depth] = empty
    bands = x_parts[starts[0] : starts[1], :width]
    sx = x_parts[starts[1] : starts[2], :EARLY]
    sums[...] = tensor_sums(
        own, bands, sx, None, diagonal, z_parts, across, filtered, grads, products
    )
    for copy in copies:
        copy.wait()


def late_kernel(
    starts, own, far, near, x_late, z_parts, diagonal, early_sums, temp, cure, out_hbm,
    window, across, filtered, grads, products, mask, out, sems,
):
    pairs, width, double = own.shape
    rows, depth = 2 * pairs, double // 2
    count, lanes = temp.shape
    odd = is_odd()
    depths, layer = lax.axis_size("depth"), lax.axis_index("depth")
    outer, outer_columns = edges_of(far, rows)
    inner, inner_columns = edges_of(near, rows)
    values = []
    for row in range(rows):
        half = (row % 2) * depth
        middle = own[row // 2, :, half : half + depth].astype(jnp.float32)
        left = jnp.where(odd, inner[row], outer[row])
        right = jnp.where(odd, outer[row], inner[row])
        whole = jnp.concatenate([left, middle, right], axis=0)
        window[row // 2, :, half : half + depth] = whole.astype(jnp.bfloat16)
        values.append(whole)
    left = jnp.where(odd, inner_columns, outer_columns)
    right = jnp.where(odd, outer_columns, inner_columns)

    products_x, voxels = own_columns(count)
    folded, stride = fold(voxels), COARSE * count
    below = packed_rows(values, RIM, depth - RIM)
    above = pltpu.roll(packed_rows(values, RIM, 0), rows * RIM, 1)
    lane = lax.broadcasted_iota(jnp.int32, below.shape, 1)
    tiles = [jnp.where(lane < rows * RIM, below, above), above, pltpu.roll(above, HALF, 1)]
    missing = stride * (depths - 1) + voxels - below.shape[0]
    if missing > 0:
        spare = jnp.zeros((-(-missing // 8) * 8, LANES), jnp.float32)
        tiles = [jnp.concatenate([tile, spare], axis=0) for tile in tiles]

    height = count + 2 * HALO
    half_lane = lax.broadcasted_iota(jnp.int32, (folded, LANES), 1) < HALF
    order = meeting_order(out.shape[0])
    for position, target in enumerate(order):
        at = stride * target
        second = jnp.where(
            half_lane,
            tiles[1][at : at + folded],
            tiles[2][at + voxels - folded : at + voxels],
        )
        rims = jnp.concatenate([tiles[0][at : at + voxels], second], axis=0)
        out[position, 0 : voxels + folded, :] = rims.astype(jnp.bfloat16)
    split = (pl.ds(0, voxels + folded), pl.ds(voxels + folded, out.shape[1] - voxels - folded))
    copies = [
        pltpu.make_async_copy(out.at[:, part, :], out_hbm.at[:, part, :], sems.at[index])
        for index, part in enumerate(split)
    ]
    copies[0].start()

    late = across.shape[1] // 2
    mask[...] = late_mask(late, width)
    bands = x_late[starts[0] : starts[1], :]
    sx = x_late[starts[1] : starts[2], :late]
    sums = early_sums[...] + tensor_sums(
        window, bands, sx, mask, diagonal, z_parts, across, filtered, grads, products
    )
    high = sx.shape[0]
    total = [sums[index * high : (index + 1) * high] for index in range(6)]
    trace = total[0] + total[1] + total[2]
    lane = lax.broadcasted_iota(jnp.int32, trace.shape, 1)
    three = jnp.where(lane < SLOT, trace, pltpu.roll(total[1], SLOT, 1))
    three = jnp.where(lane < 2 * SLOT, three, pltpu.roll(total[2], 2 * SLOT, 1))
    xz = [total[5]] + [pltpu.roll(total[5], index * SLOT, 1) for index in range(1, 3)]

    own_first, own_last = column_rows(temp, cure, 0), column_rows(temp, cure, count - GHOST)
    for position, target in enumerate(order):
        piece = jnp.where(layer == target - 1, own_last, 0.0)
        piece = jnp.where(layer == target + 1, own_first, piece)
        if target == 0:
            piece = jnp.where(layer == depths - 1, left, piece)
        if target == out.shape[0] - 1:
            piece = jnp.where(layer == 0, right, piece)
        at = count * target
        pieces = [three[at : at + height], jnp.zeros((4, LANES), jnp.float32)]
        for index in range(3):
            size = min(4, height - 4 * index)
            if size > 0:
                part = xz[index][at + 4 * index : at + 4 * index + size]
                if size < 4:
                    spare = jnp.zeros((4 - size, LANES), jnp.float32)
                    part = jnp.concatenate([part, spare], axis=0)
                pieces[1] = jnp.where(lane[:4] < index * SLOT, pieces[1], part)
        for slot in range(lanes // LANES):
            pieces.append(piece[0 : 2 * GHOST, slot * LANES : (slot + 1) * LANES])
        filled = sum(part.shape[0] for part in pieces)
        if filled < 24:
            pieces.append(jnp.zeros((24 - filled, LANES), jnp.float32))
        sent = two_parts(jnp.concatenate(pieces, axis=0))
        out[position, voxels + folded :, :] = sent.astype(jnp.bfloat16)
    copies[1].start()
    for copy in copies:
        copy.wait()


def rim_sums(chunks, count, starts, flat, steep, cells):
    parts = chunks.shape[0]
    rows_x, voxels = own_columns(count)
    folded = fold(voxels)
    tall = -(-voxels // 16) * 16
    spare = [jnp.zeros((tall - voxels, LANES), jnp.float32)] if tall > voxels else []
    tiles = []
    order = meeting_order(parts)
    for part in range(parts):
        rims = chunks[order.index(part), 0 : voxels + folded, :].astype(jnp.float32)
        second = rims[voxels:]
        second = [second[: voxels - folded], pltpu.roll(second, HALF, 1)]
        for tile in ([rims[:voxels]], second):
            tiles.append(jnp.concatenate(tile + spare, axis=0).astype(jnp.bfloat16))
    result = product(
        steep[starts[1] : starts[2], :tall], jnp.concatenate(tiles, axis=1)
    ).astype(jnp.bfloat16)
    kinds = []
    for kind in range(2):
        values = result[kind * rows_x : (kind + 1) * rows_x]
        tile = lambda index: values[:, index * LANES : (index + 1) * LANES]
        stack = [
            jnp.concatenate([tile(2 * part), tile(2 * part + 2), tile(2 * part + 3)], axis=1)
            for part in range(parts - 1)
        ]
        kinds.append(jnp.concatenate(stack, axis=0))
    both = product(kinds[0], flat[...])
    three = (both[:, :LANES], product(kinds[1], steep[starts[0] : starts[1], :]), both[:, LANES:])

    index = lax.axis_index("plane") * lax.axis_size("depth") + lax.axis_index("depth")
    total = lax.axis_size("plane") * lax.axis_size("depth") * count * COARSE
    place = lax.rem(lax.broadcasted_iota(jnp.int32, three[0].shape, 0), rows_x)
    place = place + (index * count - HALO) * COARSE - R2
    inside = jnp.where((place >= 0) & (place < total), 1.0, 0.0)
    wide = []
    for term in weighted_products(three, inside):
        term = term.astype(jnp.bfloat16)
        wide += [term[part * rows_x : (part + 1) * rows_x] for part in range(parts - 1)]
    sx = steep[starts[2] : starts[3], :rows_x]
    along = product(sx, jnp.concatenate(wide, axis=1)).astype(jnp.bfloat16)
    step = (parts - 1) * LANES
    along = [along[:, kind * step : (kind + 1) * step] for kind in range(6)]
    sums = product(jnp.concatenate(along, axis=0), cells[...])
    return [sums[kind * 16 : (kind + 1) * 16] for kind in range(6)]


def cure_kernel(
    cells, starts, chunks, temp_in, cure_in, tools, flat, steep, rim_bands, temp_hbm, cure_hbm,
    conduct_hbm, temp_out, cure_out, conduct_out, sems,
):
    count, lanes = temp_in.shape
    parts = chunks.shape[0]
    planes, depths = lax.axis_size("plane"), lax.axis_size("depth")
    plane, layer = lax.axis_index("plane"), lax.axis_index("depth")
    height = count + 2 * HALO
    own = cells - BEFORE - AFTER
    lane = lax.broadcasted_iota(jnp.int32, (16, lanes), 1)
    row = lax.broadcasted_iota(jnp.int32, (16, lanes), 0)
    at_sums = chunks.shape[1] - 48
    order = meeting_order(parts)

    near = rim_sums(chunks, count, starts, flat, steep, rim_bands)
    sums = [near[0] + near[1] + near[2], near[1], near[2], near[5]]
    blocks = []
    for part in range(parts):
        first_cell = own * part - BEFORE
        here = (lane >= first_cell) & (lane < first_cell + cells)
        values = joined(chunks[order.index(part), at_sums:, :].astype(jnp.float32))
        blocks.append(values)
        xz = values[height : height + 4]
        xz = [xz] + [pltpu.roll(xz, LANES - index * SLOT, 1) for index in range(1, 3)]
        spare = jnp.zeros((4, LANES), jnp.float32)
        xz = jnp.concatenate([*xz, spare], axis=0)
        for index in range(4):
            chunk = values[0:16] if index < 3 else xz
            if lanes > LANES:
                spare = jnp.zeros((16, lanes - LANES), jnp.float32)
                chunk = jnp.concatenate([chunk, spare], axis=1)
            shift = (first_cell - (index % 3) * SLOT) % lanes
            moved = chunk if shift == 0 else pltpu.roll(chunk, shift, 1)
            sums[index] = sums[index] + jnp.where(here, moved, 0.0)
    trace = sums[0]
    scale = (conduct_fiber - conduct_matrix) / (2.0 * trace + tensor_eps)
    conduct = [
        conduct_matrix + scale * (trace - sums[1]),
        -scale * sums[3],
        conduct_matrix + scale * (trace - sums[2]),
    ]
    for kind in range(3):
        conduct_out[kind] = conduct[kind][HALO : HALO + count]
    copies = [
        pltpu.make_async_copy(conduct_out, conduct_hbm, sems.at[0]),
        pltpu.make_async_copy(temp_out, temp_hbm, sems.at[1]),
        pltpu.make_async_copy(cure_out, cure_hbm, sems.at[2]),
    ]
    copies[0].start()

    slots = range(height + 4, height + 4 + 2 * GHOST * (lanes // LANES), 2 * GHOST)
    columns = [
        jnp.concatenate([values[at : at + 2 * GHOST] for at in slots], axis=1) for values in blocks
    ]
    before, after = columns[parts - 1], columns[0]
    for part in range(parts - 1):
        before = jnp.where(layer == part + 1, columns[part], before)
        after = jnp.where(layer == part, columns[part + 1], after)
    spare = jnp.full((16 - count - 2 * GHOST, lanes), 0.5, jnp.float32)
    temp = jnp.concatenate([before[:GHOST], temp_in[...], after[:GHOST], 8.0 * spare], axis=0)
    cure = jnp.concatenate([before[GHOST:], cure_in[...], after[GHOST:], spare], axis=0)
    gap = GHOST - HALO
    xx, xz, zz = [pltpu.roll(part, gap, 0) for part in conduct]

    first = (plane == 0) & (layer == 0)
    last = (plane == planes - 1) & (layer == depths - 1)
    for step in range(STEPS):
        top, bottom = tools[2 * step : 2 * step + 1, :], tools[2 * step + 1 : 2 * step + 2, :]
        temp = jnp.where((row < GHOST) & first, temp[GHOST : GHOST + 1], temp)
        temp = jnp.where(
            (row >= GHOST + count) & last, temp[GHOST + count - 1 : GHOST + count], temp
        )
        cooler = jnp.where(lane == 0, top, pltpu.roll(temp, 1, 1))
        later = jnp.where(lane == lanes - 1, bottom, pltpu.roll(temp, lanes - 1, 1))
        slant = later - cooler
        second_x = pltpu.roll(temp, 15, 0) - 2.0 * temp + pltpu.roll(temp, 1, 0)
        second_z = later - 2.0 * temp + cooler
        cross = 0.25 * (pltpu.roll(slant, 15, 0) - pltpu.roll(slant, 1, 0))
        spread = xx * second_x + 2.0 * xz * cross + zz * second_z
        inverse = 1.0 / reference_temp - 1.0 / temp
        left = 1.0 - cure
        rate = rate_first * jnp.exp(energy_first * inverse) + rate_second * jnp.exp(
            energy_second * inverse
        ) * jnp.sqrt(cure)
        rate = rate * (left * jnp.sqrt(left))
        temp = temp + time_step * (spread + heat_release * rate)
        cure = cure + time_step * rate
    temp_out[...] = temp[GHOST : GHOST + count]
    cure_out[...] = cure[GHOST : GHOST + count]
    for copy in copies[1:]:
        copy.start()
    for copy in copies:
        copy.wait()


def on_device(intensity, temp_start, cure_start, tool_levels, plan):
    rows, width, depth = intensity.shape
    count, lanes = temp_start.shape
    planes, depths = lax.axis_size("plane"), lax.axis_size("depth")
    columns, cells = sizes(width, depth)
    bf16 = jnp.bfloat16
    slots = rows * EDGE + 16 * (lanes // LANES)
    params = pltpu.CompilerParams(vmem_limit_bytes=24 * 1024 * 1024)
    vmem = pl.BlockSpec(memory_space=pltpu.VMEM)
    stay = pl.BlockSpec(memory_space=pltpu.HBM)

    fixed = lambda values: pltpu.with_memory_space_constraint(values, pltpu.HBM)
    bands, coarse = x_bands(width), coarse_x_bands(width)
    late = bands.shape[1] - EARLY
    middle = bands[:, :EARLY, EDGE : EDGE + width]
    x_hbm, early_starts = stacked(middle.reshape(2 * EARLY, -1), coarse[:, :EARLY])
    z_hbm, _ = stacked(*depth_bands(depth), coarse_depth_bands(depth))
    x_late, late_starts = stacked(bands[:, EARLY:].reshape(2 * late, -1), coarse[:, EARLY:])
    rims = rim_bands(rows)
    flat, _ = stacked(np.concatenate([rims[0], rims[2]], axis=1))
    steep, rim_starts = stacked(rims[1], *rim_x_bands(count))
    cell_bands, _ = stacked(rim_cells(rows, depth, depths))
    constants = (x_late, flat, steep, cell_bands)
    far, near, own, x_parts, z_parts, temp, cure = pl.pallas_call(
        pack_kernel,
        name="pack",
        out_shape=(
            pltpu.VMEM((slots, depth), bf16),
            pltpu.VMEM((slots, depth), bf16),
            pltpu.VMEM((rows // 2, width, 2 * depth), bf16),
            pltpu.VMEM(x_hbm.shape, bf16),
            pltpu.VMEM(z_hbm.shape, bf16),
            pltpu.VMEM((count, lanes), jnp.float32),
            pltpu.VMEM((count, lanes), jnp.float32),
        ),
        in_specs=[stay] * 5,
        scratch_shapes=[
            pltpu.VMEM((rows, width, depth), jnp.int32),
            pltpu.SemaphoreType.DMA((5,)),
        ],
        compiler_params=params,
    )(*[fixed(values) for values in (intensity, temp_start, cure_start, x_hbm, z_hbm)])

    def moved(values, pairs):
        index = [(p * depths + d, q * depths + e) for (p, d), (q, e) in pairs]
        return lax.ppermute(values, ("plane", "depth"), index)

    def swapped(values, first):
        pairs = [(p, p + 1) for p in range(first, planes - 1, 2)]
        pairs += [(q, p) for p, q in pairs]
        return moved(values, [((p, d), (q, d)) for p, q in pairs for d in range(depths)])

    far = swapped(far, 1)
    near = swapped(near, 0)

    high = coarse.shape[0]

    def scratch(count):
        return [
            pltpu.VMEM((rows // 2, 2 * count, 2 * depth), jnp.float32),
            pltpu.VMEM((3, rows // 2, count, 2 * depth), bf16),
            pltpu.VMEM((3, rows // 2, count, 2 * depth), jnp.float32),
            pltpu.VMEM((6, count, depth), bf16),
        ]

    def cost(count):
        return pl.CostEstimate(
            flops=2 * rows * (2 * count) * 160 * depth * 4,
            bytes_accessed=4_000_000,
            transcendentals=0,
        )

    early_sums, diagonal, x_late, flat, steep, cell_bands = pl.pallas_call(
        functools.partial(early_kernel, early_starts),
        name="early",
        out_shape=(
            pltpu.VMEM((6 * high, LANES), jnp.float32),
            pltpu.VMEM((4 * depth, 2 * depth), bf16),
            *[pltpu.VMEM(values.shape, bf16) for values in constants],
        ),
        in_specs=[vmem] * 3 + [stay] * len(constants),
        scratch_shapes=scratch(EARLY) + [pltpu.SemaphoreType.DMA((len(constants),))],
        cost_estimate=cost(EARLY),
        compiler_params=params,
    )(own, x_parts, z_parts, *[fixed(values) for values in constants])

    products_x, voxels = own_columns(count)
    chunk_shape = (depths, voxels + fold(voxels) + 48, LANES)
    chunks = pl.pallas_call(
        functools.partial(late_kernel, late_starts),
        name="late",
        out_shape=pltpu.HBM(chunk_shape, bf16),
        in_specs=[vmem] * 9,
        out_specs=stay,
        scratch_shapes=[pltpu.VMEM((rows // 2, width + 2 * EDGE, 2 * depth), bf16)]
        + scratch(late)
        + [
            pltpu.VMEM((late, LANES), jnp.float32),
            pltpu.VMEM(chunk_shape, bf16),
            pltpu.SemaphoreType.DMA((2,)),
        ],
        cost_estimate=cost(late),
        compiler_params=params,
    )(own, far, near, x_late, z_parts, diagonal, early_sums, temp, cure)

    faces = plan.reshape(2 * STEPS, 1) == jnp.arange(tool_levels.shape[0], dtype=jnp.int32)
    tools = jnp.sum(
        jnp.where(faces, tool_levels, jnp.zeros_like(tool_levels)), axis=1, keepdims=True
    )

    chunks = lax.all_to_all(
        chunks,
        "depth",
        split_axis=0,
        concat_axis=0,
        tiled=True,
        axis_index_groups=[meeting_order(depths)],
    )

    return pl.pallas_call(
        functools.partial(cure_kernel, cells, rim_starts),
        name="cure",
        out_shape=(
            pltpu.HBM((count, lanes), jnp.float32),
            pltpu.HBM((count, lanes), jnp.float32),
            pltpu.HBM((3, count, lanes), jnp.float32),
        ),
        in_specs=[vmem] * 7,
        out_specs=(stay, stay, stay),
        scratch_shapes=[
            pltpu.VMEM((count, lanes), jnp.float32),
            pltpu.VMEM((count, lanes), jnp.float32),
            pltpu.VMEM((3, count, lanes), jnp.float32),
            pltpu.SemaphoreType.DMA((3,)),
        ],
        compiler_params=params,
    )(chunks, temp, cure, tools, flat, steep, cell_bands)


def solution(mesh):
    return jax.shard_map(
        on_device,
        mesh=mesh,
        in_specs=(
            P(None, "plane", "depth"),
            P(("plane", "depth"), None),
            P(("plane", "depth"), None),
            P(),
            P(),
        ),
        out_specs=(
            P(("plane", "depth"), None),
            P(("plane", "depth"), None),
            P(None, ("plane", "depth"), None),
        ),
        check_vma=False,
    )
```

```python
import functools

import jax
import jax.numpy as jnp
import ml_dtypes
import numpy as np
from jax import lax
from jax.experimental import pallas as pl
from jax.experimental.pallas import tpu as pltpu
from jax.sharding import PartitionSpec as P

ROWS = 8
R1 = 6
R2 = 10
COARSE = 4
STEPS = 3

sigma_grad = 2.0
sigma_tensor = 3.3
conduct_matrix = 0.3
conduct_fiber = 1.5
time_step = 0.25
heat_release = 0.4
rate_first = 0.15
rate_second = 0.6
energy_first = 30.0
energy_second = 25.0
reference_temp = 4.2
tensor_eps = 1e-06

LANES = 128
HALO = 2
EDGE = HALO * COARSE + R1 + R2
EARLY = 80
GHOST = 3
RIM = 2 * R1
BEFORE = -(-(R2 - R1) // COARSE)
AFTER = BEFORE
HALF = LANES // 2
SLOT = 40
ROW_KINDS = (1, 0, 0)
X_KINDS = (0, 1, 0)
DEPTH_KINDS = (0, 0, 1)


def smooth_taps(radius, sigma):
    offsets = np.arange(-radius, radius + 1) * 1.0
    weights = np.exp(-0.5 * offsets * offsets / (sigma * sigma))
    return weights / weights.sum()


def slope_taps(radius, sigma):
    offsets = np.arange(-radius, radius + 1) * 1.0
    weights = np.exp(-0.5 * offsets * offsets / (sigma * sigma))
    return offsets * weights / np.sum(offsets * offsets * weights)


def row_weights(count, radius, sigma):
    taps = smooth_taps(radius, sigma)
    result = np.zeros(count)
    for source in range(count):
        for target in range(count):
            offset = target - source
            if abs(offset) <= radius:
                result[source] += taps[offset + radius]
    return result


def rounded(taps):
    best = None
    for factor in np.linspace(1.0, 2.0, 20001)[:-1]:
        near = (taps * factor).astype(np.float32).astype(ml_dtypes.bfloat16).astype(np.float64)
        error = np.abs(near / factor - taps).sum()
        if best is None or error < best[0]:
            best = (error, near, factor)
    return best[1], best[2]


def as_bfloat16(matrix):
    return matrix.astype(np.float32).astype(ml_dtypes.bfloat16)


def halves(matrix):
    high = as_bfloat16(matrix)
    return high, as_bfloat16(matrix - high.astype(np.float64))


def sizes(width, depth):
    columns = width // COARSE + 2 * HALO
    cells = depth // COARSE + BEFORE + AFTER
    return columns, cells


def product_rows(width):
    places = [*range(R1, width - R1), *range(R1 - EDGE, R1), *range(width - R1, width + EDGE - R1)]
    return places + [None] * (-len(places) % 16)


GRAD_TAPS = tuple(
    rounded(taps(R1, sigma_grad)) for taps in (smooth_taps, slope_taps)
)
GRAD_FACTOR = GRAD_TAPS[0][1] ** 2 * GRAD_TAPS[1][1]


def grad_taps(kind):
    return GRAD_TAPS[kind][0]


def tap(taps, offset):
    radius = (len(taps) - 1) // 2
    return float(taps[offset + radius]) if abs(offset) <= radius else 0.0


def x_bands(width):
    places = product_rows(width)
    bands = np.zeros((2, len(places), width + 2 * EDGE))
    for kind in range(2):
        for row, place in enumerate(places):
            if place is not None:
                first = place + EDGE - R1
                bands[kind, row, first : first + 2 * R1 + 1] = grad_taps(kind)
    return bands


def rim_bands(rows):
    bands = np.zeros((3, 3 * LANES, LANES))
    for part in range(3):
        row_taps, depth_taps = grad_taps(ROW_KINDS[part]), grad_taps(DEPTH_KINDS[part])
        for source in range(rows):
            for target in range(rows):
                row_tap = tap(row_taps, source - target)
                for near in range(-RIM, RIM):
                    lane = source * RIM + near % RIM
                    if near >= 0:
                        lane += rows * RIM + LANES
                    for place in range(-R1, R1):
                        value = row_tap * tap(depth_taps, near - place)
                        bands[part, lane, target * 2 * R1 + R1 + place] = value
    return bands


def rim_cells(rows, depth, blocks):
    taps = smooth_taps(R2, sigma_tensor)
    weights = product_weights(rows)
    bands = np.zeros((blocks - 1, LANES, blocks * depth // COARSE))
    for boundary in range(blocks - 1):
        middle = (boundary + 1) * depth
        for cell in range(bands.shape[2]):
            for voxel in range(cell * COARSE, (cell + 1) * COARSE):
                for place in range(-R1, R1):
                    value = tap(taps, middle + place - voxel)
                    for row in range(rows):
                        bands[boundary, row * 2 * R1 + R1 + place, cell] += weights[row] * value
    return bands.reshape(-1, bands.shape[2])


def meeting_order(blocks):
    middle = blocks // 2
    return [middle, *range(middle + 1, blocks), *range(middle - 1, -1, -1)]


def own_columns(count):
    products = (count + 2 * HALO) * COARSE + 2 * R2
    voxels = products + 2 * R1
    return -(-products // 16) * 16, -(-voxels // 8) * 8


def fold(voxels):
    return -(-voxels // 16) * 8


def rim_x_bands(count):
    products, voxels = own_columns(count)
    bands = np.zeros((2, products, -(-voxels // 16) * 16))
    valid = (count + 2 * HALO) * COARSE + 2 * R2
    for kind in range(2):
        for row in range(valid):
            bands[kind, row, row : row + 2 * R1 + 1] = grad_taps(kind)
    taps = smooth_taps(R2, sigma_tensor)
    coarse = np.zeros((16, products))
    for column in range(count + 2 * HALO):
        for voxel in range(column * COARSE, (column + 1) * COARSE):
            coarse[column, voxel : voxel + 2 * R2 + 1] += taps
    return bands.reshape(2 * products, -1), coarse


def depth_bands(depth):
    bands = np.zeros((2, depth, depth))
    for kind in range(2):
        for place in range(depth):
            for near in range(max(place - R1, 0), min(place + R1 + 1, depth)):
                bands[kind, near, place] = tap(grad_taps(kind), near - place)
    return bands


def product_weights(rows):
    return row_weights(rows, R2, sigma_tensor) / (255.0 * GRAD_FACTOR) ** 2


def coarse_depth_bands(depth):
    taps = smooth_taps(R2, sigma_tensor)
    columns, cells = sizes(0, depth)
    bands = np.zeros((depth, LANES))
    for cell in range(cells):
        for voxel in range(COARSE):
            place = (cell - BEFORE) * COARSE + voxel
            for near in range(max(place - R2, 0), min(place + R2 + 1, depth)):
                bands[near, cell] += tap(taps, near - place)
    return bands


def coarse_x_bands(width):
    taps = smooth_taps(R2, sigma_tensor)
    places = product_rows(width)
    columns, cells = sizes(width, 0)
    bands = np.zeros((-(-columns // 16) * 16, len(places)))
    for column in range(columns):
        for voxel in range(COARSE):
            middle = (column - HALO) * COARSE + voxel
            for row, place in enumerate(places):
                if place is not None:
                    bands[column, row] += tap(taps, place - middle)
    return bands


def stacked(*pieces):
    widest = max(piece.shape[1] for piece in pieces)
    padded = [np.pad(piece, ((0, 0), (0, widest - piece.shape[1]))) for piece in pieces]
    starts = np.cumsum([0] + [len(piece) for piece in pieces])
    return jnp.asarray(as_bfloat16(np.concatenate(padded))), tuple(int(start) for start in starts)


def two_parts(values):
    high = values.astype(jnp.bfloat16).astype(jnp.float32)
    return jnp.concatenate([high, (values - high).astype(jnp.bfloat16).astype(jnp.float32)], axis=0)


def joined(parts):
    half = parts.shape[0] // 2
    return parts[:half] + parts[half:]


def column_rows(temp, cure, first):
    pad = jnp.zeros((8 - 2 * GHOST, temp.shape[1]), jnp.float32)
    return jnp.concatenate(
        [temp[first : first + GHOST, :], cure[first : first + GHOST, :], pad], axis=0
    )


def is_odd():
    return lax.rem(lax.axis_index("plane"), 2) == 1


def pack_kernel(
    intensity, temp_hbm, cure_hbm, x_hbm, z_hbm, far, near, own, x_parts, z_parts, temp, cure,
    grey, sems,
):
    rows, width, depth = intensity.shape
    parts = [(0, EDGE), (width - EDGE, EDGE), (EDGE, width - 2 * EDGE)]
    copies = [
        pltpu.make_async_copy(
            intensity.at[:, pl.ds(*part), :], grey.at[:, pl.ds(*part), :], sems.at[index]
        )
        for index, part in enumerate(parts)
    ]
    copies[2:2] = [
        pltpu.make_async_copy(temp_hbm, temp, sems.at[3]),
        pltpu.make_async_copy(cure_hbm, cure, sems.at[4]),
    ]
    copies += [
        pltpu.make_async_copy(x_hbm, x_parts, sems.at[5]),
        pltpu.make_async_copy(z_hbm, z_parts, sems.at[6]),
    ]
    for copy in copies:
        copy.start()
    for copy in copies[:4]:
        copy.wait()
    odd = is_odd()
    count = temp.shape[0]
    sides = [
        two_parts(column_rows(temp, cure, first)).astype(jnp.bfloat16)
        for first in (0, count - GHOST)
    ]

    def send(left, right):
        for place, target, columns in ((0, left, sides[0]), (width - EDGE, right, sides[1])):
            for pair in range(rows // 2):
                two = [grey[2 * pair + i, place : place + EDGE, :] for i in range(2)]
                two = jnp.concatenate(two, axis=0).astype(jnp.float32)
                target[2 * EDGE * pair : 2 * EDGE * (pair + 1), :] = two.astype(jnp.bfloat16)
            for slot in range(temp.shape[1] // LANES):
                at = rows * EDGE + 16 * slot
                target[at : at + 16, :] = columns[:, slot * LANES : (slot + 1) * LANES]

    @pl.when(odd)
    def _():
        send(near, far)

    @pl.when(jnp.logical_not(odd))
    def _():
        send(far, near)

    for copy in copies[4:]:
        copy.wait()
    for row in range(rows):
        half = (row % 2) * depth
        own[row // 2, :, half : half + depth] = grey[row].astype(jnp.float32).astype(jnp.bfloat16)


def packed_rows(values, size, first):
    depth = values[0].shape[1]
    lane = lax.broadcasted_iota(jnp.int32, values[0].shape, 1)
    packed = None
    for block, value in enumerate(values):
        shift = (size * block - first) % depth
        moved = value if shift == 0 else pltpu.roll(value, shift, 1)
        packed = moved if block == 0 else jnp.where(lane >= size * block, moved, packed)
    return packed


def edges_of(ref, rows):
    two = [
        ref[2 * EDGE * pair : 2 * EDGE * (pair + 1), :].astype(jnp.float32)
        for pair in range(rows // 2)
    ]
    voxels = [two[row // 2][row % 2 * EDGE : (row % 2 + 1) * EDGE] for row in range(rows)]
    slots = range(rows * EDGE, ref.shape[0], 16)
    columns = [joined(ref[at : at + 16, :].astype(jnp.float32)) for at in slots]
    return voxels, jnp.concatenate(columns, axis=1)


def product(first, second):
    return jnp.dot(first, second, preferred_element_type=jnp.float32)


def mirrored_filter(kind, values, even):
    rows = len(values)
    use_sum = even == (kind == 0)
    sign = 1.0 if use_sum else -1.0
    half = [values[row] + sign * values[rows - 1 - row] for row in range(rows // 2)]
    results = []
    for row in range(rows // 2):
        total = None
        for source, value in enumerate(half):
            near = tap(grad_taps(kind), source - row)
            far = tap(grad_taps(kind), rows - 1 - source - row)
            weight = 0.5 * (near + sign * far)
            total = weight * value if total is None else total + weight * value
        results.append(total)
    return results


def weighted_products(three, weight):
    pairs = ((0, 0), (1, 1), (2, 2), (0, 1), (0, 2), (1, 2))
    first = [weight * value for value in three]
    return [first[a] * three[b] for a, b in pairs]


def late_mask(count, width):
    row = lax.broadcasted_iota(jnp.int32, (count, LANES), 0)
    left = width - 2 * R1 - EARLY
    place = jnp.where(row < left + EDGE, row - left + R1 - EDGE, row - left - EDGE + width - R1)
    place = place + lax.axis_index("plane") * width
    inside = (place >= 0) & (place < lax.axis_size("plane") * width)
    return jnp.where(inside | (row < left), 1.0, 0.0)


USED = (0, 1, 2, 5)
UNUSED = (3, 4)


def all_sums(products, coarse, sx):
    sums = [None] * 6
    for kinds in (USED, UNUSED):
        tiles = [tile for index in kinds for tile in products[index]]
        along = product(sx, jnp.concatenate(tiles, axis=1)).astype(jnp.bfloat16)
        step = along.shape[1] // len(kinds)
        parts = [along[:, index * step : (index + 1) * step] for index in range(len(kinds))]
        total = product(jnp.concatenate(parts, axis=0), coarse)
        high = sx.shape[0]
        for index, kind in enumerate(kinds):
            sums[kind] = total[index * high : (index + 1) * high]
    return sums


def tensor_sums(window, bands, sx, mask, diagonal, z_parts, across, filtered, grads):
    pairs, height, double = window.shape
    rows, depth = 2 * pairs, double // 2
    count = bands.shape[0] // 2
    whole = jnp.concatenate([window[pair] for pair in range(pairs)], axis=1)
    across[...] = product(bands, whole)

    for start in range(0, count, 16):
        kinds = [
            [
                across[kind * count + start : kind * count + start + 16, row * depth : (row + 1) * depth]
                for row in range(rows)
            ]
            for kind in range(2)
        ]
        for part in range(3):
            values = kinds[X_KINDS[part]]
            results = mirrored_filter(ROW_KINDS[part], values, True)
            results += mirrored_filter(ROW_KINDS[part], values, False)
            for row, result in enumerate(results):
                at = (part * pairs + row // 2) * count + start
                lanes = slice((row % 2) * depth, (row % 2 + 1) * depth)
                filtered[at : at + 16, lanes] = result.astype(jnp.bfloat16)

    at = 2 * pairs * count
    grads[:at] = product(filtered[:at, :], diagonal[0:double, :])
    grads[at:] = product(filtered[at:, :], diagonal[double : 2 * double, :])

    weights = product_weights(rows)
    layer = lax.axis_index("depth")
    first, last = layer == 0, layer == lax.axis_size("depth") - 1
    place = lax.broadcasted_iota(jnp.int32, (16, depth), 1)
    complete = ((place >= R1) | first) & ((place < depth - R1) | last)
    complete = jnp.where(complete, 1.0, 0.0)
    groups = [[] for _ in range(6)]
    for start in range(0, count, 16):
        inside = complete if mask is None else complete * mask[start : start + 16]
        totals = None
        for row in range(rows):
            lanes = slice((row % 2) * depth, (row % 2 + 1) * depth)
            three = []
            for part in range(3):
                at = (part * pairs + row // 2) * count + start
                three.append(grads[at : at + 16, lanes])
            terms = weighted_products(three, 2.0 * float(weights[row % (rows // 2)]))
            totals = terms if row == 0 else [a + b for a, b in zip(totals, terms)]
        for index in range(6):
            groups[index].append((totals[index] * inside).astype(jnp.bfloat16))
    products = [[jnp.concatenate(group, axis=0)] for group in groups]
    return all_sums(products, z_parts[double : double + depth, :], sx)


def early_kernel(*refs):
    starts, own, x_parts, z_parts, *rest = refs
    count = (len(rest) - 6) // 2
    constants, (sums, diagonal), held = rest[:count], rest[count : count + 2], rest[count + 2 : -4]
    across, filtered, grads, sems = rest[-4:]
    copies = [
        pltpu.make_async_copy(source, target, sems.at[index])
        for index, (source, target) in enumerate(zip(constants, held))
    ]
    for copy in copies:
        copy.start()
    pairs, width, double = own.shape
    depth = double // 2
    empty = jnp.zeros((depth, depth), jnp.bfloat16)
    for kind in range(2):
        for half in range(2):
            at = pl.ds(kind * double + half * depth, depth)
            band = z_parts[kind * depth : (kind + 1) * depth, :]
            diagonal[at, half * depth : (half + 1) * depth] = band
            diagonal[at, (1 - half) * depth : (2 - half) * depth] = empty
    bands = x_parts[starts[0] : starts[1], :width]
    sx = x_parts[starts[1] : starts[2], :EARLY]
    results = tensor_sums(own, bands, sx, None, diagonal, z_parts, across, filtered, grads)
    for index, kind in enumerate(USED):
        sums[index] = results[kind]
    for copy in copies:
        copy.wait()


def late_kernel(
    starts, own, far, near, x_late, z_parts, diagonal, early_sums, temp, cure, out_hbm,
    window, across, filtered, grads, out, sems,
):
    pairs, width, double = own.shape
    rows, depth = 2 * pairs, double // 2
    count, lanes = temp.shape
    odd = is_odd()
    depths, layer = lax.axis_size("depth"), lax.axis_index("depth")
    outer, outer_columns = edges_of(far, rows)
    inner, inner_columns = edges_of(near, rows)
    values = []
    for row in range(rows):
        half = (row % 2) * depth
        middle = own[row // 2, :, half : half + depth].astype(jnp.float32)
        left = jnp.where(odd, inner[row], outer[row])
        right = jnp.where(odd, outer[row], inner[row])
        whole = jnp.concatenate([left, middle, right], axis=0)
        window[row // 2, :, half : half + depth] = whole.astype(jnp.bfloat16)
        values.append(whole)
    left = jnp.where(odd, inner_columns, outer_columns)
    right = jnp.where(odd, outer_columns, inner_columns)

    products_x, voxels = own_columns(count)
    folded, stride = fold(voxels), COARSE * count
    below = packed_rows(values, RIM, depth - RIM)
    above = pltpu.roll(packed_rows(values, RIM, 0), rows * RIM, 1)
    lane = lax.broadcasted_iota(jnp.int32, below.shape, 1)
    tiles = [jnp.where(lane < rows * RIM, below, above), above, pltpu.roll(above, HALF, 1)]
    missing = stride * (depths - 1) + voxels - below.shape[0]
    if missing > 0:
        spare = jnp.zeros((-(-missing // 8) * 8, LANES), jnp.float32)
        tiles = [jnp.concatenate([tile, spare], axis=0) for tile in tiles]

    height = count + 2 * HALO
    half_lane = lax.broadcasted_iota(jnp.int32, (folded, LANES), 1) < HALF
    order = meeting_order(out.shape[0])
    for position, target in enumerate(order):
        at = stride * target
        second = jnp.where(
            half_lane,
            tiles[1][at : at + folded],
            tiles[2][at + voxels - folded : at + voxels],
        )
        rims = jnp.concatenate([tiles[0][at : at + voxels], second], axis=0)
        out[position, 0 : voxels + folded, :] = rims.astype(jnp.bfloat16)
    split = (pl.ds(0, voxels + folded), pl.ds(voxels + folded, out.shape[1] - voxels - folded))
    copies = [
        pltpu.make_async_copy(out.at[:, part, :], out_hbm.at[:, part, :], sems.at[index])
        for index, part in enumerate(split)
    ]
    copies[0].start()

    late = across.shape[0] // 2
    bands = x_late[starts[0] : starts[1], :]
    sx = x_late[starts[1] : starts[2], :late]
    results = tensor_sums(
        window, bands, sx, late_mask(late, width), diagonal, z_parts, across, filtered, grads
    )
    yy, xx, zz, xz = [early_sums[index] + results[kind] for index, kind in enumerate(USED)]
    trace = yy + xx + zz
    lane = lax.broadcasted_iota(jnp.int32, trace.shape, 1)
    three = jnp.where(lane < SLOT, trace, pltpu.roll(xx, SLOT, 1))
    three = jnp.where(lane < 2 * SLOT, three, pltpu.roll(zz, 2 * SLOT, 1))
    xz = [xz] + [pltpu.roll(xz, index * SLOT, 1) for index in range(1, 3)]

    own_first, own_last = column_rows(temp, cure, 0), column_rows(temp, cure, count - GHOST)
    for position, target in enumerate(order):
        piece = jnp.where(layer == target - 1, own_last, 0.0)
        piece = jnp.where(layer == target + 1, own_first, piece)
        if target == 0:
            piece = jnp.where(layer == depths - 1, left, piece)
        if target == out.shape[0] - 1:
            piece = jnp.where(layer == 0, right, piece)
        at = count * target
        pieces = [three[at : at + height], jnp.zeros((4, LANES), jnp.float32)]
        for index in range(3):
            size = min(4, height - 4 * index)
            if size > 0:
                part = xz[index][at + 4 * index : at + 4 * index + size]
                if size < 4:
                    spare = jnp.zeros((4 - size, LANES), jnp.float32)
                    part = jnp.concatenate([part, spare], axis=0)
                pieces[1] = jnp.where(lane[:4] < index * SLOT, pieces[1], part)
        for slot in range(lanes // LANES):
            pieces.append(piece[0 : 2 * GHOST, slot * LANES : (slot + 1) * LANES])
        filled = sum(part.shape[0] for part in pieces)
        if filled < 24:
            pieces.append(jnp.zeros((24 - filled, LANES), jnp.float32))
        sent = two_parts(jnp.concatenate(pieces, axis=0))
        out[position, voxels + folded :, :] = sent.astype(jnp.bfloat16)
    copies[1].start()
    for copy in copies:
        copy.wait()


def rim_sums(chunks, count, starts, flat, steep, cells):
    parts = chunks.shape[0]
    rows_x, voxels = own_columns(count)
    folded = fold(voxels)
    tall = -(-voxels // 16) * 16
    spare = [jnp.zeros((tall - voxels, LANES), jnp.float32)] if tall > voxels else []
    tiles = []
    order = meeting_order(parts)
    for part in range(parts):
        rims = chunks[order.index(part), 0 : voxels + folded, :].astype(jnp.float32)
        second = rims[voxels:]
        second = [second[: voxels - folded], pltpu.roll(second, HALF, 1)]
        for tile in ([rims[:voxels]], second):
            tiles.append(jnp.concatenate(tile + spare, axis=0).astype(jnp.bfloat16))
    result = product(
        steep[starts[1] : starts[2], :tall], jnp.concatenate(tiles, axis=1)
    ).astype(jnp.bfloat16)
    kinds = []
    for kind in range(2):
        values = result[kind * rows_x : (kind + 1) * rows_x]
        tile = lambda index: values[:, index * LANES : (index + 1) * LANES]
        stack = [
            jnp.concatenate([tile(2 * part), tile(2 * part + 2), tile(2 * part + 3)], axis=1)
            for part in range(parts - 1)
        ]
        kinds.append(jnp.concatenate(stack, axis=0))
    both = product(kinds[0], flat[...])
    three = (both[:, :LANES], product(kinds[1], steep[starts[0] : starts[1], :]), both[:, LANES:])

    index = lax.axis_index("plane") * lax.axis_size("depth") + lax.axis_index("depth")
    total = lax.axis_size("plane") * lax.axis_size("depth") * count * COARSE
    place = lax.rem(lax.broadcasted_iota(jnp.int32, three[0].shape, 0), rows_x)
    place = place + (index * count - HALO) * COARSE - R2
    inside = jnp.where((place >= 0) & (place < total), 1.0, 0.0)
    products = [
        [
            term[part * rows_x : (part + 1) * rows_x].astype(jnp.bfloat16)
            for part in range(parts - 1)
        ]
        for term in weighted_products(three, inside)
    ]
    return all_sums(products, cells[...], steep[starts[2] : starts[3], :rows_x])


def cure_kernel(
    cells, starts, chunks, temp_in, cure_in, tools, flat, steep, rim_bands, temp_hbm, cure_hbm,
    conduct_hbm, temp_out, cure_out, conduct_out, sems,
):
    count, lanes = temp_in.shape
    parts = chunks.shape[0]
    planes, depths = lax.axis_size("plane"), lax.axis_size("depth")
    plane, layer = lax.axis_index("plane"), lax.axis_index("depth")
    height = count + 2 * HALO
    own = cells - BEFORE - AFTER
    lane = lax.broadcasted_iota(jnp.int32, (16, lanes), 1)
    row = lax.broadcasted_iota(jnp.int32, (16, lanes), 0)
    at_sums = chunks.shape[1] - 48
    order = meeting_order(parts)

    near = rim_sums(chunks, count, starts, flat, steep, rim_bands)
    sums = [near[0] + near[1] + near[2], near[1], near[2], near[5]]
    blocks = []
    for part in range(parts):
        first_cell = own * part - BEFORE
        here = (lane >= first_cell) & (lane < first_cell + cells)
        values = joined(chunks[order.index(part), at_sums:, :].astype(jnp.float32))
        blocks.append(values)
        xz = values[height : height + 4]
        xz = [xz] + [pltpu.roll(xz, LANES - index * SLOT, 1) for index in range(1, 3)]
        spare = jnp.zeros((4, LANES), jnp.float32)
        xz = jnp.concatenate([*xz, spare], axis=0)
        for index in range(4):
            chunk = values[0:16] if index < 3 else xz
            if lanes > LANES:
                spare = jnp.zeros((16, lanes - LANES), jnp.float32)
                chunk = jnp.concatenate([chunk, spare], axis=1)
            shift = (first_cell - (index % 3) * SLOT) % lanes
            moved = chunk if shift == 0 else pltpu.roll(chunk, shift, 1)
            sums[index] = sums[index] + jnp.where(here, moved, 0.0)
    trace = sums[0]
    scale = (conduct_fiber - conduct_matrix) / (2.0 * trace + tensor_eps)
    conduct = [
        conduct_matrix + scale * (trace - sums[1]),
        -scale * sums[3],
        conduct_matrix + scale * (trace - sums[2]),
    ]
    for kind in range(3):
        conduct_out[kind] = conduct[kind][HALO : HALO + count]
    copies = [
        pltpu.make_async_copy(conduct_out, conduct_hbm, sems.at[0]),
        pltpu.make_async_copy(temp_out, temp_hbm, sems.at[1]),
        pltpu.make_async_copy(cure_out, cure_hbm, sems.at[2]),
    ]
    copies[0].start()

    slots = range(height + 4, height + 4 + 2 * GHOST * (lanes // LANES), 2 * GHOST)
    columns = [
        jnp.concatenate([values[at : at + 2 * GHOST] for at in slots], axis=1) for values in blocks
    ]
    before, after = columns[parts - 1], columns[0]
    for part in range(parts - 1):
        before = jnp.where(layer == part + 1, columns[part], before)
        after = jnp.where(layer == part, columns[part + 1], after)
    spare = jnp.full((16 - count - 2 * GHOST, lanes), 0.5, jnp.float32)
    temp = jnp.concatenate([before[:GHOST], temp_in[...], after[:GHOST], 8.0 * spare], axis=0)
    cure = jnp.concatenate([before[GHOST:], cure_in[...], after[GHOST:], spare], axis=0)
    gap = GHOST - HALO
    xx, xz, zz = [pltpu.roll(part, gap, 0) for part in conduct]

    first = (plane == 0) & (layer == 0)
    last = (plane == planes - 1) & (layer == depths - 1)
    for step in range(STEPS):
        top, bottom = tools[2 * step : 2 * step + 1, :], tools[2 * step + 1 : 2 * step + 2, :]
        temp = jnp.where((row < GHOST) & first, temp[GHOST : GHOST + 1], temp)
        temp = jnp.where(
            (row >= GHOST + count) & last, temp[GHOST + count - 1 : GHOST + count], temp
        )
        cooler = jnp.where(lane == 0, top, pltpu.roll(temp, 1, 1))
        later = jnp.where(lane == lanes - 1, bottom, pltpu.roll(temp, lanes - 1, 1))
        slant = later - cooler
        second_x = pltpu.roll(temp, 15, 0) - 2.0 * temp + pltpu.roll(temp, 1, 0)
        second_z = later - 2.0 * temp + cooler
        cross = 0.25 * (pltpu.roll(slant, 15, 0) - pltpu.roll(slant, 1, 0))
        spread = xx * second_x + 2.0 * xz * cross + zz * second_z
        inverse = 1.0 / reference_temp - 1.0 / temp
        left = 1.0 - cure
        rate = rate_first * jnp.exp(energy_first * inverse) + rate_second * jnp.exp(
            energy_second * inverse
        ) * jnp.sqrt(cure)
        rate = rate * (left * jnp.sqrt(left))
        temp = temp + time_step * (spread + heat_release * rate)
        cure = cure + time_step * rate
    temp_out[...] = temp[GHOST : GHOST + count]
    cure_out[...] = cure[GHOST : GHOST + count]
    for copy in copies[1:]:
        copy.start()
    for copy in copies:
        copy.wait()


def on_device(intensity, temp_start, cure_start, tool_levels, plan):
    rows, width, depth = intensity.shape
    count, lanes = temp_start.shape
    planes, depths = lax.axis_size("plane"), lax.axis_size("depth")
    columns, cells = sizes(width, depth)
    bf16 = jnp.bfloat16
    slots = rows * EDGE + 16 * (lanes // LANES)
    params = pltpu.CompilerParams(vmem_limit_bytes=24 * 1024 * 1024)
    vmem = pl.BlockSpec(memory_space=pltpu.VMEM)
    stay = pl.BlockSpec(memory_space=pltpu.HBM)

    fixed = lambda values: pltpu.with_memory_space_constraint(values, pltpu.HBM)
    bands, coarse = x_bands(width), coarse_x_bands(width)
    late = bands.shape[1] - EARLY
    middle = bands[:, :EARLY, EDGE : EDGE + width]
    x_hbm, early_starts = stacked(middle.reshape(2 * EARLY, -1), coarse[:, :EARLY])
    z_hbm, _ = stacked(*depth_bands(depth), coarse_depth_bands(depth))
    x_late, late_starts = stacked(bands[:, EARLY:].reshape(2 * late, -1), coarse[:, EARLY:])
    rims = rim_bands(rows)
    flat, _ = stacked(np.concatenate([rims[0], rims[2]], axis=1))
    steep, rim_starts = stacked(rims[1], *rim_x_bands(count))
    cell_bands, _ = stacked(rim_cells(rows, depth, depths))
    constants = (x_late, flat, steep, cell_bands)
    far, near, own, x_parts, z_parts, temp, cure = pl.pallas_call(
        pack_kernel,
        name="pack",
        out_shape=(
            pltpu.VMEM((slots, depth), bf16),
            pltpu.VMEM((slots, depth), bf16),
            pltpu.VMEM((rows // 2, width, 2 * depth), bf16),
            pltpu.VMEM(x_hbm.shape, bf16),
            pltpu.VMEM(z_hbm.shape, bf16),
            pltpu.VMEM((count, lanes), jnp.float32),
            pltpu.VMEM((count, lanes), jnp.float32),
        ),
        in_specs=[stay] * 5,
        scratch_shapes=[
            pltpu.VMEM((rows, width, depth), jnp.int32),
            pltpu.SemaphoreType.DMA((7,)),
        ],
        compiler_params=params,
    )(*[fixed(values) for values in (intensity, temp_start, cure_start, x_hbm, z_hbm)])

    def moved(values, pairs):
        index = [(p * depths + d, q * depths + e) for (p, d), (q, e) in pairs]
        return lax.ppermute(values, ("plane", "depth"), index)

    def swapped(values, first):
        pairs = [(p, p + 1) for p in range(first, planes - 1, 2)]
        pairs += [(q, p) for p, q in pairs]
        return moved(values, [((p, d), (q, d)) for p, q in pairs for d in range(depths)])

    far = swapped(far, 1)
    near = swapped(near, 0)

    high = coarse.shape[0]

    def scratch(count):
        return [
            pltpu.VMEM((2 * count, rows * depth), jnp.float32),
            pltpu.VMEM((3 * rows // 2 * count, 2 * depth), bf16),
            pltpu.VMEM((3 * rows // 2 * count, 2 * depth), jnp.float32),
        ]

    def cost(count):
        return pl.CostEstimate(
            flops=2 * rows * (2 * count) * 160 * depth * 4,
            bytes_accessed=4_000_000,
            transcendentals=0,
        )

    early_sums, diagonal, x_late, flat, steep, cell_bands = pl.pallas_call(
        functools.partial(early_kernel, early_starts),
        name="early",
        out_shape=(
            pltpu.VMEM((len(USED), high, LANES), jnp.float32),
            pltpu.VMEM((4 * depth, 2 * depth), bf16),
            *[pltpu.VMEM(values.shape, bf16) for values in constants],
        ),
        in_specs=[vmem] * 3 + [stay] * len(constants),
        scratch_shapes=scratch(EARLY) + [pltpu.SemaphoreType.DMA((len(constants),))],
        cost_estimate=cost(EARLY),
        compiler_params=params,
    )(own, x_parts, z_parts, *[fixed(values) for values in constants])

    products_x, voxels = own_columns(count)
    chunk_shape = (depths, voxels + fold(voxels) + 48, LANES)
    chunks = pl.pallas_call(
        functools.partial(late_kernel, late_starts),
        name="late",
        out_shape=pltpu.HBM(chunk_shape, bf16),
        in_specs=[vmem] * 9,
        out_specs=stay,
        scratch_shapes=[pltpu.VMEM((rows // 2, width + 2 * EDGE, 2 * depth), bf16)]
        + scratch(late)
        + [
            pltpu.VMEM(chunk_shape, bf16),
            pltpu.SemaphoreType.DMA((2,)),
        ],
        cost_estimate=cost(late),
        compiler_params=params,
    )(own, far, near, x_late, z_parts, diagonal, early_sums, temp, cure)

    faces = plan.reshape(2 * STEPS, 1) == jnp.arange(tool_levels.shape[0], dtype=jnp.int32)
    tools = jnp.sum(
        jnp.where(faces, tool_levels, jnp.zeros_like(tool_levels)), axis=1, keepdims=True
    )

    chunks = lax.all_to_all(
        chunks,
        "depth",
        split_axis=0,
        concat_axis=0,
        tiled=True,
        axis_index_groups=[meeting_order(depths)],
    )

    return pl.pallas_call(
        functools.partial(cure_kernel, cells, rim_starts),
        name="cure",
        out_shape=(
            pltpu.HBM((count, lanes), jnp.float32),
            pltpu.HBM((count, lanes), jnp.float32),
            pltpu.HBM((3, count, lanes), jnp.float32),
        ),
        in_specs=[vmem] * 7,
        out_specs=(stay, stay, stay),
        scratch_shapes=[
            pltpu.VMEM((count, lanes), jnp.float32),
            pltpu.VMEM((count, lanes), jnp.float32),
            pltpu.VMEM((3, count, lanes), jnp.float32),
            pltpu.SemaphoreType.DMA((3,)),
        ],
        compiler_params=params,
    )(chunks, temp, cure, tools, flat, steep, cell_bands)


def solution(mesh):
    return jax.shard_map(
        on_device,
        mesh=mesh,
        in_specs=(
            P(None, "plane", "depth"),
            P(("plane", "depth"), None),
            P(("plane", "depth"), None),
            P(),
            P(),
        ),
        out_specs=(
            P(("plane", "depth"), None),
            P(("plane", "depth"), None),
            P(None, ("plane", "depth"), None),
        ),
        check_vma=False,
    )
```

```python
import functools

import jax
import jax.numpy as jnp
import ml_dtypes
import numpy as np
from jax import lax
from jax.experimental import pallas as pl
from jax.experimental.pallas import tpu as pltpu
from jax.sharding import PartitionSpec as P

ROWS = 8
R1 = 6
R2 = 10
COARSE = 4
STEPS = 3

sigma_grad = 2.0
sigma_tensor = 3.3
conduct_matrix = 0.3
conduct_fiber = 1.5
time_step = 0.25
heat_release = 0.4
rate_first = 0.15
rate_second = 0.6
energy_first = 30.0
energy_second = 25.0
reference_temp = 4.2
tensor_eps = 1e-06

LANES = 128
HALO = 2
EDGE = HALO * COARSE + R1 + R2
EARLY = 96
GHOST = 3
COLUMN_ROWS = 2 * GHOST - 1
RIM = 2 * R1
BEFORE = -(-(R2 - R1) // COARSE)
AFTER = BEFORE
HALF = LANES // 2
ROW_KINDS = (1, 0, 0)
X_KINDS = (0, 1, 0)
DEPTH_KINDS = (0, 0, 1)


def smooth_taps(radius, sigma):
    offsets = np.arange(-radius, radius + 1) * 1.0
    weights = np.exp(-0.5 * offsets * offsets / (sigma * sigma))
    return weights / weights.sum()


def slope_taps(radius, sigma):
    offsets = np.arange(-radius, radius + 1) * 1.0
    weights = np.exp(-0.5 * offsets * offsets / (sigma * sigma))
    return offsets * weights / np.sum(offsets * offsets * weights)


def row_weights(count, radius, sigma):
    taps = smooth_taps(radius, sigma)
    result = np.zeros(count)
    for source in range(count):
        for target in range(count):
            offset = target - source
            if abs(offset) <= radius:
                result[source] += taps[offset + radius]
    return result


def rounded(taps):
    best = None
    for factor in np.linspace(1.0, 2.0, 20001)[:-1]:
        near = (taps * factor).astype(np.float32).astype(ml_dtypes.bfloat16).astype(np.float64)
        error = np.abs(near / factor - taps).sum()
        if best is None or error < best[0]:
            best = (error, near, factor)
    return best[1], best[2]


def as_bfloat16(matrix):
    return matrix.astype(np.float32).astype(ml_dtypes.bfloat16)


def halves(matrix):
    high = as_bfloat16(matrix)
    return high, as_bfloat16(matrix - high.astype(np.float64))


def sizes(width, depth):
    columns = width // COARSE + 2 * HALO
    cells = depth // COARSE + BEFORE + AFTER
    return columns, cells


def product_rows(width):
    places = [*range(R1, width - R1)]
    places += [None] * max(EARLY - len(places), 0)
    places += [*range(R1 - EDGE, R1), *range(width - R1, width + EDGE - R1)]
    return places + [None] * (-len(places) % 16)


GRAD_TAPS = tuple(
    rounded(taps(R1, sigma_grad)) for taps in (smooth_taps, slope_taps)
)
GRAD_FACTOR = GRAD_TAPS[0][1] ** 2 * GRAD_TAPS[1][1]


def grad_taps(kind):
    return GRAD_TAPS[kind][0]


def tap(taps, offset):
    radius = (len(taps) - 1) // 2
    return float(taps[offset + radius]) if abs(offset) <= radius else 0.0


def x_bands(width):
    places = product_rows(width)
    bands = np.zeros((2, len(places), width + 2 * EDGE))
    for kind in range(2):
        for row, place in enumerate(places):
            if place is not None:
                first = place + EDGE - R1
                bands[kind, row, first : first + 2 * R1 + 1] = grad_taps(kind)
    return bands


def rim_bands(rows):
    bands = np.zeros((3, 3 * LANES, LANES))
    for part in range(3):
        row_taps, depth_taps = grad_taps(ROW_KINDS[part]), grad_taps(DEPTH_KINDS[part])
        for source in range(rows):
            for target in range(rows):
                row_tap = tap(row_taps, source - target)
                for near in range(-RIM, RIM):
                    lane = source * RIM + near % RIM
                    if near >= 0:
                        lane += rows * RIM + LANES
                    for place in range(-R1, R1):
                        value = row_tap * tap(depth_taps, near - place)
                        bands[part, lane, target * 2 * R1 + R1 + place] = value
    return bands


def rim_cells(rows, depth, blocks):
    taps = smooth_taps(R2, sigma_tensor)
    weights = product_weights(rows)
    bands = np.zeros((blocks - 1, LANES, blocks * depth // COARSE))
    for boundary in range(blocks - 1):
        middle = (boundary + 1) * depth
        for cell in range(bands.shape[2]):
            for voxel in range(cell * COARSE, (cell + 1) * COARSE):
                for place in range(-R1, R1):
                    value = tap(taps, middle + place - voxel)
                    for row in range(rows):
                        bands[boundary, row * 2 * R1 + R1 + place, cell] += weights[row] * value
    return bands.reshape(-1, bands.shape[2])


def meeting_order(blocks):
    middle = blocks // 2
    return [middle, *range(middle + 1, blocks), *range(middle - 1, -1, -1)]


def own_columns(count):
    products = (count + 2 * HALO) * COARSE + 2 * R2
    voxels = products + 2 * R1
    return -(-products // 16) * 16, -(-voxels // 8) * 8


def fold(voxels):
    return -(-voxels // 16) * 8


def rim_x_bands(count):
    products, voxels = own_columns(count)
    bands = np.zeros((2, products, -(-voxels // 16) * 16))
    valid = (count + 2 * HALO) * COARSE + 2 * R2
    for kind in range(2):
        for row in range(valid):
            bands[kind, row, row : row + 2 * R1 + 1] = grad_taps(kind)
    taps = smooth_taps(R2, sigma_tensor)
    coarse = np.zeros((16, products))
    for column in range(count + 2 * HALO):
        for voxel in range(column * COARSE, (column + 1) * COARSE):
            coarse[column, voxel : voxel + 2 * R2 + 1] += taps
    return bands.reshape(2 * products, -1), coarse


def depth_bands(depth):
    bands = np.zeros((2, depth, depth))
    for kind in range(2):
        for place in range(depth):
            for near in range(max(place - R1, 0), min(place + R1 + 1, depth)):
                bands[kind, near, place] = tap(grad_taps(kind), near - place)
    return bands


def product_weights(rows):
    return row_weights(rows, R2, sigma_tensor) / (255.0 * GRAD_FACTOR) ** 2


def coarse_depth_bands(depth):
    taps = smooth_taps(R2, sigma_tensor)
    columns, cells = sizes(0, depth)
    bands = np.zeros((depth, LANES))
    for cell in range(cells):
        for voxel in range(COARSE):
            place = (cell - BEFORE) * COARSE + voxel
            for near in range(max(place - R2, 0), min(place + R2 + 1, depth)):
                bands[near, cell] += tap(taps, near - place)
    return bands


def coarse_x_bands(width):
    taps = smooth_taps(R2, sigma_tensor)
    places = product_rows(width)
    columns, cells = sizes(width, 0)
    bands = np.zeros((-(-columns // 16) * 16, len(places)))
    for column in range(columns):
        for voxel in range(COARSE):
            middle = (column - HALO) * COARSE + voxel
            for row, place in enumerate(places):
                if place is not None:
                    bands[column, row] += tap(taps, place - middle)
    return bands


def stacked(*pieces):
    widest = max(piece.shape[1] for piece in pieces)
    padded = [np.pad(piece, ((0, 0), (0, widest - piece.shape[1]))) for piece in pieces]
    starts = np.cumsum([0] + [len(piece) for piece in pieces])
    return jnp.asarray(as_bfloat16(np.concatenate(padded))), tuple(int(start) for start in starts)


def two_parts(values):
    high = values.astype(jnp.bfloat16).astype(jnp.float32)
    return jnp.concatenate([high, (values - high).astype(jnp.bfloat16).astype(jnp.float32)], axis=0)


def joined(parts):
    half = parts.shape[0] // 2
    return parts[:half] + parts[half:]


def column_rows(temp, cure, at_end):
    count = temp.shape[0]
    first, second = (count - GHOST, count - GHOST + 1) if at_end else (0, 0)
    pad = jnp.zeros((8 - COLUMN_ROWS, temp.shape[1]), jnp.float32)
    return jnp.concatenate(
        [temp[first : first + GHOST, :], cure[second : second + GHOST - 1, :], pad], axis=0
    )


def chunk_rows(count, lanes):
    products, voxels = own_columns(count)
    held = count + 2 * HALO + 1 + COLUMN_ROWS * (lanes // LANES)
    return voxels + fold(voxels), -(-held // 8) * 8


def is_odd():
    return lax.rem(lax.axis_index("plane"), 2) == 1


def pack_kernel(
    intensity, temp_hbm, cure_hbm, x_hbm, z_hbm, far, near, own, x_parts, z_parts, temp, cure,
    grey, sems,
):
    rows, width, depth = intensity.shape
    copies = [
        pltpu.make_async_copy(intensity, grey, sems.at[0]),
        pltpu.make_async_copy(temp_hbm, temp, sems.at[1]),
        pltpu.make_async_copy(cure_hbm, cure, sems.at[2]),
        pltpu.make_async_copy(x_hbm, x_parts, sems.at[3]),
        pltpu.make_async_copy(z_hbm, z_parts, sems.at[4]),
    ]
    for copy in copies:
        copy.start()
    for copy in copies[:3]:
        copy.wait()
    odd = is_odd()
    sides = [
        two_parts(column_rows(temp, cure, at_end)).astype(jnp.bfloat16)
        for at_end in (False, True)
    ]

    def send(left, right):
        for place, target, columns in ((0, left, sides[0]), (width - EDGE, right, sides[1])):
            for pair in range(rows // 2):
                two = [grey[2 * pair + i, place : place + EDGE, :] for i in range(2)]
                two = jnp.concatenate(two, axis=0).astype(jnp.float32)
                target[2 * EDGE * pair : 2 * EDGE * (pair + 1), :] = two.astype(jnp.bfloat16)
            for slot in range(temp.shape[1] // LANES):
                at = rows * EDGE + 16 * slot
                target[at : at + 16, :] = columns[:, slot * LANES : (slot + 1) * LANES]

    @pl.when(odd)
    def _():
        send(near, far)

    @pl.when(jnp.logical_not(odd))
    def _():
        send(far, near)

    for row in range(rows):
        half = (row % 2) * depth
        own[row // 2, :, half : half + depth] = grey[row].astype(jnp.float32).astype(jnp.bfloat16)
    for copy in copies[3:]:
        copy.wait()


def packed_rows(values, size, first):
    depth = values[0].shape[1]
    lane = lax.broadcasted_iota(jnp.int32, values[0].shape, 1)
    packed = None
    for block, value in enumerate(values):
        shift = (size * block - first) % depth
        moved = value if shift == 0 else pltpu.roll(value, shift, 1)
        packed = moved if block == 0 else jnp.where(lane >= size * block, moved, packed)
    return packed


def edges_of(ref, rows):
    two = [
        ref[2 * EDGE * pair : 2 * EDGE * (pair + 1), :].astype(jnp.float32)
        for pair in range(rows // 2)
    ]
    voxels = [two[row // 2][row % 2 * EDGE : (row % 2 + 1) * EDGE] for row in range(rows)]
    slots = range(rows * EDGE, ref.shape[0], 16)
    columns = [joined(ref[at : at + 16, :].astype(jnp.float32)) for at in slots]
    return voxels, jnp.concatenate(columns, axis=1)


def product(first, second):
    return jnp.dot(first, second, preferred_element_type=jnp.float32)


def mirrored_filter(kind, values, even):
    rows = len(values)
    use_sum = even == (kind == 0)
    sign = 1.0 if use_sum else -1.0
    half = [values[row] + sign * values[rows - 1 - row] for row in range(rows // 2)]
    results = []
    for row in range(rows // 2):
        total = None
        for source, value in enumerate(half):
            near = tap(grad_taps(kind), source - row)
            far = tap(grad_taps(kind), rows - 1 - source - row)
            weight = 0.5 * (near + sign * far)
            total = weight * value if total is None else total + weight * value
        results.append(total)
    return results


def weighted_products(three, weight):
    pairs = ((0, 0), (1, 1), (2, 2), (0, 1), (0, 2), (1, 2))
    first = [weight * value for value in three]
    return [first[a] * three[b] for a, b in pairs]


def late_mask(count, width):
    row = lax.broadcasted_iota(jnp.int32, (count, LANES), 0)
    left = max(width - 2 * R1 - EARLY, 0)
    place = jnp.where(row < left + EDGE, row - left + R1 - EDGE, row - left - EDGE + width - R1)
    place = place + lax.axis_index("plane") * width
    inside = (place >= 0) & (place < lax.axis_size("plane") * width)
    return jnp.where(inside | (row < left), 1.0, 0.0)


USED = (0, 1, 2, 5)
UNUSED = (3, 4)


def all_sums(products, coarse, sx):
    sums = [None] * 6
    for kinds in (USED, UNUSED):
        tiles = [tile for index in kinds for tile in products[index]]
        along = product(sx, jnp.concatenate(tiles, axis=1)).astype(jnp.bfloat16)
        step = along.shape[1] // len(kinds)
        parts = [along[:, index * step : (index + 1) * step] for index in range(len(kinds))]
        total = product(jnp.concatenate(parts, axis=0), coarse)
        high = sx.shape[0]
        for index, kind in enumerate(kinds):
            sums[kind] = total[index * high : (index + 1) * high]
    return sums


def tensor_sums(window, bands, sx, mask, diagonal, z_parts, across, filtered, grads):
    pairs, height, double = window.shape
    rows, depth = 2 * pairs, double // 2
    count = bands.shape[0] // 2
    whole = jnp.concatenate([window[pair] for pair in range(pairs)], axis=1)
    across[...] = product(bands, whole)

    for start in range(0, count, 16):
        kinds = [
            [
                across[kind * count + start : kind * count + start + 16, row * depth : (row + 1) * depth]
                for row in range(rows)
            ]
            for kind in range(2)
        ]
        for part in range(3):
            values = kinds[X_KINDS[part]]
            results = mirrored_filter(ROW_KINDS[part], values, True)
            results += mirrored_filter(ROW_KINDS[part], values, False)
            for row, result in enumerate(results):
                at = (part * pairs + row // 2) * count + start
                lanes = slice((row % 2) * depth, (row % 2 + 1) * depth)
                filtered[at : at + 16, lanes] = result.astype(jnp.bfloat16)

    at = 2 * pairs * count
    grads[:at] = product(filtered[:at, :], diagonal[0:double, :])
    grads[at:] = product(filtered[at:, :], diagonal[double : 2 * double, :])

    weights = product_weights(rows)
    layer = lax.axis_index("depth")
    first, last = layer == 0, layer == lax.axis_size("depth") - 1
    place = lax.broadcasted_iota(jnp.int32, (16, depth), 1)
    complete = ((place >= R1) | first) & ((place < depth - R1) | last)
    complete = jnp.where(complete, 1.0, 0.0)
    groups = [[] for _ in range(6)]
    for start in range(0, count, 16):
        inside = complete if mask is None else complete * mask[start : start + 16]
        totals = None
        for row in range(rows):
            lanes = slice((row % 2) * depth, (row % 2 + 1) * depth)
            three = []
            for part in range(3):
                at = (part * pairs + row // 2) * count + start
                three.append(grads[at : at + 16, lanes])
            terms = weighted_products(three, 2.0 * float(weights[row % (rows // 2)]))
            totals = terms if row == 0 else [a + b for a, b in zip(totals, terms)]
        for index in range(6):
            groups[index].append((totals[index] * inside).astype(jnp.bfloat16))
    products = [[jnp.concatenate(group, axis=0)] for group in groups]
    return all_sums(products, z_parts[double : double + depth, :], sx)


def early_kernel(*refs):
    starts, own, x_parts, z_parts, *rest = refs
    count = (len(rest) - 6) // 2
    constants, (sums, diagonal), held = rest[:count], rest[count : count + 2], rest[count + 2 : -4]
    across, filtered, grads, sems = rest[-4:]
    copies = [
        pltpu.make_async_copy(source, target, sems.at[index])
        for index, (source, target) in enumerate(zip(constants, held))
    ]
    for copy in copies:
        copy.start()
    pairs, width, double = own.shape
    depth = double // 2
    empty = jnp.zeros((depth, depth), jnp.bfloat16)
    for kind in range(2):
        for half in range(2):
            at = pl.ds(kind * double + half * depth, depth)
            band = z_parts[kind * depth : (kind + 1) * depth, :]
            diagonal[at, half * depth : (half + 1) * depth] = band
            diagonal[at, (1 - half) * depth : (2 - half) * depth] = empty
    bands = x_parts[starts[0] : starts[1], :width]
    sx = x_parts[starts[1] : starts[2], :EARLY]
    results = tensor_sums(own, bands, sx, None, diagonal, z_parts, across, filtered, grads)
    for index, kind in enumerate(USED):
        sums[index] = results[kind]
    for copy in copies:
        copy.wait()


def late_kernel(
    starts, own, far, near, x_late, z_parts, diagonal, early_sums, temp, cure, out_hbm,
    window, across, filtered, grads, out, sems,
):
    pairs, width, double = own.shape
    rows, depth = 2 * pairs, double // 2
    count, lanes = temp.shape
    odd = is_odd()
    depths, layer = lax.axis_size("depth"), lax.axis_index("depth")
    outer, outer_columns = edges_of(far, rows)
    inner, inner_columns = edges_of(near, rows)
    values = []
    for row in range(rows):
        half = (row % 2) * depth
        middle = own[row // 2, :, half : half + depth].astype(jnp.float32)
        left = jnp.where(odd, inner[row], outer[row])
        right = jnp.where(odd, outer[row], inner[row])
        whole = jnp.concatenate([left, middle, right], axis=0)
        window[row // 2, :, half : half + depth] = whole.astype(jnp.bfloat16)
        values.append(whole)
    left = jnp.where(odd, inner_columns, outer_columns)
    right = jnp.where(odd, outer_columns, inner_columns)

    products_x, voxels = own_columns(count)
    folded, stride = fold(voxels), COARSE * count
    below = packed_rows(values, RIM, depth - RIM)
    above = pltpu.roll(packed_rows(values, RIM, 0), rows * RIM, 1)
    lane = lax.broadcasted_iota(jnp.int32, below.shape, 1)
    tiles = [jnp.where(lane < rows * RIM, below, above), above, pltpu.roll(above, HALF, 1)]
    missing = stride * (depths - 1) + voxels - below.shape[0]
    if missing > 0:
        spare = jnp.zeros((-(-missing // 8) * 8, LANES), jnp.float32)
        tiles = [jnp.concatenate([tile, spare], axis=0) for tile in tiles]

    height = count + 2 * HALO
    half_lane = lax.broadcasted_iota(jnp.int32, (folded, LANES), 1) < HALF
    order = meeting_order(out.shape[0])
    for position, target in enumerate(order):
        at = stride * target
        second = jnp.where(
            half_lane,
            tiles[1][at : at + folded],
            tiles[2][at + voxels - folded : at + voxels],
        )
        rims = jnp.concatenate([tiles[0][at : at + voxels], second], axis=0)
        out[position, 0 : voxels + folded, :] = rims.astype(jnp.bfloat16)
    split = (pl.ds(0, voxels + folded), pl.ds(voxels + folded, out.shape[1] - voxels - folded))
    copies = [
        pltpu.make_async_copy(out.at[:, part, :], out_hbm.at[:, part, :], sems.at[index])
        for index, part in enumerate(split)
    ]
    copies[0].start()

    late = across.shape[0] // 2
    bands = x_late[starts[0] : starts[1], :]
    sx = x_late[starts[1] : starts[2], :late]
    results = tensor_sums(
        window, bands, sx, late_mask(late, width), diagonal, z_parts, across, filtered, grads
    )
    yy, xx, zz, xz = [early_sums[index] + results[kind] for index, kind in enumerate(USED)]
    trace = yy + xx + zz
    lane = lax.broadcasted_iota(jnp.int32, trace.shape, 1)
    columns, cells = sizes(width, depth)
    tail = 4 * cells - LANES
    joint = pltpu.roll(xz, 3 * cells, 1)
    rest = jnp.where(lane < tail, joint, 0.0)
    rest = pltpu.roll(rest, 0, 1, stride=tail, stride_axis=0)
    for index, part in ((2, zz), (1, xx), (0, trace)):
        moved = part if index == 0 else pltpu.roll(part, index * cells, 1)
        joint = jnp.where(lane < (index + 1) * cells, moved, joint)

    own_first, own_last = column_rows(temp, cure, False), column_rows(temp, cure, True)
    half = chunk_rows(count, lanes)[1]
    for position, target in enumerate(order):
        piece = jnp.where(layer == target - 1, own_last, 0.0)
        piece = jnp.where(layer == target + 1, own_first, piece)
        if target == 0:
            piece = jnp.where(layer == depths - 1, left, piece)
        if target == out.shape[0] - 1:
            piece = jnp.where(layer == 0, right, piece)
        mine = slice(count * target, count * target + height)
        pieces = [joint[mine], jnp.sum(rest[mine], axis=0, keepdims=True)]
        for slot in range(lanes // LANES):
            pieces.append(piece[0:COLUMN_ROWS, slot * LANES : (slot + 1) * LANES])
        filled = sum(part.shape[0] for part in pieces)
        if filled < half:
            pieces.append(jnp.zeros((half - filled, LANES), jnp.float32))
        sent = two_parts(jnp.concatenate(pieces, axis=0))
        out[position, voxels + folded :, :] = sent.astype(jnp.bfloat16)
    copies[1].start()
    for copy in copies:
        copy.wait()


def rim_sums(chunks, count, starts, flat, steep, cells):
    parts = chunks.shape[0]
    rows_x, voxels = own_columns(count)
    folded = fold(voxels)
    tall = -(-voxels // 16) * 16
    spare = [jnp.zeros((tall - voxels, LANES), jnp.float32)] if tall > voxels else []
    tiles = []
    order = meeting_order(parts)
    for part in range(parts):
        rims = chunks[order.index(part), 0 : voxels + folded, :].astype(jnp.float32)
        second = rims[voxels:]
        second = [second[: voxels - folded], pltpu.roll(second, HALF, 1)]
        for tile in ([rims[:voxels]], second):
            tiles.append(jnp.concatenate(tile + spare, axis=0).astype(jnp.bfloat16))
    result = product(
        steep[starts[1] : starts[2], :tall], jnp.concatenate(tiles, axis=1)
    ).astype(jnp.bfloat16)
    kinds = []
    for kind in range(2):
        values = result[kind * rows_x : (kind + 1) * rows_x]
        tile = lambda index: values[:, index * LANES : (index + 1) * LANES]
        stack = [
            jnp.concatenate([tile(2 * part), tile(2 * part + 2), tile(2 * part + 3)], axis=1)
            for part in range(parts - 1)
        ]
        kinds.append(jnp.concatenate(stack, axis=0))
    both = product(kinds[0], flat[...])
    three = (both[:, :LANES], product(kinds[1], steep[starts[0] : starts[1], :]), both[:, LANES:])

    index = lax.axis_index("plane") * lax.axis_size("depth") + lax.axis_index("depth")
    total = lax.axis_size("plane") * lax.axis_size("depth") * count * COARSE
    place = lax.rem(lax.broadcasted_iota(jnp.int32, three[0].shape, 0), rows_x)
    place = place + (index * count - HALO) * COARSE - R2
    inside = jnp.where((place >= 0) & (place < total), 1.0, 0.0)
    products = [
        [
            term[part * rows_x : (part + 1) * rows_x].astype(jnp.bfloat16)
            for part in range(parts - 1)
        ]
        for term in weighted_products(three, inside)
    ]
    return all_sums(products, cells[...], steep[starts[2] : starts[3], :rows_x])


def cure_kernel(
    cells, starts, chunks, temp_in, cure_in, tools, flat, steep, rim_bands, temp_hbm, cure_hbm,
    conduct_hbm, temp_out, cure_out, conduct_out, sems,
):
    count, lanes = temp_in.shape
    parts = chunks.shape[0]
    planes, depths = lax.axis_size("plane"), lax.axis_size("depth")
    plane, layer = lax.axis_index("plane"), lax.axis_index("depth")
    height = count + 2 * HALO
    own = cells - BEFORE - AFTER
    lane = lax.broadcasted_iota(jnp.int32, (16, lanes), 1)
    row = lax.broadcasted_iota(jnp.int32, (16, lanes), 0)
    at_sums, half = chunk_rows(count, lanes)
    tail = 4 * cells - LANES
    narrow_lane = lax.broadcasted_iota(jnp.int32, (16, LANES), 1)
    order = meeting_order(parts)

    near = rim_sums(chunks, count, starts, flat, steep, rim_bands)
    sums = [near[0] + near[1] + near[2], near[1], near[2], near[5]]
    blocks = [
        joined(chunks[order.index(part), at_sums:, :].astype(jnp.float32)) for part in range(parts)
    ]
    tails = [block[height : height + 1] for block in blocks]
    if parts % 8:
        tails.append(jnp.zeros((-parts % 8, LANES), jnp.float32))
    tails = jnp.concatenate(tails, axis=0)
    tails = pltpu.roll(tails, lax.rem(LANES - lax.rem(tail * count * layer, LANES), LANES), 1)
    narrow_row = lax.broadcasted_iota(jnp.int32, (16, LANES), 0)
    rests = [jnp.zeros((16, LANES), jnp.float32) for _ in range(parts)]
    for column in range(height):
        moved = pltpu.roll(tails, LANES - tail * column, 1) if column else tails
        for part in range(parts):
            rests[part] = jnp.where(narrow_row == column, moved[part : part + 1], rests[part])
    for part in range(parts):
        first_cell = own * part - BEFORE
        here = (lane >= first_cell) & (lane < first_cell + cells)
        values = blocks[part]
        joint = values[0:16]
        xz = pltpu.roll(jnp.where(narrow_lane < tail, rests[part], joint), LANES - 3 * cells, 1)
        for index in range(4):
            chunk = xz if index == 3 else joint
            if lanes > LANES:
                spare = jnp.zeros((16, lanes - LANES), jnp.float32)
                chunk = jnp.concatenate([chunk, spare], axis=1)
            shift = (first_cell - (index % 3) * cells) % lanes
            moved = chunk if shift == 0 else pltpu.roll(chunk, shift, 1)
            sums[index] = sums[index] + jnp.where(here, moved, 0.0)
    trace = sums[0]
    scale = (conduct_fiber - conduct_matrix) / (2.0 * trace + tensor_eps)
    conduct = [
        conduct_matrix + scale * (trace - sums[1]),
        -scale * sums[3],
        conduct_matrix + scale * (trace - sums[2]),
    ]
    for kind in range(3):
        conduct_out[kind] = conduct[kind][HALO : HALO + count]
    copies = [
        pltpu.make_async_copy(conduct_out, conduct_hbm, sems.at[0]),
        pltpu.make_async_copy(temp_out, temp_hbm, sems.at[1]),
        pltpu.make_async_copy(cure_out, cure_hbm, sems.at[2]),
    ]
    copies[0].start()

    slots = range(height + 1, height + 1 + COLUMN_ROWS * (lanes // LANES), COLUMN_ROWS)
    columns = [
        jnp.concatenate([values[at : at + COLUMN_ROWS] for at in slots], axis=1) for values in blocks
    ]
    before, after = columns[parts - 1], columns[0]
    for part in range(parts - 1):
        before = jnp.where(layer == part + 1, columns[part], before)
        after = jnp.where(layer == part, columns[part + 1], after)
    spare = jnp.full((16 - count - 2 * GHOST, lanes), 0.5, jnp.float32)
    temp = jnp.concatenate([before[:GHOST], temp_in[...], after[:GHOST], 8.0 * spare], axis=0)
    cure = jnp.concatenate([spare[:1], before[GHOST:], cure_in[...], after[GHOST:], spare[:1], spare], axis=0)
    gap = GHOST - HALO
    xx, xz, zz = [pltpu.roll(part, gap, 0) for part in conduct]

    first = (plane == 0) & (layer == 0)
    last = (plane == planes - 1) & (layer == depths - 1)
    for step in range(STEPS):
        top, bottom = tools[2 * step : 2 * step + 1, :], tools[2 * step + 1 : 2 * step + 2, :]
        temp = jnp.where((row < GHOST) & first, temp[GHOST : GHOST + 1], temp)
        temp = jnp.where(
            (row >= GHOST + count) & last, temp[GHOST + count - 1 : GHOST + count], temp
        )
        cooler = jnp.where(lane == 0, top, pltpu.roll(temp, 1, 1))
        later = jnp.where(lane == lanes - 1, bottom, pltpu.roll(temp, lanes - 1, 1))
        slant = later - cooler
        second_x = pltpu.roll(temp, 15, 0) - 2.0 * temp + pltpu.roll(temp, 1, 0)
        second_z = later - 2.0 * temp + cooler
        cross = 0.25 * (pltpu.roll(slant, 15, 0) - pltpu.roll(slant, 1, 0))
        spread = xx * second_x + 2.0 * xz * cross + zz * second_z
        inverse = 1.0 / reference_temp - 1.0 / temp
        left = 1.0 - cure
        rate = rate_first * jnp.exp(energy_first * inverse) + rate_second * jnp.exp(
            energy_second * inverse
        ) * jnp.sqrt(cure)
        rate = rate * (left * jnp.sqrt(left))
        temp = temp + time_step * (spread + heat_release * rate)
        cure = cure + time_step * rate
    temp_out[...] = temp[GHOST : GHOST + count]
    cure_out[...] = cure[GHOST : GHOST + count]
    for copy in copies[1:]:
        copy.start()
    for copy in copies:
        copy.wait()


def on_device(intensity, temp_start, cure_start, tool_levels, plan):
    rows, width, depth = intensity.shape
    count, lanes = temp_start.shape
    planes, depths = lax.axis_size("plane"), lax.axis_size("depth")
    columns, cells = sizes(width, depth)
    bf16 = jnp.bfloat16
    slots = rows * EDGE + 16 * (lanes // LANES)
    params = pltpu.CompilerParams(vmem_limit_bytes=24 * 1024 * 1024)
    vmem = pl.BlockSpec(memory_space=pltpu.VMEM)
    stay = pl.BlockSpec(memory_space=pltpu.HBM)

    fixed = lambda values: pltpu.with_memory_space_constraint(values, pltpu.HBM)
    bands, coarse = x_bands(width), coarse_x_bands(width)
    late = bands.shape[1] - EARLY
    middle = bands[:, :EARLY, EDGE : EDGE + width]
    x_hbm, early_starts = stacked(middle.reshape(2 * EARLY, -1), coarse[:, :EARLY])
    z_hbm, _ = stacked(*depth_bands(depth), coarse_depth_bands(depth))
    x_late, late_starts = stacked(bands[:, EARLY:].reshape(2 * late, -1), coarse[:, EARLY:])
    rims = rim_bands(rows)
    flat, _ = stacked(np.concatenate([rims[0], rims[2]], axis=1))
    steep, rim_starts = stacked(rims[1], *rim_x_bands(count))
    cell_bands, _ = stacked(rim_cells(rows, depth, depths))
    constants = (x_late, flat, steep, cell_bands)
    far, near, own, x_parts, z_parts, temp, cure = pl.pallas_call(
        pack_kernel,
        name="pack",
        out_shape=(
            pltpu.VMEM((slots, depth), bf16),
            pltpu.VMEM((slots, depth), bf16),
            pltpu.VMEM((rows // 2, width, 2 * depth), bf16),
            pltpu.VMEM(x_hbm.shape, bf16),
            pltpu.VMEM(z_hbm.shape, bf16),
            pltpu.VMEM((count, lanes), jnp.float32),
            pltpu.VMEM((count, lanes), jnp.float32),
        ),
        in_specs=[stay] * 5,
        scratch_shapes=[
            pltpu.VMEM((rows, width, depth), jnp.int32),
            pltpu.SemaphoreType.DMA((5,)),
        ],
        compiler_params=params,
    )(*[fixed(values) for values in (intensity, temp_start, cure_start, x_hbm, z_hbm)])

    def moved(values, pairs):
        index = [(p * depths + d, q * depths + e) for (p, d), (q, e) in pairs]
        return lax.ppermute(values, ("plane", "depth"), index)

    def swapped(values, first):
        pairs = [(p, p + 1) for p in range(first, planes - 1, 2)]
        pairs += [(q, p) for p, q in pairs]
        return moved(values, [((p, d), (q, d)) for p, q in pairs for d in range(depths)])

    far = swapped(far, 1)
    near = swapped(near, 0)

    high = coarse.shape[0]

    def scratch(count):
        return [
            pltpu.VMEM((2 * count, rows * depth), jnp.float32),
            pltpu.VMEM((3 * rows // 2 * count, 2 * depth), bf16),
            pltpu.VMEM((3 * rows // 2 * count, 2 * depth), jnp.float32),
        ]

    def cost(count):
        return pl.CostEstimate(
            flops=2 * rows * (2 * count) * 160 * depth * 4,
            bytes_accessed=4_000_000,
            transcendentals=0,
        )

    early_sums, diagonal, x_late, flat, steep, cell_bands = pl.pallas_call(
        functools.partial(early_kernel, early_starts),
        name="early",
        out_shape=(
            pltpu.VMEM((len(USED), high, LANES), jnp.float32),
            pltpu.VMEM((4 * depth, 2 * depth), bf16),
            *[pltpu.VMEM(values.shape, bf16) for values in constants],
        ),
        in_specs=[vmem] * 3 + [stay] * len(constants),
        scratch_shapes=scratch(EARLY) + [pltpu.SemaphoreType.DMA((len(constants),))],
        cost_estimate=cost(EARLY),
        compiler_params=params,
    )(own, x_parts, z_parts, *[fixed(values) for values in constants])

    products_x, voxels = own_columns(count)
    at_sums, half = chunk_rows(count, lanes)
    chunk_shape = (depths, at_sums + 2 * half, LANES)
    chunks = pl.pallas_call(
        functools.partial(late_kernel, late_starts),
        name="late",
        out_shape=pltpu.HBM(chunk_shape, bf16),
        in_specs=[vmem] * 9,
        out_specs=stay,
        scratch_shapes=[pltpu.VMEM((rows // 2, width + 2 * EDGE, 2 * depth), bf16)]
        + scratch(late)
        + [
            pltpu.VMEM(chunk_shape, bf16),
            pltpu.SemaphoreType.DMA((2,)),
        ],
        cost_estimate=cost(late),
        compiler_params=params,
    )(own, far, near, x_late, z_parts, diagonal, early_sums, temp, cure)

    faces = plan.reshape(2 * STEPS, 1) == jnp.arange(tool_levels.shape[0], dtype=jnp.int32)
    tools = jnp.sum(
        jnp.where(faces, tool_levels, jnp.zeros_like(tool_levels)), axis=1, keepdims=True
    )

    chunks = lax.all_to_all(
        chunks,
        "depth",
        split_axis=0,
        concat_axis=0,
        tiled=True,
        axis_index_groups=[meeting_order(depths)],
    )

    return pl.pallas_call(
        functools.partial(cure_kernel, cells, rim_starts),
        name="cure",
        out_shape=(
            pltpu.HBM((count, lanes), jnp.float32),
            pltpu.HBM((count, lanes), jnp.float32),
            pltpu.HBM((3, count, lanes), jnp.float32),
        ),
        in_specs=[vmem] * 7,
        out_specs=(stay, stay, stay),
        scratch_shapes=[
            pltpu.VMEM((count, lanes), jnp.float32),
            pltpu.VMEM((count, lanes), jnp.float32),
            pltpu.VMEM((3, count, lanes), jnp.float32),
            pltpu.SemaphoreType.DMA((3,)),
        ],
        compiler_params=params,
    )(chunks, temp, cure, tools, flat, steep, cell_bands)


def solution(mesh):
    return jax.shard_map(
        on_device,
        mesh=mesh,
        in_specs=(
            P(None, "plane", "depth"),
            P(("plane", "depth"), None),
            P(("plane", "depth"), None),
            P(),
            P(),
        ),
        out_specs=(
            P(("plane", "depth"), None),
            P(("plane", "depth"), None),
            P(None, ("plane", "depth"), None),
        ),
        check_vma=False,
    )
```

```python
import functools

import jax
import jax.numpy as jnp
import ml_dtypes
import numpy as np
from jax import lax
from jax.experimental import pallas as pl
from jax.experimental.pallas import tpu as pltpu
from jax.sharding import PartitionSpec as P

ROWS = 8
R1 = 6
R2 = 10
COARSE = 4
STEPS = 3

sigma_grad = 2.0
sigma_tensor = 3.3
conduct_matrix = 0.3
conduct_fiber = 1.5
time_step = 0.25
heat_release = 0.4
rate_first = 0.15
rate_second = 0.6
energy_first = 30.0
energy_second = 25.0
reference_temp = 4.2
tensor_eps = 1e-06

LANES = 128
HALO = 2
EDGE = HALO * COARSE + R1 + R2
EARLY = 96
GHOST = 3
COLUMN_ROWS = 2 * GHOST - 1
RIM = 2 * R1
BEFORE = -(-(R2 - R1) // COARSE)
AFTER = BEFORE
HALF = LANES // 2
ROW_KINDS = (1, 0, 0)
X_KINDS = (0, 1, 0)
DEPTH_KINDS = (0, 0, 1)


def smooth_taps(radius, sigma):
    offsets = np.arange(-radius, radius + 1) * 1.0
    weights = np.exp(-0.5 * offsets * offsets / (sigma * sigma))
    return weights / weights.sum()


def slope_taps(radius, sigma):
    offsets = np.arange(-radius, radius + 1) * 1.0
    weights = np.exp(-0.5 * offsets * offsets / (sigma * sigma))
    return offsets * weights / np.sum(offsets * offsets * weights)


def row_weights(count, radius, sigma):
    taps = smooth_taps(radius, sigma)
    result = np.zeros(count)
    for source in range(count):
        for target in range(count):
            offset = target - source
            if abs(offset) <= radius:
                result[source] += taps[offset + radius]
    return result


def rounded(taps):
    best = None
    for factor in np.linspace(1.0, 2.0, 20001)[:-1]:
        near = (taps * factor).astype(np.float32).astype(ml_dtypes.bfloat16).astype(np.float64)
        error = np.abs(near / factor - taps).sum()
        if best is None or error < best[0]:
            best = (error, near, factor)
    return best[1], best[2]


def as_bfloat16(matrix):
    return matrix.astype(np.float32).astype(ml_dtypes.bfloat16)


def halves(matrix):
    high = as_bfloat16(matrix)
    return high, as_bfloat16(matrix - high.astype(np.float64))


def sizes(width, depth):
    columns = width // COARSE + 2 * HALO
    cells = depth // COARSE + BEFORE + AFTER
    return columns, cells


def product_rows(width):
    places = [*range(R1, width - R1)]
    places += [None] * max(EARLY - len(places), 0)
    places += [*range(R1 - EDGE, R1), *range(width - R1, width + EDGE - R1)]
    return places + [None] * (-len(places) % 16)


GRAD_TAPS = tuple(
    rounded(taps(R1, sigma_grad)) for taps in (smooth_taps, slope_taps)
)
GRAD_FACTOR = GRAD_TAPS[0][1] ** 2 * GRAD_TAPS[1][1]


def grad_taps(kind):
    return GRAD_TAPS[kind][0]


def tap(taps, offset):
    radius = (len(taps) - 1) // 2
    return float(taps[offset + radius]) if abs(offset) <= radius else 0.0


def x_bands(width):
    places = product_rows(width)
    bands = np.zeros((2, len(places), width + 2 * EDGE))
    for kind in range(2):
        for row, place in enumerate(places):
            if place is not None:
                first = place + EDGE - R1
                bands[kind, row, first : first + 2 * R1 + 1] = grad_taps(kind)
    return bands


def rim_bands(rows):
    bands = np.zeros((3, 3 * LANES, LANES))
    for part in range(3):
        row_taps, depth_taps = grad_taps(ROW_KINDS[part]), grad_taps(DEPTH_KINDS[part])
        for source in range(rows):
            for target in range(rows):
                row_tap = tap(row_taps, source - target)
                for near in range(-RIM, RIM):
                    lane = source * RIM + near % RIM
                    if near >= 0:
                        lane += rows * RIM + LANES
                    for place in range(-R1, R1):
                        value = row_tap * tap(depth_taps, near - place)
                        bands[part, lane, target * 2 * R1 + R1 + place] = value
    return bands


def rim_cells(rows, depth, blocks):
    taps = smooth_taps(R2, sigma_tensor)
    weights = product_weights(rows)
    bands = np.zeros((blocks - 1, LANES, blocks * depth // COARSE))
    for boundary in range(blocks - 1):
        middle = (boundary + 1) * depth
        for cell in range(bands.shape[2]):
            for voxel in range(cell * COARSE, (cell + 1) * COARSE):
                for place in range(-R1, R1):
                    value = tap(taps, middle + place - voxel)
                    for row in range(rows):
                        bands[boundary, row * 2 * R1 + R1 + place, cell] += weights[row] * value
    return bands.reshape(-1, bands.shape[2])


def meeting_order(blocks):
    middle = blocks // 2
    rest = [block for block in range(blocks) if block != middle]
    ends = [rest.pop(0 if turn % 2 == 0 else -1) for turn in range(blocks - 1)]
    return [middle, *ends]


def own_columns(count):
    products = (count + 2 * HALO) * COARSE + 2 * R2
    voxels = products + 2 * R1
    return -(-products // 16) * 16, -(-voxels // 8) * 8


def fold(voxels):
    return -(-voxels // 16) * 8


def rim_x_bands(count):
    products, voxels = own_columns(count)
    bands = np.zeros((2, products, -(-voxels // 16) * 16))
    valid = (count + 2 * HALO) * COARSE + 2 * R2
    for kind in range(2):
        for row in range(valid):
            bands[kind, row, row : row + 2 * R1 + 1] = grad_taps(kind)
    taps = smooth_taps(R2, sigma_tensor)
    coarse = np.zeros((16, products))
    for column in range(count + 2 * HALO):
        for voxel in range(column * COARSE, (column + 1) * COARSE):
            coarse[column, voxel : voxel + 2 * R2 + 1] += taps
    return bands.reshape(2 * products, -1), coarse


def depth_bands(depth):
    bands = np.zeros((2, depth, depth))
    for kind in range(2):
        for place in range(depth):
            for near in range(max(place - R1, 0), min(place + R1 + 1, depth)):
                bands[kind, near, place] = tap(grad_taps(kind), near - place)
    return bands


def product_weights(rows):
    return row_weights(rows, R2, sigma_tensor) / (255.0 * GRAD_FACTOR) ** 2


def coarse_depth_bands(depth):
    taps = smooth_taps(R2, sigma_tensor)
    columns, cells = sizes(0, depth)
    bands = np.zeros((depth, LANES))
    for cell in range(cells):
        for voxel in range(COARSE):
            place = (cell - BEFORE) * COARSE + voxel
            for near in range(max(place - R2, 0), min(place + R2 + 1, depth)):
                bands[near, cell] += tap(taps, near - place)
    return bands


def coarse_x_bands(width):
    taps = smooth_taps(R2, sigma_tensor)
    places = product_rows(width)
    columns, cells = sizes(width, 0)
    bands = np.zeros((-(-columns // 16) * 16, len(places)))
    for column in range(columns):
        for voxel in range(COARSE):
            middle = (column - HALO) * COARSE + voxel
            for row, place in enumerate(places):
                if place is not None:
                    bands[column, row] += tap(taps, place - middle)
    return bands


def stacked(*pieces):
    widest = max(piece.shape[1] for piece in pieces)
    padded = [np.pad(piece, ((0, 0), (0, widest - piece.shape[1]))) for piece in pieces]
    starts = np.cumsum([0] + [len(piece) for piece in pieces])
    return jnp.asarray(as_bfloat16(np.concatenate(padded))), tuple(int(start) for start in starts)


def two_parts(values):
    high = values.astype(jnp.bfloat16).astype(jnp.float32)
    return jnp.concatenate([high, (values - high).astype(jnp.bfloat16).astype(jnp.float32)], axis=0)


def joined(parts):
    half = parts.shape[0] // 2
    return parts[:half] + parts[half:]


def column_rows(temp, cure, at_end):
    count = temp.shape[0]
    first, second = (count - GHOST, count - GHOST + 1) if at_end else (0, 0)
    pad = jnp.zeros((8 - COLUMN_ROWS, temp.shape[1]), jnp.float32)
    return jnp.concatenate(
        [temp[first : first + GHOST, :], cure[second : second + GHOST - 1, :], pad], axis=0
    )


def chunk_rows(count, lanes):
    products, voxels = own_columns(count)
    held = count + 2 * HALO + 1 + COLUMN_ROWS * (lanes // LANES)
    return voxels + fold(voxels), -(-held // 8) * 8


def is_odd():
    return lax.rem(lax.axis_index("plane"), 2) == 1


def pack_kernel(
    intensity, temp_hbm, cure_hbm, x_hbm, z_hbm, far, near, own, x_parts, z_parts, temp, cure,
    grey, sems,
):
    rows, width, depth = intensity.shape
    copies = [
        pltpu.make_async_copy(intensity, grey, sems.at[0]),
        pltpu.make_async_copy(temp_hbm, temp, sems.at[1]),
        pltpu.make_async_copy(cure_hbm, cure, sems.at[2]),
        pltpu.make_async_copy(x_hbm, x_parts, sems.at[3]),
        pltpu.make_async_copy(z_hbm, z_parts, sems.at[4]),
    ]
    for copy in copies:
        copy.start()
    for copy in copies[:3]:
        copy.wait()
    odd = is_odd()
    sides = [
        two_parts(column_rows(temp, cure, at_end)).astype(jnp.bfloat16)
        for at_end in (False, True)
    ]

    def send(left, right):
        for place, target, columns in ((0, left, sides[0]), (width - EDGE, right, sides[1])):
            for pair in range(rows // 2):
                two = [grey[2 * pair + i, place : place + EDGE, :] for i in range(2)]
                two = jnp.concatenate(two, axis=0).astype(jnp.float32)
                target[2 * EDGE * pair : 2 * EDGE * (pair + 1), :] = two.astype(jnp.bfloat16)
            for slot in range(temp.shape[1] // LANES):
                at = rows * EDGE + 16 * slot
                target[at : at + 16, :] = columns[:, slot * LANES : (slot + 1) * LANES]

    @pl.when(odd)
    def _():
        send(near, far)

    @pl.when(jnp.logical_not(odd))
    def _():
        send(far, near)

    for row in range(rows):
        half = (row % 2) * depth
        own[row // 2, :, half : half + depth] = grey[row].astype(jnp.float32).astype(jnp.bfloat16)
    for copy in copies[3:]:
        copy.wait()


def packed_rows(values, size, first):
    depth = values[0].shape[1]
    lane = lax.broadcasted_iota(jnp.int32, values[0].shape, 1)
    packed = None
    for block, value in enumerate(values):
        shift = (size * block - first) % depth
        moved = value if shift == 0 else pltpu.roll(value, shift, 1)
        packed = moved if block == 0 else jnp.where(lane >= size * block, moved, packed)
    return packed


def edges_of(ref, rows):
    two = [
        ref[2 * EDGE * pair : 2 * EDGE * (pair + 1), :].astype(jnp.float32)
        for pair in range(rows // 2)
    ]
    voxels = [two[row // 2][row % 2 * EDGE : (row % 2 + 1) * EDGE] for row in range(rows)]
    slots = range(rows * EDGE, ref.shape[0], 16)
    columns = [joined(ref[at : at + 16, :].astype(jnp.float32)) for at in slots]
    return voxels, jnp.concatenate(columns, axis=1)


def product(first, second):
    return jnp.dot(first, second, preferred_element_type=jnp.float32)


def mirrored_filter(kind, values, even):
    rows = len(values)
    use_sum = even == (kind == 0)
    sign = 1.0 if use_sum else -1.0
    half = [values[row] + sign * values[rows - 1 - row] for row in range(rows // 2)]
    results = []
    for row in range(rows // 2):
        total = None
        for source, value in enumerate(half):
            near = tap(grad_taps(kind), source - row)
            far = tap(grad_taps(kind), rows - 1 - source - row)
            weight = 0.5 * (near + sign * far)
            total = weight * value if total is None else total + weight * value
        results.append(total)
    return results


def weighted_products(three, weight):
    pairs = ((0, 0), (1, 1), (2, 2), (0, 1), (0, 2), (1, 2))
    first = [weight * value for value in three]
    return [first[a] * three[b] for a, b in pairs]


def late_mask(count, width):
    row = lax.broadcasted_iota(jnp.int32, (count, LANES), 0)
    left = max(width - 2 * R1 - EARLY, 0)
    place = jnp.where(row < left + EDGE, row - left + R1 - EDGE, row - left - EDGE + width - R1)
    place = place + lax.axis_index("plane") * width
    inside = (place >= 0) & (place < lax.axis_size("plane") * width)
    return jnp.where(inside | (row < left), 1.0, 0.0)


USED = (0, 1, 2, 5)
UNUSED = (3, 4)


def all_sums(products, coarse, sx):
    sums = [None] * 6
    for kinds in (USED, UNUSED):
        tiles = [tile for index in kinds for tile in products[index]]
        along = product(sx, jnp.concatenate(tiles, axis=1)).astype(jnp.bfloat16)
        step = along.shape[1] // len(kinds)
        parts = [along[:, index * step : (index + 1) * step] for index in range(len(kinds))]
        total = product(jnp.concatenate(parts, axis=0), coarse)
        high = sx.shape[0]
        for index, kind in enumerate(kinds):
            sums[kind] = total[index * high : (index + 1) * high]
    return sums


def tensor_sums(window, bands, sx, mask, diagonal, z_parts, across, filtered, grads):
    pairs, height, double = window.shape
    rows, depth = 2 * pairs, double // 2
    count = bands.shape[0] // 2
    whole = jnp.concatenate([window[pair] for pair in range(pairs)], axis=1)
    across[...] = product(bands, whole)

    for start in range(0, count, 16):
        kinds = [
            [
                across[kind * count + start : kind * count + start + 16, row * depth : (row + 1) * depth]
                for row in range(rows)
            ]
            for kind in range(2)
        ]
        for part in range(3):
            values = kinds[X_KINDS[part]]
            results = mirrored_filter(ROW_KINDS[part], values, True)
            results += mirrored_filter(ROW_KINDS[part], values, False)
            for row, result in enumerate(results):
                at = (part * pairs + row // 2) * count + start
                lanes = slice((row % 2) * depth, (row % 2 + 1) * depth)
                filtered[at : at + 16, lanes] = result.astype(jnp.bfloat16)

    at = 2 * pairs * count
    grads[:at] = product(filtered[:at, :], diagonal[0:double, :])
    grads[at:] = product(filtered[at:, :], diagonal[double : 2 * double, :])

    weights = product_weights(rows)
    layer = lax.axis_index("depth")
    first, last = layer == 0, layer == lax.axis_size("depth") - 1
    place = lax.broadcasted_iota(jnp.int32, (16, depth), 1)
    complete = ((place >= R1) | first) & ((place < depth - R1) | last)
    complete = jnp.where(complete, 1.0, 0.0)
    groups = [[] for _ in range(6)]
    for start in range(0, count, 16):
        inside = complete if mask is None else complete * mask[start : start + 16]
        totals = None
        for row in range(rows):
            lanes = slice((row % 2) * depth, (row % 2 + 1) * depth)
            three = []
            for part in range(3):
                at = (part * pairs + row // 2) * count + start
                three.append(grads[at : at + 16, lanes])
            terms = weighted_products(three, 2.0 * float(weights[row % (rows // 2)]))
            totals = terms if row == 0 else [a + b for a, b in zip(totals, terms)]
        for index in range(6):
            groups[index].append((totals[index] * inside).astype(jnp.bfloat16))
    products = [[jnp.concatenate(group, axis=0)] for group in groups]
    return all_sums(products, z_parts[double : double + depth, :], sx)


def early_kernel(*refs):
    starts, own, x_parts, z_parts, *rest = refs
    count = (len(rest) - 6) // 2
    constants, (sums, diagonal), held = rest[:count], rest[count : count + 2], rest[count + 2 : -4]
    across, filtered, grads, sems = rest[-4:]
    copies = [
        pltpu.make_async_copy(source, target, sems.at[index])
        for index, (source, target) in enumerate(zip(constants, held))
    ]
    for copy in copies:
        copy.start()
    pairs, width, double = own.shape
    depth = double // 2
    empty = jnp.zeros((depth, depth), jnp.bfloat16)
    for kind in range(2):
        for half in range(2):
            at = pl.ds(kind * double + half * depth, depth)
            band = z_parts[kind * depth : (kind + 1) * depth, :]
            diagonal[at, half * depth : (half + 1) * depth] = band
            diagonal[at, (1 - half) * depth : (2 - half) * depth] = empty
    bands = x_parts[starts[0] : starts[1], :width]
    sx = x_parts[starts[1] : starts[2], :EARLY]
    results = tensor_sums(own, bands, sx, None, diagonal, z_parts, across, filtered, grads)
    for index, kind in enumerate(USED):
        sums[index] = results[kind]
    for copy in copies:
        copy.wait()


def late_kernel(
    starts, own, far, near, x_late, z_parts, diagonal, early_sums, temp, cure, out_hbm,
    window, across, filtered, grads, out, sems,
):
    pairs, width, double = own.shape
    rows, depth = 2 * pairs, double // 2
    count, lanes = temp.shape
    odd = is_odd()
    depths, layer = lax.axis_size("depth"), lax.axis_index("depth")
    outer, outer_columns = edges_of(far, rows)
    inner, inner_columns = edges_of(near, rows)
    values = []
    for row in range(rows):
        half = (row % 2) * depth
        middle = own[row // 2, :, half : half + depth].astype(jnp.float32)
        left = jnp.where(odd, inner[row], outer[row])
        right = jnp.where(odd, outer[row], inner[row])
        whole = jnp.concatenate([left, middle, right], axis=0)
        window[row // 2, :, half : half + depth] = whole.astype(jnp.bfloat16)
        values.append(whole)
    left = jnp.where(odd, inner_columns, outer_columns)
    right = jnp.where(odd, outer_columns, inner_columns)

    products_x, voxels = own_columns(count)
    folded, stride = fold(voxels), COARSE * count
    below = packed_rows(values, RIM, depth - RIM)
    above = pltpu.roll(packed_rows(values, RIM, 0), rows * RIM, 1)
    lane = lax.broadcasted_iota(jnp.int32, below.shape, 1)
    tiles = [jnp.where(lane < rows * RIM, below, above), above, pltpu.roll(above, HALF, 1)]
    missing = stride * (depths - 1) + voxels - below.shape[0]
    if missing > 0:
        spare = jnp.zeros((-(-missing // 8) * 8, LANES), jnp.float32)
        tiles = [jnp.concatenate([tile, spare], axis=0) for tile in tiles]

    height = count + 2 * HALO
    half_lane = lax.broadcasted_iota(jnp.int32, (folded, LANES), 1) < HALF
    order = meeting_order(out.shape[0])
    for position, target in enumerate(order):
        at = stride * target
        second = jnp.where(
            half_lane,
            tiles[1][at : at + folded],
            tiles[2][at + voxels - folded : at + voxels],
        )
        rims = jnp.concatenate([tiles[0][at : at + voxels], second], axis=0)
        out[position, 0 : voxels + folded, :] = rims.astype(jnp.bfloat16)
    split = (pl.ds(0, voxels + folded), pl.ds(voxels + folded, out.shape[1] - voxels - folded))
    copies = [
        pltpu.make_async_copy(out.at[:, part, :], out_hbm.at[:, part, :], sems.at[index])
        for index, part in enumerate(split)
    ]
    copies[0].start()

    late = across.shape[0] // 2
    bands = x_late[starts[0] : starts[1], :]
    sx = x_late[starts[1] : starts[2], :late]
    results = tensor_sums(
        window, bands, sx, late_mask(late, width), diagonal, z_parts, across, filtered, grads
    )
    yy, xx, zz, xz = [early_sums[index] + results[kind] for index, kind in enumerate(USED)]
    trace = yy + xx + zz
    lane = lax.broadcasted_iota(jnp.int32, trace.shape, 1)
    columns, cells = sizes(width, depth)
    tail = 4 * cells - LANES
    joint = pltpu.roll(xz, 3 * cells, 1)
    rest = jnp.where(lane < tail, joint, 0.0)
    rest = pltpu.roll(rest, 0, 1, stride=tail, stride_axis=0)
    for index, part in ((2, zz), (1, xx), (0, trace)):
        moved = part if index == 0 else pltpu.roll(part, index * cells, 1)
        joint = jnp.where(lane < (index + 1) * cells, moved, joint)

    own_first, own_last = column_rows(temp, cure, False), column_rows(temp, cure, True)
    half = chunk_rows(count, lanes)[1]
    for position, target in enumerate(order):
        piece = jnp.where(layer == target - 1, own_last, 0.0)
        piece = jnp.where(layer == target + 1, own_first, piece)
        if target == 0:
            piece = jnp.where(layer == depths - 1, left, piece)
        if target == out.shape[0] - 1:
            piece = jnp.where(layer == 0, right, piece)
        mine = slice(count * target, count * target + height)
        pieces = [joint[mine], jnp.sum(rest[mine], axis=0, keepdims=True)]
        for slot in range(lanes // LANES):
            pieces.append(piece[0:COLUMN_ROWS, slot * LANES : (slot + 1) * LANES])
        filled = sum(part.shape[0] for part in pieces)
        if filled < half:
            pieces.append(jnp.zeros((half - filled, LANES), jnp.float32))
        sent = two_parts(jnp.concatenate(pieces, axis=0))
        out[position, voxels + folded :, :] = sent.astype(jnp.bfloat16)
    copies[1].start()
    for copy in copies:
        copy.wait()


def rim_sums(chunks, count, starts, flat, steep, cells):
    parts = chunks.shape[0]
    rows_x, voxels = own_columns(count)
    folded = fold(voxels)
    tall = -(-voxels // 16) * 16
    spare = [jnp.zeros((tall - voxels, LANES), jnp.float32)] if tall > voxels else []
    tiles = []
    order = meeting_order(parts)
    for part in range(parts):
        rims = chunks[order.index(part), 0 : voxels + folded, :].astype(jnp.float32)
        second = rims[voxels:]
        second = [second[: voxels - folded], pltpu.roll(second, HALF, 1)]
        for tile in ([rims[:voxels]], second):
            tiles.append(jnp.concatenate(tile + spare, axis=0).astype(jnp.bfloat16))
    result = product(
        steep[starts[1] : starts[2], :tall], jnp.concatenate(tiles, axis=1)
    ).astype(jnp.bfloat16)
    kinds = []
    for kind in range(2):
        values = result[kind * rows_x : (kind + 1) * rows_x]
        tile = lambda index: values[:, index * LANES : (index + 1) * LANES]
        stack = [
            jnp.concatenate([tile(2 * part), tile(2 * part + 2), tile(2 * part + 3)], axis=1)
            for part in range(parts - 1)
        ]
        kinds.append(jnp.concatenate(stack, axis=0))
    both = product(kinds[0], flat[...])
    three = (both[:, :LANES], product(kinds[1], steep[starts[0] : starts[1], :]), both[:, LANES:])

    index = lax.axis_index("plane") * lax.axis_size("depth") + lax.axis_index("depth")
    total = lax.axis_size("plane") * lax.axis_size("depth") * count * COARSE
    place = lax.rem(lax.broadcasted_iota(jnp.int32, three[0].shape, 0), rows_x)
    place = place + (index * count - HALO) * COARSE - R2
    inside = jnp.where((place >= 0) & (place < total), 1.0, 0.0)
    products = [
        [
            term[part * rows_x : (part + 1) * rows_x].astype(jnp.bfloat16)
            for part in range(parts - 1)
        ]
        for term in weighted_products(three, inside)
    ]
    return all_sums(products, cells[...], steep[starts[2] : starts[3], :rows_x])


def cure_kernel(
    cells, starts, chunks, temp_in, cure_in, tools, flat, steep, rim_bands, temp_hbm, cure_hbm,
    conduct_hbm, temp_out, cure_out, conduct_out, sems,
):
    count, lanes = temp_in.shape
    parts = chunks.shape[0]
    planes, depths = lax.axis_size("plane"), lax.axis_size("depth")
    plane, layer = lax.axis_index("plane"), lax.axis_index("depth")
    height = count + 2 * HALO
    own = cells - BEFORE - AFTER
    lane = lax.broadcasted_iota(jnp.int32, (16, lanes), 1)
    row = lax.broadcasted_iota(jnp.int32, (16, lanes), 0)
    at_sums, half = chunk_rows(count, lanes)
    tail = 4 * cells - LANES
    narrow_lane = lax.broadcasted_iota(jnp.int32, (16, LANES), 1)
    order = meeting_order(parts)

    near = rim_sums(chunks, count, starts, flat, steep, rim_bands)
    sums = [near[0] + near[1] + near[2], near[1], near[2], near[5]]
    blocks = [
        joined(chunks[order.index(part), at_sums:, :].astype(jnp.float32)) for part in range(parts)
    ]
    tails = [block[height : height + 1] for block in blocks]
    if parts % 8:
        tails.append(jnp.zeros((-parts % 8, LANES), jnp.float32))
    tails = jnp.concatenate(tails, axis=0)
    tails = pltpu.roll(tails, lax.rem(LANES - lax.rem(tail * count * layer, LANES), LANES), 1)
    narrow_row = lax.broadcasted_iota(jnp.int32, (16, LANES), 0)
    rests = [jnp.zeros((16, LANES), jnp.float32) for _ in range(parts)]
    for column in range(height):
        moved = pltpu.roll(tails, LANES - tail * column, 1) if column else tails
        for part in range(parts):
            rests[part] = jnp.where(narrow_row == column, moved[part : part + 1], rests[part])
    for part in range(parts):
        first_cell = own * part - BEFORE
        here = (lane >= first_cell) & (lane < first_cell + cells)
        values = blocks[part]
        joint = values[0:16]
        xz = pltpu.roll(jnp.where(narrow_lane < tail, rests[part], joint), LANES - 3 * cells, 1)
        for index in range(4):
            chunk = xz if index == 3 else joint
            if lanes > LANES:
                spare = jnp.zeros((16, lanes - LANES), jnp.float32)
                chunk = jnp.concatenate([chunk, spare], axis=1)
            shift = (first_cell - (index % 3) * cells) % lanes
            moved = chunk if shift == 0 else pltpu.roll(chunk, shift, 1)
            sums[index] = sums[index] + jnp.where(here, moved, 0.0)
    trace = sums[0]
    scale = (conduct_fiber - conduct_matrix) / (2.0 * trace + tensor_eps)
    conduct = [
        conduct_matrix + scale * (trace - sums[1]),
        -scale * sums[3],
        conduct_matrix + scale * (trace - sums[2]),
    ]
    for kind in range(3):
        conduct_out[kind] = conduct[kind][HALO : HALO + count]
    copies = [
        pltpu.make_async_copy(conduct_out, conduct_hbm, sems.at[0]),
        pltpu.make_async_copy(temp_out, temp_hbm, sems.at[1]),
        pltpu.make_async_copy(cure_out, cure_hbm, sems.at[2]),
    ]
    copies[0].start()

    slots = range(height + 1, height + 1 + COLUMN_ROWS * (lanes // LANES), COLUMN_ROWS)
    columns = [
        jnp.concatenate([values[at : at + COLUMN_ROWS] for at in slots], axis=1) for values in blocks
    ]
    before, after = columns[parts - 1], columns[0]
    for part in range(parts - 1):
        before = jnp.where(layer == part + 1, columns[part], before)
        after = jnp.where(layer == part, columns[part + 1], after)
    spare = jnp.full((16 - count - 2 * GHOST, lanes), 0.5, jnp.float32)
    temp = jnp.concatenate([before[:GHOST], temp_in[...], after[:GHOST], 8.0 * spare], axis=0)
    cure = jnp.concatenate([spare[:1], before[GHOST:], cure_in[...], after[GHOST:], spare[:1], spare], axis=0)
    gap = GHOST - HALO
    xx, xz, zz = [pltpu.roll(part, gap, 0) for part in conduct]

    first = (plane == 0) & (layer == 0)
    last = (plane == planes - 1) & (layer == depths - 1)
    for step in range(STEPS):
        top, bottom = tools[2 * step : 2 * step + 1, :], tools[2 * step + 1 : 2 * step + 2, :]
        temp = jnp.where((row < GHOST) & first, temp[GHOST : GHOST + 1], temp)
        temp = jnp.where(
            (row >= GHOST + count) & last, temp[GHOST + count - 1 : GHOST + count], temp
        )
        cooler = jnp.where(lane == 0, top, pltpu.roll(temp, 1, 1))
        later = jnp.where(lane == lanes - 1, bottom, pltpu.roll(temp, lanes - 1, 1))
        slant = later - cooler
        second_x = pltpu.roll(temp, 15, 0) - 2.0 * temp + pltpu.roll(temp, 1, 0)
        second_z = later - 2.0 * temp + cooler
        cross = 0.25 * (pltpu.roll(slant, 15, 0) - pltpu.roll(slant, 1, 0))
        spread = xx * second_x + 2.0 * xz * cross + zz * second_z
        inverse = 1.0 / reference_temp - 1.0 / temp
        left = 1.0 - cure
        rate = rate_first * jnp.exp(energy_first * inverse) + rate_second * jnp.exp(
            energy_second * inverse
        ) * jnp.sqrt(cure)
        rate = rate * (left * jnp.sqrt(left))
        temp = temp + time_step * (spread + heat_release * rate)
        cure = cure + time_step * rate
    temp_out[...] = temp[GHOST : GHOST + count]
    cure_out[...] = cure[GHOST : GHOST + count]
    for copy in copies[1:]:
        copy.start()
    for copy in copies:
        copy.wait()


def on_device(intensity, temp_start, cure_start, tool_levels, plan):
    rows, width, depth = intensity.shape
    count, lanes = temp_start.shape
    planes, depths = lax.axis_size("plane"), lax.axis_size("depth")
    columns, cells = sizes(width, depth)
    bf16 = jnp.bfloat16
    slots = rows * EDGE + 16 * (lanes // LANES)
    params = pltpu.CompilerParams(vmem_limit_bytes=24 * 1024 * 1024)
    vmem = pl.BlockSpec(memory_space=pltpu.VMEM)
    stay = pl.BlockSpec(memory_space=pltpu.HBM)

    fixed = lambda values: pltpu.with_memory_space_constraint(values, pltpu.HBM)
    bands, coarse = x_bands(width), coarse_x_bands(width)
    late = bands.shape[1] - EARLY
    middle = bands[:, :EARLY, EDGE : EDGE + width]
    x_hbm, early_starts = stacked(middle.reshape(2 * EARLY, -1), coarse[:, :EARLY])
    z_hbm, _ = stacked(*depth_bands(depth), coarse_depth_bands(depth))
    x_late, late_starts = stacked(bands[:, EARLY:].reshape(2 * late, -1), coarse[:, EARLY:])
    rims = rim_bands(rows)
    flat, _ = stacked(np.concatenate([rims[0], rims[2]], axis=1))
    steep, rim_starts = stacked(rims[1], *rim_x_bands(count))
    cell_bands, _ = stacked(rim_cells(rows, depth, depths))
    constants = (x_late, flat, steep, cell_bands)
    far, near, own, x_parts, z_parts, temp, cure = pl.pallas_call(
        pack_kernel,
        name="pack",
        out_shape=(
            pltpu.VMEM((slots, depth), bf16),
            pltpu.VMEM((slots, depth), bf16),
            pltpu.VMEM((rows // 2, width, 2 * depth), bf16),
            pltpu.VMEM(x_hbm.shape, bf16),
            pltpu.VMEM(z_hbm.shape, bf16),
            pltpu.VMEM((count, lanes), jnp.float32),
            pltpu.VMEM((count, lanes), jnp.float32),
        ),
        in_specs=[stay] * 5,
        scratch_shapes=[
            pltpu.VMEM((rows, width, depth), jnp.int32),
            pltpu.SemaphoreType.DMA((5,)),
        ],
        compiler_params=params,
    )(*[fixed(values) for values in (intensity, temp_start, cure_start, x_hbm, z_hbm)])

    def moved(values, pairs):
        index = [(p * depths + d, q * depths + e) for (p, d), (q, e) in pairs]
        return lax.ppermute(values, ("plane", "depth"), index)

    def swapped(values, first):
        pairs = [(p, p + 1) for p in range(first, planes - 1, 2)]
        pairs += [(q, p) for p, q in pairs]
        return moved(values, [((p, d), (q, d)) for p, q in pairs for d in range(depths)])

    far = swapped(far, 1)
    near = swapped(near, 0)

    high = coarse.shape[0]

    def scratch(count):
        return [
            pltpu.VMEM((2 * count, rows * depth), jnp.float32),
            pltpu.VMEM((3 * rows // 2 * count, 2 * depth), bf16),
            pltpu.VMEM((3 * rows // 2 * count, 2 * depth), jnp.float32),
        ]

    def cost(count):
        return pl.CostEstimate(
            flops=2 * rows * (2 * count) * 160 * depth * 4,
            bytes_accessed=4_000_000,
            transcendentals=0,
        )

    early_sums, diagonal, x_late, flat, steep, cell_bands = pl.pallas_call(
        functools.partial(early_kernel, early_starts),
        name="early",
        out_shape=(
            pltpu.VMEM((len(USED), high, LANES), jnp.float32),
            pltpu.VMEM((4 * depth, 2 * depth), bf16),
            *[pltpu.VMEM(values.shape, bf16) for values in constants],
        ),
        in_specs=[vmem] * 3 + [stay] * len(constants),
        scratch_shapes=scratch(EARLY) + [pltpu.SemaphoreType.DMA((len(constants),))],
        cost_estimate=cost(EARLY),
        compiler_params=params,
    )(own, x_parts, z_parts, *[fixed(values) for values in constants])

    products_x, voxels = own_columns(count)
    at_sums, half = chunk_rows(count, lanes)
    chunk_shape = (depths, at_sums + 2 * half, LANES)
    chunks = pl.pallas_call(
        functools.partial(late_kernel, late_starts),
        name="late",
        out_shape=pltpu.HBM(chunk_shape, bf16),
        in_specs=[vmem] * 9,
        out_specs=stay,
        scratch_shapes=[pltpu.VMEM((rows // 2, width + 2 * EDGE, 2 * depth), bf16)]
        + scratch(late)
        + [
            pltpu.VMEM(chunk_shape, bf16),
            pltpu.SemaphoreType.DMA((2,)),
        ],
        cost_estimate=cost(late),
        compiler_params=params,
    )(own, far, near, x_late, z_parts, diagonal, early_sums, temp, cure)

    faces = plan.reshape(2 * STEPS, 1) == jnp.arange(tool_levels.shape[0], dtype=jnp.int32)
    tools = jnp.sum(
        jnp.where(faces, tool_levels, jnp.zeros_like(tool_levels)), axis=1, keepdims=True
    )

    chunks = lax.all_to_all(
        chunks,
        "depth",
        split_axis=0,
        concat_axis=0,
        tiled=True,
        axis_index_groups=[meeting_order(depths)],
    )

    return pl.pallas_call(
        functools.partial(cure_kernel, cells, rim_starts),
        name="cure",
        out_shape=(
            pltpu.HBM((count, lanes), jnp.float32),
            pltpu.HBM((count, lanes), jnp.float32),
            pltpu.HBM((3, count, lanes), jnp.float32),
        ),
        in_specs=[vmem] * 7,
        out_specs=(stay, stay, stay),
        scratch_shapes=[
            pltpu.VMEM((count, lanes), jnp.float32),
            pltpu.VMEM((count, lanes), jnp.float32),
            pltpu.VMEM((3, count, lanes), jnp.float32),
            pltpu.SemaphoreType.DMA((3,)),
        ],
        compiler_params=params,
    )(chunks, temp, cure, tools, flat, steep, cell_bands)


def solution(mesh):
    return jax.shard_map(
        on_device,
        mesh=mesh,
        in_specs=(
            P(None, "plane", "depth"),
            P(("plane", "depth"), None),
            P(("plane", "depth"), None),
            P(),
            P(),
        ),
        out_specs=(
            P(("plane", "depth"), None),
            P(("plane", "depth"), None),
            P(None, ("plane", "depth"), None),
        ),
        check_vma=False,
    )
```

```python
import functools

import jax
import jax.numpy as jnp
import ml_dtypes
import numpy as np
from jax import lax
from jax.experimental import pallas as pl
from jax.experimental.pallas import tpu as pltpu
from jax.sharding import PartitionSpec as P

ROWS = 8
R1 = 6
R2 = 10
COARSE = 4
STEPS = 3

sigma_grad = 2.0
sigma_tensor = 3.3
conduct_matrix = 0.3
conduct_fiber = 1.5
time_step = 0.25
heat_release = 0.4
rate_first = 0.15
rate_second = 0.6
energy_first = 30.0
energy_second = 25.0
reference_temp = 4.2
tensor_eps = 1e-06

LANES = 128
HALO = 2
EDGE = HALO * COARSE + R1 + R2
EARLY = 96
GHOST = 3
COLUMN_ROWS = 2 * GHOST - 1
RIM = 2 * R1
BEFORE = -(-(R2 - R1) // COARSE)
AFTER = BEFORE
HALF = LANES // 2
ROW_KINDS = (1, 0, 0)
X_KINDS = (0, 1, 0)
DEPTH_KINDS = (0, 0, 1)


def smooth_taps(radius, sigma):
    offsets = np.arange(-radius, radius + 1) * 1.0
    weights = np.exp(-0.5 * offsets * offsets / (sigma * sigma))
    return weights / weights.sum()


def slope_taps(radius, sigma):
    offsets = np.arange(-radius, radius + 1) * 1.0
    weights = np.exp(-0.5 * offsets * offsets / (sigma * sigma))
    return offsets * weights / np.sum(offsets * offsets * weights)


def row_weights(count, radius, sigma):
    taps = smooth_taps(radius, sigma)
    result = np.zeros(count)
    for source in range(count):
        for target in range(count):
            offset = target - source
            if abs(offset) <= radius:
                result[source] += taps[offset + radius]
    return result


def rounded(taps):
    best = None
    for factor in np.linspace(1.0, 2.0, 20001)[:-1]:
        near = (taps * factor).astype(np.float32).astype(ml_dtypes.bfloat16).astype(np.float64)
        error = np.abs(near / factor - taps).sum()
        if best is None or error < best[0]:
            best = (error, near, factor)
    return best[1], best[2]


def as_bfloat16(matrix):
    return matrix.astype(np.float32).astype(ml_dtypes.bfloat16)


def halves(matrix):
    high = as_bfloat16(matrix)
    return high, as_bfloat16(matrix - high.astype(np.float64))


def sizes(width, depth):
    columns = width // COARSE + 2 * HALO
    cells = depth // COARSE + BEFORE + AFTER
    return columns, cells


def product_rows(width):
    places = [*range(R1, width - R1)]
    places += [None] * max(EARLY - len(places), 0)
    places += [*range(R1 - EDGE, R1), *range(width - R1, width + EDGE - R1)]
    return places + [None] * (-len(places) % 16)


GRAD_TAPS = tuple(
    rounded(taps(R1, sigma_grad)) for taps in (smooth_taps, slope_taps)
)
GRAD_FACTOR = GRAD_TAPS[0][1] ** 2 * GRAD_TAPS[1][1]


def grad_taps(kind):
    return GRAD_TAPS[kind][0]


def tap(taps, offset):
    radius = (len(taps) - 1) // 2
    return float(taps[offset + radius]) if abs(offset) <= radius else 0.0


def x_bands(width):
    places = product_rows(width)
    bands = np.zeros((2, len(places), width + 2 * EDGE))
    for kind in range(2):
        for row, place in enumerate(places):
            if place is not None:
                first = place + EDGE - R1
                bands[kind, row, first : first + 2 * R1 + 1] = grad_taps(kind)
    return bands


def rim_bands(rows):
    bands = np.zeros((3, 3 * LANES, LANES))
    for part in range(3):
        row_taps, depth_taps = grad_taps(ROW_KINDS[part]), grad_taps(DEPTH_KINDS[part])
        for source in range(rows):
            for target in range(rows):
                row_tap = tap(row_taps, source - target)
                for near in range(-RIM, RIM):
                    lane = source * RIM + near % RIM
                    if near >= 0:
                        lane += rows * RIM + LANES
                    for place in range(-R1, R1):
                        value = row_tap * tap(depth_taps, near - place)
                        bands[part, lane, target * 2 * R1 + R1 + place] = value
    return bands


def rim_cells(rows, depth, blocks):
    taps = smooth_taps(R2, sigma_tensor)
    weights = product_weights(rows)
    bands = np.zeros((blocks - 1, LANES, blocks * depth // COARSE))
    for boundary in range(blocks - 1):
        middle = (boundary + 1) * depth
        for cell in range(bands.shape[2]):
            for voxel in range(cell * COARSE, (cell + 1) * COARSE):
                for place in range(-R1, R1):
                    value = tap(taps, middle + place - voxel)
                    for row in range(rows):
                        bands[boundary, row * 2 * R1 + R1 + place, cell] += weights[row] * value
    return bands.reshape(-1, bands.shape[2])


def meeting_order(blocks):
    middle = blocks // 2
    rest = [block for block in range(blocks) if block != middle]
    ends = [rest.pop(0 if turn % 2 == 0 else -1) for turn in range(blocks - 1)]
    return [middle, *ends]


def own_columns(count):
    products = (count + 2 * HALO) * COARSE + 2 * R2
    voxels = products + 2 * R1
    return -(-products // 16) * 16, -(-voxels // 8) * 8


def fold(voxels):
    return -(-voxels // 16) * 8


def rim_x_bands(count):
    products, voxels = own_columns(count)
    bands = np.zeros((2, products, -(-voxels // 16) * 16))
    valid = (count + 2 * HALO) * COARSE + 2 * R2
    for kind in range(2):
        for row in range(valid):
            bands[kind, row, row : row + 2 * R1 + 1] = grad_taps(kind)
    taps = smooth_taps(R2, sigma_tensor)
    coarse = np.zeros((16, products))
    for column in range(count + 2 * HALO):
        for voxel in range(column * COARSE, (column + 1) * COARSE):
            coarse[column, voxel : voxel + 2 * R2 + 1] += taps
    return bands.reshape(2 * products, -1), coarse


def depth_bands(depth):
    bands = np.zeros((2, depth, depth))
    for kind in range(2):
        for place in range(depth):
            for near in range(max(place - R1, 0), min(place + R1 + 1, depth)):
                bands[kind, near, place] = tap(grad_taps(kind), near - place)
    return bands


def product_weights(rows):
    return row_weights(rows, R2, sigma_tensor) / (255.0 * GRAD_FACTOR) ** 2


def coarse_depth_bands(depth):
    taps = smooth_taps(R2, sigma_tensor)
    columns, cells = sizes(0, depth)
    bands = np.zeros((depth, LANES))
    for cell in range(cells):
        for voxel in range(COARSE):
            place = (cell - BEFORE) * COARSE + voxel
            for near in range(max(place - R2, 0), min(place + R2 + 1, depth)):
                bands[near, cell] += tap(taps, near - place)
    return bands


def coarse_x_bands(width):
    taps = smooth_taps(R2, sigma_tensor)
    places = product_rows(width)
    columns, cells = sizes(width, 0)
    bands = np.zeros((-(-columns // 16) * 16, len(places)))
    for column in range(columns):
        for voxel in range(COARSE):
            middle = (column - HALO) * COARSE + voxel
            for row, place in enumerate(places):
                if place is not None:
                    bands[column, row] += tap(taps, place - middle)
    return bands


def stacked(*pieces):
    widest = max(piece.shape[1] for piece in pieces)
    padded = [np.pad(piece, ((0, 0), (0, widest - piece.shape[1]))) for piece in pieces]
    starts = np.cumsum([0] + [len(piece) for piece in pieces])
    return jnp.asarray(as_bfloat16(np.concatenate(padded))), tuple(int(start) for start in starts)


def two_parts(values):
    high = values.astype(jnp.bfloat16).astype(jnp.float32)
    return jnp.concatenate([high, (values - high).astype(jnp.bfloat16).astype(jnp.float32)], axis=0)


def joined(parts):
    half = parts.shape[0] // 2
    return parts[:half] + parts[half:]


def column_rows(temp, cure, at_end):
    count = temp.shape[0]
    first, second = (count - GHOST, count - GHOST + 1) if at_end else (0, 0)
    pad = jnp.zeros((8 - COLUMN_ROWS, temp.shape[1]), jnp.float32)
    return jnp.concatenate(
        [temp[first : first + GHOST, :], cure[second : second + GHOST - 1, :], pad], axis=0
    )


def chunk_rows(count, lanes):
    products, voxels = own_columns(count)
    held = count + 2 * HALO + 1 + COLUMN_ROWS * (lanes // LANES)
    return voxels + fold(voxels), -(-held // 8) * 8


def is_odd():
    return lax.rem(lax.axis_index("plane"), 2) == 1


def pack_kernel(
    intensity, temp_hbm, cure_hbm, x_hbm, z_hbm, far, near, own, x_parts, z_parts, temp, cure,
    grey, sems,
):
    rows, width, depth = intensity.shape
    copies = [
        pltpu.make_async_copy(intensity, grey, sems.at[0]),
        pltpu.make_async_copy(temp_hbm, temp, sems.at[1]),
        pltpu.make_async_copy(cure_hbm, cure, sems.at[2]),
        pltpu.make_async_copy(x_hbm, x_parts, sems.at[3]),
        pltpu.make_async_copy(z_hbm, z_parts, sems.at[4]),
    ]
    for copy in copies:
        copy.start()
    for copy in copies[:3]:
        copy.wait()
    odd = is_odd()
    sides = [
        two_parts(column_rows(temp, cure, at_end)).astype(jnp.bfloat16)
        for at_end in (False, True)
    ]

    def send(left, right):
        for place, target, columns in ((0, left, sides[0]), (width - EDGE, right, sides[1])):
            for pair in range(rows // 2):
                two = [grey[2 * pair + i, place : place + EDGE, :] for i in range(2)]
                two = jnp.concatenate(two, axis=0).astype(jnp.float32)
                target[2 * EDGE * pair : 2 * EDGE * (pair + 1), :] = two.astype(jnp.bfloat16)
            for slot in range(temp.shape[1] // LANES):
                at = rows * EDGE + 16 * slot
                target[at : at + 16, :] = columns[:, slot * LANES : (slot + 1) * LANES]

    @pl.when(odd)
    def _():
        send(near, far)

    @pl.when(jnp.logical_not(odd))
    def _():
        send(far, near)

    for row in range(rows):
        half = (row % 2) * depth
        own[row // 2, :, half : half + depth] = grey[row].astype(jnp.float32).astype(jnp.bfloat16)
    for copy in copies[3:]:
        copy.wait()


def packed_rows(values, size, first):
    depth = values[0].shape[1]
    lane = lax.broadcasted_iota(jnp.int32, values[0].shape, 1)
    packed = None
    for block, value in enumerate(values):
        shift = (size * block - first) % depth
        moved = value if shift == 0 else pltpu.roll(value, shift, 1)
        packed = moved if block == 0 else jnp.where(lane >= size * block, moved, packed)
    return packed


def edges_of(ref, rows):
    two = [
        ref[2 * EDGE * pair : 2 * EDGE * (pair + 1), :].astype(jnp.float32)
        for pair in range(rows // 2)
    ]
    voxels = [two[row // 2][row % 2 * EDGE : (row % 2 + 1) * EDGE] for row in range(rows)]
    slots = range(rows * EDGE, ref.shape[0], 16)
    columns = [joined(ref[at : at + 16, :].astype(jnp.float32)) for at in slots]
    return voxels, jnp.concatenate(columns, axis=1)


def product(first, second):
    return jnp.dot(first, second, preferred_element_type=jnp.float32)


def mirrored_filter(kind, values, even):
    rows = len(values)
    use_sum = even == (kind == 0)
    sign = 1.0 if use_sum else -1.0
    half = [values[row] + sign * values[rows - 1 - row] for row in range(rows // 2)]
    results = []
    for row in range(rows // 2):
        total = None
        for source, value in enumerate(half):
            near = tap(grad_taps(kind), source - row)
            far = tap(grad_taps(kind), rows - 1 - source - row)
            weight = 0.5 * (near + sign * far)
            total = weight * value if total is None else total + weight * value
        results.append(total)
    return results


def weighted_products(three, weight):
    pairs = ((0, 0), (1, 1), (2, 2), (0, 1), (0, 2), (1, 2))
    first = [weight * value for value in three]
    return [first[a] * three[b] for a, b in pairs]


def late_mask(count, width):
    row = lax.broadcasted_iota(jnp.int32, (count, LANES), 0)
    left = max(width - 2 * R1 - EARLY, 0)
    place = jnp.where(row < left + EDGE, row - left + R1 - EDGE, row - left - EDGE + width - R1)
    place = place + lax.axis_index("plane") * width
    inside = (place >= 0) & (place < lax.axis_size("plane") * width)
    return jnp.where(inside | (row < left), 1.0, 0.0)


USED = (0, 1, 2, 5)
UNUSED = (3, 4)


def all_sums(products, coarse, sx):
    sums = [None] * 6
    for kinds in (USED, UNUSED):
        tiles = [tile for index in kinds for tile in products[index]]
        along = product(sx, jnp.concatenate(tiles, axis=1)).astype(jnp.bfloat16)
        step = along.shape[1] // len(kinds)
        parts = [along[:, index * step : (index + 1) * step] for index in range(len(kinds))]
        total = product(jnp.concatenate(parts, axis=0), coarse)
        high = sx.shape[0]
        for index, kind in enumerate(kinds):
            sums[kind] = total[index * high : (index + 1) * high]
    return sums


def tensor_sums(across, sx, mask, diagonal, z_parts, filtered, grads):
    double = diagonal.shape[1]
    depth, pairs = double // 2, across.shape[1] // double
    rows, count = 2 * pairs, across.shape[0] // 2
    for start in range(0, count, 16):
        kinds = [
            [
                across[kind * count + start : kind * count + start + 16, row * depth : (row + 1) * depth]
                for row in range(rows)
            ]
            for kind in range(2)
        ]
        for part in range(3):
            values = kinds[X_KINDS[part]]
            results = mirrored_filter(ROW_KINDS[part], values, True)
            results += mirrored_filter(ROW_KINDS[part], values, False)
            for row, result in enumerate(results):
                at = (part * pairs + row // 2) * count + start
                lanes = slice((row % 2) * depth, (row % 2 + 1) * depth)
                filtered[at : at + 16, lanes] = result.astype(jnp.bfloat16)

    at = 2 * pairs * count
    grads[:at] = product(filtered[:at, :], diagonal[0:double, :])
    grads[at:] = product(filtered[at:, :], diagonal[double : 2 * double, :])

    weights = product_weights(rows)
    layer = lax.axis_index("depth")
    first, last = layer == 0, layer == lax.axis_size("depth") - 1
    place = lax.broadcasted_iota(jnp.int32, (16, depth), 1)
    complete = ((place >= R1) | first) & ((place < depth - R1) | last)
    complete = jnp.where(complete, 1.0, 0.0)
    groups = [[] for _ in range(6)]
    for start in range(0, count, 16):
        inside = complete if mask is None else complete * mask[start : start + 16]
        totals = None
        for row in range(rows):
            lanes = slice((row % 2) * depth, (row % 2 + 1) * depth)
            three = []
            for part in range(3):
                at = (part * pairs + row // 2) * count + start
                three.append(grads[at : at + 16, lanes])
            terms = weighted_products(three, 2.0 * float(weights[row % (rows // 2)]))
            totals = terms if row == 0 else [a + b for a, b in zip(totals, terms)]
        for index in range(6):
            groups[index].append((totals[index] * inside).astype(jnp.bfloat16))
    products = [[jnp.concatenate(group, axis=0)] for group in groups]
    return all_sums(products, z_parts[double : double + depth, :], sx)


def rim_tiles(values):
    rows, depth = len(values), values[0].shape[1]
    below = packed_rows(values, RIM, depth - RIM)
    above = pltpu.roll(packed_rows(values, RIM, 0), rows * RIM, 1)
    lane = lax.broadcasted_iota(jnp.int32, below.shape, 1)
    return [jnp.where(lane < rows * RIM, below, above), above, pltpu.roll(above, HALF, 1)]


def early_kernel(
    starts, own, x_parts, z_parts, late_hbm, sums, diagonal, sides, tiles, x_late, across,
    filtered, grads, sem,
):
    copy = pltpu.make_async_copy(late_hbm, x_late, sem.at[0])
    copy.start()
    pairs, width, double = own.shape
    rows, depth = 2 * pairs, double // 2
    empty = jnp.zeros((depth, depth), jnp.bfloat16)
    for kind in range(2):
        for half in range(2):
            at = pl.ds(kind * double + half * depth, depth)
            band = z_parts[kind * depth : (kind + 1) * depth, :]
            diagonal[at, half * depth : (half + 1) * depth] = band
            diagonal[at, (1 - half) * depth : (2 - half) * depth] = empty
    whole = jnp.concatenate([own[pair] for pair in range(pairs)], axis=1)
    result = product(x_parts[starts[0] : starts[2], :width], whole)
    across[...] = result[: starts[1]]
    sides[...] = result[starts[1] :]
    sx = x_parts[starts[2] : starts[3], :EARLY]
    results = tensor_sums(across, sx, None, diagonal, z_parts, filtered, grads)
    for index, kind in enumerate(USED):
        sums[index] = results[kind]
    values = [
        own[row // 2, :, (row % 2) * depth : (row % 2 + 1) * depth].astype(jnp.float32)
        for row in range(rows)
    ]
    for index, tile in enumerate(rim_tiles(values)):
        tiles[index] = tile
    copy.wait()


def late_kernel(
    starts, width, far, near, x_late, z_parts, diagonal, early_sums, sides, own_tiles, temp, cure,
    flat_hbm, steep_hbm, cells_hbm, out_hbm, flat, steep, cell_bands, across, filtered, grads,
    out, sems,
):
    constants = [
        pltpu.make_async_copy(source, target, sems.at[2 + index])
        for index, (source, target) in enumerate(
            ((flat_hbm, flat), (steep_hbm, steep), (cells_hbm, cell_bands))
        )
    ]
    for copy in constants:
        copy.start()
    double = diagonal.shape[1]
    depth = double // 2
    rows = across.shape[1] // depth
    count, lanes = temp.shape
    odd = is_odd()
    depths, layer = lax.axis_size("depth"), lax.axis_index("depth")
    outer, outer_columns = edges_of(far, rows)
    inner, inner_columns = edges_of(near, rows)
    values = []
    for row in range(rows):
        left = jnp.where(odd, inner[row], outer[row])
        right = jnp.where(odd, outer[row], inner[row])
        values.append(jnp.concatenate([left, right], axis=0))
    left = jnp.where(odd, inner_columns, outer_columns)
    right = jnp.where(odd, outer_columns, inner_columns)

    late = across.shape[0] // 2
    halos = jnp.concatenate([value.astype(jnp.bfloat16) for value in values], axis=1)
    across[...] = sides[...] + product(x_late[starts[0] : starts[1], : 2 * EDGE], halos)

    products_x, voxels = own_columns(count)
    folded, stride = fold(voxels), COARSE * count
    tiles = [
        jnp.concatenate([tile[:EDGE], own_tiles[index], tile[EDGE:]], axis=0)
        for index, tile in enumerate(rim_tiles(values))
    ]
    missing = stride * (depths - 1) + voxels - tiles[0].shape[0]
    if missing > 0:
        spare = jnp.zeros((-(-missing // 8) * 8, LANES), jnp.float32)
        tiles = [jnp.concatenate([tile, spare], axis=0) for tile in tiles]

    height = count + 2 * HALO
    half_lane = lax.broadcasted_iota(jnp.int32, (folded, LANES), 1) < HALF
    order = meeting_order(out.shape[0])
    for position, target in enumerate(order):
        at = stride * target
        second = jnp.where(
            half_lane,
            tiles[1][at : at + folded],
            tiles[2][at + voxels - folded : at + voxels],
        )
        rims = jnp.concatenate([tiles[0][at : at + voxels], second], axis=0)
        out[position, 0 : voxels + folded, :] = rims.astype(jnp.bfloat16)
    split = (pl.ds(0, voxels + folded), pl.ds(voxels + folded, out.shape[1] - voxels - folded))
    copies = [
        pltpu.make_async_copy(out.at[:, part, :], out_hbm.at[:, part, :], sems.at[index])
        for index, part in enumerate(split)
    ]
    copies[0].start()

    sx = x_late[starts[1] : starts[2], :late]
    results = tensor_sums(
        across, sx, late_mask(late, width), diagonal, z_parts, filtered, grads
    )
    yy, xx, zz, xz = [early_sums[index] + results[kind] for index, kind in enumerate(USED)]
    trace = yy + xx + zz
    lane = lax.broadcasted_iota(jnp.int32, trace.shape, 1)
    columns, cells = sizes(width, depth)
    tail = 4 * cells - LANES
    joint = pltpu.roll(xz, 3 * cells, 1)
    rest = jnp.where(lane < tail, joint, 0.0)
    rest = pltpu.roll(rest, 0, 1, stride=tail, stride_axis=0)
    for index, part in ((2, zz), (1, xx), (0, trace)):
        moved = part if index == 0 else pltpu.roll(part, index * cells, 1)
        joint = jnp.where(lane < (index + 1) * cells, moved, joint)

    own_first, own_last = column_rows(temp, cure, False), column_rows(temp, cure, True)
    half = chunk_rows(count, lanes)[1]
    for position, target in enumerate(order):
        piece = jnp.where(layer == target - 1, own_last, 0.0)
        piece = jnp.where(layer == target + 1, own_first, piece)
        if target == 0:
            piece = jnp.where(layer == depths - 1, left, piece)
        if target == out.shape[0] - 1:
            piece = jnp.where(layer == 0, right, piece)
        mine = slice(count * target, count * target + height)
        pieces = [joint[mine], jnp.sum(rest[mine], axis=0, keepdims=True)]
        for slot in range(lanes // LANES):
            pieces.append(piece[0:COLUMN_ROWS, slot * LANES : (slot + 1) * LANES])
        filled = sum(part.shape[0] for part in pieces)
        if filled < half:
            pieces.append(jnp.zeros((half - filled, LANES), jnp.float32))
        sent = two_parts(jnp.concatenate(pieces, axis=0))
        out[position, voxels + folded :, :] = sent.astype(jnp.bfloat16)
    copies[1].start()
    for copy in copies + constants:
        copy.wait()


def rim_sums(chunks, count, starts, flat, steep, cells):
    parts = chunks.shape[0]
    rows_x, voxels = own_columns(count)
    folded = fold(voxels)
    tall = -(-voxels // 16) * 16
    spare = [jnp.zeros((tall - voxels, LANES), jnp.float32)] if tall > voxels else []
    tiles = []
    order = meeting_order(parts)
    for part in range(parts):
        rims = chunks[order.index(part), 0 : voxels + folded, :].astype(jnp.float32)
        second = rims[voxels:]
        second = [second[: voxels - folded], pltpu.roll(second, HALF, 1)]
        for tile in ([rims[:voxels]], second):
            tiles.append(jnp.concatenate(tile + spare, axis=0).astype(jnp.bfloat16))
    result = product(
        steep[starts[1] : starts[2], :tall], jnp.concatenate(tiles, axis=1)
    ).astype(jnp.bfloat16)
    kinds = []
    for kind in range(2):
        values = result[kind * rows_x : (kind + 1) * rows_x]
        tile = lambda index: values[:, index * LANES : (index + 1) * LANES]
        stack = [
            jnp.concatenate([tile(2 * part), tile(2 * part + 2), tile(2 * part + 3)], axis=1)
            for part in range(parts - 1)
        ]
        kinds.append(jnp.concatenate(stack, axis=0))
    both = product(kinds[0], flat[...])
    three = (both[:, :LANES], product(kinds[1], steep[starts[0] : starts[1], :]), both[:, LANES:])

    index = lax.axis_index("plane") * lax.axis_size("depth") + lax.axis_index("depth")
    total = lax.axis_size("plane") * lax.axis_size("depth") * count * COARSE
    place = lax.rem(lax.broadcasted_iota(jnp.int32, three[0].shape, 0), rows_x)
    place = place + (index * count - HALO) * COARSE - R2
    inside = jnp.where((place >= 0) & (place < total), 1.0, 0.0)
    products = [
        [
            term[part * rows_x : (part + 1) * rows_x].astype(jnp.bfloat16)
            for part in range(parts - 1)
        ]
        for term in weighted_products(three, inside)
    ]
    return all_sums(products, cells[...], steep[starts[2] : starts[3], :rows_x])


def cure_kernel(
    cells, starts, chunks, temp_in, cure_in, tools, flat, steep, rim_bands, temp_hbm, cure_hbm,
    conduct_hbm, temp_out, cure_out, conduct_out, sems,
):
    count, lanes = temp_in.shape
    parts = chunks.shape[0]
    planes, depths = lax.axis_size("plane"), lax.axis_size("depth")
    plane, layer = lax.axis_index("plane"), lax.axis_index("depth")
    height = count + 2 * HALO
    own = cells - BEFORE - AFTER
    lane = lax.broadcasted_iota(jnp.int32, (16, lanes), 1)
    row = lax.broadcasted_iota(jnp.int32, (16, lanes), 0)
    at_sums, half = chunk_rows(count, lanes)
    tail = 4 * cells - LANES
    narrow_lane = lax.broadcasted_iota(jnp.int32, (16, LANES), 1)
    order = meeting_order(parts)

    near = rim_sums(chunks, count, starts, flat, steep, rim_bands)
    sums = [near[0] + near[1] + near[2], near[1], near[2], near[5]]
    blocks = [
        joined(chunks[order.index(part), at_sums:, :].astype(jnp.float32)) for part in range(parts)
    ]
    tails = [block[height : height + 1] for block in blocks]
    if parts % 8:
        tails.append(jnp.zeros((-parts % 8, LANES), jnp.float32))
    tails = jnp.concatenate(tails, axis=0)
    tails = pltpu.roll(tails, lax.rem(LANES - lax.rem(tail * count * layer, LANES), LANES), 1)
    narrow_row = lax.broadcasted_iota(jnp.int32, (16, LANES), 0)
    rests = [jnp.zeros((16, LANES), jnp.float32) for _ in range(parts)]
    for column in range(height):
        moved = pltpu.roll(tails, LANES - tail * column, 1) if column else tails
        for part in range(parts):
            rests[part] = jnp.where(narrow_row == column, moved[part : part + 1], rests[part])
    for part in range(parts):
        first_cell = own * part - BEFORE
        here = (lane >= first_cell) & (lane < first_cell + cells)
        values = blocks[part]
        joint = values[0:16]
        xz = pltpu.roll(jnp.where(narrow_lane < tail, rests[part], joint), LANES - 3 * cells, 1)
        for index in range(4):
            chunk = xz if index == 3 else joint
            if lanes > LANES:
                spare = jnp.zeros((16, lanes - LANES), jnp.float32)
                chunk = jnp.concatenate([chunk, spare], axis=1)
            shift = (first_cell - (index % 3) * cells) % lanes
            moved = chunk if shift == 0 else pltpu.roll(chunk, shift, 1)
            sums[index] = sums[index] + jnp.where(here, moved, 0.0)
    trace = sums[0]
    scale = (conduct_fiber - conduct_matrix) / (2.0 * trace + tensor_eps)
    conduct = [
        conduct_matrix + scale * (trace - sums[1]),
        -scale * sums[3],
        conduct_matrix + scale * (trace - sums[2]),
    ]
    for kind in range(3):
        conduct_out[kind] = conduct[kind][HALO : HALO + count]
    copies = [
        pltpu.make_async_copy(conduct_out, conduct_hbm, sems.at[0]),
        pltpu.make_async_copy(temp_out, temp_hbm, sems.at[1]),
        pltpu.make_async_copy(cure_out, cure_hbm, sems.at[2]),
    ]
    copies[0].start()

    slots = range(height + 1, height + 1 + COLUMN_ROWS * (lanes // LANES), COLUMN_ROWS)
    columns = [
        jnp.concatenate([values[at : at + COLUMN_ROWS] for at in slots], axis=1) for values in blocks
    ]
    before, after = columns[parts - 1], columns[0]
    for part in range(parts - 1):
        before = jnp.where(layer == part + 1, columns[part], before)
        after = jnp.where(layer == part, columns[part + 1], after)
    spare = jnp.full((16 - count - 2 * GHOST, lanes), 0.5, jnp.float32)
    temp = jnp.concatenate([before[:GHOST], temp_in[...], after[:GHOST], 8.0 * spare], axis=0)
    cure = jnp.concatenate([spare[:1], before[GHOST:], cure_in[...], after[GHOST:], spare[:1], spare], axis=0)
    gap = GHOST - HALO
    xx, xz, zz = [pltpu.roll(part, gap, 0) for part in conduct]

    first = (plane == 0) & (layer == 0)
    last = (plane == planes - 1) & (layer == depths - 1)
    for step in range(STEPS):
        top, bottom = tools[2 * step : 2 * step + 1, :], tools[2 * step + 1 : 2 * step + 2, :]
        temp = jnp.where((row < GHOST) & first, temp[GHOST : GHOST + 1], temp)
        temp = jnp.where(
            (row >= GHOST + count) & last, temp[GHOST + count - 1 : GHOST + count], temp
        )
        cooler = jnp.where(lane == 0, top, pltpu.roll(temp, 1, 1))
        later = jnp.where(lane == lanes - 1, bottom, pltpu.roll(temp, lanes - 1, 1))
        slant = later - cooler
        second_x = pltpu.roll(temp, 15, 0) - 2.0 * temp + pltpu.roll(temp, 1, 0)
        second_z = later - 2.0 * temp + cooler
        cross = 0.25 * (pltpu.roll(slant, 15, 0) - pltpu.roll(slant, 1, 0))
        spread = xx * second_x + 2.0 * xz * cross + zz * second_z
        inverse = 1.0 / reference_temp - 1.0 / temp
        left = 1.0 - cure
        rate = rate_first * jnp.exp(energy_first * inverse) + rate_second * jnp.exp(
            energy_second * inverse
        ) * jnp.sqrt(cure)
        rate = rate * (left * jnp.sqrt(left))
        temp = temp + time_step * (spread + heat_release * rate)
        cure = cure + time_step * rate
    temp_out[...] = temp[GHOST : GHOST + count]
    cure_out[...] = cure[GHOST : GHOST + count]
    for copy in copies[1:]:
        copy.start()
    for copy in copies:
        copy.wait()


def on_device(intensity, temp_start, cure_start, tool_levels, plan):
    rows, width, depth = intensity.shape
    count, lanes = temp_start.shape
    planes, depths = lax.axis_size("plane"), lax.axis_size("depth")
    columns, cells = sizes(width, depth)
    bf16 = jnp.bfloat16
    slots = rows * EDGE + 16 * (lanes // LANES)
    params = pltpu.CompilerParams(vmem_limit_bytes=24 * 1024 * 1024)
    vmem = pl.BlockSpec(memory_space=pltpu.VMEM)
    stay = pl.BlockSpec(memory_space=pltpu.HBM)

    fixed = lambda values: pltpu.with_memory_space_constraint(values, pltpu.HBM)
    bands, coarse = x_bands(width), coarse_x_bands(width)
    late = bands.shape[1] - EARLY
    middle = bands[:, :EARLY, EDGE : EDGE + width]
    sides = bands[:, EARLY:].reshape(2 * late, -1)
    x_hbm, early_starts = stacked(
        middle.reshape(2 * EARLY, -1), sides[:, EDGE : EDGE + width], coarse[:, :EARLY]
    )
    z_hbm, _ = stacked(*depth_bands(depth), coarse_depth_bands(depth))
    halos = np.concatenate([sides[:, :EDGE], sides[:, EDGE + width :]], axis=1)
    x_late, late_starts = stacked(halos, coarse[:, EARLY:])
    rims = rim_bands(rows)
    flat, _ = stacked(np.concatenate([rims[0], rims[2]], axis=1))
    steep, rim_starts = stacked(rims[1], *rim_x_bands(count))
    cell_bands, _ = stacked(rim_cells(rows, depth, depths))
    constants = (flat, steep, cell_bands)
    far, near, own, x_parts, z_parts, temp, cure = pl.pallas_call(
        pack_kernel,
        name="pack",
        out_shape=(
            pltpu.VMEM((slots, depth), bf16),
            pltpu.VMEM((slots, depth), bf16),
            pltpu.VMEM((rows // 2, width, 2 * depth), bf16),
            pltpu.VMEM(x_hbm.shape, bf16),
            pltpu.VMEM(z_hbm.shape, bf16),
            pltpu.VMEM((count, lanes), jnp.float32),
            pltpu.VMEM((count, lanes), jnp.float32),
        ),
        in_specs=[stay] * 5,
        scratch_shapes=[
            pltpu.VMEM((rows, width, depth), jnp.int32),
            pltpu.SemaphoreType.DMA((5,)),
        ],
        compiler_params=params,
    )(*[fixed(values) for values in (intensity, temp_start, cure_start, x_hbm, z_hbm)])

    def moved(values, pairs):
        index = [(p * depths + d, q * depths + e) for (p, d), (q, e) in pairs]
        return lax.ppermute(values, ("plane", "depth"), index)

    def swapped(values, first):
        pairs = [(p, p + 1) for p in range(first, planes - 1, 2)]
        pairs += [(q, p) for p, q in pairs]
        return moved(values, [((p, d), (q, d)) for p, q in pairs for d in range(depths)])

    far = swapped(far, 1)
    near = swapped(near, 0)

    high = coarse.shape[0]

    def scratch(count):
        return [
            pltpu.VMEM((2 * count, rows * depth), jnp.float32),
            pltpu.VMEM((3 * rows // 2 * count, 2 * depth), bf16),
            pltpu.VMEM((3 * rows // 2 * count, 2 * depth), jnp.float32),
        ]

    def cost(count):
        return pl.CostEstimate(
            flops=2 * rows * (2 * count) * 160 * depth * 4,
            bytes_accessed=4_000_000,
            transcendentals=0,
        )

    early_sums, diagonal, sides, own_tiles, x_late = pl.pallas_call(
        functools.partial(early_kernel, early_starts),
        name="early",
        out_shape=(
            pltpu.VMEM((len(USED), high, LANES), jnp.float32),
            pltpu.VMEM((4 * depth, 2 * depth), bf16),
            pltpu.VMEM((2 * late, rows * depth), jnp.float32),
            pltpu.VMEM((3, width, LANES), jnp.float32),
            pltpu.VMEM(x_late.shape, bf16),
        ),
        in_specs=[vmem] * 3 + [stay],
        scratch_shapes=scratch(EARLY) + [pltpu.SemaphoreType.DMA((1,))],
        cost_estimate=cost(EARLY),
        compiler_params=params,
    )(own, x_parts, z_parts, fixed(x_late))

    products_x, voxels = own_columns(count)
    at_sums, half = chunk_rows(count, lanes)
    chunk_shape = (depths, at_sums + 2 * half, LANES)
    chunks, flat, steep, cell_bands = pl.pallas_call(
        functools.partial(late_kernel, late_starts, width),
        name="late",
        out_shape=(
            pltpu.HBM(chunk_shape, bf16),
            *[pltpu.VMEM(values.shape, bf16) for values in constants],
        ),
        in_specs=[vmem] * 10 + [stay] * 3,
        out_specs=(stay, vmem, vmem, vmem),
        scratch_shapes=scratch(late)
        + [pltpu.VMEM(chunk_shape, bf16), pltpu.SemaphoreType.DMA((5,))],
        cost_estimate=cost(late),
        compiler_params=params,
    )(
        far, near, x_late, z_parts, diagonal, early_sums, sides, own_tiles, temp, cure,
        *[fixed(values) for values in constants],
    )

    faces = plan.reshape(2 * STEPS, 1) == jnp.arange(tool_levels.shape[0], dtype=jnp.int32)
    tools = jnp.sum(
        jnp.where(faces, tool_levels, jnp.zeros_like(tool_levels)), axis=1, keepdims=True
    )

    chunks = lax.all_to_all(
        chunks,
        "depth",
        split_axis=0,
        concat_axis=0,
        tiled=True,
        axis_index_groups=[meeting_order(depths)],
    )

    return pl.pallas_call(
        functools.partial(cure_kernel, cells, rim_starts),
        name="cure",
        out_shape=(
            pltpu.HBM((count, lanes), jnp.float32),
            pltpu.HBM((count, lanes), jnp.float32),
            pltpu.HBM((3, count, lanes), jnp.float32),
        ),
        in_specs=[vmem] * 7,
        out_specs=(stay, stay, stay),
        scratch_shapes=[
            pltpu.VMEM((count, lanes), jnp.float32),
            pltpu.VMEM((count, lanes), jnp.float32),
            pltpu.VMEM((3, count, lanes), jnp.float32),
            pltpu.SemaphoreType.DMA((3,)),
        ],
        compiler_params=params,
    )(chunks, temp, cure, tools, flat, steep, cell_bands)


def solution(mesh):
    return jax.shard_map(
        on_device,
        mesh=mesh,
        in_specs=(
            P(None, "plane", "depth"),
            P(("plane", "depth"), None),
            P(("plane", "depth"), None),
            P(),
            P(),
        ),
        out_specs=(
            P(("plane", "depth"), None),
            P(("plane", "depth"), None),
            P(None, ("plane", "depth"), None),
        ),
        check_vma=False,
    )
```

```python
import functools

import jax
import jax.numpy as jnp
import ml_dtypes
import numpy as np
from jax import lax
from jax.experimental import pallas as pl
from jax.experimental.pallas import tpu as pltpu
from jax.sharding import PartitionSpec as P

ROWS = 8
R1 = 6
R2 = 10
COARSE = 4
STEPS = 3

sigma_grad = 2.0
sigma_tensor = 3.3
conduct_matrix = 0.3
conduct_fiber = 1.5
time_step = 0.25
heat_release = 0.4
rate_first = 0.15
rate_second = 0.6
energy_first = 30.0
energy_second = 25.0
reference_temp = 4.2
tensor_eps = 1e-06

LANES = 128
HALO = 2
EDGE = HALO * COARSE + R1 + R2
EARLY = 96
GHOST = 3
COLUMN_ROWS = 2 * GHOST - 1
RIM = 2 * R1
BEFORE = -(-(R2 - R1) // COARSE)
AFTER = BEFORE
HALF = LANES // 2
ROW_KINDS = (1, 0, 0)
X_KINDS = (0, 1, 0)
DEPTH_KINDS = (0, 0, 1)


def smooth_taps(radius, sigma):
    offsets = np.arange(-radius, radius + 1) * 1.0
    weights = np.exp(-0.5 * offsets * offsets / (sigma * sigma))
    return weights / weights.sum()


def slope_taps(radius, sigma):
    offsets = np.arange(-radius, radius + 1) * 1.0
    weights = np.exp(-0.5 * offsets * offsets / (sigma * sigma))
    return offsets * weights / np.sum(offsets * offsets * weights)


def row_weights(count, radius, sigma):
    taps = smooth_taps(radius, sigma)
    result = np.zeros(count)
    for source in range(count):
        for target in range(count):
            offset = target - source
            if abs(offset) <= radius:
                result[source] += taps[offset + radius]
    return result


def rounded(taps):
    best = None
    for factor in np.linspace(1.0, 2.0, 20001)[:-1]:
        near = (taps * factor).astype(np.float32).astype(ml_dtypes.bfloat16).astype(np.float64)
        error = np.abs(near / factor - taps).sum()
        if best is None or error < best[0]:
            best = (error, near, factor)
    return best[1], best[2]


def as_bfloat16(matrix):
    return matrix.astype(np.float32).astype(ml_dtypes.bfloat16)


def halves(matrix):
    high = as_bfloat16(matrix)
    return high, as_bfloat16(matrix - high.astype(np.float64))


def sizes(width, depth):
    columns = width // COARSE + 2 * HALO
    cells = depth // COARSE + BEFORE + AFTER
    return columns, cells


def product_rows(width):
    places = [*range(R1, width - R1)]
    places += [None] * max(EARLY - len(places), 0)
    places += [*range(R1 - EDGE, R1), *range(width - R1, width + EDGE - R1)]
    return places + [None] * (-len(places) % 16)


GRAD_TAPS = tuple(
    rounded(taps(R1, sigma_grad)) for taps in (smooth_taps, slope_taps)
)
GRAD_FACTOR = GRAD_TAPS[0][1] ** 2 * GRAD_TAPS[1][1]


def grad_taps(kind):
    return GRAD_TAPS[kind][0]


def tap(taps, offset):
    radius = (len(taps) - 1) // 2
    return float(taps[offset + radius]) if abs(offset) <= radius else 0.0


def x_bands(width):
    places = product_rows(width)
    bands = np.zeros((2, len(places), width + 2 * EDGE))
    for kind in range(2):
        for row, place in enumerate(places):
            if place is not None:
                first = place + EDGE - R1
                bands[kind, row, first : first + 2 * R1 + 1] = grad_taps(kind)
    return bands


def rim_bands(rows):
    bands = np.zeros((3, 3 * LANES, LANES))
    for part in range(3):
        row_taps, depth_taps = grad_taps(ROW_KINDS[part]), grad_taps(DEPTH_KINDS[part])
        for source in range(rows):
            for target in range(rows):
                row_tap = tap(row_taps, source - target)
                for near in range(-RIM, RIM):
                    lane = source * RIM + near % RIM
                    if near >= 0:
                        lane += rows * RIM + LANES
                    for place in range(-R1, R1):
                        value = row_tap * tap(depth_taps, near - place)
                        bands[part, lane, target * 2 * R1 + R1 + place] = value
    return bands


def rim_cells(rows, depth, blocks):
    taps = smooth_taps(R2, sigma_tensor)
    weights = product_weights(rows)
    bands = np.zeros((blocks - 1, LANES, blocks * depth // COARSE))
    for boundary in range(blocks - 1):
        middle = (boundary + 1) * depth
        for cell in range(bands.shape[2]):
            for voxel in range(cell * COARSE, (cell + 1) * COARSE):
                for place in range(-R1, R1):
                    value = tap(taps, middle + place - voxel)
                    for row in range(rows):
                        bands[boundary, row * 2 * R1 + R1 + place, cell] += weights[row] * value
    return bands.reshape(-1, bands.shape[2])


def meeting_order(blocks):
    middle = blocks // 2
    rest = [block for block in range(blocks) if block != middle]
    ends = [rest.pop(0 if turn % 2 == 0 else -1) for turn in range(blocks - 1)]
    return [middle, *ends]


def own_columns(count):
    products = (count + 2 * HALO) * COARSE + 2 * R2
    voxels = products + 2 * R1
    return -(-products // 16) * 16, -(-voxels // 8) * 8


def fold(voxels):
    return -(-voxels // 16) * 8


def rim_x_bands(count):
    products, voxels = own_columns(count)
    bands = np.zeros((2, products, -(-voxels // 16) * 16))
    valid = (count + 2 * HALO) * COARSE + 2 * R2
    for kind in range(2):
        for row in range(valid):
            bands[kind, row, row : row + 2 * R1 + 1] = grad_taps(kind)
    taps = smooth_taps(R2, sigma_tensor)
    coarse = np.zeros((16, products))
    for column in range(count + 2 * HALO):
        for voxel in range(column * COARSE, (column + 1) * COARSE):
            coarse[column, voxel : voxel + 2 * R2 + 1] += taps
    return bands.reshape(2 * products, -1), coarse


def depth_bands(depth):
    bands = np.zeros((2, depth, depth))
    for kind in range(2):
        for place in range(depth):
            for near in range(max(place - R1, 0), min(place + R1 + 1, depth)):
                bands[kind, near, place] = tap(grad_taps(kind), near - place)
    return bands


def product_weights(rows):
    return row_weights(rows, R2, sigma_tensor) / (255.0 * GRAD_FACTOR) ** 2


def coarse_depth_bands(depth):
    taps = smooth_taps(R2, sigma_tensor)
    columns, cells = sizes(0, depth)
    bands = np.zeros((depth, LANES))
    for cell in range(cells):
        for voxel in range(COARSE):
            place = (cell - BEFORE) * COARSE + voxel
            for near in range(max(place - R2, 0), min(place + R2 + 1, depth)):
                bands[near, cell] += tap(taps, near - place)
    return bands


def coarse_x_bands(width):
    taps = smooth_taps(R2, sigma_tensor)
    places = product_rows(width)
    columns, cells = sizes(width, 0)
    bands = np.zeros((-(-columns // 16) * 16, len(places)))
    for column in range(columns):
        for voxel in range(COARSE):
            middle = (column - HALO) * COARSE + voxel
            for row, place in enumerate(places):
                if place is not None:
                    bands[column, row] += tap(taps, place - middle)
    return bands


def stacked(*pieces):
    widest = max(piece.shape[1] for piece in pieces)
    padded = [np.pad(piece, ((0, 0), (0, widest - piece.shape[1]))) for piece in pieces]
    starts = np.cumsum([0] + [len(piece) for piece in pieces])
    return jnp.asarray(as_bfloat16(np.concatenate(padded))), tuple(int(start) for start in starts)


def two_parts(values):
    high = values.astype(jnp.bfloat16).astype(jnp.float32)
    return jnp.concatenate([high, (values - high).astype(jnp.bfloat16).astype(jnp.float32)], axis=0)


def joined(parts):
    half = parts.shape[0] // 2
    return parts[:half] + parts[half:]


def column_rows(temp, cure, at_end):
    count = temp.shape[0]
    first, second = (count - GHOST, count - GHOST + 1) if at_end else (0, 0)
    pad = jnp.zeros((8 - COLUMN_ROWS, temp.shape[1]), jnp.float32)
    return jnp.concatenate(
        [temp[first : first + GHOST, :], cure[second : second + GHOST - 1, :], pad], axis=0
    )


def chunk_rows(count, lanes):
    products, voxels = own_columns(count)
    held = count + 2 * HALO + 1 + COLUMN_ROWS * (lanes // LANES)
    return voxels + fold(voxels), -(-held // 8) * 8


def is_odd():
    return lax.rem(lax.axis_index("plane"), 2) == 1


def pack_kernel(
    intensity, temp_hbm, cure_hbm, x_hbm, z_hbm, far, near, own, x_parts, z_parts, temp, cure,
    grey, sems,
):
    rows, width, depth = intensity.shape
    copies = [
        pltpu.make_async_copy(intensity, grey, sems.at[0]),
        pltpu.make_async_copy(temp_hbm, temp, sems.at[1]),
        pltpu.make_async_copy(cure_hbm, cure, sems.at[2]),
        pltpu.make_async_copy(x_hbm, x_parts, sems.at[3]),
        pltpu.make_async_copy(z_hbm, z_parts, sems.at[4]),
    ]
    for copy in copies:
        copy.start()
    for copy in copies[:3]:
        copy.wait()
    odd = is_odd()
    sides = [
        two_parts(column_rows(temp, cure, at_end)).astype(jnp.bfloat16)
        for at_end in (False, True)
    ]

    def send(left, right):
        for place, target, columns in ((0, left, sides[0]), (width - EDGE, right, sides[1])):
            for pair in range(rows // 2):
                two = [grey[2 * pair + i, place : place + EDGE, :] for i in range(2)]
                two = jnp.concatenate(two, axis=0).astype(jnp.float32)
                target[2 * EDGE * pair : 2 * EDGE * (pair + 1), :] = two.astype(jnp.bfloat16)
            for slot in range(temp.shape[1] // LANES):
                at = rows * EDGE + 16 * slot
                target[at : at + 16, :] = columns[:, slot * LANES : (slot + 1) * LANES]

    @pl.when(odd)
    def _():
        send(near, far)

    @pl.when(jnp.logical_not(odd))
    def _():
        send(far, near)

    for row in range(rows):
        half = (row % 2) * depth
        own[row // 2, :, half : half + depth] = grey[row].astype(jnp.float32).astype(jnp.bfloat16)
    for copy in copies[3:]:
        copy.wait()


def packed_rows(values, size, first):
    depth = values[0].shape[1]
    lane = lax.broadcasted_iota(jnp.int32, values[0].shape, 1)
    packed = None
    for block, value in enumerate(values):
        shift = (size * block - first) % depth
        moved = value if shift == 0 else pltpu.roll(value, shift, 1)
        packed = moved if block == 0 else jnp.where(lane >= size * block, moved, packed)
    return packed


def edges_of(ref, rows):
    two = [
        ref[2 * EDGE * pair : 2 * EDGE * (pair + 1), :].astype(jnp.float32)
        for pair in range(rows // 2)
    ]
    voxels = [two[row // 2][row % 2 * EDGE : (row % 2 + 1) * EDGE] for row in range(rows)]
    slots = range(rows * EDGE, ref.shape[0], 16)
    columns = [joined(ref[at : at + 16, :].astype(jnp.float32)) for at in slots]
    return voxels, jnp.concatenate(columns, axis=1)


def product(first, second):
    return jnp.dot(first, second, preferred_element_type=jnp.float32)


def mirrored_filter(kind, values, even):
    rows = len(values)
    use_sum = even == (kind == 0)
    sign = 1.0 if use_sum else -1.0
    half = [values[row] + sign * values[rows - 1 - row] for row in range(rows // 2)]
    results = []
    for row in range(rows // 2):
        total = None
        for source, value in enumerate(half):
            near = tap(grad_taps(kind), source - row)
            far = tap(grad_taps(kind), rows - 1 - source - row)
            weight = 0.5 * (near + sign * far)
            total = weight * value if total is None else total + weight * value
        results.append(total)
    return results


def weighted_products(three, weight):
    pairs = ((0, 0), (1, 1), (2, 2), (0, 1), (0, 2), (1, 2))
    first = [weight * value for value in three]
    return [first[a] * three[b] for a, b in pairs]


def late_mask(count, width):
    row = lax.broadcasted_iota(jnp.int32, (count, LANES), 0)
    left = max(width - 2 * R1 - EARLY, 0)
    place = jnp.where(row < left + EDGE, row - left + R1 - EDGE, row - left - EDGE + width - R1)
    place = place + lax.axis_index("plane") * width
    inside = (place >= 0) & (place < lax.axis_size("plane") * width)
    return jnp.where(inside | (row < left), 1.0, 0.0)


USED = (0, 1, 2, 5)
UNUSED = (3, 4)


def all_sums(products, coarse, sx):
    sums = [None] * 6
    for kinds in (USED, UNUSED):
        tiles = [tile for index in kinds for tile in products[index]]
        along = product(sx, jnp.concatenate(tiles, axis=1)).astype(jnp.bfloat16)
        step = along.shape[1] // len(kinds)
        parts = [along[:, index * step : (index + 1) * step] for index in range(len(kinds))]
        total = product(jnp.concatenate(parts, axis=0), coarse)
        high = sx.shape[0]
        for index, kind in enumerate(kinds):
            sums[kind] = total[index * high : (index + 1) * high]
    return sums


def tensor_sums(across, sx, mask, diagonal, z_parts, filtered, grads):
    double = diagonal.shape[1]
    depth, pairs = double // 2, across.shape[1] // double
    rows, count = 2 * pairs, across.shape[0] // 2
    for start in range(0, count, 16):
        kinds = [
            [
                across[kind * count + start : kind * count + start + 16, row * depth : (row + 1) * depth]
                for row in range(rows)
            ]
            for kind in range(2)
        ]
        for part in range(3):
            values = kinds[X_KINDS[part]]
            results = mirrored_filter(ROW_KINDS[part], values, True)
            results += mirrored_filter(ROW_KINDS[part], values, False)
            for row, result in enumerate(results):
                at = (part * pairs + row // 2) * count + start
                lanes = slice((row % 2) * depth, (row % 2 + 1) * depth)
                filtered[at : at + 16, lanes] = result.astype(jnp.bfloat16)

    at = 2 * pairs * count
    grads[:at] = product(filtered[:at, :], diagonal[0:double, :])
    grads[at:] = product(filtered[at:, :], diagonal[double : 2 * double, :])

    weights = product_weights(rows)
    layer = lax.axis_index("depth")
    first, last = layer == 0, layer == lax.axis_size("depth") - 1
    place = lax.broadcasted_iota(jnp.int32, (16, depth), 1)
    complete = ((place >= R1) | first) & ((place < depth - R1) | last)
    complete = jnp.where(complete, 1.0, 0.0)
    groups = [[] for _ in range(6)]
    for start in range(0, count, 16):
        inside = complete if mask is None else complete * mask[start : start + 16]
        totals = None
        for row in range(rows):
            lanes = slice((row % 2) * depth, (row % 2 + 1) * depth)
            three = []
            for part in range(3):
                at = (part * pairs + row // 2) * count + start
                three.append(grads[at : at + 16, lanes])
            terms = weighted_products(three, 2.0 * float(weights[row % (rows // 2)]))
            totals = terms if row == 0 else [a + b for a, b in zip(totals, terms)]
        for index in range(6):
            groups[index].append((totals[index] * inside).astype(jnp.bfloat16))
    products = [[jnp.concatenate(group, axis=0)] for group in groups]
    return all_sums(products, z_parts[double : double + depth, :], sx)


def rim_tiles(values):
    rows, depth = len(values), values[0].shape[1]
    below = packed_rows(values, RIM, depth - RIM)
    above = pltpu.roll(packed_rows(values, RIM, 0), rows * RIM, 1)
    lane = lax.broadcasted_iota(jnp.int32, below.shape, 1)
    return [jnp.where(lane < rows * RIM, below, above), above, pltpu.roll(above, HALF, 1)]


def early_kernel(
    starts, own, x_parts, z_parts, late_hbm, sums, diagonal, sides, tiles, x_late, across,
    filtered, grads, sem,
):
    copy = pltpu.make_async_copy(late_hbm, x_late, sem.at[0])
    copy.start()
    pairs, width, double = own.shape
    rows, depth = 2 * pairs, double // 2
    empty = jnp.zeros((depth, depth), jnp.bfloat16)
    for kind in range(2):
        for half in range(2):
            at = pl.ds(kind * double + half * depth, depth)
            band = z_parts[kind * depth : (kind + 1) * depth, :]
            diagonal[at, half * depth : (half + 1) * depth] = band
            diagonal[at, (1 - half) * depth : (2 - half) * depth] = empty
    whole = jnp.concatenate([own[pair] for pair in range(pairs)], axis=1)
    result = product(x_parts[starts[0] : starts[2], :width], whole)
    across[...] = result[: starts[1]]
    sides[...] = result[starts[1] :]
    sx = x_parts[starts[2] : starts[3], :EARLY]
    results = tensor_sums(across, sx, None, diagonal, z_parts, filtered, grads)
    for index, kind in enumerate(USED):
        sums[index] = results[kind]
    values = [
        own[row // 2, :, (row % 2) * depth : (row % 2 + 1) * depth].astype(jnp.float32)
        for row in range(rows)
    ]
    for index, tile in enumerate(rim_tiles(values)):
        tiles[index] = tile
    copy.wait()


def late_kernel(
    starts, width, far, near, x_late, z_parts, diagonal, early_sums, sides, own_tiles, temp, cure,
    out_hbm, across, filtered, grads, out, sems,
):
    double = diagonal.shape[1]
    depth = double // 2
    rows = across.shape[1] // depth
    count, lanes = temp.shape
    odd = is_odd()
    depths, layer = lax.axis_size("depth"), lax.axis_index("depth")
    outer, outer_columns = edges_of(far, rows)
    inner, inner_columns = edges_of(near, rows)
    values = []
    for row in range(rows):
        left = jnp.where(odd, inner[row], outer[row])
        right = jnp.where(odd, outer[row], inner[row])
        values.append(jnp.concatenate([left, right], axis=0))
    left = jnp.where(odd, inner_columns, outer_columns)
    right = jnp.where(odd, outer_columns, inner_columns)

    late = across.shape[0] // 2
    halos = jnp.concatenate([value.astype(jnp.bfloat16) for value in values], axis=1)
    across[...] = sides[...] + product(x_late[starts[0] : starts[1], : 2 * EDGE], halos)

    products_x, voxels = own_columns(count)
    folded, stride = fold(voxels), COARSE * count
    tiles = [
        jnp.concatenate([tile[:EDGE], own_tiles[index], tile[EDGE:]], axis=0)
        for index, tile in enumerate(rim_tiles(values))
    ]
    missing = stride * (depths - 1) + voxels - tiles[0].shape[0]
    if missing > 0:
        spare = jnp.zeros((-(-missing // 8) * 8, LANES), jnp.float32)
        tiles = [jnp.concatenate([tile, spare], axis=0) for tile in tiles]

    height = count + 2 * HALO
    half_lane = lax.broadcasted_iota(jnp.int32, (folded, LANES), 1) < HALF
    order = meeting_order(out.shape[0])
    for position, target in enumerate(order):
        at = stride * target
        second = jnp.where(
            half_lane,
            tiles[1][at : at + folded],
            tiles[2][at + voxels - folded : at + voxels],
        )
        rims = jnp.concatenate([tiles[0][at : at + voxels], second], axis=0)
        out[position, 0 : voxels + folded, :] = rims.astype(jnp.bfloat16)
    split = (pl.ds(0, voxels + folded), pl.ds(voxels + folded, out.shape[1] - voxels - folded))
    copies = [
        pltpu.make_async_copy(out.at[:, part, :], out_hbm.at[:, part, :], sems.at[index])
        for index, part in enumerate(split)
    ]
    copies[0].start()

    sx = x_late[starts[1] : starts[2], :late]
    results = tensor_sums(
        across, sx, late_mask(late, width), diagonal, z_parts, filtered, grads
    )
    yy, xx, zz, xz = [early_sums[index] + results[kind] for index, kind in enumerate(USED)]
    trace = yy + xx + zz
    lane = lax.broadcasted_iota(jnp.int32, trace.shape, 1)
    columns, cells = sizes(width, depth)
    tail = 4 * cells - LANES
    joint = pltpu.roll(xz, 3 * cells, 1)
    rest = jnp.where(lane < tail, joint, 0.0)
    rest = pltpu.roll(rest, 0, 1, stride=tail, stride_axis=0)
    for index, part in ((2, zz), (1, xx), (0, trace)):
        moved = part if index == 0 else pltpu.roll(part, index * cells, 1)
        joint = jnp.where(lane < (index + 1) * cells, moved, joint)

    own_first, own_last = column_rows(temp, cure, False), column_rows(temp, cure, True)
    half = chunk_rows(count, lanes)[1]
    for position, target in enumerate(order):
        piece = jnp.where(layer == target - 1, own_last, 0.0)
        piece = jnp.where(layer == target + 1, own_first, piece)
        if target == 0:
            piece = jnp.where(layer == depths - 1, left, piece)
        if target == out.shape[0] - 1:
            piece = jnp.where(layer == 0, right, piece)
        mine = slice(count * target, count * target + height)
        pieces = [joint[mine], jnp.sum(rest[mine], axis=0, keepdims=True)]
        for slot in range(lanes // LANES):
            pieces.append(piece[0:COLUMN_ROWS, slot * LANES : (slot + 1) * LANES])
        filled = sum(part.shape[0] for part in pieces)
        if filled < half:
            pieces.append(jnp.zeros((half - filled, LANES), jnp.float32))
        sent = two_parts(jnp.concatenate(pieces, axis=0))
        out[position, voxels + folded :, :] = sent.astype(jnp.bfloat16)
    copies[1].start()
    for copy in copies:
        copy.wait()


def rim_sums(chunks, count, starts, flat, steep, cells):
    parts = chunks.shape[0]
    rows_x, voxels = own_columns(count)
    folded = fold(voxels)
    tall = -(-voxels // 16) * 16
    spare = [jnp.zeros((tall - voxels, LANES), jnp.float32)] if tall > voxels else []
    tiles = []
    order = meeting_order(parts)
    for part in range(parts):
        rims = chunks[order.index(part), 0 : voxels + folded, :].astype(jnp.float32)
        second = rims[voxels:]
        second = [second[: voxels - folded], pltpu.roll(second, HALF, 1)]
        for tile in ([rims[:voxels]], second):
            tiles.append(jnp.concatenate(tile + spare, axis=0).astype(jnp.bfloat16))
    result = product(
        steep[starts[1] : starts[2], :tall], jnp.concatenate(tiles, axis=1)
    ).astype(jnp.bfloat16)
    kinds = []
    for kind in range(2):
        values = result[kind * rows_x : (kind + 1) * rows_x]
        tile = lambda index: values[:, index * LANES : (index + 1) * LANES]
        stack = [
            jnp.concatenate([tile(2 * part), tile(2 * part + 2), tile(2 * part + 3)], axis=1)
            for part in range(parts - 1)
        ]
        kinds.append(jnp.concatenate(stack, axis=0))
    both = product(kinds[0], flat[...])
    three = (both[:, :LANES], product(kinds[1], steep[starts[0] : starts[1], :]), both[:, LANES:])

    index = lax.axis_index("plane") * lax.axis_size("depth") + lax.axis_index("depth")
    total = lax.axis_size("plane") * lax.axis_size("depth") * count * COARSE
    place = lax.rem(lax.broadcasted_iota(jnp.int32, three[0].shape, 0), rows_x)
    place = place + (index * count - HALO) * COARSE - R2
    inside = jnp.where((place >= 0) & (place < total), 1.0, 0.0)
    products = [
        [
            term[part * rows_x : (part + 1) * rows_x].astype(jnp.bfloat16)
            for part in range(parts - 1)
        ]
        for term in weighted_products(three, inside)
    ]
    return all_sums(products, cells[...], steep[starts[2] : starts[3], :rows_x])


def cure_kernel(
    cells, starts, chunks, temp_in, cure_in, tools, flat, steep, rim_bands, temp_hbm, cure_hbm,
    conduct_hbm, temp_out, cure_out, conduct_out, sems,
):
    count, lanes = temp_in.shape
    parts = chunks.shape[0]
    planes, depths = lax.axis_size("plane"), lax.axis_size("depth")
    plane, layer = lax.axis_index("plane"), lax.axis_index("depth")
    height = count + 2 * HALO
    own = cells - BEFORE - AFTER
    lane = lax.broadcasted_iota(jnp.int32, (16, lanes), 1)
    row = lax.broadcasted_iota(jnp.int32, (16, lanes), 0)
    at_sums, half = chunk_rows(count, lanes)
    tail = 4 * cells - LANES
    narrow_lane = lax.broadcasted_iota(jnp.int32, (16, LANES), 1)
    order = meeting_order(parts)

    near = rim_sums(chunks, count, starts, flat, steep, rim_bands)
    sums = [near[0] + near[1] + near[2], near[1], near[2], near[5]]
    blocks = [
        joined(chunks[order.index(part), at_sums:, :].astype(jnp.float32)) for part in range(parts)
    ]
    tails = [block[height : height + 1] for block in blocks]
    if parts % 8:
        tails.append(jnp.zeros((-parts % 8, LANES), jnp.float32))
    tails = jnp.concatenate(tails, axis=0)
    tails = pltpu.roll(tails, lax.rem(LANES - lax.rem(tail * count * layer, LANES), LANES), 1)
    narrow_row = lax.broadcasted_iota(jnp.int32, (16, LANES), 0)
    rests = [jnp.zeros((16, LANES), jnp.float32) for _ in range(parts)]
    for column in range(height):
        moved = pltpu.roll(tails, LANES - tail * column, 1) if column else tails
        for part in range(parts):
            rests[part] = jnp.where(narrow_row == column, moved[part : part + 1], rests[part])
    for part in range(parts):
        first_cell = own * part - BEFORE
        here = (lane >= first_cell) & (lane < first_cell + cells)
        values = blocks[part]
        joint = values[0:16]
        xz = pltpu.roll(jnp.where(narrow_lane < tail, rests[part], joint), LANES - 3 * cells, 1)
        for index in range(4):
            chunk = xz if index == 3 else joint
            if lanes > LANES:
                spare = jnp.zeros((16, lanes - LANES), jnp.float32)
                chunk = jnp.concatenate([chunk, spare], axis=1)
            shift = (first_cell - (index % 3) * cells) % lanes
            moved = chunk if shift == 0 else pltpu.roll(chunk, shift, 1)
            sums[index] = sums[index] + jnp.where(here, moved, 0.0)
    trace = sums[0]
    scale = (conduct_fiber - conduct_matrix) / (2.0 * trace + tensor_eps)
    conduct = [
        conduct_matrix + scale * (trace - sums[1]),
        -scale * sums[3],
        conduct_matrix + scale * (trace - sums[2]),
    ]
    for kind in range(3):
        conduct_out[kind] = conduct[kind][HALO : HALO + count]
    copies = [
        pltpu.make_async_copy(conduct_out, conduct_hbm, sems.at[0]),
        pltpu.make_async_copy(temp_out, temp_hbm, sems.at[1]),
        pltpu.make_async_copy(cure_out, cure_hbm, sems.at[2]),
    ]
    copies[0].start()

    slots = range(height + 1, height + 1 + COLUMN_ROWS * (lanes // LANES), COLUMN_ROWS)
    columns = [
        jnp.concatenate([values[at : at + COLUMN_ROWS] for at in slots], axis=1) for values in blocks
    ]
    before, after = columns[parts - 1], columns[0]
    for part in range(parts - 1):
        before = jnp.where(layer == part + 1, columns[part], before)
        after = jnp.where(layer == part, columns[part + 1], after)
    spare = jnp.full((16 - count - 2 * GHOST, lanes), 0.5, jnp.float32)
    temp = jnp.concatenate([before[:GHOST], temp_in[...], after[:GHOST], 8.0 * spare], axis=0)
    cure = jnp.concatenate([spare[:1], before[GHOST:], cure_in[...], after[GHOST:], spare[:1], spare], axis=0)
    gap = GHOST - HALO
    xx, xz, zz = [pltpu.roll(part, gap, 0) for part in conduct]

    first = (plane == 0) & (layer == 0)
    last = (plane == planes - 1) & (layer == depths - 1)
    for step in range(STEPS):
        top, bottom = tools[2 * step : 2 * step + 1, :], tools[2 * step + 1 : 2 * step + 2, :]
        temp = jnp.where((row < GHOST) & first, temp[GHOST : GHOST + 1], temp)
        temp = jnp.where(
            (row >= GHOST + count) & last, temp[GHOST + count - 1 : GHOST + count], temp
        )
        cooler = jnp.where(lane == 0, top, pltpu.roll(temp, 1, 1))
        later = jnp.where(lane == lanes - 1, bottom, pltpu.roll(temp, lanes - 1, 1))
        slant = later - cooler
        second_x = pltpu.roll(temp, 15, 0) - 2.0 * temp + pltpu.roll(temp, 1, 0)
        second_z = later - 2.0 * temp + cooler
        cross = 0.25 * (pltpu.roll(slant, 15, 0) - pltpu.roll(slant, 1, 0))
        spread = xx * second_x + 2.0 * xz * cross + zz * second_z
        inverse = 1.0 / reference_temp - 1.0 / temp
        left = 1.0 - cure
        rate = rate_first * jnp.exp(energy_first * inverse) + rate_second * jnp.exp(
            energy_second * inverse
        ) * jnp.sqrt(cure)
        rate = rate * (left * jnp.sqrt(left))
        temp = temp + time_step * (spread + heat_release * rate)
        cure = cure + time_step * rate
    temp_out[...] = temp[GHOST : GHOST + count]
    cure_out[...] = cure[GHOST : GHOST + count]
    for copy in copies[1:]:
        copy.start()
    for copy in copies:
        copy.wait()


def on_device(intensity, temp_start, cure_start, tool_levels, plan):
    rows, width, depth = intensity.shape
    count, lanes = temp_start.shape
    planes, depths = lax.axis_size("plane"), lax.axis_size("depth")
    columns, cells = sizes(width, depth)
    bf16 = jnp.bfloat16
    slots = rows * EDGE + 16 * (lanes // LANES)
    params = pltpu.CompilerParams(vmem_limit_bytes=24 * 1024 * 1024)
    vmem = pl.BlockSpec(memory_space=pltpu.VMEM)
    stay = pl.BlockSpec(memory_space=pltpu.HBM)

    fixed = lambda values: pltpu.with_memory_space_constraint(values, pltpu.HBM)
    bands, coarse = x_bands(width), coarse_x_bands(width)
    late = bands.shape[1] - EARLY
    middle = bands[:, :EARLY, EDGE : EDGE + width]
    sides = bands[:, EARLY:].reshape(2 * late, -1)
    x_hbm, early_starts = stacked(
        middle.reshape(2 * EARLY, -1), sides[:, EDGE : EDGE + width], coarse[:, :EARLY]
    )
    z_hbm, _ = stacked(*depth_bands(depth), coarse_depth_bands(depth))
    halos = np.concatenate([sides[:, :EDGE], sides[:, EDGE + width :]], axis=1)
    x_late, late_starts = stacked(halos, coarse[:, EARLY:])
    rims = rim_bands(rows)
    flat, _ = stacked(np.concatenate([rims[0], rims[2]], axis=1))
    steep, rim_starts = stacked(rims[1], *rim_x_bands(count))
    cell_bands, _ = stacked(rim_cells(rows, depth, depths))
    far, near, own, x_parts, z_parts, temp, cure = pl.pallas_call(
        pack_kernel,
        name="pack",
        out_shape=(
            pltpu.VMEM((slots, depth), bf16),
            pltpu.VMEM((slots, depth), bf16),
            pltpu.VMEM((rows // 2, width, 2 * depth), bf16),
            pltpu.VMEM(x_hbm.shape, bf16),
            pltpu.VMEM(z_hbm.shape, bf16),
            pltpu.VMEM((count, lanes), jnp.float32),
            pltpu.VMEM((count, lanes), jnp.float32),
        ),
        in_specs=[stay] * 5,
        scratch_shapes=[
            pltpu.VMEM((rows, width, depth), jnp.int32),
            pltpu.SemaphoreType.DMA((5,)),
        ],
        compiler_params=params,
    )(*[fixed(values) for values in (intensity, temp_start, cure_start, x_hbm, z_hbm)])

    def moved(values, pairs):
        index = [(p * depths + d, q * depths + e) for (p, d), (q, e) in pairs]
        return lax.ppermute(values, ("plane", "depth"), index)

    def swapped(values, first):
        pairs = [(p, p + 1) for p in range(first, planes - 1, 2)]
        pairs += [(q, p) for p, q in pairs]
        return moved(values, [((p, d), (q, d)) for p, q in pairs for d in range(depths)])

    far = swapped(far, 1)
    near = swapped(near, 0)

    high = coarse.shape[0]

    def scratch(count):
        return [
            pltpu.VMEM((2 * count, rows * depth), jnp.float32),
            pltpu.VMEM((3 * rows // 2 * count, 2 * depth), bf16),
            pltpu.VMEM((3 * rows // 2 * count, 2 * depth), jnp.float32),
        ]

    def cost(count):
        return pl.CostEstimate(
            flops=2 * rows * (2 * count) * 160 * depth * 4,
            bytes_accessed=4_000_000,
            transcendentals=0,
        )

    early_sums, diagonal, sides, own_tiles, x_late = pl.pallas_call(
        functools.partial(early_kernel, early_starts),
        name="early",
        out_shape=(
            pltpu.VMEM((len(USED), high, LANES), jnp.float32),
            pltpu.VMEM((4 * depth, 2 * depth), bf16),
            pltpu.VMEM((2 * late, rows * depth), jnp.float32),
            pltpu.VMEM((3, width, LANES), jnp.float32),
            pltpu.VMEM(x_late.shape, bf16),
        ),
        in_specs=[vmem] * 3 + [stay],
        scratch_shapes=scratch(EARLY) + [pltpu.SemaphoreType.DMA((1,))],
        cost_estimate=cost(EARLY),
        compiler_params=params,
    )(own, x_parts, z_parts, fixed(x_late))

    products_x, voxels = own_columns(count)
    at_sums, half = chunk_rows(count, lanes)
    chunk_shape = (depths, at_sums + 2 * half, LANES)
    chunks = pl.pallas_call(
        functools.partial(late_kernel, late_starts, width),
        name="late",
        out_shape=pltpu.HBM(chunk_shape, bf16),
        in_specs=[vmem] * 10,
        out_specs=stay,
        scratch_shapes=scratch(late)
        + [pltpu.VMEM(chunk_shape, bf16), pltpu.SemaphoreType.DMA((2,))],
        cost_estimate=cost(late),
        compiler_params=params,
    )(far, near, x_late, z_parts, diagonal, early_sums, sides, own_tiles, temp, cure)

    faces = plan.reshape(2 * STEPS, 1) == jnp.arange(tool_levels.shape[0], dtype=jnp.int32)
    tools = jnp.sum(
        jnp.where(faces, tool_levels, jnp.zeros_like(tool_levels)), axis=1, keepdims=True
    )

    chunks = lax.all_to_all(
        chunks,
        "depth",
        split_axis=0,
        concat_axis=0,
        tiled=True,
        axis_index_groups=[meeting_order(depths)],
    )

    return pl.pallas_call(
        functools.partial(cure_kernel, cells, rim_starts),
        name="cure",
        out_shape=(
            pltpu.HBM((count, lanes), jnp.float32),
            pltpu.HBM((count, lanes), jnp.float32),
            pltpu.HBM((3, count, lanes), jnp.float32),
        ),
        in_specs=[vmem] * 7,
        out_specs=(stay, stay, stay),
        scratch_shapes=[
            pltpu.VMEM((count, lanes), jnp.float32),
            pltpu.VMEM((count, lanes), jnp.float32),
            pltpu.VMEM((3, count, lanes), jnp.float32),
            pltpu.SemaphoreType.DMA((3,)),
        ],
        compiler_params=params,
    )(chunks, temp, cure, tools, flat, steep, cell_bands)


def solution(mesh):
    return jax.shard_map(
        on_device,
        mesh=mesh,
        in_specs=(
            P(None, "plane", "depth"),
            P(("plane", "depth"), None),
            P(("plane", "depth"), None),
            P(),
            P(),
        ),
        out_specs=(
            P(("plane", "depth"), None),
            P(("plane", "depth"), None),
            P(None, ("plane", "depth"), None),
        ),
        check_vma=False,
    )
```

```python
import functools

import jax
import jax.numpy as jnp
import ml_dtypes
import numpy as np
from jax import lax
from jax.experimental import pallas as pl
from jax.experimental.pallas import tpu as pltpu
from jax.sharding import PartitionSpec as P

ROWS = 8
R1 = 6
R2 = 10
COARSE = 4
STEPS = 3

sigma_grad = 2.0
sigma_tensor = 3.3
conduct_matrix = 0.3
conduct_fiber = 1.5
time_step = 0.25
heat_release = 0.4
rate_first = 0.15
rate_second = 0.6
energy_first = 30.0
energy_second = 25.0
reference_temp = 4.2
tensor_eps = 1e-06

LANES = 128
HALO = 2
EDGE = HALO * COARSE + R1 + R2
EARLY = 96
GHOST = 3
COLUMN_ROWS = 2 * GHOST - 1
RIM = 2 * R1
BEFORE = -(-(R2 - R1) // COARSE)
AFTER = BEFORE
HALF = LANES // 2
ROW_KINDS = (1, 0, 0)
X_KINDS = (0, 1, 0)
DEPTH_KINDS = (0, 0, 1)


def smooth_taps(radius, sigma):
    offsets = np.arange(-radius, radius + 1) * 1.0
    weights = np.exp(-0.5 * offsets * offsets / (sigma * sigma))
    return weights / weights.sum()


def slope_taps(radius, sigma):
    offsets = np.arange(-radius, radius + 1) * 1.0
    weights = np.exp(-0.5 * offsets * offsets / (sigma * sigma))
    return offsets * weights / np.sum(offsets * offsets * weights)


def row_weights(count, radius, sigma):
    taps = smooth_taps(radius, sigma)
    result = np.zeros(count)
    for source in range(count):
        for target in range(count):
            offset = target - source
            if abs(offset) <= radius:
                result[source] += taps[offset + radius]
    return result


def rounded(taps):
    best = None
    for factor in np.linspace(1.0, 2.0, 20001)[:-1]:
        near = (taps * factor).astype(np.float32).astype(ml_dtypes.bfloat16).astype(np.float64)
        error = np.abs(near / factor - taps).sum()
        if best is None or error < best[0]:
            best = (error, near, factor)
    return best[1], best[2]


def as_bfloat16(matrix):
    return matrix.astype(np.float32).astype(ml_dtypes.bfloat16)


def halves(matrix):
    high = as_bfloat16(matrix)
    return high, as_bfloat16(matrix - high.astype(np.float64))


def sizes(width, depth):
    columns = width // COARSE + 2 * HALO
    cells = depth // COARSE + BEFORE + AFTER
    return columns, cells


def product_rows(width):
    places = [*range(R1, width - R1)]
    places += [None] * max(EARLY - len(places), 0)
    places += [*range(R1 - EDGE, R1), *range(width - R1, width + EDGE - R1)]
    return places + [None] * (-len(places) % 16)


GRAD_TAPS = tuple(
    rounded(taps(R1, sigma_grad)) for taps in (smooth_taps, slope_taps)
)
GRAD_FACTOR = GRAD_TAPS[0][1] ** 2 * GRAD_TAPS[1][1]


def grad_taps(kind):
    return GRAD_TAPS[kind][0]


def tap(taps, offset):
    radius = (len(taps) - 1) // 2
    return float(taps[offset + radius]) if abs(offset) <= radius else 0.0


def x_bands(width):
    places = product_rows(width)
    bands = np.zeros((2, len(places), width + 2 * EDGE))
    for kind in range(2):
        for row, place in enumerate(places):
            if place is not None:
                first = place + EDGE - R1
                bands[kind, row, first : first + 2 * R1 + 1] = grad_taps(kind)
    return bands


def rim_bands(rows):
    bands = np.zeros((3, 3 * LANES, LANES))
    for part in range(3):
        row_taps, depth_taps = grad_taps(ROW_KINDS[part]), grad_taps(DEPTH_KINDS[part])
        for source in range(rows):
            for target in range(rows):
                row_tap = tap(row_taps, source - target)
                for near in range(-RIM, RIM):
                    lane = source * RIM + near % RIM
                    if near >= 0:
                        lane += rows * RIM + LANES
                    for place in range(-R1, R1):
                        value = row_tap * tap(depth_taps, near - place)
                        bands[part, lane, target * 2 * R1 + R1 + place] = value
    return bands


def rim_cells(rows, depth, blocks):
    taps = smooth_taps(R2, sigma_tensor)
    weights = product_weights(rows)
    bands = np.zeros((blocks - 1, LANES, blocks * depth // COARSE))
    for boundary in range(blocks - 1):
        middle = (boundary + 1) * depth
        for cell in range(bands.shape[2]):
            for voxel in range(cell * COARSE, (cell + 1) * COARSE):
                for place in range(-R1, R1):
                    value = tap(taps, middle + place - voxel)
                    for row in range(rows):
                        bands[boundary, row * 2 * R1 + R1 + place, cell] += weights[row] * value
    return bands.reshape(-1, bands.shape[2])


def meeting_order(blocks):
    middle = blocks // 2
    rest = [block for block in range(blocks) if block != middle]
    ends = [rest.pop(0 if turn % 2 == 0 else -1) for turn in range(blocks - 1)]
    return [middle, *ends]


def own_columns(count):
    products = (count + 2 * HALO) * COARSE + 2 * R2
    voxels = products + 2 * R1
    return -(-products // 16) * 16, -(-voxels // 8) * 8


def fold(voxels):
    return -(-voxels // 16) * 8


def rim_x_bands(count):
    products, voxels = own_columns(count)
    bands = np.zeros((2, products, -(-voxels // 16) * 16))
    valid = (count + 2 * HALO) * COARSE + 2 * R2
    for kind in range(2):
        for row in range(valid):
            bands[kind, row, row : row + 2 * R1 + 1] = grad_taps(kind)
    taps = smooth_taps(R2, sigma_tensor)
    coarse = np.zeros((16, products))
    for column in range(count + 2 * HALO):
        for voxel in range(column * COARSE, (column + 1) * COARSE):
            coarse[column, voxel : voxel + 2 * R2 + 1] += taps
    return bands.reshape(2 * products, -1), coarse


def depth_bands(depth):
    bands = np.zeros((2, depth, depth))
    for kind in range(2):
        for place in range(depth):
            for near in range(max(place - R1, 0), min(place + R1 + 1, depth)):
                bands[kind, near, place] = tap(grad_taps(kind), near - place)
    return bands


def product_weights(rows):
    return row_weights(rows, R2, sigma_tensor) / (255.0 * GRAD_FACTOR) ** 2


def coarse_depth_bands(depth):
    taps = smooth_taps(R2, sigma_tensor)
    columns, cells = sizes(0, depth)
    bands = np.zeros((depth, LANES))
    for cell in range(cells):
        for voxel in range(COARSE):
            place = (cell - BEFORE) * COARSE + voxel
            for near in range(max(place - R2, 0), min(place + R2 + 1, depth)):
                bands[near, cell] += tap(taps, near - place)
    return bands


def coarse_x_bands(width):
    taps = smooth_taps(R2, sigma_tensor)
    places = product_rows(width)
    columns, cells = sizes(width, 0)
    bands = np.zeros((-(-columns // 16) * 16, len(places)))
    for column in range(columns):
        for voxel in range(COARSE):
            middle = (column - HALO) * COARSE + voxel
            for row, place in enumerate(places):
                if place is not None:
                    bands[column, row] += tap(taps, place - middle)
    return bands


def stacked(*pieces):
    widest = max(piece.shape[1] for piece in pieces)
    padded = [np.pad(piece, ((0, 0), (0, widest - piece.shape[1]))) for piece in pieces]
    starts = np.cumsum([0] + [len(piece) for piece in pieces])
    return jnp.asarray(as_bfloat16(np.concatenate(padded))), tuple(int(start) for start in starts)


def two_parts(values):
    high = values.astype(jnp.bfloat16).astype(jnp.float32)
    return jnp.concatenate([high, (values - high).astype(jnp.bfloat16).astype(jnp.float32)], axis=0)


def joined(parts):
    half = parts.shape[0] // 2
    return parts[:half] + parts[half:]


def column_rows(temp, cure, at_end):
    count = temp.shape[0]
    first, second = (count - GHOST, count - GHOST + 1) if at_end else (0, 0)
    pad = jnp.zeros((8 - COLUMN_ROWS, temp.shape[1]), jnp.float32)
    return jnp.concatenate(
        [temp[first : first + GHOST, :], cure[second : second + GHOST - 1, :], pad], axis=0
    )


def chunk_rows(count, lanes):
    products, voxels = own_columns(count)
    held = count + 2 * HALO + 1 + COLUMN_ROWS * (lanes // LANES)
    return voxels + fold(voxels), -(-held // 8) * 8


def is_odd():
    return lax.rem(lax.axis_index("plane"), 2) == 1


def pack_kernel(intensity, temp_hbm, cure_hbm, far, near, temp, cure, edges, sems):
    rows, width, depth = intensity.shape
    copies = [
        pltpu.make_async_copy(
            intensity.at[:, pl.ds(place, EDGE), :], edges.at[side], sems.at[side]
        )
        for side, place in enumerate((0, width - EDGE))
    ]
    copies += [
        pltpu.make_async_copy(temp_hbm, temp, sems.at[2]),
        pltpu.make_async_copy(cure_hbm, cure, sems.at[3]),
    ]
    for copy in copies:
        copy.start()
    for copy in copies:
        copy.wait()
    odd = is_odd()
    sides = [
        two_parts(column_rows(temp, cure, at_end)).astype(jnp.bfloat16)
        for at_end in (False, True)
    ]

    def send(left, right):
        for side, (target, columns) in enumerate(((left, sides[0]), (right, sides[1]))):
            for pair in range(rows // 2):
                two = [edges[side, 2 * pair + i] for i in range(2)]
                two = jnp.concatenate(two, axis=0).astype(jnp.float32)
                target[2 * EDGE * pair : 2 * EDGE * (pair + 1), :] = two.astype(jnp.bfloat16)
            for slot in range(temp.shape[1] // LANES):
                at = rows * EDGE + 16 * slot
                target[at : at + 16, :] = columns[:, slot * LANES : (slot + 1) * LANES]

    @pl.when(odd)
    def _():
        send(near, far)

    @pl.when(jnp.logical_not(odd))
    def _():
        send(far, near)


def packed_rows(values, size, first):
    depth = values[0].shape[1]
    lane = lax.broadcasted_iota(jnp.int32, values[0].shape, 1)
    packed = None
    for block, value in enumerate(values):
        shift = (size * block - first) % depth
        moved = value if shift == 0 else pltpu.roll(value, shift, 1)
        packed = moved if block == 0 else jnp.where(lane >= size * block, moved, packed)
    return packed


def edges_of(ref, rows):
    two = [
        ref[2 * EDGE * pair : 2 * EDGE * (pair + 1), :].astype(jnp.float32)
        for pair in range(rows // 2)
    ]
    voxels = [two[row // 2][row % 2 * EDGE : (row % 2 + 1) * EDGE] for row in range(rows)]
    slots = range(rows * EDGE, ref.shape[0], 16)
    columns = [joined(ref[at : at + 16, :].astype(jnp.float32)) for at in slots]
    return voxels, jnp.concatenate(columns, axis=1)


def product(first, second):
    return jnp.dot(first, second, preferred_element_type=jnp.float32)


def mirrored_filter(kind, values, even):
    rows = len(values)
    use_sum = even == (kind == 0)
    sign = 1.0 if use_sum else -1.0
    half = [values[row] + sign * values[rows - 1 - row] for row in range(rows // 2)]
    results = []
    for row in range(rows // 2):
        total = None
        for source, value in enumerate(half):
            near = tap(grad_taps(kind), source - row)
            far = tap(grad_taps(kind), rows - 1 - source - row)
            weight = 0.5 * (near + sign * far)
            total = weight * value if total is None else total + weight * value
        results.append(total)
    return results


def weighted_products(three, weight):
    pairs = ((0, 0), (1, 1), (2, 2), (0, 1), (0, 2), (1, 2))
    first = [weight * value for value in three]
    return [first[a] * three[b] for a, b in pairs]


def late_mask(count, width):
    row = lax.broadcasted_iota(jnp.int32, (count, LANES), 0)
    left = max(width - 2 * R1 - EARLY, 0)
    place = jnp.where(row < left + EDGE, row - left + R1 - EDGE, row - left - EDGE + width - R1)
    place = place + lax.axis_index("plane") * width
    inside = (place >= 0) & (place < lax.axis_size("plane") * width)
    return jnp.where(inside | (row < left), 1.0, 0.0)


USED = (0, 1, 2, 5)
UNUSED = (3, 4)


def all_sums(products, coarse, sx):
    sums = [None] * 6
    for kinds in (USED, UNUSED):
        tiles = [tile for index in kinds for tile in products[index]]
        along = product(sx, jnp.concatenate(tiles, axis=1)).astype(jnp.bfloat16)
        step = along.shape[1] // len(kinds)
        parts = [along[:, index * step : (index + 1) * step] for index in range(len(kinds))]
        total = product(jnp.concatenate(parts, axis=0), coarse)
        high = sx.shape[0]
        for index, kind in enumerate(kinds):
            sums[kind] = total[index * high : (index + 1) * high]
    return sums


def tensor_sums(across, sx, mask, diagonal, z_parts, filtered, grads):
    double = diagonal.shape[1]
    depth, pairs = double // 2, across.shape[1] // double
    rows, count = 2 * pairs, across.shape[0] // 2
    for start in range(0, count, 16):
        kinds = [
            [
                across[kind * count + start : kind * count + start + 16, row * depth : (row + 1) * depth]
                for row in range(rows)
            ]
            for kind in range(2)
        ]
        for part in range(3):
            values = kinds[X_KINDS[part]]
            results = mirrored_filter(ROW_KINDS[part], values, True)
            results += mirrored_filter(ROW_KINDS[part], values, False)
            for row, result in enumerate(results):
                at = (part * pairs + row // 2) * count + start
                lanes = slice((row % 2) * depth, (row % 2 + 1) * depth)
                filtered[at : at + 16, lanes] = result.astype(jnp.bfloat16)

    at = 2 * pairs * count
    grads[:at] = product(filtered[:at, :], diagonal[0:double, :])
    grads[at:] = product(filtered[at:, :], diagonal[double : 2 * double, :])

    weights = product_weights(rows)
    layer = lax.axis_index("depth")
    first, last = layer == 0, layer == lax.axis_size("depth") - 1
    place = lax.broadcasted_iota(jnp.int32, (16, depth), 1)
    complete = ((place >= R1) | first) & ((place < depth - R1) | last)
    complete = jnp.where(complete, 1.0, 0.0)
    groups = [[] for _ in range(6)]
    for start in range(0, count, 16):
        inside = complete if mask is None else complete * mask[start : start + 16]
        totals = None
        for row in range(rows):
            lanes = slice((row % 2) * depth, (row % 2 + 1) * depth)
            three = []
            for part in range(3):
                at = (part * pairs + row // 2) * count + start
                three.append(grads[at : at + 16, lanes])
            terms = weighted_products(three, 2.0 * float(weights[row % (rows // 2)]))
            totals = terms if row == 0 else [a + b for a, b in zip(totals, terms)]
        for index in range(6):
            groups[index].append((totals[index] * inside).astype(jnp.bfloat16))
    products = [[jnp.concatenate(group, axis=0)] for group in groups]
    return all_sums(products, z_parts[double : double + depth, :], sx)


def rim_tiles(values):
    rows, depth = len(values), values[0].shape[1]
    below = packed_rows(values, RIM, depth - RIM)
    above = pltpu.roll(packed_rows(values, RIM, 0), rows * RIM, 1)
    lane = lax.broadcasted_iota(jnp.int32, below.shape, 1)
    return [jnp.where(lane < rows * RIM, below, above), above, pltpu.roll(above, HALF, 1)]


def early_kernel(
    starts, grey, x_parts, z_parts, sums, diagonal, sides, tiles, across, filtered, grads
):
    rows, width, depth = grey.shape
    double = 2 * depth
    empty = jnp.zeros((depth, depth), jnp.bfloat16)
    for kind in range(2):
        for half in range(2):
            at = pl.ds(kind * double + half * depth, depth)
            band = z_parts[kind * depth : (kind + 1) * depth, :]
            diagonal[at, half * depth : (half + 1) * depth] = band
            diagonal[at, (1 - half) * depth : (2 - half) * depth] = empty
    values = [grey[row].astype(jnp.float32) for row in range(rows)]
    whole = jnp.concatenate([value.astype(jnp.bfloat16) for value in values], axis=1)
    result = product(x_parts[starts[0] : starts[2], :width], whole)
    across[...] = result[: starts[1]]
    sides[...] = result[starts[1] :]
    sx = x_parts[starts[2] : starts[3], :EARLY]
    results = tensor_sums(across, sx, None, diagonal, z_parts, filtered, grads)
    for index, kind in enumerate(USED):
        sums[index] = results[kind]
    for index, tile in enumerate(rim_tiles(values)):
        tiles[index] = tile


def late_kernel(
    starts, width, far, near, x_late, z_parts, diagonal, early_sums, sides, own_tiles, temp, cure,
    out_hbm, across, filtered, grads, out, sems,
):
    double = diagonal.shape[1]
    depth = double // 2
    rows = across.shape[1] // depth
    count, lanes = temp.shape
    odd = is_odd()
    depths, layer = lax.axis_size("depth"), lax.axis_index("depth")
    outer, outer_columns = edges_of(far, rows)
    inner, inner_columns = edges_of(near, rows)
    values = []
    for row in range(rows):
        left = jnp.where(odd, inner[row], outer[row])
        right = jnp.where(odd, outer[row], inner[row])
        values.append(jnp.concatenate([left, right], axis=0))
    left = jnp.where(odd, inner_columns, outer_columns)
    right = jnp.where(odd, outer_columns, inner_columns)

    late = across.shape[0] // 2
    halos = jnp.concatenate([value.astype(jnp.bfloat16) for value in values], axis=1)
    across[...] = sides[...] + product(x_late[starts[0] : starts[1], : 2 * EDGE], halos)

    products_x, voxels = own_columns(count)
    folded, stride = fold(voxels), COARSE * count
    tiles = [
        jnp.concatenate([tile[:EDGE], own_tiles[index], tile[EDGE:]], axis=0)
        for index, tile in enumerate(rim_tiles(values))
    ]
    missing = stride * (depths - 1) + voxels - tiles[0].shape[0]
    if missing > 0:
        spare = jnp.zeros((-(-missing // 8) * 8, LANES), jnp.float32)
        tiles = [jnp.concatenate([tile, spare], axis=0) for tile in tiles]

    height = count + 2 * HALO
    half_lane = lax.broadcasted_iota(jnp.int32, (folded, LANES), 1) < HALF
    order = meeting_order(out.shape[0])
    for position, target in enumerate(order):
        at = stride * target
        second = jnp.where(
            half_lane,
            tiles[1][at : at + folded],
            tiles[2][at + voxels - folded : at + voxels],
        )
        rims = jnp.concatenate([tiles[0][at : at + voxels], second], axis=0)
        out[position, 0 : voxels + folded, :] = rims.astype(jnp.bfloat16)
    split = (pl.ds(0, voxels + folded), pl.ds(voxels + folded, out.shape[1] - voxels - folded))
    copies = [
        pltpu.make_async_copy(out.at[:, part, :], out_hbm.at[:, part, :], sems.at[index])
        for index, part in enumerate(split)
    ]
    copies[0].start()

    sx = x_late[starts[1] : starts[2], :late]
    results = tensor_sums(
        across, sx, late_mask(late, width), diagonal, z_parts, filtered, grads
    )
    yy, xx, zz, xz = [early_sums[index] + results[kind] for index, kind in enumerate(USED)]
    trace = yy + xx + zz
    lane = lax.broadcasted_iota(jnp.int32, trace.shape, 1)
    columns, cells = sizes(width, depth)
    tail = 4 * cells - LANES
    joint = pltpu.roll(xz, 3 * cells, 1)
    rest = jnp.where(lane < tail, joint, 0.0)
    rest = pltpu.roll(rest, 0, 1, stride=tail, stride_axis=0)
    for index, part in ((2, zz), (1, xx), (0, trace)):
        moved = part if index == 0 else pltpu.roll(part, index * cells, 1)
        joint = jnp.where(lane < (index + 1) * cells, moved, joint)

    own_first, own_last = column_rows(temp, cure, False), column_rows(temp, cure, True)
    half = chunk_rows(count, lanes)[1]
    for position, target in enumerate(order):
        piece = jnp.where(layer == target - 1, own_last, 0.0)
        piece = jnp.where(layer == target + 1, own_first, piece)
        if target == 0:
            piece = jnp.where(layer == depths - 1, left, piece)
        if target == out.shape[0] - 1:
            piece = jnp.where(layer == 0, right, piece)
        mine = slice(count * target, count * target + height)
        pieces = [joint[mine], jnp.sum(rest[mine], axis=0, keepdims=True)]
        for slot in range(lanes // LANES):
            pieces.append(piece[0:COLUMN_ROWS, slot * LANES : (slot + 1) * LANES])
        filled = sum(part.shape[0] for part in pieces)
        if filled < half:
            pieces.append(jnp.zeros((half - filled, LANES), jnp.float32))
        sent = two_parts(jnp.concatenate(pieces, axis=0))
        out[position, voxels + folded :, :] = sent.astype(jnp.bfloat16)
    copies[1].start()
    for copy in copies:
        copy.wait()


def rim_sums(chunks, count, starts, flat, steep, cells):
    parts = chunks.shape[0]
    rows_x, voxels = own_columns(count)
    folded = fold(voxels)
    tall = -(-voxels // 16) * 16
    spare = [jnp.zeros((tall - voxels, LANES), jnp.float32)] if tall > voxels else []
    tiles = []
    order = meeting_order(parts)
    for part in range(parts):
        rims = chunks[order.index(part), 0 : voxels + folded, :].astype(jnp.float32)
        second = rims[voxels:]
        second = [second[: voxels - folded], pltpu.roll(second, HALF, 1)]
        for tile in ([rims[:voxels]], second):
            tiles.append(jnp.concatenate(tile + spare, axis=0).astype(jnp.bfloat16))
    result = product(
        steep[starts[1] : starts[2], :tall], jnp.concatenate(tiles, axis=1)
    ).astype(jnp.bfloat16)
    kinds = []
    for kind in range(2):
        values = result[kind * rows_x : (kind + 1) * rows_x]
        tile = lambda index: values[:, index * LANES : (index + 1) * LANES]
        stack = [
            jnp.concatenate([tile(2 * part), tile(2 * part + 2), tile(2 * part + 3)], axis=1)
            for part in range(parts - 1)
        ]
        kinds.append(jnp.concatenate(stack, axis=0))
    both = product(kinds[0], flat[...])
    three = (both[:, :LANES], product(kinds[1], steep[starts[0] : starts[1], :]), both[:, LANES:])

    index = lax.axis_index("plane") * lax.axis_size("depth") + lax.axis_index("depth")
    total = lax.axis_size("plane") * lax.axis_size("depth") * count * COARSE
    place = lax.rem(lax.broadcasted_iota(jnp.int32, three[0].shape, 0), rows_x)
    place = place + (index * count - HALO) * COARSE - R2
    inside = jnp.where((place >= 0) & (place < total), 1.0, 0.0)
    products = [
        [
            term[part * rows_x : (part + 1) * rows_x].astype(jnp.bfloat16)
            for part in range(parts - 1)
        ]
        for term in weighted_products(three, inside)
    ]
    return all_sums(products, cells[...], steep[starts[2] : starts[3], :rows_x])


def cure_kernel(
    cells, starts, chunks, temp_in, cure_in, tools, flat, steep, rim_bands, temp_hbm, cure_hbm,
    conduct_hbm, temp_out, cure_out, conduct_out, sems,
):
    count, lanes = temp_in.shape
    parts = chunks.shape[0]
    planes, depths = lax.axis_size("plane"), lax.axis_size("depth")
    plane, layer = lax.axis_index("plane"), lax.axis_index("depth")
    height = count + 2 * HALO
    own = cells - BEFORE - AFTER
    lane = lax.broadcasted_iota(jnp.int32, (16, lanes), 1)
    row = lax.broadcasted_iota(jnp.int32, (16, lanes), 0)
    at_sums, half = chunk_rows(count, lanes)
    tail = 4 * cells - LANES
    narrow_lane = lax.broadcasted_iota(jnp.int32, (16, LANES), 1)
    order = meeting_order(parts)

    near = rim_sums(chunks, count, starts, flat, steep, rim_bands)
    sums = [near[0] + near[1] + near[2], near[1], near[2], near[5]]
    blocks = [
        joined(chunks[order.index(part), at_sums:, :].astype(jnp.float32)) for part in range(parts)
    ]
    tails = [block[height : height + 1] for block in blocks]
    if parts % 8:
        tails.append(jnp.zeros((-parts % 8, LANES), jnp.float32))
    tails = jnp.concatenate(tails, axis=0)
    tails = pltpu.roll(tails, lax.rem(LANES - lax.rem(tail * count * layer, LANES), LANES), 1)
    narrow_row = lax.broadcasted_iota(jnp.int32, (16, LANES), 0)
    rests = [jnp.zeros((16, LANES), jnp.float32) for _ in range(parts)]
    for column in range(height):
        moved = pltpu.roll(tails, LANES - tail * column, 1) if column else tails
        for part in range(parts):
            rests[part] = jnp.where(narrow_row == column, moved[part : part + 1], rests[part])
    for part in range(parts):
        first_cell = own * part - BEFORE
        here = (lane >= first_cell) & (lane < first_cell + cells)
        values = blocks[part]
        joint = values[0:16]
        xz = pltpu.roll(jnp.where(narrow_lane < tail, rests[part], joint), LANES - 3 * cells, 1)
        for index in range(4):
            chunk = xz if index == 3 else joint
            if lanes > LANES:
                spare = jnp.zeros((16, lanes - LANES), jnp.float32)
                chunk = jnp.concatenate([chunk, spare], axis=1)
            shift = (first_cell - (index % 3) * cells) % lanes
            moved = chunk if shift == 0 else pltpu.roll(chunk, shift, 1)
            sums[index] = sums[index] + jnp.where(here, moved, 0.0)
    trace = sums[0]
    scale = (conduct_fiber - conduct_matrix) / (2.0 * trace + tensor_eps)
    conduct = [
        conduct_matrix + scale * (trace - sums[1]),
        -scale * sums[3],
        conduct_matrix + scale * (trace - sums[2]),
    ]
    for kind in range(3):
        conduct_out[kind] = conduct[kind][HALO : HALO + count]
    copies = [
        pltpu.make_async_copy(conduct_out, conduct_hbm, sems.at[0]),
        pltpu.make_async_copy(temp_out, temp_hbm, sems.at[1]),
        pltpu.make_async_copy(cure_out, cure_hbm, sems.at[2]),
    ]
    copies[0].start()

    slots = range(height + 1, height + 1 + COLUMN_ROWS * (lanes // LANES), COLUMN_ROWS)
    columns = [
        jnp.concatenate([values[at : at + COLUMN_ROWS] for at in slots], axis=1) for values in blocks
    ]
    before, after = columns[parts - 1], columns[0]
    for part in range(parts - 1):
        before = jnp.where(layer == part + 1, columns[part], before)
        after = jnp.where(layer == part, columns[part + 1], after)
    spare = jnp.full((16 - count - 2 * GHOST, lanes), 0.5, jnp.float32)
    temp = jnp.concatenate([before[:GHOST], temp_in[...], after[:GHOST], 8.0 * spare], axis=0)
    cure = jnp.concatenate([spare[:1], before[GHOST:], cure_in[...], after[GHOST:], spare[:1], spare], axis=0)
    gap = GHOST - HALO
    xx, xz, zz = [pltpu.roll(part, gap, 0) for part in conduct]

    first = (plane == 0) & (layer == 0)
    last = (plane == planes - 1) & (layer == depths - 1)
    for step in range(STEPS):
        top, bottom = tools[2 * step : 2 * step + 1, :], tools[2 * step + 1 : 2 * step + 2, :]
        temp = jnp.where((row < GHOST) & first, temp[GHOST : GHOST + 1], temp)
        temp = jnp.where(
            (row >= GHOST + count) & last, temp[GHOST + count - 1 : GHOST + count], temp
        )
        cooler = jnp.where(lane == 0, top, pltpu.roll(temp, 1, 1))
        later = jnp.where(lane == lanes - 1, bottom, pltpu.roll(temp, lanes - 1, 1))
        slant = later - cooler
        second_x = pltpu.roll(temp, 15, 0) - 2.0 * temp + pltpu.roll(temp, 1, 0)
        second_z = later - 2.0 * temp + cooler
        cross = 0.25 * (pltpu.roll(slant, 15, 0) - pltpu.roll(slant, 1, 0))
        spread = xx * second_x + 2.0 * xz * cross + zz * second_z
        inverse = 1.0 / reference_temp - 1.0 / temp
        left = 1.0 - cure
        rate = rate_first * jnp.exp(energy_first * inverse) + rate_second * jnp.exp(
            energy_second * inverse
        ) * jnp.sqrt(cure)
        rate = rate * (left * jnp.sqrt(left))
        temp = temp + time_step * (spread + heat_release * rate)
        cure = cure + time_step * rate
    temp_out[...] = temp[GHOST : GHOST + count]
    cure_out[...] = cure[GHOST : GHOST + count]
    for copy in copies[1:]:
        copy.start()
    for copy in copies:
        copy.wait()


def on_device(intensity, temp_start, cure_start, tool_levels, plan):
    rows, width, depth = intensity.shape
    count, lanes = temp_start.shape
    planes, depths = lax.axis_size("plane"), lax.axis_size("depth")
    columns, cells = sizes(width, depth)
    bf16 = jnp.bfloat16
    slots = rows * EDGE + 16 * (lanes // LANES)
    params = pltpu.CompilerParams(vmem_limit_bytes=24 * 1024 * 1024)
    vmem = pl.BlockSpec(memory_space=pltpu.VMEM)
    stay = pl.BlockSpec(memory_space=pltpu.HBM)

    fixed = lambda values: pltpu.with_memory_space_constraint(values, pltpu.HBM)
    bands, coarse = x_bands(width), coarse_x_bands(width)
    late = bands.shape[1] - EARLY
    middle = bands[:, :EARLY, EDGE : EDGE + width]
    sides = bands[:, EARLY:].reshape(2 * late, -1)
    x_parts, early_starts = stacked(
        middle.reshape(2 * EARLY, -1), sides[:, EDGE : EDGE + width], coarse[:, :EARLY]
    )
    z_parts, _ = stacked(*depth_bands(depth), coarse_depth_bands(depth))
    halos = np.concatenate([sides[:, :EDGE], sides[:, EDGE + width :]], axis=1)
    x_late, late_starts = stacked(halos, coarse[:, EARLY:])
    rims = rim_bands(rows)
    flat, _ = stacked(np.concatenate([rims[0], rims[2]], axis=1))
    steep, rim_starts = stacked(rims[1], *rim_x_bands(count))
    cell_bands, _ = stacked(rim_cells(rows, depth, depths))
    far, near, temp, cure = pl.pallas_call(
        pack_kernel,
        name="pack",
        out_shape=(
            pltpu.VMEM((slots, depth), bf16),
            pltpu.VMEM((slots, depth), bf16),
            pltpu.VMEM((count, lanes), jnp.float32),
            pltpu.VMEM((count, lanes), jnp.float32),
        ),
        in_specs=[stay] * 3,
        scratch_shapes=[
            pltpu.VMEM((2, rows, EDGE, depth), jnp.int32),
            pltpu.SemaphoreType.DMA((4,)),
        ],
        compiler_params=params,
    )(*[fixed(values) for values in (intensity, temp_start, cure_start)])

    def moved(values, pairs):
        index = [(p * depths + d, q * depths + e) for (p, d), (q, e) in pairs]
        return lax.ppermute(values, ("plane", "depth"), index)

    def swapped(values, first):
        pairs = [(p, p + 1) for p in range(first, planes - 1, 2)]
        pairs += [(q, p) for p, q in pairs]
        return moved(values, [((p, d), (q, d)) for p, q in pairs for d in range(depths)])

    far = swapped(far, 1)
    near = swapped(near, 0)

    high = coarse.shape[0]

    def scratch(count):
        return [
            pltpu.VMEM((2 * count, rows * depth), jnp.float32),
            pltpu.VMEM((3 * rows // 2 * count, 2 * depth), bf16),
            pltpu.VMEM((3 * rows // 2 * count, 2 * depth), jnp.float32),
        ]

    def cost(count):
        return pl.CostEstimate(
            flops=2 * rows * (2 * count) * 160 * depth * 4,
            bytes_accessed=4_000_000,
            transcendentals=0,
        )

    early_sums, diagonal, sides, own_tiles = pl.pallas_call(
        functools.partial(early_kernel, early_starts),
        name="early",
        out_shape=(
            pltpu.VMEM((len(USED), high, LANES), jnp.float32),
            pltpu.VMEM((4 * depth, 2 * depth), bf16),
            pltpu.VMEM((2 * late, rows * depth), jnp.float32),
            pltpu.VMEM((3, width, LANES), jnp.float32),
        ),
        scratch_shapes=scratch(EARLY),
        cost_estimate=cost(EARLY),
        compiler_params=params,
    )(intensity, x_parts, z_parts)

    products_x, voxels = own_columns(count)
    at_sums, half = chunk_rows(count, lanes)
    chunk_shape = (depths, at_sums + 2 * half, LANES)
    chunks = pl.pallas_call(
        functools.partial(late_kernel, late_starts, width),
        name="late",
        out_shape=pltpu.HBM(chunk_shape, bf16),
        in_specs=[vmem] * 10,
        out_specs=stay,
        scratch_shapes=scratch(late)
        + [pltpu.VMEM(chunk_shape, bf16), pltpu.SemaphoreType.DMA((2,))],
        cost_estimate=cost(late),
        compiler_params=params,
    )(far, near, x_late, z_parts, diagonal, early_sums, sides, own_tiles, temp, cure)

    faces = plan.reshape(2 * STEPS, 1) == jnp.arange(tool_levels.shape[0], dtype=jnp.int32)
    tools = jnp.sum(
        jnp.where(faces, tool_levels, jnp.zeros_like(tool_levels)), axis=1, keepdims=True
    )

    chunks = lax.all_to_all(
        chunks,
        "depth",
        split_axis=0,
        concat_axis=0,
        tiled=True,
        axis_index_groups=[meeting_order(depths)],
    )

    return pl.pallas_call(
        functools.partial(cure_kernel, cells, rim_starts),
        name="cure",
        out_shape=(
            pltpu.HBM((count, lanes), jnp.float32),
            pltpu.HBM((count, lanes), jnp.float32),
            pltpu.HBM((3, count, lanes), jnp.float32),
        ),
        in_specs=[vmem] * 7,
        out_specs=(stay, stay, stay),
        scratch_shapes=[
            pltpu.VMEM((count, lanes), jnp.float32),
            pltpu.VMEM((count, lanes), jnp.float32),
            pltpu.VMEM((3, count, lanes), jnp.float32),
            pltpu.SemaphoreType.DMA((3,)),
        ],
        compiler_params=params,
    )(chunks, temp, cure, tools, flat, steep, cell_bands)


def solution(mesh):
    return jax.shard_map(
        on_device,
        mesh=mesh,
        in_specs=(
            P(None, "plane", "depth"),
            P(("plane", "depth"), None),
            P(("plane", "depth"), None),
            P(),
            P(),
        ),
        out_specs=(
            P(("plane", "depth"), None),
            P(("plane", "depth"), None),
            P(None, ("plane", "depth"), None),
        ),
        check_vma=False,
    )
```

```python
import functools

import jax
import jax.numpy as jnp
import ml_dtypes
import numpy as np
from jax import lax
from jax.experimental import pallas as pl
from jax.experimental.pallas import tpu as pltpu
from jax.sharding import PartitionSpec as P

ROWS = 8
R1 = 6
R2 = 10
COARSE = 4
STEPS = 3

sigma_grad = 2.0
sigma_tensor = 3.3
conduct_matrix = 0.3
conduct_fiber = 1.5
time_step = 0.25
heat_release = 0.4
rate_first = 0.15
rate_second = 0.6
energy_first = 30.0
energy_second = 25.0
reference_temp = 4.2
tensor_eps = 1e-06

LANES = 128
HALO = 2
EDGE = HALO * COARSE + R1 + R2
EARLY = 96
GHOST = 3
COLUMN_ROWS = 2 * GHOST - 1
CODE_SCALE = 2.0**20
RIM = 2 * R1
BEFORE = -(-(R2 - R1) // COARSE)
AFTER = BEFORE
HALF = LANES // 2
ROW_KINDS = (1, 0, 0)
X_KINDS = (0, 1, 0)
DEPTH_KINDS = (0, 0, 1)


def smooth_taps(radius, sigma):
    offsets = np.arange(-radius, radius + 1) * 1.0
    weights = np.exp(-0.5 * offsets * offsets / (sigma * sigma))
    return weights / weights.sum()


def slope_taps(radius, sigma):
    offsets = np.arange(-radius, radius + 1) * 1.0
    weights = np.exp(-0.5 * offsets * offsets / (sigma * sigma))
    return offsets * weights / np.sum(offsets * offsets * weights)


def row_weights(count, radius, sigma):
    taps = smooth_taps(radius, sigma)
    result = np.zeros(count)
    for source in range(count):
        for target in range(count):
            offset = target - source
            if abs(offset) <= radius:
                result[source] += taps[offset + radius]
    return result


def rounded(taps):
    best = None
    for factor in np.linspace(1.0, 2.0, 20001)[:-1]:
        near = (taps * factor).astype(np.float32).astype(ml_dtypes.bfloat16).astype(np.float64)
        error = np.abs(near / factor - taps).sum()
        if best is None or error < best[0]:
            best = (error, near, factor)
    return best[1], best[2]


def as_bfloat16(matrix):
    return matrix.astype(np.float32).astype(ml_dtypes.bfloat16)


def halves(matrix):
    high = as_bfloat16(matrix)
    return high, as_bfloat16(matrix - high.astype(np.float64))


def sizes(width, depth):
    columns = width // COARSE + 2 * HALO
    cells = depth // COARSE + BEFORE + AFTER
    return columns, cells


def product_rows(width):
    places = [*range(R1, width - R1)]
    places += [None] * max(EARLY - len(places), 0)
    places += [*range(R1 - EDGE, R1), *range(width - R1, width + EDGE - R1)]
    return places + [None] * (-len(places) % 16)


GRAD_TAPS = tuple(
    rounded(taps(R1, sigma_grad)) for taps in (smooth_taps, slope_taps)
)
GRAD_FACTOR = GRAD_TAPS[0][1] ** 2 * GRAD_TAPS[1][1]


def grad_taps(kind):
    return GRAD_TAPS[kind][0]


def tap(taps, offset):
    radius = (len(taps) - 1) // 2
    return float(taps[offset + radius]) if abs(offset) <= radius else 0.0


def x_bands(width):
    places = product_rows(width)
    bands = np.zeros((2, len(places), width + 2 * EDGE))
    for kind in range(2):
        for row, place in enumerate(places):
            if place is not None:
                first = place + EDGE - R1
                bands[kind, row, first : first + 2 * R1 + 1] = grad_taps(kind)
    return bands


def rim_bands(rows):
    bands = np.zeros((3, 3 * LANES, LANES))
    for part in range(3):
        row_taps, depth_taps = grad_taps(ROW_KINDS[part]), grad_taps(DEPTH_KINDS[part])
        for source in range(rows):
            for target in range(rows):
                row_tap = tap(row_taps, source - target)
                for near in range(-RIM, RIM):
                    lane = source * RIM + near % RIM
                    if near >= 0:
                        lane += rows * RIM + LANES
                    for place in range(-R1, R1):
                        value = row_tap * tap(depth_taps, near - place)
                        bands[part, lane, target * 2 * R1 + R1 + place] = value
    return bands


def rim_cells(rows, depth, blocks):
    taps = smooth_taps(R2, sigma_tensor)
    weights = product_weights(rows)
    bands = np.zeros((blocks - 1, LANES, blocks * depth // COARSE))
    for boundary in range(blocks - 1):
        middle = (boundary + 1) * depth
        for cell in range(bands.shape[2]):
            for voxel in range(cell * COARSE, (cell + 1) * COARSE):
                for place in range(-R1, R1):
                    value = tap(taps, middle + place - voxel)
                    for row in range(rows):
                        bands[boundary, row * 2 * R1 + R1 + place, cell] += weights[row] * value
    return bands.reshape(-1, bands.shape[2])


def meeting_order(blocks):
    middle = blocks // 2
    rest = [block for block in range(blocks) if block != middle]
    ends = [rest.pop(0 if turn % 2 == 0 else -1) for turn in range(blocks - 1)]
    return [middle, *ends]


def own_columns(count):
    products = (count + 2 * HALO) * COARSE + 2 * R2
    voxels = products + 2 * R1
    return -(-products // 16) * 16, -(-voxels // 8) * 8


def fold(voxels):
    return -(-voxels // 16) * 8


def rim_x_bands(count):
    products, voxels = own_columns(count)
    bands = np.zeros((2, products, -(-voxels // 16) * 16))
    valid = (count + 2 * HALO) * COARSE + 2 * R2
    for kind in range(2):
        for row in range(valid):
            bands[kind, row, row : row + 2 * R1 + 1] = grad_taps(kind)
    taps = smooth_taps(R2, sigma_tensor)
    coarse = np.zeros((16, products))
    for column in range(count + 2 * HALO):
        for voxel in range(column * COARSE, (column + 1) * COARSE):
            coarse[column, voxel : voxel + 2 * R2 + 1] += taps
    return bands.reshape(2 * products, -1), coarse


def depth_bands(depth):
    bands = np.zeros((2, depth, depth))
    for kind in range(2):
        for place in range(depth):
            for near in range(max(place - R1, 0), min(place + R1 + 1, depth)):
                bands[kind, near, place] = tap(grad_taps(kind), near - place)
    return bands


def product_weights(rows):
    return row_weights(rows, R2, sigma_tensor) / (255.0 * GRAD_FACTOR) ** 2


def coarse_depth_bands(depth):
    taps = smooth_taps(R2, sigma_tensor)
    columns, cells = sizes(0, depth)
    bands = np.zeros((depth, LANES))
    for cell in range(cells):
        for voxel in range(COARSE):
            place = (cell - BEFORE) * COARSE + voxel
            for near in range(max(place - R2, 0), min(place + R2 + 1, depth)):
                bands[near, cell] += tap(taps, near - place)
    return bands


def coarse_x_bands(width):
    taps = smooth_taps(R2, sigma_tensor)
    places = product_rows(width)
    columns, cells = sizes(width, 0)
    bands = np.zeros((-(-columns // 16) * 16, len(places)))
    for column in range(columns):
        for voxel in range(COARSE):
            middle = (column - HALO) * COARSE + voxel
            for row, place in enumerate(places):
                if place is not None:
                    bands[column, row] += tap(taps, place - middle)
    return bands


def stacked(*pieces):
    widest = max(piece.shape[1] for piece in pieces)
    padded = [np.pad(piece, ((0, 0), (0, widest - piece.shape[1]))) for piece in pieces]
    starts = np.cumsum([0] + [len(piece) for piece in pieces])
    return jnp.asarray(as_bfloat16(np.concatenate(padded))), tuple(int(start) for start in starts)


def two_parts(values):
    high = values.astype(jnp.bfloat16).astype(jnp.float32)
    return jnp.concatenate([high, (values - high).astype(jnp.bfloat16).astype(jnp.float32)], axis=0)


def joined(parts):
    half = parts.shape[0] // 2
    return parts[:half] + parts[half:]


def coded(values):
    values = values * CODE_SCALE
    return (values * jnp.abs(values)) * (values * values)


def decoded(values):
    size = jnp.sqrt(jnp.sqrt(jnp.abs(values))) * (1.0 / CODE_SCALE)
    return jnp.where(values < 0.0, -size, size)


def column_rows(temp, cure, at_end):
    count = temp.shape[0]
    first, second = (count - GHOST, count - GHOST + 1) if at_end else (0, 0)
    pad = jnp.zeros((8 - COLUMN_ROWS, temp.shape[1]), jnp.float32)
    return jnp.concatenate(
        [temp[first : first + GHOST, :], cure[second : second + GHOST - 1, :], pad], axis=0
    )


def chunk_rows(count, lanes):
    products, voxels = own_columns(count)
    held = count + 2 * HALO + 1 + COLUMN_ROWS * (lanes // LANES)
    return voxels + fold(voxels), -(-held // 16) * 16


def is_odd():
    return lax.rem(lax.axis_index("plane"), 2) == 1


def pack_kernel(
    intensity, temp_hbm, cure_hbm, x_hbm, z_hbm, far, near, temp, cure, x_parts, z_parts, edges,
    sems,
):
    rows, width, depth = intensity.shape
    copies = [
        pltpu.make_async_copy(
            intensity.at[:, pl.ds(place, EDGE), :], edges.at[side], sems.at[side]
        )
        for side, place in enumerate((0, width - EDGE))
    ]
    copies += [
        pltpu.make_async_copy(temp_hbm, temp, sems.at[2]),
        pltpu.make_async_copy(cure_hbm, cure, sems.at[3]),
        pltpu.make_async_copy(x_hbm, x_parts, sems.at[4]),
        pltpu.make_async_copy(z_hbm, z_parts, sems.at[5]),
    ]
    for copy in copies:
        copy.start()
    for copy in copies:
        copy.wait()
    odd = is_odd()
    sides = [
        two_parts(column_rows(temp, cure, at_end)).astype(jnp.bfloat16)
        for at_end in (False, True)
    ]

    def send(left, right):
        for side, (target, columns) in enumerate(((left, sides[0]), (right, sides[1]))):
            for pair in range(rows // 2):
                two = [edges[side, 2 * pair + i] for i in range(2)]
                two = jnp.concatenate(two, axis=0).astype(jnp.float32)
                target[2 * EDGE * pair : 2 * EDGE * (pair + 1), :] = two.astype(jnp.bfloat16)
            for slot in range(temp.shape[1] // LANES):
                at = rows * EDGE + 16 * slot
                target[at : at + 16, :] = columns[:, slot * LANES : (slot + 1) * LANES]

    @pl.when(odd)
    def _():
        send(near, far)

    @pl.when(jnp.logical_not(odd))
    def _():
        send(far, near)


def packed_rows(values, size, first):
    depth = values[0].shape[1]
    lane = lax.broadcasted_iota(jnp.int32, values[0].shape, 1)
    packed = None
    for block, value in enumerate(values):
        shift = (size * block - first) % depth
        moved = value if shift == 0 else pltpu.roll(value, shift, 1)
        packed = moved if block == 0 else jnp.where(lane >= size * block, moved, packed)
    return packed


def edges_of(ref, rows):
    two = [
        ref[2 * EDGE * pair : 2 * EDGE * (pair + 1), :].astype(jnp.float32)
        for pair in range(rows // 2)
    ]
    voxels = [two[row // 2][row % 2 * EDGE : (row % 2 + 1) * EDGE] for row in range(rows)]
    slots = range(rows * EDGE, ref.shape[0], 16)
    columns = [joined(ref[at : at + 16, :].astype(jnp.float32)) for at in slots]
    return voxels, jnp.concatenate(columns, axis=1)


def product(first, second):
    return jnp.dot(first, second, preferred_element_type=jnp.float32)


def mirrored_filter(kind, values, even):
    rows = len(values)
    use_sum = even == (kind == 0)
    sign = 1.0 if use_sum else -1.0
    half = [values[row] + sign * values[rows - 1 - row] for row in range(rows // 2)]
    results = []
    for row in range(rows // 2):
        total = None
        for source, value in enumerate(half):
            near = tap(grad_taps(kind), source - row)
            far = tap(grad_taps(kind), rows - 1 - source - row)
            weight = 0.5 * (near + sign * far)
            total = weight * value if total is None else total + weight * value
        results.append(total)
    return results


def weighted_products(three, weight):
    pairs = ((0, 0), (1, 1), (2, 2), (0, 1), (0, 2), (1, 2))
    first = [weight * value for value in three]
    return [first[a] * three[b] for a, b in pairs]


def late_mask(count, width):
    row = lax.broadcasted_iota(jnp.int32, (count, LANES), 0)
    left = max(width - 2 * R1 - EARLY, 0)
    place = jnp.where(row < left + EDGE, row - left + R1 - EDGE, row - left - EDGE + width - R1)
    place = place + lax.axis_index("plane") * width
    inside = (place >= 0) & (place < lax.axis_size("plane") * width)
    return jnp.where(inside | (row < left), 1.0, 0.0)


USED = (0, 1, 2, 5)
UNUSED = (3, 4)


def all_sums(products, coarse, sx):
    sums = [None] * 6
    for kinds in (USED, UNUSED):
        tiles = [tile for index in kinds for tile in products[index]]
        along = product(sx, jnp.concatenate(tiles, axis=1)).astype(jnp.bfloat16)
        step = along.shape[1] // len(kinds)
        parts = [along[:, index * step : (index + 1) * step] for index in range(len(kinds))]
        total = product(jnp.concatenate(parts, axis=0), coarse)
        high = sx.shape[0]
        for index, kind in enumerate(kinds):
            sums[kind] = total[index * high : (index + 1) * high]
    return sums


def tensor_sums(across, sx, mask, diagonal, z_parts, filtered, grads):
    double = diagonal.shape[1]
    depth, pairs = double // 2, across.shape[1] // double
    rows, count = 2 * pairs, across.shape[0] // 2
    for start in range(0, count, 16):
        kinds = [
            [
                across[kind * count + start : kind * count + start + 16, row * depth : (row + 1) * depth]
                for row in range(rows)
            ]
            for kind in range(2)
        ]
        for part in range(3):
            values = kinds[X_KINDS[part]]
            results = mirrored_filter(ROW_KINDS[part], values, True)
            results += mirrored_filter(ROW_KINDS[part], values, False)
            for row, result in enumerate(results):
                at = (part * pairs + row // 2) * count + start
                lanes = slice((row % 2) * depth, (row % 2 + 1) * depth)
                filtered[at : at + 16, lanes] = result.astype(jnp.bfloat16)

    at = 2 * pairs * count
    grads[:at] = product(filtered[:at, :], diagonal[0:double, :])
    grads[at:] = product(filtered[at:, :], diagonal[double : 2 * double, :])

    weights = product_weights(rows)
    layer = lax.axis_index("depth")
    first, last = layer == 0, layer == lax.axis_size("depth") - 1
    place = lax.broadcasted_iota(jnp.int32, (16, depth), 1)
    complete = ((place >= R1) | first) & ((place < depth - R1) | last)
    complete = jnp.where(complete, 1.0, 0.0)
    groups = [[] for _ in range(6)]
    for start in range(0, count, 16):
        inside = complete if mask is None else complete * mask[start : start + 16]
        totals = None
        for row in range(rows):
            lanes = slice((row % 2) * depth, (row % 2 + 1) * depth)
            three = []
            for part in range(3):
                at = (part * pairs + row // 2) * count + start
                three.append(grads[at : at + 16, lanes])
            terms = weighted_products(three, 2.0 * float(weights[row % (rows // 2)]))
            totals = terms if row == 0 else [a + b for a, b in zip(totals, terms)]
        for index in range(6):
            groups[index].append((totals[index] * inside).astype(jnp.bfloat16))
    products = [[jnp.concatenate(group, axis=0)] for group in groups]
    return all_sums(products, z_parts[double : double + depth, :], sx)


def rim_tiles(values):
    rows, depth = len(values), values[0].shape[1]
    below = packed_rows(values, RIM, depth - RIM)
    above = pltpu.roll(packed_rows(values, RIM, 0), rows * RIM, 1)
    lane = lax.broadcasted_iota(jnp.int32, below.shape, 1)
    return [jnp.where(lane < rows * RIM, below, above), above, pltpu.roll(above, HALF, 1)]


def early_kernel(
    starts, grey, x_parts, z_parts, sums, diagonal, sides, tiles, across, filtered, grads
):
    rows, width, depth = grey.shape
    double = 2 * depth
    empty = jnp.zeros((depth, depth), jnp.bfloat16)
    for kind in range(2):
        for half in range(2):
            at = pl.ds(kind * double + half * depth, depth)
            band = z_parts[kind * depth : (kind + 1) * depth, :]
            diagonal[at, half * depth : (half + 1) * depth] = band
            diagonal[at, (1 - half) * depth : (2 - half) * depth] = empty
    values = [grey[row].astype(jnp.float32) for row in range(rows)]
    whole = jnp.concatenate([value.astype(jnp.bfloat16) for value in values], axis=1)
    result = product(x_parts[starts[0] : starts[2], :width], whole)
    across[...] = result[: starts[1]]
    sides[...] = result[starts[1] :]
    sx = x_parts[starts[2] : starts[3], :EARLY]
    results = tensor_sums(across, sx, None, diagonal, z_parts, filtered, grads)
    for index, kind in enumerate(USED):
        sums[index] = results[kind]
    for index, tile in enumerate(rim_tiles(values)):
        tiles[index] = tile


def late_kernel(
    starts, width, far, near, x_late, z_parts, diagonal, early_sums, sides, own_tiles, temp, cure,
    out_hbm, across, filtered, grads, out, sems,
):
    double = diagonal.shape[1]
    depth = double // 2
    rows = across.shape[1] // depth
    count, lanes = temp.shape
    odd = is_odd()
    depths, layer = lax.axis_size("depth"), lax.axis_index("depth")
    outer, outer_columns = edges_of(far, rows)
    inner, inner_columns = edges_of(near, rows)
    values = []
    for row in range(rows):
        left = jnp.where(odd, inner[row], outer[row])
        right = jnp.where(odd, outer[row], inner[row])
        values.append(jnp.concatenate([left, right], axis=0))
    left = jnp.where(odd, inner_columns, outer_columns)
    right = jnp.where(odd, outer_columns, inner_columns)

    late = across.shape[0] // 2
    halos = jnp.concatenate([value.astype(jnp.bfloat16) for value in values], axis=1)
    across[...] = sides[...] + product(x_late[starts[0] : starts[1], : 2 * EDGE], halos)

    products_x, voxels = own_columns(count)
    folded, stride = fold(voxels), COARSE * count
    tiles = [
        jnp.concatenate([tile[:EDGE], own_tiles[index], tile[EDGE:]], axis=0)
        for index, tile in enumerate(rim_tiles(values))
    ]
    missing = stride * (depths - 1) + voxels - tiles[0].shape[0]
    if missing > 0:
        spare = jnp.zeros((-(-missing // 8) * 8, LANES), jnp.float32)
        tiles = [jnp.concatenate([tile, spare], axis=0) for tile in tiles]

    height = count + 2 * HALO
    half_lane = lax.broadcasted_iota(jnp.int32, (folded, LANES), 1) < HALF
    order = meeting_order(out.shape[0])
    for position, target in enumerate(order):
        at = stride * target
        second = jnp.where(
            half_lane,
            tiles[1][at : at + folded],
            tiles[2][at + voxels - folded : at + voxels],
        )
        rims = jnp.concatenate([tiles[0][at : at + voxels], second], axis=0)
        out[position, 0 : voxels + folded, :] = rims.astype(jnp.bfloat16)
    split = (pl.ds(0, voxels + folded), pl.ds(voxels + folded, out.shape[1] - voxels - folded))
    copies = [
        pltpu.make_async_copy(out.at[:, part, :], out_hbm.at[:, part, :], sems.at[index])
        for index, part in enumerate(split)
    ]
    copies[0].start()

    sx = x_late[starts[1] : starts[2], :late]
    results = tensor_sums(
        across, sx, late_mask(late, width), diagonal, z_parts, filtered, grads
    )
    yy, xx, zz, xz = [early_sums[index] + results[kind] for index, kind in enumerate(USED)]
    trace = yy + xx + zz
    lane = lax.broadcasted_iota(jnp.int32, trace.shape, 1)
    columns, cells = sizes(width, depth)
    tail = 4 * cells - LANES
    joint = pltpu.roll(xz, 3 * cells, 1)
    rest = jnp.where(lane < tail, joint, 0.0)
    rest = pltpu.roll(rest, 0, 1, stride=tail, stride_axis=0)
    for index, part in ((2, zz), (1, xx), (0, trace)):
        moved = part if index == 0 else pltpu.roll(part, index * cells, 1)
        joint = jnp.where(lane < (index + 1) * cells, moved, joint)

    own_first, own_last = column_rows(temp, cure, False), column_rows(temp, cure, True)
    half = chunk_rows(count, lanes)[1]
    for position, target in enumerate(order):
        piece = jnp.where(layer == target - 1, own_last, 0.0)
        piece = jnp.where(layer == target + 1, own_first, piece)
        if target == 0:
            piece = jnp.where(layer == depths - 1, left, piece)
        if target == out.shape[0] - 1:
            piece = jnp.where(layer == 0, right, piece)
        mine = slice(count * target, count * target + height)
        pieces = [coded(joint[mine]), coded(jnp.sum(rest[mine], axis=0, keepdims=True))]
        for slot in range(lanes // LANES):
            part = piece[:, slot * LANES : (slot + 1) * LANES]
            pieces += [part[:GHOST] - reference_temp, part[GHOST:COLUMN_ROWS]]
        filled = sum(part.shape[0] for part in pieces)
        if filled < half:
            pieces.append(jnp.zeros((half - filled, LANES), jnp.float32))
        out[position, voxels + folded :, :] = jnp.concatenate(pieces, axis=0).astype(jnp.bfloat16)
    copies[1].start()
    for copy in copies:
        copy.wait()


def rim_sums(chunks, count, starts, flat, steep, cells):
    parts = chunks.shape[0]
    rows_x, voxels = own_columns(count)
    folded = fold(voxels)
    tall = -(-voxels // 16) * 16
    spare = [jnp.zeros((tall - voxels, LANES), jnp.float32)] if tall > voxels else []
    tiles = []
    order = meeting_order(parts)
    for part in range(parts):
        rims = chunks[order.index(part), 0 : voxels + folded, :].astype(jnp.float32)
        second = rims[voxels:]
        second = [second[: voxels - folded], pltpu.roll(second, HALF, 1)]
        for tile in ([rims[:voxels]], second):
            tiles.append(jnp.concatenate(tile + spare, axis=0).astype(jnp.bfloat16))
    result = product(
        steep[starts[1] : starts[2], :tall], jnp.concatenate(tiles, axis=1)
    ).astype(jnp.bfloat16)
    kinds = []
    for kind in range(2):
        values = result[kind * rows_x : (kind + 1) * rows_x]
        tile = lambda index: values[:, index * LANES : (index + 1) * LANES]
        stack = [
            jnp.concatenate([tile(2 * part), tile(2 * part + 2), tile(2 * part + 3)], axis=1)
            for part in range(parts - 1)
        ]
        kinds.append(jnp.concatenate(stack, axis=0))
    both = product(kinds[0], flat[...])
    three = (both[:, :LANES], product(kinds[1], steep[starts[0] : starts[1], :]), both[:, LANES:])

    index = lax.axis_index("plane") * lax.axis_size("depth") + lax.axis_index("depth")
    total = lax.axis_size("plane") * lax.axis_size("depth") * count * COARSE
    place = lax.rem(lax.broadcasted_iota(jnp.int32, three[0].shape, 0), rows_x)
    place = place + (index * count - HALO) * COARSE - R2
    inside = jnp.where((place >= 0) & (place < total), 1.0, 0.0)
    products = [
        [
            term[part * rows_x : (part + 1) * rows_x].astype(jnp.bfloat16)
            for part in range(parts - 1)
        ]
        for term in weighted_products(three, inside)
    ]
    return all_sums(products, cells[...], steep[starts[2] : starts[3], :rows_x])


def cure_kernel(
    cells, starts, chunks, temp_in, cure_in, tools, flat, steep, rim_bands, temp_hbm, cure_hbm,
    conduct_hbm, temp_out, cure_out, conduct_out, sems,
):
    count, lanes = temp_in.shape
    parts = chunks.shape[0]
    planes, depths = lax.axis_size("plane"), lax.axis_size("depth")
    plane, layer = lax.axis_index("plane"), lax.axis_index("depth")
    height = count + 2 * HALO
    own = cells - BEFORE - AFTER
    lane = lax.broadcasted_iota(jnp.int32, (16, lanes), 1)
    row = lax.broadcasted_iota(jnp.int32, (16, lanes), 0)
    at_sums, half = chunk_rows(count, lanes)
    tail = 4 * cells - LANES
    narrow_lane = lax.broadcasted_iota(jnp.int32, (16, LANES), 1)
    order = meeting_order(parts)

    near = rim_sums(chunks, count, starts, flat, steep, rim_bands)
    sums = [near[0] + near[1] + near[2], near[1], near[2], near[5]]
    blocks = [chunks[order.index(part), at_sums:, :].astype(jnp.float32) for part in range(parts)]
    columns = [
        jnp.concatenate(
            [
                block[at : at + COLUMN_ROWS]
                for at in range(
                    height + 1, height + 1 + COLUMN_ROWS * (lanes // LANES), COLUMN_ROWS
                )
            ],
            axis=1,
        )
        for block in blocks
    ]
    blocks = [decoded(block[0:16]) for block in blocks]
    tails = [block[height : height + 1] for block in blocks]
    if parts % 8:
        tails.append(jnp.zeros((-parts % 8, LANES), jnp.float32))
    tails = jnp.concatenate(tails, axis=0)
    tails = pltpu.roll(tails, lax.rem(LANES - lax.rem(tail * count * layer, LANES), LANES), 1)
    narrow_row = lax.broadcasted_iota(jnp.int32, (16, LANES), 0)
    rests = [jnp.zeros((16, LANES), jnp.float32) for _ in range(parts)]
    for column in range(height):
        moved = pltpu.roll(tails, LANES - tail * column, 1) if column else tails
        for part in range(parts):
            rests[part] = jnp.where(narrow_row == column, moved[part : part + 1], rests[part])
    for part in range(parts):
        first_cell = own * part - BEFORE
        here = (lane >= first_cell) & (lane < first_cell + cells)
        values = blocks[part]
        joint = values[0:16]
        xz = pltpu.roll(jnp.where(narrow_lane < tail, rests[part], joint), LANES - 3 * cells, 1)
        for index in range(4):
            chunk = xz if index == 3 else joint
            if lanes > LANES:
                spare = jnp.zeros((16, lanes - LANES), jnp.float32)
                chunk = jnp.concatenate([chunk, spare], axis=1)
            shift = (first_cell - (index % 3) * cells) % lanes
            moved = chunk if shift == 0 else pltpu.roll(chunk, shift, 1)
            sums[index] = sums[index] + jnp.where(here, moved, 0.0)
    trace = sums[0]
    scale = (conduct_fiber - conduct_matrix) / (2.0 * trace + tensor_eps)
    conduct = [
        conduct_matrix + scale * (trace - sums[1]),
        -scale * sums[3],
        conduct_matrix + scale * (trace - sums[2]),
    ]
    for kind in range(3):
        conduct_out[kind] = conduct[kind][HALO : HALO + count]
    copies = [
        pltpu.make_async_copy(conduct_out, conduct_hbm, sems.at[0]),
        pltpu.make_async_copy(temp_out, temp_hbm, sems.at[1]),
        pltpu.make_async_copy(cure_out, cure_hbm, sems.at[2]),
    ]
    copies[0].start()

    before, after = columns[parts - 1], columns[0]
    for part in range(parts - 1):
        before = jnp.where(layer == part + 1, columns[part], before)
        after = jnp.where(layer == part, columns[part + 1], after)
    spare = jnp.full((16 - count - 2 * GHOST, lanes), 0.5, jnp.float32)
    temp = jnp.concatenate([
            before[:GHOST] + reference_temp,
            temp_in[...],
            after[:GHOST] + reference_temp,
            8.0 * spare,
        ], axis=0)
    cure = jnp.concatenate([spare[:1], before[GHOST:], cure_in[...], after[GHOST:], spare[:1], spare], axis=0)
    gap = GHOST - HALO
    xx, xz, zz = [pltpu.roll(part, gap, 0) for part in conduct]

    first = (plane == 0) & (layer == 0)
    last = (plane == planes - 1) & (layer == depths - 1)
    for step in range(STEPS):
        top, bottom = tools[2 * step : 2 * step + 1, :], tools[2 * step + 1 : 2 * step + 2, :]
        temp = jnp.where((row < GHOST) & first, temp[GHOST : GHOST + 1], temp)
        temp = jnp.where(
            (row >= GHOST + count) & last, temp[GHOST + count - 1 : GHOST + count], temp
        )
        cooler = jnp.where(lane == 0, top, pltpu.roll(temp, 1, 1))
        later = jnp.where(lane == lanes - 1, bottom, pltpu.roll(temp, lanes - 1, 1))
        slant = later - cooler
        second_x = pltpu.roll(temp, 15, 0) - 2.0 * temp + pltpu.roll(temp, 1, 0)
        second_z = later - 2.0 * temp + cooler
        cross = 0.25 * (pltpu.roll(slant, 15, 0) - pltpu.roll(slant, 1, 0))
        spread = xx * second_x + 2.0 * xz * cross + zz * second_z
        inverse = 1.0 / reference_temp - 1.0 / temp
        left = 1.0 - cure
        rate = rate_first * jnp.exp(energy_first * inverse) + rate_second * jnp.exp(
            energy_second * inverse
        ) * jnp.sqrt(cure)
        rate = rate * (left * jnp.sqrt(left))
        temp = temp + time_step * (spread + heat_release * rate)
        cure = cure + time_step * rate
    temp_out[...] = temp[GHOST : GHOST + count]
    cure_out[...] = cure[GHOST : GHOST + count]
    for copy in copies[1:]:
        copy.start()
    for copy in copies:
        copy.wait()


def on_device(intensity, temp_start, cure_start, tool_levels, plan):
    rows, width, depth = intensity.shape
    count, lanes = temp_start.shape
    planes, depths = lax.axis_size("plane"), lax.axis_size("depth")
    columns, cells = sizes(width, depth)
    bf16 = jnp.bfloat16
    slots = rows * EDGE + 16 * (lanes // LANES)
    params = pltpu.CompilerParams(vmem_limit_bytes=24 * 1024 * 1024)
    vmem = pl.BlockSpec(memory_space=pltpu.VMEM)
    stay = pl.BlockSpec(memory_space=pltpu.HBM)

    fixed = lambda values: pltpu.with_memory_space_constraint(values, pltpu.HBM)
    bands, coarse = x_bands(width), coarse_x_bands(width)
    late = bands.shape[1] - EARLY
    middle = bands[:, :EARLY, EDGE : EDGE + width]
    sides = bands[:, EARLY:].reshape(2 * late, -1)
    x_hbm, early_starts = stacked(
        middle.reshape(2 * EARLY, -1), sides[:, EDGE : EDGE + width], coarse[:, :EARLY]
    )
    z_hbm, _ = stacked(*depth_bands(depth), coarse_depth_bands(depth))
    halos = np.concatenate([sides[:, :EDGE], sides[:, EDGE + width :]], axis=1)
    x_late, late_starts = stacked(halos, coarse[:, EARLY:])
    rims = rim_bands(rows)
    flat, _ = stacked(np.concatenate([rims[0], rims[2]], axis=1))
    steep, rim_starts = stacked(rims[1], *rim_x_bands(count))
    cell_bands, _ = stacked(rim_cells(rows, depth, depths))
    far, near, temp, cure, x_parts, z_parts = pl.pallas_call(
        pack_kernel,
        name="pack",
        out_shape=(
            pltpu.VMEM((slots, depth), bf16),
            pltpu.VMEM((slots, depth), bf16),
            pltpu.VMEM((count, lanes), jnp.float32),
            pltpu.VMEM((count, lanes), jnp.float32),
            pltpu.VMEM(x_hbm.shape, bf16),
            pltpu.VMEM(z_hbm.shape, bf16),
        ),
        in_specs=[stay] * 5,
        scratch_shapes=[
            pltpu.VMEM((2, rows, EDGE, depth), jnp.int32),
            pltpu.SemaphoreType.DMA((6,)),
        ],
        compiler_params=params,
    )(*[fixed(values) for values in (intensity, temp_start, cure_start, x_hbm, z_hbm)])

    def moved(values, pairs):
        index = [(p * depths + d, q * depths + e) for (p, d), (q, e) in pairs]
        return lax.ppermute(values, ("plane", "depth"), index)

    def swapped(values, first):
        pairs = [(p, p + 1) for p in range(first, planes - 1, 2)]
        pairs += [(q, p) for p, q in pairs]
        return moved(values, [((p, d), (q, d)) for p, q in pairs for d in range(depths)])

    far = swapped(far, 1)
    near = swapped(near, 0)

    high = coarse.shape[0]

    def scratch(count):
        return [
            pltpu.VMEM((2 * count, rows * depth), jnp.float32),
            pltpu.VMEM((3 * rows // 2 * count, 2 * depth), bf16),
            pltpu.VMEM((3 * rows // 2 * count, 2 * depth), jnp.float32),
        ]

    def cost(count):
        return pl.CostEstimate(
            flops=2 * rows * (2 * count) * 160 * depth * 4,
            bytes_accessed=4_000_000,
            transcendentals=0,
        )

    early_sums, diagonal, sides, own_tiles = pl.pallas_call(
        functools.partial(early_kernel, early_starts),
        name="early",
        out_shape=(
            pltpu.VMEM((len(USED), high, LANES), jnp.float32),
            pltpu.VMEM((4 * depth, 2 * depth), bf16),
            pltpu.VMEM((2 * late, rows * depth), jnp.float32),
            pltpu.VMEM((3, width, LANES), jnp.float32),
        ),
        scratch_shapes=scratch(EARLY),
        cost_estimate=cost(EARLY),
        compiler_params=params,
    )(intensity, x_parts, z_parts)

    products_x, voxels = own_columns(count)
    at_sums, half = chunk_rows(count, lanes)
    chunk_shape = (depths, at_sums + half, LANES)
    chunks = pl.pallas_call(
        functools.partial(late_kernel, late_starts, width),
        name="late",
        out_shape=pltpu.HBM(chunk_shape, bf16),
        in_specs=[vmem] * 10,
        out_specs=stay,
        scratch_shapes=scratch(late)
        + [pltpu.VMEM(chunk_shape, bf16), pltpu.SemaphoreType.DMA((2,))],
        cost_estimate=cost(late),
        compiler_params=params,
    )(far, near, x_late, z_parts, diagonal, early_sums, sides, own_tiles, temp, cure)

    faces = plan.reshape(2 * STEPS, 1) == jnp.arange(tool_levels.shape[0], dtype=jnp.int32)
    tools = jnp.sum(
        jnp.where(faces, tool_levels, jnp.zeros_like(tool_levels)), axis=1, keepdims=True
    )

    chunks = lax.all_to_all(
        chunks,
        "depth",
        split_axis=0,
        concat_axis=0,
        tiled=True,
        axis_index_groups=[meeting_order(depths)],
    )

    return pl.pallas_call(
        functools.partial(cure_kernel, cells, rim_starts),
        name="cure",
        out_shape=(
            pltpu.HBM((count, lanes), jnp.float32),
            pltpu.HBM((count, lanes), jnp.float32),
            pltpu.HBM((3, count, lanes), jnp.float32),
        ),
        in_specs=[vmem] * 7,
        out_specs=(stay, stay, stay),
        scratch_shapes=[
            pltpu.VMEM((count, lanes), jnp.float32),
            pltpu.VMEM((count, lanes), jnp.float32),
            pltpu.VMEM((3, count, lanes), jnp.float32),
            pltpu.SemaphoreType.DMA((3,)),
        ],
        compiler_params=params,
    )(chunks, temp, cure, tools, flat, steep, cell_bands)


def solution(mesh):
    return jax.shard_map(
        on_device,
        mesh=mesh,
        in_specs=(
            P(None, "plane", "depth"),
            P(("plane", "depth"), None),
            P(("plane", "depth"), None),
            P(),
            P(),
        ),
        out_specs=(
            P(("plane", "depth"), None),
            P(("plane", "depth"), None),
            P(None, ("plane", "depth"), None),
        ),
        check_vma=False,
    )
```

```python
import functools

import jax
import jax.numpy as jnp
import ml_dtypes
import numpy as np
from jax import lax
from jax.experimental import pallas as pl
from jax.experimental.pallas import tpu as pltpu
from jax.sharding import PartitionSpec as P

ROWS = 8
R1 = 6
R2 = 10
COARSE = 4
STEPS = 3

sigma_grad = 2.0
sigma_tensor = 3.3
conduct_matrix = 0.3
conduct_fiber = 1.5
time_step = 0.25
heat_release = 0.4
rate_first = 0.15
rate_second = 0.6
energy_first = 30.0
energy_second = 25.0
reference_temp = 4.2
tensor_eps = 1e-06

LANES = 128
HALO = 2
EDGE = HALO * COARSE + R1 + R2
EARLY = 96
GHOST = 3
COLUMN_ROWS = 2 * GHOST - 1
RIM = 2 * R1
BEFORE = -(-(R2 - R1) // COARSE)
AFTER = BEFORE
HALF = LANES // 2
ROW_KINDS = (1, 0, 0)
X_KINDS = (0, 1, 0)
DEPTH_KINDS = (0, 0, 1)


def smooth_taps(radius, sigma):
    offsets = np.arange(-radius, radius + 1) * 1.0
    weights = np.exp(-0.5 * offsets * offsets / (sigma * sigma))
    return weights / weights.sum()


def slope_taps(radius, sigma):
    offsets = np.arange(-radius, radius + 1) * 1.0
    weights = np.exp(-0.5 * offsets * offsets / (sigma * sigma))
    return offsets * weights / np.sum(offsets * offsets * weights)


def row_weights(count, radius, sigma):
    taps = smooth_taps(radius, sigma)
    result = np.zeros(count)
    for source in range(count):
        for target in range(count):
            offset = target - source
            if abs(offset) <= radius:
                result[source] += taps[offset + radius]
    return result


def rounded(taps):
    best = None
    for factor in np.linspace(1.0, 2.0, 20001)[:-1]:
        near = (taps * factor).astype(np.float32).astype(ml_dtypes.bfloat16).astype(np.float64)
        error = np.abs(near / factor - taps).sum()
        if best is None or error < best[0]:
            best = (error, near, factor)
    return best[1], best[2]


def as_bfloat16(matrix):
    return matrix.astype(np.float32).astype(ml_dtypes.bfloat16)


def halves(matrix):
    high = as_bfloat16(matrix)
    return high, as_bfloat16(matrix - high.astype(np.float64))


def sizes(width, depth):
    columns = width // COARSE + 2 * HALO
    cells = depth // COARSE + BEFORE + AFTER
    return columns, cells


def product_rows(width):
    places = [*range(R1, width - R1)]
    places += [None] * max(EARLY - len(places), 0)
    places += [*range(R1 - EDGE, R1), *range(width - R1, width + EDGE - R1)]
    return places + [None] * (-len(places) % 16)


GRAD_TAPS = tuple(
    rounded(taps(R1, sigma_grad)) for taps in (smooth_taps, slope_taps)
)
GRAD_FACTOR = GRAD_TAPS[0][1] ** 2 * GRAD_TAPS[1][1]


def grad_taps(kind):
    return GRAD_TAPS[kind][0]


def tap(taps, offset):
    radius = (len(taps) - 1) // 2
    return float(taps[offset + radius]) if abs(offset) <= radius else 0.0


def x_bands(width):
    places = product_rows(width)
    bands = np.zeros((2, len(places), width + 2 * EDGE))
    for kind in range(2):
        for row, place in enumerate(places):
            if place is not None:
                first = place + EDGE - R1
                bands[kind, row, first : first + 2 * R1 + 1] = grad_taps(kind)
    return bands


def rim_bands(rows):
    bands = np.zeros((3, 3 * LANES, LANES))
    for part in range(3):
        row_taps, depth_taps = grad_taps(ROW_KINDS[part]), grad_taps(DEPTH_KINDS[part])
        for source in range(rows):
            for target in range(rows):
                row_tap = tap(row_taps, source - target)
                for near in range(-RIM, RIM):
                    lane = source * RIM + near % RIM
                    if near >= 0:
                        lane += rows * RIM + LANES
                    for place in range(-R1, R1):
                        value = row_tap * tap(depth_taps, near - place)
                        bands[part, lane, target * 2 * R1 + R1 + place] = value
    return bands


def rim_cells(rows, depth, blocks):
    taps = smooth_taps(R2, sigma_tensor)
    weights = product_weights(rows)
    bands = np.zeros((blocks - 1, LANES, blocks * depth // COARSE))
    for boundary in range(blocks - 1):
        middle = (boundary + 1) * depth
        for cell in range(bands.shape[2]):
            for voxel in range(cell * COARSE, (cell + 1) * COARSE):
                for place in range(-R1, R1):
                    value = tap(taps, middle + place - voxel)
                    for row in range(rows):
                        bands[boundary, row * 2 * R1 + R1 + place, cell] += weights[row] * value
    return bands.reshape(-1, bands.shape[2])


def meeting_order(blocks):
    middle = (blocks - 1) // 2
    rest = [block for block in range(blocks) if block != middle]
    ends = [rest.pop(0 if turn % 2 == 0 else -1) for turn in range(blocks - 1)]
    return [middle, *ends]


def own_columns(count):
    products = (count + 2 * HALO) * COARSE + 2 * R2
    voxels = products + 2 * R1
    return -(-products // 16) * 16, -(-voxels // 8) * 8


def fold(voxels):
    return -(-voxels // 16) * 8


def rim_x_bands(count):
    products, voxels = own_columns(count)
    bands = np.zeros((2, products, -(-voxels // 16) * 16))
    valid = (count + 2 * HALO) * COARSE + 2 * R2
    for kind in range(2):
        for row in range(valid):
            bands[kind, row, row : row + 2 * R1 + 1] = grad_taps(kind)
    taps = smooth_taps(R2, sigma_tensor)
    coarse = np.zeros((16, products))
    for column in range(count + 2 * HALO):
        for voxel in range(column * COARSE, (column + 1) * COARSE):
            coarse[column, voxel : voxel + 2 * R2 + 1] += taps
    return bands.reshape(2 * products, -1), coarse


def depth_bands(depth):
    bands = np.zeros((2, depth, depth))
    for kind in range(2):
        for place in range(depth):
            for near in range(max(place - R1, 0), min(place + R1 + 1, depth)):
                bands[kind, near, place] = tap(grad_taps(kind), near - place)
    return bands


def product_weights(rows):
    return row_weights(rows, R2, sigma_tensor) / (255.0 * GRAD_FACTOR) ** 2


def coarse_depth_bands(depth):
    taps = smooth_taps(R2, sigma_tensor)
    columns, cells = sizes(0, depth)
    bands = np.zeros((depth, LANES))
    for cell in range(cells):
        for voxel in range(COARSE):
            place = (cell - BEFORE) * COARSE + voxel
            for near in range(max(place - R2, 0), min(place + R2 + 1, depth)):
                bands[near, cell] += tap(taps, near - place)
    return bands


def coarse_x_bands(width):
    taps = smooth_taps(R2, sigma_tensor)
    places = product_rows(width)
    columns, cells = sizes(width, 0)
    bands = np.zeros((-(-columns // 16) * 16, len(places)))
    for column in range(columns):
        for voxel in range(COARSE):
            middle = (column - HALO) * COARSE + voxel
            for row, place in enumerate(places):
                if place is not None:
                    bands[column, row] += tap(taps, place - middle)
    return bands


def stacked(*pieces):
    widest = max(piece.shape[1] for piece in pieces)
    padded = [np.pad(piece, ((0, 0), (0, widest - piece.shape[1]))) for piece in pieces]
    starts = np.cumsum([0] + [len(piece) for piece in pieces])
    return jnp.asarray(as_bfloat16(np.concatenate(padded))), tuple(int(start) for start in starts)


def two_parts(values):
    high = values.astype(jnp.bfloat16).astype(jnp.float32)
    return jnp.concatenate([high, (values - high).astype(jnp.bfloat16).astype(jnp.float32)], axis=0)


def joined(parts):
    half = parts.shape[0] // 2
    return parts[:half] + parts[half:]


def column_rows(temp, cure, at_end):
    count = temp.shape[0]
    first, second = (count - GHOST, count - GHOST + 1) if at_end else (0, 0)
    pad = jnp.zeros((8 - COLUMN_ROWS, temp.shape[1]), jnp.float32)
    return jnp.concatenate(
        [temp[first : first + GHOST, :], cure[second : second + GHOST - 1, :], pad], axis=0
    )


def chunk_rows(count, lanes):
    products, voxels = own_columns(count)
    held = count + 2 * HALO + 1 + COLUMN_ROWS * (lanes // LANES)
    return voxels + fold(voxels), -(-held // 8) * 8


def is_odd():
    return lax.rem(lax.axis_index("plane"), 2) == 1


def pack_kernel(
    intensity, temp_hbm, cure_hbm, x_hbm, z_hbm, far, near, own, x_parts, z_parts, temp, cure,
    grey, sems,
):
    rows, width, depth = intensity.shape
    copies = [
        pltpu.make_async_copy(intensity, grey, sems.at[0]),
        pltpu.make_async_copy(temp_hbm, temp, sems.at[1]),
        pltpu.make_async_copy(cure_hbm, cure, sems.at[2]),
        pltpu.make_async_copy(x_hbm, x_parts, sems.at[3]),
        pltpu.make_async_copy(z_hbm, z_parts, sems.at[4]),
    ]
    for copy in copies:
        copy.start()
    for copy in copies[:3]:
        copy.wait()
    odd = is_odd()
    sides = [
        two_parts(column_rows(temp, cure, at_end)).astype(jnp.bfloat16)
        for at_end in (False, True)
    ]

    def send(left, right):
        for place, target, columns in ((0, left, sides[0]), (width - EDGE, right, sides[1])):
            for pair in range(rows // 2):
                two = [grey[2 * pair + i, place : place + EDGE, :] for i in range(2)]
                two = jnp.concatenate(two, axis=0).astype(jnp.float32)
                target[2 * EDGE * pair : 2 * EDGE * (pair + 1), :] = two.astype(jnp.bfloat16)
            for slot in range(temp.shape[1] // LANES):
                at = rows * EDGE + 16 * slot
                target[at : at + 16, :] = columns[:, slot * LANES : (slot + 1) * LANES]

    @pl.when(odd)
    def _():
        send(near, far)

    @pl.when(jnp.logical_not(odd))
    def _():
        send(far, near)

    for row in range(rows):
        half = (row % 2) * depth
        own[row // 2, :, half : half + depth] = grey[row].astype(jnp.float32).astype(jnp.bfloat16)
    for copy in copies[3:]:
        copy.wait()


def packed_rows(values, size, first):
    depth = values[0].shape[1]
    lane = lax.broadcasted_iota(jnp.int32, values[0].shape, 1)
    packed = None
    for block, value in enumerate(values):
        shift = (size * block - first) % depth
        moved = value if shift == 0 else pltpu.roll(value, shift, 1)
        packed = moved if block == 0 else jnp.where(lane >= size * block, moved, packed)
    return packed


def edges_of(ref, rows):
    two = [
        ref[2 * EDGE * pair : 2 * EDGE * (pair + 1), :].astype(jnp.float32)
        for pair in range(rows // 2)
    ]
    voxels = [two[row // 2][row % 2 * EDGE : (row % 2 + 1) * EDGE] for row in range(rows)]
    slots = range(rows * EDGE, ref.shape[0], 16)
    columns = [joined(ref[at : at + 16, :].astype(jnp.float32)) for at in slots]
    return voxels, jnp.concatenate(columns, axis=1)


def product(first, second):
    return jnp.dot(first, second, preferred_element_type=jnp.float32)


def mirrored_filter(kind, values, even):
    rows = len(values)
    use_sum = even == (kind == 0)
    sign = 1.0 if use_sum else -1.0
    half = [values[row] + sign * values[rows - 1 - row] for row in range(rows // 2)]
    results = []
    for row in range(rows // 2):
        total = None
        for source, value in enumerate(half):
            near = tap(grad_taps(kind), source - row)
            far = tap(grad_taps(kind), rows - 1 - source - row)
            weight = 0.5 * (near + sign * far)
            total = weight * value if total is None else total + weight * value
        results.append(total)
    return results


def weighted_products(three, weight):
    pairs = ((0, 0), (1, 1), (2, 2), (0, 1), (0, 2), (1, 2))
    first = [weight * value for value in three]
    return [first[a] * three[b] for a, b in pairs]


def late_mask(count, width):
    row = lax.broadcasted_iota(jnp.int32, (count, LANES), 0)
    left = max(width - 2 * R1 - EARLY, 0)
    place = jnp.where(row < left + EDGE, row - left + R1 - EDGE, row - left - EDGE + width - R1)
    place = place + lax.axis_index("plane") * width
    inside = (place >= 0) & (place < lax.axis_size("plane") * width)
    return jnp.where(inside | (row < left), 1.0, 0.0)


USED = (0, 1, 2, 5)
UNUSED = (3, 4)


def all_sums(products, coarse, sx):
    sums = [None] * 6
    for kinds in (USED, UNUSED):
        tiles = [tile for index in kinds for tile in products[index]]
        along = product(sx, jnp.concatenate(tiles, axis=1)).astype(jnp.bfloat16)
        step = along.shape[1] // len(kinds)
        parts = [along[:, index * step : (index + 1) * step] for index in range(len(kinds))]
        total = product(jnp.concatenate(parts, axis=0), coarse)
        high = sx.shape[0]
        for index, kind in enumerate(kinds):
            sums[kind] = total[index * high : (index + 1) * high]
    return sums


def tensor_sums(across, sx, mask, diagonal, z_parts, filtered, grads):
    double = diagonal.shape[1]
    depth, pairs = double // 2, across.shape[1] // double
    rows, count = 2 * pairs, across.shape[0] // 2
    for start in range(0, count, 16):
        kinds = [
            [
                across[kind * count + start : kind * count + start + 16, row * depth : (row + 1) * depth]
                for row in range(rows)
            ]
            for kind in range(2)
        ]
        for part in range(3):
            values = kinds[X_KINDS[part]]
            results = mirrored_filter(ROW_KINDS[part], values, True)
            results += mirrored_filter(ROW_KINDS[part], values, False)
            for row, result in enumerate(results):
                at = (part * pairs + row // 2) * count + start
                lanes = slice((row % 2) * depth, (row % 2 + 1) * depth)
                filtered[at : at + 16, lanes] = result.astype(jnp.bfloat16)

    at = 2 * pairs * count
    grads[:at] = product(filtered[:at, :], diagonal[0:double, :])
    grads[at:] = product(filtered[at:, :], diagonal[double : 2 * double, :])

    weights = product_weights(rows)
    layer = lax.axis_index("depth")
    first, last = layer == 0, layer == lax.axis_size("depth") - 1
    place = lax.broadcasted_iota(jnp.int32, (16, depth), 1)
    complete = ((place >= R1) | first) & ((place < depth - R1) | last)
    complete = jnp.where(complete, 1.0, 0.0)
    groups = [[] for _ in range(6)]
    for start in range(0, count, 16):
        inside = complete if mask is None else complete * mask[start : start + 16]
        totals = None
        for row in range(rows):
            lanes = slice((row % 2) * depth, (row % 2 + 1) * depth)
            three = []
            for part in range(3):
                at = (part * pairs + row // 2) * count + start
                three.append(grads[at : at + 16, lanes])
            terms = weighted_products(three, 2.0 * float(weights[row % (rows // 2)]))
            totals = terms if row == 0 else [a + b for a, b in zip(totals, terms)]
        for index in range(6):
            groups[index].append((totals[index] * inside).astype(jnp.bfloat16))
    products = [[jnp.concatenate(group, axis=0)] for group in groups]
    return all_sums(products, z_parts[double : double + depth, :], sx)


def rim_tiles(values):
    rows, depth = len(values), values[0].shape[1]
    below = packed_rows(values, RIM, depth - RIM)
    above = pltpu.roll(packed_rows(values, RIM, 0), rows * RIM, 1)
    lane = lax.broadcasted_iota(jnp.int32, below.shape, 1)
    return [jnp.where(lane < rows * RIM, below, above), above, pltpu.roll(above, HALF, 1)]


def early_kernel(
    starts, own, x_parts, z_parts, late_hbm, sums, diagonal, sides, tiles, x_late, across,
    filtered, grads, sem,
):
    copy = pltpu.make_async_copy(late_hbm, x_late, sem.at[0])
    copy.start()
    pairs, width, double = own.shape
    rows, depth = 2 * pairs, double // 2
    empty = jnp.zeros((depth, depth), jnp.bfloat16)
    for kind in range(2):
        for half in range(2):
            at = pl.ds(kind * double + half * depth, depth)
            band = z_parts[kind * depth : (kind + 1) * depth, :]
            diagonal[at, half * depth : (half + 1) * depth] = band
            diagonal[at, (1 - half) * depth : (2 - half) * depth] = empty
    whole = jnp.concatenate([own[pair] for pair in range(pairs)], axis=1)
    result = product(x_parts[starts[0] : starts[2], :width], whole)
    across[...] = result[: starts[1]]
    sides[...] = result[starts[1] :]
    sx = x_parts[starts[2] : starts[3], :EARLY]
    results = tensor_sums(across, sx, None, diagonal, z_parts, filtered, grads)
    for index, kind in enumerate(USED):
        sums[index] = results[kind]
    values = [
        own[row // 2, :, (row % 2) * depth : (row % 2 + 1) * depth].astype(jnp.float32)
        for row in range(rows)
    ]
    for index, tile in enumerate(rim_tiles(values)):
        tiles[index] = tile
    copy.wait()


def late_kernel(
    starts, width, far, near, x_late, z_parts, diagonal, early_sums, sides, own_tiles, temp, cure,
    out_hbm, across, filtered, grads, out, sems,
):
    double = diagonal.shape[1]
    depth = double // 2
    rows = across.shape[1] // depth
    count, lanes = temp.shape
    odd = is_odd()
    depths, layer = lax.axis_size("depth"), lax.axis_index("depth")
    outer, outer_columns = edges_of(far, rows)
    inner, inner_columns = edges_of(near, rows)
    values = []
    for row in range(rows):
        left = jnp.where(odd, inner[row], outer[row])
        right = jnp.where(odd, outer[row], inner[row])
        values.append(jnp.concatenate([left, right], axis=0))
    left = jnp.where(odd, inner_columns, outer_columns)
    right = jnp.where(odd, outer_columns, inner_columns)

    late = across.shape[0] // 2
    halos = jnp.concatenate([value.astype(jnp.bfloat16) for value in values], axis=1)
    across[...] = sides[...] + product(x_late[starts[0] : starts[1], : 2 * EDGE], halos)

    products_x, voxels = own_columns(count)
    folded, stride = fold(voxels), COARSE * count
    tiles = [
        jnp.concatenate([tile[:EDGE], own_tiles[index], tile[EDGE:]], axis=0)
        for index, tile in enumerate(rim_tiles(values))
    ]
    missing = stride * (depths - 1) + voxels - tiles[0].shape[0]
    if missing > 0:
        spare = jnp.zeros((-(-missing // 8) * 8, LANES), jnp.float32)
        tiles = [jnp.concatenate([tile, spare], axis=0) for tile in tiles]

    height = count + 2 * HALO
    half_lane = lax.broadcasted_iota(jnp.int32, (folded, LANES), 1) < HALF
    order = meeting_order(out.shape[0])
    for position, target in enumerate(order):
        at = stride * target
        second = jnp.where(
            half_lane,
            tiles[1][at : at + folded],
            tiles[2][at + voxels - folded : at + voxels],
        )
        rims = jnp.concatenate([tiles[0][at : at + voxels], second], axis=0)
        out[position, 0 : voxels + folded, :] = rims.astype(jnp.bfloat16)
    split = (pl.ds(0, voxels + folded), pl.ds(voxels + folded, out.shape[1] - voxels - folded))
    copies = [
        pltpu.make_async_copy(out.at[:, part, :], out_hbm.at[:, part, :], sems.at[index])
        for index, part in enumerate(split)
    ]
    copies[0].start()

    sx = x_late[starts[1] : starts[2], :late]
    results = tensor_sums(
        across, sx, late_mask(late, width), diagonal, z_parts, filtered, grads
    )
    yy, xx, zz, xz = [early_sums[index] + results[kind] for index, kind in enumerate(USED)]
    trace = yy + xx + zz
    lane = lax.broadcasted_iota(jnp.int32, trace.shape, 1)
    columns, cells = sizes(width, depth)
    tail = 4 * cells - LANES
    joint = pltpu.roll(xz, 3 * cells, 1)
    rest = jnp.where(lane < tail, joint, 0.0)
    rest = pltpu.roll(rest, 0, 1, stride=tail, stride_axis=0)
    for index, part in ((2, zz), (1, xx), (0, trace)):
        moved = part if index == 0 else pltpu.roll(part, index * cells, 1)
        joint = jnp.where(lane < (index + 1) * cells, moved, joint)

    own_first, own_last = column_rows(temp, cure, False), column_rows(temp, cure, True)
    half = chunk_rows(count, lanes)[1]
    for position, target in enumerate(order):
        piece = jnp.where(layer == target - 1, own_last, 0.0)
        piece = jnp.where(layer == target + 1, own_first, piece)
        if target == 0:
            piece = jnp.where(layer == depths - 1, left, piece)
        if target == out.shape[0] - 1:
            piece = jnp.where(layer == 0, right, piece)
        mine = slice(count * target, count * target + height)
        pieces = [joint[mine], jnp.sum(rest[mine], axis=0, keepdims=True)]
        for slot in range(lanes // LANES):
            pieces.append(piece[0:COLUMN_ROWS, slot * LANES : (slot + 1) * LANES])
        filled = sum(part.shape[0] for part in pieces)
        if filled < half:
            pieces.append(jnp.zeros((half - filled, LANES), jnp.float32))
        sent = two_parts(jnp.concatenate(pieces, axis=0))
        out[position, voxels + folded :, :] = sent.astype(jnp.bfloat16)
    copies[1].start()
    for copy in copies:
        copy.wait()


def rim_sums(chunks, count, starts, flat, steep, cells):
    parts = chunks.shape[0]
    rows_x, voxels = own_columns(count)
    folded = fold(voxels)
    tall = -(-voxels // 16) * 16
    spare = [jnp.zeros((tall - voxels, LANES), jnp.float32)] if tall > voxels else []
    tiles = []
    order = meeting_order(parts)
    for part in range(parts):
        rims = chunks[order.index(part), 0 : voxels + folded, :].astype(jnp.float32)
        second = rims[voxels:]
        second = [second[: voxels - folded], pltpu.roll(second, HALF, 1)]
        for tile in ([rims[:voxels]], second):
            tiles.append(jnp.concatenate(tile + spare, axis=0).astype(jnp.bfloat16))
    result = product(
        steep[starts[1] : starts[2], :tall], jnp.concatenate(tiles, axis=1)
    ).astype(jnp.bfloat16)
    kinds = []
    for kind in range(2):
        values = result[kind * rows_x : (kind + 1) * rows_x]
        tile = lambda index: values[:, index * LANES : (index + 1) * LANES]
        stack = [
            jnp.concatenate([tile(2 * part), tile(2 * part + 2), tile(2 * part + 3)], axis=1)
            for part in range(parts - 1)
        ]
        kinds.append(jnp.concatenate(stack, axis=0))
    both = product(kinds[0], flat[...])
    three = (both[:, :LANES], product(kinds[1], steep[starts[0] : starts[1], :]), both[:, LANES:])

    index = lax.axis_index("plane") * lax.axis_size("depth") + lax.axis_index("depth")
    total = lax.axis_size("plane") * lax.axis_size("depth") * count * COARSE
    place = lax.rem(lax.broadcasted_iota(jnp.int32, three[0].shape, 0), rows_x)
    place = place + (index * count - HALO) * COARSE - R2
    inside = jnp.where((place >= 0) & (place < total), 1.0, 0.0)
    products = [
        [
            term[part * rows_x : (part + 1) * rows_x].astype(jnp.bfloat16)
            for part in range(parts - 1)
        ]
        for term in weighted_products(three, inside)
    ]
    return all_sums(products, cells[...], steep[starts[2] : starts[3], :rows_x])


def cure_kernel(
    cells, starts, chunks, temp_in, cure_in, tools, flat, steep, rim_bands, temp_hbm, cure_hbm,
    conduct_hbm, temp_out, cure_out, conduct_out, sems,
):
    count, lanes = temp_in.shape
    parts = chunks.shape[0]
    planes, depths = lax.axis_size("plane"), lax.axis_size("depth")
    plane, layer = lax.axis_index("plane"), lax.axis_index("depth")
    height = count + 2 * HALO
    own = cells - BEFORE - AFTER
    lane = lax.broadcasted_iota(jnp.int32, (16, lanes), 1)
    row = lax.broadcasted_iota(jnp.int32, (16, lanes), 0)
    at_sums, half = chunk_rows(count, lanes)
    tail = 4 * cells - LANES
    narrow_lane = lax.broadcasted_iota(jnp.int32, (16, LANES), 1)
    order = meeting_order(parts)

    near = rim_sums(chunks, count, starts, flat, steep, rim_bands)
    sums = [near[0] + near[1] + near[2], near[1], near[2], near[5]]
    blocks = [
        joined(chunks[order.index(part), at_sums:, :].astype(jnp.float32)) for part in range(parts)
    ]
    tails = [block[height : height + 1] for block in blocks]
    if parts % 8:
        tails.append(jnp.zeros((-parts % 8, LANES), jnp.float32))
    tails = jnp.concatenate(tails, axis=0)
    tails = pltpu.roll(tails, lax.rem(LANES - lax.rem(tail * count * layer, LANES), LANES), 1)
    narrow_row = lax.broadcasted_iota(jnp.int32, (16, LANES), 0)
    rests = [jnp.zeros((16, LANES), jnp.float32) for _ in range(parts)]
    for column in range(height):
        moved = pltpu.roll(tails, LANES - tail * column, 1) if column else tails
        for part in range(parts):
            rests[part] = jnp.where(narrow_row == column, moved[part : part + 1], rests[part])
    for part in range(parts):
        first_cell = own * part - BEFORE
        here = (lane >= first_cell) & (lane < first_cell + cells)
        values = blocks[part]
        joint = values[0:16]
        xz = pltpu.roll(jnp.where(narrow_lane < tail, rests[part], joint), LANES - 3 * cells, 1)
        for index in range(4):
            chunk = xz if index == 3 else joint
            if lanes > LANES:
                spare = jnp.zeros((16, lanes - LANES), jnp.float32)
                chunk = jnp.concatenate([chunk, spare], axis=1)
            shift = (first_cell - (index % 3) * cells) % lanes
            moved = chunk if shift == 0 else pltpu.roll(chunk, shift, 1)
            sums[index] = sums[index] + jnp.where(here, moved, 0.0)
    trace = sums[0]
    scale = (conduct_fiber - conduct_matrix) / (2.0 * trace + tensor_eps)
    conduct = [
        conduct_matrix + scale * (trace - sums[1]),
        -scale * sums[3],
        conduct_matrix + scale * (trace - sums[2]),
    ]
    for kind in range(3):
        conduct_out[kind] = conduct[kind][HALO : HALO + count]
    copies = [
        pltpu.make_async_copy(conduct_out, conduct_hbm, sems.at[0]),
        pltpu.make_async_copy(temp_out, temp_hbm, sems.at[1]),
        pltpu.make_async_copy(cure_out, cure_hbm, sems.at[2]),
    ]
    copies[0].start()

    slots = range(height + 1, height + 1 + COLUMN_ROWS * (lanes // LANES), COLUMN_ROWS)
    columns = [
        jnp.concatenate([values[at : at + COLUMN_ROWS] for at in slots], axis=1) for values in blocks
    ]
    before, after = columns[parts - 1], columns[0]
    for part in range(parts - 1):
        before = jnp.where(layer == part + 1, columns[part], before)
        after = jnp.where(layer == part, columns[part + 1], after)
    spare = jnp.full((16 - count - 2 * GHOST, lanes), 0.5, jnp.float32)
    temp = jnp.concatenate([before[:GHOST], temp_in[...], after[:GHOST], 8.0 * spare], axis=0)
    cure = jnp.concatenate([spare[:1], before[GHOST:], cure_in[...], after[GHOST:], spare[:1], spare], axis=0)
    gap = GHOST - HALO
    xx, xz, zz = [pltpu.roll(part, gap, 0) for part in conduct]

    first = (plane == 0) & (layer == 0)
    last = (plane == planes - 1) & (layer == depths - 1)
    for step in range(STEPS):
        top, bottom = tools[2 * step : 2 * step + 1, :], tools[2 * step + 1 : 2 * step + 2, :]
        temp = jnp.where((row < GHOST) & first, temp[GHOST : GHOST + 1], temp)
        temp = jnp.where(
            (row >= GHOST + count) & last, temp[GHOST + count - 1 : GHOST + count], temp
        )
        cooler = jnp.where(lane == 0, top, pltpu.roll(temp, 1, 1))
        later = jnp.where(lane == lanes - 1, bottom, pltpu.roll(temp, lanes - 1, 1))
        slant = later - cooler
        second_x = pltpu.roll(temp, 15, 0) - 2.0 * temp + pltpu.roll(temp, 1, 0)
        second_z = later - 2.0 * temp + cooler
        cross = 0.25 * (pltpu.roll(slant, 15, 0) - pltpu.roll(slant, 1, 0))
        spread = xx * second_x + 2.0 * xz * cross + zz * second_z
        inverse = 1.0 / reference_temp - 1.0 / temp
        left = 1.0 - cure
        rate = rate_first * jnp.exp(energy_first * inverse) + rate_second * jnp.exp(
            energy_second * inverse
        ) * jnp.sqrt(cure)
        rate = rate * (left * jnp.sqrt(left))
        temp = temp + time_step * (spread + heat_release * rate)
        cure = cure + time_step * rate
    temp_out[...] = temp[GHOST : GHOST + count]
    cure_out[...] = cure[GHOST : GHOST + count]
    for copy in copies[1:]:
        copy.start()
    for copy in copies:
        copy.wait()


def on_device(intensity, temp_start, cure_start, tool_levels, plan):
    rows, width, depth = intensity.shape
    count, lanes = temp_start.shape
    planes, depths = lax.axis_size("plane"), lax.axis_size("depth")
    columns, cells = sizes(width, depth)
    bf16 = jnp.bfloat16
    slots = rows * EDGE + 16 * (lanes // LANES)
    params = pltpu.CompilerParams(vmem_limit_bytes=24 * 1024 * 1024)
    vmem = pl.BlockSpec(memory_space=pltpu.VMEM)
    stay = pl.BlockSpec(memory_space=pltpu.HBM)

    fixed = lambda values: pltpu.with_memory_space_constraint(values, pltpu.HBM)
    bands, coarse = x_bands(width), coarse_x_bands(width)
    late = bands.shape[1] - EARLY
    middle = bands[:, :EARLY, EDGE : EDGE + width]
    sides = bands[:, EARLY:].reshape(2 * late, -1)
    x_hbm, early_starts = stacked(
        middle.reshape(2 * EARLY, -1), sides[:, EDGE : EDGE + width], coarse[:, :EARLY]
    )
    z_hbm, _ = stacked(*depth_bands(depth), coarse_depth_bands(depth))
    halos = np.concatenate([sides[:, :EDGE], sides[:, EDGE + width :]], axis=1)
    x_late, late_starts = stacked(halos, coarse[:, EARLY:])
    rims = rim_bands(rows)
    flat, _ = stacked(np.concatenate([rims[0], rims[2]], axis=1))
    steep, rim_starts = stacked(rims[1], *rim_x_bands(count))
    cell_bands, _ = stacked(rim_cells(rows, depth, depths))
    far, near, own, x_parts, z_parts, temp, cure = pl.pallas_call(
        pack_kernel,
        name="pack",
        out_shape=(
            pltpu.VMEM((slots, depth), bf16),
            pltpu.VMEM((slots, depth), bf16),
            pltpu.VMEM((rows // 2, width, 2 * depth), bf16),
            pltpu.VMEM(x_hbm.shape, bf16),
            pltpu.VMEM(z_hbm.shape, bf16),
            pltpu.VMEM((count, lanes), jnp.float32),
            pltpu.VMEM((count, lanes), jnp.float32),
        ),
        in_specs=[stay] * 5,
        scratch_shapes=[
            pltpu.VMEM((rows, width, depth), jnp.int32),
            pltpu.SemaphoreType.DMA((5,)),
        ],
        compiler_params=params,
    )(*[fixed(values) for values in (intensity, temp_start, cure_start, x_hbm, z_hbm)])

    def moved(values, pairs):
        index = [(p * depths + d, q * depths + e) for (p, d), (q, e) in pairs]
        return lax.ppermute(values, ("plane", "depth"), index)

    def swapped(values, first):
        pairs = [(p, p + 1) for p in range(first, planes - 1, 2)]
        pairs += [(q, p) for p, q in pairs]
        return moved(values, [((p, d), (q, d)) for p, q in pairs for d in range(depths)])

    far = swapped(far, 1)
    near = swapped(near, 0)

    high = coarse.shape[0]

    def scratch(count):
        return [
            pltpu.VMEM((2 * count, rows * depth), jnp.float32),
            pltpu.VMEM((3 * rows // 2 * count, 2 * depth), bf16),
            pltpu.VMEM((3 * rows // 2 * count, 2 * depth), jnp.float32),
        ]

    def cost(count):
        return pl.CostEstimate(
            flops=2 * rows * (2 * count) * 160 * depth * 4,
            bytes_accessed=4_000_000,
            transcendentals=0,
        )

    early_sums, diagonal, sides, own_tiles, x_late = pl.pallas_call(
        functools.partial(early_kernel, early_starts),
        name="early",
        out_shape=(
            pltpu.VMEM((len(USED), high, LANES), jnp.float32),
            pltpu.VMEM((4 * depth, 2 * depth), bf16),
            pltpu.VMEM((2 * late, rows * depth), jnp.float32),
            pltpu.VMEM((3, width, LANES), jnp.float32),
            pltpu.VMEM(x_late.shape, bf16),
        ),
        in_specs=[vmem] * 3 + [stay],
        scratch_shapes=scratch(EARLY) + [pltpu.SemaphoreType.DMA((1,))],
        cost_estimate=cost(EARLY),
        compiler_params=params,
    )(own, x_parts, z_parts, fixed(x_late))

    products_x, voxels = own_columns(count)
    at_sums, half = chunk_rows(count, lanes)
    chunk_shape = (depths, at_sums + 2 * half, LANES)
    chunks = pl.pallas_call(
        functools.partial(late_kernel, late_starts, width),
        name="late",
        out_shape=pltpu.HBM(chunk_shape, bf16),
        in_specs=[vmem] * 10,
        out_specs=stay,
        scratch_shapes=scratch(late)
        + [pltpu.VMEM(chunk_shape, bf16), pltpu.SemaphoreType.DMA((2,))],
        cost_estimate=cost(late),
        compiler_params=params,
    )(far, near, x_late, z_parts, diagonal, early_sums, sides, own_tiles, temp, cure)

    faces = plan.reshape(2 * STEPS, 1) == jnp.arange(tool_levels.shape[0], dtype=jnp.int32)
    tools = jnp.sum(
        jnp.where(faces, tool_levels, jnp.zeros_like(tool_levels)), axis=1, keepdims=True
    )

    chunks = lax.all_to_all(
        chunks,
        "depth",
        split_axis=0,
        concat_axis=0,
        tiled=True,
        axis_index_groups=[meeting_order(depths)],
    )

    return pl.pallas_call(
        functools.partial(cure_kernel, cells, rim_starts),
        name="cure",
        out_shape=(
            pltpu.HBM((count, lanes), jnp.float32),
            pltpu.HBM((count, lanes), jnp.float32),
            pltpu.HBM((3, count, lanes), jnp.float32),
        ),
        in_specs=[vmem] * 7,
        out_specs=(stay, stay, stay),
        scratch_shapes=[
            pltpu.VMEM((count, lanes), jnp.float32),
            pltpu.VMEM((count, lanes), jnp.float32),
            pltpu.VMEM((3, count, lanes), jnp.float32),
            pltpu.SemaphoreType.DMA((3,)),
        ],
        compiler_params=params,
    )(chunks, temp, cure, tools, flat, steep, cell_bands)


def solution(mesh):
    return jax.shard_map(
        on_device,
        mesh=mesh,
        in_specs=(
            P(None, "plane", "depth"),
            P(("plane", "depth"), None),
            P(("plane", "depth"), None),
            P(),
            P(),
        ),
        out_specs=(
            P(("plane", "depth"), None),
            P(("plane", "depth"), None),
            P(None, ("plane", "depth"), None),
        ),
        check_vma=False,
    )
```

```python
import functools

import jax
import jax.numpy as jnp
import ml_dtypes
import numpy as np
from jax import lax
from jax.experimental import pallas as pl
from jax.experimental.pallas import tpu as pltpu
from jax.sharding import PartitionSpec as P

ROWS = 8
R1 = 6
R2 = 10
COARSE = 4
STEPS = 3

sigma_grad = 2.0
sigma_tensor = 3.3
conduct_matrix = 0.3
conduct_fiber = 1.5
time_step = 0.25
heat_release = 0.4
rate_first = 0.15
rate_second = 0.6
energy_first = 30.0
energy_second = 25.0
reference_temp = 4.2
tensor_eps = 1e-06

LANES = 128
HALO = 2
EDGE = HALO * COARSE + R1 + R2
EARLY = 96
GHOST = 3
COLUMN_ROWS = 2 * GHOST - 1
RIM = 2 * R1
BEFORE = -(-(R2 - R1) // COARSE)
AFTER = BEFORE
HALF = LANES // 2
ROW_KINDS = (1, 0, 0)
X_KINDS = (0, 1, 0)
DEPTH_KINDS = (0, 0, 1)


def smooth_taps(radius, sigma):
    offsets = np.arange(-radius, radius + 1) * 1.0
    weights = np.exp(-0.5 * offsets * offsets / (sigma * sigma))
    return weights / weights.sum()


def slope_taps(radius, sigma):
    offsets = np.arange(-radius, radius + 1) * 1.0
    weights = np.exp(-0.5 * offsets * offsets / (sigma * sigma))
    return offsets * weights / np.sum(offsets * offsets * weights)


def row_weights(count, radius, sigma):
    taps = smooth_taps(radius, sigma)
    result = np.zeros(count)
    for source in range(count):
        for target in range(count):
            offset = target - source
            if abs(offset) <= radius:
                result[source] += taps[offset + radius]
    return result


def rounded(taps):
    best = None
    for factor in np.linspace(1.0, 2.0, 20001)[:-1]:
        near = (taps * factor).astype(np.float32).astype(ml_dtypes.bfloat16).astype(np.float64)
        error = np.abs(near / factor - taps).sum()
        if best is None or error < best[0]:
            best = (error, near, factor)
    return best[1], best[2]


def as_bfloat16(matrix):
    return matrix.astype(np.float32).astype(ml_dtypes.bfloat16)


def halves(matrix):
    high = as_bfloat16(matrix)
    return high, as_bfloat16(matrix - high.astype(np.float64))


def sizes(width, depth):
    columns = width // COARSE + 2 * HALO
    cells = depth // COARSE + BEFORE + AFTER
    return columns, cells


def product_rows(width):
    places = [*range(R1, width - R1)]
    places += [None] * max(EARLY - len(places), 0)
    places += [*range(R1 - EDGE, R1), *range(width - R1, width + EDGE - R1)]
    return places + [None] * (-len(places) % 16)


GRAD_TAPS = tuple(
    rounded(taps(R1, sigma_grad)) for taps in (smooth_taps, slope_taps)
)
GRAD_FACTOR = GRAD_TAPS[0][1] ** 2 * GRAD_TAPS[1][1]


def grad_taps(kind):
    return GRAD_TAPS[kind][0]


def tap(taps, offset):
    radius = (len(taps) - 1) // 2
    return float(taps[offset + radius]) if abs(offset) <= radius else 0.0


def x_bands(width):
    places = product_rows(width)
    bands = np.zeros((2, len(places), width + 2 * EDGE))
    for kind in range(2):
        for row, place in enumerate(places):
            if place is not None:
                first = place + EDGE - R1
                bands[kind, row, first : first + 2 * R1 + 1] = grad_taps(kind)
    return bands


def rim_bands(rows):
    bands = np.zeros((3, 3 * LANES, LANES))
    for part in range(3):
        row_taps, depth_taps = grad_taps(ROW_KINDS[part]), grad_taps(DEPTH_KINDS[part])
        for source in range(rows):
            for target in range(rows):
                row_tap = tap(row_taps, source - target)
                for near in range(-RIM, RIM):
                    lane = source * RIM + near % RIM
                    if near >= 0:
                        lane += rows * RIM + LANES
                    for place in range(-R1, R1):
                        value = row_tap * tap(depth_taps, near - place)
                        bands[part, lane, target * 2 * R1 + R1 + place] = value
    return bands


def rim_cells(rows, depth, blocks):
    taps = smooth_taps(R2, sigma_tensor)
    weights = product_weights(rows)
    bands = np.zeros((blocks - 1, LANES, blocks * depth // COARSE))
    for boundary in range(blocks - 1):
        middle = (boundary + 1) * depth
        for cell in range(bands.shape[2]):
            for voxel in range(cell * COARSE, (cell + 1) * COARSE):
                for place in range(-R1, R1):
                    value = tap(taps, middle + place - voxel)
                    for row in range(rows):
                        bands[boundary, row * 2 * R1 + R1 + place, cell] += weights[row] * value
    return bands.reshape(-1, bands.shape[2])


def meeting_order(blocks):
    middle = blocks // 2
    return [*range(middle, blocks), *range(middle)]


def own_columns(count):
    products = (count + 2 * HALO) * COARSE + 2 * R2
    voxels = products + 2 * R1
    return -(-products // 16) * 16, -(-voxels // 8) * 8


def fold(voxels):
    return -(-voxels // 16) * 8


def rim_x_bands(count):
    products, voxels = own_columns(count)
    bands = np.zeros((2, products, -(-voxels // 16) * 16))
    valid = (count + 2 * HALO) * COARSE + 2 * R2
    for kind in range(2):
        for row in range(valid):
            bands[kind, row, row : row + 2 * R1 + 1] = grad_taps(kind)
    taps = smooth_taps(R2, sigma_tensor)
    coarse = np.zeros((16, products))
    for column in range(count + 2 * HALO):
        for voxel in range(column * COARSE, (column + 1) * COARSE):
            coarse[column, voxel : voxel + 2 * R2 + 1] += taps
    return bands.reshape(2 * products, -1), coarse


def depth_bands(depth):
    bands = np.zeros((2, depth, depth))
    for kind in range(2):
        for place in range(depth):
            for near in range(max(place - R1, 0), min(place + R1 + 1, depth)):
                bands[kind, near, place] = tap(grad_taps(kind), near - place)
    return bands


def product_weights(rows):
    return row_weights(rows, R2, sigma_tensor) / (255.0 * GRAD_FACTOR) ** 2


def coarse_depth_bands(depth):
    taps = smooth_taps(R2, sigma_tensor)
    columns, cells = sizes(0, depth)
    bands = np.zeros((depth, LANES))
    for cell in range(cells):
        for voxel in range(COARSE):
            place = (cell - BEFORE) * COARSE + voxel
            for near in range(max(place - R2, 0), min(place + R2 + 1, depth)):
                bands[near, cell] += tap(taps, near - place)
    return bands


def coarse_x_bands(width):
    taps = smooth_taps(R2, sigma_tensor)
    places = product_rows(width)
    columns, cells = sizes(width, 0)
    bands = np.zeros((-(-columns // 16) * 16, len(places)))
    for column in range(columns):
        for voxel in range(COARSE):
            middle = (column - HALO) * COARSE + voxel
            for row, place in enumerate(places):
                if place is not None:
                    bands[column, row] += tap(taps, place - middle)
    return bands


def stacked(*pieces):
    widest = max(piece.shape[1] for piece in pieces)
    padded = [np.pad(piece, ((0, 0), (0, widest - piece.shape[1]))) for piece in pieces]
    starts = np.cumsum([0] + [len(piece) for piece in pieces])
    return jnp.asarray(as_bfloat16(np.concatenate(padded))), tuple(int(start) for start in starts)


def two_parts(values):
    high = values.astype(jnp.bfloat16).astype(jnp.float32)
    return jnp.concatenate([high, (values - high).astype(jnp.bfloat16).astype(jnp.float32)], axis=0)


def joined(parts):
    half = parts.shape[0] // 2
    return parts[:half] + parts[half:]


def column_rows(temp, cure, at_end):
    count = temp.shape[0]
    first, second = (count - GHOST, count - GHOST + 1) if at_end else (0, 0)
    pad = jnp.zeros((8 - COLUMN_ROWS, temp.shape[1]), jnp.float32)
    return jnp.concatenate(
        [temp[first : first + GHOST, :], cure[second : second + GHOST - 1, :], pad], axis=0
    )


def chunk_rows(count, lanes):
    products, voxels = own_columns(count)
    held = count + 2 * HALO + 1 + COLUMN_ROWS * (lanes // LANES)
    return voxels + fold(voxels), -(-held // 8) * 8


def is_odd():
    return lax.rem(lax.axis_index("plane"), 2) == 1


def pack_kernel(
    intensity, temp_hbm, cure_hbm, x_hbm, z_hbm, far, near, own, x_parts, z_parts, temp, cure,
    grey, sems,
):
    rows, width, depth = intensity.shape
    copies = [
        pltpu.make_async_copy(intensity, grey, sems.at[0]),
        pltpu.make_async_copy(temp_hbm, temp, sems.at[1]),
        pltpu.make_async_copy(cure_hbm, cure, sems.at[2]),
        pltpu.make_async_copy(x_hbm, x_parts, sems.at[3]),
        pltpu.make_async_copy(z_hbm, z_parts, sems.at[4]),
    ]
    for copy in copies:
        copy.start()
    for copy in copies[:3]:
        copy.wait()
    odd = is_odd()
    sides = [
        two_parts(column_rows(temp, cure, at_end)).astype(jnp.bfloat16)
        for at_end in (False, True)
    ]

    def send(left, right):
        for place, target, columns in ((0, left, sides[0]), (width - EDGE, right, sides[1])):
            for pair in range(rows // 2):
                two = [grey[2 * pair + i, place : place + EDGE, :] for i in range(2)]
                two = jnp.concatenate(two, axis=0).astype(jnp.float32)
                target[2 * EDGE * pair : 2 * EDGE * (pair + 1), :] = two.astype(jnp.bfloat16)
            for slot in range(temp.shape[1] // LANES):
                at = rows * EDGE + 16 * slot
                target[at : at + 16, :] = columns[:, slot * LANES : (slot + 1) * LANES]

    @pl.when(odd)
    def _():
        send(near, far)

    @pl.when(jnp.logical_not(odd))
    def _():
        send(far, near)

    for row in range(rows):
        half = (row % 2) * depth
        own[row // 2, :, half : half + depth] = grey[row].astype(jnp.float32).astype(jnp.bfloat16)
    for copy in copies[3:]:
        copy.wait()


def packed_rows(values, size, first):
    depth = values[0].shape[1]
    lane = lax.broadcasted_iota(jnp.int32, values[0].shape, 1)
    packed = None
    for block, value in enumerate(values):
        shift = (size * block - first) % depth
        moved = value if shift == 0 else pltpu.roll(value, shift, 1)
        packed = moved if block == 0 else jnp.where(lane >= size * block, moved, packed)
    return packed


def edges_of(ref, rows):
    two = [
        ref[2 * EDGE * pair : 2 * EDGE * (pair + 1), :].astype(jnp.float32)
        for pair in range(rows // 2)
    ]
    voxels = [two[row // 2][row % 2 * EDGE : (row % 2 + 1) * EDGE] for row in range(rows)]
    slots = range(rows * EDGE, ref.shape[0], 16)
    columns = [joined(ref[at : at + 16, :].astype(jnp.float32)) for at in slots]
    return voxels, jnp.concatenate(columns, axis=1)


def product(first, second):
    return jnp.dot(first, second, preferred_element_type=jnp.float32)


def mirrored_filter(kind, values, even):
    rows = len(values)
    use_sum = even == (kind == 0)
    sign = 1.0 if use_sum else -1.0
    half = [values[row] + sign * values[rows - 1 - row] for row in range(rows // 2)]
    results = []
    for row in range(rows // 2):
        total = None
        for source, value in enumerate(half):
            near = tap(grad_taps(kind), source - row)
            far = tap(grad_taps(kind), rows - 1 - source - row)
            weight = 0.5 * (near + sign * far)
            total = weight * value if total is None else total + weight * value
        results.append(total)
    return results


def weighted_products(three, weight):
    pairs = ((0, 0), (1, 1), (2, 2), (0, 1), (0, 2), (1, 2))
    first = [weight * value for value in three]
    return [first[a] * three[b] for a, b in pairs]


def late_mask(count, width):
    row = lax.broadcasted_iota(jnp.int32, (count, LANES), 0)
    left = max(width - 2 * R1 - EARLY, 0)
    place = jnp.where(row < left + EDGE, row - left + R1 - EDGE, row - left - EDGE + width - R1)
    place = place + lax.axis_index("plane") * width
    inside = (place >= 0) & (place < lax.axis_size("plane") * width)
    return jnp.where(inside | (row < left), 1.0, 0.0)


USED = (0, 1, 2, 5)
UNUSED = (3, 4)


def all_sums(products, coarse, sx):
    sums = [None] * 6
    for kinds in (USED, UNUSED):
        tiles = [tile for index in kinds for tile in products[index]]
        along = product(sx, jnp.concatenate(tiles, axis=1)).astype(jnp.bfloat16)
        step = along.shape[1] // len(kinds)
        parts = [along[:, index * step : (index + 1) * step] for index in range(len(kinds))]
        total = product(jnp.concatenate(parts, axis=0), coarse)
        high = sx.shape[0]
        for index, kind in enumerate(kinds):
            sums[kind] = total[index * high : (index + 1) * high]
    return sums


def tensor_sums(across, sx, mask, diagonal, z_parts, filtered, grads):
    double = diagonal.shape[1]
    depth, pairs = double // 2, across.shape[1] // double
    rows, count = 2 * pairs, across.shape[0] // 2
    for start in range(0, count, 16):
        kinds = [
            [
                across[kind * count + start : kind * count + start + 16, row * depth : (row + 1) * depth]
                for row in range(rows)
            ]
            for kind in range(2)
        ]
        for part in range(3):
            values = kinds[X_KINDS[part]]
            results = mirrored_filter(ROW_KINDS[part], values, True)
            results += mirrored_filter(ROW_KINDS[part], values, False)
            for row, result in enumerate(results):
                at = (part * pairs + row // 2) * count + start
                lanes = slice((row % 2) * depth, (row % 2 + 1) * depth)
                filtered[at : at + 16, lanes] = result.astype(jnp.bfloat16)

    at = 2 * pairs * count
    grads[:at] = product(filtered[:at, :], diagonal[0:double, :])
    grads[at:] = product(filtered[at:, :], diagonal[double : 2 * double, :])

    weights = product_weights(rows)
    layer = lax.axis_index("depth")
    first, last = layer == 0, layer == lax.axis_size("depth") - 1
    place = lax.broadcasted_iota(jnp.int32, (16, depth), 1)
    complete = ((place >= R1) | first) & ((place < depth - R1) | last)
    complete = jnp.where(complete, 1.0, 0.0)
    groups = [[] for _ in range(6)]
    for start in range(0, count, 16):
        inside = complete if mask is None else complete * mask[start : start + 16]
        totals = None
        for row in range(rows):
            lanes = slice((row % 2) * depth, (row % 2 + 1) * depth)
            three = []
            for part in range(3):
                at = (part * pairs + row // 2) * count + start
                three.append(grads[at : at + 16, lanes])
            terms = weighted_products(three, 2.0 * float(weights[row % (rows // 2)]))
            totals = terms if row == 0 else [a + b for a, b in zip(totals, terms)]
        for index in range(6):
            groups[index].append((totals[index] * inside).astype(jnp.bfloat16))
    products = [[jnp.concatenate(group, axis=0)] for group in groups]
    return all_sums(products, z_parts[double : double + depth, :], sx)


def rim_tiles(values):
    rows, depth = len(values), values[0].shape[1]
    below = packed_rows(values, RIM, depth - RIM)
    above = pltpu.roll(packed_rows(values, RIM, 0), rows * RIM, 1)
    lane = lax.broadcasted_iota(jnp.int32, below.shape, 1)
    return [jnp.where(lane < rows * RIM, below, above), above, pltpu.roll(above, HALF, 1)]


def early_kernel(
    starts, own, x_parts, z_parts, late_hbm, sums, diagonal, sides, tiles, x_late, across,
    filtered, grads, sem,
):
    copy = pltpu.make_async_copy(late_hbm, x_late, sem.at[0])
    copy.start()
    pairs, width, double = own.shape
    rows, depth = 2 * pairs, double // 2
    empty = jnp.zeros((depth, depth), jnp.bfloat16)
    for kind in range(2):
        for half in range(2):
            at = pl.ds(kind * double + half * depth, depth)
            band = z_parts[kind * depth : (kind + 1) * depth, :]
            diagonal[at, half * depth : (half + 1) * depth] = band
            diagonal[at, (1 - half) * depth : (2 - half) * depth] = empty
    whole = jnp.concatenate([own[pair] for pair in range(pairs)], axis=1)
    result = product(x_parts[starts[0] : starts[2], :width], whole)
    across[...] = result[: starts[1]]
    sides[...] = result[starts[1] :]
    sx = x_parts[starts[2] : starts[3], :EARLY]
    results = tensor_sums(across, sx, None, diagonal, z_parts, filtered, grads)
    for index, kind in enumerate(USED):
        sums[index] = results[kind]
    values = [
        own[row // 2, :, (row % 2) * depth : (row % 2 + 1) * depth].astype(jnp.float32)
        for row in range(rows)
    ]
    for index, tile in enumerate(rim_tiles(values)):
        tiles[index] = tile
    copy.wait()


def late_kernel(
    starts, width, far, near, x_late, z_parts, diagonal, early_sums, sides, own_tiles, temp, cure,
    out_hbm, across, filtered, grads, out, sems,
):
    double = diagonal.shape[1]
    depth = double // 2
    rows = across.shape[1] // depth
    count, lanes = temp.shape
    odd = is_odd()
    depths, layer = lax.axis_size("depth"), lax.axis_index("depth")
    outer, outer_columns = edges_of(far, rows)
    inner, inner_columns = edges_of(near, rows)
    values = []
    for row in range(rows):
        left = jnp.where(odd, inner[row], outer[row])
        right = jnp.where(odd, outer[row], inner[row])
        values.append(jnp.concatenate([left, right], axis=0))
    left = jnp.where(odd, inner_columns, outer_columns)
    right = jnp.where(odd, outer_columns, inner_columns)

    late = across.shape[0] // 2
    halos = jnp.concatenate([value.astype(jnp.bfloat16) for value in values], axis=1)
    across[...] = sides[...] + product(x_late[starts[0] : starts[1], : 2 * EDGE], halos)

    products_x, voxels = own_columns(count)
    folded, stride = fold(voxels), COARSE * count
    tiles = [
        jnp.concatenate([tile[:EDGE], own_tiles[index], tile[EDGE:]], axis=0)
        for index, tile in enumerate(rim_tiles(values))
    ]
    missing = stride * (depths - 1) + voxels - tiles[0].shape[0]
    if missing > 0:
        spare = jnp.zeros((-(-missing // 8) * 8, LANES), jnp.float32)
        tiles = [jnp.concatenate([tile, spare], axis=0) for tile in tiles]

    height = count + 2 * HALO
    half_lane = lax.broadcasted_iota(jnp.int32, (folded, LANES), 1) < HALF
    order = meeting_order(out.shape[0])
    for position, target in enumerate(order):
        at = stride * target
        second = jnp.where(
            half_lane,
            tiles[1][at : at + folded],
            tiles[2][at + voxels - folded : at + voxels],
        )
        rims = jnp.concatenate([tiles[0][at : at + voxels], second], axis=0)
        out[position, 0 : voxels + folded, :] = rims.astype(jnp.bfloat16)
    split = (pl.ds(0, voxels + folded), pl.ds(voxels + folded, out.shape[1] - voxels - folded))
    copies = [
        pltpu.make_async_copy(out.at[:, part, :], out_hbm.at[:, part, :], sems.at[index])
        for index, part in enumerate(split)
    ]
    copies[0].start()

    sx = x_late[starts[1] : starts[2], :late]
    results = tensor_sums(
        across, sx, late_mask(late, width), diagonal, z_parts, filtered, grads
    )
    yy, xx, zz, xz = [early_sums[index] + results[kind] for index, kind in enumerate(USED)]
    trace = yy + xx + zz
    lane = lax.broadcasted_iota(jnp.int32, trace.shape, 1)
    columns, cells = sizes(width, depth)
    tail = 4 * cells - LANES
    joint = pltpu.roll(xz, 3 * cells, 1)
    rest = jnp.where(lane < tail, joint, 0.0)
    rest = pltpu.roll(rest, 0, 1, stride=tail, stride_axis=0)
    for index, part in ((2, zz), (1, xx), (0, trace)):
        moved = part if index == 0 else pltpu.roll(part, index * cells, 1)
        joint = jnp.where(lane < (index + 1) * cells, moved, joint)

    own_first, own_last = column_rows(temp, cure, False), column_rows(temp, cure, True)
    half = chunk_rows(count, lanes)[1]
    for position, target in enumerate(order):
        piece = jnp.where(layer == target - 1, own_last, 0.0)
        piece = jnp.where(layer == target + 1, own_first, piece)
        if target == 0:
            piece = jnp.where(layer == depths - 1, left, piece)
        if target == out.shape[0] - 1:
            piece = jnp.where(layer == 0, right, piece)
        mine = slice(count * target, count * target + height)
        pieces = [joint[mine], jnp.sum(rest[mine], axis=0, keepdims=True)]
        for slot in range(lanes // LANES):
            pieces.append(piece[0:COLUMN_ROWS, slot * LANES : (slot + 1) * LANES])
        filled = sum(part.shape[0] for part in pieces)
        if filled < half:
            pieces.append(jnp.zeros((half - filled, LANES), jnp.float32))
        sent = two_parts(jnp.concatenate(pieces, axis=0))
        out[position, voxels + folded :, :] = sent.astype(jnp.bfloat16)
    copies[1].start()
    for copy in copies:
        copy.wait()


def rim_sums(chunks, count, starts, flat, steep, cells):
    parts = chunks.shape[0]
    rows_x, voxels = own_columns(count)
    folded = fold(voxels)
    tall = -(-voxels // 16) * 16
    spare = [jnp.zeros((tall - voxels, LANES), jnp.float32)] if tall > voxels else []
    tiles = []
    order = meeting_order(parts)
    for part in range(parts):
        rims = chunks[order.index(part), 0 : voxels + folded, :].astype(jnp.float32)
        second = rims[voxels:]
        second = [second[: voxels - folded], pltpu.roll(second, HALF, 1)]
        for tile in ([rims[:voxels]], second):
            tiles.append(jnp.concatenate(tile + spare, axis=0).astype(jnp.bfloat16))
    result = product(
        steep[starts[1] : starts[2], :tall], jnp.concatenate(tiles, axis=1)
    ).astype(jnp.bfloat16)
    kinds = []
    for kind in range(2):
        values = result[kind * rows_x : (kind + 1) * rows_x]
        tile = lambda index: values[:, index * LANES : (index + 1) * LANES]
        stack = [
            jnp.concatenate([tile(2 * part), tile(2 * part + 2), tile(2 * part + 3)], axis=1)
            for part in range(parts - 1)
        ]
        kinds.append(jnp.concatenate(stack, axis=0))
    both = product(kinds[0], flat[...])
    three = (both[:, :LANES], product(kinds[1], steep[starts[0] : starts[1], :]), both[:, LANES:])

    index = lax.axis_index("plane") * lax.axis_size("depth") + lax.axis_index("depth")
    total = lax.axis_size("plane") * lax.axis_size("depth") * count * COARSE
    place = lax.rem(lax.broadcasted_iota(jnp.int32, three[0].shape, 0), rows_x)
    place = place + (index * count - HALO) * COARSE - R2
    inside = jnp.where((place >= 0) & (place < total), 1.0, 0.0)
    products = [
        [
            term[part * rows_x : (part + 1) * rows_x].astype(jnp.bfloat16)
            for part in range(parts - 1)
        ]
        for term in weighted_products(three, inside)
    ]
    return all_sums(products, cells[...], steep[starts[2] : starts[3], :rows_x])


def cure_kernel(
    cells, starts, chunks, temp_in, cure_in, tools, flat, steep, rim_bands, temp_hbm, cure_hbm,
    conduct_hbm, temp_out, cure_out, conduct_out, sems,
):
    count, lanes = temp_in.shape
    parts = chunks.shape[0]
    planes, depths = lax.axis_size("plane"), lax.axis_size("depth")
    plane, layer = lax.axis_index("plane"), lax.axis_index("depth")
    height = count + 2 * HALO
    own = cells - BEFORE - AFTER
    lane = lax.broadcasted_iota(jnp.int32, (16, lanes), 1)
    row = lax.broadcasted_iota(jnp.int32, (16, lanes), 0)
    at_sums, half = chunk_rows(count, lanes)
    tail = 4 * cells - LANES
    narrow_lane = lax.broadcasted_iota(jnp.int32, (16, LANES), 1)
    order = meeting_order(parts)

    near = rim_sums(chunks, count, starts, flat, steep, rim_bands)
    sums = [near[0] + near[1] + near[2], near[1], near[2], near[5]]
    blocks = [
        joined(chunks[order.index(part), at_sums:, :].astype(jnp.float32)) for part in range(parts)
    ]
    tails = [block[height : height + 1] for block in blocks]
    if parts % 8:
        tails.append(jnp.zeros((-parts % 8, LANES), jnp.float32))
    tails = jnp.concatenate(tails, axis=0)
    tails = pltpu.roll(tails, lax.rem(LANES - lax.rem(tail * count * layer, LANES), LANES), 1)
    narrow_row = lax.broadcasted_iota(jnp.int32, (16, LANES), 0)
    rests = [jnp.zeros((16, LANES), jnp.float32) for _ in range(parts)]
    for column in range(height):
        moved = pltpu.roll(tails, LANES - tail * column, 1) if column else tails
        for part in range(parts):
            rests[part] = jnp.where(narrow_row == column, moved[part : part + 1], rests[part])
    for part in range(parts):
        first_cell = own * part - BEFORE
        here = (lane >= first_cell) & (lane < first_cell + cells)
        values = blocks[part]
        joint = values[0:16]
        xz = pltpu.roll(jnp.where(narrow_lane < tail, rests[part], joint), LANES - 3 * cells, 1)
        for index in range(4):
            chunk = xz if index == 3 else joint
            if lanes > LANES:
                spare = jnp.zeros((16, lanes - LANES), jnp.float32)
                chunk = jnp.concatenate([chunk, spare], axis=1)
            shift = (first_cell - (index % 3) * cells) % lanes
            moved = chunk if shift == 0 else pltpu.roll(chunk, shift, 1)
            sums[index] = sums[index] + jnp.where(here, moved, 0.0)
    trace = sums[0]
    scale = (conduct_fiber - conduct_matrix) / (2.0 * trace + tensor_eps)
    conduct = [
        conduct_matrix + scale * (trace - sums[1]),
        -scale * sums[3],
        conduct_matrix + scale * (trace - sums[2]),
    ]
    for kind in range(3):
        conduct_out[kind] = conduct[kind][HALO : HALO + count]
    copies = [
        pltpu.make_async_copy(conduct_out, conduct_hbm, sems.at[0]),
        pltpu.make_async_copy(temp_out, temp_hbm, sems.at[1]),
        pltpu.make_async_copy(cure_out, cure_hbm, sems.at[2]),
    ]
    copies[0].start()

    slots = range(height + 1, height + 1 + COLUMN_ROWS * (lanes // LANES), COLUMN_ROWS)
    columns = [
        jnp.concatenate([values[at : at + COLUMN_ROWS] for at in slots], axis=1) for values in blocks
    ]
    before, after = columns[parts - 1], columns[0]
    for part in range(parts - 1):
        before = jnp.where(layer == part + 1, columns[part], before)
        after = jnp.where(layer == part, columns[part + 1], after)
    spare = jnp.full((16 - count - 2 * GHOST, lanes), 0.5, jnp.float32)
    temp = jnp.concatenate([before[:GHOST], temp_in[...], after[:GHOST], 8.0 * spare], axis=0)
    cure = jnp.concatenate([spare[:1], before[GHOST:], cure_in[...], after[GHOST:], spare[:1], spare], axis=0)
    gap = GHOST - HALO
    xx, xz, zz = [pltpu.roll(part, gap, 0) for part in conduct]

    first = (plane == 0) & (layer == 0)
    last = (plane == planes - 1) & (layer == depths - 1)
    for step in range(STEPS):
        top, bottom = tools[2 * step : 2 * step + 1, :], tools[2 * step + 1 : 2 * step + 2, :]
        temp = jnp.where((row < GHOST) & first, temp[GHOST : GHOST + 1], temp)
        temp = jnp.where(
            (row >= GHOST + count) & last, temp[GHOST + count - 1 : GHOST + count], temp
        )
        cooler = jnp.where(lane == 0, top, pltpu.roll(temp, 1, 1))
        later = jnp.where(lane == lanes - 1, bottom, pltpu.roll(temp, lanes - 1, 1))
        slant = later - cooler
        second_x = pltpu.roll(temp, 15, 0) - 2.0 * temp + pltpu.roll(temp, 1, 0)
        second_z = later - 2.0 * temp + cooler
        cross = 0.25 * (pltpu.roll(slant, 15, 0) - pltpu.roll(slant, 1, 0))
        spread = xx * second_x + 2.0 * xz * cross + zz * second_z
        inverse = 1.0 / reference_temp - 1.0 / temp
        left = 1.0 - cure
        rate = rate_first * jnp.exp(energy_first * inverse) + rate_second * jnp.exp(
            energy_second * inverse
        ) * jnp.sqrt(cure)
        rate = rate * (left * jnp.sqrt(left))
        temp = temp + time_step * (spread + heat_release * rate)
        cure = cure + time_step * rate
    temp_out[...] = temp[GHOST : GHOST + count]
    cure_out[...] = cure[GHOST : GHOST + count]
    for copy in copies[1:]:
        copy.start()
    for copy in copies:
        copy.wait()


def on_device(intensity, temp_start, cure_start, tool_levels, plan):
    rows, width, depth = intensity.shape
    count, lanes = temp_start.shape
    planes, depths = lax.axis_size("plane"), lax.axis_size("depth")
    columns, cells = sizes(width, depth)
    bf16 = jnp.bfloat16
    slots = rows * EDGE + 16 * (lanes // LANES)
    params = pltpu.CompilerParams(vmem_limit_bytes=24 * 1024 * 1024)
    vmem = pl.BlockSpec(memory_space=pltpu.VMEM)
    stay = pl.BlockSpec(memory_space=pltpu.HBM)

    fixed = lambda values: pltpu.with_memory_space_constraint(values, pltpu.HBM)
    bands, coarse = x_bands(width), coarse_x_bands(width)
    late = bands.shape[1] - EARLY
    middle = bands[:, :EARLY, EDGE : EDGE + width]
    sides = bands[:, EARLY:].reshape(2 * late, -1)
    x_hbm, early_starts = stacked(
        middle.reshape(2 * EARLY, -1), sides[:, EDGE : EDGE + width], coarse[:, :EARLY]
    )
    z_hbm, _ = stacked(*depth_bands(depth), coarse_depth_bands(depth))
    halos = np.concatenate([sides[:, :EDGE], sides[:, EDGE + width :]], axis=1)
    x_late, late_starts = stacked(halos, coarse[:, EARLY:])
    rims = rim_bands(rows)
    flat, _ = stacked(np.concatenate([rims[0], rims[2]], axis=1))
    steep, rim_starts = stacked(rims[1], *rim_x_bands(count))
    cell_bands, _ = stacked(rim_cells(rows, depth, depths))
    far, near, own, x_parts, z_parts, temp, cure = pl.pallas_call(
        pack_kernel,
        name="pack",
        out_shape=(
            pltpu.VMEM((slots, depth), bf16),
            pltpu.VMEM((slots, depth), bf16),
            pltpu.VMEM((rows // 2, width, 2 * depth), bf16),
            pltpu.VMEM(x_hbm.shape, bf16),
            pltpu.VMEM(z_hbm.shape, bf16),
            pltpu.VMEM((count, lanes), jnp.float32),
            pltpu.VMEM((count, lanes), jnp.float32),
        ),
        in_specs=[stay] * 5,
        scratch_shapes=[
            pltpu.VMEM((rows, width, depth), jnp.int32),
            pltpu.SemaphoreType.DMA((5,)),
        ],
        compiler_params=params,
    )(*[fixed(values) for values in (intensity, temp_start, cure_start, x_hbm, z_hbm)])

    def moved(values, pairs):
        index = [(p * depths + d, q * depths + e) for (p, d), (q, e) in pairs]
        return lax.ppermute(values, ("plane", "depth"), index)

    def swapped(values, first):
        pairs = [(p, p + 1) for p in range(first, planes - 1, 2)]
        pairs += [(q, p) for p, q in pairs]
        return moved(values, [((p, d), (q, d)) for p, q in pairs for d in range(depths)])

    far = swapped(far, 1)
    near = swapped(near, 0)

    high = coarse.shape[0]

    def scratch(count):
        return [
            pltpu.VMEM((2 * count, rows * depth), jnp.float32),
            pltpu.VMEM((3 * rows // 2 * count, 2 * depth), bf16),
            pltpu.VMEM((3 * rows // 2 * count, 2 * depth), jnp.float32),
        ]

    def cost(count):
        return pl.CostEstimate(
            flops=2 * rows * (2 * count) * 160 * depth * 4,
            bytes_accessed=4_000_000,
            transcendentals=0,
        )

    early_sums, diagonal, sides, own_tiles, x_late = pl.pallas_call(
        functools.partial(early_kernel, early_starts),
        name="early",
        out_shape=(
            pltpu.VMEM((len(USED), high, LANES), jnp.float32),
            pltpu.VMEM((4 * depth, 2 * depth), bf16),
            pltpu.VMEM((2 * late, rows * depth), jnp.float32),
            pltpu.VMEM((3, width, LANES), jnp.float32),
            pltpu.VMEM(x_late.shape, bf16),
        ),
        in_specs=[vmem] * 3 + [stay],
        scratch_shapes=scratch(EARLY) + [pltpu.SemaphoreType.DMA((1,))],
        cost_estimate=cost(EARLY),
        compiler_params=params,
    )(own, x_parts, z_parts, fixed(x_late))

    products_x, voxels = own_columns(count)
    at_sums, half = chunk_rows(count, lanes)
    chunk_shape = (depths, at_sums + 2 * half, LANES)
    chunks = pl.pallas_call(
        functools.partial(late_kernel, late_starts, width),
        name="late",
        out_shape=pltpu.HBM(chunk_shape, bf16),
        in_specs=[vmem] * 10,
        out_specs=stay,
        scratch_shapes=scratch(late)
        + [pltpu.VMEM(chunk_shape, bf16), pltpu.SemaphoreType.DMA((2,))],
        cost_estimate=cost(late),
        compiler_params=params,
    )(far, near, x_late, z_parts, diagonal, early_sums, sides, own_tiles, temp, cure)

    faces = plan.reshape(2 * STEPS, 1) == jnp.arange(tool_levels.shape[0], dtype=jnp.int32)
    tools = jnp.sum(
        jnp.where(faces, tool_levels, jnp.zeros_like(tool_levels)), axis=1, keepdims=True
    )

    chunks = lax.all_to_all(
        chunks,
        "depth",
        split_axis=0,
        concat_axis=0,
        tiled=True,
        axis_index_groups=[meeting_order(depths)],
    )

    return pl.pallas_call(
        functools.partial(cure_kernel, cells, rim_starts),
        name="cure",
        out_shape=(
            pltpu.HBM((count, lanes), jnp.float32),
            pltpu.HBM((count, lanes), jnp.float32),
            pltpu.HBM((3, count, lanes), jnp.float32),
        ),
        in_specs=[vmem] * 7,
        out_specs=(stay, stay, stay),
        scratch_shapes=[
            pltpu.VMEM((count, lanes), jnp.float32),
            pltpu.VMEM((count, lanes), jnp.float32),
            pltpu.VMEM((3, count, lanes), jnp.float32),
            pltpu.SemaphoreType.DMA((3,)),
        ],
        compiler_params=params,
    )(chunks, temp, cure, tools, flat, steep, cell_bands)


def solution(mesh):
    return jax.shard_map(
        on_device,
        mesh=mesh,
        in_specs=(
            P(None, "plane", "depth"),
            P(("plane", "depth"), None),
            P(("plane", "depth"), None),
            P(),
            P(),
        ),
        out_specs=(
            P(("plane", "depth"), None),
            P(("plane", "depth"), None),
            P(None, ("plane", "depth"), None),
        ),
        check_vma=False,
    )
```

```python
import functools

import jax
import jax.numpy as jnp
import ml_dtypes
import numpy as np
from jax import lax
from jax.experimental import pallas as pl
from jax.experimental.pallas import tpu as pltpu
from jax.sharding import PartitionSpec as P

ROWS = 8
R1 = 6
R2 = 10
COARSE = 4
STEPS = 3

sigma_grad = 2.0
sigma_tensor = 3.3
conduct_matrix = 0.3
conduct_fiber = 1.5
time_step = 0.25
heat_release = 0.4
rate_first = 0.15
rate_second = 0.6
energy_first = 30.0
energy_second = 25.0
reference_temp = 4.2
tensor_eps = 1e-06

LANES = 128
HALO = 2
EDGE = HALO * COARSE + R1 + R2
EARLY = 96
GHOST = 3
COLUMN_ROWS = 2 * GHOST - 1
CODE_SCALE = 2.0**20
RIM = 2 * R1
BEFORE = -(-(R2 - R1) // COARSE)
AFTER = BEFORE
HALF = LANES // 2
ROW_KINDS = (1, 0, 0)
X_KINDS = (0, 1, 0)
DEPTH_KINDS = (0, 0, 1)


def smooth_taps(radius, sigma):
    offsets = np.arange(-radius, radius + 1) * 1.0
    weights = np.exp(-0.5 * offsets * offsets / (sigma * sigma))
    return weights / weights.sum()


def slope_taps(radius, sigma):
    offsets = np.arange(-radius, radius + 1) * 1.0
    weights = np.exp(-0.5 * offsets * offsets / (sigma * sigma))
    return offsets * weights / np.sum(offsets * offsets * weights)


def row_weights(count, radius, sigma):
    taps = smooth_taps(radius, sigma)
    result = np.zeros(count)
    for source in range(count):
        for target in range(count):
            offset = target - source
            if abs(offset) <= radius:
                result[source] += taps[offset + radius]
    return result


def rounded(taps):
    best = None
    for factor in np.linspace(1.0, 2.0, 20001)[:-1]:
        near = (taps * factor).astype(np.float32).astype(ml_dtypes.bfloat16).astype(np.float64)
        error = np.abs(near / factor - taps).sum()
        if best is None or error < best[0]:
            best = (error, near, factor)
    return best[1], best[2]


def as_bfloat16(matrix):
    return matrix.astype(np.float32).astype(ml_dtypes.bfloat16)


def halves(matrix):
    high = as_bfloat16(matrix)
    return high, as_bfloat16(matrix - high.astype(np.float64))


def sizes(width, depth):
    columns = width // COARSE + 2 * HALO
    cells = depth // COARSE + BEFORE + AFTER
    return columns, cells


def product_rows(width):
    places = [*range(R1, width - R1)]
    places += [None] * max(EARLY - len(places), 0)
    places += [*range(R1 - EDGE, R1), *range(width - R1, width + EDGE - R1)]
    return places + [None] * (-len(places) % 16)


GRAD_TAPS = tuple(
    rounded(taps(R1, sigma_grad)) for taps in (smooth_taps, slope_taps)
)
GRAD_FACTOR = GRAD_TAPS[0][1] ** 2 * GRAD_TAPS[1][1]


def grad_taps(kind):
    return GRAD_TAPS[kind][0]


def tap(taps, offset):
    radius = (len(taps) - 1) // 2
    return float(taps[offset + radius]) if abs(offset) <= radius else 0.0


def x_bands(width):
    places = product_rows(width)
    bands = np.zeros((2, len(places), width + 2 * EDGE))
    for kind in range(2):
        for row, place in enumerate(places):
            if place is not None:
                first = place + EDGE - R1
                bands[kind, row, first : first + 2 * R1 + 1] = grad_taps(kind)
    return bands


def rim_bands(rows):
    bands = np.zeros((3, 3 * LANES, LANES))
    for part in range(3):
        row_taps, depth_taps = grad_taps(ROW_KINDS[part]), grad_taps(DEPTH_KINDS[part])
        for source in range(rows):
            for target in range(rows):
                row_tap = tap(row_taps, source - target)
                for near in range(-RIM, RIM):
                    lane = source * RIM + near % RIM
                    if near >= 0:
                        lane += rows * RIM + LANES
                    for place in range(-R1, R1):
                        value = row_tap * tap(depth_taps, near - place)
                        bands[part, lane, target * 2 * R1 + R1 + place] = value
    return bands


def rim_cells(rows, depth, blocks):
    taps = smooth_taps(R2, sigma_tensor)
    weights = product_weights(rows)
    bands = np.zeros((blocks - 1, LANES, blocks * depth // COARSE))
    for boundary in range(blocks - 1):
        middle = (boundary + 1) * depth
        for cell in range(bands.shape[2]):
            for voxel in range(cell * COARSE, (cell + 1) * COARSE):
                for place in range(-R1, R1):
                    value = tap(taps, middle + place - voxel)
                    for row in range(rows):
                        bands[boundary, row * 2 * R1 + R1 + place, cell] += weights[row] * value
    return bands.reshape(-1, bands.shape[2])


def meeting_order(blocks):
    middle = blocks // 2
    return [*range(middle, blocks), *range(middle)]


def own_columns(count):
    products = (count + 2 * HALO) * COARSE + 2 * R2
    voxels = products + 2 * R1
    return -(-products // 16) * 16, -(-voxels // 8) * 8


def fold(voxels):
    return -(-voxels // 16) * 8


def rim_x_bands(count):
    products, voxels = own_columns(count)
    bands = np.zeros((2, products, -(-voxels // 16) * 16))
    valid = (count + 2 * HALO) * COARSE + 2 * R2
    for kind in range(2):
        for row in range(valid):
            bands[kind, row, row : row + 2 * R1 + 1] = grad_taps(kind)
    taps = smooth_taps(R2, sigma_tensor)
    coarse = np.zeros((16, products))
    for column in range(count + 2 * HALO):
        for voxel in range(column * COARSE, (column + 1) * COARSE):
            coarse[column, voxel : voxel + 2 * R2 + 1] += taps
    return bands.reshape(2 * products, -1), coarse


def depth_bands(depth):
    bands = np.zeros((2, depth, depth))
    for kind in range(2):
        for place in range(depth):
            for near in range(max(place - R1, 0), min(place + R1 + 1, depth)):
                bands[kind, near, place] = tap(grad_taps(kind), near - place)
    return bands


def product_weights(rows):
    return row_weights(rows, R2, sigma_tensor) / (255.0 * GRAD_FACTOR) ** 2


def coarse_depth_bands(depth):
    taps = smooth_taps(R2, sigma_tensor)
    columns, cells = sizes(0, depth)
    bands = np.zeros((depth, LANES))
    for cell in range(cells):
        for voxel in range(COARSE):
            place = (cell - BEFORE) * COARSE + voxel
            for near in range(max(place - R2, 0), min(place + R2 + 1, depth)):
                bands[near, cell] += tap(taps, near - place)
    return bands


def coarse_x_bands(width):
    taps = smooth_taps(R2, sigma_tensor)
    places = product_rows(width)
    columns, cells = sizes(width, 0)
    bands = np.zeros((-(-columns // 16) * 16, len(places)))
    for column in range(columns):
        for voxel in range(COARSE):
            middle = (column - HALO) * COARSE + voxel
            for row, place in enumerate(places):
                if place is not None:
                    bands[column, row] += tap(taps, place - middle)
    return bands


def stacked(*pieces):
    widest = max(piece.shape[1] for piece in pieces)
    padded = [np.pad(piece, ((0, 0), (0, widest - piece.shape[1]))) for piece in pieces]
    starts = np.cumsum([0] + [len(piece) for piece in pieces])
    return jnp.asarray(as_bfloat16(np.concatenate(padded))), tuple(int(start) for start in starts)


def two_parts(values):
    high = values.astype(jnp.bfloat16).astype(jnp.float32)
    return jnp.concatenate([high, (values - high).astype(jnp.bfloat16).astype(jnp.float32)], axis=0)


def joined(parts):
    half = parts.shape[0] // 2
    return parts[:half] + parts[half:]


def coded(values):
    values = values * CODE_SCALE
    return (values * jnp.abs(values)) * (values * values)


def decoded(values):
    size = jnp.sqrt(jnp.sqrt(jnp.abs(values))) * (1.0 / CODE_SCALE)
    return jnp.where(values < 0.0, -size, size)


def column_rows(temp, cure, at_end):
    count = temp.shape[0]
    first, second = (count - GHOST, count - GHOST + 1) if at_end else (0, 0)
    pad = jnp.zeros((8 - COLUMN_ROWS, temp.shape[1]), jnp.float32)
    return jnp.concatenate(
        [temp[first : first + GHOST, :], cure[second : second + GHOST - 1, :], pad], axis=0
    )


def chunk_rows(count, lanes):
    products, voxels = own_columns(count)
    held = count + 2 * HALO + 1 + COLUMN_ROWS * (lanes // LANES)
    return voxels + fold(voxels), -(-held // 16) * 16


def is_odd():
    return lax.rem(lax.axis_index("plane"), 2) == 1


def pack_kernel(
    intensity, temp_hbm, cure_hbm, x_hbm, z_hbm, far, near, own, x_parts, z_parts, temp, cure,
    grey, sems,
):
    rows, width, depth = intensity.shape
    copies = [
        pltpu.make_async_copy(intensity, grey, sems.at[0]),
        pltpu.make_async_copy(temp_hbm, temp, sems.at[1]),
        pltpu.make_async_copy(cure_hbm, cure, sems.at[2]),
        pltpu.make_async_copy(x_hbm, x_parts, sems.at[3]),
        pltpu.make_async_copy(z_hbm, z_parts, sems.at[4]),
    ]
    for copy in copies:
        copy.start()
    for copy in copies[:3]:
        copy.wait()
    odd = is_odd()
    sides = [
        two_parts(column_rows(temp, cure, at_end)).astype(jnp.bfloat16)
        for at_end in (False, True)
    ]

    def send(left, right):
        for place, target, columns in ((0, left, sides[0]), (width - EDGE, right, sides[1])):
            for pair in range(rows // 2):
                two = [grey[2 * pair + i, place : place + EDGE, :] for i in range(2)]
                two = jnp.concatenate(two, axis=0).astype(jnp.float32)
                target[2 * EDGE * pair : 2 * EDGE * (pair + 1), :] = two.astype(jnp.bfloat16)
            for slot in range(temp.shape[1] // LANES):
                at = rows * EDGE + 16 * slot
                target[at : at + 16, :] = columns[:, slot * LANES : (slot + 1) * LANES]

    @pl.when(odd)
    def _():
        send(near, far)

    @pl.when(jnp.logical_not(odd))
    def _():
        send(far, near)

    for row in range(rows):
        half = (row % 2) * depth
        own[row // 2, :, half : half + depth] = grey[row].astype(jnp.float32).astype(jnp.bfloat16)
    for copy in copies[3:]:
        copy.wait()


def packed_rows(values, size, first):
    depth = values[0].shape[1]
    lane = lax.broadcasted_iota(jnp.int32, values[0].shape, 1)
    packed = None
    for block, value in enumerate(values):
        shift = (size * block - first) % depth
        moved = value if shift == 0 else pltpu.roll(value, shift, 1)
        packed = moved if block == 0 else jnp.where(lane >= size * block, moved, packed)
    return packed


def edges_of(ref, rows):
    two = [
        ref[2 * EDGE * pair : 2 * EDGE * (pair + 1), :].astype(jnp.float32)
        for pair in range(rows // 2)
    ]
    voxels = [two[row // 2][row % 2 * EDGE : (row % 2 + 1) * EDGE] for row in range(rows)]
    slots = range(rows * EDGE, ref.shape[0], 16)
    columns = [joined(ref[at : at + 16, :].astype(jnp.float32)) for at in slots]
    return voxels, jnp.concatenate(columns, axis=1)


def product(first, second):
    return jnp.dot(first, second, preferred_element_type=jnp.float32)


def mirrored_filter(kind, values, even):
    rows = len(values)
    use_sum = even == (kind == 0)
    sign = 1.0 if use_sum else -1.0
    half = [values[row] + sign * values[rows - 1 - row] for row in range(rows // 2)]
    results = []
    for row in range(rows // 2):
        total = None
        for source, value in enumerate(half):
            near = tap(grad_taps(kind), source - row)
            far = tap(grad_taps(kind), rows - 1 - source - row)
            weight = 0.5 * (near + sign * far)
            total = weight * value if total is None else total + weight * value
        results.append(total)
    return results


def weighted_products(three, weight):
    pairs = ((0, 0), (1, 1), (2, 2), (0, 1), (0, 2), (1, 2))
    first = [weight * value for value in three]
    return [first[a] * three[b] for a, b in pairs]


def late_mask(count, width):
    row = lax.broadcasted_iota(jnp.int32, (count, LANES), 0)
    left = max(width - 2 * R1 - EARLY, 0)
    place = jnp.where(row < left + EDGE, row - left + R1 - EDGE, row - left - EDGE + width - R1)
    place = place + lax.axis_index("plane") * width
    inside = (place >= 0) & (place < lax.axis_size("plane") * width)
    return jnp.where(inside | (row < left), 1.0, 0.0)


USED = (0, 1, 2, 5)
UNUSED = (3, 4)


def all_sums(products, coarse, sx):
    sums = [None] * 6
    for kinds in (USED, UNUSED):
        tiles = [tile for index in kinds for tile in products[index]]
        along = product(sx, jnp.concatenate(tiles, axis=1)).astype(jnp.bfloat16)
        step = along.shape[1] // len(kinds)
        parts = [along[:, index * step : (index + 1) * step] for index in range(len(kinds))]
        total = product(jnp.concatenate(parts, axis=0), coarse)
        high = sx.shape[0]
        for index, kind in enumerate(kinds):
            sums[kind] = total[index * high : (index + 1) * high]
    return sums


def tensor_sums(across, sx, mask, diagonal, z_parts, filtered, grads):
    double = diagonal.shape[1]
    depth, pairs = double // 2, across.shape[1] // double
    rows, count = 2 * pairs, across.shape[0] // 2
    for start in range(0, count, 16):
        kinds = [
            [
                across[kind * count + start : kind * count + start + 16, row * depth : (row + 1) * depth]
                for row in range(rows)
            ]
            for kind in range(2)
        ]
        for part in range(3):
            values = kinds[X_KINDS[part]]
            results = mirrored_filter(ROW_KINDS[part], values, True)
            results += mirrored_filter(ROW_KINDS[part], values, False)
            for row, result in enumerate(results):
                at = (part * pairs + row // 2) * count + start
                lanes = slice((row % 2) * depth, (row % 2 + 1) * depth)
                filtered[at : at + 16, lanes] = result.astype(jnp.bfloat16)

    at = 2 * pairs * count
    grads[:at] = product(filtered[:at, :], diagonal[0:double, :])
    grads[at:] = product(filtered[at:, :], diagonal[double : 2 * double, :])

    weights = product_weights(rows)
    layer = lax.axis_index("depth")
    first, last = layer == 0, layer == lax.axis_size("depth") - 1
    place = lax.broadcasted_iota(jnp.int32, (16, depth), 1)
    complete = ((place >= R1) | first) & ((place < depth - R1) | last)
    complete = jnp.where(complete, 1.0, 0.0)
    groups = [[] for _ in range(6)]
    for start in range(0, count, 16):
        inside = complete if mask is None else complete * mask[start : start + 16]
        totals = None
        for row in range(rows):
            lanes = slice((row % 2) * depth, (row % 2 + 1) * depth)
            three = []
            for part in range(3):
                at = (part * pairs + row // 2) * count + start
                three.append(grads[at : at + 16, lanes])
            terms = weighted_products(three, 2.0 * float(weights[row % (rows // 2)]))
            totals = terms if row == 0 else [a + b for a, b in zip(totals, terms)]
        for index in range(6):
            groups[index].append((totals[index] * inside).astype(jnp.bfloat16))
    products = [[jnp.concatenate(group, axis=0)] for group in groups]
    return all_sums(products, z_parts[double : double + depth, :], sx)


def rim_tiles(values):
    rows, depth = len(values), values[0].shape[1]
    below = packed_rows(values, RIM, depth - RIM)
    above = pltpu.roll(packed_rows(values, RIM, 0), rows * RIM, 1)
    lane = lax.broadcasted_iota(jnp.int32, below.shape, 1)
    return [jnp.where(lane < rows * RIM, below, above), above, pltpu.roll(above, HALF, 1)]


def early_kernel(
    starts, own, x_parts, z_parts, late_hbm, sums, diagonal, sides, tiles, x_late, across,
    filtered, grads, sem,
):
    copy = pltpu.make_async_copy(late_hbm, x_late, sem.at[0])
    copy.start()
    pairs, width, double = own.shape
    rows, depth = 2 * pairs, double // 2
    empty = jnp.zeros((depth, depth), jnp.bfloat16)
    for kind in range(2):
        for half in range(2):
            at = pl.ds(kind * double + half * depth, depth)
            band = z_parts[kind * depth : (kind + 1) * depth, :]
            diagonal[at, half * depth : (half + 1) * depth] = band
            diagonal[at, (1 - half) * depth : (2 - half) * depth] = empty
    whole = jnp.concatenate([own[pair] for pair in range(pairs)], axis=1)
    result = product(x_parts[starts[0] : starts[2], :width], whole)
    across[...] = result[: starts[1]]
    sides[...] = result[starts[1] :]
    sx = x_parts[starts[2] : starts[3], :EARLY]
    results = tensor_sums(across, sx, None, diagonal, z_parts, filtered, grads)
    for index, kind in enumerate(USED):
        sums[index] = results[kind]
    values = [
        own[row // 2, :, (row % 2) * depth : (row % 2 + 1) * depth].astype(jnp.float32)
        for row in range(rows)
    ]
    for index, tile in enumerate(rim_tiles(values)):
        tiles[index] = tile
    copy.wait()


def late_kernel(
    starts, width, far, near, x_late, z_parts, diagonal, early_sums, sides, own_tiles, temp, cure,
    out_hbm, across, filtered, grads, out, sems,
):
    double = diagonal.shape[1]
    depth = double // 2
    rows = across.shape[1] // depth
    count, lanes = temp.shape
    odd = is_odd()
    depths, layer = lax.axis_size("depth"), lax.axis_index("depth")
    outer, outer_columns = edges_of(far, rows)
    inner, inner_columns = edges_of(near, rows)
    values = []
    for row in range(rows):
        left = jnp.where(odd, inner[row], outer[row])
        right = jnp.where(odd, outer[row], inner[row])
        values.append(jnp.concatenate([left, right], axis=0))
    left = jnp.where(odd, inner_columns, outer_columns)
    right = jnp.where(odd, outer_columns, inner_columns)

    late = across.shape[0] // 2
    halos = jnp.concatenate([value.astype(jnp.bfloat16) for value in values], axis=1)
    across[...] = sides[...] + product(x_late[starts[0] : starts[1], : 2 * EDGE], halos)

    products_x, voxels = own_columns(count)
    folded, stride = fold(voxels), COARSE * count
    tiles = [
        jnp.concatenate([tile[:EDGE], own_tiles[index], tile[EDGE:]], axis=0)
        for index, tile in enumerate(rim_tiles(values))
    ]
    missing = stride * (depths - 1) + voxels - tiles[0].shape[0]
    if missing > 0:
        spare = jnp.zeros((-(-missing // 8) * 8, LANES), jnp.float32)
        tiles = [jnp.concatenate([tile, spare], axis=0) for tile in tiles]

    height = count + 2 * HALO
    half_lane = lax.broadcasted_iota(jnp.int32, (folded, LANES), 1) < HALF
    order = meeting_order(out.shape[0])
    for position, target in enumerate(order):
        at = stride * target
        second = jnp.where(
            half_lane,
            tiles[1][at : at + folded],
            tiles[2][at + voxels - folded : at + voxels],
        )
        rims = jnp.concatenate([tiles[0][at : at + voxels], second], axis=0)
        out[position, 0 : voxels + folded, :] = rims.astype(jnp.bfloat16)
    split = (pl.ds(0, voxels + folded), pl.ds(voxels + folded, out.shape[1] - voxels - folded))
    copies = [
        pltpu.make_async_copy(out.at[:, part, :], out_hbm.at[:, part, :], sems.at[index])
        for index, part in enumerate(split)
    ]
    copies[0].start()

    sx = x_late[starts[1] : starts[2], :late]
    results = tensor_sums(
        across, sx, late_mask(late, width), diagonal, z_parts, filtered, grads
    )
    yy, xx, zz, xz = [early_sums[index] + results[kind] for index, kind in enumerate(USED)]
    trace = yy + xx + zz
    lane = lax.broadcasted_iota(jnp.int32, trace.shape, 1)
    columns, cells = sizes(width, depth)
    tail = 4 * cells - LANES
    joint = pltpu.roll(xz, 3 * cells, 1)
    rest = jnp.where(lane < tail, joint, 0.0)
    rest = pltpu.roll(rest, 0, 1, stride=tail, stride_axis=0)
    for index, part in ((2, zz), (1, xx), (0, trace)):
        moved = part if index == 0 else pltpu.roll(part, index * cells, 1)
        joint = jnp.where(lane < (index + 1) * cells, moved, joint)

    own_first, own_last = column_rows(temp, cure, False), column_rows(temp, cure, True)
    half = chunk_rows(count, lanes)[1]
    for position, target in enumerate(order):
        piece = jnp.where(layer == target - 1, own_last, 0.0)
        piece = jnp.where(layer == target + 1, own_first, piece)
        if target == 0:
            piece = jnp.where(layer == depths - 1, left, piece)
        if target == out.shape[0] - 1:
            piece = jnp.where(layer == 0, right, piece)
        mine = slice(count * target, count * target + height)
        pieces = [coded(joint[mine]), coded(jnp.sum(rest[mine], axis=0, keepdims=True))]
        for slot in range(lanes // LANES):
            part = piece[:, slot * LANES : (slot + 1) * LANES]
            pieces += [part[:GHOST] - reference_temp, part[GHOST:COLUMN_ROWS]]
        filled = sum(part.shape[0] for part in pieces)
        if filled < half:
            pieces.append(jnp.zeros((half - filled, LANES), jnp.float32))
        out[position, voxels + folded :, :] = jnp.concatenate(pieces, axis=0).astype(jnp.bfloat16)
    copies[1].start()
    for copy in copies:
        copy.wait()


def rim_sums(chunks, count, starts, flat, steep, cells):
    parts = chunks.shape[0]
    rows_x, voxels = own_columns(count)
    folded = fold(voxels)
    tall = -(-voxels // 16) * 16
    spare = [jnp.zeros((tall - voxels, LANES), jnp.float32)] if tall > voxels else []
    tiles = []
    order = meeting_order(parts)
    for part in range(parts):
        rims = chunks[order.index(part), 0 : voxels + folded, :].astype(jnp.float32)
        second = rims[voxels:]
        second = [second[: voxels - folded], pltpu.roll(second, HALF, 1)]
        for tile in ([rims[:voxels]], second):
            tiles.append(jnp.concatenate(tile + spare, axis=0).astype(jnp.bfloat16))
    result = product(
        steep[starts[1] : starts[2], :tall], jnp.concatenate(tiles, axis=1)
    ).astype(jnp.bfloat16)
    kinds = []
    for kind in range(2):
        values = result[kind * rows_x : (kind + 1) * rows_x]
        tile = lambda index: values[:, index * LANES : (index + 1) * LANES]
        stack = [
            jnp.concatenate([tile(2 * part), tile(2 * part + 2), tile(2 * part + 3)], axis=1)
            for part in range(parts - 1)
        ]
        kinds.append(jnp.concatenate(stack, axis=0))
    both = product(kinds[0], flat[...])
    three = (both[:, :LANES], product(kinds[1], steep[starts[0] : starts[1], :]), both[:, LANES:])

    index = lax.axis_index("plane") * lax.axis_size("depth") + lax.axis_index("depth")
    total = lax.axis_size("plane") * lax.axis_size("depth") * count * COARSE
    place = lax.rem(lax.broadcasted_iota(jnp.int32, three[0].shape, 0), rows_x)
    place = place + (index * count - HALO) * COARSE - R2
    inside = jnp.where((place >= 0) & (place < total), 1.0, 0.0)
    products = [
        [
            term[part * rows_x : (part + 1) * rows_x].astype(jnp.bfloat16)
            for part in range(parts - 1)
        ]
        for term in weighted_products(three, inside)
    ]
    return all_sums(products, cells[...], steep[starts[2] : starts[3], :rows_x])


def cure_kernel(
    cells, starts, chunks, temp_in, cure_in, tools, flat, steep, rim_bands, temp_hbm, cure_hbm,
    conduct_hbm, temp_out, cure_out, conduct_out, sems,
):
    count, lanes = temp_in.shape
    parts = chunks.shape[0]
    planes, depths = lax.axis_size("plane"), lax.axis_size("depth")
    plane, layer = lax.axis_index("plane"), lax.axis_index("depth")
    height = count + 2 * HALO
    own = cells - BEFORE - AFTER
    lane = lax.broadcasted_iota(jnp.int32, (16, lanes), 1)
    row = lax.broadcasted_iota(jnp.int32, (16, lanes), 0)
    at_sums, half = chunk_rows(count, lanes)
    tail = 4 * cells - LANES
    narrow_lane = lax.broadcasted_iota(jnp.int32, (16, LANES), 1)
    order = meeting_order(parts)

    near = rim_sums(chunks, count, starts, flat, steep, rim_bands)
    sums = [near[0] + near[1] + near[2], near[1], near[2], near[5]]
    blocks = [chunks[order.index(part), at_sums:, :].astype(jnp.float32) for part in range(parts)]
    columns = [
        jnp.concatenate(
            [
                block[at : at + COLUMN_ROWS]
                for at in range(
                    height + 1, height + 1 + COLUMN_ROWS * (lanes // LANES), COLUMN_ROWS
                )
            ],
            axis=1,
        )
        for block in blocks
    ]
    blocks = [decoded(block[0:16]) for block in blocks]
    tails = [block[height : height + 1] for block in blocks]
    if parts % 8:
        tails.append(jnp.zeros((-parts % 8, LANES), jnp.float32))
    tails = jnp.concatenate(tails, axis=0)
    tails = pltpu.roll(tails, lax.rem(LANES - lax.rem(tail * count * layer, LANES), LANES), 1)
    narrow_row = lax.broadcasted_iota(jnp.int32, (16, LANES), 0)
    rests = [jnp.zeros((16, LANES), jnp.float32) for _ in range(parts)]
    for column in range(height):
        moved = pltpu.roll(tails, LANES - tail * column, 1) if column else tails
        for part in range(parts):
            rests[part] = jnp.where(narrow_row == column, moved[part : part + 1], rests[part])
    for part in range(parts):
        first_cell = own * part - BEFORE
        here = (lane >= first_cell) & (lane < first_cell + cells)
        values = blocks[part]
        joint = values[0:16]
        xz = pltpu.roll(jnp.where(narrow_lane < tail, rests[part], joint), LANES - 3 * cells, 1)
        for index in range(4):
            chunk = xz if index == 3 else joint
            if lanes > LANES:
                spare = jnp.zeros((16, lanes - LANES), jnp.float32)
                chunk = jnp.concatenate([chunk, spare], axis=1)
            shift = (first_cell - (index % 3) * cells) % lanes
            moved = chunk if shift == 0 else pltpu.roll(chunk, shift, 1)
            sums[index] = sums[index] + jnp.where(here, moved, 0.0)
    trace = sums[0]
    scale = (conduct_fiber - conduct_matrix) / (2.0 * trace + tensor_eps)
    conduct = [
        conduct_matrix + scale * (trace - sums[1]),
        -scale * sums[3],
        conduct_matrix + scale * (trace - sums[2]),
    ]
    for kind in range(3):
        conduct_out[kind] = conduct[kind][HALO : HALO + count]
    copies = [
        pltpu.make_async_copy(conduct_out, conduct_hbm, sems.at[0]),
        pltpu.make_async_copy(temp_out, temp_hbm, sems.at[1]),
        pltpu.make_async_copy(cure_out, cure_hbm, sems.at[2]),
    ]
    copies[0].start()

    before, after = columns[parts - 1], columns[0]
    for part in range(parts - 1):
        before = jnp.where(layer == part + 1, columns[part], before)
        after = jnp.where(layer == part, columns[part + 1], after)
    spare = jnp.full((16 - count - 2 * GHOST, lanes), 0.5, jnp.float32)
    temp = jnp.concatenate([
            before[:GHOST] + reference_temp,
            temp_in[...],
            after[:GHOST] + reference_temp,
            8.0 * spare,
        ], axis=0)
    cure = jnp.concatenate([spare[:1], before[GHOST:], cure_in[...], after[GHOST:], spare[:1], spare], axis=0)
    gap = GHOST - HALO
    xx, xz, zz = [pltpu.roll(part, gap, 0) for part in conduct]

    first = (plane == 0) & (layer == 0)
    last = (plane == planes - 1) & (layer == depths - 1)
    for step in range(STEPS):
        top, bottom = tools[2 * step : 2 * step + 1, :], tools[2 * step + 1 : 2 * step + 2, :]
        temp = jnp.where((row < GHOST) & first, temp[GHOST : GHOST + 1], temp)
        temp = jnp.where(
            (row >= GHOST + count) & last, temp[GHOST + count - 1 : GHOST + count], temp
        )
        cooler = jnp.where(lane == 0, top, pltpu.roll(temp, 1, 1))
        later = jnp.where(lane == lanes - 1, bottom, pltpu.roll(temp, lanes - 1, 1))
        slant = later - cooler
        second_x = pltpu.roll(temp, 15, 0) - 2.0 * temp + pltpu.roll(temp, 1, 0)
        second_z = later - 2.0 * temp + cooler
        cross = 0.25 * (pltpu.roll(slant, 15, 0) - pltpu.roll(slant, 1, 0))
        spread = xx * second_x + 2.0 * xz * cross + zz * second_z
        inverse = 1.0 / reference_temp - 1.0 / temp
        left = 1.0 - cure
        rate = rate_first * jnp.exp(energy_first * inverse) + rate_second * jnp.exp(
            energy_second * inverse
        ) * jnp.sqrt(cure)
        rate = rate * (left * jnp.sqrt(left))
        temp = temp + time_step * (spread + heat_release * rate)
        cure = cure + time_step * rate
    temp_out[...] = temp[GHOST : GHOST + count]
    cure_out[...] = cure[GHOST : GHOST + count]
    for copy in copies[1:]:
        copy.start()
    for copy in copies:
        copy.wait()


def on_device(intensity, temp_start, cure_start, tool_levels, plan):
    rows, width, depth = intensity.shape
    count, lanes = temp_start.shape
    planes, depths = lax.axis_size("plane"), lax.axis_size("depth")
    columns, cells = sizes(width, depth)
    bf16 = jnp.bfloat16
    slots = rows * EDGE + 16 * (lanes // LANES)
    params = pltpu.CompilerParams(vmem_limit_bytes=24 * 1024 * 1024)
    vmem = pl.BlockSpec(memory_space=pltpu.VMEM)
    stay = pl.BlockSpec(memory_space=pltpu.HBM)

    fixed = lambda values: pltpu.with_memory_space_constraint(values, pltpu.HBM)
    bands, coarse = x_bands(width), coarse_x_bands(width)
    late = bands.shape[1] - EARLY
    middle = bands[:, :EARLY, EDGE : EDGE + width]
    sides = bands[:, EARLY:].reshape(2 * late, -1)
    x_hbm, early_starts = stacked(
        middle.reshape(2 * EARLY, -1), sides[:, EDGE : EDGE + width], coarse[:, :EARLY]
    )
    z_hbm, _ = stacked(*depth_bands(depth), coarse_depth_bands(depth))
    halos = np.concatenate([sides[:, :EDGE], sides[:, EDGE + width :]], axis=1)
    x_late, late_starts = stacked(halos, coarse[:, EARLY:])
    rims = rim_bands(rows)
    flat, _ = stacked(np.concatenate([rims[0], rims[2]], axis=1))
    steep, rim_starts = stacked(rims[1], *rim_x_bands(count))
    cell_bands, _ = stacked(rim_cells(rows, depth, depths))
    far, near, own, x_parts, z_parts, temp, cure = pl.pallas_call(
        pack_kernel,
        name="pack",
        out_shape=(
            pltpu.VMEM((slots, depth), bf16),
            pltpu.VMEM((slots, depth), bf16),
            pltpu.VMEM((rows // 2, width, 2 * depth), bf16),
            pltpu.VMEM(x_hbm.shape, bf16),
            pltpu.VMEM(z_hbm.shape, bf16),
            pltpu.VMEM((count, lanes), jnp.float32),
            pltpu.VMEM((count, lanes), jnp.float32),
        ),
        in_specs=[stay] * 5,
        scratch_shapes=[
            pltpu.VMEM((rows, width, depth), jnp.int32),
            pltpu.SemaphoreType.DMA((5,)),
        ],
        compiler_params=params,
    )(*[fixed(values) for values in (intensity, temp_start, cure_start, x_hbm, z_hbm)])

    def moved(values, pairs):
        index = [(p * depths + d, q * depths + e) for (p, d), (q, e) in pairs]
        return lax.ppermute(values, ("plane", "depth"), index)

    def swapped(values, first):
        pairs = [(p, p + 1) for p in range(first, planes - 1, 2)]
        pairs += [(q, p) for p, q in pairs]
        return moved(values, [((p, d), (q, d)) for p, q in pairs for d in range(depths)])

    far = swapped(far, 1)
    near = swapped(near, 0)

    high = coarse.shape[0]

    def scratch(count):
        return [
            pltpu.VMEM((2 * count, rows * depth), jnp.float32),
            pltpu.VMEM((3 * rows // 2 * count, 2 * depth), bf16),
            pltpu.VMEM((3 * rows // 2 * count, 2 * depth), jnp.float32),
        ]

    def cost(count):
        return pl.CostEstimate(
            flops=2 * rows * (2 * count) * 160 * depth * 4,
            bytes_accessed=4_000_000,
            transcendentals=0,
        )

    early_sums, diagonal, sides, own_tiles, x_late = pl.pallas_call(
        functools.partial(early_kernel, early_starts),
        name="early",
        out_shape=(
            pltpu.VMEM((len(USED), high, LANES), jnp.float32),
            pltpu.VMEM((4 * depth, 2 * depth), bf16),
            pltpu.VMEM((2 * late, rows * depth), jnp.float32),
            pltpu.VMEM((3, width, LANES), jnp.float32),
            pltpu.VMEM(x_late.shape, bf16),
        ),
        in_specs=[vmem] * 3 + [stay],
        scratch_shapes=scratch(EARLY) + [pltpu.SemaphoreType.DMA((1,))],
        cost_estimate=cost(EARLY),
        compiler_params=params,
    )(own, x_parts, z_parts, fixed(x_late))

    products_x, voxels = own_columns(count)
    at_sums, half = chunk_rows(count, lanes)
    chunk_shape = (depths, at_sums + half, LANES)
    chunks = pl.pallas_call(
        functools.partial(late_kernel, late_starts, width),
        name="late",
        out_shape=pltpu.HBM(chunk_shape, bf16),
        in_specs=[vmem] * 10,
        out_specs=stay,
        scratch_shapes=scratch(late)
        + [pltpu.VMEM(chunk_shape, bf16), pltpu.SemaphoreType.DMA((2,))],
        cost_estimate=cost(late),
        compiler_params=params,
    )(far, near, x_late, z_parts, diagonal, early_sums, sides, own_tiles, temp, cure)

    faces = plan.reshape(2 * STEPS, 1) == jnp.arange(tool_levels.shape[0], dtype=jnp.int32)
    tools = jnp.sum(
        jnp.where(faces, tool_levels, jnp.zeros_like(tool_levels)), axis=1, keepdims=True
    )

    chunks = lax.all_to_all(
        chunks,
        "depth",
        split_axis=0,
        concat_axis=0,
        tiled=True,
        axis_index_groups=[meeting_order(depths)],
    )

    return pl.pallas_call(
        functools.partial(cure_kernel, cells, rim_starts),
        name="cure",
        out_shape=(
            pltpu.HBM((count, lanes), jnp.float32),
            pltpu.HBM((count, lanes), jnp.float32),
            pltpu.HBM((3, count, lanes), jnp.float32),
        ),
        in_specs=[vmem] * 7,
        out_specs=(stay, stay, stay),
        scratch_shapes=[
            pltpu.VMEM((count, lanes), jnp.float32),
            pltpu.VMEM((count, lanes), jnp.float32),
            pltpu.VMEM((3, count, lanes), jnp.float32),
            pltpu.SemaphoreType.DMA((3,)),
        ],
        compiler_params=params,
    )(chunks, temp, cure, tools, flat, steep, cell_bands)


def solution(mesh):
    return jax.shard_map(
        on_device,
        mesh=mesh,
        in_specs=(
            P(None, "plane", "depth"),
            P(("plane", "depth"), None),
            P(("plane", "depth"), None),
            P(),
            P(),
        ),
        out_specs=(
            P(("plane", "depth"), None),
            P(("plane", "depth"), None),
            P(None, ("plane", "depth"), None),
        ),
        check_vma=False,
    )
```

```python
import functools

import jax
import jax.numpy as jnp
import ml_dtypes
import numpy as np
from jax import lax
from jax.experimental import pallas as pl
from jax.experimental.pallas import tpu as pltpu
from jax.sharding import PartitionSpec as P

ROWS = 8
R1 = 6
R2 = 10
COARSE = 4
STEPS = 3

sigma_grad = 2.0
sigma_tensor = 3.3
conduct_matrix = 0.3
conduct_fiber = 1.5
time_step = 0.25
heat_release = 0.4
rate_first = 0.15
rate_second = 0.6
energy_first = 30.0
energy_second = 25.0
reference_temp = 4.2
tensor_eps = 1e-06

LANES = 128
HALO = 2
EDGE = HALO * COARSE + R1 + R2
EARLY = 96
GHOST = 3
COLUMN_ROWS = 2 * GHOST - 1
CODE_SCALE = 2.0**20
RIM = 2 * R1
BEFORE = -(-(R2 - R1) // COARSE)
AFTER = BEFORE
HALF = LANES // 2
ROW_KINDS = (1, 0, 0)
X_KINDS = (0, 1, 0)
DEPTH_KINDS = (0, 0, 1)


def smooth_taps(radius, sigma):
    offsets = np.arange(-radius, radius + 1) * 1.0
    weights = np.exp(-0.5 * offsets * offsets / (sigma * sigma))
    return weights / weights.sum()


def slope_taps(radius, sigma):
    offsets = np.arange(-radius, radius + 1) * 1.0
    weights = np.exp(-0.5 * offsets * offsets / (sigma * sigma))
    return offsets * weights / np.sum(offsets * offsets * weights)


def row_weights(count, radius, sigma):
    taps = smooth_taps(radius, sigma)
    result = np.zeros(count)
    for source in range(count):
        for target in range(count):
            offset = target - source
            if abs(offset) <= radius:
                result[source] += taps[offset + radius]
    return result


def rounded(taps):
    best = None
    for factor in np.linspace(1.0, 2.0, 20001)[:-1]:
        near = (taps * factor).astype(np.float32).astype(ml_dtypes.bfloat16).astype(np.float64)
        error = np.abs(near / factor - taps).sum()
        if best is None or error < best[0]:
            best = (error, near, factor)
    return best[1], best[2]


def as_bfloat16(matrix):
    return matrix.astype(np.float32).astype(ml_dtypes.bfloat16)


def halves(matrix):
    high = as_bfloat16(matrix)
    return high, as_bfloat16(matrix - high.astype(np.float64))


def sizes(width, depth):
    columns = width // COARSE + 2 * HALO
    cells = depth // COARSE + BEFORE + AFTER
    return columns, cells


def product_rows(width):
    places = [*range(R1, width - R1)]
    places += [None] * max(EARLY - len(places), 0)
    places += [*range(R1 - EDGE, R1), *range(width - R1, width + EDGE - R1)]
    return places + [None] * (-len(places) % 16)


GRAD_TAPS = tuple(
    rounded(taps(R1, sigma_grad)) for taps in (smooth_taps, slope_taps)
)
GRAD_FACTOR = GRAD_TAPS[0][1] ** 2 * GRAD_TAPS[1][1]


def grad_taps(kind):
    return GRAD_TAPS[kind][0]


def tap(taps, offset):
    radius = (len(taps) - 1) // 2
    return float(taps[offset + radius]) if abs(offset) <= radius else 0.0


def x_bands(width):
    places = product_rows(width)
    bands = np.zeros((2, len(places), width + 2 * EDGE))
    for kind in range(2):
        for row, place in enumerate(places):
            if place is not None:
                first = place + EDGE - R1
                bands[kind, row, first : first + 2 * R1 + 1] = grad_taps(kind)
    return bands


def rim_bands(rows):
    bands = np.zeros((3, 3 * LANES, LANES))
    for part in range(3):
        row_taps, depth_taps = grad_taps(ROW_KINDS[part]), grad_taps(DEPTH_KINDS[part])
        for source in range(rows):
            for target in range(rows):
                row_tap = tap(row_taps, source - target)
                for near in range(-RIM, RIM):
                    lane = source * RIM + near % RIM
                    if near >= 0:
                        lane += rows * RIM + LANES
                    for place in range(-R1, R1):
                        value = row_tap * tap(depth_taps, near - place)
                        bands[part, lane, target * 2 * R1 + R1 + place] = value
    return bands


def rim_cells(rows, depth, blocks):
    taps = smooth_taps(R2, sigma_tensor)
    weights = product_weights(rows)
    bands = np.zeros((blocks - 1, LANES, blocks * depth // COARSE))
    for boundary in range(blocks - 1):
        middle = (boundary + 1) * depth
        for cell in range(bands.shape[2]):
            for voxel in range(cell * COARSE, (cell + 1) * COARSE):
                for place in range(-R1, R1):
                    value = tap(taps, middle + place - voxel)
                    for row in range(rows):
                        bands[boundary, row * 2 * R1 + R1 + place, cell] += weights[row] * value
    return bands.reshape(-1, bands.shape[2])


def meeting_order(blocks):
    middle = blocks // 2
    return [*range(middle, blocks), *range(middle)]


def own_columns(count):
    products = (count + 2 * HALO) * COARSE + 2 * R2
    voxels = products + 2 * R1
    return -(-products // 16) * 16, -(-voxels // 8) * 8


def fold(voxels):
    return -(-voxels // 16) * 8


def rim_x_bands(count):
    products, voxels = own_columns(count)
    bands = np.zeros((2, products, -(-voxels // 16) * 16))
    valid = (count + 2 * HALO) * COARSE + 2 * R2
    for kind in range(2):
        for row in range(valid):
            bands[kind, row, row : row + 2 * R1 + 1] = grad_taps(kind)
    taps = smooth_taps(R2, sigma_tensor)
    coarse = np.zeros((16, products))
    for column in range(count + 2 * HALO):
        for voxel in range(column * COARSE, (column + 1) * COARSE):
            coarse[column, voxel : voxel + 2 * R2 + 1] += taps
    return bands.reshape(2 * products, -1), coarse


def depth_bands(depth):
    bands = np.zeros((2, depth, depth))
    for kind in range(2):
        for place in range(depth):
            for near in range(max(place - R1, 0), min(place + R1 + 1, depth)):
                bands[kind, near, place] = tap(grad_taps(kind), near - place)
    return bands


def product_weights(rows):
    return row_weights(rows, R2, sigma_tensor) / (255.0 * GRAD_FACTOR) ** 2


def coarse_depth_bands(depth):
    taps = smooth_taps(R2, sigma_tensor)
    columns, cells = sizes(0, depth)
    bands = np.zeros((depth, LANES))
    for cell in range(cells):
        for voxel in range(COARSE):
            place = (cell - BEFORE) * COARSE + voxel
            for near in range(max(place - R2, 0), min(place + R2 + 1, depth)):
                bands[near, cell] += tap(taps, near - place)
    return bands


def coarse_x_bands(width):
    taps = smooth_taps(R2, sigma_tensor)
    places = product_rows(width)
    columns, cells = sizes(width, 0)
    bands = np.zeros((-(-columns // 16) * 16, len(places)))
    for column in range(columns):
        for voxel in range(COARSE):
            middle = (column - HALO) * COARSE + voxel
            for row, place in enumerate(places):
                if place is not None:
                    bands[column, row] += tap(taps, place - middle)
    return bands


def stacked(*pieces):
    widest = max(piece.shape[1] for piece in pieces)
    padded = [np.pad(piece, ((0, 0), (0, widest - piece.shape[1]))) for piece in pieces]
    starts = np.cumsum([0] + [len(piece) for piece in pieces])
    return jnp.asarray(as_bfloat16(np.concatenate(padded))), tuple(int(start) for start in starts)


def two_parts(values):
    high = values.astype(jnp.bfloat16).astype(jnp.float32)
    return jnp.concatenate([high, (values - high).astype(jnp.bfloat16).astype(jnp.float32)], axis=0)


def joined(parts):
    half = parts.shape[0] // 2
    return parts[:half] + parts[half:]


def coded(values):
    values = values * CODE_SCALE
    return (values * jnp.abs(values)) * (values * values)


def decoded(values):
    size = jnp.sqrt(jnp.sqrt(jnp.abs(values))) * (1.0 / CODE_SCALE)
    return jnp.where(values < 0.0, -size, size)


def column_rows(temp, cure, at_end):
    count = temp.shape[0]
    first, second = (count - GHOST, count - GHOST + 1) if at_end else (0, 0)
    pad = jnp.zeros((8 - COLUMN_ROWS, temp.shape[1]), jnp.float32)
    return jnp.concatenate(
        [temp[first : first + GHOST, :], cure[second : second + GHOST - 1, :], pad], axis=0
    )


def chunk_rows(count, lanes):
    products, voxels = own_columns(count)
    held = count + 2 * HALO + 1 + COLUMN_ROWS * (lanes // LANES)
    return voxels + fold(voxels), -(-held // 16) * 16


def is_odd():
    return lax.rem(lax.axis_index("plane"), 2) == 1


def pack_kernel(
    intensity, temp_hbm, cure_hbm, x_hbm, z_hbm, far, near, grey, x_parts, z_parts, temp, cure,
    sems,
):
    rows, width, depth = intensity.shape
    copies = [
        pltpu.make_async_copy(intensity, grey, sems.at[0]),
        pltpu.make_async_copy(temp_hbm, temp, sems.at[1]),
        pltpu.make_async_copy(cure_hbm, cure, sems.at[2]),
        pltpu.make_async_copy(x_hbm, x_parts, sems.at[3]),
        pltpu.make_async_copy(z_hbm, z_parts, sems.at[4]),
    ]
    for copy in copies:
        copy.start()
    for copy in copies[:3]:
        copy.wait()
    odd = is_odd()
    sides = [
        two_parts(column_rows(temp, cure, at_end)).astype(jnp.bfloat16)
        for at_end in (False, True)
    ]

    def send(left, right):
        for place, target, columns in ((0, left, sides[0]), (width - EDGE, right, sides[1])):
            for pair in range(rows // 2):
                two = [grey[2 * pair + i, place : place + EDGE, :] for i in range(2)]
                two = jnp.concatenate(two, axis=0).astype(jnp.float32)
                target[2 * EDGE * pair : 2 * EDGE * (pair + 1), :] = two.astype(jnp.bfloat16)
            for slot in range(temp.shape[1] // LANES):
                at = rows * EDGE + 16 * slot
                target[at : at + 16, :] = columns[:, slot * LANES : (slot + 1) * LANES]

    @pl.when(odd)
    def _():
        send(near, far)

    @pl.when(jnp.logical_not(odd))
    def _():
        send(far, near)

    for copy in copies[3:]:
        copy.wait()


def packed_rows(values, size, first):
    depth = values[0].shape[1]
    lane = lax.broadcasted_iota(jnp.int32, values[0].shape, 1)
    packed = None
    for block, value in enumerate(values):
        shift = (size * block - first) % depth
        moved = value if shift == 0 else pltpu.roll(value, shift, 1)
        packed = moved if block == 0 else jnp.where(lane >= size * block, moved, packed)
    return packed


def edges_of(ref, rows):
    two = [
        ref[2 * EDGE * pair : 2 * EDGE * (pair + 1), :].astype(jnp.float32)
        for pair in range(rows // 2)
    ]
    voxels = [two[row // 2][row % 2 * EDGE : (row % 2 + 1) * EDGE] for row in range(rows)]
    slots = range(rows * EDGE, ref.shape[0], 16)
    columns = [joined(ref[at : at + 16, :].astype(jnp.float32)) for at in slots]
    return voxels, jnp.concatenate(columns, axis=1)


def product(first, second):
    return jnp.dot(first, second, preferred_element_type=jnp.float32)


def mirrored_filter(kind, values, even):
    rows = len(values)
    use_sum = even == (kind == 0)
    sign = 1.0 if use_sum else -1.0
    half = [values[row] + sign * values[rows - 1 - row] for row in range(rows // 2)]
    results = []
    for row in range(rows // 2):
        total = None
        for source, value in enumerate(half):
            near = tap(grad_taps(kind), source - row)
            far = tap(grad_taps(kind), rows - 1 - source - row)
            weight = 0.5 * (near + sign * far)
            total = weight * value if total is None else total + weight * value
        results.append(total)
    return results


def weighted_products(three, weight):
    pairs = ((0, 0), (1, 1), (2, 2), (0, 1), (0, 2), (1, 2))
    first = [weight * value for value in three]
    return [first[a] * three[b] for a, b in pairs]


def late_mask(count, width):
    row = lax.broadcasted_iota(jnp.int32, (count, LANES), 0)
    left = max(width - 2 * R1 - EARLY, 0)
    place = jnp.where(row < left + EDGE, row - left + R1 - EDGE, row - left - EDGE + width - R1)
    place = place + lax.axis_index("plane") * width
    inside = (place >= 0) & (place < lax.axis_size("plane") * width)
    return jnp.where(inside | (row < left), 1.0, 0.0)


USED = (0, 1, 2, 5)
UNUSED = (3, 4)


def all_sums(products, coarse, sx):
    sums = [None] * 6
    for kinds in (USED, UNUSED):
        tiles = [tile for index in kinds for tile in products[index]]
        along = product(sx, jnp.concatenate(tiles, axis=1)).astype(jnp.bfloat16)
        step = along.shape[1] // len(kinds)
        parts = [along[:, index * step : (index + 1) * step] for index in range(len(kinds))]
        total = product(jnp.concatenate(parts, axis=0), coarse)
        high = sx.shape[0]
        for index, kind in enumerate(kinds):
            sums[kind] = total[index * high : (index + 1) * high]
    return sums


def tensor_sums(across, sx, mask, diagonal, z_parts, filtered, grads):
    double = diagonal.shape[1]
    depth, pairs = double // 2, across.shape[1] // double
    rows, count = 2 * pairs, across.shape[0] // 2
    for start in range(0, count, 16):
        kinds = [
            [
                across[kind * count + start : kind * count + start + 16, row * depth : (row + 1) * depth]
                for row in range(rows)
            ]
            for kind in range(2)
        ]
        for part in range(3):
            values = kinds[X_KINDS[part]]
            results = mirrored_filter(ROW_KINDS[part], values, True)
            results += mirrored_filter(ROW_KINDS[part], values, False)
            for row, result in enumerate(results):
                at = (part * pairs + row // 2) * count + start
                lanes = slice((row % 2) * depth, (row % 2 + 1) * depth)
                filtered[at : at + 16, lanes] = result.astype(jnp.bfloat16)

    at = 2 * pairs * count
    grads[:at] = product(filtered[:at, :], diagonal[0:double, :])
    grads[at:] = product(filtered[at:, :], diagonal[double : 2 * double, :])

    weights = product_weights(rows)
    layer = lax.axis_index("depth")
    first, last = layer == 0, layer == lax.axis_size("depth") - 1
    place = lax.broadcasted_iota(jnp.int32, (16, depth), 1)
    complete = ((place >= R1) | first) & ((place < depth - R1) | last)
    complete = jnp.where(complete, 1.0, 0.0)
    groups = [[] for _ in range(6)]
    for start in range(0, count, 16):
        inside = complete if mask is None else complete * mask[start : start + 16]
        totals = None
        for row in range(rows):
            lanes = slice((row % 2) * depth, (row % 2 + 1) * depth)
            three = []
            for part in range(3):
                at = (part * pairs + row // 2) * count + start
                three.append(grads[at : at + 16, lanes])
            terms = weighted_products(three, 2.0 * float(weights[row % (rows // 2)]))
            totals = terms if row == 0 else [a + b for a, b in zip(totals, terms)]
        for index in range(6):
            groups[index].append((totals[index] * inside).astype(jnp.bfloat16))
    products = [[jnp.concatenate(group, axis=0)] for group in groups]
    return all_sums(products, z_parts[double : double + depth, :], sx)


def rim_tiles(values):
    rows, depth = len(values), values[0].shape[1]
    below = packed_rows(values, RIM, depth - RIM)
    above = pltpu.roll(packed_rows(values, RIM, 0), rows * RIM, 1)
    lane = lax.broadcasted_iota(jnp.int32, below.shape, 1)
    return [jnp.where(lane < rows * RIM, below, above), above, pltpu.roll(above, HALF, 1)]


def early_kernel(
    starts, grey, x_parts, z_parts, sums, diagonal, sides, tiles, across, filtered, grads
):
    rows, width, depth = grey.shape
    double = 2 * depth
    empty = jnp.zeros((depth, depth), jnp.bfloat16)
    for kind in range(2):
        for half in range(2):
            at = pl.ds(kind * double + half * depth, depth)
            band = z_parts[kind * depth : (kind + 1) * depth, :]
            diagonal[at, half * depth : (half + 1) * depth] = band
            diagonal[at, (1 - half) * depth : (2 - half) * depth] = empty
    values = [grey[row].astype(jnp.float32) for row in range(rows)]
    whole = jnp.concatenate([value.astype(jnp.bfloat16) for value in values], axis=1)
    result = product(x_parts[starts[0] : starts[2], :width], whole)
    across[...] = result[: starts[1]]
    sides[...] = result[starts[1] :]
    sx = x_parts[starts[2] : starts[3], :EARLY]
    results = tensor_sums(across, sx, None, diagonal, z_parts, filtered, grads)
    for index, kind in enumerate(USED):
        sums[index] = results[kind]
    for index, tile in enumerate(rim_tiles(values)):
        tiles[index] = tile


def late_kernel(
    starts, width, far, near, x_late, z_parts, diagonal, early_sums, sides, own_tiles, temp, cure,
    out_hbm, across, filtered, grads, out, sems,
):
    double = diagonal.shape[1]
    depth = double // 2
    rows = across.shape[1] // depth
    count, lanes = temp.shape
    odd = is_odd()
    depths, layer = lax.axis_size("depth"), lax.axis_index("depth")
    outer, outer_columns = edges_of(far, rows)
    inner, inner_columns = edges_of(near, rows)
    values = []
    for row in range(rows):
        left = jnp.where(odd, inner[row], outer[row])
        right = jnp.where(odd, outer[row], inner[row])
        values.append(jnp.concatenate([left, right], axis=0))
    left = jnp.where(odd, inner_columns, outer_columns)
    right = jnp.where(odd, outer_columns, inner_columns)

    late = across.shape[0] // 2
    halos = jnp.concatenate([value.astype(jnp.bfloat16) for value in values], axis=1)
    across[...] = sides[...] + product(x_late[starts[0] : starts[1], : 2 * EDGE], halos)

    products_x, voxels = own_columns(count)
    folded, stride = fold(voxels), COARSE * count
    tiles = [
        jnp.concatenate([tile[:EDGE], own_tiles[index], tile[EDGE:]], axis=0)
        for index, tile in enumerate(rim_tiles(values))
    ]
    missing = stride * (depths - 1) + voxels - tiles[0].shape[0]
    if missing > 0:
        spare = jnp.zeros((-(-missing // 8) * 8, LANES), jnp.float32)
        tiles = [jnp.concatenate([tile, spare], axis=0) for tile in tiles]

    height = count + 2 * HALO
    half_lane = lax.broadcasted_iota(jnp.int32, (folded, LANES), 1) < HALF
    order = meeting_order(out.shape[0])
    for position, target in enumerate(order):
        at = stride * target
        second = jnp.where(
            half_lane,
            tiles[1][at : at + folded],
            tiles[2][at + voxels - folded : at + voxels],
        )
        rims = jnp.concatenate([tiles[0][at : at + voxels], second], axis=0)
        out[position, 0 : voxels + folded, :] = rims.astype(jnp.bfloat16)
    split = (pl.ds(0, voxels + folded), pl.ds(voxels + folded, out.shape[1] - voxels - folded))
    copies = [
        pltpu.make_async_copy(out.at[:, part, :], out_hbm.at[:, part, :], sems.at[index])
        for index, part in enumerate(split)
    ]
    copies[0].start()

    sx = x_late[starts[1] : starts[2], :late]
    results = tensor_sums(
        across, sx, late_mask(late, width), diagonal, z_parts, filtered, grads
    )
    yy, xx, zz, xz = [early_sums[index] + results[kind] for index, kind in enumerate(USED)]
    trace = yy + xx + zz
    lane = lax.broadcasted_iota(jnp.int32, trace.shape, 1)
    columns, cells = sizes(width, depth)
    tail = 4 * cells - LANES
    joint = pltpu.roll(xz, 3 * cells, 1)
    rest = jnp.where(lane < tail, joint, 0.0)
    rest = pltpu.roll(rest, 0, 1, stride=tail, stride_axis=0)
    for index, part in ((2, zz), (1, xx), (0, trace)):
        moved = part if index == 0 else pltpu.roll(part, index * cells, 1)
        joint = jnp.where(lane < (index + 1) * cells, moved, joint)

    own_first, own_last = column_rows(temp, cure, False), column_rows(temp, cure, True)
    half = chunk_rows(count, lanes)[1]
    for position, target in enumerate(order):
        piece = jnp.where(layer == target - 1, own_last, 0.0)
        piece = jnp.where(layer == target + 1, own_first, piece)
        if target == 0:
            piece = jnp.where(layer == depths - 1, left, piece)
        if target == out.shape[0] - 1:
            piece = jnp.where(layer == 0, right, piece)
        mine = slice(count * target, count * target + height)
        pieces = [coded(joint[mine]), coded(jnp.sum(rest[mine], axis=0, keepdims=True))]
        for slot in range(lanes // LANES):
            part = piece[:, slot * LANES : (slot + 1) * LANES]
            pieces += [part[:GHOST] - reference_temp, part[GHOST:COLUMN_ROWS]]
        filled = sum(part.shape[0] for part in pieces)
        if filled < half:
            pieces.append(jnp.zeros((half - filled, LANES), jnp.float32))
        out[position, voxels + folded :, :] = jnp.concatenate(pieces, axis=0).astype(jnp.bfloat16)
    copies[1].start()
    for copy in copies:
        copy.wait()


def rim_sums(chunks, count, starts, flat, steep, cells):
    parts = chunks.shape[0]
    rows_x, voxels = own_columns(count)
    folded = fold(voxels)
    tall = -(-voxels // 16) * 16
    spare = [jnp.zeros((tall - voxels, LANES), jnp.float32)] if tall > voxels else []
    tiles = []
    order = meeting_order(parts)
    for part in range(parts):
        rims = chunks[order.index(part), 0 : voxels + folded, :].astype(jnp.float32)
        second = rims[voxels:]
        second = [second[: voxels - folded], pltpu.roll(second, HALF, 1)]
        for tile in ([rims[:voxels]], second)[: 2 if part else 1]:
            tiles.append(jnp.concatenate(tile + spare, axis=0).astype(jnp.bfloat16))
    result = product(
        steep[starts[1] : starts[2], :tall], jnp.concatenate(tiles, axis=1)
    ).astype(jnp.bfloat16)
    kinds = []
    for kind in range(2):
        values = result[kind * rows_x : (kind + 1) * rows_x]
        tile = lambda index: values[:, index * LANES : (index + 1) * LANES]
        stack = [
            jnp.concatenate(
                [tile(max(2 * part - 1, 0)), tile(2 * part + 1), tile(2 * part + 2)], axis=1
            )
            for part in range(parts - 1)
        ]
        kinds.append(jnp.concatenate(stack, axis=0))
    both = product(kinds[0], flat[...])
    three = (both[:, :LANES], product(kinds[1], steep[starts[0] : starts[1], :]), both[:, LANES:])

    index = lax.axis_index("plane") * lax.axis_size("depth") + lax.axis_index("depth")
    total = lax.axis_size("plane") * lax.axis_size("depth") * count * COARSE
    place = lax.rem(lax.broadcasted_iota(jnp.int32, three[0].shape, 0), rows_x)
    place = place + (index * count - HALO) * COARSE - R2
    inside = jnp.where((place >= 0) & (place < total), 1.0, 0.0)
    products = [
        [
            term[part * rows_x : (part + 1) * rows_x].astype(jnp.bfloat16)
            for part in range(parts - 1)
        ]
        for term in weighted_products(three, inside)
    ]
    return all_sums(products, cells[...], steep[starts[2] : starts[3], :rows_x])


def cure_kernel(
    cells, starts, chunks, temp_in, cure_in, tools, flat, steep, rim_bands, temp_hbm, cure_hbm,
    conduct_hbm, temp_out, cure_out, conduct_out, sems,
):
    count, lanes = temp_in.shape
    parts = chunks.shape[0]
    planes, depths = lax.axis_size("plane"), lax.axis_size("depth")
    plane, layer = lax.axis_index("plane"), lax.axis_index("depth")
    height = count + 2 * HALO
    own = cells - BEFORE - AFTER
    lane = lax.broadcasted_iota(jnp.int32, (16, lanes), 1)
    row = lax.broadcasted_iota(jnp.int32, (16, lanes), 0)
    at_sums, half = chunk_rows(count, lanes)
    tail = 4 * cells - LANES
    narrow_lane = lax.broadcasted_iota(jnp.int32, (16, LANES), 1)
    order = meeting_order(parts)

    near = rim_sums(chunks, count, starts, flat, steep, rim_bands)
    sums = [near[0] + near[1] + near[2], near[1], near[2], near[5]]
    blocks = [chunks[order.index(part), at_sums:, :].astype(jnp.float32) for part in range(parts)]
    columns = [
        jnp.concatenate(
            [
                block[at : at + COLUMN_ROWS]
                for at in range(
                    height + 1, height + 1 + COLUMN_ROWS * (lanes // LANES), COLUMN_ROWS
                )
            ],
            axis=1,
        )
        for block in blocks
    ]
    blocks = [decoded(block[0:16]) for block in blocks]
    tails = [block[height : height + 1] for block in blocks]
    if parts % 8:
        tails.append(jnp.zeros((-parts % 8, LANES), jnp.float32))
    tails = jnp.concatenate(tails, axis=0)
    tails = pltpu.roll(tails, lax.rem(LANES - lax.rem(tail * count * layer, LANES), LANES), 1)
    narrow_row = lax.broadcasted_iota(jnp.int32, (16, LANES), 0)
    rests = [jnp.zeros((16, LANES), jnp.float32) for _ in range(parts)]
    for column in range(height):
        moved = pltpu.roll(tails, LANES - tail * column, 1) if column else tails
        for part in range(parts):
            rests[part] = jnp.where(narrow_row == column, moved[part : part + 1], rests[part])
    for part in range(parts):
        first_cell = own * part - BEFORE
        here = (lane >= first_cell) & (lane < first_cell + cells)
        values = blocks[part]
        joint = values[0:16]
        xz = pltpu.roll(jnp.where(narrow_lane < tail, rests[part], joint), LANES - 3 * cells, 1)
        for index in range(4):
            chunk = xz if index == 3 else joint
            if lanes > LANES:
                spare = jnp.zeros((16, lanes - LANES), jnp.float32)
                chunk = jnp.concatenate([chunk, spare], axis=1)
            shift = (first_cell - (index % 3) * cells) % lanes
            moved = chunk if shift == 0 else pltpu.roll(chunk, shift, 1)
            sums[index] = sums[index] + jnp.where(here, moved, 0.0)
    trace = sums[0]
    scale = (conduct_fiber - conduct_matrix) / (2.0 * trace + tensor_eps)
    conduct = [
        conduct_matrix + scale * (trace - sums[1]),
        -scale * sums[3],
        conduct_matrix + scale * (trace - sums[2]),
    ]
    for kind in range(3):
        conduct_out[kind] = conduct[kind][HALO : HALO + count]
    copies = [
        pltpu.make_async_copy(conduct_out, conduct_hbm, sems.at[0]),
        pltpu.make_async_copy(temp_out, temp_hbm, sems.at[1]),
        pltpu.make_async_copy(cure_out, cure_hbm, sems.at[2]),
    ]
    copies[0].start()

    before, after = columns[parts - 1], columns[0]
    for part in range(parts - 1):
        before = jnp.where(layer == part + 1, columns[part], before)
        after = jnp.where(layer == part, columns[part + 1], after)
    spare = jnp.full((16 - count - 2 * GHOST, lanes), 0.5, jnp.float32)
    temp = jnp.concatenate([
            before[:GHOST] + reference_temp,
            temp_in[...],
            after[:GHOST] + reference_temp,
            8.0 * spare,
        ], axis=0)
    cure = jnp.concatenate([spare[:1], before[GHOST:], cure_in[...], after[GHOST:], spare[:1], spare], axis=0)
    gap = GHOST - HALO
    xx, xz, zz = [pltpu.roll(part, gap, 0) for part in conduct]

    first = (plane == 0) & (layer == 0)
    last = (plane == planes - 1) & (layer == depths - 1)
    for step in range(STEPS):
        top, bottom = tools[2 * step : 2 * step + 1, :], tools[2 * step + 1 : 2 * step + 2, :]
        temp = jnp.where((row < GHOST) & first, temp[GHOST : GHOST + 1], temp)
        temp = jnp.where(
            (row >= GHOST + count) & last, temp[GHOST + count - 1 : GHOST + count], temp
        )
        cooler = jnp.where(lane == 0, top, pltpu.roll(temp, 1, 1))
        later = jnp.where(lane == lanes - 1, bottom, pltpu.roll(temp, lanes - 1, 1))
        slant = later - cooler
        second_x = pltpu.roll(temp, 15, 0) - 2.0 * temp + pltpu.roll(temp, 1, 0)
        second_z = later - 2.0 * temp + cooler
        cross = 0.25 * (pltpu.roll(slant, 15, 0) - pltpu.roll(slant, 1, 0))
        spread = xx * second_x + 2.0 * xz * cross + zz * second_z
        inverse = 1.0 / reference_temp - 1.0 / temp
        left = 1.0 - cure
        rate = rate_first * jnp.exp(energy_first * inverse) + rate_second * jnp.exp(
            energy_second * inverse
        ) * jnp.sqrt(cure)
        rate = rate * (left * jnp.sqrt(left))
        temp = temp + time_step * (spread + heat_release * rate)
        cure = cure + time_step * rate
    temp_out[...] = temp[GHOST : GHOST + count]
    cure_out[...] = cure[GHOST : GHOST + count]
    for copy in copies[1:]:
        copy.start()
    for copy in copies:
        copy.wait()


def on_device(intensity, temp_start, cure_start, tool_levels, plan):
    rows, width, depth = intensity.shape
    count, lanes = temp_start.shape
    planes, depths = lax.axis_size("plane"), lax.axis_size("depth")
    columns, cells = sizes(width, depth)
    bf16 = jnp.bfloat16
    slots = rows * EDGE + 16 * (lanes // LANES)
    params = pltpu.CompilerParams(vmem_limit_bytes=24 * 1024 * 1024)
    vmem = pl.BlockSpec(memory_space=pltpu.VMEM)
    stay = pl.BlockSpec(memory_space=pltpu.HBM)

    fixed = lambda values: pltpu.with_memory_space_constraint(values, pltpu.HBM)
    bands, coarse = x_bands(width), coarse_x_bands(width)
    late = bands.shape[1] - EARLY
    middle = bands[:, :EARLY, EDGE : EDGE + width]
    sides = bands[:, EARLY:].reshape(2 * late, -1)
    x_hbm, early_starts = stacked(
        middle.reshape(2 * EARLY, -1), sides[:, EDGE : EDGE + width], coarse[:, :EARLY]
    )
    z_hbm, _ = stacked(*depth_bands(depth), coarse_depth_bands(depth))
    halos = np.concatenate([sides[:, :EDGE], sides[:, EDGE + width :]], axis=1)
    x_late, late_starts = stacked(halos, coarse[:, EARLY:])
    rims = rim_bands(rows)
    flat, _ = stacked(np.concatenate([rims[0], rims[2]], axis=1))
    steep, rim_starts = stacked(rims[1], *rim_x_bands(count))
    cell_bands, _ = stacked(rim_cells(rows, depth, depths))
    far, near, grey, x_parts, z_parts, temp, cure = pl.pallas_call(
        pack_kernel,
        name="pack",
        out_shape=(
            pltpu.VMEM((slots, depth), bf16),
            pltpu.VMEM((slots, depth), bf16),
            pltpu.VMEM((rows, width, depth), jnp.int32),
            pltpu.VMEM(x_hbm.shape, bf16),
            pltpu.VMEM(z_hbm.shape, bf16),
            pltpu.VMEM((count, lanes), jnp.float32),
            pltpu.VMEM((count, lanes), jnp.float32),
        ),
        in_specs=[stay] * 5,
        scratch_shapes=[
            pltpu.SemaphoreType.DMA((5,)),
        ],
        compiler_params=params,
    )(*[fixed(values) for values in (intensity, temp_start, cure_start, x_hbm, z_hbm)])

    def moved(values, pairs):
        index = [(p * depths + d, q * depths + e) for (p, d), (q, e) in pairs]
        return lax.ppermute(values, ("plane", "depth"), index)

    def swapped(values, first):
        pairs = [(p, p + 1) for p in range(first, planes - 1, 2)]
        pairs += [(q, p) for p, q in pairs]
        return moved(values, [((p, d), (q, d)) for p, q in pairs for d in range(depths)])

    far = swapped(far, 1)
    near = swapped(near, 0)

    high = coarse.shape[0]

    def scratch(count):
        return [
            pltpu.VMEM((2 * count, rows * depth), jnp.float32),
            pltpu.VMEM((3 * rows // 2 * count, 2 * depth), bf16),
            pltpu.VMEM((3 * rows // 2 * count, 2 * depth), jnp.float32),
        ]

    def cost(count):
        return pl.CostEstimate(
            flops=2 * rows * (2 * count) * 160 * depth * 4,
            bytes_accessed=4_000_000,
            transcendentals=0,
        )

    early_sums, diagonal, sides, own_tiles = pl.pallas_call(
        functools.partial(early_kernel, early_starts),
        name="early",
        out_shape=(
            pltpu.VMEM((len(USED), high, LANES), jnp.float32),
            pltpu.VMEM((4 * depth, 2 * depth), bf16),
            pltpu.VMEM((2 * late, rows * depth), jnp.float32),
            pltpu.VMEM((3, width, LANES), jnp.float32),
        ),
        scratch_shapes=scratch(EARLY),
        cost_estimate=cost(EARLY),
        compiler_params=params,
    )(grey, x_parts, z_parts)

    products_x, voxels = own_columns(count)
    at_sums, half = chunk_rows(count, lanes)
    chunk_shape = (depths, at_sums + half, LANES)
    chunks = pl.pallas_call(
        functools.partial(late_kernel, late_starts, width),
        name="late",
        out_shape=pltpu.HBM(chunk_shape, bf16),
        in_specs=[vmem] * 10,
        out_specs=stay,
        scratch_shapes=scratch(late)
        + [pltpu.VMEM(chunk_shape, bf16), pltpu.SemaphoreType.DMA((2,))],
        cost_estimate=cost(late),
        compiler_params=params,
    )(far, near, x_late, z_parts, diagonal, early_sums, sides, own_tiles, temp, cure)

    faces = plan.reshape(2 * STEPS, 1) == jnp.arange(tool_levels.shape[0], dtype=jnp.int32)
    tools = jnp.sum(
        jnp.where(faces, tool_levels, jnp.zeros_like(tool_levels)), axis=1, keepdims=True
    )

    chunks = lax.all_to_all(
        chunks,
        "depth",
        split_axis=0,
        concat_axis=0,
        tiled=True,
        axis_index_groups=[meeting_order(depths)],
    )

    return pl.pallas_call(
        functools.partial(cure_kernel, cells, rim_starts),
        name="cure",
        out_shape=(
            pltpu.HBM((count, lanes), jnp.float32),
            pltpu.HBM((count, lanes), jnp.float32),
            pltpu.HBM((3, count, lanes), jnp.float32),
        ),
        in_specs=[vmem] * 7,
        out_specs=(stay, stay, stay),
        scratch_shapes=[
            pltpu.VMEM((count, lanes), jnp.float32),
            pltpu.VMEM((count, lanes), jnp.float32),
            pltpu.VMEM((3, count, lanes), jnp.float32),
            pltpu.SemaphoreType.DMA((3,)),
        ],
        compiler_params=params,
    )(chunks, temp, cure, tools, flat, steep, cell_bands)


def solution(mesh):
    return jax.shard_map(
        on_device,
        mesh=mesh,
        in_specs=(
            P(None, "plane", "depth"),
            P(("plane", "depth"), None),
            P(("plane", "depth"), None),
            P(),
            P(),
        ),
        out_specs=(
            P(("plane", "depth"), None),
            P(("plane", "depth"), None),
            P(None, ("plane", "depth"), None),
        ),
        check_vma=False,
    )
```

```python
import functools

import jax
import jax.numpy as jnp
import ml_dtypes
import numpy as np
from jax import lax
from jax.experimental import pallas as pl
from jax.experimental.pallas import tpu as pltpu
from jax.sharding import PartitionSpec as P

ROWS = 8
R1 = 6
R2 = 10
COARSE = 4
STEPS = 3

sigma_grad = 2.0
sigma_tensor = 3.3
conduct_matrix = 0.3
conduct_fiber = 1.5
time_step = 0.25
heat_release = 0.4
rate_first = 0.15
rate_second = 0.6
energy_first = 30.0
energy_second = 25.0
reference_temp = 4.2
tensor_eps = 1e-06

LANES = 128
HALO = 2
EDGE = HALO * COARSE + R1 + R2
EARLY = 96
GHOST = 3
COLUMN_ROWS = 2 * GHOST - 1
CODE_SCALE = 2.0**20
RIM = 2 * R1
BEFORE = -(-(R2 - R1) // COARSE)
AFTER = BEFORE
HALF = LANES // 2
ROW_KINDS = (1, 0, 0)
X_KINDS = (0, 1, 0)
DEPTH_KINDS = (0, 0, 1)


def smooth_taps(radius, sigma):
    offsets = np.arange(-radius, radius + 1) * 1.0
    weights = np.exp(-0.5 * offsets * offsets / (sigma * sigma))
    return weights / weights.sum()


def slope_taps(radius, sigma):
    offsets = np.arange(-radius, radius + 1) * 1.0
    weights = np.exp(-0.5 * offsets * offsets / (sigma * sigma))
    return offsets * weights / np.sum(offsets * offsets * weights)


def row_weights(count, radius, sigma):
    taps = smooth_taps(radius, sigma)
    result = np.zeros(count)
    for source in range(count):
        for target in range(count):
            offset = target - source
            if abs(offset) <= radius:
                result[source] += taps[offset + radius]
    return result


def rounded(taps):
    best = None
    for factor in np.linspace(1.0, 2.0, 20001)[:-1]:
        near = (taps * factor).astype(np.float32).astype(ml_dtypes.bfloat16).astype(np.float64)
        error = np.abs(near / factor - taps).sum()
        if best is None or error < best[0]:
            best = (error, near, factor)
    return best[1], best[2]


def as_bfloat16(matrix):
    return matrix.astype(np.float32).astype(ml_dtypes.bfloat16)


def halves(matrix):
    high = as_bfloat16(matrix)
    return high, as_bfloat16(matrix - high.astype(np.float64))


def sizes(width, depth):
    columns = width // COARSE + 2 * HALO
    cells = depth // COARSE + BEFORE + AFTER
    return columns, cells


def product_rows(width):
    places = [*range(R1, width - R1)]
    places += [None] * max(EARLY - len(places), 0)
    places += [*range(R1 - EDGE, R1), *range(width - R1, width + EDGE - R1)]
    return places + [None] * (-len(places) % 16)


GRAD_TAPS = tuple(
    rounded(taps(R1, sigma_grad)) for taps in (smooth_taps, slope_taps)
)
GRAD_FACTOR = GRAD_TAPS[0][1] ** 2 * GRAD_TAPS[1][1]


def grad_taps(kind):
    return GRAD_TAPS[kind][0]


def tap(taps, offset):
    radius = (len(taps) - 1) // 2
    return float(taps[offset + radius]) if abs(offset) <= radius else 0.0


def x_bands(width):
    places = product_rows(width)
    bands = np.zeros((2, len(places), width + 2 * EDGE))
    for kind in range(2):
        for row, place in enumerate(places):
            if place is not None:
                first = place + EDGE - R1
                bands[kind, row, first : first + 2 * R1 + 1] = grad_taps(kind)
    return bands


def rim_bands(rows):
    bands = np.zeros((3, 3 * LANES, LANES))
    for part in range(3):
        row_taps, depth_taps = grad_taps(ROW_KINDS[part]), grad_taps(DEPTH_KINDS[part])
        for source in range(rows):
            for target in range(rows):
                row_tap = tap(row_taps, source - target)
                for near in range(-RIM, RIM):
                    lane = source * RIM + near % RIM
                    if near >= 0:
                        lane += rows * RIM + LANES
                    for place in range(-R1, R1):
                        value = row_tap * tap(depth_taps, near - place)
                        bands[part, lane, target * 2 * R1 + R1 + place] = value
    return bands


def rim_cells(rows, depth, blocks):
    taps = smooth_taps(R2, sigma_tensor)
    weights = product_weights(rows)
    bands = np.zeros((blocks - 1, LANES, blocks * depth // COARSE))
    for boundary in range(blocks - 1):
        middle = (boundary + 1) * depth
        for cell in range(bands.shape[2]):
            for voxel in range(cell * COARSE, (cell + 1) * COARSE):
                for place in range(-R1, R1):
                    value = tap(taps, middle + place - voxel)
                    for row in range(rows):
                        bands[boundary, row * 2 * R1 + R1 + place, cell] += weights[row] * value
    return bands.reshape(-1, bands.shape[2])


def meeting_order(blocks):
    middle = blocks // 2
    return [middle, *range(1, middle), *range(middle + 1, blocks), 0]


def own_columns(count):
    products = (count + 2 * HALO) * COARSE + 2 * R2
    voxels = products + 2 * R1
    return -(-products // 16) * 16, -(-voxels // 8) * 8


def fold(voxels):
    return -(-voxels // 16) * 8


def rim_x_bands(count):
    products, voxels = own_columns(count)
    bands = np.zeros((2, products, -(-voxels // 16) * 16))
    valid = (count + 2 * HALO) * COARSE + 2 * R2
    for kind in range(2):
        for row in range(valid):
            bands[kind, row, row : row + 2 * R1 + 1] = grad_taps(kind)
    taps = smooth_taps(R2, sigma_tensor)
    coarse = np.zeros((16, products))
    for column in range(count + 2 * HALO):
        for voxel in range(column * COARSE, (column + 1) * COARSE):
            coarse[column, voxel : voxel + 2 * R2 + 1] += taps
    return bands.reshape(2 * products, -1), coarse


def depth_bands(depth):
    bands = np.zeros((2, depth, depth))
    for kind in range(2):
        for place in range(depth):
            for near in range(max(place - R1, 0), min(place + R1 + 1, depth)):
                bands[kind, near, place] = tap(grad_taps(kind), near - place)
    return bands


def product_weights(rows):
    return row_weights(rows, R2, sigma_tensor) / (255.0 * GRAD_FACTOR) ** 2


def coarse_depth_bands(depth):
    taps = smooth_taps(R2, sigma_tensor)
    columns, cells = sizes(0, depth)
    bands = np.zeros((depth, LANES))
    for cell in range(cells):
        for voxel in range(COARSE):
            place = (cell - BEFORE) * COARSE + voxel
            for near in range(max(place - R2, 0), min(place + R2 + 1, depth)):
                bands[near, cell] += tap(taps, near - place)
    return bands


def coarse_x_bands(width):
    taps = smooth_taps(R2, sigma_tensor)
    places = product_rows(width)
    columns, cells = sizes(width, 0)
    bands = np.zeros((-(-columns // 16) * 16, len(places)))
    for column in range(columns):
        for voxel in range(COARSE):
            middle = (column - HALO) * COARSE + voxel
            for row, place in enumerate(places):
                if place is not None:
                    bands[column, row] += tap(taps, place - middle)
    return bands


def stacked(*pieces):
    widest = max(piece.shape[1] for piece in pieces)
    padded = [np.pad(piece, ((0, 0), (0, widest - piece.shape[1]))) for piece in pieces]
    starts = np.cumsum([0] + [len(piece) for piece in pieces])
    return jnp.asarray(as_bfloat16(np.concatenate(padded))), tuple(int(start) for start in starts)


def two_parts(values):
    high = values.astype(jnp.bfloat16).astype(jnp.float32)
    return jnp.concatenate([high, (values - high).astype(jnp.bfloat16).astype(jnp.float32)], axis=0)


def joined(parts):
    half = parts.shape[0] // 2
    return parts[:half] + parts[half:]


def coded(values):
    values = values * CODE_SCALE
    return (values * jnp.abs(values)) * (values * values)


def decoded(values):
    size = jnp.sqrt(jnp.sqrt(jnp.abs(values))) * (1.0 / CODE_SCALE)
    return jnp.where(values < 0.0, -size, size)


def column_rows(temp, cure, at_end):
    count = temp.shape[0]
    first, second = (count - GHOST, count - GHOST + 1) if at_end else (0, 0)
    pad = jnp.zeros((8 - COLUMN_ROWS, temp.shape[1]), jnp.float32)
    return jnp.concatenate(
        [temp[first : first + GHOST, :], cure[second : second + GHOST - 1, :], pad], axis=0
    )


def chunk_rows(count, lanes):
    products, voxels = own_columns(count)
    held = count + 2 * HALO + 1 + COLUMN_ROWS * (lanes // LANES)
    return voxels + fold(voxels), -(-held // 16) * 16


def is_odd():
    return lax.rem(lax.axis_index("plane"), 2) == 1


def pack_kernel(
    intensity, temp_hbm, cure_hbm, x_hbm, z_hbm, far, near, grey, x_parts, z_parts, temp, cure,
    sems,
):
    rows, width, depth = intensity.shape
    copies = [
        pltpu.make_async_copy(intensity, grey, sems.at[0]),
        pltpu.make_async_copy(temp_hbm, temp, sems.at[1]),
        pltpu.make_async_copy(cure_hbm, cure, sems.at[2]),
        pltpu.make_async_copy(x_hbm, x_parts, sems.at[3]),
        pltpu.make_async_copy(z_hbm, z_parts, sems.at[4]),
    ]
    for copy in copies:
        copy.start()
    for copy in copies[:3]:
        copy.wait()
    odd = is_odd()
    sides = [
        two_parts(column_rows(temp, cure, at_end)).astype(jnp.bfloat16)
        for at_end in (False, True)
    ]

    def send(left, right):
        for place, target, columns in ((0, left, sides[0]), (width - EDGE, right, sides[1])):
            for pair in range(rows // 2):
                two = [grey[2 * pair + i, place : place + EDGE, :] for i in range(2)]
                two = jnp.concatenate(two, axis=0).astype(jnp.float32)
                target[2 * EDGE * pair : 2 * EDGE * (pair + 1), :] = two.astype(jnp.bfloat16)
            for slot in range(temp.shape[1] // LANES):
                at = rows * EDGE + 16 * slot
                target[at : at + 16, :] = columns[:, slot * LANES : (slot + 1) * LANES]

    @pl.when(odd)
    def _():
        send(near, far)

    @pl.when(jnp.logical_not(odd))
    def _():
        send(far, near)

    for copy in copies[3:]:
        copy.wait()


def packed_rows(values, size, first):
    depth = values[0].shape[1]
    lane = lax.broadcasted_iota(jnp.int32, values[0].shape, 1)
    packed = None
    for block, value in enumerate(values):
        shift = (size * block - first) % depth
        moved = value if shift == 0 else pltpu.roll(value, shift, 1)
        packed = moved if block == 0 else jnp.where(lane >= size * block, moved, packed)
    return packed


def edges_of(ref, rows):
    two = [
        ref[2 * EDGE * pair : 2 * EDGE * (pair + 1), :].astype(jnp.float32)
        for pair in range(rows // 2)
    ]
    voxels = [two[row // 2][row % 2 * EDGE : (row % 2 + 1) * EDGE] for row in range(rows)]
    slots = range(rows * EDGE, ref.shape[0], 16)
    columns = [joined(ref[at : at + 16, :].astype(jnp.float32)) for at in slots]
    return voxels, jnp.concatenate(columns, axis=1)


def product(first, second):
    return jnp.dot(first, second, preferred_element_type=jnp.float32)


def mirrored_filter(kind, values, even):
    rows = len(values)
    use_sum = even == (kind == 0)
    sign = 1.0 if use_sum else -1.0
    half = [values[row] + sign * values[rows - 1 - row] for row in range(rows // 2)]
    results = []
    for row in range(rows // 2):
        total = None
        for source, value in enumerate(half):
            near = tap(grad_taps(kind), source - row)
            far = tap(grad_taps(kind), rows - 1 - source - row)
            weight = 0.5 * (near + sign * far)
            total = weight * value if total is None else total + weight * value
        results.append(total)
    return results


def weighted_products(three, weight):
    pairs = ((0, 0), (1, 1), (2, 2), (0, 1), (0, 2), (1, 2))
    first = [weight * value for value in three]
    return [first[a] * three[b] for a, b in pairs]


def late_mask(count, width):
    row = lax.broadcasted_iota(jnp.int32, (count, LANES), 0)
    left = max(width - 2 * R1 - EARLY, 0)
    place = jnp.where(row < left + EDGE, row - left + R1 - EDGE, row - left - EDGE + width - R1)
    place = place + lax.axis_index("plane") * width
    inside = (place >= 0) & (place < lax.axis_size("plane") * width)
    return jnp.where(inside | (row < left), 1.0, 0.0)


USED = (0, 1, 2, 5)
UNUSED = (3, 4)


def all_sums(products, coarse, sx):
    sums = [None] * 6
    for kinds in (USED, UNUSED):
        tiles = [tile for index in kinds for tile in products[index]]
        along = product(sx, jnp.concatenate(tiles, axis=1)).astype(jnp.bfloat16)
        step = along.shape[1] // len(kinds)
        parts = [along[:, index * step : (index + 1) * step] for index in range(len(kinds))]
        total = product(jnp.concatenate(parts, axis=0), coarse)
        high = sx.shape[0]
        for index, kind in enumerate(kinds):
            sums[kind] = total[index * high : (index + 1) * high]
    return sums


def tensor_sums(across, sx, mask, diagonal, z_parts, filtered, grads):
    double = diagonal.shape[1]
    depth, pairs = double // 2, across.shape[1] // double
    rows, count = 2 * pairs, across.shape[0] // 2
    for start in range(0, count, 16):
        kinds = [
            [
                across[kind * count + start : kind * count + start + 16, row * depth : (row + 1) * depth]
                for row in range(rows)
            ]
            for kind in range(2)
        ]
        for part in range(3):
            values = kinds[X_KINDS[part]]
            results = mirrored_filter(ROW_KINDS[part], values, True)
            results += mirrored_filter(ROW_KINDS[part], values, False)
            for row, result in enumerate(results):
                at = (part * pairs + row // 2) * count + start
                lanes = slice((row % 2) * depth, (row % 2 + 1) * depth)
                filtered[at : at + 16, lanes] = result.astype(jnp.bfloat16)

    at = 2 * pairs * count
    grads[:at] = product(filtered[:at, :], diagonal[0:double, :])
    grads[at:] = product(filtered[at:, :], diagonal[double : 2 * double, :])

    weights = product_weights(rows)
    layer = lax.axis_index("depth")
    first, last = layer == 0, layer == lax.axis_size("depth") - 1
    place = lax.broadcasted_iota(jnp.int32, (16, depth), 1)
    complete = ((place >= R1) | first) & ((place < depth - R1) | last)
    complete = jnp.where(complete, 1.0, 0.0)
    groups = [[] for _ in range(6)]
    for start in range(0, count, 16):
        inside = complete if mask is None else complete * mask[start : start + 16]
        totals = None
        for row in range(rows):
            lanes = slice((row % 2) * depth, (row % 2 + 1) * depth)
            three = []
            for part in range(3):
                at = (part * pairs + row // 2) * count + start
                three.append(grads[at : at + 16, lanes])
            terms = weighted_products(three, 2.0 * float(weights[row % (rows // 2)]))
            totals = terms if row == 0 else [a + b for a, b in zip(totals, terms)]
        for index in range(6):
            groups[index].append((totals[index] * inside).astype(jnp.bfloat16))
    products = [[jnp.concatenate(group, axis=0)] for group in groups]
    return all_sums(products, z_parts[double : double + depth, :], sx)


def rim_tiles(values):
    rows, depth = len(values), values[0].shape[1]
    below = packed_rows(values, RIM, depth - RIM)
    above = pltpu.roll(packed_rows(values, RIM, 0), rows * RIM, 1)
    lane = lax.broadcasted_iota(jnp.int32, below.shape, 1)
    return [jnp.where(lane < rows * RIM, below, above), above, pltpu.roll(above, HALF, 1)]


def early_kernel(
    starts, grey, x_parts, z_parts, sums, diagonal, sides, tiles, across, filtered, grads
):
    rows, width, depth = grey.shape
    double = 2 * depth
    empty = jnp.zeros((depth, depth), jnp.bfloat16)
    for kind in range(2):
        for half in range(2):
            at = pl.ds(kind * double + half * depth, depth)
            band = z_parts[kind * depth : (kind + 1) * depth, :]
            diagonal[at, half * depth : (half + 1) * depth] = band
            diagonal[at, (1 - half) * depth : (2 - half) * depth] = empty
    values = [grey[row].astype(jnp.float32) for row in range(rows)]
    whole = jnp.concatenate([value.astype(jnp.bfloat16) for value in values], axis=1)
    result = product(x_parts[starts[0] : starts[2], :width], whole)
    across[...] = result[: starts[1]]
    sides[...] = result[starts[1] :]
    sx = x_parts[starts[2] : starts[3], :EARLY]
    results = tensor_sums(across, sx, None, diagonal, z_parts, filtered, grads)
    for index, kind in enumerate(USED):
        sums[index] = results[kind]
    for index, tile in enumerate(rim_tiles(values)):
        tiles[index] = tile


def late_kernel(
    starts, width, far, near, x_late, z_parts, diagonal, early_sums, sides, own_tiles, temp, cure,
    out_hbm, across, filtered, grads, out, sems,
):
    double = diagonal.shape[1]
    depth = double // 2
    rows = across.shape[1] // depth
    count, lanes = temp.shape
    odd = is_odd()
    depths, layer = lax.axis_size("depth"), lax.axis_index("depth")
    outer, outer_columns = edges_of(far, rows)
    inner, inner_columns = edges_of(near, rows)
    values = []
    for row in range(rows):
        left = jnp.where(odd, inner[row], outer[row])
        right = jnp.where(odd, outer[row], inner[row])
        values.append(jnp.concatenate([left, right], axis=0))
    left = jnp.where(odd, inner_columns, outer_columns)
    right = jnp.where(odd, outer_columns, inner_columns)

    late = across.shape[0] // 2
    halos = jnp.concatenate([value.astype(jnp.bfloat16) for value in values], axis=1)
    across[...] = sides[...] + product(x_late[starts[0] : starts[1], : 2 * EDGE], halos)

    products_x, voxels = own_columns(count)
    folded, stride = fold(voxels), COARSE * count
    tiles = [
        jnp.concatenate([tile[:EDGE], own_tiles[index], tile[EDGE:]], axis=0)
        for index, tile in enumerate(rim_tiles(values))
    ]
    missing = stride * (depths - 1) + voxels - tiles[0].shape[0]
    if missing > 0:
        spare = jnp.zeros((-(-missing // 8) * 8, LANES), jnp.float32)
        tiles = [jnp.concatenate([tile, spare], axis=0) for tile in tiles]

    height = count + 2 * HALO
    half_lane = lax.broadcasted_iota(jnp.int32, (folded, LANES), 1) < HALF
    order = meeting_order(out.shape[0])
    for position, target in enumerate(order):
        at = stride * target
        second = jnp.where(
            half_lane,
            tiles[1][at : at + folded],
            tiles[2][at + voxels - folded : at + voxels],
        )
        rims = jnp.concatenate([tiles[0][at : at + voxels], second], axis=0)
        out[position, 0 : voxels + folded, :] = rims.astype(jnp.bfloat16)
    split = (pl.ds(0, voxels + folded), pl.ds(voxels + folded, out.shape[1] - voxels - folded))
    copies = [
        pltpu.make_async_copy(out.at[:, part, :], out_hbm.at[:, part, :], sems.at[index])
        for index, part in enumerate(split)
    ]
    copies[0].start()

    sx = x_late[starts[1] : starts[2], :late]
    results = tensor_sums(
        across, sx, late_mask(late, width), diagonal, z_parts, filtered, grads
    )
    yy, xx, zz, xz = [early_sums[index] + results[kind] for index, kind in enumerate(USED)]
    trace = yy + xx + zz
    lane = lax.broadcasted_iota(jnp.int32, trace.shape, 1)
    columns, cells = sizes(width, depth)
    tail = 4 * cells - LANES
    joint = pltpu.roll(xz, 3 * cells, 1)
    rest = jnp.where(lane < tail, joint, 0.0)
    rest = pltpu.roll(rest, 0, 1, stride=tail, stride_axis=0)
    for index, part in ((2, zz), (1, xx), (0, trace)):
        moved = part if index == 0 else pltpu.roll(part, index * cells, 1)
        joint = jnp.where(lane < (index + 1) * cells, moved, joint)

    own_first, own_last = column_rows(temp, cure, False), column_rows(temp, cure, True)
    half = chunk_rows(count, lanes)[1]
    for position, target in enumerate(order):
        piece = jnp.where(layer == target - 1, own_last, 0.0)
        piece = jnp.where(layer == target + 1, own_first, piece)
        if target == 0:
            piece = jnp.where(layer == depths - 1, left, piece)
        if target == out.shape[0] - 1:
            piece = jnp.where(layer == 0, right, piece)
        mine = slice(count * target, count * target + height)
        pieces = [coded(joint[mine]), coded(jnp.sum(rest[mine], axis=0, keepdims=True))]
        for slot in range(lanes // LANES):
            part = piece[:, slot * LANES : (slot + 1) * LANES]
            pieces += [part[:GHOST] - reference_temp, part[GHOST:COLUMN_ROWS]]
        filled = sum(part.shape[0] for part in pieces)
        if filled < half:
            pieces.append(jnp.zeros((half - filled, LANES), jnp.float32))
        out[position, voxels + folded :, :] = jnp.concatenate(pieces, axis=0).astype(jnp.bfloat16)
    copies[1].start()
    for copy in copies:
        copy.wait()


def rim_sums(chunks, count, starts, flat, steep, cells):
    parts = chunks.shape[0]
    rows_x, voxels = own_columns(count)
    folded = fold(voxels)
    tall = -(-voxels // 16) * 16
    spare = [jnp.zeros((tall - voxels, LANES), jnp.float32)] if tall > voxels else []
    tiles = []
    order = meeting_order(parts)
    for part in range(parts):
        rims = chunks[order.index(part), 0 : voxels + folded, :].astype(jnp.float32)
        second = rims[voxels:]
        second = [second[: voxels - folded], pltpu.roll(second, HALF, 1)]
        for tile in ([rims[:voxels]], second)[: 2 if part else 1]:
            tiles.append(jnp.concatenate(tile + spare, axis=0).astype(jnp.bfloat16))
    result = product(
        steep[starts[1] : starts[2], :tall], jnp.concatenate(tiles, axis=1)
    ).astype(jnp.bfloat16)
    kinds = []
    for kind in range(2):
        values = result[kind * rows_x : (kind + 1) * rows_x]
        tile = lambda index: values[:, index * LANES : (index + 1) * LANES]
        stack = [
            jnp.concatenate(
                [tile(max(2 * part - 1, 0)), tile(2 * part + 1), tile(2 * part + 2)], axis=1
            )
            for part in range(parts - 1)
        ]
        kinds.append(jnp.concatenate(stack, axis=0))
    both = product(kinds[0], flat[...])
    three = (both[:, :LANES], product(kinds[1], steep[starts[0] : starts[1], :]), both[:, LANES:])

    index = lax.axis_index("plane") * lax.axis_size("depth") + lax.axis_index("depth")
    total = lax.axis_size("plane") * lax.axis_size("depth") * count * COARSE
    place = lax.rem(lax.broadcasted_iota(jnp.int32, three[0].shape, 0), rows_x)
    place = place + (index * count - HALO) * COARSE - R2
    inside = jnp.where((place >= 0) & (place < total), 1.0, 0.0)
    products = [
        [
            term[part * rows_x : (part + 1) * rows_x].astype(jnp.bfloat16)
            for part in range(parts - 1)
        ]
        for term in weighted_products(three, inside)
    ]
    return all_sums(products, cells[...], steep[starts[2] : starts[3], :rows_x])


def cure_kernel(
    cells, starts, chunks, temp_in, cure_in, tools, flat, steep, rim_bands, temp_hbm, cure_hbm,
    conduct_hbm, temp_out, cure_out, conduct_out, sems,
):
    count, lanes = temp_in.shape
    parts = chunks.shape[0]
    planes, depths = lax.axis_size("plane"), lax.axis_size("depth")
    plane, layer = lax.axis_index("plane"), lax.axis_index("depth")
    height = count + 2 * HALO
    own = cells - BEFORE - AFTER
    lane = lax.broadcasted_iota(jnp.int32, (16, lanes), 1)
    row = lax.broadcasted_iota(jnp.int32, (16, lanes), 0)
    at_sums, half = chunk_rows(count, lanes)
    tail = 4 * cells - LANES
    narrow_lane = lax.broadcasted_iota(jnp.int32, (16, LANES), 1)
    order = meeting_order(parts)

    near = rim_sums(chunks, count, starts, flat, steep, rim_bands)
    sums = [near[0] + near[1] + near[2], near[1], near[2], near[5]]
    blocks = [chunks[order.index(part), at_sums:, :].astype(jnp.float32) for part in range(parts)]
    columns = [
        jnp.concatenate(
            [
                block[at : at + COLUMN_ROWS]
                for at in range(
                    height + 1, height + 1 + COLUMN_ROWS * (lanes // LANES), COLUMN_ROWS
                )
            ],
            axis=1,
        )
        for block in blocks
    ]
    blocks = [decoded(block[0:16]) for block in blocks]
    tails = [block[height : height + 1] for block in blocks]
    if parts % 8:
        tails.append(jnp.zeros((-parts % 8, LANES), jnp.float32))
    tails = jnp.concatenate(tails, axis=0)
    tails = pltpu.roll(tails, lax.rem(LANES - lax.rem(tail * count * layer, LANES), LANES), 1)
    narrow_row = lax.broadcasted_iota(jnp.int32, (16, LANES), 0)
    rests = [jnp.zeros((16, LANES), jnp.float32) for _ in range(parts)]
    for column in range(height):
        moved = pltpu.roll(tails, LANES - tail * column, 1) if column else tails
        for part in range(parts):
            rests[part] = jnp.where(narrow_row == column, moved[part : part + 1], rests[part])
    for part in range(parts):
        first_cell = own * part - BEFORE
        here = (lane >= first_cell) & (lane < first_cell + cells)
        values = blocks[part]
        joint = values[0:16]
        xz = pltpu.roll(jnp.where(narrow_lane < tail, rests[part], joint), LANES - 3 * cells, 1)
        for index in range(4):
            chunk = xz if index == 3 else joint
            if lanes > LANES:
                spare = jnp.zeros((16, lanes - LANES), jnp.float32)
                chunk = jnp.concatenate([chunk, spare], axis=1)
            shift = (first_cell - (index % 3) * cells) % lanes
            moved = chunk if shift == 0 else pltpu.roll(chunk, shift, 1)
            sums[index] = sums[index] + jnp.where(here, moved, 0.0)
    trace = sums[0]
    scale = (conduct_fiber - conduct_matrix) / (2.0 * trace + tensor_eps)
    conduct = [
        conduct_matrix + scale * (trace - sums[1]),
        -scale * sums[3],
        conduct_matrix + scale * (trace - sums[2]),
    ]
    for kind in range(3):
        conduct_out[kind] = conduct[kind][HALO : HALO + count]
    copies = [
        pltpu.make_async_copy(conduct_out, conduct_hbm, sems.at[0]),
        pltpu.make_async_copy(temp_out, temp_hbm, sems.at[1]),
        pltpu.make_async_copy(cure_out, cure_hbm, sems.at[2]),
    ]
    copies[0].start()

    before, after = columns[parts - 1], columns[0]
    for part in range(parts - 1):
        before = jnp.where(layer == part + 1, columns[part], before)
        after = jnp.where(layer == part, columns[part + 1], after)
    spare = jnp.full((16 - count - 2 * GHOST, lanes), 0.5, jnp.float32)
    temp = jnp.concatenate([
            before[:GHOST] + reference_temp,
            temp_in[...],
            after[:GHOST] + reference_temp,
            8.0 * spare,
        ], axis=0)
    cure = jnp.concatenate([spare[:1], before[GHOST:], cure_in[...], after[GHOST:], spare[:1], spare], axis=0)
    gap = GHOST - HALO
    xx, xz, zz = [pltpu.roll(part, gap, 0) for part in conduct]

    first = (plane == 0) & (layer == 0)
    last = (plane == planes - 1) & (layer == depths - 1)
    for step in range(STEPS):
        top, bottom = tools[2 * step : 2 * step + 1, :], tools[2 * step + 1 : 2 * step + 2, :]
        temp = jnp.where((row < GHOST) & first, temp[GHOST : GHOST + 1], temp)
        temp = jnp.where(
            (row >= GHOST + count) & last, temp[GHOST + count - 1 : GHOST + count], temp
        )
        cooler = jnp.where(lane == 0, top, pltpu.roll(temp, 1, 1))
        later = jnp.where(lane == lanes - 1, bottom, pltpu.roll(temp, lanes - 1, 1))
        slant = later - cooler
        second_x = pltpu.roll(temp, 15, 0) - 2.0 * temp + pltpu.roll(temp, 1, 0)
        second_z = later - 2.0 * temp + cooler
        cross = 0.25 * (pltpu.roll(slant, 15, 0) - pltpu.roll(slant, 1, 0))
        spread = xx * second_x + 2.0 * xz * cross + zz * second_z
        inverse = 1.0 / reference_temp - 1.0 / temp
        left = 1.0 - cure
        rate = rate_first * jnp.exp(energy_first * inverse) + rate_second * jnp.exp(
            energy_second * inverse
        ) * jnp.sqrt(cure)
        rate = rate * (left * jnp.sqrt(left))
        temp = temp + time_step * (spread + heat_release * rate)
        cure = cure + time_step * rate
    temp_out[...] = temp[GHOST : GHOST + count]
    cure_out[...] = cure[GHOST : GHOST + count]
    for copy in copies[1:]:
        copy.start()
    for copy in copies:
        copy.wait()


def on_device(intensity, temp_start, cure_start, tool_levels, plan):
    rows, width, depth = intensity.shape
    count, lanes = temp_start.shape
    planes, depths = lax.axis_size("plane"), lax.axis_size("depth")
    columns, cells = sizes(width, depth)
    bf16 = jnp.bfloat16
    slots = rows * EDGE + 16 * (lanes // LANES)
    params = pltpu.CompilerParams(vmem_limit_bytes=24 * 1024 * 1024)
    vmem = pl.BlockSpec(memory_space=pltpu.VMEM)
    stay = pl.BlockSpec(memory_space=pltpu.HBM)

    fixed = lambda values: pltpu.with_memory_space_constraint(values, pltpu.HBM)
    bands, coarse = x_bands(width), coarse_x_bands(width)
    late = bands.shape[1] - EARLY
    middle = bands[:, :EARLY, EDGE : EDGE + width]
    sides = bands[:, EARLY:].reshape(2 * late, -1)
    x_hbm, early_starts = stacked(
        middle.reshape(2 * EARLY, -1), sides[:, EDGE : EDGE + width], coarse[:, :EARLY]
    )
    z_hbm, _ = stacked(*depth_bands(depth), coarse_depth_bands(depth))
    halos = np.concatenate([sides[:, :EDGE], sides[:, EDGE + width :]], axis=1)
    x_late, late_starts = stacked(halos, coarse[:, EARLY:])
    rims = rim_bands(rows)
    flat, _ = stacked(np.concatenate([rims[0], rims[2]], axis=1))
    steep, rim_starts = stacked(rims[1], *rim_x_bands(count))
    cell_bands, _ = stacked(rim_cells(rows, depth, depths))
    far, near, grey, x_parts, z_parts, temp, cure = pl.pallas_call(
        pack_kernel,
        name="pack",
        out_shape=(
            pltpu.VMEM((slots, depth), bf16),
            pltpu.VMEM((slots, depth), bf16),
            pltpu.VMEM((rows, width, depth), jnp.int32),
            pltpu.VMEM(x_hbm.shape, bf16),
            pltpu.VMEM(z_hbm.shape, bf16),
            pltpu.VMEM((count, lanes), jnp.float32),
            pltpu.VMEM((count, lanes), jnp.float32),
        ),
        in_specs=[stay] * 5,
        scratch_shapes=[
            pltpu.SemaphoreType.DMA((5,)),
        ],
        compiler_params=params,
    )(*[fixed(values) for values in (intensity, temp_start, cure_start, x_hbm, z_hbm)])

    def moved(values, pairs):
        index = [(p * depths + d, q * depths + e) for (p, d), (q, e) in pairs]
        return lax.ppermute(values, ("plane", "depth"), index)

    def swapped(values, first):
        pairs = [(p, p + 1) for p in range(first, planes - 1, 2)]
        pairs += [(q, p) for p, q in pairs]
        return moved(values, [((p, d), (q, d)) for p, q in pairs for d in range(depths)])

    far = swapped(far, 1)
    near = swapped(near, 0)

    high = coarse.shape[0]

    def scratch(count):
        return [
            pltpu.VMEM((2 * count, rows * depth), jnp.float32),
            pltpu.VMEM((3 * rows // 2 * count, 2 * depth), bf16),
            pltpu.VMEM((3 * rows // 2 * count, 2 * depth), jnp.float32),
        ]

    def cost(count):
        return pl.CostEstimate(
            flops=2 * rows * (2 * count) * 160 * depth * 4,
            bytes_accessed=4_000_000,
            transcendentals=0,
        )

    early_sums, diagonal, sides, own_tiles = pl.pallas_call(
        functools.partial(early_kernel, early_starts),
        name="early",
        out_shape=(
            pltpu.VMEM((len(USED), high, LANES), jnp.float32),
            pltpu.VMEM((4 * depth, 2 * depth), bf16),
            pltpu.VMEM((2 * late, rows * depth), jnp.float32),
            pltpu.VMEM((3, width, LANES), jnp.float32),
        ),
        scratch_shapes=scratch(EARLY),
        cost_estimate=cost(EARLY),
        compiler_params=params,
    )(grey, x_parts, z_parts)

    products_x, voxels = own_columns(count)
    at_sums, half = chunk_rows(count, lanes)
    chunk_shape = (depths, at_sums + half, LANES)
    chunks = pl.pallas_call(
        functools.partial(late_kernel, late_starts, width),
        name="late",
        out_shape=pltpu.HBM(chunk_shape, bf16),
        in_specs=[vmem] * 10,
        out_specs=stay,
        scratch_shapes=scratch(late)
        + [pltpu.VMEM(chunk_shape, bf16), pltpu.SemaphoreType.DMA((2,))],
        cost_estimate=cost(late),
        compiler_params=params,
    )(far, near, x_late, z_parts, diagonal, early_sums, sides, own_tiles, temp, cure)

    faces = plan.reshape(2 * STEPS, 1) == jnp.arange(tool_levels.shape[0], dtype=jnp.int32)
    tools = jnp.sum(
        jnp.where(faces, tool_levels, jnp.zeros_like(tool_levels)), axis=1, keepdims=True
    )

    chunks = lax.all_to_all(
        chunks,
        "depth",
        split_axis=0,
        concat_axis=0,
        tiled=True,
        axis_index_groups=[meeting_order(depths)],
    )

    return pl.pallas_call(
        functools.partial(cure_kernel, cells, rim_starts),
        name="cure",
        out_shape=(
            pltpu.HBM((count, lanes), jnp.float32),
            pltpu.HBM((count, lanes), jnp.float32),
            pltpu.HBM((3, count, lanes), jnp.float32),
        ),
        in_specs=[vmem] * 7,
        out_specs=(stay, stay, stay),
        scratch_shapes=[
            pltpu.VMEM((count, lanes), jnp.float32),
            pltpu.VMEM((count, lanes), jnp.float32),
            pltpu.VMEM((3, count, lanes), jnp.float32),
            pltpu.SemaphoreType.DMA((3,)),
        ],
        compiler_params=params,
    )(chunks, temp, cure, tools, flat, steep, cell_bands)


def solution(mesh):
    return jax.shard_map(
        on_device,
        mesh=mesh,
        in_specs=(
            P(None, "plane", "depth"),
            P(("plane", "depth"), None),
            P(("plane", "depth"), None),
            P(),
            P(),
        ),
        out_specs=(
            P(("plane", "depth"), None),
            P(("plane", "depth"), None),
            P(None, ("plane", "depth"), None),
        ),
        check_vma=False,
    )
```

```python
import functools

import jax
import jax.numpy as jnp
import ml_dtypes
import numpy as np
from jax import lax
from jax.experimental import pallas as pl
from jax.experimental.pallas import tpu as pltpu
from jax.sharding import PartitionSpec as P

ROWS = 8
R1 = 6
R2 = 10
COARSE = 4
STEPS = 3

sigma_grad = 2.0
sigma_tensor = 3.3
conduct_matrix = 0.3
conduct_fiber = 1.5
time_step = 0.25
heat_release = 0.4
rate_first = 0.15
rate_second = 0.6
energy_first = 30.0
energy_second = 25.0
reference_temp = 4.2
tensor_eps = 1e-06

LANES = 128
HALO = 2
EDGE = HALO * COARSE + R1 + R2
EARLY = 96
GHOST = 3
COLUMN_ROWS = 2 * GHOST - 1
CODE_SCALE = 2.0**20
RIM = 2 * R1
BEFORE = -(-(R2 - R1) // COARSE)
AFTER = BEFORE
HALF = LANES // 2
ROW_KINDS = (1, 0, 0)
X_KINDS = (0, 1, 0)
DEPTH_KINDS = (0, 0, 1)


def smooth_taps(radius, sigma):
    offsets = np.arange(-radius, radius + 1) * 1.0
    weights = np.exp(-0.5 * offsets * offsets / (sigma * sigma))
    return weights / weights.sum()


def slope_taps(radius, sigma):
    offsets = np.arange(-radius, radius + 1) * 1.0
    weights = np.exp(-0.5 * offsets * offsets / (sigma * sigma))
    return offsets * weights / np.sum(offsets * offsets * weights)


def row_weights(count, radius, sigma):
    taps = smooth_taps(radius, sigma)
    result = np.zeros(count)
    for source in range(count):
        for target in range(count):
            offset = target - source
            if abs(offset) <= radius:
                result[source] += taps[offset + radius]
    return result


def rounded(taps):
    best = None
    for factor in np.linspace(1.0, 2.0, 20001)[:-1]:
        near = (taps * factor).astype(np.float32).astype(ml_dtypes.bfloat16).astype(np.float64)
        error = np.abs(near / factor - taps).sum()
        if best is None or error < best[0]:
            best = (error, near, factor)
    return best[1], best[2]


def as_bfloat16(matrix):
    return matrix.astype(np.float32).astype(ml_dtypes.bfloat16)


def halves(matrix):
    high = as_bfloat16(matrix)
    return high, as_bfloat16(matrix - high.astype(np.float64))


def sizes(width, depth):
    columns = width // COARSE + 2 * HALO
    cells = depth // COARSE + BEFORE + AFTER
    return columns, cells


def product_rows(width):
    places = [*range(R1, width - R1)]
    places += [None] * max(EARLY - len(places), 0)
    places += [*range(R1 - EDGE, R1), *range(width - R1, width + EDGE - R1)]
    return places + [None] * (-len(places) % 16)


GRAD_TAPS = tuple(
    rounded(taps(R1, sigma_grad)) for taps in (smooth_taps, slope_taps)
)
GRAD_FACTOR = GRAD_TAPS[0][1] ** 2 * GRAD_TAPS[1][1]


def grad_taps(kind):
    return GRAD_TAPS[kind][0]


def tap(taps, offset):
    radius = (len(taps) - 1) // 2
    return float(taps[offset + radius]) if abs(offset) <= radius else 0.0


def x_bands(width):
    places = product_rows(width)
    bands = np.zeros((2, len(places), width + 2 * EDGE))
    for kind in range(2):
        for row, place in enumerate(places):
            if place is not None:
                first = place + EDGE - R1
                bands[kind, row, first : first + 2 * R1 + 1] = grad_taps(kind)
    return bands


def rim_bands(rows):
    bands = np.zeros((3, 2 * LANES, LANES))
    for part in range(3):
        row_taps, depth_taps = grad_taps(ROW_KINDS[part]), grad_taps(DEPTH_KINDS[part])
        for source in range(rows):
            for target in range(rows):
                row_tap = tap(row_taps, source - target)
                for near in range(-RIM, RIM):
                    lane = source * RIM + near % RIM
                    if near >= 0:
                        lane += rows * RIM
                    for place in range(-R1, R1):
                        value = row_tap * tap(depth_taps, near - place)
                        bands[part, lane, target * 2 * R1 + R1 + place] = value
    return bands


def rim_cells(rows, depth, blocks):
    taps = smooth_taps(R2, sigma_tensor)
    weights = product_weights(rows)
    bands = np.zeros((blocks - 1, LANES, blocks * depth // COARSE))
    for boundary in range(blocks - 1):
        middle = (boundary + 1) * depth
        for cell in range(bands.shape[2]):
            for voxel in range(cell * COARSE, (cell + 1) * COARSE):
                for place in range(-R1, R1):
                    value = tap(taps, middle + place - voxel)
                    for row in range(rows):
                        bands[boundary, row * 2 * R1 + R1 + place, cell] += weights[row] * value
    return bands.reshape(-1, bands.shape[2])


def meeting_order(blocks):
    middle = blocks // 2
    return [*range(middle, blocks), *range(middle)]


def own_columns(count):
    products = (count + 2 * HALO) * COARSE + 2 * R2
    voxels = products + 2 * R1
    return -(-products // 16) * 16, -(-voxels // 8) * 8


def fold(voxels):
    return -(-voxels // 16) * 8


def rim_x_bands(count):
    products, voxels = own_columns(count)
    bands = np.zeros((2, products, -(-voxels // 16) * 16))
    valid = (count + 2 * HALO) * COARSE + 2 * R2
    for kind in range(2):
        for row in range(valid):
            bands[kind, row, row : row + 2 * R1 + 1] = grad_taps(kind)
    taps = smooth_taps(R2, sigma_tensor)
    coarse = np.zeros((16, products))
    for column in range(count + 2 * HALO):
        for voxel in range(column * COARSE, (column + 1) * COARSE):
            coarse[column, voxel : voxel + 2 * R2 + 1] += taps
    return bands.reshape(2 * products, -1), coarse


def depth_bands(depth):
    bands = np.zeros((2, depth, depth))
    for kind in range(2):
        for place in range(depth):
            for near in range(max(place - R1, 0), min(place + R1 + 1, depth)):
                bands[kind, near, place] = tap(grad_taps(kind), near - place)
    return bands


def product_weights(rows):
    return row_weights(rows, R2, sigma_tensor) / (255.0 * GRAD_FACTOR) ** 2


def coarse_depth_bands(depth):
    taps = smooth_taps(R2, sigma_tensor)
    columns, cells = sizes(0, depth)
    bands = np.zeros((depth, LANES))
    for cell in range(cells):
        for voxel in range(COARSE):
            place = (cell - BEFORE) * COARSE + voxel
            for near in range(max(place - R2, 0), min(place + R2 + 1, depth)):
                bands[near, cell] += tap(taps, near - place)
    return bands


def coarse_x_bands(width):
    taps = smooth_taps(R2, sigma_tensor)
    places = product_rows(width)
    columns, cells = sizes(width, 0)
    bands = np.zeros((-(-columns // 16) * 16, len(places)))
    for column in range(columns):
        for voxel in range(COARSE):
            middle = (column - HALO) * COARSE + voxel
            for row, place in enumerate(places):
                if place is not None:
                    bands[column, row] += tap(taps, place - middle)
    return bands


def stacked(*pieces):
    widest = max(piece.shape[1] for piece in pieces)
    padded = [np.pad(piece, ((0, 0), (0, widest - piece.shape[1]))) for piece in pieces]
    starts = np.cumsum([0] + [len(piece) for piece in pieces])
    return jnp.asarray(as_bfloat16(np.concatenate(padded))), tuple(int(start) for start in starts)


def two_parts(values):
    high = values.astype(jnp.bfloat16).astype(jnp.float32)
    return jnp.concatenate([high, (values - high).astype(jnp.bfloat16).astype(jnp.float32)], axis=0)


def joined(parts):
    half = parts.shape[0] // 2
    return parts[:half] + parts[half:]


def coded(values):
    values = values * CODE_SCALE
    return (values * jnp.abs(values)) * (values * values)


def decoded(values):
    size = jnp.sqrt(jnp.sqrt(jnp.abs(values))) * (1.0 / CODE_SCALE)
    return jnp.where(values < 0.0, -size, size)


def column_rows(temp, cure, at_end):
    count = temp.shape[0]
    first, second = (count - GHOST, count - GHOST + 1) if at_end else (0, 0)
    pad = jnp.zeros((8 - COLUMN_ROWS, temp.shape[1]), jnp.float32)
    return jnp.concatenate(
        [temp[first : first + GHOST, :], cure[second : second + GHOST - 1, :], pad], axis=0
    )


def chunk_rows(count, lanes):
    products, voxels = own_columns(count)
    held = count + 2 * HALO + 1 + COLUMN_ROWS * (lanes // LANES)
    return voxels + fold(voxels), -(-held // 16) * 16


def is_odd():
    return lax.rem(lax.axis_index("plane"), 2) == 1


def pack_kernel(
    intensity, temp_hbm, cure_hbm, x_hbm, z_hbm, far, near, grey, x_parts, z_parts, temp, cure,
    sems,
):
    rows, width, depth = intensity.shape
    copies = [
        pltpu.make_async_copy(intensity, grey, sems.at[0]),
        pltpu.make_async_copy(temp_hbm, temp, sems.at[1]),
        pltpu.make_async_copy(cure_hbm, cure, sems.at[2]),
        pltpu.make_async_copy(x_hbm, x_parts, sems.at[3]),
        pltpu.make_async_copy(z_hbm, z_parts, sems.at[4]),
    ]
    for copy in copies:
        copy.start()
    for copy in copies[:3]:
        copy.wait()
    odd = is_odd()
    sides = [
        two_parts(column_rows(temp, cure, at_end)).astype(jnp.bfloat16)
        for at_end in (False, True)
    ]

    def send(left, right):
        for place, target, columns in ((0, left, sides[0]), (width - EDGE, right, sides[1])):
            for pair in range(rows // 2):
                two = [grey[2 * pair + i, place : place + EDGE, :] for i in range(2)]
                two = jnp.concatenate(two, axis=0).astype(jnp.float32)
                target[2 * EDGE * pair : 2 * EDGE * (pair + 1), :] = two.astype(jnp.bfloat16)
            for slot in range(temp.shape[1] // LANES):
                at = rows * EDGE + 16 * slot
                target[at : at + 16, :] = columns[:, slot * LANES : (slot + 1) * LANES]

    @pl.when(odd)
    def _():
        send(near, far)

    @pl.when(jnp.logical_not(odd))
    def _():
        send(far, near)

    for copy in copies[3:]:
        copy.wait()


def packed_rows(values, size, first):
    depth = values[0].shape[1]
    lane = lax.broadcasted_iota(jnp.int32, values[0].shape, 1)
    packed = None
    for block, value in enumerate(values):
        shift = (size * block - first) % depth
        moved = value if shift == 0 else pltpu.roll(value, shift, 1)
        packed = moved if block == 0 else jnp.where(lane >= size * block, moved, packed)
    return packed


def edges_of(ref, rows):
    two = [
        ref[2 * EDGE * pair : 2 * EDGE * (pair + 1), :].astype(jnp.float32)
        for pair in range(rows // 2)
    ]
    voxels = [two[row // 2][row % 2 * EDGE : (row % 2 + 1) * EDGE] for row in range(rows)]
    slots = range(rows * EDGE, ref.shape[0], 16)
    columns = [joined(ref[at : at + 16, :].astype(jnp.float32)) for at in slots]
    return voxels, jnp.concatenate(columns, axis=1)


def product(first, second):
    return jnp.dot(first, second, preferred_element_type=jnp.float32)


def mirrored_filter(kind, values, even):
    rows = len(values)
    use_sum = even == (kind == 0)
    sign = 1.0 if use_sum else -1.0
    half = [values[row] + sign * values[rows - 1 - row] for row in range(rows // 2)]
    results = []
    for row in range(rows // 2):
        total = None
        for source, value in enumerate(half):
            near = tap(grad_taps(kind), source - row)
            far = tap(grad_taps(kind), rows - 1 - source - row)
            weight = 0.5 * (near + sign * far)
            total = weight * value if total is None else total + weight * value
        results.append(total)
    return results


def weighted_products(three, weight):
    pairs = ((0, 0), (1, 1), (2, 2), (0, 1), (0, 2), (1, 2))
    first = [weight * value for value in three]
    return [first[a] * three[b] for a, b in pairs]


def late_mask(count, width):
    row = lax.broadcasted_iota(jnp.int32, (count, LANES), 0)
    left = max(width - 2 * R1 - EARLY, 0)
    place = jnp.where(row < left + EDGE, row - left + R1 - EDGE, row - left - EDGE + width - R1)
    place = place + lax.axis_index("plane") * width
    inside = (place >= 0) & (place < lax.axis_size("plane") * width)
    return jnp.where(inside | (row < left), 1.0, 0.0)


USED = (0, 1, 2, 5)
UNUSED = (3, 4)


def all_sums(products, coarse, sx):
    sums = [None] * 6
    for kinds in (USED, UNUSED):
        tiles = [tile for index in kinds for tile in products[index]]
        along = product(sx, jnp.concatenate(tiles, axis=1)).astype(jnp.bfloat16)
        step = along.shape[1] // len(kinds)
        parts = [along[:, index * step : (index + 1) * step] for index in range(len(kinds))]
        total = product(jnp.concatenate(parts, axis=0), coarse)
        high = sx.shape[0]
        for index, kind in enumerate(kinds):
            sums[kind] = total[index * high : (index + 1) * high]
    return sums


def tensor_sums(across, sx, mask, diagonal, z_parts, filtered, grads):
    double = diagonal.shape[1]
    depth, pairs = double // 2, across.shape[1] // double
    rows, count = 2 * pairs, across.shape[0] // 2
    for start in range(0, count, 16):
        kinds = [
            [
                across[kind * count + start : kind * count + start + 16, row * depth : (row + 1) * depth]
                for row in range(rows)
            ]
            for kind in range(2)
        ]
        for part in range(3):
            values = kinds[X_KINDS[part]]
            results = mirrored_filter(ROW_KINDS[part], values, True)
            results += mirrored_filter(ROW_KINDS[part], values, False)
            for row, result in enumerate(results):
                at = (part * pairs + row // 2) * count + start
                lanes = slice((row % 2) * depth, (row % 2 + 1) * depth)
                filtered[at : at + 16, lanes] = result.astype(jnp.bfloat16)

    at = 2 * pairs * count
    grads[:at] = product(filtered[:at, :], diagonal[0:double, :])
    grads[at:] = product(filtered[at:, :], diagonal[double : 2 * double, :])

    weights = product_weights(rows)
    layer = lax.axis_index("depth")
    first, last = layer == 0, layer == lax.axis_size("depth") - 1
    place = lax.broadcasted_iota(jnp.int32, (16, depth), 1)
    complete = ((place >= R1) | first) & ((place < depth - R1) | last)
    complete = jnp.where(complete, 1.0, 0.0)
    groups = [[] for _ in range(6)]
    for start in range(0, count, 16):
        inside = complete if mask is None else complete * mask[start : start + 16]
        totals = None
        for row in range(rows):
            lanes = slice((row % 2) * depth, (row % 2 + 1) * depth)
            three = []
            for part in range(3):
                at = (part * pairs + row // 2) * count + start
                three.append(grads[at : at + 16, lanes])
            terms = weighted_products(three, 2.0 * float(weights[row % (rows // 2)]))
            totals = terms if row == 0 else [a + b for a, b in zip(totals, terms)]
        for index in range(6):
            groups[index].append((totals[index] * inside).astype(jnp.bfloat16))
    products = [[jnp.concatenate(group, axis=0)] for group in groups]
    return all_sums(products, z_parts[double : double + depth, :], sx)


def rim_tiles(values):
    rows, depth = len(values), values[0].shape[1]
    below = packed_rows(values, RIM, depth - RIM)
    above = pltpu.roll(packed_rows(values, RIM, 0), rows * RIM, 1)
    lane = lax.broadcasted_iota(jnp.int32, below.shape, 1)
    return [jnp.where(lane < rows * RIM, below, above), above, pltpu.roll(above, HALF, 1)]


def early_kernel(
    starts, grey, x_parts, z_parts, sums, diagonal, sides, tiles, across, filtered, grads
):
    rows, width, depth = grey.shape
    double = 2 * depth
    empty = jnp.zeros((depth, depth), jnp.bfloat16)
    for kind in range(2):
        for half in range(2):
            at = pl.ds(kind * double + half * depth, depth)
            band = z_parts[kind * depth : (kind + 1) * depth, :]
            diagonal[at, half * depth : (half + 1) * depth] = band
            diagonal[at, (1 - half) * depth : (2 - half) * depth] = empty
    values = [grey[row].astype(jnp.float32) for row in range(rows)]
    whole = jnp.concatenate([value.astype(jnp.bfloat16) for value in values], axis=1)
    result = product(x_parts[starts[0] : starts[2], :width], whole)
    across[...] = result[: starts[1]]
    sides[...] = result[starts[1] :]
    sx = x_parts[starts[2] : starts[3], :EARLY]
    results = tensor_sums(across, sx, None, diagonal, z_parts, filtered, grads)
    for index, kind in enumerate(USED):
        sums[index] = results[kind]
    for index, tile in enumerate(rim_tiles(values)):
        tiles[index] = tile


def late_kernel(
    starts, width, far, near, x_late, z_parts, diagonal, early_sums, sides, own_tiles, temp, cure,
    out_hbm, across, filtered, grads, out, sems,
):
    double = diagonal.shape[1]
    depth = double // 2
    rows = across.shape[1] // depth
    count, lanes = temp.shape
    odd = is_odd()
    depths, layer = lax.axis_size("depth"), lax.axis_index("depth")
    outer, outer_columns = edges_of(far, rows)
    inner, inner_columns = edges_of(near, rows)
    values = []
    for row in range(rows):
        left = jnp.where(odd, inner[row], outer[row])
        right = jnp.where(odd, outer[row], inner[row])
        values.append(jnp.concatenate([left, right], axis=0))
    left = jnp.where(odd, inner_columns, outer_columns)
    right = jnp.where(odd, outer_columns, inner_columns)

    late = across.shape[0] // 2
    halos = jnp.concatenate([value.astype(jnp.bfloat16) for value in values], axis=1)
    across[...] = sides[...] + product(x_late[starts[0] : starts[1], : 2 * EDGE], halos)

    products_x, voxels = own_columns(count)
    folded, stride = fold(voxels), COARSE * count
    tiles = [
        jnp.concatenate([tile[:EDGE], own_tiles[index], tile[EDGE:]], axis=0)
        for index, tile in enumerate(rim_tiles(values))
    ]
    missing = stride * (depths - 1) + voxels - tiles[0].shape[0]
    if missing > 0:
        spare = jnp.zeros((-(-missing // 8) * 8, LANES), jnp.float32)
        tiles = [jnp.concatenate([tile, spare], axis=0) for tile in tiles]

    height = count + 2 * HALO
    half_lane = lax.broadcasted_iota(jnp.int32, (folded, LANES), 1) < HALF
    order = meeting_order(out.shape[0])
    for position, target in enumerate(order):
        at = stride * target
        second = jnp.where(
            half_lane,
            tiles[1][at : at + folded],
            tiles[2][at + voxels - folded : at + voxels],
        )
        rims = jnp.concatenate([tiles[0][at : at + voxels], second], axis=0)
        out[position, 0 : voxels + folded, :] = rims.astype(jnp.bfloat16)
    split = (pl.ds(0, voxels + folded), pl.ds(voxels + folded, out.shape[1] - voxels - folded))
    copies = [
        pltpu.make_async_copy(out.at[:, part, :], out_hbm.at[:, part, :], sems.at[index])
        for index, part in enumerate(split)
    ]
    copies[0].start()

    sx = x_late[starts[1] : starts[2], :late]
    results = tensor_sums(
        across, sx, late_mask(late, width), diagonal, z_parts, filtered, grads
    )
    yy, xx, zz, xz = [early_sums[index] + results[kind] for index, kind in enumerate(USED)]
    trace = yy + xx + zz
    lane = lax.broadcasted_iota(jnp.int32, trace.shape, 1)
    columns, cells = sizes(width, depth)
    tail = 4 * cells - LANES
    joint = pltpu.roll(xz, 3 * cells, 1)
    rest = jnp.where(lane < tail, joint, 0.0)
    rest = pltpu.roll(rest, 0, 1, stride=tail, stride_axis=0)
    for index, part in ((2, zz), (1, xx), (0, trace)):
        moved = part if index == 0 else pltpu.roll(part, index * cells, 1)
        joint = jnp.where(lane < (index + 1) * cells, moved, joint)

    own_first, own_last = column_rows(temp, cure, False), column_rows(temp, cure, True)
    half = chunk_rows(count, lanes)[1]
    for position, target in enumerate(order):
        piece = jnp.where(layer == target - 1, own_last, 0.0)
        piece = jnp.where(layer == target + 1, own_first, piece)
        if target == 0:
            piece = jnp.where(layer == depths - 1, left, piece)
        if target == out.shape[0] - 1:
            piece = jnp.where(layer == 0, right, piece)
        mine = slice(count * target, count * target + height)
        pieces = [coded(joint[mine]), coded(jnp.sum(rest[mine], axis=0, keepdims=True))]
        for slot in range(lanes // LANES):
            part = piece[:, slot * LANES : (slot + 1) * LANES]
            pieces += [part[:GHOST] - reference_temp, part[GHOST:COLUMN_ROWS]]
        filled = sum(part.shape[0] for part in pieces)
        if filled < half:
            pieces.append(jnp.zeros((half - filled, LANES), jnp.float32))
        out[position, voxels + folded :, :] = jnp.concatenate(pieces, axis=0).astype(jnp.bfloat16)
    copies[1].start()
    for copy in copies:
        copy.wait()


def rim_sums(chunks, count, starts, flat, steep, cells):
    parts = chunks.shape[0]
    rows_x, voxels = own_columns(count)
    folded = fold(voxels)
    tall = -(-voxels // 16) * 16
    spare = [jnp.zeros((tall - voxels, LANES), jnp.float32)] if tall > voxels else []
    lane = lax.broadcasted_iota(jnp.int32, (voxels, LANES), 1)
    order = meeting_order(parts)
    rims = [
        chunks[order.index(part), 0 : voxels + folded, :].astype(jnp.float32)
        for part in range(parts)
    ]
    tiles = []
    for below, above in zip(rims[:-1], rims[1:]):
        first = jnp.where(lane < ROWS * RIM, below[:voxels], above[:voxels])
        second = above[voxels:]
        second = [second[: voxels - folded], pltpu.roll(second, HALF, 1)]
        for tile in ([first], second):
            tiles.append(jnp.concatenate(tile + spare, axis=0).astype(jnp.bfloat16))
    result = product(
        steep[starts[1] : starts[2], :tall], jnp.concatenate(tiles, axis=1)
    ).astype(jnp.bfloat16)
    kinds = []
    for kind in range(2):
        values = result[kind * rows_x : (kind + 1) * rows_x]
        stack = [
            values[:, 2 * part * LANES : 2 * (part + 1) * LANES] for part in range(parts - 1)
        ]
        kinds.append(jnp.concatenate(stack, axis=0))
    both = product(kinds[0], flat[...])
    three = (both[:, :LANES], product(kinds[1], steep[starts[0] : starts[1], :]), both[:, LANES:])

    index = lax.axis_index("plane") * lax.axis_size("depth") + lax.axis_index("depth")
    total = lax.axis_size("plane") * lax.axis_size("depth") * count * COARSE
    place = lax.rem(lax.broadcasted_iota(jnp.int32, three[0].shape, 0), rows_x)
    place = place + (index * count - HALO) * COARSE - R2
    inside = jnp.where((place >= 0) & (place < total), 1.0, 0.0)
    products = [
        [
            term[part * rows_x : (part + 1) * rows_x].astype(jnp.bfloat16)
            for part in range(parts - 1)
        ]
        for term in weighted_products(three, inside)
    ]
    return all_sums(products, cells[...], steep[starts[2] : starts[3], :rows_x])


def cure_kernel(
    cells, starts, chunks, temp_in, cure_in, tools, flat, steep, rim_bands, temp_hbm, cure_hbm,
    conduct_hbm, temp_out, cure_out, conduct_out, sems,
):
    count, lanes = temp_in.shape
    parts = chunks.shape[0]
    planes, depths = lax.axis_size("plane"), lax.axis_size("depth")
    plane, layer = lax.axis_index("plane"), lax.axis_index("depth")
    height = count + 2 * HALO
    own = cells - BEFORE - AFTER
    lane = lax.broadcasted_iota(jnp.int32, (16, lanes), 1)
    row = lax.broadcasted_iota(jnp.int32, (16, lanes), 0)
    at_sums, half = chunk_rows(count, lanes)
    tail = 4 * cells - LANES
    narrow_lane = lax.broadcasted_iota(jnp.int32, (16, LANES), 1)
    order = meeting_order(parts)

    near = rim_sums(chunks, count, starts, flat, steep, rim_bands)
    sums = [near[0] + near[1] + near[2], near[1], near[2], near[5]]
    blocks = [chunks[order.index(part), at_sums:, :].astype(jnp.float32) for part in range(parts)]
    columns = [
        jnp.concatenate(
            [
                block[at : at + COLUMN_ROWS]
                for at in range(
                    height + 1, height + 1 + COLUMN_ROWS * (lanes // LANES), COLUMN_ROWS
                )
            ],
            axis=1,
        )
        for block in blocks
    ]
    blocks = [decoded(block[0:16]) for block in blocks]
    tails = [block[height : height + 1] for block in blocks]
    if parts % 8:
        tails.append(jnp.zeros((-parts % 8, LANES), jnp.float32))
    tails = jnp.concatenate(tails, axis=0)
    tails = pltpu.roll(tails, lax.rem(LANES - lax.rem(tail * count * layer, LANES), LANES), 1)
    narrow_row = lax.broadcasted_iota(jnp.int32, (16, LANES), 0)
    rests = [jnp.zeros((16, LANES), jnp.float32) for _ in range(parts)]
    for column in range(height):
        moved = pltpu.roll(tails, LANES - tail * column, 1) if column else tails
        for part in range(parts):
            rests[part] = jnp.where(narrow_row == column, moved[part : part + 1], rests[part])
    for part in range(parts):
        first_cell = own * part - BEFORE
        here = (lane >= first_cell) & (lane < first_cell + cells)
        values = blocks[part]
        joint = values[0:16]
        xz = pltpu.roll(jnp.where(narrow_lane < tail, rests[part], joint), LANES - 3 * cells, 1)
        for index in range(4):
            chunk = xz if index == 3 else joint
            if lanes > LANES:
                spare = jnp.zeros((16, lanes - LANES), jnp.float32)
                chunk = jnp.concatenate([chunk, spare], axis=1)
            shift = (first_cell - (index % 3) * cells) % lanes
            moved = chunk if shift == 0 else pltpu.roll(chunk, shift, 1)
            sums[index] = sums[index] + jnp.where(here, moved, 0.0)
    trace = sums[0]
    scale = (conduct_fiber - conduct_matrix) / (2.0 * trace + tensor_eps)
    conduct = [
        conduct_matrix + scale * (trace - sums[1]),
        -scale * sums[3],
        conduct_matrix + scale * (trace - sums[2]),
    ]
    for kind in range(3):
        conduct_out[kind] = conduct[kind][HALO : HALO + count]
    copies = [
        pltpu.make_async_copy(conduct_out, conduct_hbm, sems.at[0]),
        pltpu.make_async_copy(temp_out, temp_hbm, sems.at[1]),
        pltpu.make_async_copy(cure_out, cure_hbm, sems.at[2]),
    ]
    copies[0].start()

    before, after = columns[parts - 1], columns[0]
    for part in range(parts - 1):
        before = jnp.where(layer == part + 1, columns[part], before)
        after = jnp.where(layer == part, columns[part + 1], after)
    spare = jnp.full((16 - count - 2 * GHOST, lanes), 0.5, jnp.float32)
    temp = jnp.concatenate([
            before[:GHOST] + reference_temp,
            temp_in[...],
            after[:GHOST] + reference_temp,
            8.0 * spare,
        ], axis=0)
    cure = jnp.concatenate([spare[:1], before[GHOST:], cure_in[...], after[GHOST:], spare[:1], spare], axis=0)
    gap = GHOST - HALO
    xx, xz, zz = [pltpu.roll(part, gap, 0) for part in conduct]

    first = (plane == 0) & (layer == 0)
    last = (plane == planes - 1) & (layer == depths - 1)
    for step in range(STEPS):
        top, bottom = tools[2 * step : 2 * step + 1, :], tools[2 * step + 1 : 2 * step + 2, :]
        temp = jnp.where((row < GHOST) & first, temp[GHOST : GHOST + 1], temp)
        temp = jnp.where(
            (row >= GHOST + count) & last, temp[GHOST + count - 1 : GHOST + count], temp
        )
        cooler = jnp.where(lane == 0, top, pltpu.roll(temp, 1, 1))
        later = jnp.where(lane == lanes - 1, bottom, pltpu.roll(temp, lanes - 1, 1))
        slant = later - cooler
        second_x = pltpu.roll(temp, 15, 0) - 2.0 * temp + pltpu.roll(temp, 1, 0)
        second_z = later - 2.0 * temp + cooler
        cross = 0.25 * (pltpu.roll(slant, 15, 0) - pltpu.roll(slant, 1, 0))
        spread = xx * second_x + 2.0 * xz * cross + zz * second_z
        inverse = 1.0 / reference_temp - 1.0 / temp
        left = 1.0 - cure
        rate = rate_first * jnp.exp(energy_first * inverse) + rate_second * jnp.exp(
            energy_second * inverse
        ) * jnp.sqrt(cure)
        rate = rate * (left * jnp.sqrt(left))
        temp = temp + time_step * (spread + heat_release * rate)
        cure = cure + time_step * rate
    temp_out[...] = temp[GHOST : GHOST + count]
    cure_out[...] = cure[GHOST : GHOST + count]
    for copy in copies[1:]:
        copy.start()
    for copy in copies:
        copy.wait()


def on_device(intensity, temp_start, cure_start, tool_levels, plan):
    rows, width, depth = intensity.shape
    count, lanes = temp_start.shape
    planes, depths = lax.axis_size("plane"), lax.axis_size("depth")
    columns, cells = sizes(width, depth)
    bf16 = jnp.bfloat16
    slots = rows * EDGE + 16 * (lanes // LANES)
    params = pltpu.CompilerParams(vmem_limit_bytes=24 * 1024 * 1024)
    vmem = pl.BlockSpec(memory_space=pltpu.VMEM)
    stay = pl.BlockSpec(memory_space=pltpu.HBM)

    fixed = lambda values: pltpu.with_memory_space_constraint(values, pltpu.HBM)
    bands, coarse = x_bands(width), coarse_x_bands(width)
    late = bands.shape[1] - EARLY
    middle = bands[:, :EARLY, EDGE : EDGE + width]
    sides = bands[:, EARLY:].reshape(2 * late, -1)
    x_hbm, early_starts = stacked(
        middle.reshape(2 * EARLY, -1), sides[:, EDGE : EDGE + width], coarse[:, :EARLY]
    )
    z_hbm, _ = stacked(*depth_bands(depth), coarse_depth_bands(depth))
    halos = np.concatenate([sides[:, :EDGE], sides[:, EDGE + width :]], axis=1)
    x_late, late_starts = stacked(halos, coarse[:, EARLY:])
    rims = rim_bands(rows)
    flat, _ = stacked(np.concatenate([rims[0], rims[2]], axis=1))
    steep, rim_starts = stacked(rims[1], *rim_x_bands(count))
    cell_bands, _ = stacked(rim_cells(rows, depth, depths))
    far, near, grey, x_parts, z_parts, temp, cure = pl.pallas_call(
        pack_kernel,
        name="pack",
        out_shape=(
            pltpu.VMEM((slots, depth), bf16),
            pltpu.VMEM((slots, depth), bf16),
            pltpu.VMEM((rows, width, depth), jnp.int32),
            pltpu.VMEM(x_hbm.shape, bf16),
            pltpu.VMEM(z_hbm.shape, bf16),
            pltpu.VMEM((count, lanes), jnp.float32),
            pltpu.VMEM((count, lanes), jnp.float32),
        ),
        in_specs=[stay] * 5,
        scratch_shapes=[
            pltpu.SemaphoreType.DMA((5,)),
        ],
        compiler_params=params,
    )(*[fixed(values) for values in (intensity, temp_start, cure_start, x_hbm, z_hbm)])

    def moved(values, pairs):
        index = [(p * depths + d, q * depths + e) for (p, d), (q, e) in pairs]
        return lax.ppermute(values, ("plane", "depth"), index)

    def swapped(values, first):
        pairs = [(p, p + 1) for p in range(first, planes - 1, 2)]
        pairs += [(q, p) for p, q in pairs]
        return moved(values, [((p, d), (q, d)) for p, q in pairs for d in range(depths)])

    far = swapped(far, 1)
    near = swapped(near, 0)

    high = coarse.shape[0]

    def scratch(count):
        return [
            pltpu.VMEM((2 * count, rows * depth), jnp.float32),
            pltpu.VMEM((3 * rows // 2 * count, 2 * depth), bf16),
            pltpu.VMEM((3 * rows // 2 * count, 2 * depth), jnp.float32),
        ]

    def cost(count):
        return pl.CostEstimate(
            flops=2 * rows * (2 * count) * 160 * depth * 4,
            bytes_accessed=4_000_000,
            transcendentals=0,
        )

    early_sums, diagonal, sides, own_tiles = pl.pallas_call(
        functools.partial(early_kernel, early_starts),
        name="early",
        out_shape=(
            pltpu.VMEM((len(USED), high, LANES), jnp.float32),
            pltpu.VMEM((4 * depth, 2 * depth), bf16),
            pltpu.VMEM((2 * late, rows * depth), jnp.float32),
            pltpu.VMEM((3, width, LANES), jnp.float32),
        ),
        scratch_shapes=scratch(EARLY),
        cost_estimate=cost(EARLY),
        compiler_params=params,
    )(grey, x_parts, z_parts)

    products_x, voxels = own_columns(count)
    at_sums, half = chunk_rows(count, lanes)
    chunk_shape = (depths, at_sums + half, LANES)
    chunks = pl.pallas_call(
        functools.partial(late_kernel, late_starts, width),
        name="late",
        out_shape=pltpu.HBM(chunk_shape, bf16),
        in_specs=[vmem] * 10,
        out_specs=stay,
        scratch_shapes=scratch(late)
        + [pltpu.VMEM(chunk_shape, bf16), pltpu.SemaphoreType.DMA((2,))],
        cost_estimate=cost(late),
        compiler_params=params,
    )(far, near, x_late, z_parts, diagonal, early_sums, sides, own_tiles, temp, cure)

    faces = plan.reshape(2 * STEPS, 1) == jnp.arange(tool_levels.shape[0], dtype=jnp.int32)
    tools = jnp.sum(
        jnp.where(faces, tool_levels, jnp.zeros_like(tool_levels)), axis=1, keepdims=True
    )

    chunks = lax.all_to_all(
        chunks,
        "depth",
        split_axis=0,
        concat_axis=0,
        tiled=True,
        axis_index_groups=[meeting_order(depths)],
    )

    return pl.pallas_call(
        functools.partial(cure_kernel, cells, rim_starts),
        name="cure",
        out_shape=(
            pltpu.HBM((count, lanes), jnp.float32),
            pltpu.HBM((count, lanes), jnp.float32),
            pltpu.HBM((3, count, lanes), jnp.float32),
        ),
        in_specs=[vmem] * 7,
        out_specs=(stay, stay, stay),
        scratch_shapes=[
            pltpu.VMEM((count, lanes), jnp.float32),
            pltpu.VMEM((count, lanes), jnp.float32),
            pltpu.VMEM((3, count, lanes), jnp.float32),
            pltpu.SemaphoreType.DMA((3,)),
        ],
        compiler_params=params,
    )(chunks, temp, cure, tools, flat, steep, cell_bands)


def solution(mesh):
    return jax.shard_map(
        on_device,
        mesh=mesh,
        in_specs=(
            P(None, "plane", "depth"),
            P(("plane", "depth"), None),
            P(("plane", "depth"), None),
            P(),
            P(),
        ),
        out_specs=(
            P(("plane", "depth"), None),
            P(("plane", "depth"), None),
            P(None, ("plane", "depth"), None),
        ),
        check_vma=False,
    )
```

```python
import functools

import jax
import jax.numpy as jnp
import ml_dtypes
import numpy as np
from jax import lax
from jax.experimental import pallas as pl
from jax.experimental.pallas import tpu as pltpu
from jax.sharding import PartitionSpec as P

ROWS = 8
R1 = 6
R2 = 10
COARSE = 4
STEPS = 3

sigma_grad = 2.0
sigma_tensor = 3.3
conduct_matrix = 0.3
conduct_fiber = 1.5
time_step = 0.25
heat_release = 0.4
rate_first = 0.15
rate_second = 0.6
energy_first = 30.0
energy_second = 25.0
reference_temp = 4.2
tensor_eps = 1e-06

LANES = 128
HALO = 2
EDGE = HALO * COARSE + R1 + R2
EARLY = 96
GHOST = 3
COLUMN_ROWS = 2 * GHOST - 1
CODE_SCALE = 2.0**20
RIM = 2 * R1
BEFORE = -(-(R2 - R1) // COARSE)
AFTER = BEFORE
HALF = LANES // 2
ROW_KINDS = (1, 0, 0)
X_KINDS = (0, 1, 0)
DEPTH_KINDS = (0, 0, 1)


def smooth_taps(radius, sigma):
    offsets = np.arange(-radius, radius + 1) * 1.0
    weights = np.exp(-0.5 * offsets * offsets / (sigma * sigma))
    return weights / weights.sum()


def slope_taps(radius, sigma):
    offsets = np.arange(-radius, radius + 1) * 1.0
    weights = np.exp(-0.5 * offsets * offsets / (sigma * sigma))
    return offsets * weights / np.sum(offsets * offsets * weights)


def row_weights(count, radius, sigma):
    taps = smooth_taps(radius, sigma)
    result = np.zeros(count)
    for source in range(count):
        for target in range(count):
            offset = target - source
            if abs(offset) <= radius:
                result[source] += taps[offset + radius]
    return result


def rounded(taps):
    best = None
    for factor in np.linspace(1.0, 2.0, 20001)[:-1]:
        near = (taps * factor).astype(np.float32).astype(ml_dtypes.bfloat16).astype(np.float64)
        error = np.abs(near / factor - taps).sum()
        if best is None or error < best[0]:
            best = (error, near, factor)
    return best[1], best[2]


def as_bfloat16(matrix):
    return matrix.astype(np.float32).astype(ml_dtypes.bfloat16)


def halves(matrix):
    high = as_bfloat16(matrix)
    return high, as_bfloat16(matrix - high.astype(np.float64))


def sizes(width, depth):
    columns = width // COARSE + 2 * HALO
    cells = depth // COARSE + BEFORE + AFTER
    return columns, cells


def product_rows(width):
    places = [*range(R1, width - R1)]
    places += [None] * max(EARLY - len(places), 0)
    places += [*range(R1 - EDGE, R1), *range(width - R1, width + EDGE - R1)]
    return places + [None] * (-len(places) % 16)


GRAD_TAPS = tuple(
    rounded(taps(R1, sigma_grad)) for taps in (smooth_taps, slope_taps)
)
GRAD_FACTOR = GRAD_TAPS[0][1] ** 2 * GRAD_TAPS[1][1]


def grad_taps(kind):
    return GRAD_TAPS[kind][0]


def tap(taps, offset):
    radius = (len(taps) - 1) // 2
    return float(taps[offset + radius]) if abs(offset) <= radius else 0.0


def x_bands(width):
    places = product_rows(width)
    bands = np.zeros((2, len(places), width + 2 * EDGE))
    for kind in range(2):
        for row, place in enumerate(places):
            if place is not None:
                first = place + EDGE - R1
                bands[kind, row, first : first + 2 * R1 + 1] = grad_taps(kind)
    return bands


def rim_bands(rows):
    bands = np.zeros((3, 2 * LANES, LANES))
    for part in range(3):
        row_taps, depth_taps = grad_taps(ROW_KINDS[part]), grad_taps(DEPTH_KINDS[part])
        for source in range(rows):
            for target in range(rows):
                row_tap = tap(row_taps, source - target)
                for near in range(-RIM, RIM):
                    lane = source * RIM + near % RIM
                    if near >= 0:
                        lane += rows * RIM
                    for place in range(-R1, R1):
                        value = row_tap * tap(depth_taps, near - place)
                        bands[part, lane, target * 2 * R1 + R1 + place] = value
    return bands


def rim_cells(rows, depth, blocks):
    taps = smooth_taps(R2, sigma_tensor)
    weights = product_weights(rows)
    bands = np.zeros((blocks - 1, LANES, blocks * depth // COARSE))
    for boundary in range(blocks - 1):
        middle = (boundary + 1) * depth
        for cell in range(bands.shape[2]):
            for voxel in range(cell * COARSE, (cell + 1) * COARSE):
                for place in range(-R1, R1):
                    value = tap(taps, middle + place - voxel)
                    for row in range(rows):
                        bands[boundary, row * 2 * R1 + R1 + place, cell] += weights[row] * value
    return bands.reshape(-1, bands.shape[2])


def meeting_order(blocks):
    middle = blocks // 2
    return [*range(middle, blocks), *range(middle)]


def own_columns(count):
    products = (count + 2 * HALO) * COARSE + 2 * R2
    voxels = products + 2 * R1
    return -(-products // 16) * 16, -(-voxels // 8) * 8


def fold(voxels):
    return -(-voxels // 16) * 8


def rim_x_bands(count):
    products, voxels = own_columns(count)
    bands = np.zeros((2, products, -(-voxels // 16) * 16))
    valid = (count + 2 * HALO) * COARSE + 2 * R2
    for kind in range(2):
        for row in range(valid):
            bands[kind, row, row : row + 2 * R1 + 1] = grad_taps(kind)
    taps = smooth_taps(R2, sigma_tensor)
    coarse = np.zeros((16, products))
    for column in range(count + 2 * HALO):
        for voxel in range(column * COARSE, (column + 1) * COARSE):
            coarse[column, voxel : voxel + 2 * R2 + 1] += taps
    return bands.reshape(2 * products, -1), coarse


def depth_bands(depth):
    bands = np.zeros((2, depth, depth))
    for kind in range(2):
        for place in range(depth):
            for near in range(max(place - R1, 0), min(place + R1 + 1, depth)):
                bands[kind, near, place] = tap(grad_taps(kind), near - place)
    return bands


def product_weights(rows):
    return row_weights(rows, R2, sigma_tensor) / (255.0 * GRAD_FACTOR) ** 2


def coarse_depth_bands(depth):
    taps = smooth_taps(R2, sigma_tensor)
    columns, cells = sizes(0, depth)
    bands = np.zeros((depth, LANES))
    for cell in range(cells):
        for voxel in range(COARSE):
            place = (cell - BEFORE) * COARSE + voxel
            for near in range(max(place - R2, 0), min(place + R2 + 1, depth)):
                bands[near, cell] += tap(taps, near - place)
    return bands


def coarse_x_bands(width):
    taps = smooth_taps(R2, sigma_tensor)
    places = product_rows(width)
    columns, cells = sizes(width, 0)
    bands = np.zeros((-(-columns // 16) * 16, len(places)))
    for column in range(columns):
        for voxel in range(COARSE):
            middle = (column - HALO) * COARSE + voxel
            for row, place in enumerate(places):
                if place is not None:
                    bands[column, row] += tap(taps, place - middle)
    return bands


def stacked(*pieces):
    widest = max(piece.shape[1] for piece in pieces)
    padded = [np.pad(piece, ((0, 0), (0, widest - piece.shape[1]))) for piece in pieces]
    starts = np.cumsum([0] + [len(piece) for piece in pieces])
    return jnp.asarray(as_bfloat16(np.concatenate(padded))), tuple(int(start) for start in starts)


def two_parts(values):
    high = values.astype(jnp.bfloat16).astype(jnp.float32)
    return jnp.concatenate([high, (values - high).astype(jnp.bfloat16).astype(jnp.float32)], axis=0)


def joined(parts):
    half = parts.shape[0] // 2
    return parts[:half] + parts[half:]


def coded(values):
    values = values * CODE_SCALE
    return (values * jnp.abs(values)) * (values * values)


def decoded(values):
    size = jnp.sqrt(jnp.sqrt(jnp.abs(values))) * (1.0 / CODE_SCALE)
    return jnp.where(values < 0.0, -size, size)


def column_rows(temp, cure, at_end):
    count = temp.shape[0]
    first, second = (count - GHOST, count - GHOST + 1) if at_end else (0, 0)
    pad = jnp.zeros((8 - COLUMN_ROWS, temp.shape[1]), jnp.float32)
    return jnp.concatenate(
        [temp[first : first + GHOST, :], cure[second : second + GHOST - 1, :], pad], axis=0
    )


def chunk_rows(count, lanes):
    products, voxels = own_columns(count)
    held = count + 2 * HALO + 1 + COLUMN_ROWS * (lanes // LANES)
    return voxels + fold(voxels), -(-held // 16) * 16


def is_odd():
    return lax.rem(lax.axis_index("plane"), 2) == 1


def pack_kernel(
    intensity, temp_hbm, cure_hbm, x_hbm, z_hbm, far, near, grey, x_parts, z_parts, temp, cure,
    sems,
):
    rows, width, depth = intensity.shape
    copies = [
        pltpu.make_async_copy(intensity, grey, sems.at[0]),
        pltpu.make_async_copy(temp_hbm, temp, sems.at[1]),
        pltpu.make_async_copy(cure_hbm, cure, sems.at[2]),
        pltpu.make_async_copy(x_hbm, x_parts, sems.at[3]),
        pltpu.make_async_copy(z_hbm, z_parts, sems.at[4]),
    ]
    for copy in copies:
        copy.start()
    for copy in copies[:3]:
        copy.wait()
    odd = is_odd()
    sides = [
        two_parts(column_rows(temp, cure, at_end)).astype(jnp.bfloat16)
        for at_end in (False, True)
    ]

    def send(left, right):
        for place, target, columns in ((0, left, sides[0]), (width - EDGE, right, sides[1])):
            for pair in range(rows // 2):
                two = [grey[2 * pair + i, place : place + EDGE, :] for i in range(2)]
                two = jnp.concatenate(two, axis=0).astype(jnp.float32)
                target[2 * EDGE * pair : 2 * EDGE * (pair + 1), :] = two.astype(jnp.bfloat16)
            for slot in range(temp.shape[1] // LANES):
                at = rows * EDGE + 16 * slot
                target[at : at + 16, :] = columns[:, slot * LANES : (slot + 1) * LANES]

    @pl.when(odd)
    def _():
        send(near, far)

    @pl.when(jnp.logical_not(odd))
    def _():
        send(far, near)

    for copy in copies[3:]:
        copy.wait()


def packed_rows(values, size, first):
    depth = values[0].shape[1]
    lane = lax.broadcasted_iota(jnp.int32, values[0].shape, 1)
    packed = None
    for block, value in enumerate(values):
        shift = (size * block - first) % depth
        moved = value if shift == 0 else pltpu.roll(value, shift, 1)
        packed = moved if block == 0 else jnp.where(lane >= size * block, moved, packed)
    return packed


def edges_of(ref, rows):
    two = [
        ref[2 * EDGE * pair : 2 * EDGE * (pair + 1), :].astype(jnp.float32)
        for pair in range(rows // 2)
    ]
    voxels = [two[row // 2][row % 2 * EDGE : (row % 2 + 1) * EDGE] for row in range(rows)]
    slots = range(rows * EDGE, ref.shape[0], 16)
    columns = [joined(ref[at : at + 16, :].astype(jnp.float32)) for at in slots]
    return voxels, jnp.concatenate(columns, axis=1)


def product(first, second):
    return jnp.dot(first, second, preferred_element_type=jnp.float32)


def mirrored_filter(kind, values, even):
    rows = len(values)
    use_sum = even == (kind == 0)
    sign = 1.0 if use_sum else -1.0
    half = [values[row] + sign * values[rows - 1 - row] for row in range(rows // 2)]
    results = []
    for row in range(rows // 2):
        total = None
        for source, value in enumerate(half):
            near = tap(grad_taps(kind), source - row)
            far = tap(grad_taps(kind), rows - 1 - source - row)
            weight = 0.5 * (near + sign * far)
            total = weight * value if total is None else total + weight * value
        results.append(total)
    return results


def weighted_products(three, weight):
    pairs = ((0, 0), (1, 1), (2, 2), (0, 1), (0, 2), (1, 2))
    first = [weight * value for value in three]
    return [first[a] * three[b] for a, b in pairs]


def late_mask(count, width):
    row = lax.broadcasted_iota(jnp.int32, (count, LANES), 0)
    left = max(width - 2 * R1 - EARLY, 0)
    place = jnp.where(row < left + EDGE, row - left + R1 - EDGE, row - left - EDGE + width - R1)
    place = place + lax.axis_index("plane") * width
    inside = (place >= 0) & (place < lax.axis_size("plane") * width)
    return jnp.where(inside | (row < left), 1.0, 0.0)


USED = (0, 1, 2, 5)
UNUSED = (3, 4)


def all_sums(products, coarse, sx):
    sums = [None] * 6
    for kinds in (USED, UNUSED):
        tiles = [tile for index in kinds for tile in products[index]]
        along = product(sx, jnp.concatenate(tiles, axis=1)).astype(jnp.bfloat16)
        step = along.shape[1] // len(kinds)
        parts = [along[:, index * step : (index + 1) * step] for index in range(len(kinds))]
        total = product(jnp.concatenate(parts, axis=0), coarse)
        high = sx.shape[0]
        for index, kind in enumerate(kinds):
            sums[kind] = total[index * high : (index + 1) * high]
    return sums


def tensor_sums(across, sx, mask, diagonal, z_parts, filtered, grads):
    double = diagonal.shape[1]
    depth, pairs = double // 2, across.shape[1] // double
    rows, count = 2 * pairs, across.shape[0] // 2
    for start in range(0, count, 16):
        kinds = [
            [
                across[kind * count + start : kind * count + start + 16, row * depth : (row + 1) * depth]
                for row in range(rows)
            ]
            for kind in range(2)
        ]
        for part in range(3):
            values = kinds[X_KINDS[part]]
            results = mirrored_filter(ROW_KINDS[part], values, True)
            results += mirrored_filter(ROW_KINDS[part], values, False)
            for row, result in enumerate(results):
                at = (part * pairs + row // 2) * count + start
                lanes = slice((row % 2) * depth, (row % 2 + 1) * depth)
                filtered[at : at + 16, lanes] = result.astype(jnp.bfloat16)

    at = 2 * pairs * count
    grads[:at] = product(filtered[:at, :], diagonal[0:double, :])
    grads[at:] = product(filtered[at:, :], diagonal[double : 2 * double, :])

    weights = product_weights(rows)
    layer = lax.axis_index("depth")
    first, last = layer == 0, layer == lax.axis_size("depth") - 1
    place = lax.broadcasted_iota(jnp.int32, (16, depth), 1)
    complete = ((place >= R1) | first) & ((place < depth - R1) | last)
    complete = jnp.where(complete, 1.0, 0.0)
    groups = [[] for _ in range(6)]
    for start in range(0, count, 16):
        inside = complete if mask is None else complete * mask[start : start + 16]
        totals = None
        for row in range(rows):
            lanes = slice((row % 2) * depth, (row % 2 + 1) * depth)
            three = []
            for part in range(3):
                at = (part * pairs + row // 2) * count + start
                three.append(grads[at : at + 16, lanes])
            terms = weighted_products(three, 2.0 * float(weights[row % (rows // 2)]))
            totals = terms if row == 0 else [a + b for a, b in zip(totals, terms)]
        for index in range(6):
            groups[index].append((totals[index] * inside).astype(jnp.bfloat16))
    products = [[jnp.concatenate(group, axis=0)] for group in groups]
    return all_sums(products, z_parts[double : double + depth, :], sx)


def rim_tiles(values):
    rows, depth = len(values), values[0].shape[1]
    below = packed_rows(values, RIM, depth - RIM)
    above = pltpu.roll(packed_rows(values, RIM, 0), rows * RIM, 1)
    lane = lax.broadcasted_iota(jnp.int32, below.shape, 1)
    return [jnp.where(lane < rows * RIM, below, above), above, pltpu.roll(above, HALF, 1)]


def early_kernel(
    starts, grey, x_parts, z_parts, sums, diagonal, sides, tiles, across, filtered, grads
):
    rows, width, depth = grey.shape
    double = 2 * depth
    empty = jnp.zeros((depth, depth), jnp.bfloat16)
    for kind in range(2):
        for half in range(2):
            at = pl.ds(kind * double + half * depth, depth)
            band = z_parts[kind * depth : (kind + 1) * depth, :]
            diagonal[at, half * depth : (half + 1) * depth] = band
            diagonal[at, (1 - half) * depth : (2 - half) * depth] = empty
    values = [grey[row].astype(jnp.float32) for row in range(rows)]
    whole = jnp.concatenate([value.astype(jnp.bfloat16) for value in values], axis=1)
    result = product(x_parts[starts[0] : starts[2], :width], whole)
    across[...] = result[: starts[1]]
    sides[...] = result[starts[1] :]
    sx = x_parts[starts[2] : starts[3], :EARLY]
    results = tensor_sums(across, sx, None, diagonal, z_parts, filtered, grads)
    for index, kind in enumerate(USED):
        sums[index] = results[kind]
    for index, tile in enumerate(rim_tiles(values)):
        tiles[index] = tile


def late_kernel(
    starts, width, far, near, x_late, z_parts, diagonal, early_sums, sides, own_tiles, temp, cure,
    out_hbm, across, filtered, grads, out, sems,
):
    double = diagonal.shape[1]
    depth = double // 2
    rows = across.shape[1] // depth
    count, lanes = temp.shape
    odd = is_odd()
    depths, layer = lax.axis_size("depth"), lax.axis_index("depth")
    outer, outer_columns = edges_of(far, rows)
    inner, inner_columns = edges_of(near, rows)
    values = []
    for row in range(rows):
        left = jnp.where(odd, inner[row], outer[row])
        right = jnp.where(odd, outer[row], inner[row])
        values.append(jnp.concatenate([left, right], axis=0))
    left = jnp.where(odd, inner_columns, outer_columns)
    right = jnp.where(odd, outer_columns, inner_columns)

    late = across.shape[0] // 2
    halos = jnp.concatenate([value.astype(jnp.bfloat16) for value in values], axis=1)
    across[...] = sides[...] + product(x_late[starts[0] : starts[1], : 2 * EDGE], halos)

    products_x, voxels = own_columns(count)
    folded, stride = fold(voxels), COARSE * count
    tiles = [
        jnp.concatenate([tile[:EDGE], own_tiles[index], tile[EDGE:]], axis=0)
        for index, tile in enumerate(rim_tiles(values))
    ]
    missing = stride * (depths - 1) + voxels - tiles[0].shape[0]
    if missing > 0:
        spare = jnp.zeros((-(-missing // 8) * 8, LANES), jnp.float32)
        tiles = [jnp.concatenate([tile, spare], axis=0) for tile in tiles]

    height = count + 2 * HALO
    half_lane = lax.broadcasted_iota(jnp.int32, (folded, LANES), 1) < HALF
    order = meeting_order(out.shape[0])
    for position, target in enumerate(order):
        at = stride * target
        second = jnp.where(
            half_lane,
            tiles[1][at : at + folded],
            tiles[2][at + voxels - folded : at + voxels],
        )
        rims = jnp.concatenate([tiles[0][at : at + voxels], second], axis=0)
        out[position, 0 : voxels + folded, :] = rims.astype(jnp.bfloat16)
    split = (pl.ds(0, voxels + folded), pl.ds(voxels + folded, out.shape[1] - voxels - folded))
    copies = [
        pltpu.make_async_copy(out.at[:, part, :], out_hbm.at[:, part, :], sems.at[index])
        for index, part in enumerate(split)
    ]
    copies[0].start()

    sx = x_late[starts[1] : starts[2], :late]
    results = tensor_sums(
        across, sx, late_mask(late, width), diagonal, z_parts, filtered, grads
    )
    yy, xx, zz, xz = [early_sums[index] + results[kind] for index, kind in enumerate(USED)]
    lane = lax.broadcasted_iota(jnp.int32, yy.shape, 1)
    columns, cells = sizes(width, depth)
    tail = 4 * cells - LANES
    joint = pltpu.roll(xz, 3 * cells, 1)
    rest = jnp.where(lane < tail, joint, 0.0)
    rest = pltpu.roll(rest, 0, 1, stride=tail, stride_axis=0)
    for index, part in ((2, zz), (1, xx), (0, yy)):
        moved = part if index == 0 else pltpu.roll(part, index * cells, 1)
        joint = jnp.where(lane < (index + 1) * cells, moved, joint)

    own_first, own_last = column_rows(temp, cure, False), column_rows(temp, cure, True)
    half = chunk_rows(count, lanes)[1]
    for position, target in enumerate(order):
        piece = jnp.where(layer == target - 1, own_last, 0.0)
        piece = jnp.where(layer == target + 1, own_first, piece)
        if target == 0:
            piece = jnp.where(layer == depths - 1, left, piece)
        if target == out.shape[0] - 1:
            piece = jnp.where(layer == 0, right, piece)
        mine = slice(count * target, count * target + height)
        pieces = [coded(joint[mine]), coded(jnp.sum(rest[mine], axis=0, keepdims=True))]
        for slot in range(lanes // LANES):
            part = piece[:, slot * LANES : (slot + 1) * LANES]
            pieces += [part[:GHOST] - reference_temp, part[GHOST:COLUMN_ROWS]]
        filled = sum(part.shape[0] for part in pieces)
        if filled < half:
            pieces.append(jnp.zeros((half - filled, LANES), jnp.float32))
        out[position, voxels + folded :, :] = jnp.concatenate(pieces, axis=0).astype(jnp.bfloat16)
    copies[1].start()
    for copy in copies:
        copy.wait()


def rim_sums(chunks, count, starts, flat, steep, cells):
    parts = chunks.shape[0]
    rows_x, voxels = own_columns(count)
    folded = fold(voxels)
    tall = -(-voxels // 16) * 16
    spare = [jnp.zeros((tall - voxels, LANES), jnp.float32)] if tall > voxels else []
    lane = lax.broadcasted_iota(jnp.int32, (voxels, LANES), 1)
    order = meeting_order(parts)
    rims = [
        chunks[order.index(part), 0 : voxels + folded, :].astype(jnp.float32)
        for part in range(parts)
    ]
    tiles = []
    for below, above in zip(rims[:-1], rims[1:]):
        first = jnp.where(lane < ROWS * RIM, below[:voxels], above[:voxels])
        second = above[voxels:]
        second = [second[: voxels - folded], pltpu.roll(second, HALF, 1)]
        for tile in ([first], second):
            tiles.append(jnp.concatenate(tile + spare, axis=0).astype(jnp.bfloat16))
    result = product(
        steep[starts[1] : starts[2], :tall], jnp.concatenate(tiles, axis=1)
    ).astype(jnp.bfloat16)
    kinds = []
    for kind in range(2):
        values = result[kind * rows_x : (kind + 1) * rows_x]
        stack = [
            values[:, 2 * part * LANES : 2 * (part + 1) * LANES] for part in range(parts - 1)
        ]
        kinds.append(jnp.concatenate(stack, axis=0))
    both = product(kinds[0], flat[...])
    three = (both[:, :LANES], product(kinds[1], steep[starts[0] : starts[1], :]), both[:, LANES:])

    index = lax.axis_index("plane") * lax.axis_size("depth") + lax.axis_index("depth")
    total = lax.axis_size("plane") * lax.axis_size("depth") * count * COARSE
    place = lax.rem(lax.broadcasted_iota(jnp.int32, three[0].shape, 0), rows_x)
    place = place + (index * count - HALO) * COARSE - R2
    inside = jnp.where((place >= 0) & (place < total), 1.0, 0.0)
    products = [
        [
            term[part * rows_x : (part + 1) * rows_x].astype(jnp.bfloat16)
            for part in range(parts - 1)
        ]
        for term in weighted_products(three, inside)
    ]
    return all_sums(products, cells[...], steep[starts[2] : starts[3], :rows_x])


def cure_kernel(
    cells, starts, chunks, temp_in, cure_in, tools, flat, steep, rim_bands, temp_hbm, cure_hbm,
    conduct_hbm, temp_out, cure_out, conduct_out, sems,
):
    count, lanes = temp_in.shape
    parts = chunks.shape[0]
    planes, depths = lax.axis_size("plane"), lax.axis_size("depth")
    plane, layer = lax.axis_index("plane"), lax.axis_index("depth")
    height = count + 2 * HALO
    own = cells - BEFORE - AFTER
    lane = lax.broadcasted_iota(jnp.int32, (16, lanes), 1)
    row = lax.broadcasted_iota(jnp.int32, (16, lanes), 0)
    at_sums, half = chunk_rows(count, lanes)
    tail = 4 * cells - LANES
    narrow_lane = lax.broadcasted_iota(jnp.int32, (16, LANES), 1)
    order = meeting_order(parts)

    near = rim_sums(chunks, count, starts, flat, steep, rim_bands)
    sums = [near[kind] for kind in USED]
    blocks = [chunks[order.index(part), at_sums:, :].astype(jnp.float32) for part in range(parts)]
    columns = [
        jnp.concatenate(
            [
                block[at : at + COLUMN_ROWS]
                for at in range(
                    height + 1, height + 1 + COLUMN_ROWS * (lanes // LANES), COLUMN_ROWS
                )
            ],
            axis=1,
        )
        for block in blocks
    ]
    blocks = [decoded(block[0:16]) for block in blocks]
    tails = [block[height : height + 1] for block in blocks]
    if parts % 8:
        tails.append(jnp.zeros((-parts % 8, LANES), jnp.float32))
    tails = jnp.concatenate(tails, axis=0)
    tails = pltpu.roll(tails, lax.rem(LANES - lax.rem(tail * count * layer, LANES), LANES), 1)
    narrow_row = lax.broadcasted_iota(jnp.int32, (16, LANES), 0)
    rests = [jnp.zeros((16, LANES), jnp.float32) for _ in range(parts)]
    for column in range(height):
        moved = pltpu.roll(tails, LANES - tail * column, 1) if column else tails
        for part in range(parts):
            rests[part] = jnp.where(narrow_row == column, moved[part : part + 1], rests[part])
    for part in range(parts):
        first_cell = own * part - BEFORE
        here = (lane >= first_cell) & (lane < first_cell + cells)
        values = blocks[part]
        joint = values[0:16]
        xz = pltpu.roll(jnp.where(narrow_lane < tail, rests[part], joint), LANES - 3 * cells, 1)
        for index in range(4):
            chunk = xz if index == 3 else joint
            if lanes > LANES:
                spare = jnp.zeros((16, lanes - LANES), jnp.float32)
                chunk = jnp.concatenate([chunk, spare], axis=1)
            shift = (first_cell - (index % 3) * cells) % lanes
            moved = chunk if shift == 0 else pltpu.roll(chunk, shift, 1)
            sums[index] = sums[index] + jnp.where(here, moved, 0.0)
    trace = sums[0] + sums[1] + sums[2]
    scale = (conduct_fiber - conduct_matrix) / (2.0 * trace + tensor_eps)
    conduct = [
        conduct_matrix + scale * (trace - sums[1]),
        -scale * sums[3],
        conduct_matrix + scale * (trace - sums[2]),
    ]
    for kind in range(3):
        conduct_out[kind] = conduct[kind][HALO : HALO + count]
    copies = [
        pltpu.make_async_copy(conduct_out, conduct_hbm, sems.at[0]),
        pltpu.make_async_copy(temp_out, temp_hbm, sems.at[1]),
        pltpu.make_async_copy(cure_out, cure_hbm, sems.at[2]),
    ]
    copies[0].start()

    before, after = columns[parts - 1], columns[0]
    for part in range(parts - 1):
        before = jnp.where(layer == part + 1, columns[part], before)
        after = jnp.where(layer == part, columns[part + 1], after)
    spare = jnp.full((16 - count - 2 * GHOST, lanes), 0.5, jnp.float32)
    temp = jnp.concatenate([
            before[:GHOST] + reference_temp,
            temp_in[...],
            after[:GHOST] + reference_temp,
            8.0 * spare,
        ], axis=0)
    cure = jnp.concatenate([spare[:1], before[GHOST:], cure_in[...], after[GHOST:], spare[:1], spare], axis=0)
    gap = GHOST - HALO
    xx, xz, zz = [pltpu.roll(part, gap, 0) for part in conduct]

    first = (plane == 0) & (layer == 0)
    last = (plane == planes - 1) & (layer == depths - 1)
    for step in range(STEPS):
        top, bottom = tools[2 * step : 2 * step + 1, :], tools[2 * step + 1 : 2 * step + 2, :]
        temp = jnp.where((row < GHOST) & first, temp[GHOST : GHOST + 1], temp)
        temp = jnp.where(
            (row >= GHOST + count) & last, temp[GHOST + count - 1 : GHOST + count], temp
        )
        cooler = jnp.where(lane == 0, top, pltpu.roll(temp, 1, 1))
        later = jnp.where(lane == lanes - 1, bottom, pltpu.roll(temp, lanes - 1, 1))
        slant = later - cooler
        second_x = pltpu.roll(temp, 15, 0) - 2.0 * temp + pltpu.roll(temp, 1, 0)
        second_z = later - 2.0 * temp + cooler
        cross = 0.25 * (pltpu.roll(slant, 15, 0) - pltpu.roll(slant, 1, 0))
        spread = xx * second_x + 2.0 * xz * cross + zz * second_z
        inverse = 1.0 / reference_temp - 1.0 / temp
        left = 1.0 - cure
        rate = rate_first * jnp.exp(energy_first * inverse) + rate_second * jnp.exp(
            energy_second * inverse
        ) * jnp.sqrt(cure)
        rate = rate * (left * jnp.sqrt(left))
        temp = temp + time_step * (spread + heat_release * rate)
        cure = cure + time_step * rate
    temp_out[...] = temp[GHOST : GHOST + count]
    cure_out[...] = cure[GHOST : GHOST + count]
    for copy in copies[1:]:
        copy.start()
    for copy in copies:
        copy.wait()


def on_device(intensity, temp_start, cure_start, tool_levels, plan):
    rows, width, depth = intensity.shape
    count, lanes = temp_start.shape
    planes, depths = lax.axis_size("plane"), lax.axis_size("depth")
    columns, cells = sizes(width, depth)
    bf16 = jnp.bfloat16
    slots = rows * EDGE + 16 * (lanes // LANES)
    params = pltpu.CompilerParams(vmem_limit_bytes=24 * 1024 * 1024)
    vmem = pl.BlockSpec(memory_space=pltpu.VMEM)
    stay = pl.BlockSpec(memory_space=pltpu.HBM)

    fixed = lambda values: pltpu.with_memory_space_constraint(values, pltpu.HBM)
    bands, coarse = x_bands(width), coarse_x_bands(width)
    late = bands.shape[1] - EARLY
    middle = bands[:, :EARLY, EDGE : EDGE + width]
    sides = bands[:, EARLY:].reshape(2 * late, -1)
    x_hbm, early_starts = stacked(
        middle.reshape(2 * EARLY, -1), sides[:, EDGE : EDGE + width], coarse[:, :EARLY]
    )
    z_hbm, _ = stacked(*depth_bands(depth), coarse_depth_bands(depth))
    halos = np.concatenate([sides[:, :EDGE], sides[:, EDGE + width :]], axis=1)
    x_late, late_starts = stacked(halos, coarse[:, EARLY:])
    rims = rim_bands(rows)
    flat, _ = stacked(np.concatenate([rims[0], rims[2]], axis=1))
    steep, rim_starts = stacked(rims[1], *rim_x_bands(count))
    cell_bands, _ = stacked(rim_cells(rows, depth, depths))
    far, near, grey, x_parts, z_parts, temp, cure = pl.pallas_call(
        pack_kernel,
        name="pack",
        out_shape=(
            pltpu.VMEM((slots, depth), bf16),
            pltpu.VMEM((slots, depth), bf16),
            pltpu.VMEM((rows, width, depth), jnp.int32),
            pltpu.VMEM(x_hbm.shape, bf16),
            pltpu.VMEM(z_hbm.shape, bf16),
            pltpu.VMEM((count, lanes), jnp.float32),
            pltpu.VMEM((count, lanes), jnp.float32),
        ),
        in_specs=[stay] * 5,
        scratch_shapes=[
            pltpu.SemaphoreType.DMA((5,)),
        ],
        compiler_params=params,
    )(*[fixed(values) for values in (intensity, temp_start, cure_start, x_hbm, z_hbm)])

    def moved(values, pairs):
        index = [(p * depths + d, q * depths + e) for (p, d), (q, e) in pairs]
        return lax.ppermute(values, ("plane", "depth"), index)

    def swapped(values, first):
        pairs = [(p, p + 1) for p in range(first, planes - 1, 2)]
        pairs += [(q, p) for p, q in pairs]
        return moved(values, [((p, d), (q, d)) for p, q in pairs for d in range(depths)])

    far = swapped(far, 1)
    near = swapped(near, 0)

    high = coarse.shape[0]

    def scratch(count):
        return [
            pltpu.VMEM((2 * count, rows * depth), jnp.float32),
            pltpu.VMEM((3 * rows // 2 * count, 2 * depth), bf16),
            pltpu.VMEM((3 * rows // 2 * count, 2 * depth), jnp.float32),
        ]

    def cost(count):
        return pl.CostEstimate(
            flops=2 * rows * (2 * count) * 160 * depth * 4,
            bytes_accessed=4_000_000,
            transcendentals=0,
        )

    early_sums, diagonal, sides, own_tiles = pl.pallas_call(
        functools.partial(early_kernel, early_starts),
        name="early",
        out_shape=(
            pltpu.VMEM((len(USED), high, LANES), jnp.float32),
            pltpu.VMEM((4 * depth, 2 * depth), bf16),
            pltpu.VMEM((2 * late, rows * depth), jnp.float32),
            pltpu.VMEM((3, width, LANES), jnp.float32),
        ),
        scratch_shapes=scratch(EARLY),
        cost_estimate=cost(EARLY),
        compiler_params=params,
    )(grey, x_parts, z_parts)

    products_x, voxels = own_columns(count)
    at_sums, half = chunk_rows(count, lanes)
    chunk_shape = (depths, at_sums + half, LANES)
    chunks = pl.pallas_call(
        functools.partial(late_kernel, late_starts, width),
        name="late",
        out_shape=pltpu.HBM(chunk_shape, bf16),
        in_specs=[vmem] * 10,
        out_specs=stay,
        scratch_shapes=scratch(late)
        + [pltpu.VMEM(chunk_shape, bf16), pltpu.SemaphoreType.DMA((2,))],
        cost_estimate=cost(late),
        compiler_params=params,
    )(far, near, x_late, z_parts, diagonal, early_sums, sides, own_tiles, temp, cure)

    faces = plan.reshape(2 * STEPS, 1) == jnp.arange(tool_levels.shape[0], dtype=jnp.int32)
    tools = jnp.sum(
        jnp.where(faces, tool_levels, jnp.zeros_like(tool_levels)), axis=1, keepdims=True
    )

    chunks = lax.all_to_all(
        chunks,
        "depth",
        split_axis=0,
        concat_axis=0,
        tiled=True,
        axis_index_groups=[meeting_order(depths)],
    )

    return pl.pallas_call(
        functools.partial(cure_kernel, cells, rim_starts),
        name="cure",
        out_shape=(
            pltpu.HBM((count, lanes), jnp.float32),
            pltpu.HBM((count, lanes), jnp.float32),
            pltpu.HBM((3, count, lanes), jnp.float32),
        ),
        in_specs=[vmem] * 7,
        out_specs=(stay, stay, stay),
        scratch_shapes=[
            pltpu.VMEM((count, lanes), jnp.float32),
            pltpu.VMEM((count, lanes), jnp.float32),
            pltpu.VMEM((3, count, lanes), jnp.float32),
            pltpu.SemaphoreType.DMA((3,)),
        ],
        compiler_params=params,
    )(chunks, temp, cure, tools, flat, steep, cell_bands)


def solution(mesh):
    return jax.shard_map(
        on_device,
        mesh=mesh,
        in_specs=(
            P(None, "plane", "depth"),
            P(("plane", "depth"), None),
            P(("plane", "depth"), None),
            P(),
            P(),
        ),
        out_specs=(
            P(("plane", "depth"), None),
            P(("plane", "depth"), None),
            P(None, ("plane", "depth"), None),
        ),
        check_vma=False,
    )
```

```python
import functools

import jax
import jax.numpy as jnp
import ml_dtypes
import numpy as np
from jax import lax
from jax.experimental import pallas as pl
from jax.experimental.pallas import tpu as pltpu
from jax.sharding import PartitionSpec as P

ROWS = 8
R1 = 6
R2 = 10
COARSE = 4
STEPS = 3

sigma_grad = 2.0
sigma_tensor = 3.3
conduct_matrix = 0.3
conduct_fiber = 1.5
time_step = 0.25
heat_release = 0.4
rate_first = 0.15
rate_second = 0.6
energy_first = 30.0
energy_second = 25.0
reference_temp = 4.2
tensor_eps = 1e-06

LANES = 128
HALO = 2
EDGE = HALO * COARSE + R1 + R2
EARLY = 96
GHOST = 3
COLUMN_ROWS = 2 * GHOST - 1
CODE_SCALE = 2.0**20
RIM = 2 * R1
BEFORE = -(-(R2 - R1) // COARSE)
AFTER = BEFORE
HALF = LANES // 2
ROW_KINDS = (1, 0, 0)
X_KINDS = (0, 1, 0)
DEPTH_KINDS = (0, 0, 1)


def smooth_taps(radius, sigma):
    offsets = np.arange(-radius, radius + 1) * 1.0
    weights = np.exp(-0.5 * offsets * offsets / (sigma * sigma))
    return weights / weights.sum()


def slope_taps(radius, sigma):
    offsets = np.arange(-radius, radius + 1) * 1.0
    weights = np.exp(-0.5 * offsets * offsets / (sigma * sigma))
    return offsets * weights / np.sum(offsets * offsets * weights)


def row_weights(count, radius, sigma):
    taps = smooth_taps(radius, sigma)
    result = np.zeros(count)
    for source in range(count):
        for target in range(count):
            offset = target - source
            if abs(offset) <= radius:
                result[source] += taps[offset + radius]
    return result


def as_bfloat16(matrix):
    return matrix.astype(np.float32).astype(ml_dtypes.bfloat16)


def halves(matrix, axis):
    high = as_bfloat16(matrix).astype(np.float64)
    return np.concatenate([high, as_bfloat16(matrix - high).astype(np.float64)], axis=axis)


def sizes(width, depth):
    columns = width // COARSE + 2 * HALO
    cells = depth // COARSE + BEFORE + AFTER
    return columns, cells


def product_rows(width):
    places = [*range(R1, width - R1)]
    places += [None] * max(EARLY - len(places), 0)
    places += [*range(R1 - EDGE, R1), *range(width - R1, width + EDGE - R1)]
    return places + [None] * (-len(places) % 16)


def grad_taps(kind):
    return slope_taps(R1, sigma_grad) if kind else smooth_taps(R1, sigma_grad)


def tap(taps, offset):
    radius = (len(taps) - 1) // 2
    return float(taps[offset + radius]) if abs(offset) <= radius else 0.0


def x_bands(width):
    places = product_rows(width)
    bands = np.zeros((2, len(places), width + 2 * EDGE))
    for kind in range(2):
        for row, place in enumerate(places):
            if place is not None:
                first = place + EDGE - R1
                bands[kind, row, first : first + 2 * R1 + 1] = grad_taps(kind)
    return bands


def rim_bands(rows):
    bands = np.zeros((3, 2 * LANES, LANES))
    for part in range(3):
        row_taps, depth_taps = grad_taps(ROW_KINDS[part]), grad_taps(DEPTH_KINDS[part])
        for source in range(rows):
            for target in range(rows):
                row_tap = tap(row_taps, source - target)
                for near in range(-RIM, RIM):
                    lane = source * RIM + near % RIM
                    if near >= 0:
                        lane += rows * RIM
                    for place in range(-R1, R1):
                        value = row_tap * tap(depth_taps, near - place)
                        bands[part, lane, target * 2 * R1 + R1 + place] = value
    return bands


def rim_cells(rows, depth, blocks):
    taps = smooth_taps(R2, sigma_tensor)
    weights = product_weights(rows)
    bands = np.zeros((blocks - 1, LANES, blocks * depth // COARSE))
    for boundary in range(blocks - 1):
        middle = (boundary + 1) * depth
        for cell in range(bands.shape[2]):
            for voxel in range(cell * COARSE, (cell + 1) * COARSE):
                for place in range(-R1, R1):
                    value = tap(taps, middle + place - voxel)
                    for row in range(rows):
                        bands[boundary, row * 2 * R1 + R1 + place, cell] += weights[row] * value
    return bands.reshape(-1, bands.shape[2])


def meeting_order(blocks):
    middle = blocks // 2
    return [*range(middle, blocks), *range(middle)]


def own_columns(count):
    products = (count + 2 * HALO) * COARSE + 2 * R2
    voxels = products + 2 * R1
    return -(-products // 16) * 16, -(-voxels // 8) * 8


def fold(voxels):
    return -(-voxels // 16) * 8


def rim_x_bands(count):
    products, voxels = own_columns(count)
    bands = np.zeros((2, products, -(-voxels // 16) * 16))
    valid = (count + 2 * HALO) * COARSE + 2 * R2
    for kind in range(2):
        for row in range(valid):
            bands[kind, row, row : row + 2 * R1 + 1] = grad_taps(kind)
    taps = smooth_taps(R2, sigma_tensor)
    coarse = np.zeros((16, products))
    for column in range(count + 2 * HALO):
        for voxel in range(column * COARSE, (column + 1) * COARSE):
            coarse[column, voxel : voxel + 2 * R2 + 1] += taps
    return halves(bands.reshape(2 * products, -1), 1), coarse


def depth_bands(depth):
    bands = np.zeros((2, depth, depth))
    for kind in range(2):
        for place in range(depth):
            for near in range(max(place - R1, 0), min(place + R1 + 1, depth)):
                bands[kind, near, place] = tap(grad_taps(kind), near - place)
    return bands


def product_weights(rows):
    return row_weights(rows, R2, sigma_tensor) / 255.0**2


def coarse_depth_bands(depth):
    taps = smooth_taps(R2, sigma_tensor)
    columns, cells = sizes(0, depth)
    bands = np.zeros((depth, LANES))
    for cell in range(cells):
        for voxel in range(COARSE):
            place = (cell - BEFORE) * COARSE + voxel
            for near in range(max(place - R2, 0), min(place + R2 + 1, depth)):
                bands[near, cell] += tap(taps, near - place)
    return bands


def coarse_x_bands(width):
    taps = smooth_taps(R2, sigma_tensor)
    places = product_rows(width)
    columns, cells = sizes(width, 0)
    bands = np.zeros((-(-columns // 16) * 16, len(places)))
    for column in range(columns):
        for voxel in range(COARSE):
            middle = (column - HALO) * COARSE + voxel
            for row, place in enumerate(places):
                if place is not None:
                    bands[column, row] += tap(taps, place - middle)
    return bands


def stacked(*pieces):
    widest = max(piece.shape[1] for piece in pieces)
    padded = [np.pad(piece, ((0, 0), (0, widest - piece.shape[1]))) for piece in pieces]
    starts = np.cumsum([0] + [len(piece) for piece in pieces])
    return jnp.asarray(as_bfloat16(np.concatenate(padded))), tuple(int(start) for start in starts)


def two_parts(values):
    high = values.astype(jnp.bfloat16).astype(jnp.float32)
    return jnp.concatenate([high, (values - high).astype(jnp.bfloat16).astype(jnp.float32)], axis=0)


def joined(parts):
    half = parts.shape[0] // 2
    return parts[:half] + parts[half:]


def coded(values):
    values = values * CODE_SCALE
    return (values * jnp.abs(values)) * (values * values)


def decoded(values):
    size = jnp.sqrt(jnp.sqrt(jnp.abs(values))) * (1.0 / CODE_SCALE)
    return jnp.where(values < 0.0, -size, size)


def column_rows(temp, cure, at_end):
    count = temp.shape[0]
    first, second = (count - GHOST, count - GHOST + 1) if at_end else (0, 0)
    pad = jnp.zeros((8 - COLUMN_ROWS, temp.shape[1]), jnp.float32)
    return jnp.concatenate(
        [temp[first : first + GHOST, :], cure[second : second + GHOST - 1, :], pad], axis=0
    )


def chunk_rows(count, lanes):
    products, voxels = own_columns(count)
    held = count + 2 * HALO + 1 + COLUMN_ROWS * (lanes // LANES)
    return voxels + fold(voxels), -(-held // 16) * 16


def is_odd():
    return lax.rem(lax.axis_index("plane"), 2) == 1


def pack_kernel(
    intensity, temp_hbm, cure_hbm, x_hbm, z_hbm, far, near, grey, x_parts, z_parts, temp, cure,
    sems,
):
    rows, width, depth = intensity.shape
    copies = [
        pltpu.make_async_copy(intensity, grey, sems.at[0]),
        pltpu.make_async_copy(temp_hbm, temp, sems.at[1]),
        pltpu.make_async_copy(cure_hbm, cure, sems.at[2]),
        pltpu.make_async_copy(x_hbm, x_parts, sems.at[3]),
        pltpu.make_async_copy(z_hbm, z_parts, sems.at[4]),
    ]
    for copy in copies:
        copy.start()
    for copy in copies[:3]:
        copy.wait()
    odd = is_odd()
    sides = [
        two_parts(column_rows(temp, cure, at_end)).astype(jnp.bfloat16)
        for at_end in (False, True)
    ]

    def send(left, right):
        for place, target, columns in ((0, left, sides[0]), (width - EDGE, right, sides[1])):
            for pair in range(rows // 2):
                two = [grey[2 * pair + i, place : place + EDGE, :] for i in range(2)]
                two = jnp.concatenate(two, axis=0).astype(jnp.float32)
                target[2 * EDGE * pair : 2 * EDGE * (pair + 1), :] = two.astype(jnp.bfloat16)
            for slot in range(temp.shape[1] // LANES):
                at = rows * EDGE + 16 * slot
                target[at : at + 16, :] = columns[:, slot * LANES : (slot + 1) * LANES]

    @pl.when(odd)
    def _():
        send(near, far)

    @pl.when(jnp.logical_not(odd))
    def _():
        send(far, near)

    for copy in copies[3:]:
        copy.wait()


def packed_rows(values, size, first):
    depth = values[0].shape[1]
    lane = lax.broadcasted_iota(jnp.int32, values[0].shape, 1)
    packed = None
    for block, value in enumerate(values):
        shift = (size * block - first) % depth
        moved = value if shift == 0 else pltpu.roll(value, shift, 1)
        packed = moved if block == 0 else jnp.where(lane >= size * block, moved, packed)
    return packed


def edges_of(ref, rows):
    two = [
        ref[2 * EDGE * pair : 2 * EDGE * (pair + 1), :].astype(jnp.float32)
        for pair in range(rows // 2)
    ]
    voxels = [two[row // 2][row % 2 * EDGE : (row % 2 + 1) * EDGE] for row in range(rows)]
    slots = range(rows * EDGE, ref.shape[0], 16)
    columns = [joined(ref[at : at + 16, :].astype(jnp.float32)) for at in slots]
    return voxels, jnp.concatenate(columns, axis=1)


def product(first, second):
    return jnp.dot(first, second, preferred_element_type=jnp.float32)


def mirrored_filter(kind, values, even):
    rows = len(values)
    use_sum = even == (kind == 0)
    sign = 1.0 if use_sum else -1.0
    half = [values[row] + sign * values[rows - 1 - row] for row in range(rows // 2)]
    results = []
    for row in range(rows // 2):
        total = None
        for source, value in enumerate(half):
            near = tap(grad_taps(kind), source - row)
            far = tap(grad_taps(kind), rows - 1 - source - row)
            weight = 0.5 * (near + sign * far)
            total = weight * value if total is None else total + weight * value
        results.append(total)
    return results


def weighted_products(three, weight):
    pairs = ((0, 0), (1, 1), (2, 2), (0, 1), (0, 2), (1, 2))
    first = [weight * value for value in three]
    return [first[a] * three[b] for a, b in pairs]


def late_mask(count, width):
    row = lax.broadcasted_iota(jnp.int32, (count, LANES), 0)
    left = max(width - 2 * R1 - EARLY, 0)
    place = jnp.where(row < left + EDGE, row - left + R1 - EDGE, row - left - EDGE + width - R1)
    place = place + lax.axis_index("plane") * width
    inside = (place >= 0) & (place < lax.axis_size("plane") * width)
    return jnp.where(inside | (row < left), 1.0, 0.0)


USED = (0, 1, 2, 5)
UNUSED = (3, 4)


def all_sums(products, coarse, sx):
    sums = [None] * 6
    for kinds in (USED, UNUSED):
        tiles = [tile for index in kinds for tile in products[index]]
        along = product(sx, jnp.concatenate(tiles, axis=1)).astype(jnp.bfloat16)
        step = along.shape[1] // len(kinds)
        parts = [along[:, index * step : (index + 1) * step] for index in range(len(kinds))]
        total = product(jnp.concatenate(parts, axis=0), coarse)
        high = sx.shape[0]
        for index, kind in enumerate(kinds):
            sums[kind] = total[index * high : (index + 1) * high]
    return sums


def tensor_sums(across, sx, mask, diagonal, z_parts, filtered, grads):
    double = diagonal.shape[1]
    depth, pairs = double // 2, across.shape[1] // double
    rows, count = 2 * pairs, across.shape[0] // 2
    for start in range(0, count, 16):
        kinds = [
            [
                across[kind * count + start : kind * count + start + 16, row * depth : (row + 1) * depth]
                for row in range(rows)
            ]
            for kind in range(2)
        ]
        for part in range(3):
            values = kinds[X_KINDS[part]]
            results = mirrored_filter(ROW_KINDS[part], values, True)
            results += mirrored_filter(ROW_KINDS[part], values, False)
            for row, result in enumerate(results):
                at = (part * pairs + row // 2) * count + start
                lanes = slice((row % 2) * depth, (row % 2 + 1) * depth)
                filtered[at : at + 16, lanes] = result.astype(jnp.bfloat16)

    at = 2 * pairs * count
    for kind, part in enumerate((slice(0, at), slice(at, filtered.shape[0]))):
        twice = jnp.concatenate([filtered[part, :], filtered[part, :]], axis=1)
        grads[part, :] = product(
            twice, diagonal[2 * kind * double : 2 * (kind + 1) * double, :]
        )

    weights = product_weights(rows)
    layer = lax.axis_index("depth")
    first, last = layer == 0, layer == lax.axis_size("depth") - 1
    place = lax.broadcasted_iota(jnp.int32, (16, depth), 1)
    complete = ((place >= R1) | first) & ((place < depth - R1) | last)
    complete = jnp.where(complete, 1.0, 0.0)
    groups = [[] for _ in range(6)]
    for start in range(0, count, 16):
        inside = complete if mask is None else complete * mask[start : start + 16]
        totals = None
        for row in range(rows):
            lanes = slice((row % 2) * depth, (row % 2 + 1) * depth)
            three = []
            for part in range(3):
                at = (part * pairs + row // 2) * count + start
                three.append(grads[at : at + 16, lanes])
            terms = weighted_products(three, 2.0 * float(weights[row % (rows // 2)]))
            totals = terms if row == 0 else [a + b for a, b in zip(totals, terms)]
        for index in range(6):
            groups[index].append((totals[index] * inside).astype(jnp.bfloat16))
    products = [[jnp.concatenate(group, axis=0)] for group in groups]
    return all_sums(products, z_parts[2 * double : 2 * double + depth, :], sx)


def rim_tiles(values):
    rows, depth = len(values), values[0].shape[1]
    below = packed_rows(values, RIM, depth - RIM)
    above = pltpu.roll(packed_rows(values, RIM, 0), rows * RIM, 1)
    lane = lax.broadcasted_iota(jnp.int32, below.shape, 1)
    return [jnp.where(lane < rows * RIM, below, above), above, pltpu.roll(above, HALF, 1)]


def early_kernel(
    starts, grey, x_parts, z_parts, sums, diagonal, sides, tiles, across, filtered, grads
):
    rows, width, depth = grey.shape
    double = 2 * depth
    empty = jnp.zeros((depth, depth), jnp.bfloat16)
    for part in range(4):
        for half in range(2):
            at = pl.ds(part * double + half * depth, depth)
            band = z_parts[part * depth : (part + 1) * depth, :]
            diagonal[at, half * depth : (half + 1) * depth] = band
            diagonal[at, (1 - half) * depth : (2 - half) * depth] = empty
    values = [grey[row].astype(jnp.float32) for row in range(rows)]
    whole = jnp.concatenate([value.astype(jnp.bfloat16) for value in values], axis=1)
    twice = jnp.concatenate([whole, whole], axis=0)
    result = product(x_parts[starts[0] : starts[2], : 2 * width], twice)
    across[...] = result[: starts[1]]
    sides[...] = result[starts[1] :]
    sx = x_parts[starts[2] : starts[3], :EARLY]
    results = tensor_sums(across, sx, None, diagonal, z_parts, filtered, grads)
    for index, kind in enumerate(USED):
        sums[index] = results[kind]
    for index, tile in enumerate(rim_tiles(values)):
        tiles[index] = tile


def late_kernel(
    starts, width, far, near, x_late, z_parts, diagonal, early_sums, sides, own_tiles, temp, cure,
    out_hbm, across, filtered, grads, out, sems,
):
    double = diagonal.shape[1]
    depth = double // 2
    rows = across.shape[1] // depth
    count, lanes = temp.shape
    odd = is_odd()
    depths, layer = lax.axis_size("depth"), lax.axis_index("depth")
    outer, outer_columns = edges_of(far, rows)
    inner, inner_columns = edges_of(near, rows)
    values = []
    for row in range(rows):
        left = jnp.where(odd, inner[row], outer[row])
        right = jnp.where(odd, outer[row], inner[row])
        values.append(jnp.concatenate([left, right], axis=0))
    left = jnp.where(odd, inner_columns, outer_columns)
    right = jnp.where(odd, outer_columns, inner_columns)

    late = across.shape[0] // 2
    halos = jnp.concatenate([value.astype(jnp.bfloat16) for value in values], axis=1)
    halos = jnp.concatenate([halos, halos], axis=0)
    across[...] = sides[...] + product(x_late[starts[0] : starts[1], : 4 * EDGE], halos)

    products_x, voxels = own_columns(count)
    folded, stride = fold(voxels), COARSE * count
    tiles = [
        jnp.concatenate([tile[:EDGE], own_tiles[index], tile[EDGE:]], axis=0)
        for index, tile in enumerate(rim_tiles(values))
    ]
    missing = stride * (depths - 1) + voxels - tiles[0].shape[0]
    if missing > 0:
        spare = jnp.zeros((-(-missing // 8) * 8, LANES), jnp.float32)
        tiles = [jnp.concatenate([tile, spare], axis=0) for tile in tiles]

    height = count + 2 * HALO
    half_lane = lax.broadcasted_iota(jnp.int32, (folded, LANES), 1) < HALF
    order = meeting_order(out.shape[0])
    for position, target in enumerate(order):
        at = stride * target
        second = jnp.where(
            half_lane,
            tiles[1][at : at + folded],
            tiles[2][at + voxels - folded : at + voxels],
        )
        rims = jnp.concatenate([tiles[0][at : at + voxels], second], axis=0)
        out[position, 0 : voxels + folded, :] = rims.astype(jnp.bfloat16)
    split = (pl.ds(0, voxels + folded), pl.ds(voxels + folded, out.shape[1] - voxels - folded))
    copies = [
        pltpu.make_async_copy(out.at[:, part, :], out_hbm.at[:, part, :], sems.at[index])
        for index, part in enumerate(split)
    ]
    copies[0].start()

    sx = x_late[starts[1] : starts[2], :late]
    results = tensor_sums(
        across, sx, late_mask(late, width), diagonal, z_parts, filtered, grads
    )
    yy, xx, zz, xz = [early_sums[index] + results[kind] for index, kind in enumerate(USED)]
    lane = lax.broadcasted_iota(jnp.int32, yy.shape, 1)
    columns, cells = sizes(width, depth)
    tail = 4 * cells - LANES
    joint = pltpu.roll(xz, 3 * cells, 1)
    rest = jnp.where(lane < tail, joint, 0.0)
    rest = pltpu.roll(rest, 0, 1, stride=tail, stride_axis=0)
    for index, part in ((2, zz), (1, xx), (0, yy)):
        moved = part if index == 0 else pltpu.roll(part, index * cells, 1)
        joint = jnp.where(lane < (index + 1) * cells, moved, joint)

    own_first, own_last = column_rows(temp, cure, False), column_rows(temp, cure, True)
    half = chunk_rows(count, lanes)[1]
    for position, target in enumerate(order):
        piece = jnp.where(layer == target - 1, own_last, 0.0)
        piece = jnp.where(layer == target + 1, own_first, piece)
        if target == 0:
            piece = jnp.where(layer == depths - 1, left, piece)
        if target == out.shape[0] - 1:
            piece = jnp.where(layer == 0, right, piece)
        mine = slice(count * target, count * target + height)
        pieces = [coded(joint[mine]), coded(jnp.sum(rest[mine], axis=0, keepdims=True))]
        for slot in range(lanes // LANES):
            part = piece[:, slot * LANES : (slot + 1) * LANES]
            pieces += [part[:GHOST] - reference_temp, part[GHOST:COLUMN_ROWS]]
        filled = sum(part.shape[0] for part in pieces)
        if filled < half:
            pieces.append(jnp.zeros((half - filled, LANES), jnp.float32))
        out[position, voxels + folded :, :] = jnp.concatenate(pieces, axis=0).astype(jnp.bfloat16)
    copies[1].start()
    for copy in copies:
        copy.wait()


def rim_sums(chunks, count, starts, flat, steep, cells):
    parts = chunks.shape[0]
    rows_x, voxels = own_columns(count)
    folded = fold(voxels)
    tall = -(-voxels // 16) * 16
    spare = [jnp.zeros((tall - voxels, LANES), jnp.float32)] if tall > voxels else []
    lane = lax.broadcasted_iota(jnp.int32, (voxels, LANES), 1)
    order = meeting_order(parts)
    rims = [
        chunks[order.index(part), 0 : voxels + folded, :].astype(jnp.float32)
        for part in range(parts)
    ]
    tiles = []
    for below, above in zip(rims[:-1], rims[1:]):
        first = jnp.where(lane < ROWS * RIM, below[:voxels], above[:voxels])
        second = above[voxels:]
        second = [second[: voxels - folded], pltpu.roll(second, HALF, 1)]
        for tile in ([first], second):
            tiles.append(jnp.concatenate(tile + spare, axis=0).astype(jnp.bfloat16))
    wide = jnp.concatenate(tiles, axis=1)
    result = product(
        steep[starts[1] : starts[2], : 2 * tall], jnp.concatenate([wide, wide], axis=0)
    ).astype(jnp.bfloat16)
    kinds = []
    for kind in range(2):
        values = result[kind * rows_x : (kind + 1) * rows_x]
        stack = [
            values[:, 2 * part * LANES : 2 * (part + 1) * LANES] for part in range(parts - 1)
        ]
        stack = jnp.concatenate(stack, axis=0)
        kinds.append(jnp.concatenate([stack, stack], axis=1))
    both = product(kinds[0], flat[...])
    three = (both[:, :LANES], product(kinds[1], steep[starts[0] : starts[1], :LANES]), both[:, LANES:])

    index = lax.axis_index("plane") * lax.axis_size("depth") + lax.axis_index("depth")
    total = lax.axis_size("plane") * lax.axis_size("depth") * count * COARSE
    place = lax.rem(lax.broadcasted_iota(jnp.int32, three[0].shape, 0), rows_x)
    place = place + (index * count - HALO) * COARSE - R2
    inside = jnp.where((place >= 0) & (place < total), 1.0, 0.0)
    products = [
        [
            term[part * rows_x : (part + 1) * rows_x].astype(jnp.bfloat16)
            for part in range(parts - 1)
        ]
        for term in weighted_products(three, inside)
    ]
    return all_sums(products, cells[...], steep[starts[2] : starts[3], :rows_x])


def cure_kernel(
    cells, starts, chunks, temp_in, cure_in, tools, flat, steep, rim_bands, temp_hbm, cure_hbm,
    conduct_hbm, temp_out, cure_out, conduct_out, sems,
):
    count, lanes = temp_in.shape
    parts = chunks.shape[0]
    planes, depths = lax.axis_size("plane"), lax.axis_size("depth")
    plane, layer = lax.axis_index("plane"), lax.axis_index("depth")
    height = count + 2 * HALO
    own = cells - BEFORE - AFTER
    lane = lax.broadcasted_iota(jnp.int32, (16, lanes), 1)
    row = lax.broadcasted_iota(jnp.int32, (16, lanes), 0)
    at_sums, half = chunk_rows(count, lanes)
    tail = 4 * cells - LANES
    narrow_lane = lax.broadcasted_iota(jnp.int32, (16, LANES), 1)
    order = meeting_order(parts)

    near = rim_sums(chunks, count, starts, flat, steep, rim_bands)
    sums = [near[kind] for kind in USED]
    blocks = [chunks[order.index(part), at_sums:, :].astype(jnp.float32) for part in range(parts)]
    columns = [
        jnp.concatenate(
            [
                block[at : at + COLUMN_ROWS]
                for at in range(
                    height + 1, height + 1 + COLUMN_ROWS * (lanes // LANES), COLUMN_ROWS
                )
            ],
            axis=1,
        )
        for block in blocks
    ]
    blocks = [decoded(block[0:16]) for block in blocks]
    tails = [block[height : height + 1] for block in blocks]
    if parts % 8:
        tails.append(jnp.zeros((-parts % 8, LANES), jnp.float32))
    tails = jnp.concatenate(tails, axis=0)
    tails = pltpu.roll(tails, lax.rem(LANES - lax.rem(tail * count * layer, LANES), LANES), 1)
    narrow_row = lax.broadcasted_iota(jnp.int32, (16, LANES), 0)
    rests = [jnp.zeros((16, LANES), jnp.float32) for _ in range(parts)]
    for column in range(height):
        moved = pltpu.roll(tails, LANES - tail * column, 1) if column else tails
        for part in range(parts):
            rests[part] = jnp.where(narrow_row == column, moved[part : part + 1], rests[part])
    for part in range(parts):
        first_cell = own * part - BEFORE
        here = (lane >= first_cell) & (lane < first_cell + cells)
        values = blocks[part]
        joint = values[0:16]
        xz = pltpu.roll(jnp.where(narrow_lane < tail, rests[part], joint), LANES - 3 * cells, 1)
        for index in range(4):
            chunk = xz if index == 3 else joint
            if lanes > LANES:
                spare = jnp.zeros((16, lanes - LANES), jnp.float32)
                chunk = jnp.concatenate([chunk, spare], axis=1)
            shift = (first_cell - (index % 3) * cells) % lanes
            moved = chunk if shift == 0 else pltpu.roll(chunk, shift, 1)
            sums[index] = sums[index] + jnp.where(here, moved, 0.0)
    trace = sums[0] + sums[1] + sums[2]
    scale = (conduct_fiber - conduct_matrix) / (2.0 * trace + tensor_eps)
    conduct = [
        conduct_matrix + scale * (trace - sums[1]),
        -scale * sums[3],
        conduct_matrix + scale * (trace - sums[2]),
    ]
    for kind in range(3):
        conduct_out[kind] = conduct[kind][HALO : HALO + count]
    copies = [
        pltpu.make_async_copy(conduct_out, conduct_hbm, sems.at[0]),
        pltpu.make_async_copy(temp_out, temp_hbm, sems.at[1]),
        pltpu.make_async_copy(cure_out, cure_hbm, sems.at[2]),
    ]
    copies[0].start()

    before, after = columns[parts - 1], columns[0]
    for part in range(parts - 1):
        before = jnp.where(layer == part + 1, columns[part], before)
        after = jnp.where(layer == part, columns[part + 1], after)
    spare = jnp.full((16 - count - 2 * GHOST, lanes), 0.5, jnp.float32)
    temp = jnp.concatenate([
            before[:GHOST] + reference_temp,
            temp_in[...],
            after[:GHOST] + reference_temp,
            8.0 * spare,
        ], axis=0)
    cure = jnp.concatenate([spare[:1], before[GHOST:], cure_in[...], after[GHOST:], spare[:1], spare], axis=0)
    gap = GHOST - HALO
    xx, xz, zz = [pltpu.roll(part, gap, 0) for part in conduct]

    first = (plane == 0) & (layer == 0)
    last = (plane == planes - 1) & (layer == depths - 1)
    for step in range(STEPS):
        top, bottom = tools[2 * step : 2 * step + 1, :], tools[2 * step + 1 : 2 * step + 2, :]
        temp = jnp.where((row < GHOST) & first, temp[GHOST : GHOST + 1], temp)
        temp = jnp.where(
            (row >= GHOST + count) & last, temp[GHOST + count - 1 : GHOST + count], temp
        )
        cooler = jnp.where(lane == 0, top, pltpu.roll(temp, 1, 1))
        later = jnp.where(lane == lanes - 1, bottom, pltpu.roll(temp, lanes - 1, 1))
        slant = later - cooler
        second_x = pltpu.roll(temp, 15, 0) - 2.0 * temp + pltpu.roll(temp, 1, 0)
        second_z = later - 2.0 * temp + cooler
        cross = 0.25 * (pltpu.roll(slant, 15, 0) - pltpu.roll(slant, 1, 0))
        spread = xx * second_x + 2.0 * xz * cross + zz * second_z
        inverse = 1.0 / reference_temp - 1.0 / temp
        left = 1.0 - cure
        rate = rate_first * jnp.exp(energy_first * inverse) + rate_second * jnp.exp(
            energy_second * inverse
        ) * jnp.sqrt(cure)
        rate = rate * (left * jnp.sqrt(left))
        temp = temp + time_step * (spread + heat_release * rate)
        cure = cure + time_step * rate
    temp_out[...] = temp[GHOST : GHOST + count]
    cure_out[...] = cure[GHOST : GHOST + count]
    for copy in copies[1:]:
        copy.start()
    for copy in copies:
        copy.wait()


def on_device(intensity, temp_start, cure_start, tool_levels, plan):
    rows, width, depth = intensity.shape
    count, lanes = temp_start.shape
    planes, depths = lax.axis_size("plane"), lax.axis_size("depth")
    columns, cells = sizes(width, depth)
    bf16 = jnp.bfloat16
    slots = rows * EDGE + 16 * (lanes // LANES)
    params = pltpu.CompilerParams(vmem_limit_bytes=24 * 1024 * 1024)
    vmem = pl.BlockSpec(memory_space=pltpu.VMEM)
    stay = pl.BlockSpec(memory_space=pltpu.HBM)

    fixed = lambda values: pltpu.with_memory_space_constraint(values, pltpu.HBM)
    bands, coarse = x_bands(width), coarse_x_bands(width)
    late = bands.shape[1] - EARLY
    middle = bands[:, :EARLY, EDGE : EDGE + width]
    sides = bands[:, EARLY:].reshape(2 * late, -1)
    x_hbm, early_starts = stacked(
        halves(middle.reshape(2 * EARLY, -1), 1),
        halves(sides[:, EDGE : EDGE + width], 1),
        coarse[:, :EARLY],
    )
    z_hbm, _ = stacked(
        *[halves(bands, 0) for bands in depth_bands(depth)], coarse_depth_bands(depth)
    )
    halos = np.concatenate([sides[:, :EDGE], sides[:, EDGE + width :]], axis=1)
    x_late, late_starts = stacked(halves(halos, 1), coarse[:, EARLY:])
    rims = rim_bands(rows)
    flat, _ = stacked(halves(np.concatenate([rims[0], rims[2]], axis=1), 0))
    steep, rim_starts = stacked(halves(rims[1], 0), *rim_x_bands(count))
    cell_bands, _ = stacked(rim_cells(rows, depth, depths))
    far, near, grey, x_parts, z_parts, temp, cure = pl.pallas_call(
        pack_kernel,
        name="pack",
        out_shape=(
            pltpu.VMEM((slots, depth), bf16),
            pltpu.VMEM((slots, depth), bf16),
            pltpu.VMEM((rows, width, depth), jnp.int32),
            pltpu.VMEM(x_hbm.shape, bf16),
            pltpu.VMEM(z_hbm.shape, bf16),
            pltpu.VMEM((count, lanes), jnp.float32),
            pltpu.VMEM((count, lanes), jnp.float32),
        ),
        in_specs=[stay] * 5,
        scratch_shapes=[
            pltpu.SemaphoreType.DMA((5,)),
        ],
        compiler_params=params,
    )(*[fixed(values) for values in (intensity, temp_start, cure_start, x_hbm, z_hbm)])

    def moved(values, pairs):
        index = [(p * depths + d, q * depths + e) for (p, d), (q, e) in pairs]
        return lax.ppermute(values, ("plane", "depth"), index)

    def swapped(values, first):
        pairs = [(p, p + 1) for p in range(first, planes - 1, 2)]
        pairs += [(q, p) for p, q in pairs]
        return moved(values, [((p, d), (q, d)) for p, q in pairs for d in range(depths)])

    far = swapped(far, 1)
    near = swapped(near, 0)

    high = coarse.shape[0]

    def scratch(count):
        return [
            pltpu.VMEM((2 * count, rows * depth), jnp.float32),
            pltpu.VMEM((3 * rows // 2 * count, 2 * depth), bf16),
            pltpu.VMEM((3 * rows // 2 * count, 2 * depth), jnp.float32),
        ]

    def cost(count):
        return pl.CostEstimate(
            flops=2 * rows * (2 * count) * 160 * depth * 4,
            bytes_accessed=4_000_000,
            transcendentals=0,
        )

    early_sums, diagonal, sides, own_tiles = pl.pallas_call(
        functools.partial(early_kernel, early_starts),
        name="early",
        out_shape=(
            pltpu.VMEM((len(USED), high, LANES), jnp.float32),
            pltpu.VMEM((8 * depth, 2 * depth), bf16),
            pltpu.VMEM((2 * late, rows * depth), jnp.float32),
            pltpu.VMEM((3, width, LANES), jnp.float32),
        ),
        scratch_shapes=scratch(EARLY),
        cost_estimate=cost(EARLY),
        compiler_params=params,
    )(grey, x_parts, z_parts)

    products_x, voxels = own_columns(count)
    at_sums, half = chunk_rows(count, lanes)
    chunk_shape = (depths, at_sums + half, LANES)
    chunks = pl.pallas_call(
        functools.partial(late_kernel, late_starts, width),
        name="late",
        out_shape=pltpu.HBM(chunk_shape, bf16),
        in_specs=[vmem] * 10,
        out_specs=stay,
        scratch_shapes=scratch(late)
        + [pltpu.VMEM(chunk_shape, bf16), pltpu.SemaphoreType.DMA((2,))],
        cost_estimate=cost(late),
        compiler_params=params,
    )(far, near, x_late, z_parts, diagonal, early_sums, sides, own_tiles, temp, cure)

    faces = plan.reshape(2 * STEPS, 1) == jnp.arange(tool_levels.shape[0], dtype=jnp.int32)
    tools = jnp.sum(
        jnp.where(faces, tool_levels, jnp.zeros_like(tool_levels)), axis=1, keepdims=True
    )

    chunks = lax.all_to_all(
        chunks,
        "depth",
        split_axis=0,
        concat_axis=0,
        tiled=True,
        axis_index_groups=[meeting_order(depths)],
    )

    return pl.pallas_call(
        functools.partial(cure_kernel, cells, rim_starts),
        name="cure",
        out_shape=(
            pltpu.HBM((count, lanes), jnp.float32),
            pltpu.HBM((count, lanes), jnp.float32),
            pltpu.HBM((3, count, lanes), jnp.float32),
        ),
        in_specs=[vmem] * 7,
        out_specs=(stay, stay, stay),
        scratch_shapes=[
            pltpu.VMEM((count, lanes), jnp.float32),
            pltpu.VMEM((count, lanes), jnp.float32),
            pltpu.VMEM((3, count, lanes), jnp.float32),
            pltpu.SemaphoreType.DMA((3,)),
        ],
        compiler_params=params,
    )(chunks, temp, cure, tools, flat, steep, cell_bands)


def solution(mesh):
    return jax.shard_map(
        on_device,
        mesh=mesh,
        in_specs=(
            P(None, "plane", "depth"),
            P(("plane", "depth"), None),
            P(("plane", "depth"), None),
            P(),
            P(),
        ),
        out_specs=(
            P(("plane", "depth"), None),
            P(("plane", "depth"), None),
            P(None, ("plane", "depth"), None),
        ),
        check_vma=False,
    )
```

```python
import functools

import jax
import jax.numpy as jnp
import ml_dtypes
import numpy as np
from jax import lax
from jax.experimental import pallas as pl
from jax.experimental.pallas import tpu as pltpu
from jax.sharding import PartitionSpec as P

ROWS = 8
R1 = 6
R2 = 10
COARSE = 4
STEPS = 3

sigma_grad = 2.0
sigma_tensor = 3.3
conduct_matrix = 0.3
conduct_fiber = 1.5
time_step = 0.25
heat_release = 0.4
rate_first = 0.15
rate_second = 0.6
energy_first = 30.0
energy_second = 25.0
reference_temp = 4.2
tensor_eps = 1e-06

LANES = 128
HALO = 2
EDGE = HALO * COARSE + R1 + R2
EARLY = 96
GHOST = 3
COLUMN_ROWS = 2 * GHOST - 1
CODE_SCALE = 2.0**20
RIM = 2 * R1
BEFORE = -(-(R2 - R1) // COARSE)
AFTER = BEFORE
HALF = LANES // 2
ROW_KINDS = (1, 0, 0)
X_KINDS = (0, 1, 0)
DEPTH_KINDS = (0, 0, 1)


def smooth_taps(radius, sigma):
    offsets = np.arange(-radius, radius + 1) * 1.0
    weights = np.exp(-0.5 * offsets * offsets / (sigma * sigma))
    return weights / weights.sum()


def slope_taps(radius, sigma):
    offsets = np.arange(-radius, radius + 1) * 1.0
    weights = np.exp(-0.5 * offsets * offsets / (sigma * sigma))
    return offsets * weights / np.sum(offsets * offsets * weights)


def row_weights(count, radius, sigma):
    taps = smooth_taps(radius, sigma)
    result = np.zeros(count)
    for source in range(count):
        for target in range(count):
            offset = target - source
            if abs(offset) <= radius:
                result[source] += taps[offset + radius]
    return result


def as_bfloat16(matrix):
    return matrix.astype(np.float32).astype(ml_dtypes.bfloat16)


def halves(matrix, axis):
    high = as_bfloat16(matrix).astype(np.float64)
    return np.concatenate([high, as_bfloat16(matrix - high).astype(np.float64)], axis=axis)


def sizes(width, depth):
    columns = width // COARSE + 2 * HALO
    cells = depth // COARSE + BEFORE + AFTER
    return columns, cells


def product_rows(width):
    places = [*range(R1, width - R1)]
    places += [None] * max(EARLY - len(places), 0)
    places += [*range(R1 - EDGE, R1), *range(width - R1, width + EDGE - R1)]
    return places + [None] * (-len(places) % 16)


def grad_taps(kind):
    return slope_taps(R1, sigma_grad) if kind else smooth_taps(R1, sigma_grad)


def tap(taps, offset):
    radius = (len(taps) - 1) // 2
    return float(taps[offset + radius]) if abs(offset) <= radius else 0.0


def x_bands(width):
    places = product_rows(width)
    bands = np.zeros((2, len(places), width + 2 * EDGE))
    for kind in range(2):
        for row, place in enumerate(places):
            if place is not None:
                first = place + EDGE - R1
                bands[kind, row, first : first + 2 * R1 + 1] = grad_taps(kind)
    return bands


def rim_bands(rows):
    bands = np.zeros((3, 2 * LANES, LANES))
    for part in range(3):
        row_taps, depth_taps = grad_taps(ROW_KINDS[part]), grad_taps(DEPTH_KINDS[part])
        for source in range(rows):
            for target in range(rows):
                row_tap = tap(row_taps, source - target)
                for near in range(-RIM, RIM):
                    lane = source * RIM + near % RIM
                    if near >= 0:
                        lane += rows * RIM
                    for place in range(-R1, R1):
                        value = row_tap * tap(depth_taps, near - place)
                        bands[part, lane, target * 2 * R1 + R1 + place] = value
    return bands


def rim_cells(rows, depth, blocks):
    taps = smooth_taps(R2, sigma_tensor)
    weights = product_weights(rows)
    bands = np.zeros((blocks - 1, LANES, blocks * depth // COARSE))
    for boundary in range(blocks - 1):
        middle = (boundary + 1) * depth
        for cell in range(bands.shape[2]):
            for voxel in range(cell * COARSE, (cell + 1) * COARSE):
                for place in range(-R1, R1):
                    value = tap(taps, middle + place - voxel)
                    for row in range(rows):
                        bands[boundary, row * 2 * R1 + R1 + place, cell] += weights[row] * value
    return bands.reshape(-1, bands.shape[2])


def meeting_order(blocks):
    middle = blocks // 2
    return [*range(middle, blocks), *range(middle)]


def own_columns(count):
    products = (count + 2 * HALO) * COARSE + 2 * R2
    voxels = products + 2 * R1
    return -(-products // 16) * 16, -(-voxels // 8) * 8


def fold(voxels):
    return -(-voxels // 16) * 8


def rim_x_bands(count):
    products, voxels = own_columns(count)
    bands = np.zeros((2, products, -(-voxels // 16) * 16))
    valid = (count + 2 * HALO) * COARSE + 2 * R2
    for kind in range(2):
        for row in range(valid):
            bands[kind, row, row : row + 2 * R1 + 1] = grad_taps(kind)
    taps = smooth_taps(R2, sigma_tensor)
    coarse = np.zeros((16, products))
    for column in range(count + 2 * HALO):
        for voxel in range(column * COARSE, (column + 1) * COARSE):
            coarse[column, voxel : voxel + 2 * R2 + 1] += taps
    return halves(bands.reshape(2 * products, -1), 1), coarse


def depth_bands(depth):
    bands = np.zeros((2, depth, depth))
    for kind in range(2):
        for place in range(depth):
            for near in range(max(place - R1, 0), min(place + R1 + 1, depth)):
                bands[kind, near, place] = tap(grad_taps(kind), near - place)
    return bands


def product_weights(rows):
    return row_weights(rows, R2, sigma_tensor) / 255.0**2


def coarse_depth_bands(depth):
    taps = smooth_taps(R2, sigma_tensor)
    columns, cells = sizes(0, depth)
    bands = np.zeros((depth, LANES))
    for cell in range(cells):
        for voxel in range(COARSE):
            place = (cell - BEFORE) * COARSE + voxel
            for near in range(max(place - R2, 0), min(place + R2 + 1, depth)):
                bands[near, cell] += tap(taps, near - place)
    return bands


def coarse_x_bands(width):
    taps = smooth_taps(R2, sigma_tensor)
    places = product_rows(width)
    columns, cells = sizes(width, 0)
    bands = np.zeros((-(-columns // 16) * 16, len(places)))
    for column in range(columns):
        for voxel in range(COARSE):
            middle = (column - HALO) * COARSE + voxel
            for row, place in enumerate(places):
                if place is not None:
                    bands[column, row] += tap(taps, place - middle)
    return bands


def stacked(*pieces):
    widest = max(piece.shape[1] for piece in pieces)
    padded = [np.pad(piece, ((0, 0), (0, widest - piece.shape[1]))) for piece in pieces]
    starts = np.cumsum([0] + [len(piece) for piece in pieces])
    return jnp.asarray(as_bfloat16(np.concatenate(padded))), tuple(int(start) for start in starts)


def two_parts(values):
    high = values.astype(jnp.bfloat16).astype(jnp.float32)
    return jnp.concatenate([high, (values - high).astype(jnp.bfloat16).astype(jnp.float32)], axis=0)


def joined(parts):
    half = parts.shape[0] // 2
    return parts[:half] + parts[half:]


def coded(values):
    values = values * CODE_SCALE
    return (values * jnp.abs(values)) * (values * values)


def decoded(values):
    size = jnp.sqrt(jnp.sqrt(jnp.abs(values))) * (1.0 / CODE_SCALE)
    return jnp.where(values < 0.0, -size, size)


def column_rows(temp, cure, at_end):
    count = temp.shape[0]
    first, second = (count - GHOST, count - GHOST + 1) if at_end else (0, 0)
    pad = jnp.zeros((8 - COLUMN_ROWS, temp.shape[1]), jnp.float32)
    return jnp.concatenate(
        [temp[first : first + GHOST, :], cure[second : second + GHOST - 1, :], pad], axis=0
    )


def chunk_rows(count, lanes):
    products, voxels = own_columns(count)
    held = count + 2 * HALO + 1 + COLUMN_ROWS * (lanes // LANES)
    return voxels + fold(voxels), -(-held // 16) * 16


def is_odd():
    return lax.rem(lax.axis_index("plane"), 2) == 1


def pack_kernel(
    intensity, temp_hbm, cure_hbm, x_hbm, z_hbm, far, near, grey, x_parts, z_parts, temp, cure,
    sems,
):
    rows, width, depth = intensity.shape
    copies = [
        pltpu.make_async_copy(intensity, grey, sems.at[0]),
        pltpu.make_async_copy(temp_hbm, temp, sems.at[1]),
        pltpu.make_async_copy(cure_hbm, cure, sems.at[2]),
        pltpu.make_async_copy(x_hbm, x_parts, sems.at[3]),
        pltpu.make_async_copy(z_hbm, z_parts, sems.at[4]),
    ]
    for copy in copies:
        copy.start()
    for copy in copies[:3]:
        copy.wait()
    odd = is_odd()
    sides = [
        two_parts(column_rows(temp, cure, at_end)).astype(jnp.bfloat16)
        for at_end in (False, True)
    ]

    def send(left, right):
        for place, target, columns in ((0, left, sides[0]), (width - EDGE, right, sides[1])):
            for pair in range(rows // 2):
                two = [grey[2 * pair + i, place : place + EDGE, :] for i in range(2)]
                two = jnp.concatenate(two, axis=0).astype(jnp.float32)
                target[2 * EDGE * pair : 2 * EDGE * (pair + 1), :] = two.astype(jnp.bfloat16)
            for slot in range(temp.shape[1] // LANES):
                at = rows * EDGE + 16 * slot
                target[at : at + 16, :] = columns[:, slot * LANES : (slot + 1) * LANES]

    @pl.when(odd)
    def _():
        send(near, far)

    @pl.when(jnp.logical_not(odd))
    def _():
        send(far, near)

    for copy in copies[3:]:
        copy.wait()


def packed_rows(values, size, first):
    depth = values[0].shape[1]
    lane = lax.broadcasted_iota(jnp.int32, values[0].shape, 1)
    packed = None
    for block, value in enumerate(values):
        shift = (size * block - first) % depth
        moved = value if shift == 0 else pltpu.roll(value, shift, 1)
        packed = moved if block == 0 else jnp.where(lane >= size * block, moved, packed)
    return packed


def edges_of(ref, rows):
    two = [
        ref[2 * EDGE * pair : 2 * EDGE * (pair + 1), :].astype(jnp.float32)
        for pair in range(rows // 2)
    ]
    voxels = [two[row // 2][row % 2 * EDGE : (row % 2 + 1) * EDGE] for row in range(rows)]
    slots = range(rows * EDGE, ref.shape[0], 16)
    columns = [joined(ref[at : at + 16, :].astype(jnp.float32)) for at in slots]
    return voxels, jnp.concatenate(columns, axis=1)


def product(first, second):
    return jnp.dot(first, second, preferred_element_type=jnp.float32)


def mirrored_filter(kind, values, even):
    rows = len(values)
    use_sum = even == (kind == 0)
    sign = 1.0 if use_sum else -1.0
    half = [values[row] + sign * values[rows - 1 - row] for row in range(rows // 2)]
    results = []
    for row in range(rows // 2):
        total = None
        for source, value in enumerate(half):
            near = tap(grad_taps(kind), source - row)
            far = tap(grad_taps(kind), rows - 1 - source - row)
            weight = 0.5 * (near + sign * far)
            total = weight * value if total is None else total + weight * value
        results.append(total)
    return results


def weighted_products(three, weight):
    pairs = ((0, 0), (1, 1), (2, 2), (0, 1), (0, 2), (1, 2))
    first = [weight * value for value in three]
    return [first[a] * three[b] for a, b in pairs]


def late_mask(count, width):
    row = lax.broadcasted_iota(jnp.int32, (count, LANES), 0)
    left = max(width - 2 * R1 - EARLY, 0)
    place = jnp.where(row < left + EDGE, row - left + R1 - EDGE, row - left - EDGE + width - R1)
    place = place + lax.axis_index("plane") * width
    inside = (place >= 0) & (place < lax.axis_size("plane") * width)
    return jnp.where(inside | (row < left), 1.0, 0.0)


USED = (0, 1, 2, 5)
UNUSED = (3, 4)


def all_sums(products, coarse, sx):
    sums = [None] * 6
    for kinds in (USED, UNUSED):
        tiles = [tile for index in kinds for tile in products[index]]
        along = product(sx, jnp.concatenate(tiles, axis=1)).astype(jnp.bfloat16)
        step = along.shape[1] // len(kinds)
        parts = [along[:, index * step : (index + 1) * step] for index in range(len(kinds))]
        total = product(jnp.concatenate(parts, axis=0), coarse)
        high = sx.shape[0]
        for index, kind in enumerate(kinds):
            sums[kind] = total[index * high : (index + 1) * high]
    return sums


def tensor_sums(across, sx, mask, diagonal, z_parts, filtered, grads):
    double = diagonal.shape[1]
    depth, pairs = double // 2, across.shape[1] // double
    rows, count = 2 * pairs, across.shape[0] // 2
    for start in range(0, count, 16):
        kinds = [
            [
                across[kind * count + start : kind * count + start + 16, row * depth : (row + 1) * depth]
                for row in range(rows)
            ]
            for kind in range(2)
        ]
        for part in range(3):
            values = kinds[X_KINDS[part]]
            results = mirrored_filter(ROW_KINDS[part], values, True)
            results += mirrored_filter(ROW_KINDS[part], values, False)
            for row, result in enumerate(results):
                at = (part * pairs + row // 2) * count + start
                lanes = slice((row % 2) * depth, (row % 2 + 1) * depth)
                high = result.astype(jnp.bfloat16)
                filtered[0, at : at + 16, lanes] = high
                low = result - high.astype(jnp.float32)
                filtered[1, at : at + 16, lanes] = low.astype(jnp.bfloat16)

    at = 2 * pairs * count
    for kind, part in enumerate((slice(0, at), slice(at, filtered.shape[1]))):
        high, low = filtered[0, part, :], filtered[1, part, :]
        high_bands = diagonal[2 * kind * double : (2 * kind + 1) * double, :]
        low_bands = diagonal[(2 * kind + 1) * double : 2 * (kind + 1) * double, :]
        grads[part, :] = product(
            jnp.concatenate([high, low, high], axis=1),
            jnp.concatenate([high_bands, high_bands, low_bands], axis=0),
        )

    weights = product_weights(rows)
    layer = lax.axis_index("depth")
    first, last = layer == 0, layer == lax.axis_size("depth") - 1
    place = lax.broadcasted_iota(jnp.int32, (16, depth), 1)
    complete = ((place >= R1) | first) & ((place < depth - R1) | last)
    complete = jnp.where(complete, 1.0, 0.0)
    groups = [[] for _ in range(6)]
    for start in range(0, count, 16):
        inside = complete if mask is None else complete * mask[start : start + 16]
        totals = None
        for row in range(rows):
            lanes = slice((row % 2) * depth, (row % 2 + 1) * depth)
            three = []
            for part in range(3):
                at = (part * pairs + row // 2) * count + start
                three.append(grads[at : at + 16, lanes])
            terms = weighted_products(three, 2.0 * float(weights[row % (rows // 2)]))
            totals = terms if row == 0 else [a + b for a, b in zip(totals, terms)]
        for index in range(6):
            groups[index].append((totals[index] * inside).astype(jnp.bfloat16))
    products = [[jnp.concatenate(group, axis=0)] for group in groups]
    return all_sums(products, z_parts[2 * double : 2 * double + depth, :], sx)


def rim_tiles(values):
    rows, depth = len(values), values[0].shape[1]
    below = packed_rows(values, RIM, depth - RIM)
    above = pltpu.roll(packed_rows(values, RIM, 0), rows * RIM, 1)
    lane = lax.broadcasted_iota(jnp.int32, below.shape, 1)
    return [jnp.where(lane < rows * RIM, below, above), above, pltpu.roll(above, HALF, 1)]


def early_kernel(
    starts, grey, x_parts, z_parts, sums, diagonal, sides, tiles, across, filtered, grads
):
    rows, width, depth = grey.shape
    double = 2 * depth
    empty = jnp.zeros((depth, depth), jnp.bfloat16)
    for part in range(4):
        for half in range(2):
            at = pl.ds(part * double + half * depth, depth)
            band = z_parts[part * depth : (part + 1) * depth, :]
            diagonal[at, half * depth : (half + 1) * depth] = band
            diagonal[at, (1 - half) * depth : (2 - half) * depth] = empty
    values = [grey[row].astype(jnp.float32) for row in range(rows)]
    whole = jnp.concatenate([value.astype(jnp.bfloat16) for value in values], axis=1)
    twice = jnp.concatenate([whole, whole], axis=0)
    result = product(x_parts[starts[0] : starts[2], : 2 * width], twice)
    across[...] = result[: starts[1]]
    sides[...] = result[starts[1] :]
    sx = x_parts[starts[2] : starts[3], :EARLY]
    results = tensor_sums(across, sx, None, diagonal, z_parts, filtered, grads)
    for index, kind in enumerate(USED):
        sums[index] = results[kind]
    for index, tile in enumerate(rim_tiles(values)):
        tiles[index] = tile


def late_kernel(
    starts, width, far, near, x_late, z_parts, diagonal, early_sums, sides, own_tiles, temp, cure,
    out_hbm, across, filtered, grads, out, sems,
):
    double = diagonal.shape[1]
    depth = double // 2
    rows = across.shape[1] // depth
    count, lanes = temp.shape
    odd = is_odd()
    depths, layer = lax.axis_size("depth"), lax.axis_index("depth")
    outer, outer_columns = edges_of(far, rows)
    inner, inner_columns = edges_of(near, rows)
    values = []
    for row in range(rows):
        left = jnp.where(odd, inner[row], outer[row])
        right = jnp.where(odd, outer[row], inner[row])
        values.append(jnp.concatenate([left, right], axis=0))
    left = jnp.where(odd, inner_columns, outer_columns)
    right = jnp.where(odd, outer_columns, inner_columns)

    late = across.shape[0] // 2
    halos = jnp.concatenate([value.astype(jnp.bfloat16) for value in values], axis=1)
    halos = jnp.concatenate([halos, halos], axis=0)
    across[...] = sides[...] + product(x_late[starts[0] : starts[1], : 4 * EDGE], halos)

    products_x, voxels = own_columns(count)
    folded, stride = fold(voxels), COARSE * count
    tiles = [
        jnp.concatenate([tile[:EDGE], own_tiles[index], tile[EDGE:]], axis=0)
        for index, tile in enumerate(rim_tiles(values))
    ]
    missing = stride * (depths - 1) + voxels - tiles[0].shape[0]
    if missing > 0:
        spare = jnp.zeros((-(-missing // 8) * 8, LANES), jnp.float32)
        tiles = [jnp.concatenate([tile, spare], axis=0) for tile in tiles]

    height = count + 2 * HALO
    half_lane = lax.broadcasted_iota(jnp.int32, (folded, LANES), 1) < HALF
    order = meeting_order(out.shape[0])
    for position, target in enumerate(order):
        at = stride * target
        second = jnp.where(
            half_lane,
            tiles[1][at : at + folded],
            tiles[2][at + voxels - folded : at + voxels],
        )
        rims = jnp.concatenate([tiles[0][at : at + voxels], second], axis=0)
        out[position, 0 : voxels + folded, :] = rims.astype(jnp.bfloat16)
    split = (pl.ds(0, voxels + folded), pl.ds(voxels + folded, out.shape[1] - voxels - folded))
    copies = [
        pltpu.make_async_copy(out.at[:, part, :], out_hbm.at[:, part, :], sems.at[index])
        for index, part in enumerate(split)
    ]
    copies[0].start()

    sx = x_late[starts[1] : starts[2], :late]
    results = tensor_sums(
        across, sx, late_mask(late, width), diagonal, z_parts, filtered, grads
    )
    yy, xx, zz, xz = [early_sums[index] + results[kind] for index, kind in enumerate(USED)]
    lane = lax.broadcasted_iota(jnp.int32, yy.shape, 1)
    columns, cells = sizes(width, depth)
    tail = 4 * cells - LANES
    joint = pltpu.roll(xz, 3 * cells, 1)
    rest = jnp.where(lane < tail, joint, 0.0)
    rest = pltpu.roll(rest, 0, 1, stride=tail, stride_axis=0)
    for index, part in ((2, zz), (1, xx), (0, yy)):
        moved = part if index == 0 else pltpu.roll(part, index * cells, 1)
        joint = jnp.where(lane < (index + 1) * cells, moved, joint)

    own_first, own_last = column_rows(temp, cure, False), column_rows(temp, cure, True)
    half = chunk_rows(count, lanes)[1]
    for position, target in enumerate(order):
        piece = jnp.where(layer == target - 1, own_last, 0.0)
        piece = jnp.where(layer == target + 1, own_first, piece)
        if target == 0:
            piece = jnp.where(layer == depths - 1, left, piece)
        if target == out.shape[0] - 1:
            piece = jnp.where(layer == 0, right, piece)
        mine = slice(count * target, count * target + height)
        pieces = [coded(joint[mine]), coded(jnp.sum(rest[mine], axis=0, keepdims=True))]
        for slot in range(lanes // LANES):
            part = piece[:, slot * LANES : (slot + 1) * LANES]
            pieces += [part[:GHOST] - reference_temp, part[GHOST:COLUMN_ROWS]]
        filled = sum(part.shape[0] for part in pieces)
        if filled < half:
            pieces.append(jnp.zeros((half - filled, LANES), jnp.float32))
        out[position, voxels + folded :, :] = jnp.concatenate(pieces, axis=0).astype(jnp.bfloat16)
    copies[1].start()
    for copy in copies:
        copy.wait()


def rim_sums(chunks, count, starts, flat, steep, cells):
    parts = chunks.shape[0]
    rows_x, voxels = own_columns(count)
    folded = fold(voxels)
    tall = -(-voxels // 16) * 16
    spare = [jnp.zeros((tall - voxels, LANES), jnp.float32)] if tall > voxels else []
    lane = lax.broadcasted_iota(jnp.int32, (voxels, LANES), 1)
    order = meeting_order(parts)
    rims = [
        chunks[order.index(part), 0 : voxels + folded, :].astype(jnp.float32)
        for part in range(parts)
    ]
    tiles = []
    for below, above in zip(rims[:-1], rims[1:]):
        first = jnp.where(lane < ROWS * RIM, below[:voxels], above[:voxels])
        second = above[voxels:]
        second = [second[: voxels - folded], pltpu.roll(second, HALF, 1)]
        for tile in ([first], second):
            tiles.append(jnp.concatenate(tile + spare, axis=0).astype(jnp.bfloat16))
    wide = jnp.concatenate(tiles, axis=1)
    result = product(
        steep[starts[1] : starts[2], : 2 * tall], jnp.concatenate([wide, wide], axis=0)
    ).astype(jnp.bfloat16)
    kinds = []
    for kind in range(2):
        values = result[kind * rows_x : (kind + 1) * rows_x]
        stack = [
            values[:, 2 * part * LANES : 2 * (part + 1) * LANES] for part in range(parts - 1)
        ]
        stack = jnp.concatenate(stack, axis=0)
        kinds.append(jnp.concatenate([stack, stack], axis=1))
    both = product(kinds[0], flat[...])
    three = (both[:, :LANES], product(kinds[1], steep[starts[0] : starts[1], :LANES]), both[:, LANES:])

    index = lax.axis_index("plane") * lax.axis_size("depth") + lax.axis_index("depth")
    total = lax.axis_size("plane") * lax.axis_size("depth") * count * COARSE
    place = lax.rem(lax.broadcasted_iota(jnp.int32, three[0].shape, 0), rows_x)
    place = place + (index * count - HALO) * COARSE - R2
    inside = jnp.where((place >= 0) & (place < total), 1.0, 0.0)
    products = [
        [
            term[part * rows_x : (part + 1) * rows_x].astype(jnp.bfloat16)
            for part in range(parts - 1)
        ]
        for term in weighted_products(three, inside)
    ]
    return all_sums(products, cells[...], steep[starts[2] : starts[3], :rows_x])


def cure_kernel(
    cells, starts, chunks, temp_in, cure_in, tools, flat, steep, rim_bands, temp_hbm, cure_hbm,
    conduct_hbm, temp_out, cure_out, conduct_out, sems,
):
    count, lanes = temp_in.shape
    parts = chunks.shape[0]
    planes, depths = lax.axis_size("plane"), lax.axis_size("depth")
    plane, layer = lax.axis_index("plane"), lax.axis_index("depth")
    height = count + 2 * HALO
    own = cells - BEFORE - AFTER
    lane = lax.broadcasted_iota(jnp.int32, (16, lanes), 1)
    row = lax.broadcasted_iota(jnp.int32, (16, lanes), 0)
    at_sums, half = chunk_rows(count, lanes)
    tail = 4 * cells - LANES
    narrow_lane = lax.broadcasted_iota(jnp.int32, (16, LANES), 1)
    order = meeting_order(parts)

    near = rim_sums(chunks, count, starts, flat, steep, rim_bands)
    sums = [near[kind] for kind in USED]
    blocks = [chunks[order.index(part), at_sums:, :].astype(jnp.float32) for part in range(parts)]
    columns = [
        jnp.concatenate(
            [
                block[at : at + COLUMN_ROWS]
                for at in range(
                    height + 1, height + 1 + COLUMN_ROWS * (lanes // LANES), COLUMN_ROWS
                )
            ],
            axis=1,
        )
        for block in blocks
    ]
    blocks = [decoded(block[0:16]) for block in blocks]
    tails = [block[height : height + 1] for block in blocks]
    if parts % 8:
        tails.append(jnp.zeros((-parts % 8, LANES), jnp.float32))
    tails = jnp.concatenate(tails, axis=0)
    tails = pltpu.roll(tails, lax.rem(LANES - lax.rem(tail * count * layer, LANES), LANES), 1)
    narrow_row = lax.broadcasted_iota(jnp.int32, (16, LANES), 0)
    rests = [jnp.zeros((16, LANES), jnp.float32) for _ in range(parts)]
    for column in range(height):
        moved = pltpu.roll(tails, LANES - tail * column, 1) if column else tails
        for part in range(parts):
            rests[part] = jnp.where(narrow_row == column, moved[part : part + 1], rests[part])
    for part in range(parts):
        first_cell = own * part - BEFORE
        here = (lane >= first_cell) & (lane < first_cell + cells)
        values = blocks[part]
        joint = values[0:16]
        xz = pltpu.roll(jnp.where(narrow_lane < tail, rests[part], joint), LANES - 3 * cells, 1)
        for index in range(4):
            chunk = xz if index == 3 else joint
            if lanes > LANES:
                spare = jnp.zeros((16, lanes - LANES), jnp.float32)
                chunk = jnp.concatenate([chunk, spare], axis=1)
            shift = (first_cell - (index % 3) * cells) % lanes
            moved = chunk if shift == 0 else pltpu.roll(chunk, shift, 1)
            sums[index] = sums[index] + jnp.where(here, moved, 0.0)
    trace = sums[0] + sums[1] + sums[2]
    scale = (conduct_fiber - conduct_matrix) / (2.0 * trace + tensor_eps)
    conduct = [
        conduct_matrix + scale * (trace - sums[1]),
        -scale * sums[3],
        conduct_matrix + scale * (trace - sums[2]),
    ]
    for kind in range(3):
        conduct_out[kind] = conduct[kind][HALO : HALO + count]
    copies = [
        pltpu.make_async_copy(conduct_out, conduct_hbm, sems.at[0]),
        pltpu.make_async_copy(temp_out, temp_hbm, sems.at[1]),
        pltpu.make_async_copy(cure_out, cure_hbm, sems.at[2]),
    ]
    copies[0].start()

    before, after = columns[parts - 1], columns[0]
    for part in range(parts - 1):
        before = jnp.where(layer == part + 1, columns[part], before)
        after = jnp.where(layer == part, columns[part + 1], after)
    spare = jnp.full((16 - count - 2 * GHOST, lanes), 0.5, jnp.float32)
    temp = jnp.concatenate([
            before[:GHOST] + reference_temp,
            temp_in[...],
            after[:GHOST] + reference_temp,
            8.0 * spare,
        ], axis=0)
    cure = jnp.concatenate([spare[:1], before[GHOST:], cure_in[...], after[GHOST:], spare[:1], spare], axis=0)
    gap = GHOST - HALO
    xx, xz, zz = [pltpu.roll(part, gap, 0) for part in conduct]

    first = (plane == 0) & (layer == 0)
    last = (plane == planes - 1) & (layer == depths - 1)
    for step in range(STEPS):
        top, bottom = tools[2 * step : 2 * step + 1, :], tools[2 * step + 1 : 2 * step + 2, :]
        temp = jnp.where((row < GHOST) & first, temp[GHOST : GHOST + 1], temp)
        temp = jnp.where(
            (row >= GHOST + count) & last, temp[GHOST + count - 1 : GHOST + count], temp
        )
        cooler = jnp.where(lane == 0, top, pltpu.roll(temp, 1, 1))
        later = jnp.where(lane == lanes - 1, bottom, pltpu.roll(temp, lanes - 1, 1))
        slant = later - cooler
        second_x = pltpu.roll(temp, 15, 0) - 2.0 * temp + pltpu.roll(temp, 1, 0)
        second_z = later - 2.0 * temp + cooler
        cross = 0.25 * (pltpu.roll(slant, 15, 0) - pltpu.roll(slant, 1, 0))
        spread = xx * second_x + 2.0 * xz * cross + zz * second_z
        inverse = 1.0 / reference_temp - 1.0 / temp
        left = 1.0 - cure
        rate = rate_first * jnp.exp(energy_first * inverse) + rate_second * jnp.exp(
            energy_second * inverse
        ) * jnp.sqrt(cure)
        rate = rate * (left * jnp.sqrt(left))
        temp = temp + time_step * (spread + heat_release * rate)
        cure = cure + time_step * rate
    temp_out[...] = temp[GHOST : GHOST + count]
    cure_out[...] = cure[GHOST : GHOST + count]
    for copy in copies[1:]:
        copy.start()
    for copy in copies:
        copy.wait()


def on_device(intensity, temp_start, cure_start, tool_levels, plan):
    rows, width, depth = intensity.shape
    count, lanes = temp_start.shape
    planes, depths = lax.axis_size("plane"), lax.axis_size("depth")
    columns, cells = sizes(width, depth)
    bf16 = jnp.bfloat16
    slots = rows * EDGE + 16 * (lanes // LANES)
    params = pltpu.CompilerParams(vmem_limit_bytes=24 * 1024 * 1024)
    vmem = pl.BlockSpec(memory_space=pltpu.VMEM)
    stay = pl.BlockSpec(memory_space=pltpu.HBM)

    fixed = lambda values: pltpu.with_memory_space_constraint(values, pltpu.HBM)
    bands, coarse = x_bands(width), coarse_x_bands(width)
    late = bands.shape[1] - EARLY
    middle = bands[:, :EARLY, EDGE : EDGE + width]
    sides = bands[:, EARLY:].reshape(2 * late, -1)
    x_hbm, early_starts = stacked(
        halves(middle.reshape(2 * EARLY, -1), 1),
        halves(sides[:, EDGE : EDGE + width], 1),
        coarse[:, :EARLY],
    )
    z_hbm, _ = stacked(
        *[halves(bands, 0) for bands in depth_bands(depth)], coarse_depth_bands(depth)
    )
    halos = np.concatenate([sides[:, :EDGE], sides[:, EDGE + width :]], axis=1)
    x_late, late_starts = stacked(halves(halos, 1), coarse[:, EARLY:])
    rims = rim_bands(rows)
    flat, _ = stacked(halves(np.concatenate([rims[0], rims[2]], axis=1), 0))
    steep, rim_starts = stacked(halves(rims[1], 0), *rim_x_bands(count))
    cell_bands, _ = stacked(rim_cells(rows, depth, depths))
    far, near, grey, x_parts, z_parts, temp, cure = pl.pallas_call(
        pack_kernel,
        name="pack",
        out_shape=(
            pltpu.VMEM((slots, depth), bf16),
            pltpu.VMEM((slots, depth), bf16),
            pltpu.VMEM((rows, width, depth), jnp.int32),
            pltpu.VMEM(x_hbm.shape, bf16),
            pltpu.VMEM(z_hbm.shape, bf16),
            pltpu.VMEM((count, lanes), jnp.float32),
            pltpu.VMEM((count, lanes), jnp.float32),
        ),
        in_specs=[stay] * 5,
        scratch_shapes=[
            pltpu.SemaphoreType.DMA((5,)),
        ],
        compiler_params=params,
    )(*[fixed(values) for values in (intensity, temp_start, cure_start, x_hbm, z_hbm)])

    def moved(values, pairs):
        index = [(p * depths + d, q * depths + e) for (p, d), (q, e) in pairs]
        return lax.ppermute(values, ("plane", "depth"), index)

    def swapped(values, first):
        pairs = [(p, p + 1) for p in range(first, planes - 1, 2)]
        pairs += [(q, p) for p, q in pairs]
        return moved(values, [((p, d), (q, d)) for p, q in pairs for d in range(depths)])

    far = swapped(far, 1)
    near = swapped(near, 0)

    high = coarse.shape[0]

    def scratch(count):
        return [
            pltpu.VMEM((2 * count, rows * depth), jnp.float32),
            pltpu.VMEM((2, 3 * rows // 2 * count, 2 * depth), bf16),
            pltpu.VMEM((3 * rows // 2 * count, 2 * depth), jnp.float32),
        ]

    def cost(count):
        return pl.CostEstimate(
            flops=2 * rows * (2 * count) * 160 * depth * 4,
            bytes_accessed=4_000_000,
            transcendentals=0,
        )

    early_sums, diagonal, sides, own_tiles = pl.pallas_call(
        functools.partial(early_kernel, early_starts),
        name="early",
        out_shape=(
            pltpu.VMEM((len(USED), high, LANES), jnp.float32),
            pltpu.VMEM((8 * depth, 2 * depth), bf16),
            pltpu.VMEM((2 * late, rows * depth), jnp.float32),
            pltpu.VMEM((3, width, LANES), jnp.float32),
        ),
        scratch_shapes=scratch(EARLY),
        cost_estimate=cost(EARLY),
        compiler_params=params,
    )(grey, x_parts, z_parts)

    products_x, voxels = own_columns(count)
    at_sums, half = chunk_rows(count, lanes)
    chunk_shape = (depths, at_sums + half, LANES)
    chunks = pl.pallas_call(
        functools.partial(late_kernel, late_starts, width),
        name="late",
        out_shape=pltpu.HBM(chunk_shape, bf16),
        in_specs=[vmem] * 10,
        out_specs=stay,
        scratch_shapes=scratch(late)
        + [pltpu.VMEM(chunk_shape, bf16), pltpu.SemaphoreType.DMA((2,))],
        cost_estimate=cost(late),
        compiler_params=params,
    )(far, near, x_late, z_parts, diagonal, early_sums, sides, own_tiles, temp, cure)

    faces = plan.reshape(2 * STEPS, 1) == jnp.arange(tool_levels.shape[0], dtype=jnp.int32)
    tools = jnp.sum(
        jnp.where(faces, tool_levels, jnp.zeros_like(tool_levels)), axis=1, keepdims=True
    )

    chunks = lax.all_to_all(
        chunks,
        "depth",
        split_axis=0,
        concat_axis=0,
        tiled=True,
        axis_index_groups=[meeting_order(depths)],
    )

    return pl.pallas_call(
        functools.partial(cure_kernel, cells, rim_starts),
        name="cure",
        out_shape=(
            pltpu.HBM((count, lanes), jnp.float32),
            pltpu.HBM((count, lanes), jnp.float32),
            pltpu.HBM((3, count, lanes), jnp.float32),
        ),
        in_specs=[vmem] * 7,
        out_specs=(stay, stay, stay),
        scratch_shapes=[
            pltpu.VMEM((count, lanes), jnp.float32),
            pltpu.VMEM((count, lanes), jnp.float32),
            pltpu.VMEM((3, count, lanes), jnp.float32),
            pltpu.SemaphoreType.DMA((3,)),
        ],
        compiler_params=params,
    )(chunks, temp, cure, tools, flat, steep, cell_bands)


def solution(mesh):
    return jax.shard_map(
        on_device,
        mesh=mesh,
        in_specs=(
            P(None, "plane", "depth"),
            P(("plane", "depth"), None),
            P(("plane", "depth"), None),
            P(),
            P(),
        ),
        out_specs=(
            P(("plane", "depth"), None),
            P(("plane", "depth"), None),
            P(None, ("plane", "depth"), None),
        ),
        check_vma=False,
    )
```

```python
import functools

import jax
import jax.numpy as jnp
import ml_dtypes
import numpy as np
from jax import lax
from jax.experimental import pallas as pl
from jax.experimental.pallas import tpu as pltpu
from jax.sharding import PartitionSpec as P

ROWS = 8
R1 = 6
R2 = 10
COARSE = 4
STEPS = 3

sigma_grad = 2.0
sigma_tensor = 3.3
conduct_matrix = 0.3
conduct_fiber = 1.5
time_step = 0.25
heat_release = 0.4
rate_first = 0.15
rate_second = 0.6
energy_first = 30.0
energy_second = 25.0
reference_temp = 4.2
tensor_eps = 1e-06

LANES = 128
HALO = 2
EDGE = HALO * COARSE + R1 + R2
EARLY = 96
GHOST = 3
COLUMN_ROWS = 2 * GHOST - 1
CODE_SCALE = 2.0**20
RIM = 2 * R1
BEFORE = -(-(R2 - R1) // COARSE)
AFTER = BEFORE
HALF = LANES // 2
ROW_KINDS = (1, 0, 0)
X_KINDS = (0, 1, 0)
DEPTH_KINDS = (0, 0, 1)


def smooth_taps(radius, sigma):
    offsets = np.arange(-radius, radius + 1) * 1.0
    weights = np.exp(-0.5 * offsets * offsets / (sigma * sigma))
    return weights / weights.sum()


def slope_taps(radius, sigma):
    offsets = np.arange(-radius, radius + 1) * 1.0
    weights = np.exp(-0.5 * offsets * offsets / (sigma * sigma))
    return offsets * weights / np.sum(offsets * offsets * weights)


def row_weights(count, radius, sigma):
    taps = smooth_taps(radius, sigma)
    result = np.zeros(count)
    for source in range(count):
        for target in range(count):
            offset = target - source
            if abs(offset) <= radius:
                result[source] += taps[offset + radius]
    return result


def as_bfloat16(matrix):
    return matrix.astype(np.float32).astype(ml_dtypes.bfloat16)


def halves(matrix, axis):
    high = as_bfloat16(matrix).astype(np.float64)
    return np.concatenate([high, as_bfloat16(matrix - high).astype(np.float64)], axis=axis)


def sizes(width, depth):
    columns = width // COARSE + 2 * HALO
    cells = depth // COARSE + BEFORE + AFTER
    return columns, cells


def product_rows(width):
    places = [*range(R1, width - R1)]
    places += [None] * max(EARLY - len(places), 0)
    places += [*range(R1 - EDGE, R1), *range(width - R1, width + EDGE - R1)]
    return places + [None] * (-len(places) % 16)


def grad_taps(kind):
    return slope_taps(R1, sigma_grad) if kind else smooth_taps(R1, sigma_grad)


def rounded(taps):
    best = None
    for factor in np.linspace(1.0, 2.0, 20001)[:-1]:
        near = as_bfloat16(taps * factor).astype(np.float64)
        error = np.abs(near / factor - taps).sum()
        if best is None or error < best[0]:
            best = (error, near, factor)
    return best[1], best[2]


DEPTH_TAPS = tuple(rounded(grad_taps(kind)) for kind in range(2))


def tap(taps, offset):
    radius = (len(taps) - 1) // 2
    return float(taps[offset + radius]) if abs(offset) <= radius else 0.0


def x_bands(width):
    places = product_rows(width)
    bands = np.zeros((2, len(places), width + 2 * EDGE))
    for kind in range(2):
        for row, place in enumerate(places):
            if place is not None:
                first = place + EDGE - R1
                bands[kind, row, first : first + 2 * R1 + 1] = grad_taps(kind)
    return bands


def rim_bands(rows):
    bands = np.zeros((3, 2 * LANES, LANES))
    for part in range(3):
        row_taps, depth_taps = grad_taps(ROW_KINDS[part]), grad_taps(DEPTH_KINDS[part])
        for source in range(rows):
            for target in range(rows):
                row_tap = tap(row_taps, source - target)
                for near in range(-RIM, RIM):
                    lane = source * RIM + near % RIM
                    if near >= 0:
                        lane += rows * RIM
                    for place in range(-R1, R1):
                        value = row_tap * tap(depth_taps, near - place)
                        bands[part, lane, target * 2 * R1 + R1 + place] = value
    return bands


def rim_cells(rows, depth, blocks):
    taps = smooth_taps(R2, sigma_tensor)
    weights = product_weights(rows)
    bands = np.zeros((blocks - 1, LANES, blocks * depth // COARSE))
    for boundary in range(blocks - 1):
        middle = (boundary + 1) * depth
        for cell in range(bands.shape[2]):
            for voxel in range(cell * COARSE, (cell + 1) * COARSE):
                for place in range(-R1, R1):
                    value = tap(taps, middle + place - voxel)
                    for row in range(rows):
                        bands[boundary, row * 2 * R1 + R1 + place, cell] += weights[row] * value
    return bands.reshape(-1, bands.shape[2])


def meeting_order(blocks):
    middle = blocks // 2
    return [*range(middle, blocks), *range(middle)]


def own_columns(count):
    products = (count + 2 * HALO) * COARSE + 2 * R2
    voxels = products + 2 * R1
    return -(-products // 16) * 16, -(-voxels // 8) * 8


def fold(voxels):
    return -(-voxels // 16) * 8


def rim_x_bands(count):
    products, voxels = own_columns(count)
    bands = np.zeros((2, products, -(-voxels // 16) * 16))
    valid = (count + 2 * HALO) * COARSE + 2 * R2
    for kind in range(2):
        for row in range(valid):
            bands[kind, row, row : row + 2 * R1 + 1] = grad_taps(kind)
    taps = smooth_taps(R2, sigma_tensor)
    coarse = np.zeros((16, products))
    for column in range(count + 2 * HALO):
        for voxel in range(column * COARSE, (column + 1) * COARSE):
            coarse[column, voxel : voxel + 2 * R2 + 1] += taps
    return halves(bands.reshape(2 * products, -1), 1), coarse


def depth_bands(depth):
    bands = np.zeros((2, depth, depth))
    for kind in range(2):
        for place in range(depth):
            for near in range(max(place - R1, 0), min(place + R1 + 1, depth)):
                bands[kind, near, place] = tap(DEPTH_TAPS[kind][0], near - place)
    return bands


def product_weights(rows):
    return row_weights(rows, R2, sigma_tensor) / 255.0**2


def coarse_depth_bands(depth):
    taps = smooth_taps(R2, sigma_tensor)
    columns, cells = sizes(0, depth)
    bands = np.zeros((depth, LANES))
    for cell in range(cells):
        for voxel in range(COARSE):
            place = (cell - BEFORE) * COARSE + voxel
            for near in range(max(place - R2, 0), min(place + R2 + 1, depth)):
                bands[near, cell] += tap(taps, near - place)
    return bands


def coarse_x_bands(width):
    taps = smooth_taps(R2, sigma_tensor)
    places = product_rows(width)
    columns, cells = sizes(width, 0)
    bands = np.zeros((-(-columns // 16) * 16, len(places)))
    for column in range(columns):
        for voxel in range(COARSE):
            middle = (column - HALO) * COARSE + voxel
            for row, place in enumerate(places):
                if place is not None:
                    bands[column, row] += tap(taps, place - middle)
    return bands


def stacked(*pieces):
    widest = max(piece.shape[1] for piece in pieces)
    padded = [np.pad(piece, ((0, 0), (0, widest - piece.shape[1]))) for piece in pieces]
    starts = np.cumsum([0] + [len(piece) for piece in pieces])
    return jnp.asarray(as_bfloat16(np.concatenate(padded))), tuple(int(start) for start in starts)


def two_parts(values):
    high = values.astype(jnp.bfloat16).astype(jnp.float32)
    return jnp.concatenate([high, (values - high).astype(jnp.bfloat16).astype(jnp.float32)], axis=0)


def joined(parts):
    half = parts.shape[0] // 2
    return parts[:half] + parts[half:]


def coded(values):
    values = values * CODE_SCALE
    return (values * jnp.abs(values)) * (values * values)


def decoded(values):
    size = jnp.sqrt(jnp.sqrt(jnp.abs(values))) * (1.0 / CODE_SCALE)
    return jnp.where(values < 0.0, -size, size)


def column_rows(temp, cure, at_end):
    count = temp.shape[0]
    first, second = (count - GHOST, count - GHOST + 1) if at_end else (0, 0)
    pad = jnp.zeros((8 - COLUMN_ROWS, temp.shape[1]), jnp.float32)
    return jnp.concatenate(
        [temp[first : first + GHOST, :], cure[second : second + GHOST - 1, :], pad], axis=0
    )


def chunk_rows(count, lanes):
    products, voxels = own_columns(count)
    held = count + 2 * HALO + 1 + COLUMN_ROWS * (lanes // LANES)
    return voxels + fold(voxels), -(-held // 16) * 16


def is_odd():
    return lax.rem(lax.axis_index("plane"), 2) == 1


def pack_kernel(
    intensity, temp_hbm, cure_hbm, x_hbm, z_hbm, far, near, grey, x_parts, z_parts, temp, cure,
    sems,
):
    rows, width, depth = intensity.shape
    copies = [
        pltpu.make_async_copy(intensity, grey, sems.at[0]),
        pltpu.make_async_copy(temp_hbm, temp, sems.at[1]),
        pltpu.make_async_copy(cure_hbm, cure, sems.at[2]),
        pltpu.make_async_copy(x_hbm, x_parts, sems.at[3]),
        pltpu.make_async_copy(z_hbm, z_parts, sems.at[4]),
    ]
    for copy in copies:
        copy.start()
    for copy in copies[:3]:
        copy.wait()
    odd = is_odd()
    sides = [
        two_parts(column_rows(temp, cure, at_end)).astype(jnp.bfloat16)
        for at_end in (False, True)
    ]

    def send(left, right):
        for place, target, columns in ((0, left, sides[0]), (width - EDGE, right, sides[1])):
            for pair in range(rows // 2):
                two = [grey[2 * pair + i, place : place + EDGE, :] for i in range(2)]
                two = jnp.concatenate(two, axis=0).astype(jnp.float32)
                target[2 * EDGE * pair : 2 * EDGE * (pair + 1), :] = two.astype(jnp.bfloat16)
            for slot in range(temp.shape[1] // LANES):
                at = rows * EDGE + 16 * slot
                target[at : at + 16, :] = columns[:, slot * LANES : (slot + 1) * LANES]

    @pl.when(odd)
    def _():
        send(near, far)

    @pl.when(jnp.logical_not(odd))
    def _():
        send(far, near)

    for copy in copies[3:]:
        copy.wait()


def packed_rows(values, size, first):
    depth = values[0].shape[1]
    lane = lax.broadcasted_iota(jnp.int32, values[0].shape, 1)
    packed = None
    for block, value in enumerate(values):
        shift = (size * block - first) % depth
        moved = value if shift == 0 else pltpu.roll(value, shift, 1)
        packed = moved if block == 0 else jnp.where(lane >= size * block, moved, packed)
    return packed


def edges_of(ref, rows):
    two = [
        ref[2 * EDGE * pair : 2 * EDGE * (pair + 1), :].astype(jnp.float32)
        for pair in range(rows // 2)
    ]
    voxels = [two[row // 2][row % 2 * EDGE : (row % 2 + 1) * EDGE] for row in range(rows)]
    slots = range(rows * EDGE, ref.shape[0], 16)
    columns = [joined(ref[at : at + 16, :].astype(jnp.float32)) for at in slots]
    return voxels, jnp.concatenate(columns, axis=1)


def product(first, second):
    return jnp.dot(first, second, preferred_element_type=jnp.float32)


def mirrored_filter(kind, values, even, factor):
    rows = len(values)
    use_sum = even == (kind == 0)
    sign = 1.0 if use_sum else -1.0
    half = [values[row] + sign * values[rows - 1 - row] for row in range(rows // 2)]
    results = []
    for row in range(rows // 2):
        total = None
        for source, value in enumerate(half):
            near = tap(grad_taps(kind), source - row)
            far = tap(grad_taps(kind), rows - 1 - source - row)
            weight = 0.5 * (near + sign * far) / factor
            total = weight * value if total is None else total + weight * value
        results.append(total)
    return results


def weighted_products(three, weight):
    pairs = ((0, 0), (1, 1), (2, 2), (0, 1), (0, 2), (1, 2))
    first = [weight * value for value in three]
    return [first[a] * three[b] for a, b in pairs]


def late_mask(count, width):
    row = lax.broadcasted_iota(jnp.int32, (count, LANES), 0)
    left = max(width - 2 * R1 - EARLY, 0)
    place = jnp.where(row < left + EDGE, row - left + R1 - EDGE, row - left - EDGE + width - R1)
    place = place + lax.axis_index("plane") * width
    inside = (place >= 0) & (place < lax.axis_size("plane") * width)
    return jnp.where(inside | (row < left), 1.0, 0.0)


USED = (0, 1, 2, 5)
UNUSED = (3, 4)


def all_sums(products, coarse, sx):
    sums = [None] * 6
    for kinds in (USED, UNUSED):
        tiles = [tile for index in kinds for tile in products[index]]
        along = product(sx, jnp.concatenate(tiles, axis=1)).astype(jnp.bfloat16)
        step = along.shape[1] // len(kinds)
        parts = [along[:, index * step : (index + 1) * step] for index in range(len(kinds))]
        total = product(jnp.concatenate(parts, axis=0), coarse)
        high = sx.shape[0]
        for index, kind in enumerate(kinds):
            sums[kind] = total[index * high : (index + 1) * high]
    return sums


def tensor_sums(across, sx, mask, diagonal, z_parts, filtered, grads):
    double = diagonal.shape[1]
    depth, pairs = double // 2, across.shape[1] // double
    rows, count = 2 * pairs, across.shape[0] // 2
    for start in range(0, count, 16):
        kinds = [
            [
                across[kind * count + start : kind * count + start + 16, row * depth : (row + 1) * depth]
                for row in range(rows)
            ]
            for kind in range(2)
        ]
        for part in range(3):
            values = kinds[X_KINDS[part]]
            factor = float(DEPTH_TAPS[DEPTH_KINDS[part]][1])
            results = mirrored_filter(ROW_KINDS[part], values, True, factor)
            results += mirrored_filter(ROW_KINDS[part], values, False, factor)
            for row, result in enumerate(results):
                at = (part * pairs + row // 2) * count + start
                lanes = slice((row % 2) * depth, (row % 2 + 1) * depth)
                high = result.astype(jnp.bfloat16)
                filtered[0, at : at + 16, lanes] = high
                low = result - high.astype(jnp.float32)
                filtered[1, at : at + 16, lanes] = low.astype(jnp.bfloat16)

    at = 2 * pairs * count
    for kind, part in enumerate((slice(0, at), slice(at, filtered.shape[1]))):
        high, low = filtered[0, part, :], filtered[1, part, :]
        band = diagonal[kind * double : (kind + 1) * double, :]
        grads[part, :] = product(
            jnp.concatenate([high, low], axis=1), jnp.concatenate([band, band], axis=0)
        )

    weights = product_weights(rows)
    layer = lax.axis_index("depth")
    first, last = layer == 0, layer == lax.axis_size("depth") - 1
    place = lax.broadcasted_iota(jnp.int32, (16, depth), 1)
    complete = ((place >= R1) | first) & ((place < depth - R1) | last)
    complete = jnp.where(complete, 1.0, 0.0)
    groups = [[] for _ in range(6)]
    for start in range(0, count, 16):
        inside = complete if mask is None else complete * mask[start : start + 16]
        totals = None
        for row in range(rows):
            lanes = slice((row % 2) * depth, (row % 2 + 1) * depth)
            three = []
            for part in range(3):
                at = (part * pairs + row // 2) * count + start
                three.append(grads[at : at + 16, lanes])
            terms = weighted_products(three, 2.0 * float(weights[row % (rows // 2)]))
            totals = terms if row == 0 else [a + b for a, b in zip(totals, terms)]
        for index in range(6):
            groups[index].append((totals[index] * inside).astype(jnp.bfloat16))
    products = [[jnp.concatenate(group, axis=0)] for group in groups]
    return all_sums(products, z_parts[double : double + depth, :], sx)


def rim_tiles(values):
    rows, depth = len(values), values[0].shape[1]
    below = packed_rows(values, RIM, depth - RIM)
    above = pltpu.roll(packed_rows(values, RIM, 0), rows * RIM, 1)
    lane = lax.broadcasted_iota(jnp.int32, below.shape, 1)
    return [jnp.where(lane < rows * RIM, below, above), above, pltpu.roll(above, HALF, 1)]


def early_kernel(
    starts, grey, x_parts, z_parts, sums, diagonal, sides, tiles, across, filtered, grads
):
    rows, width, depth = grey.shape
    double = 2 * depth
    empty = jnp.zeros((depth, depth), jnp.bfloat16)
    for part in range(2):
        for half in range(2):
            at = pl.ds(part * double + half * depth, depth)
            band = z_parts[part * depth : (part + 1) * depth, :]
            diagonal[at, half * depth : (half + 1) * depth] = band
            diagonal[at, (1 - half) * depth : (2 - half) * depth] = empty
    values = [grey[row].astype(jnp.float32) for row in range(rows)]
    whole = jnp.concatenate([value.astype(jnp.bfloat16) for value in values], axis=1)
    twice = jnp.concatenate([whole, whole], axis=0)
    result = product(x_parts[starts[0] : starts[2], : 2 * width], twice)
    across[...] = result[: starts[1]]
    sides[...] = result[starts[1] :]
    sx = x_parts[starts[2] : starts[3], :EARLY]
    results = tensor_sums(across, sx, None, diagonal, z_parts, filtered, grads)
    for index, kind in enumerate(USED):
        sums[index] = results[kind]
    for index, tile in enumerate(rim_tiles(values)):
        tiles[index] = tile


def late_kernel(
    starts, width, far, near, x_late, z_parts, diagonal, early_sums, sides, own_tiles, temp, cure,
    out_hbm, across, filtered, grads, out, sems,
):
    double = diagonal.shape[1]
    depth = double // 2
    rows = across.shape[1] // depth
    count, lanes = temp.shape
    odd = is_odd()
    depths, layer = lax.axis_size("depth"), lax.axis_index("depth")
    outer, outer_columns = edges_of(far, rows)
    inner, inner_columns = edges_of(near, rows)
    values = []
    for row in range(rows):
        left = jnp.where(odd, inner[row], outer[row])
        right = jnp.where(odd, outer[row], inner[row])
        values.append(jnp.concatenate([left, right], axis=0))
    left = jnp.where(odd, inner_columns, outer_columns)
    right = jnp.where(odd, outer_columns, inner_columns)

    late = across.shape[0] // 2
    halos = jnp.concatenate([value.astype(jnp.bfloat16) for value in values], axis=1)
    halos = jnp.concatenate([halos, halos], axis=0)
    across[...] = sides[...] + product(x_late[starts[0] : starts[1], : 4 * EDGE], halos)

    products_x, voxels = own_columns(count)
    folded, stride = fold(voxels), COARSE * count
    tiles = [
        jnp.concatenate([tile[:EDGE], own_tiles[index], tile[EDGE:]], axis=0)
        for index, tile in enumerate(rim_tiles(values))
    ]
    missing = stride * (depths - 1) + voxels - tiles[0].shape[0]
    if missing > 0:
        spare = jnp.zeros((-(-missing // 8) * 8, LANES), jnp.float32)
        tiles = [jnp.concatenate([tile, spare], axis=0) for tile in tiles]

    height = count + 2 * HALO
    half_lane = lax.broadcasted_iota(jnp.int32, (folded, LANES), 1) < HALF
    order = meeting_order(out.shape[0])
    for position, target in enumerate(order):
        at = stride * target
        second = jnp.where(
            half_lane,
            tiles[1][at : at + folded],
            tiles[2][at + voxels - folded : at + voxels],
        )
        rims = jnp.concatenate([tiles[0][at : at + voxels], second], axis=0)
        out[position, 0 : voxels + folded, :] = rims.astype(jnp.bfloat16)
    split = (pl.ds(0, voxels + folded), pl.ds(voxels + folded, out.shape[1] - voxels - folded))
    copies = [
        pltpu.make_async_copy(out.at[:, part, :], out_hbm.at[:, part, :], sems.at[index])
        for index, part in enumerate(split)
    ]
    copies[0].start()

    sx = x_late[starts[1] : starts[2], :late]
    results = tensor_sums(
        across, sx, late_mask(late, width), diagonal, z_parts, filtered, grads
    )
    yy, xx, zz, xz = [early_sums[index] + results[kind] for index, kind in enumerate(USED)]
    lane = lax.broadcasted_iota(jnp.int32, yy.shape, 1)
    columns, cells = sizes(width, depth)
    tail = 4 * cells - LANES
    joint = pltpu.roll(xz, 3 * cells, 1)
    rest = jnp.where(lane < tail, joint, 0.0)
    rest = pltpu.roll(rest, 0, 1, stride=tail, stride_axis=0)
    for index, part in ((2, zz), (1, xx), (0, yy)):
        moved = part if index == 0 else pltpu.roll(part, index * cells, 1)
        joint = jnp.where(lane < (index + 1) * cells, moved, joint)

    own_first, own_last = column_rows(temp, cure, False), column_rows(temp, cure, True)
    half = chunk_rows(count, lanes)[1]
    for position, target in enumerate(order):
        piece = jnp.where(layer == target - 1, own_last, 0.0)
        piece = jnp.where(layer == target + 1, own_first, piece)
        if target == 0:
            piece = jnp.where(layer == depths - 1, left, piece)
        if target == out.shape[0] - 1:
            piece = jnp.where(layer == 0, right, piece)
        mine = slice(count * target, count * target + height)
        pieces = [coded(joint[mine]), coded(jnp.sum(rest[mine], axis=0, keepdims=True))]
        for slot in range(lanes // LANES):
            part = piece[:, slot * LANES : (slot + 1) * LANES]
            pieces += [part[:GHOST] - reference_temp, part[GHOST:COLUMN_ROWS]]
        filled = sum(part.shape[0] for part in pieces)
        if filled < half:
            pieces.append(jnp.zeros((half - filled, LANES), jnp.float32))
        out[position, voxels + folded :, :] = jnp.concatenate(pieces, axis=0).astype(jnp.bfloat16)
    copies[1].start()
    for copy in copies:
        copy.wait()


def rim_sums(chunks, count, starts, flat, steep, cells):
    parts = chunks.shape[0]
    rows_x, voxels = own_columns(count)
    folded = fold(voxels)
    tall = -(-voxels // 16) * 16
    spare = [jnp.zeros((tall - voxels, LANES), jnp.float32)] if tall > voxels else []
    lane = lax.broadcasted_iota(jnp.int32, (voxels, LANES), 1)
    order = meeting_order(parts)
    rims = [
        chunks[order.index(part), 0 : voxels + folded, :].astype(jnp.float32)
        for part in range(parts)
    ]
    tiles = []
    for below, above in zip(rims[:-1], rims[1:]):
        first = jnp.where(lane < ROWS * RIM, below[:voxels], above[:voxels])
        second = above[voxels:]
        second = [second[: voxels - folded], pltpu.roll(second, HALF, 1)]
        for tile in ([first], second):
            tiles.append(jnp.concatenate(tile + spare, axis=0).astype(jnp.bfloat16))
    wide = jnp.concatenate(tiles, axis=1)
    result = product(
        steep[starts[1] : starts[2], : 2 * tall], jnp.concatenate([wide, wide], axis=0)
    ).astype(jnp.bfloat16)
    kinds = []
    for kind in range(2):
        values = result[kind * rows_x : (kind + 1) * rows_x]
        stack = [
            values[:, 2 * part * LANES : 2 * (part + 1) * LANES] for part in range(parts - 1)
        ]
        stack = jnp.concatenate(stack, axis=0)
        kinds.append(jnp.concatenate([stack, stack], axis=1))
    both = product(kinds[0], flat[...])
    three = (both[:, :LANES], product(kinds[1], steep[starts[0] : starts[1], :LANES]), both[:, LANES:])

    index = lax.axis_index("plane") * lax.axis_size("depth") + lax.axis_index("depth")
    total = lax.axis_size("plane") * lax.axis_size("depth") * count * COARSE
    place = lax.rem(lax.broadcasted_iota(jnp.int32, three[0].shape, 0), rows_x)
    place = place + (index * count - HALO) * COARSE - R2
    inside = jnp.where((place >= 0) & (place < total), 1.0, 0.0)
    products = [
        [
            term[part * rows_x : (part + 1) * rows_x].astype(jnp.bfloat16)
            for part in range(parts - 1)
        ]
        for term in weighted_products(three, inside)
    ]
    return all_sums(products, cells[...], steep[starts[2] : starts[3], :rows_x])


def cure_kernel(
    cells, starts, chunks, temp_in, cure_in, tools, flat, steep, rim_bands, temp_hbm, cure_hbm,
    conduct_hbm, temp_out, cure_out, conduct_out, sems,
):
    count, lanes = temp_in.shape
    parts = chunks.shape[0]
    planes, depths = lax.axis_size("plane"), lax.axis_size("depth")
    plane, layer = lax.axis_index("plane"), lax.axis_index("depth")
    height = count + 2 * HALO
    own = cells - BEFORE - AFTER
    lane = lax.broadcasted_iota(jnp.int32, (16, lanes), 1)
    row = lax.broadcasted_iota(jnp.int32, (16, lanes), 0)
    at_sums, half = chunk_rows(count, lanes)
    tail = 4 * cells - LANES
    narrow_lane = lax.broadcasted_iota(jnp.int32, (16, LANES), 1)
    order = meeting_order(parts)

    near = rim_sums(chunks, count, starts, flat, steep, rim_bands)
    sums = [near[kind] for kind in USED]
    blocks = [chunks[order.index(part), at_sums:, :].astype(jnp.float32) for part in range(parts)]
    columns = [
        jnp.concatenate(
            [
                block[at : at + COLUMN_ROWS]
                for at in range(
                    height + 1, height + 1 + COLUMN_ROWS * (lanes // LANES), COLUMN_ROWS
                )
            ],
            axis=1,
        )
        for block in blocks
    ]
    blocks = [decoded(block[0:16]) for block in blocks]
    tails = [block[height : height + 1] for block in blocks]
    if parts % 8:
        tails.append(jnp.zeros((-parts % 8, LANES), jnp.float32))
    tails = jnp.concatenate(tails, axis=0)
    tails = pltpu.roll(tails, lax.rem(LANES - lax.rem(tail * count * layer, LANES), LANES), 1)
    narrow_row = lax.broadcasted_iota(jnp.int32, (16, LANES), 0)
    rests = [jnp.zeros((16, LANES), jnp.float32) for _ in range(parts)]
    for column in range(height):
        moved = pltpu.roll(tails, LANES - tail * column, 1) if column else tails
        for part in range(parts):
            rests[part] = jnp.where(narrow_row == column, moved[part : part + 1], rests[part])
    for part in range(parts):
        first_cell = own * part - BEFORE
        here = (lane >= first_cell) & (lane < first_cell + cells)
        values = blocks[part]
        joint = values[0:16]
        xz = pltpu.roll(jnp.where(narrow_lane < tail, rests[part], joint), LANES - 3 * cells, 1)
        for index in range(4):
            chunk = xz if index == 3 else joint
            if lanes > LANES:
                spare = jnp.zeros((16, lanes - LANES), jnp.float32)
                chunk = jnp.concatenate([chunk, spare], axis=1)
            shift = (first_cell - (index % 3) * cells) % lanes
            moved = chunk if shift == 0 else pltpu.roll(chunk, shift, 1)
            sums[index] = sums[index] + jnp.where(here, moved, 0.0)
    trace = sums[0] + sums[1] + sums[2]
    scale = (conduct_fiber - conduct_matrix) / (2.0 * trace + tensor_eps)
    conduct = [
        conduct_matrix + scale * (trace - sums[1]),
        -scale * sums[3],
        conduct_matrix + scale * (trace - sums[2]),
    ]
    for kind in range(3):
        conduct_out[kind] = conduct[kind][HALO : HALO + count]
    copies = [
        pltpu.make_async_copy(conduct_out, conduct_hbm, sems.at[0]),
        pltpu.make_async_copy(temp_out, temp_hbm, sems.at[1]),
        pltpu.make_async_copy(cure_out, cure_hbm, sems.at[2]),
    ]
    copies[0].start()

    before, after = columns[parts - 1], columns[0]
    for part in range(parts - 1):
        before = jnp.where(layer == part + 1, columns[part], before)
        after = jnp.where(layer == part, columns[part + 1], after)
    spare = jnp.full((16 - count - 2 * GHOST, lanes), 0.5, jnp.float32)
    temp = jnp.concatenate([
            before[:GHOST] + reference_temp,
            temp_in[...],
            after[:GHOST] + reference_temp,
            8.0 * spare,
        ], axis=0)
    cure = jnp.concatenate([spare[:1], before[GHOST:], cure_in[...], after[GHOST:], spare[:1], spare], axis=0)
    gap = GHOST - HALO
    xx, xz, zz = [pltpu.roll(part, gap, 0) for part in conduct]

    first = (plane == 0) & (layer == 0)
    last = (plane == planes - 1) & (layer == depths - 1)
    for step in range(STEPS):
        top, bottom = tools[2 * step : 2 * step + 1, :], tools[2 * step + 1 : 2 * step + 2, :]
        temp = jnp.where((row < GHOST) & first, temp[GHOST : GHOST + 1], temp)
        temp = jnp.where(
            (row >= GHOST + count) & last, temp[GHOST + count - 1 : GHOST + count], temp
        )
        cooler = jnp.where(lane == 0, top, pltpu.roll(temp, 1, 1))
        later = jnp.where(lane == lanes - 1, bottom, pltpu.roll(temp, lanes - 1, 1))
        slant = later - cooler
        second_x = pltpu.roll(temp, 15, 0) - 2.0 * temp + pltpu.roll(temp, 1, 0)
        second_z = later - 2.0 * temp + cooler
        cross = 0.25 * (pltpu.roll(slant, 15, 0) - pltpu.roll(slant, 1, 0))
        spread = xx * second_x + 2.0 * xz * cross + zz * second_z
        inverse = 1.0 / reference_temp - 1.0 / temp
        left = 1.0 - cure
        rate = rate_first * jnp.exp(energy_first * inverse) + rate_second * jnp.exp(
            energy_second * inverse
        ) * jnp.sqrt(cure)
        rate = rate * (left * jnp.sqrt(left))
        temp = temp + time_step * (spread + heat_release * rate)
        cure = cure + time_step * rate
    temp_out[...] = temp[GHOST : GHOST + count]
    cure_out[...] = cure[GHOST : GHOST + count]
    for copy in copies[1:]:
        copy.start()
    for copy in copies:
        copy.wait()


def on_device(intensity, temp_start, cure_start, tool_levels, plan):
    rows, width, depth = intensity.shape
    count, lanes = temp_start.shape
    planes, depths = lax.axis_size("plane"), lax.axis_size("depth")
    columns, cells = sizes(width, depth)
    bf16 = jnp.bfloat16
    slots = rows * EDGE + 16 * (lanes // LANES)
    params = pltpu.CompilerParams(vmem_limit_bytes=24 * 1024 * 1024)
    vmem = pl.BlockSpec(memory_space=pltpu.VMEM)
    stay = pl.BlockSpec(memory_space=pltpu.HBM)

    fixed = lambda values: pltpu.with_memory_space_constraint(values, pltpu.HBM)
    bands, coarse = x_bands(width), coarse_x_bands(width)
    late = bands.shape[1] - EARLY
    middle = bands[:, :EARLY, EDGE : EDGE + width]
    sides = bands[:, EARLY:].reshape(2 * late, -1)
    x_hbm, early_starts = stacked(
        halves(middle.reshape(2 * EARLY, -1), 1),
        halves(sides[:, EDGE : EDGE + width], 1),
        coarse[:, :EARLY],
    )
    z_hbm, _ = stacked(
        *depth_bands(depth), coarse_depth_bands(depth)
    )
    halos = np.concatenate([sides[:, :EDGE], sides[:, EDGE + width :]], axis=1)
    x_late, late_starts = stacked(halves(halos, 1), coarse[:, EARLY:])
    rims = rim_bands(rows)
    flat, _ = stacked(halves(np.concatenate([rims[0], rims[2]], axis=1), 0))
    steep, rim_starts = stacked(halves(rims[1], 0), *rim_x_bands(count))
    cell_bands, _ = stacked(rim_cells(rows, depth, depths))
    far, near, grey, x_parts, z_parts, temp, cure = pl.pallas_call(
        pack_kernel,
        name="pack",
        out_shape=(
            pltpu.VMEM((slots, depth), bf16),
            pltpu.VMEM((slots, depth), bf16),
            pltpu.VMEM((rows, width, depth), jnp.int32),
            pltpu.VMEM(x_hbm.shape, bf16),
            pltpu.VMEM(z_hbm.shape, bf16),
            pltpu.VMEM((count, lanes), jnp.float32),
            pltpu.VMEM((count, lanes), jnp.float32),
        ),
        in_specs=[stay] * 5,
        scratch_shapes=[
            pltpu.SemaphoreType.DMA((5,)),
        ],
        compiler_params=params,
    )(*[fixed(values) for values in (intensity, temp_start, cure_start, x_hbm, z_hbm)])

    def moved(values, pairs):
        index = [(p * depths + d, q * depths + e) for (p, d), (q, e) in pairs]
        return lax.ppermute(values, ("plane", "depth"), index)

    def swapped(values, first):
        pairs = [(p, p + 1) for p in range(first, planes - 1, 2)]
        pairs += [(q, p) for p, q in pairs]
        return moved(values, [((p, d), (q, d)) for p, q in pairs for d in range(depths)])

    far = swapped(far, 1)
    near = swapped(near, 0)

    high = coarse.shape[0]

    def scratch(count):
        return [
            pltpu.VMEM((2 * count, rows * depth), jnp.float32),
            pltpu.VMEM((2, 3 * rows // 2 * count, 2 * depth), bf16),
            pltpu.VMEM((3 * rows // 2 * count, 2 * depth), jnp.float32),
        ]

    def cost(count):
        return pl.CostEstimate(
            flops=2 * rows * (2 * count) * 160 * depth * 4,
            bytes_accessed=4_000_000,
            transcendentals=0,
        )

    early_sums, diagonal, sides, own_tiles = pl.pallas_call(
        functools.partial(early_kernel, early_starts),
        name="early",
        out_shape=(
            pltpu.VMEM((len(USED), high, LANES), jnp.float32),
            pltpu.VMEM((4 * depth, 2 * depth), bf16),
            pltpu.VMEM((2 * late, rows * depth), jnp.float32),
            pltpu.VMEM((3, width, LANES), jnp.float32),
        ),
        scratch_shapes=scratch(EARLY),
        cost_estimate=cost(EARLY),
        compiler_params=params,
    )(grey, x_parts, z_parts)

    products_x, voxels = own_columns(count)
    at_sums, half = chunk_rows(count, lanes)
    chunk_shape = (depths, at_sums + half, LANES)
    chunks = pl.pallas_call(
        functools.partial(late_kernel, late_starts, width),
        name="late",
        out_shape=pltpu.HBM(chunk_shape, bf16),
        in_specs=[vmem] * 10,
        out_specs=stay,
        scratch_shapes=scratch(late)
        + [pltpu.VMEM(chunk_shape, bf16), pltpu.SemaphoreType.DMA((2,))],
        cost_estimate=cost(late),
        compiler_params=params,
    )(far, near, x_late, z_parts, diagonal, early_sums, sides, own_tiles, temp, cure)

    faces = plan.reshape(2 * STEPS, 1) == jnp.arange(tool_levels.shape[0], dtype=jnp.int32)
    tools = jnp.sum(
        jnp.where(faces, tool_levels, jnp.zeros_like(tool_levels)), axis=1, keepdims=True
    )

    chunks = lax.all_to_all(
        chunks,
        "depth",
        split_axis=0,
        concat_axis=0,
        tiled=True,
        axis_index_groups=[meeting_order(depths)],
    )

    return pl.pallas_call(
        functools.partial(cure_kernel, cells, rim_starts),
        name="cure",
        out_shape=(
            pltpu.HBM((count, lanes), jnp.float32),
            pltpu.HBM((count, lanes), jnp.float32),
            pltpu.HBM((3, count, lanes), jnp.float32),
        ),
        in_specs=[vmem] * 7,
        out_specs=(stay, stay, stay),
        scratch_shapes=[
            pltpu.VMEM((count, lanes), jnp.float32),
            pltpu.VMEM((count, lanes), jnp.float32),
            pltpu.VMEM((3, count, lanes), jnp.float32),
            pltpu.SemaphoreType.DMA((3,)),
        ],
        compiler_params=params,
    )(chunks, temp, cure, tools, flat, steep, cell_bands)


def solution(mesh):
    return jax.shard_map(
        on_device,
        mesh=mesh,
        in_specs=(
            P(None, "plane", "depth"),
            P(("plane", "depth"), None),
            P(("plane", "depth"), None),
            P(),
            P(),
        ),
        out_specs=(
            P(("plane", "depth"), None),
            P(("plane", "depth"), None),
            P(None, ("plane", "depth"), None),
        ),
        check_vma=False,
    )
```
